32 devices in a mesh: ctx: 16 (over z, y, core), wa: 2 (over x).
Axes of the slice: x: 2, y: 2, z: 4, core: 2. Of those that a mesh axis runs over, the one named last changes fastest.
Arguments:
- tokens: bfloat16 [4, 4096, 768], P('wa', 'ctx'), may hold values from -6 to 6
- teacher: bfloat16 [4, 4096, 768], P('wa', 'ctx'), may hold values from -12 to 12
- lengths: int32 [4], P('wa'), may hold values from 1024 to 4096, as said below
- block_order: int32 [32], replicated, may hold values from 0 to 31, each once
- query_weight: bfloat16 [768, 768], P('wa'), may hold values from -0.21875 to 0.21875
- query_bias: bfloat16 [768], P('wa'), may hold values from -1.796875 to 1.796875
- key_weight: bfloat16 [768, 768], P('wa'), may hold values from -0.21875 to 0.21875
- value_weight: bfloat16 [768, 768], P('wa'), may hold values from -0.21875 to 0.21875
- value_bias: bfloat16 [768], P('wa'), may hold values from -0.059814453 to 0.059814453
- out_weight: bfloat16 [768, 768], P('wa'), may hold values from -12 to 12
- out_bias: bfloat16 [768], P('wa'), may hold values from -1.796875 to 1.796875
- gain_one: bfloat16 [768], P('wa'), may hold values from 0.5 to 1.5
- shift_one: bfloat16 [768], P('wa'), may hold values from -1.796875 to 1.796875
- inner_weight: bfloat16 [768, 3072], P('wa'), may hold values from -0.21875 to 0.21875
- inner_bias: bfloat16 [3072], P('wa'), may hold values from -1.796875 to 1.796875
- outer_weight: bfloat16 [3072, 768], P('wa'), may hold values from -0.109375 to 0.109375
- outer_bias: bfloat16 [768], P('wa'), may hold values from -1.796875 to 1.796875
- gain_two: bfloat16 [768], P('wa'), may hold values from 0.5 to 1.5
- shift_two: bfloat16 [768], P('wa'), may hold values from -1.796875 to 1.796875
Outputs:
- output: bfloat16 [4, 4096, 768], P('wa', 'ctx')
- tokens_grad: float32 [4, 4096, 768], P('wa', 'ctx')
- query_weight_grad: float32 [768, 768], P('wa')
- query_bias_grad: float32 [768], P('wa')
- key_weight_grad: float32 [768, 768], P('wa')
- value_weight_grad: float32 [768, 768], P('wa')
- value_bias_grad: float32 [768], P('wa')
- out_weight_grad: float32 [768, 768], P('wa')
- out_bias_grad: float32 [768], P('wa')
- gain_one_grad: float32 [768], P('wa')
- shift_one_grad: float32 [768], P('wa')
- inner_weight_grad: float32 [768, 3072], P('wa')
- inner_bias_grad: float32 [3072], P('wa')
- outer_weight_grad: float32 [3072, 768], P('wa')
- outer_bias_grad: float32 [768], P('wa')
- gain_two_grad: float32 [768], P('wa')
- shift_two_grad: float32 [768], P('wa')
- loss: float32 [], replicated
The draws below stay inside these ranges and needn't reach their ends.
Inputs may be any that keep to these rules, and one draw needn't show every extreme that they name: `lengths`: one sequence of every draw fills all 4096 slots. `block_order`: every block number appears once.
All inputs are finite; a program needn't handle non-finite values.
Results may differ from the reference program's by a relative error of at most 0.017.
Values may be sent and summed in bfloat16 or wider, within the bound.
A program may use at most 384 MiB of HBM per device.

```python
import math
import jax
import jax.numpy as jnp
from jax import lax

D = 768
H = 12
DH = 64
FF = 3072
SLOTS = 4096
BATCH = 4
BLK = 128
BLOCKS = 32


def draw_lengths(key, part):
    first_key, second_key = jax.random.split(key)
    drawn = jax.random.randint(first_key, (BATCH,), SLOTS // 4, SLOTS + 1)
    longest = jax.random.randint(second_key, (), 0, BATCH)
    return jnp.where(jnp.arange(BATCH) == longest, SLOTS, drawn).astype(jnp.int32)


def draw_teacher(key, part):
    key = jax.random.fold_in(key, 7)
    place = jnp.arange(SLOTS, dtype=jnp.float32) / SLOTS
    raw = jnp.clip(jax.random.normal(key, (BATCH, SLOTS, D), jnp.float32), -4.0, 4.0)
    factor = 0.5 * jnp.power(6.0, place)
    return (raw * factor[None, :, None]).astype(jnp.bfloat16)


def steps_of(rng, shape, shards, low, largest):
    level, own = 1.0, jax.random.fold_in(rng, 6)
    for position, blocks in shards:
        draws = jnp.exp(jax.random.uniform(jax.random.fold_in(own, position), (blocks,), jnp.float32, low / len(shards), largest / len(shards)))
        level = level * jnp.repeat(draws, shape[position] // blocks).reshape([-1 if axis == position else 1 for axis in range(len(shape))])
    return level


def noise(stream_key, extent, scale, bound, cuts=(), held_as=jnp.bfloat16):
    values = jax.random.normal(stream_key, extent, jnp.float32) * scale
    if len(cuts) > 0:
        values = steps_of(stream_key, extent, cuts, -0.22, 0.18) * values
    return jnp.clip(values, min=-bound, max=bound).astype(held_as)


def setup_inputs(seed: int = 0) -> dict:
    key_of = jax.random.split(jax.random.key(seed), 20)
    return {
        "tokens": noise(key_of[0], (BATCH, SLOTS, D), 1.0, 6.0, ((0, 2), (1, 16))),
        "teacher": draw_teacher(jax.random.fold_in(key_of[19], 71), 0),
        "lengths": draw_lengths(jax.random.fold_in(key_of[19], 71), 0),
        "block_order": jax.random.permutation(key_of[3], BLOCKS).astype(jnp.int32),
        "query_weight": noise(key_of[4], (D, D), D ** -0.5, 0.21875, ((0, 2),)),
        "query_bias": noise(key_of[5], (D,), 0.3, 1.796875, ((0, 2),)),
        "key_weight": noise(key_of[6], (D, D), D ** -0.5, 0.21875, ((0, 2),)),
        "value_weight": noise(key_of[7], (D, D), D ** -0.5, 0.21875, ((0, 2),)),
        "value_bias": noise(key_of[8], (D,), 0.01, 0.059814453, ((0, 2),)),
        "out_weight": noise(key_of[9], (D, D), 2.0, 12.0, ((0, 2),)),
        "out_bias": noise(key_of[10], (D,), 0.3, 1.796875, ((0, 2),)),
        "gain_one": jnp.clip(1.0 + 0.1 * jax.random.normal(key_of[11], (D,), jnp.float32), 0.5, 1.5).astype(jnp.bfloat16),
        "shift_one": noise(key_of[12], (D,), 0.3, 1.796875, ((0, 2),)),
        "inner_weight": noise(key_of[13], (D, FF), D ** -0.5, 0.21875, ((0, 2),)),
        "inner_bias": noise(key_of[14], (FF,), 0.3, 1.796875, ((0, 2),)),
        "outer_weight": noise(key_of[15], (FF, D), FF ** -0.5, 0.109375, ((0, 2),)),
        "outer_bias": noise(key_of[16], (D,), 0.3, 1.796875, ((0, 2),)),
        "gain_two": jnp.clip(1.0 + 0.1 * jax.random.normal(key_of[17], (D,), jnp.float32), 0.5, 1.5).astype(jnp.bfloat16),
        "shift_two": noise(key_of[18], (D,), 0.3, 1.796875, ((0, 2),)),
    }


@jax.custom_vjp
def low(v):
    return lax.optimization_barrier(v.astype(jnp.bfloat16)).astype(jnp.float32)

@jax.custom_vjp
def low_back(v):
    return v

def low_keep(v):
    return (low(v), None)

def low_pass(kept, grad):
    return (grad,)

def back_keep(v):
    return (v, None)

def back_low(kept, grad):
    return (low(grad),)
low.defvjp(low_keep, low_pass)
low_back.defvjp(back_keep, back_low)
exact_mode = lax.Precision.HIGHEST

def matmul(left, right):
    return jnp.dot(left, right, precision=exact_mode, preferred_element_type=jnp.float32)

def normalize(values):
    average = lax.optimization_barrier(jnp.mean(values, -1, keepdims=True))
    centered = values - average
    spread = lax.optimization_barrier(jnp.mean(centered * centered, -1, keepdims=True))
    return centered * lax.rsqrt(spread + 1e-06)

def attend_block(queries, keys_all, values_all, usable):
    logits = jnp.einsum('qhd,khd->hqk', queries, keys_all, precision=exact_mode) * DH ** (-0.5)
    scores = low_back(jnp.where(usable[None, None, :], logits, -1e+30))
    logsum = jax.nn.logsumexp(scores, axis=-1, keepdims=True)
    weights = low(jnp.exp(scores - logsum))
    return jnp.einsum('hqk,khd->qhd', weights, values_all, precision=exact_mode)

def attend_sequence(queries, keys_all, values_all, usable):
    rows_block = math.gcd(SLOTS, 512)
    blocks = queries.reshape(SLOTS // rows_block, rows_block, H, DH)
    mapped = lax.map(jax.checkpoint(lambda block: attend_block(block, keys_all, values_all, usable)), blocks)
    return mapped.reshape(SLOTS, D)

def to_heads(values):
    return values.reshape(BATCH, SLOTS, H, DH)

def layer(inputs, query_weight, query_bias, key_weight, value_weight, value_bias, out_weight, out_bias, gain_one, shift_one, inner_weight, inner_bias, outer_weight, outer_bias, gain_two, shift_two, targets, usable):
    queries = low(low_back(matmul(inputs, query_weight) + query_bias))
    keys_all = low(low_back(matmul(inputs, key_weight)))
    values_all = low(low_back(matmul(inputs, value_weight) + value_bias))
    attended = lax.map(lambda group: attend_sequence(group[0], group[1], group[2], group[3]), (to_heads(queries), to_heads(keys_all), to_heads(values_all), usable))
    attended_low = low(low_back(attended))
    branch = low_back(matmul(attended_low, out_weight) + out_bias)
    first = inputs + branch
    hidden_in = normalize(first) * gain_one + shift_one
    inner_act = low_back(matmul(low(hidden_in), inner_weight) + inner_bias)
    activated = low(jax.nn.gelu(inner_act, approximate=False))
    outer = low_back(matmul(activated, outer_weight) + outer_bias)
    final_rows = normalize(hidden_in + outer) * gain_two + shift_two
    residue = jnp.where(usable[..., None], final_rows - targets, 0.0)
    return (0.5 * jnp.sum(residue * residue), final_rows)

def reference(tokens, teacher, lengths, block_order, query_weight, query_bias, key_weight, value_weight, value_bias, out_weight, out_bias, gain_one, shift_one, inner_weight, inner_bias, outer_weight, outer_bias, gain_two, shift_two):
    params = [member.astype(jnp.float32) for member in (query_weight, query_bias, key_weight, value_weight, value_bias, out_weight, out_bias, gain_one, shift_one, inner_weight, inner_bias, outer_weight, outer_bias, gain_two, shift_two)]
    slot_ids = jnp.arange(SLOTS, dtype=jnp.int32)
    positions = block_order[slot_ids // BLK] * BLK + slot_ids % BLK
    usable = positions[None, :] < lengths[:, None]
    targets = teacher.astype(jnp.float32)

    def objective(*primals):
        return layer(*primals, targets, usable)
    total, pull, final_rows = jax.vjp(objective, tokens.astype(jnp.float32), *params, has_aux=True)
    grads = pull(jnp.ones((), jnp.float32))
    count = jnp.sum(usable.astype(jnp.float32))
    loss = 2.0 * total / (count * D)
    return (final_rows.astype(jnp.bfloat16), grads[0], grads[1], grads[2], grads[3], grads[4], grads[5], grads[6], grads[7], grads[8], grads[9], grads[10], grads[11], grads[12], grads[13], grads[14], grads[15], loss)
```

```python
import functools
import math

import jax
import jax.numpy as jnp
from jax import lax
from jax.experimental import pallas as pl
from jax.experimental.pallas import tpu as pltpu
from jax.sharding import PartitionSpec as P

DH = 64
BLK = 128
GROUPS = 4
LN2 = math.log(2.0)
NT = (((1,), (1,)), ((), ()))
NN = (((1,), (0,)), ((), ()))
TN = (((0,), (0,)), ((), ()))
F32 = jnp.float32
BF16 = jnp.bfloat16
VMEM = pl.BlockSpec(memory_space=pltpu.VMEM)
SMEM = pl.BlockSpec(memory_space=pltpu.SMEM)
ANY = pl.BlockSpec(memory_space=pl.ANY)
ROOM = pltpu.CompilerParams(vmem_limit_bytes=58 * 2**20)


def dot(left, right, dims=NN):
    return lax.dot_general(left, right, dims, preferred_element_type=F32)


def cost(us):
    return pl.CostEstimate(flops=int(us * 1.15e9), bytes_accessed=1 << 20, transcendentals=0)


def weight_copies(full, own, first, second, sems, base):
    x, c = lax.axis_index("wa"), lax.rem(lax.axis_index("ctx"), 2)
    half = own.shape[0]
    quarter = half // 2
    other = (1 - x) * half
    places = (
        (own, x * half, half),
        (first, other + c * quarter, quarter),
        (second, other + (1 - c) * quarter, quarter),
    )
    return [
        pltpu.make_async_copy(
            src, full.at[pl.ds(pl.multiple_of(start, quarter), size)], sems.at[base + i]
        )
        for i, (src, start, size) in enumerate(places)
    ]


def project_kernel(tok, vec, wq, wk, wv, first, second, *rest):
    seqs, rows, width = tok.shape
    outs, (full, sems) = rest[: 2 * seqs], rest[2 * seqs :]
    quarter = wq.shape[0] // 2
    copies = []
    for i, own in enumerate((wq, wk, wv)):
        part = pl.ds(i * quarter, quarter)
        copies.append(
            weight_copies(full.at[i], own, first.at[part], second.at[part], sems, 3 * i)
        )
    for group in copies:
        for copy in group:
            copy.start()
    flat = tok[...].reshape(seqs * rows, width)
    per = width // GROUPS
    heads = per // DH
    for copy in copies[1]:
        copy.wait()
    keys = dot(flat, full[1]).astype(BF16)
    for copy in copies[2]:
        copy.wait()
    values = (dot(flat, full[2]) + vec[1:2, :]).astype(BF16)
    for s in range(seqs):
        rs = slice(s * rows, (s + 1) * rows)
        for g in range(GROUPS):
            for h in range(heads):
                cols = slice(g * per + h * DH, g * per + (h + 1) * DH)
                outs[2 * s + 1][g, :, h * 128 : (h + 1) * 128] = jnp.concatenate(
                    [keys[rs, cols], values[rs, cols]], 1
                )
    for copy in copies[0]:
        copy.wait()
    queries = ((dot(flat, full[0]) + vec[0:1, :]) * (DH**-0.5 / LN2)).astype(BF16)
    for s in range(seqs):
        rs = slice(s * rows, (s + 1) * rows)
        for g in range(GROUPS):
            outs[2 * s][g] = queries[rs, g * per : (g + 1) * per]


def project(tok, vec, wq, wk, wv, first, second):
    seqs, rows, width = tok.shape
    per = width // GROUPS
    shapes = [
        jax.ShapeDtypeStruct((GROUPS, rows, n), BF16) for _ in range(seqs) for n in (per, 2 * per)
    ]
    return pl.pallas_call(
        project_kernel,
        out_shape=shapes,
        in_specs=[VMEM, VMEM] + [ANY] * 5,
        out_specs=[VMEM] * len(shapes),
        scratch_shapes=[pltpu.VMEM((3, width, width), BF16), pltpu.SemaphoreType.DMA((9,))],
        compiler_params=ROOM,
        cost_estimate=cost(5),
        name="project",
    )(tok, vec, wq, wk, wv, first, second)


def load_pieces(pieces, kv, sems):
    per = pieces[0].shape[0]
    copies = [
        pltpu.make_async_copy(piece, kv.at[pl.ds(i * per, per)], sems.at[i])
        for i, piece in enumerate(pieces)
    ]
    for copy in copies:
        copy.start()
    for copy in copies:
        copy.wait()


def forward_kernel(wide, narrow, count, sc, q_ref, *rest):
    pieces, (o_ref, lse_ref, kv_ref, qa, acc, sums, sems) = rest[:count], rest[count:]
    blocks = q_ref.shape[0]
    heads = q_ref.shape[2] // DH
    rows = blocks * BLK
    length = sc[0]
    load_pieces(pieces, kv_ref, sems)

    def gather(h, start, n):
        return jnp.concatenate(
            [kv_ref[sc[8 + blocks + start + i], :, h * 128 : (h + 1) * 128] for i in range(n)], 0
        )

    whole = length // (wide * BLK)
    tail = whole * wide
    tails = (length - tail * BLK + narrow * BLK - 1) // (narrow * BLK)
    for h in range(heads):
        hs = slice(h * DH, (h + 1) * DH)
        own = jnp.concatenate([q_ref[b, :, hs] for b in range(blocks)], 0)
        qa[...] = jnp.concatenate([own, jnp.zeros_like(own)], 1)
        acc[...] = jnp.zeros_like(acc)
        sums[...] = jnp.zeros_like(sums)

        def step(start, n, masked, h=h):
            kv = gather(h, start, n)
            scores = dot(qa[...], kv, NT)
            if masked:
                place = lax.broadcasted_iota(jnp.int32, scores.shape, 1) + start * BLK
                scores = jnp.where(place < length, scores, -1e30)
            p = jnp.exp2(scores)
            sums[...] += sum(p[:, i * 128 : (i + 1) * 128] for i in range(n))
            acc[...] += dot(p.astype(BF16), kv)

        def wide_step(j, _, step=step):
            step(j * wide, wide, False)
            return 0

        def narrow_step(j, _, step=step):
            step(tail + j * narrow, narrow, True)
            return 0

        lax.fori_loop(0, whole, wide_step, 0)
        lax.fori_loop(0, tails, narrow_step, 0)
        total = jnp.sum(sums[...], 1, keepdims=True)
        across = jnp.transpose(jnp.broadcast_to(total, (rows, 128)))[:8]
        good = (jnp.min(across) > 2.0**-80) & (jnp.max(across) < 2.0**100)

        @pl.when(good)
        def _(h=h, hs=hs, total=total, across=across):
            lse_ref[h] = jnp.log2(across)
            o_ref[:, hs] = (acc[:, DH:] * (1.0 / total)).astype(BF16)

        @pl.when(jnp.logical_not(good))
        def _(h=h, hs=hs):
            key_blocks = (length + BLK - 1) // BLK

            def rows_step(t, _):
                part = pl.ds(pl.multiple_of(t * BLK, BLK), BLK)
                q = qa[part, :]

                def scores_of(j):
                    kv = gather(h, j, 1)
                    scores = dot(q, kv, NT)
                    place = lax.broadcasted_iota(jnp.int32, scores.shape, 1) + j * BLK
                    return kv, jnp.where(place < length, scores, -1e30)

                largest = lax.fori_loop(
                    0,
                    key_blocks,
                    lambda j, m: jnp.maximum(m, jnp.max(scores_of(j)[1], 1, keepdims=True)),
                    jnp.full((BLK, 1), -1e30, F32),
                )
                acc[part, :] = jnp.zeros((BLK, 128), F32)
                sums[part, :] = jnp.zeros((BLK, 128), F32)

                def add(j, _):
                    kv, scores = scores_of(j)
                    p = jnp.exp2(scores - largest)
                    sums[part, :] += p
                    acc[part, :] += dot(p.astype(BF16), kv)
                    return 0

                lax.fori_loop(0, key_blocks, add, 0)
                row_total = jnp.sum(sums[part, :], 1, keepdims=True)
                lse = largest + jnp.log2(row_total)
                lse_ref[h, :, part] = jnp.transpose(jnp.broadcast_to(lse, (BLK, 128)))[:8]
                o_ref[part, hs] = (acc[part, :][:, DH:] * (1.0 / row_total)).astype(BF16)
                return 0

            lax.fori_loop(0, rows // BLK, rows_step, 0)


def attend(sc, q, pieces):
    blocks, _, per = q.shape
    rows, heads = blocks * BLK, per // DH
    key_blocks = len(pieces) * pieces[0].shape[0]
    return pl.pallas_call(
        functools.partial(forward_kernel, 8, 2, len(pieces)),
        out_shape=(
            jax.ShapeDtypeStruct((rows, per), BF16),
            jax.ShapeDtypeStruct((heads, 8, rows), F32),
        ),
        in_specs=[SMEM, VMEM] + [ANY] * len(pieces),
        out_specs=(VMEM, VMEM),
        scratch_shapes=[
            pltpu.VMEM((key_blocks, BLK, 2 * per), BF16),
            pltpu.VMEM((rows, 128), BF16),
            pltpu.VMEM((rows, 128), F32),
            pltpu.VMEM((rows, 128), F32),
            pltpu.SemaphoreType.DMA((len(pieces),)),
        ],
        compiler_params=ROOM,
        cost_estimate=cost(20),
        name="attend",
    )(sc, q, *pieces)


def backward_kernel(qn, kn, count, sc, q_ref, do_ref, o_ref, lse_ref, *rest):
    pieces, dq_ref, outs = rest[:count], rest[count], rest[count + 1 : 2 * count + 1]
    kv_ref, both, dkv, dq, lse_row, delta_row, sems = rest[2 * count + 1 :]
    blocks = q_ref.shape[0]
    heads = q_ref.shape[2] // DH
    key_blocks = kv_ref.shape[0]
    tile = qn * BLK
    length, used = sc[0], sc[1]
    whole = length // (kn * BLK)
    parts = (length + kn * BLK - 1) // (kn * BLK)
    tiles = (used + qn - 1) // qn
    ones = jnp.ones((8, DH), BF16)
    load_pieces(pieces, kv_ref, sems)
    for h in range(heads):
        hs = slice(h * DH, (h + 1) * DH)

        def clear(i, _):
            dkv[pl.ds(pl.multiple_of(i * 1024, 1024), 1024), :] = jnp.zeros((1024, 128), F32)
            return 0

        lax.fori_loop(0, key_blocks // 8, clear, 0)
        dq[...] = jnp.zeros_like(dq)

        def prepare(t, _, h=h, hs=hs):
            base = pl.multiple_of(t * (2 * tile), 2 * tile)
            start = pl.multiple_of(t * tile, tile)
            places = [sc[8 + t * qn + i] for i in range(qn)]
            q = jnp.concatenate([q_ref[s, :, hs] for s in places], 0)
            do = jnp.concatenate([do_ref[s, :, hs] for s in places], 0)
            o = jnp.concatenate([o_ref[s, :, hs] for s in places], 0)
            zero = jnp.zeros_like(q)
            both[pl.ds(base, tile), :] = jnp.concatenate([q, zero], 1)
            both[pl.ds(base + tile, tile), :] = jnp.concatenate([zero, do], 1)
            product = do.astype(F32) * o.astype(F32)
            high = product.astype(BF16)
            rest_of = (product - high.astype(F32)).astype(BF16)
            delta_row[:, pl.ds(start, tile)] = dot(ones, high, NT) + dot(ones, rest_of, NT)
            lse_row[:, pl.ds(start, tile)] = jnp.concatenate(
                [lse_ref[h, :, pl.ds(pl.multiple_of(s * BLK, BLK), BLK)] for s in places], 1
            )
            return 0

        lax.fori_loop(0, tiles, prepare, 0)

        def rows_step(t, _, h=h):
            base = pl.multiple_of(t * (2 * tile), 2 * tile)
            span = pl.ds(pl.multiple_of(t * tile, tile), tile)

            def step(j, masked):
                places = [sc[8 + blocks + j * kn + i] for i in range(kn)]
                kv = jnp.concatenate([kv_ref[s, :, h * 128 : (h + 1) * 128] for s in places], 0)
                b = both[pl.ds(base, 2 * tile), :]
                found = dot(kv, b, NT)
                p = jnp.exp2(found[:, :tile] - lse_row[:1, span])
                if masked:
                    place = lax.broadcasted_iota(jnp.int32, p.shape, 0) + j * (kn * BLK)
                    p = jnp.where(place < length, p, 0.0)
                ds = (p * (found[:, tile:] - delta_row[:1, span])).astype(BF16)
                grads = dot(jnp.concatenate([ds, p.astype(BF16)], 1), b)
                for i, s in enumerate(places):
                    dkv[pl.ds(pl.multiple_of(s * BLK, BLK), BLK), :] += grads[
                        i * BLK : (i + 1) * BLK
                    ]
                dq[span, :] += dot(ds, kv, TN)

            def whole_step(j, _):
                step(j, False)
                return 0

            lax.fori_loop(0, whole, whole_step, 0)

            @pl.when(parts > whole)
            def _():
                step(whole, True)

            return 0

        lax.fori_loop(0, tiles, rows_step, 0)
        for i in range(blocks):
            dq_ref[sc[8 + i], :, hs] = (
                dq[i * BLK : (i + 1) * BLK, :DH] * DH**-0.5
            ).astype(BF16)
        level = jnp.where(lax.broadcasted_iota(jnp.int32, (1, 128), 1) < DH, LN2, 1.0)
        per_piece = key_blocks // count
        for n, out in enumerate(outs):
            for i in range(per_piece):
                b = n * per_piece + i
                out[i, :, h * 128 : (h + 1) * 128] = (
                    dkv[b * BLK : (b + 1) * BLK, :] * level
                ).astype(BF16)


def attend_back(sc, q, do, o, lse, pieces):
    blocks, _, per = q.shape
    rows = blocks * BLK
    key_blocks = len(pieces) * pieces[0].shape[0]
    return pl.pallas_call(
        functools.partial(backward_kernel, 4, 4, len(pieces)),
        out_shape=[jax.ShapeDtypeStruct(q.shape, BF16)]
        + [jax.ShapeDtypeStruct(p.shape, BF16) for p in pieces],
        in_specs=[SMEM] + [VMEM] * 4 + [ANY] * len(pieces),
        out_specs=[VMEM] * (1 + len(pieces)),
        scratch_shapes=[
            pltpu.VMEM((key_blocks, BLK, 2 * per), BF16),
            pltpu.VMEM((2 * rows, 128), BF16),
            pltpu.VMEM((key_blocks * BLK, 128), F32),
            pltpu.VMEM((rows, 128), F32),
            pltpu.VMEM((8, rows), F32),
            pltpu.VMEM((8, rows), F32),
            pltpu.SemaphoreType.DMA((len(pieces),)),
        ],
        compiler_params=ROOM,
        cost_estimate=cost(45),
        name="attend_back",
    )(sc, q, do, o, lse, *pieces)


def norm(values):
    centered = values - jnp.mean(values, -1, keepdims=True)
    inverse = lax.rsqrt(jnp.mean(centered * centered, -1, keepdims=True) + 1e-6)
    return centered * inverse, inverse


def norm_back(upstream, normed, inverse):
    return inverse * (
        upstream
        - jnp.mean(upstream, -1, keepdims=True)
        - normed * jnp.mean(upstream * normed, -1, keepdims=True)
    )


def normal_parts(x):
    z = jnp.abs(x) * (0.5**0.5)
    bell = jnp.exp(-0.5 * x * x)
    t = 1.0 / (1.0 + 0.3275911 * z)
    poly = t * (
        0.254829592
        + t * (-0.284496736 + t * (1.421413741 + t * (-1.453152027 + t * 1.061405429)))
    )
    upper = 0.5 * poly * bell
    return jnp.where(x >= 0, 1.0 - upper, upper), bell * (2.0 * math.pi) ** -0.5


def dense_kernel(sc, att4, tok, teach, vec, wide_vec, *rest):
    weights, rest = rest[:9], rest[9:]
    outs, (wo, wi, wu, slope, sems) = rest[:11], rest[11:]
    out, fg, ag, att_o, br_o, hl_o, il_o, act_o, ol_o, sums, wide_sums = outs
    rows, width = tok.shape
    hidden = wi.shape[1]
    tile = 512
    copies = [
        weight_copies(full, *weights[3 * i : 3 * i + 3], sems, 3 * i)
        for i, full in enumerate((wo, wi, wu))
    ]
    for group in copies:
        for copy in group:
            copy.start()
    per = att4.shape[2]
    att = jnp.concatenate([att4[g] for g in range(GROUPS)], 1)
    att_o[...] = att
    row = lax.broadcasted_iota(jnp.int32, (rows, 1), 0)
    mask = jnp.where(
        row < BLK, jnp.where(row < sc[0], 1.0, 0.0), jnp.where(row - BLK < sc[1], 1.0, 0.0)
    )
    out_bias, gain_one, shift_one = vec[0:1, :], vec[1:2, :], vec[2:3, :]
    outer_bias, gain_two, shift_two = vec[3:4, :], vec[4:5, :], vec[5:6, :]
    for copy in copies[0]:
        copy.wait()
    first = tok[...].astype(F32) + dot(att, wo[...]) + out_bias
    normed_one, inverse_one = norm(first)
    hidden_in = normed_one * gain_one + shift_one
    hl = hidden_in.astype(BF16)
    hl_o[...] = hl
    for copy in copies[1] + copies[2]:
        copy.wait()
    second = hidden_in + outer_bias
    for n in range(hidden // tile):
        cols = slice(n * tile, (n + 1) * tile)
        inner = dot(hl, wi[:, cols]) + wide_vec[0:1, cols]
        below, density = normal_parts(inner)
        act = (inner * below).astype(BF16)
        act_o[:, cols] = act
        slope[:, cols] = below + inner * density
        second += dot(act, wu[cols, :])
    normed_two, inverse_two = norm(second)
    final = normed_two * gain_two + shift_two
    out[...] = final.astype(BF16)
    residue = (final - teach[...].astype(F32)) * mask
    add = functools.partial(jnp.sum, axis=0, keepdims=True)
    second_grad = norm_back(residue * gain_two, normed_two, inverse_two)
    ol = second_grad.astype(BF16)
    ol_o[...] = ol
    hidden_grad = second_grad
    for n in range(hidden // tile):
        cols = slice(n * tile, (n + 1) * tile)
        il = (dot(ol, wu[cols, :], NT) * slope[:, cols]).astype(BF16)
        il_o[:, cols] = il
        wide_sums[0:1, cols] = add(il.astype(F32))
        hidden_grad += dot(il, wi[:, cols], NT)
    first_grad = norm_back(hidden_grad * gain_one, normed_one, inverse_one)
    fg[...] = first_grad
    br = first_grad.astype(BF16)
    br_o[...] = br
    att_grad = dot(br, wo[...], NT).astype(BF16)
    for g in range(GROUPS):
        ag[g] = att_grad[:, g * per : (g + 1) * per]
    sums[0:1, :] = add(residue * normed_two)
    sums[1:2, :] = add(residue)
    sums[2:3, :] = add(ol.astype(F32))
    sums[3:4, :] = add(hidden_grad * normed_one)
    sums[4:5, :] = add(hidden_grad)
    sums[5:6, :] = add(br.astype(F32))
    sums[6:7, :] = add(residue * residue)
    sums[7:8, :] = jnp.zeros((1, width), F32)


def dense(sc, att4, tok, teach, vec, wide_vec, weights):
    rows, width = tok.shape
    hidden = wide_vec.shape[1]
    narrow = jax.ShapeDtypeStruct((rows, width), BF16)
    wide = jax.ShapeDtypeStruct((rows, hidden), BF16)
    return pl.pallas_call(
        dense_kernel,
        out_shape=[
            narrow,
            jax.ShapeDtypeStruct((rows, width), F32),
            jax.ShapeDtypeStruct(att4.shape, BF16),
            narrow,
            narrow,
            narrow,
            wide,
            wide,
            narrow,
            jax.ShapeDtypeStruct((8, width), F32),
            jax.ShapeDtypeStruct((1, hidden), F32),
        ],
        in_specs=[SMEM] + [VMEM] * 5 + [ANY] * 9,
        out_specs=[VMEM] * 11,
        scratch_shapes=[
            pltpu.VMEM((width, width), BF16),
            pltpu.VMEM((width, hidden), BF16),
            pltpu.VMEM((hidden, width), BF16),
            pltpu.VMEM((rows, hidden), F32),
            pltpu.SemaphoreType.DMA((9,)),
        ],
        compiler_params=ROOM,
        cost_estimate=cost(15),
        name="dense",
    )(sc, att4, tok, teach, vec, wide_vec, *weights)


def dense_grads_kernel(seqs, *refs):
    ins, (g_out, g_inner, g_outer) = refs[: 6 * seqs], refs[6 * seqs :]
    att, br, hl, il, act, ol = (
        jnp.concatenate([ins[6 * s + i][...] for s in range(seqs)], 0) for i in range(6)
    )
    for target, left, right in ((g_out, att, br), (g_inner, hl, il), (g_outer, act, ol)):
        rows = target.shape[1]
        for n in range(4):
            piece = left[:, n * rows : (n + 1) * rows]
            for t in range(right.shape[1] // 768):
                cols = slice(t * 768, (t + 1) * 768)
                target[n, :, cols] = dot(piece, right[:, cols], TN).astype(BF16)


def dense_grads(saved):
    seqs = len(saved)
    width, hidden = saved[0][0].shape[1], saved[0][3].shape[1]
    return pl.pallas_call(
        functools.partial(dense_grads_kernel, seqs),
        out_shape=[
            jax.ShapeDtypeStruct((4, width // 4, width), BF16),
            jax.ShapeDtypeStruct((4, width // 4, hidden), BF16),
            jax.ShapeDtypeStruct((4, hidden // 4, width), BF16),
        ],
        in_specs=[VMEM] * (6 * seqs),
        out_specs=[VMEM] * 3,
        compiler_params=ROOM,
        cost_estimate=cost(10),
        name="dense_grads",
    )(*[member for group in saved for member in group])


def project_grads_kernel(seqs, tok, *refs):
    fgs, refs = refs[:seqs], refs[seqs:]
    dqs, refs = refs[:seqs], refs[seqs:]
    dkvs, refs = refs[:seqs], refs[seqs:]
    wq, wk, wv, first, second, tg, grads, sums, full, sems = refs
    rows, width = tok.shape[1:]
    per = width // GROUPS
    heads = per // DH
    quarter = wq.shape[0] // 2
    copies = []
    for i, own in enumerate((wq, wk, wv)):
        part = pl.ds(i * quarter, quarter)
        copies += weight_copies(full.at[i], own, first.at[part], second.at[part], sems, 3 * i)
    for copy in copies:
        copy.start()
    dq = jnp.concatenate(
        [jnp.concatenate([dqs[s][g] for g in range(GROUPS)], 1) for s in range(seqs)], 0
    )
    pair = [
        jnp.concatenate([dkvs[s][g] for g in range(GROUPS)], 1) for s in range(seqs)
    ]
    pair = jnp.concatenate(pair, 0)
    halves = [
        jnp.concatenate(
            [
                pair[:, n * 128 + part * DH : n * 128 + (part + 1) * DH]
                for n in range(GROUPS * heads)
            ],
            1,
        )
        for part in (0, 1)
    ]
    flat = tok[...].reshape(seqs * rows, width)
    for copy in copies:
        copy.wait()
    total = jnp.concatenate([fgs[s][...] for s in range(seqs)], 0)
    for i, grad in enumerate((dq, *halves)):
        total += dot(grad, full[i], NT)
        found = dot(flat, grad, TN).astype(BF16)
        for n in range(4):
            grads[n, i * quarter : (i + 1) * quarter, :] = found[n * quarter : (n + 1) * quarter]
    tg[...] = total.reshape(seqs, rows, width)
    sums[0:1, :] = jnp.sum(dq.astype(F32), 0, keepdims=True)
    sums[1:2, :] = jnp.sum(halves[1].astype(F32), 0, keepdims=True)
    sums[2:8, :] = jnp.zeros((6, width), F32)


def project_grads(tok, fgs, dqs, dkvs, wq, wk, wv, first, second):
    seqs, rows, width = tok.shape
    return pl.pallas_call(
        functools.partial(project_grads_kernel, seqs),
        out_shape=[
            jax.ShapeDtypeStruct(tok.shape, F32),
            jax.ShapeDtypeStruct((4, 3 * (width // 4), width), BF16),
            jax.ShapeDtypeStruct((8, width), F32),
        ],
        in_specs=[VMEM] * (1 + 3 * seqs) + [ANY] * 5,
        out_specs=[VMEM] * 3,
        scratch_shapes=[pltpu.VMEM((3, width, width), BF16), pltpu.SemaphoreType.DMA((9,))],
        compiler_params=ROOM,
        cost_estimate=cost(10),
        name="project_grads",
    )(tok, *fgs, *dqs, *dkvs, wq, wk, wv, first, second)


def pick(table, index):
    places = jnp.arange(table.shape[0], dtype=jnp.int32)
    return jnp.sum(jnp.where(index[..., None] == places, table, 0), -1)


def shards(
    size,
    tokens,
    teacher,
    lengths,
    block_order,
    query_weight,
    query_bias,
    key_weight,
    value_weight,
    value_bias,
    out_weight,
    out_bias,
    gain_one,
    shift_one,
    inner_weight,
    inner_bias,
    outer_weight,
    outer_bias,
    gain_two,
    shift_two,
):
    seqs, rows, width = tokens.shape
    per_plane = size // GROUPS
    blocks_each = rows // BLK
    ctx, x = lax.axis_index("ctx"), lax.axis_index("wa")
    c, place = lax.rem(ctx, 2), lax.rem(ctx, per_plane)
    masks = [1 << b for b in reversed(range(per_plane.bit_length() - 1))]
    offsets = [0]
    for m in masks:
        offsets += [o ^ m for o in offsets]

    def across(value):
        return lax.ppermute(value, "wa", [(0, 1), (1, 0)])

    def flip(value, m):
        return lax.ppermute(value, "ctx", [(i, i ^ m) for i in range(size)])

    lines = [[g * per_plane + r for g in range(GROUPS)] for r in range(per_plane)]

    def turn(value):
        return lax.all_to_all(value, "ctx", 0, 0, axis_index_groups=lines)

    vectors = (
        query_bias,
        value_bias,
        out_bias,
        gain_one,
        shift_one,
        outer_bias,
        gain_two,
        shift_two,
        inner_bias,
    )
    own_vec = jnp.concatenate(vectors)[None]
    other_vec = across(own_vec)
    pair = jnp.where(
        x == 0, jnp.stack([own_vec, other_vec]), jnp.stack([other_vec, own_vec])
    ).astype(F32)
    half = width // 2
    narrow = pair[:, 0, : 8 * half].reshape(2, 8, half).swapaxes(0, 1).reshape(8, width)
    wide_vec = pair[:, 0, 8 * half :].reshape(1, -1)

    def quarter(weight):
        n = weight.shape[0] // 2
        return lax.dynamic_slice_in_dim(weight, c * n, n, 0)

    first_qkv = across(
        jnp.concatenate([quarter(w) for w in (query_weight, key_weight, value_weight)], 0)
    )
    second_qkv = flip(first_qkv, 1)
    dense_weights = []
    last = first_qkv
    for weight in (out_weight, inner_weight, outer_weight):
        piece, last = lax.optimization_barrier((quarter(weight), last))
        last = across(piece)
        dense_weights += [weight, last, flip(last, 1)]

    count = block_order.shape[0]
    ids = jnp.arange(count, dtype=jnp.int32)
    owner = ids // blocks_each
    index_of = jnp.array([offsets.index(o) for o in range(per_plane)], jnp.int32)
    piece_of = pick(index_of, (owner % per_plane) ^ place)
    spot = (piece_of * GROUPS + owner // per_plane) * blocks_each + ids % blocks_each
    key_order = jnp.sum(jnp.where(block_order[None, :] == ids[:, None], spot[None, :], 0), 1)
    near = jnp.arange(GROUPS * blocks_each, dtype=jnp.int32)
    near_ids = (near // blocks_each * per_plane + place) * blocks_each + near % blocks_each
    near_pos = pick(block_order, near_ids)
    rank = jnp.sum((near_pos[None, :] < near_pos[:, None]).astype(jnp.int32), 1)
    query_order = jnp.sum(jnp.where(rank[None, :] == near[:, None], near[None, :], 0), 1)
    own_pos = pick(block_order, ctx * blocks_each + jnp.arange(blocks_each, dtype=jnp.int32))
    scalars, row_counts = [], []
    for s in range(seqs):
        used = jnp.sum((near_pos * BLK < lengths[s]).astype(jnp.int32))
        head = jnp.concatenate([lengths[s][None], used[None], jnp.zeros((6,), jnp.int32)])
        scalars.append(jnp.concatenate([head, query_order, key_order]))
        row_counts.append(jnp.clip(lengths[s] - own_pos * BLK, 0, BLK))

    projected = project(
        tokens, narrow, query_weight, key_weight, value_weight, first_qkv, second_qkv
    )
    queries, pieces = [], []
    for s in range(seqs):
        kv = turn(projected[2 * s + 1])
        queries.append(turn(projected[2 * s]).reshape(-1, BLK, width // GROUPS))
        held = [kv.reshape(-1, BLK, kv.shape[2])]
        for m in masks:
            held += [flip(piece, m) for piece in held]
        pieces.append(held)

    attended, lses, dense_out = [], [], []
    for s in range(seqs):
        o, lse = attend(scalars[s], queries[s], pieces[s])
        attended.append(o.reshape(queries[s].shape))
        lses.append(lse)
    for s in range(seqs):
        o4 = turn(attended[s].reshape(GROUPS, rows, -1))
        dense_out.append(
            dense(
                row_counts[s], o4, tokens[s], teacher[s], narrow[2:], wide_vec, dense_weights
            )
        )
    saved = [d[3:9] for d in dense_out]
    heads_grad = [turn(d[2]).reshape(queries[s].shape) for s, d in enumerate(dense_out)]
    g_dense = dense_grads(saved)

    dqs, dkvs = [], []
    for s in range(seqs):
        found = attend_back(
            scalars[s], queries[s], heads_grad[s], attended[s], lses[s], pieces[s]
        )
        dqs.append(turn(found[0].reshape(GROUPS, rows, -1)))
        held = list(found[1:])
        for m in reversed(masks):
            n = len(held) // 2
            held = [
                (mine.astype(F32) + flip(theirs, m).astype(F32)).astype(BF16)
                for mine, theirs in zip(held[:n], held[n:])
            ]
        dkvs.append(turn(held[0].reshape(GROUPS, rows, -1)))
    tokens_grad, g_qkv, sums_qkv = project_grads(
        tokens,
        [d[1] for d in dense_out],
        dqs,
        dkvs,
        query_weight,
        key_weight,
        value_weight,
        first_qkv,
        second_qkv,
    )

    cores = [[i for i in range(size) if i % 2 == k] for k in range(2)]

    def reduced(grad):
        four = grad.reshape(2, 2, *grad.shape[1:])
        keep = lax.dynamic_index_in_dim(four, c, 1, False)
        send = lax.dynamic_index_in_dim(four, 1 - c, 1, False)
        keep = (keep.astype(F32) + flip(send, 1).astype(F32)).astype(BF16)
        mine = lax.dynamic_index_in_dim(keep, x, 0, False)
        theirs = across(lax.dynamic_index_in_dim(keep, 1 - x, 0, False))
        mine = (mine.astype(F32) + theirs.astype(F32)).astype(BF16)
        mine = lax.psum(mine, "ctx", axis_index_groups=cores)
        sibling = flip(mine, 1)
        return jnp.where(c == 0, jnp.stack([mine, sibling]), jnp.stack([sibling, mine]))

    out_grad, inner_grad, outer_grad = (
        reduced(g).reshape(-1, g.shape[2]).astype(F32) for g in g_dense
    )
    qkv = reduced(g_qkv).reshape(2, 3, width // 4, width).astype(F32)
    query_grad, key_grad, value_grad = (qkv[:, i].reshape(half, width) for i in range(3))

    sums = sum(d[9] for d in dense_out)
    wide_sums = sum(d[10] for d in dense_out)
    loss_part = jnp.sum(sums[6])
    valid = sum(jnp.sum(r) for r in row_counts).astype(F32)
    small = jnp.concatenate(
        [sums[:6].reshape(-1), sums_qkv[:2].reshape(-1), wide_sums[0], jnp.stack([loss_part, valid])]
    )
    small = lax.psum(small, ("ctx", "wa"))

    def vector(start, length):
        return lax.dynamic_slice_in_dim(small, start + x * (length // 2), length // 2, 0)

    end = 8 * width
    hidden = wide_vec.shape[1]
    loss = small[end + hidden] / (small[end + hidden + 1] * width)
    return (
        jnp.stack([d[0] for d in dense_out]),
        tokens_grad,
        query_grad,
        vector(6 * width, width),
        key_grad,
        value_grad,
        vector(7 * width, width),
        out_grad,
        vector(5 * width, width),
        vector(3 * width, width),
        vector(4 * width, width),
        inner_grad,
        vector(end, hidden),
        outer_grad,
        vector(2 * width, width),
        vector(0, width),
        vector(width, width),
        loss,
    )


def solution(mesh):
    row, split, both = P("wa"), P("wa", None), P("wa", "ctx", None)
    placed = (both, both, row, P(), split, row, split, split, row, split, row, row, row)
    placed += (split, row, split, row, row, row)
    return jax.shard_map(
        functools.partial(shards, mesh.shape["ctx"]),
        mesh=mesh,
        in_specs=placed,
        out_specs=(
            both,
            both,
            split,
            row,
            split,
            split,
            row,
            split,
            row,
            row,
            row,
            split,
            row,
            split,
            row,
            row,
            row,
            P(),
        ),
        check_vma=False,
    )
```

```python
import functools
import math

import jax
import jax.numpy as jnp
from jax import lax
from jax.experimental import pallas as pl
from jax.experimental.pallas import tpu as pltpu
from jax.sharding import PartitionSpec as P

DH = 64
BLK = 128
GROUPS = 4
LN2 = math.log(2.0)
NT = (((1,), (1,)), ((), ()))
NN = (((1,), (0,)), ((), ()))
TN = (((0,), (0,)), ((), ()))
F32 = jnp.float32
BF16 = jnp.bfloat16
VMEM = pl.BlockSpec(memory_space=pltpu.VMEM)
SMEM = pl.BlockSpec(memory_space=pltpu.SMEM)
ANY = pl.BlockSpec(memory_space=pl.ANY)
ROOM = pltpu.CompilerParams(vmem_limit_bytes=58 * 2**20)


def dot(left, right, dims=NN):
    return lax.dot_general(left, right, dims, preferred_element_type=F32)


def cost(us):
    return pl.CostEstimate(flops=int(us * 1.15e9), bytes_accessed=1 << 20, transcendentals=0)


def weight_copies(full, own, first, second, sems, base):
    x, c = lax.axis_index("wa"), lax.rem(lax.axis_index("ctx"), 2)
    half = own.shape[0]
    quarter = half // 2
    other = (1 - x) * half
    places = (
        (own, x * half, half),
        (first, other + c * quarter, quarter),
        (second, other + (1 - c) * quarter, quarter),
    )
    return [
        pltpu.make_async_copy(
            src, full.at[pl.ds(pl.multiple_of(start, quarter), size)], sems.at[base + i]
        )
        for i, (src, start, size) in enumerate(places)
    ]


def project_kernel(tok, vec, wq, wk, wv, first, second, *rest):
    seqs, rows, width = tok.shape
    outs, (full, sems) = rest[: 2 * seqs], rest[2 * seqs :]
    quarter = wq.shape[0] // 2
    copies = []
    for i, own in enumerate((wq, wk, wv)):
        part = pl.ds(i * quarter, quarter)
        copies.append(
            weight_copies(full.at[i], own, first.at[part], second.at[part], sems, 3 * i)
        )
    for group in copies:
        for copy in group:
            copy.start()
    flat = tok[...].reshape(seqs * rows, width)
    per = width // GROUPS
    heads = per // DH
    for copy in copies[1]:
        copy.wait()
    keys = dot(flat, full[1]).astype(BF16)
    for copy in copies[2]:
        copy.wait()
    values = (dot(flat, full[2]) + vec[1:2, :]).astype(BF16)
    for s in range(seqs):
        rs = slice(s * rows, (s + 1) * rows)
        for g in range(GROUPS):
            for h in range(heads):
                cols = slice(g * per + h * DH, g * per + (h + 1) * DH)
                outs[2 * s + 1][g, :, h * 128 : (h + 1) * 128] = jnp.concatenate(
                    [keys[rs, cols], values[rs, cols]], 1
                )
    for copy in copies[0]:
        copy.wait()
    queries = ((dot(flat, full[0]) + vec[0:1, :]) * (DH**-0.5 / LN2)).astype(BF16)
    for s in range(seqs):
        rs = slice(s * rows, (s + 1) * rows)
        for g in range(GROUPS):
            outs[2 * s][g] = queries[rs, g * per : (g + 1) * per]


def project(tok, vec, wq, wk, wv, first, second):
    seqs, rows, width = tok.shape
    per = width // GROUPS
    shapes = [
        jax.ShapeDtypeStruct((GROUPS, rows, n), BF16) for _ in range(seqs) for n in (per, 2 * per)
    ]
    return pl.pallas_call(
        project_kernel,
        out_shape=shapes,
        in_specs=[VMEM, VMEM] + [ANY] * 5,
        out_specs=[VMEM] * len(shapes),
        scratch_shapes=[pltpu.VMEM((3, width, width), BF16), pltpu.SemaphoreType.DMA((9,))],
        compiler_params=ROOM,
        cost_estimate=cost(5),
        name="project",
    )(tok, vec, wq, wk, wv, first, second)


def load_pieces(pieces, kv, sems):
    per = pieces[0].shape[0]
    copies = [
        pltpu.make_async_copy(piece, kv.at[pl.ds(i * per, per)], sems.at[i])
        for i, piece in enumerate(pieces)
    ]
    for copy in copies:
        copy.start()
    for copy in copies:
        copy.wait()


def forward_kernel(wide, narrow, count, sc, q_ref, *rest):
    pieces, (o_ref, lse_ref, kv_ref, qa, acc, sums, sems) = rest[:count], rest[count:]
    blocks = q_ref.shape[0]
    heads = q_ref.shape[2] // DH
    rows = blocks * BLK
    length = sc[0]
    load_pieces(pieces, kv_ref, sems)

    def gather(h, start, n):
        return jnp.concatenate(
            [kv_ref[sc[8 + blocks + start + i], :, h * 128 : (h + 1) * 128] for i in range(n)], 0
        )

    whole = length // (wide * BLK)
    tail = whole * wide
    tails = (length - tail * BLK + narrow * BLK - 1) // (narrow * BLK)
    for h in range(heads):
        hs = slice(h * DH, (h + 1) * DH)
        own = jnp.concatenate([q_ref[b, :, hs] for b in range(blocks)], 0)
        qa[...] = jnp.concatenate([own, jnp.zeros_like(own)], 1)
        acc[...] = jnp.zeros_like(acc)
        sums[...] = jnp.zeros_like(sums)

        def step(start, n, masked, h=h):
            kv = gather(h, start, n)
            scores = dot(qa[...], kv, NT)
            if masked:
                place = lax.broadcasted_iota(jnp.int32, scores.shape, 1) + start * BLK
                scores = jnp.where(place < length, scores, -1e30)
            p = jnp.exp2(scores)
            sums[...] += sum(p[:, i * 128 : (i + 1) * 128] for i in range(n))
            acc[...] += dot(p.astype(BF16), kv)

        def wide_step(j, _, step=step):
            step(j * wide, wide, False)
            return 0

        def narrow_step(j, _, step=step):
            step(tail + j * narrow, narrow, True)
            return 0

        lax.fori_loop(0, whole, wide_step, 0)
        lax.fori_loop(0, tails, narrow_step, 0)
        total = jnp.sum(sums[...], 1, keepdims=True)
        across = jnp.transpose(jnp.broadcast_to(total, (rows, 128)))[:8]
        good = (jnp.min(across) > 2.0**-80) & (jnp.max(across) < 2.0**100)

        @pl.when(good)
        def _(h=h, hs=hs, total=total, across=across):
            lse_ref[h] = jnp.log2(across)
            o_ref[:, hs] = (acc[:, DH:] * (1.0 / total)).astype(BF16)

        @pl.when(jnp.logical_not(good))
        def _(h=h, hs=hs):
            key_blocks = (length + BLK - 1) // BLK

            def rows_step(t, _):
                part = pl.ds(pl.multiple_of(t * BLK, BLK), BLK)
                q = qa[part, :]

                def scores_of(j):
                    kv = gather(h, j, 1)
                    scores = dot(q, kv, NT)
                    place = lax.broadcasted_iota(jnp.int32, scores.shape, 1) + j * BLK
                    return kv, jnp.where(place < length, scores, -1e30)

                largest = lax.fori_loop(
                    0,
                    key_blocks,
                    lambda j, m: jnp.maximum(m, jnp.max(scores_of(j)[1], 1, keepdims=True)),
                    jnp.full((BLK, 1), -1e30, F32),
                )
                acc[part, :] = jnp.zeros((BLK, 128), F32)
                sums[part, :] = jnp.zeros((BLK, 128), F32)

                def add(j, _):
                    kv, scores = scores_of(j)
                    p = jnp.exp2(scores - largest)
                    sums[part, :] += p
                    acc[part, :] += dot(p.astype(BF16), kv)
                    return 0

                lax.fori_loop(0, key_blocks, add, 0)
                row_total = jnp.sum(sums[part, :], 1, keepdims=True)
                lse = largest + jnp.log2(row_total)
                lse_ref[h, :, part] = jnp.transpose(jnp.broadcast_to(lse, (BLK, 128)))[:8]
                o_ref[part, hs] = (acc[part, :][:, DH:] * (1.0 / row_total)).astype(BF16)
                return 0

            lax.fori_loop(0, rows // BLK, rows_step, 0)


def attend(sc, q, pieces):
    blocks, _, per = q.shape
    rows, heads = blocks * BLK, per // DH
    key_blocks = len(pieces) * pieces[0].shape[0]
    return pl.pallas_call(
        functools.partial(forward_kernel, 8, 2, len(pieces)),
        out_shape=(
            jax.ShapeDtypeStruct((rows, per), BF16),
            jax.ShapeDtypeStruct((heads, 8, rows), F32),
        ),
        in_specs=[SMEM, VMEM] + [ANY] * len(pieces),
        out_specs=(VMEM, VMEM),
        scratch_shapes=[
            pltpu.VMEM((key_blocks, BLK, 2 * per), BF16),
            pltpu.VMEM((rows, 128), BF16),
            pltpu.VMEM((rows, 128), F32),
            pltpu.VMEM((rows, 128), F32),
            pltpu.SemaphoreType.DMA((len(pieces),)),
        ],
        compiler_params=ROOM,
        cost_estimate=cost(20),
        name="attend",
    )(sc, q, *pieces)


def backward_kernel(qn, kn, count, sc, q_ref, do_ref, o_ref, lse_ref, *rest):
    pieces, dq_ref, outs = rest[:count], rest[count], rest[count + 1 : 2 * count + 1]
    kv_ref, both, dkv, dq, lse_row, delta_row, sems = rest[2 * count + 1 :]
    blocks = q_ref.shape[0]
    heads = q_ref.shape[2] // DH
    key_blocks = kv_ref.shape[0]
    tile = qn * BLK
    length, used = sc[0], sc[1]
    whole = length // (kn * BLK)
    parts = (length + kn * BLK - 1) // (kn * BLK)
    tiles = (used + qn - 1) // qn
    ones = jnp.ones((8, DH), BF16)
    load_pieces(pieces, kv_ref, sems)
    for h in range(heads):
        hs = slice(h * DH, (h + 1) * DH)

        def clear(i, _):
            dkv[pl.ds(pl.multiple_of(i * 1024, 1024), 1024), :] = jnp.zeros((1024, 128), F32)
            return 0

        lax.fori_loop(0, key_blocks // 8, clear, 0)
        dq[...] = jnp.zeros_like(dq)

        def prepare(t, _, h=h, hs=hs):
            base = pl.multiple_of(t * (2 * tile), 2 * tile)
            start = pl.multiple_of(t * tile, tile)
            places = [sc[8 + t * qn + i] for i in range(qn)]
            q = jnp.concatenate([q_ref[s, :, hs] for s in places], 0)
            do = jnp.concatenate([do_ref[s, :, hs] for s in places], 0)
            o = jnp.concatenate([o_ref[s, :, hs] for s in places], 0)
            zero = jnp.zeros_like(q)
            both[pl.ds(base, tile), :] = jnp.concatenate([q, zero], 1)
            both[pl.ds(base + tile, tile), :] = jnp.concatenate([zero, do], 1)
            product = do.astype(F32) * o.astype(F32)
            high = product.astype(BF16)
            rest_of = (product - high.astype(F32)).astype(BF16)
            delta_row[:, pl.ds(start, tile)] = dot(ones, high, NT) + dot(ones, rest_of, NT)
            lse_row[:, pl.ds(start, tile)] = jnp.concatenate(
                [lse_ref[h, :, pl.ds(pl.multiple_of(s * BLK, BLK), BLK)] for s in places], 1
            )
            return 0

        lax.fori_loop(0, tiles, prepare, 0)

        def rows_step(t, _, h=h):
            base = pl.multiple_of(t * (2 * tile), 2 * tile)
            span = pl.ds(pl.multiple_of(t * tile, tile), tile)

            def step(j, masked):
                places = [sc[8 + blocks + j * kn + i] for i in range(kn)]
                kv = jnp.concatenate([kv_ref[s, :, h * 128 : (h + 1) * 128] for s in places], 0)
                b = both[pl.ds(base, 2 * tile), :]
                found = dot(kv, b, NT)
                p = jnp.exp2(found[:, :tile] - lse_row[:1, span])
                if masked:
                    place = lax.broadcasted_iota(jnp.int32, p.shape, 0) + j * (kn * BLK)
                    p = jnp.where(place < length, p, 0.0)
                ds = (p * (found[:, tile:] - delta_row[:1, span])).astype(BF16)
                grads = dot(jnp.concatenate([ds, p.astype(BF16)], 1), b)
                for i, s in enumerate(places):
                    dkv[pl.ds(pl.multiple_of(s * BLK, BLK), BLK), :] += grads[
                        i * BLK : (i + 1) * BLK
                    ]
                dq[span, :] += dot(ds, kv, TN)

            def whole_step(j, _):
                step(j, False)
                return 0

            lax.fori_loop(0, whole, whole_step, 0)

            @pl.when(parts > whole)
            def _():
                step(whole, True)

            return 0

        lax.fori_loop(0, tiles, rows_step, 0)
        for i in range(blocks):
            dq_ref[sc[8 + i], :, hs] = (
                dq[i * BLK : (i + 1) * BLK, :DH] * DH**-0.5
            ).astype(BF16)
        level = jnp.where(lax.broadcasted_iota(jnp.int32, (1, 128), 1) < DH, LN2, 1.0)
        per_piece = key_blocks // count
        for n, out in enumerate(outs):
            for i in range(per_piece):
                b = n * per_piece + i
                out[i, :, h * 128 : (h + 1) * 128] = (
                    dkv[b * BLK : (b + 1) * BLK, :] * level
                ).astype(BF16)


def attend_back(sc, q, do, o, lse, pieces):
    blocks, _, per = q.shape
    rows = blocks * BLK
    key_blocks = len(pieces) * pieces[0].shape[0]
    return pl.pallas_call(
        functools.partial(backward_kernel, 4, 4, len(pieces)),
        out_shape=[jax.ShapeDtypeStruct(q.shape, BF16)]
        + [jax.ShapeDtypeStruct(p.shape, BF16) for p in pieces],
        in_specs=[SMEM] + [VMEM] * 4 + [ANY] * len(pieces),
        out_specs=[VMEM] * (1 + len(pieces)),
        scratch_shapes=[
            pltpu.VMEM((key_blocks, BLK, 2 * per), BF16),
            pltpu.VMEM((2 * rows, 128), BF16),
            pltpu.VMEM((key_blocks * BLK, 128), F32),
            pltpu.VMEM((rows, 128), F32),
            pltpu.VMEM((8, rows), F32),
            pltpu.VMEM((8, rows), F32),
            pltpu.SemaphoreType.DMA((len(pieces),)),
        ],
        compiler_params=ROOM,
        cost_estimate=cost(45),
        name="attend_back",
    )(sc, q, do, o, lse, *pieces)


def norm(values):
    centered = values - jnp.mean(values, -1, keepdims=True)
    inverse = lax.rsqrt(jnp.mean(centered * centered, -1, keepdims=True) + 1e-6)
    return centered * inverse, inverse


def norm_back(upstream, normed, inverse):
    return inverse * (
        upstream
        - jnp.mean(upstream, -1, keepdims=True)
        - normed * jnp.mean(upstream * normed, -1, keepdims=True)
    )


def normal_parts(x):
    z = jnp.abs(x) * (0.5**0.5)
    bell = jnp.exp(-0.5 * x * x)
    t = 1.0 / (1.0 + 0.3275911 * z)
    poly = t * (
        0.254829592
        + t * (-0.284496736 + t * (1.421413741 + t * (-1.453152027 + t * 1.061405429)))
    )
    upper = 0.5 * poly * bell
    return jnp.where(x >= 0, 1.0 - upper, upper), bell * (2.0 * math.pi) ** -0.5


def dense_kernel(sc, att4, tok, teach, vec, wide_vec, *rest):
    weights, rest = rest[:9], rest[9:]
    outs, (wo, wi, wu, slope, sems) = rest[:11], rest[11:]
    out, fg, ag, att_o, br_o, hl_o, il_o, act_o, ol_o, sums, wide_sums = outs
    rows, width = tok.shape
    hidden = wi.shape[1]
    tile = 512
    copies = [
        weight_copies(full, *weights[3 * i : 3 * i + 3], sems, 3 * i)
        for i, full in enumerate((wo, wi, wu))
    ]
    for group in copies:
        for copy in group:
            copy.start()
    per = att4.shape[2]
    att = jnp.concatenate([att4[g] for g in range(GROUPS)], 1)
    att_o[...] = att
    row = lax.broadcasted_iota(jnp.int32, (rows, 1), 0)
    mask = jnp.where(
        row < BLK, jnp.where(row < sc[0], 1.0, 0.0), jnp.where(row - BLK < sc[1], 1.0, 0.0)
    )
    out_bias, gain_one, shift_one = vec[0:1, :], vec[1:2, :], vec[2:3, :]
    outer_bias, gain_two, shift_two = vec[3:4, :], vec[4:5, :], vec[5:6, :]
    for copy in copies[0]:
        copy.wait()
    first = tok[...].astype(F32) + dot(att, wo[...]) + out_bias
    normed_one, inverse_one = norm(first)
    hidden_in = normed_one * gain_one + shift_one
    hl = hidden_in.astype(BF16)
    hl_o[...] = hl
    for copy in copies[1] + copies[2]:
        copy.wait()
    second = hidden_in + outer_bias
    for n in range(hidden // tile):
        cols = slice(n * tile, (n + 1) * tile)
        inner = dot(hl, wi[:, cols]) + wide_vec[0:1, cols]
        below, density = normal_parts(inner)
        act = (inner * below).astype(BF16)
        act_o[:, cols] = act
        slope[:, cols] = below + inner * density
        second += dot(act, wu[cols, :])
    normed_two, inverse_two = norm(second)
    final = normed_two * gain_two + shift_two
    out[...] = final.astype(BF16)
    residue = (final - teach[...].astype(F32)) * mask
    add = functools.partial(jnp.sum, axis=0, keepdims=True)
    second_grad = norm_back(residue * gain_two, normed_two, inverse_two)
    ol = second_grad.astype(BF16)
    ol_o[...] = ol
    hidden_grad = second_grad
    for n in range(hidden // tile):
        cols = slice(n * tile, (n + 1) * tile)
        il = (dot(ol, wu[cols, :], NT) * slope[:, cols]).astype(BF16)
        il_o[:, cols] = il
        wide_sums[0:1, cols] = add(il.astype(F32))
        hidden_grad += dot(il, wi[:, cols], NT)
    first_grad = norm_back(hidden_grad * gain_one, normed_one, inverse_one)
    fg[...] = first_grad
    br = first_grad.astype(BF16)
    br_o[...] = br
    att_grad = dot(br, wo[...], NT).astype(BF16)
    for g in range(GROUPS):
        ag[g] = att_grad[:, g * per : (g + 1) * per]
    sums[0:1, :] = add(residue * normed_two)
    sums[1:2, :] = add(residue)
    sums[2:3, :] = add(ol.astype(F32))
    sums[3:4, :] = add(hidden_grad * normed_one)
    sums[4:5, :] = add(hidden_grad)
    sums[5:6, :] = add(br.astype(F32))
    sums[6:7, :] = add(residue * residue)
    sums[7:8, :] = jnp.zeros((1, width), F32)


def dense(sc, att4, tok, teach, vec, wide_vec, weights):
    rows, width = tok.shape
    hidden = wide_vec.shape[1]
    narrow = jax.ShapeDtypeStruct((rows, width), BF16)
    wide = jax.ShapeDtypeStruct((rows, hidden), BF16)
    return pl.pallas_call(
        dense_kernel,
        out_shape=[
            narrow,
            jax.ShapeDtypeStruct((rows, width), F32),
            jax.ShapeDtypeStruct(att4.shape, BF16),
            narrow,
            narrow,
            narrow,
            wide,
            wide,
            narrow,
            jax.ShapeDtypeStruct((8, width), F32),
            jax.ShapeDtypeStruct((1, hidden), F32),
        ],
        in_specs=[SMEM] + [VMEM] * 5 + [ANY] * 9,
        out_specs=[VMEM] * 11,
        scratch_shapes=[
            pltpu.VMEM((width, width), BF16),
            pltpu.VMEM((width, hidden), BF16),
            pltpu.VMEM((hidden, width), BF16),
            pltpu.VMEM((rows, hidden), F32),
            pltpu.SemaphoreType.DMA((9,)),
        ],
        compiler_params=ROOM,
        cost_estimate=cost(15),
        name="dense",
    )(sc, att4, tok, teach, vec, wide_vec, *weights)


def dense_grads_kernel(seqs, *refs):
    ins, (g_out, g_inner, g_outer) = refs[: 6 * seqs], refs[6 * seqs :]
    att, br, hl, il, act, ol = (
        jnp.concatenate([ins[6 * s + i][...] for s in range(seqs)], 0) for i in range(6)
    )
    for target, left, right in ((g_out, att, br), (g_inner, hl, il), (g_outer, act, ol)):
        rows = target.shape[1]
        for n in range(4):
            piece = left[:, n * rows : (n + 1) * rows]
            for t in range(right.shape[1] // 768):
                cols = slice(t * 768, (t + 1) * 768)
                target[n, :, cols] = dot(piece, right[:, cols], TN).astype(BF16)


def dense_grads(saved):
    seqs = len(saved)
    width, hidden = saved[0][0].shape[1], saved[0][3].shape[1]
    return pl.pallas_call(
        functools.partial(dense_grads_kernel, seqs),
        out_shape=[
            jax.ShapeDtypeStruct((4, width // 4, width), BF16),
            jax.ShapeDtypeStruct((4, width // 4, hidden), BF16),
            jax.ShapeDtypeStruct((4, hidden // 4, width), BF16),
        ],
        in_specs=[VMEM] * (6 * seqs),
        out_specs=[VMEM] * 3,
        compiler_params=ROOM,
        cost_estimate=cost(10),
        name="dense_grads",
    )(*[member for group in saved for member in group])


def project_grads_kernel(seqs, tok, *refs):
    fgs, refs = refs[:seqs], refs[seqs:]
    dqs, refs = refs[:seqs], refs[seqs:]
    dkvs, refs = refs[:seqs], refs[seqs:]
    wq, wk, wv, first, second, tg, grads, sums, full, sems = refs
    rows, width = tok.shape[1:]
    per = width // GROUPS
    heads = per // DH
    quarter = wq.shape[0] // 2
    copies = []
    for i, own in enumerate((wq, wk, wv)):
        part = pl.ds(i * quarter, quarter)
        copies += weight_copies(full.at[i], own, first.at[part], second.at[part], sems, 3 * i)
    for copy in copies:
        copy.start()
    dq = jnp.concatenate(
        [jnp.concatenate([dqs[s][g] for g in range(GROUPS)], 1) for s in range(seqs)], 0
    )
    pair = [
        jnp.concatenate([dkvs[s][g] for g in range(GROUPS)], 1) for s in range(seqs)
    ]
    pair = jnp.concatenate(pair, 0)
    halves = [
        jnp.concatenate(
            [
                pair[:, n * 128 + part * DH : n * 128 + (part + 1) * DH]
                for n in range(GROUPS * heads)
            ],
            1,
        )
        for part in (0, 1)
    ]
    flat = tok[...].reshape(seqs * rows, width)
    for copy in copies:
        copy.wait()
    total = jnp.concatenate([fgs[s][...] for s in range(seqs)], 0)
    for i, grad in enumerate((dq, *halves)):
        total += dot(grad, full[i], NT)
        found = dot(flat, grad, TN).astype(BF16)
        half = width // 2
        for n in range(2):
            for t in range(width // 128):
                grads[t % 3, t // 3, n, i * half : (i + 1) * half, :] = found[
                    n * half : (n + 1) * half, t * 128 : (t + 1) * 128
                ]
    tg[...] = total.reshape(seqs, rows, width)
    sums[0:1, :] = jnp.sum(dq.astype(F32), 0, keepdims=True)
    sums[1:2, :] = jnp.sum(halves[1].astype(F32), 0, keepdims=True)
    sums[2:8, :] = jnp.zeros((6, width), F32)


def project_grads(tok, fgs, dqs, dkvs, wq, wk, wv, first, second):
    seqs, rows, width = tok.shape
    return pl.pallas_call(
        functools.partial(project_grads_kernel, seqs),
        out_shape=[
            jax.ShapeDtypeStruct(tok.shape, F32),
            jax.ShapeDtypeStruct((3, 2, 2, 3 * (width // 2), 128), BF16),
            jax.ShapeDtypeStruct((8, width), F32),
        ],
        in_specs=[VMEM] * (1 + 3 * seqs) + [ANY] * 5,
        out_specs=[VMEM] * 3,
        scratch_shapes=[pltpu.VMEM((3, width, width), BF16), pltpu.SemaphoreType.DMA((9,))],
        compiler_params=ROOM,
        cost_estimate=cost(10),
        name="project_grads",
    )(tok, *fgs, *dqs, *dkvs, wq, wk, wv, first, second)


MESH = pl.DeviceIdType.MESH


def position():
    ctx = lax.axis_index("ctx")
    return ctx // 4, lax.rem(ctx // 2, 2), lax.rem(ctx, 2), lax.axis_index("wa")


def device(z, y, c, x):
    return z * 4 + y * 2 + c, x


def greet(others):
    barrier = pltpu.get_barrier_semaphore()
    for other in others:
        pl.semaphore_signal(barrier, inc=1, device_id=other, device_id_type=MESH)
    pl.semaphore_wait(barrier, len(others))


def send(src, dst, sems, to):
    copy = pltpu.make_async_remote_copy(
        src_ref=src,
        dst_ref=dst,
        send_sem=sems[0],
        recv_sem=sems[1],
        device_id=to,
        device_id_type=MESH,
    )
    copy.start()
    return copy


def add_low(left, right):
    return (left.astype(F32) + right.astype(F32)).astype(BF16)


def return_kernel(seqs, *refs):
    ins, outs = refs[: 5 * seqs], refs[5 * seqs : 7 * seqs]
    held, from_core, from_y, local_sem, q_sem, c_sem, y_sem, z_sem = refs[7 * seqs :]
    z, y, c, x = position()
    sibling, beside = device(z, y, 1 - c, x), device(z, 1 - y, c, x)
    line = [None] + [device(z ^ d, y, c, x) for d in range(1, GROUPS)]
    greet([sibling, beside] + line[1:])
    waits = []
    for s in range(seqs):
        for d in range(1, GROUPS):
            sems = q_sem.at[0, s, d], q_sem.at[1, s, d]
            waits.append(send(ins[5 * s].at[z ^ d], outs[2 * s].at[z], sems, line[d]))
    core = {}
    for s in range(seqs):
        for d in range(GROUPS):
            for i in (1, 0):
                sems = c_sem.at[0, s, d, i], c_sem.at[1, s, d, i]
                core[s, d, i] = send(
                    ins[5 * s + 3 + i].at[z ^ d], from_core.at[s, i, z ^ d], sems, sibling
                )
    local = {}
    for s in range(seqs):
        for i in (1, 0):
            local[s, i] = pltpu.make_async_copy(
                ins[5 * s + 1 + i], held.at[s, i], local_sem.at[s, i]
            )
            local[s, i].start()
        own = pltpu.make_async_copy(ins[5 * s].at[z], outs[2 * s].at[z], local_sem.at[s, 2])
        own.start()
        waits.append(own)
    order = [1, 2, 3, 0]
    to_y = {}
    for s in range(seqs):
        local[s, 1].wait()
        local[s, 0].wait()
        for d in order:
            core[s, d, 1].wait()
            held[s, 1, z ^ d] = add_low(held[s, 1, z ^ d], from_core[s, 1, z ^ d])
            sems = y_sem.at[0, s, d], y_sem.at[1, s, d]
            to_y[s, d] = send(held.at[s, 1, z ^ d], from_y.at[s, z ^ d], sems, beside)
            core[s, d, 0].wait()
            held[s, 0, z ^ d] = add_low(held[s, 0, z ^ d], from_core[s, 0, z ^ d])
    for s in range(seqs):
        for d in order:
            to_y[s, d].wait()
            held[s, 0, z ^ d] = add_low(held[s, 0, z ^ d], from_y[s, z ^ d])
            if d == 0:
                own = pltpu.make_async_copy(
                    held.at[s, 0, z], outs[2 * s + 1].at[z], local_sem.at[s, 3]
                )
                own.start()
                waits.append(own)
            else:
                sems = z_sem.at[0, s, d], z_sem.at[1, s, d]
                waits.append(send(held.at[s, 0, z ^ d], outs[2 * s + 1].at[z], sems, line[d]))
    for copy in waits:
        copy.wait()


def return_grads(dqs, dkvs):
    seqs = len(dqs)
    groups, rows, per = dqs[0].shape
    args, shapes = [], []
    for dq, pieces in zip(dqs, dkvs):
        args += [dq, *pieces]
        shapes += [jax.ShapeDtypeStruct(dq.shape, BF16), jax.ShapeDtypeStruct(pieces[0].shape, BF16)]
    dma = pltpu.SemaphoreType.DMA
    slab = (groups, rows, 2 * per)
    return pl.pallas_call(
        functools.partial(return_kernel, seqs),
        out_shape=shapes,
        in_specs=[ANY] * len(args),
        out_specs=[ANY] * len(shapes),
        scratch_shapes=[
            pltpu.VMEM((seqs, 2, *slab), BF16),
            pltpu.VMEM((seqs, 2, *slab), BF16),
            pltpu.VMEM((seqs, *slab), BF16),
            dma((seqs, 4)),
            dma((2, seqs, groups)),
            dma((2, seqs, groups, 2)),
            dma((2, seqs, groups)),
            dma((2, seqs, groups)),
        ],
        compiler_params=pltpu.CompilerParams(
            vmem_limit_bytes=40 * 2**20, collective_id=1, has_side_effects=True
        ),
        cost_estimate=cost(70),
        name="return_grads",
    )(*args)


def sum_kernel(grads, small, out, small_out, *rest):
    acc, from_core, from_x, from_y, from_z, res, vec, vec_in, sems, small_sems, last_sem = rest
    z, y, c, x = position()
    sibling, beside, over = device(z, y, 1 - c, x), device(z, 1 - y, c, x), device(z, y, c, 1 - x)
    line = [None] + [device(z ^ d, y, c, x) for d in range(1, GROUPS)]
    parts, rows = grads.shape[0], grads.shape[3]
    half, piece = rows // 2, rows // 8
    own_half = pl.ds(pl.multiple_of(y * half, half), half)
    other_half = pl.ds(pl.multiple_of((1 - y) * half, half), half)

    def piece_of(g):
        return pl.ds(pl.multiple_of(y * half + g * piece, piece), piece)

    greet([sibling, beside, over] + line[1:])

    def pair(k, p):
        return sems.at[0, k, p], sems.at[1, k, p]

    def small_pair(k):
        return small_sems.at[0, k], small_sems.at[1, k]

    core = [
        send(grads.at[p, 1 - c], from_core.at[p], pair(0, p), sibling) for p in range(parts)
    ]
    short = send(small, vec_in.at[0], small_pair(0), sibling)
    flows = []
    for p in range(parts):
        core[p].wait()
        acc[p] = add_low(grads[p, c], from_core[p])
        if p == 1:
            flows.append(send(acc.at[p, :, other_half], from_y.at[p], pair(1, p), beside))
        else:
            flows.append(send(acc.at[p, 1 - x], from_x.at[p], pair(1, p), over))
    short.wait()
    vec[...] = small[...] + vec_in[0]
    short = send(vec, vec_in.at[1], small_pair(1), over)
    for p in (1, 0, 2):
        flows[p].wait()
        if p == 1:
            for k in range(2):
                acc[p, k, own_half] = add_low(acc[p, k, own_half], from_y[p, k])
            flows[p] = send(acc.at[p, 1 - x, own_half], from_x.at[p, own_half], pair(2, p), over)
        else:
            acc[p, x] = add_low(acc[p, x], from_x[p])
            flows[p] = send(acc.at[p, x, other_half], from_y.at[p, 0], pair(2, p), beside)
    short.wait()
    vec[...] = vec[...] + vec_in[1]
    short = send(vec, vec_in.at[2], small_pair(2), beside)
    lines = {}
    for p in (1, 0, 2):
        flows[p].wait()
        if p == 1:
            acc[p, x, own_half] = add_low(acc[p, x, own_half], from_x[p, own_half])
        else:
            acc[p, x, own_half] = add_low(acc[p, x, own_half], from_y[p, 0])
        for d in range(1, GROUPS):
            lines[p, d] = send(
                acc.at[p, x, piece_of(z ^ d)], from_z.at[p, d], pair(2 + d, p), line[d]
            )
    short.wait()
    vec[...] = vec[...] + vec_in[2]
    vec_in[4 + z] = vec[...]
    shorts = [
        send(vec, vec_in.at[4 + z], small_pair(2 + d), line[d]) for d in range(1, GROUPS)
    ]
    spread = {}
    for p in (1, 0, 2):
        total = acc[p, x, piece_of(z)].astype(F32)
        for d in range(1, GROUPS):
            lines[p, d].wait()
            total += from_z[p, d].astype(F32)
        res[c, p, piece_of(z)] = total.astype(BF16)
        for d in range(1, GROUPS):
            spread[p, d] = send(
                res.at[c, p, piece_of(z)],
                res.at[c, p, piece_of(z)],
                pair(5 + d, p),
                line[d],
            )
    for p in (1, 0, 2):
        for d in range(1, GROUPS):
            spread[p, d].wait()
        flows[p] = send(
            res.at[c, p, own_half], res.at[c, p, own_half], pair(9, p), beside
        )
    for copy in shorts:
        copy.wait()
    small_out[...] = vec_in[4] + vec_in[5] + (vec_in[6] + vec_in[7])
    for p in (1, 0, 2):
        flows[p].wait()
        flows[p] = send(res.at[c, p], res.at[c, p], pair(10, p), sibling)
    for p in (1, 0, 2):
        flows[p].wait()
    done = pltpu.make_async_copy(res, out, last_sem)
    done.start()
    done.wait()


def sum_grads(grads, small):
    parts, _, _, rows, lanes = grads.shape
    dma = pltpu.SemaphoreType.DMA
    return pl.pallas_call(
        sum_kernel,
        out_shape=[
            jax.ShapeDtypeStruct((2, parts, rows, lanes), BF16),
            jax.ShapeDtypeStruct(small.shape, F32),
        ],
        in_specs=[VMEM, VMEM],
        out_specs=[ANY, VMEM],
        scratch_shapes=[
            pltpu.VMEM((parts, 2, rows, lanes), BF16),
            pltpu.VMEM((parts, 2, rows, lanes), BF16),
            pltpu.VMEM((parts, rows, lanes), BF16),
            pltpu.VMEM((parts, 2, rows // 2, lanes), BF16),
            pltpu.VMEM((parts, GROUPS, rows // 8, lanes), BF16),
            pltpu.VMEM((2, parts, rows, lanes), BF16),
            pltpu.VMEM(small.shape, F32),
            pltpu.VMEM((8, *small.shape), F32),
            dma((2, 11, parts)),
            dma((2, 6)),
            dma,
        ],
        compiler_params=pltpu.CompilerParams(
            vmem_limit_bytes=40 * 2**20, collective_id=2, has_side_effects=True
        ),
        cost_estimate=cost(50),
        name="sum_grads",
    )(grads, small)


def pick(table, index):
    places = jnp.arange(table.shape[0], dtype=jnp.int32)
    return jnp.sum(jnp.where(index[..., None] == places, table, 0), -1)


def shards(
    size,
    tokens,
    teacher,
    lengths,
    block_order,
    query_weight,
    query_bias,
    key_weight,
    value_weight,
    value_bias,
    out_weight,
    out_bias,
    gain_one,
    shift_one,
    inner_weight,
    inner_bias,
    outer_weight,
    outer_bias,
    gain_two,
    shift_two,
):
    seqs, rows, width = tokens.shape
    per_plane = size // GROUPS
    blocks_each = rows // BLK
    ctx, x = lax.axis_index("ctx"), lax.axis_index("wa")
    c, place = lax.rem(ctx, 2), lax.rem(ctx, per_plane)
    masks = [1 << b for b in reversed(range(per_plane.bit_length() - 1))]
    offsets = [0]
    for m in masks:
        offsets += [o ^ m for o in offsets]

    def across(value):
        return lax.ppermute(value, "wa", [(0, 1), (1, 0)])

    def flip(value, m):
        return lax.ppermute(value, "ctx", [(i, i ^ m) for i in range(size)])

    lines = [[g * per_plane + r for g in range(GROUPS)] for r in range(per_plane)]

    def turn(value):
        return lax.all_to_all(value, "ctx", 0, 0, axis_index_groups=lines)

    cores = [[i for i in range(size) if i % 2 == k] for k in range(2)]

    def paired(mine):
        sibling = flip(mine, 1)
        return jnp.where(c == 0, jnp.stack([mine, sibling]), jnp.stack([sibling, mine]))

    def reduced(grad):
        four = grad.reshape(2, 2, *grad.shape[1:])
        keep = lax.dynamic_index_in_dim(four, c, 1, False)
        give = lax.dynamic_index_in_dim(four, 1 - c, 1, False)
        keep = add_low(keep, flip(give, 1))
        mine = lax.dynamic_index_in_dim(keep, x, 0, False)
        mine = add_low(mine, across(lax.dynamic_index_in_dim(keep, 1 - x, 0, False)))
        return paired(lax.psum(mine, "ctx", axis_index_groups=cores))

    def reduced_dense(grad):
        four = grad.reshape(2, 2, *grad.shape[1:])
        keep = lax.dynamic_index_in_dim(four, c, 1, False)
        give = lax.dynamic_index_in_dim(four, 1 - c, 1, False)
        keep = add_low(keep, flip(give, 1))
        mine = lax.psum_scatter(
            keep.reshape(-1, keep.shape[-1]), "wa", scatter_dimension=0, tiled=True
        )
        return lax.psum(mine, "ctx", axis_index_groups=cores)

    vectors = (
        query_bias,
        value_bias,
        out_bias,
        gain_one,
        shift_one,
        outer_bias,
        gain_two,
        shift_two,
        inner_bias,
    )
    own_vec = jnp.concatenate(vectors)[None]
    other_vec = across(own_vec)
    pair = jnp.where(
        x == 0, jnp.stack([own_vec, other_vec]), jnp.stack([other_vec, own_vec])
    ).astype(F32)
    half = width // 2
    narrow = pair[:, 0, : 8 * half].reshape(2, 8, half).swapaxes(0, 1).reshape(8, width)
    wide_vec = pair[:, 0, 8 * half :].reshape(1, -1)

    def quarter(weight):
        n = weight.shape[0] // 2
        return lax.dynamic_slice_in_dim(weight, c * n, n, 0)

    first_qkv = across(
        jnp.concatenate([quarter(w) for w in (query_weight, key_weight, value_weight)], 0)
    )
    second_qkv = flip(first_qkv, 1)
    dense_weights = []
    last = first_qkv
    for weight in (out_weight, inner_weight, outer_weight):
        piece, last = lax.optimization_barrier((quarter(weight), last))
        last = across(piece)
        dense_weights += [weight, last, flip(last, 1)]

    count = block_order.shape[0]
    ids = jnp.arange(count, dtype=jnp.int32)
    owner = ids // blocks_each
    index_of = jnp.array([offsets.index(o) for o in range(per_plane)], jnp.int32)
    piece_of = pick(index_of, (owner % per_plane) ^ place)
    spot = (piece_of * GROUPS + owner // per_plane) * blocks_each + ids % blocks_each
    key_order = jnp.sum(jnp.where(block_order[None, :] == ids[:, None], spot[None, :], 0), 1)
    near = jnp.arange(GROUPS * blocks_each, dtype=jnp.int32)
    near_ids = (near // blocks_each * per_plane + place) * blocks_each + near % blocks_each
    near_pos = pick(block_order, near_ids)
    rank = jnp.sum((near_pos[None, :] < near_pos[:, None]).astype(jnp.int32), 1)
    query_order = jnp.sum(jnp.where(rank[None, :] == near[:, None], near[None, :], 0), 1)
    own_pos = pick(block_order, ctx * blocks_each + jnp.arange(blocks_each, dtype=jnp.int32))
    scalars, row_counts = [], []
    for s in range(seqs):
        used = jnp.sum((near_pos * BLK < lengths[s]).astype(jnp.int32))
        head = jnp.concatenate([lengths[s][None], used[None], jnp.zeros((6,), jnp.int32)])
        scalars.append(jnp.concatenate([head, query_order, key_order]))
        row_counts.append(jnp.clip(lengths[s] - own_pos * BLK, 0, BLK))

    projected = project(
        tokens, narrow, query_weight, key_weight, value_weight, first_qkv, second_qkv
    )
    queries, pieces = [], []
    for s in range(seqs):
        kv = turn(projected[2 * s + 1])
        queries.append(turn(projected[2 * s]).reshape(-1, BLK, width // GROUPS))
        held = [kv.reshape(-1, BLK, kv.shape[2])]
        for m in masks:
            held += [flip(piece, m) for piece in held]
        pieces.append(held)

    attended, lses, dense_out = [], [], []
    for s in range(seqs):
        o, lse = attend(scalars[s], queries[s], pieces[s])
        attended.append(o.reshape(queries[s].shape))
        lses.append(lse)
    for s in range(seqs):
        o4 = turn(attended[s].reshape(GROUPS, rows, -1))
        dense_out.append(
            dense(
                row_counts[s], o4, tokens[s], teacher[s], narrow[2:], wide_vec, dense_weights
            )
        )
    saved = [d[3:9] for d in dense_out]
    heads_grad = [turn(d[2]).reshape(queries[s].shape) for s, d in enumerate(dense_out)]
    g_dense = dense_grads(saved)

    dense_sums = [reduced_dense(g) for g in g_dense]
    fused = per_plane == 4
    dqs, dkvs = [], []
    for s in range(seqs):
        found = attend_back(
            scalars[s], queries[s], heads_grad[s], attended[s], lses[s], pieces[s]
        )
        dqs.append(found[0].reshape(GROUPS, rows, -1))
        dkvs.append([piece.reshape(GROUPS, rows, -1) for piece in found[1:]])
    if fused:
        returned = return_grads(dqs, dkvs)
        dqs, dkvs = returned[0::2], returned[1::2]
    else:
        for s in range(seqs):
            dqs[s] = turn(dqs[s])
            held = dkvs[s]
            for m in reversed(masks):
                n = len(held) // 2
                held = [add_low(mine, flip(theirs, m)) for mine, theirs in zip(held[:n], held[n:])]
            dkvs[s] = turn(held[0])
    tokens_grad, g_qkv, sums_qkv = project_grads(
        tokens,
        [d[1] for d in dense_out],
        dqs,
        dkvs,
        query_weight,
        key_weight,
        value_weight,
        first_qkv,
        second_qkv,
    )

    sums = sum(d[9] for d in dense_out)
    wide_sums = sum(d[10] for d in dense_out)
    loss_part = jnp.sum(sums[6])
    valid = sum(jnp.sum(r) for r in row_counts).astype(F32)
    small = jnp.concatenate(
        [
            sums[:6].reshape(-1),
            sums_qkv[:2].reshape(-1),
            wide_sums[0],
            jnp.stack([loss_part, valid]),
        ]
    )
    small = jnp.pad(small, (0, -small.shape[0] % 1024)).reshape(-1, 128)
    if fused:
        qkv, small = sum_grads(g_qkv, small)
    else:
        small = lax.psum(small, ("ctx", "wa"))
        qkv = reduced(jnp.moveaxis(g_qkv, (2, 1), (0, 1)).reshape(4, 3, -1, 128))
    *dense_sums, small = lax.optimization_barrier((*dense_sums, small))
    small = small.reshape(-1)
    qkv = qkv.reshape(6, 3, half, 128).astype(F32)
    query_grad, key_grad, value_grad = (
        qkv[:, i].swapaxes(0, 1).reshape(half, width) for i in range(3)
    )
    out_grad, inner_grad, outer_grad = (
        paired(g).reshape(-1, g.shape[-1]).astype(F32) for g in dense_sums
    )

    def vector(start, length):
        return lax.dynamic_slice_in_dim(small, start + x * (length // 2), length // 2, 0)

    end = 8 * width
    hidden = wide_vec.shape[1]
    loss = small[end + hidden] / (small[end + hidden + 1] * width)
    return (
        jnp.stack([d[0] for d in dense_out]),
        tokens_grad,
        query_grad,
        vector(6 * width, width),
        key_grad,
        value_grad,
        vector(7 * width, width),
        out_grad,
        vector(5 * width, width),
        vector(3 * width, width),
        vector(4 * width, width),
        inner_grad,
        vector(end, hidden),
        outer_grad,
        vector(2 * width, width),
        vector(0, width),
        vector(width, width),
        loss,
    )


def solution(mesh):
    row, split, both = P("wa"), P("wa", None), P("wa", "ctx", None)
    placed = (both, both, row, P(), split, row, split, split, row, split, row, row, row)
    placed += (split, row, split, row, row, row)
    return jax.shard_map(
        functools.partial(shards, mesh.shape["ctx"]),
        mesh=mesh,
        in_specs=placed,
        out_specs=(
            both,
            both,
            split,
            row,
            split,
            split,
            row,
            split,
            row,
            row,
            row,
            split,
            row,
            split,
            row,
            row,
            row,
            P(),
        ),
        check_vma=False,
    )
```

```python
import functools
import math

import jax
import jax.numpy as jnp
from jax import lax
from jax.experimental import pallas as pl
from jax.experimental.pallas import tpu as pltpu
from jax.sharding import PartitionSpec as P

DH = 64
BLK = 128
GROUPS = 4
LN2 = math.log(2.0)
NT = (((1,), (1,)), ((), ()))
NN = (((1,), (0,)), ((), ()))
TN = (((0,), (0,)), ((), ()))
F32 = jnp.float32
BF16 = jnp.bfloat16
VMEM = pl.BlockSpec(memory_space=pltpu.VMEM)
SMEM = pl.BlockSpec(memory_space=pltpu.SMEM)
ANY = pl.BlockSpec(memory_space=pl.ANY)
ROOM = pltpu.CompilerParams(vmem_limit_bytes=58 * 2**20)


def dot(left, right, dims=NN):
    return lax.dot_general(left, right, dims, preferred_element_type=F32)


def cost(us):
    return pl.CostEstimate(flops=int(us * 1.15e9), bytes_accessed=1 << 20, transcendentals=0)


def weight_copies(full, own, first, second, sems, base):
    x, c = lax.axis_index("wa"), lax.rem(lax.axis_index("ctx"), 2)
    half = own.shape[0]
    quarter = half // 2
    other = (1 - x) * half
    places = (
        (own, x * half, half),
        (first, other + c * quarter, quarter),
        (second, other + (1 - c) * quarter, quarter),
    )
    return [
        pltpu.make_async_copy(
            src, full.at[pl.ds(pl.multiple_of(start, quarter), size)], sems.at[base + i]
        )
        for i, (src, start, size) in enumerate(places)
    ]


def project_kernel(tok, vec, wq, wk, wv, first, second, *rest):
    seqs, rows, width = tok.shape
    outs, (full, sems) = rest[: 2 * seqs], rest[2 * seqs :]
    quarter = wq.shape[0] // 2
    copies = []
    for i, own in enumerate((wq, wk, wv)):
        part = pl.ds(i * quarter, quarter)
        copies.append(
            weight_copies(full.at[i], own, first.at[part], second.at[part], sems, 3 * i)
        )
    for group in copies:
        for copy in group:
            copy.start()
    flat = tok[...].reshape(seqs * rows, width)
    per = width // GROUPS
    heads = per // DH
    for copy in copies[1]:
        copy.wait()
    keys = dot(flat, full[1]).astype(BF16)
    for copy in copies[2]:
        copy.wait()
    values = (dot(flat, full[2]) + vec[1:2, :]).astype(BF16)
    for s in range(seqs):
        rs = slice(s * rows, (s + 1) * rows)
        for g in range(GROUPS):
            for h in range(heads):
                cols = slice(g * per + h * DH, g * per + (h + 1) * DH)
                outs[2 * s + 1][g, :, h * 128 : (h + 1) * 128] = jnp.concatenate(
                    [keys[rs, cols], values[rs, cols]], 1
                )
    for copy in copies[0]:
        copy.wait()
    queries = ((dot(flat, full[0]) + vec[0:1, :]) * (DH**-0.5 / LN2)).astype(BF16)
    for s in range(seqs):
        rs = slice(s * rows, (s + 1) * rows)
        for g in range(GROUPS):
            outs[2 * s][g] = queries[rs, g * per : (g + 1) * per]


def project(tok, vec, wq, wk, wv, first, second):
    seqs, rows, width = tok.shape
    per = width // GROUPS
    shapes = [
        jax.ShapeDtypeStruct((GROUPS, rows, n), BF16) for _ in range(seqs) for n in (per, 2 * per)
    ]
    return pl.pallas_call(
        project_kernel,
        out_shape=shapes,
        in_specs=[VMEM, VMEM] + [ANY] * 5,
        out_specs=[VMEM] * len(shapes),
        scratch_shapes=[pltpu.VMEM((3, width, width), BF16), pltpu.SemaphoreType.DMA((9,))],
        compiler_params=ROOM,
        cost_estimate=cost(5),
        name="project",
    )(tok, vec, wq, wk, wv, first, second)


def load_pieces(pieces, kv, sems):
    per = pieces[0].shape[0]
    copies = [
        pltpu.make_async_copy(piece, kv.at[pl.ds(i * per, per)], sems.at[i])
        for i, piece in enumerate(pieces)
    ]
    for copy in copies:
        copy.start()
    for copy in copies:
        copy.wait()


def forward_kernel(wide, narrow, count, sc, q_ref, *rest):
    pieces, (o_ref, lse_ref, kv_ref, qa, acc, sums, sems) = rest[:count], rest[count:]
    blocks = q_ref.shape[0]
    heads = q_ref.shape[2] // DH
    rows = blocks * BLK
    length = sc[0]
    load_pieces(pieces, kv_ref, sems)

    def gather(h, start, n):
        return jnp.concatenate(
            [kv_ref[sc[8 + blocks + start + i], :, h * 128 : (h + 1) * 128] for i in range(n)], 0
        )

    whole = length // (wide * BLK)
    tail = whole * wide
    tails = (length - tail * BLK + narrow * BLK - 1) // (narrow * BLK)
    for h in range(heads):
        hs = slice(h * DH, (h + 1) * DH)
        own = jnp.concatenate([q_ref[b, :, hs] for b in range(blocks)], 0)
        qa[...] = jnp.concatenate([own, jnp.zeros_like(own)], 1)
        acc[...] = jnp.zeros_like(acc)
        sums[...] = jnp.zeros_like(sums)

        def step(start, n, masked, h=h):
            kv = gather(h, start, n)
            scores = dot(qa[...], kv, NT)
            if masked:
                place = lax.broadcasted_iota(jnp.int32, scores.shape, 1) + start * BLK
                scores = jnp.where(place < length, scores, -1e30)
            p = jnp.exp2(scores)
            sums[...] += sum(p[:, i * 128 : (i + 1) * 128] for i in range(n))
            acc[...] += dot(p.astype(BF16), kv)

        def wide_step(j, _, step=step):
            step(j * wide, wide, False)
            return 0

        def narrow_step(j, _, step=step):
            step(tail + j * narrow, narrow, True)
            return 0

        lax.fori_loop(0, whole, wide_step, 0)
        lax.fori_loop(0, tails, narrow_step, 0)
        total = jnp.sum(sums[...], 1, keepdims=True)
        across = jnp.transpose(jnp.broadcast_to(total, (rows, 128)))[:8]
        good = (jnp.min(across) > 2.0**-80) & (jnp.max(across) < 2.0**100)

        @pl.when(good)
        def _(h=h, hs=hs, total=total, across=across):
            lse_ref[h] = jnp.log2(across)
            o_ref[:, hs] = (acc[:, DH:] * (1.0 / total)).astype(BF16)

        @pl.when(jnp.logical_not(good))
        def _(h=h, hs=hs):
            key_blocks = (length + BLK - 1) // BLK

            def rows_step(t, _):
                part = pl.ds(pl.multiple_of(t * BLK, BLK), BLK)
                q = qa[part, :]

                def scores_of(j):
                    kv = gather(h, j, 1)
                    scores = dot(q, kv, NT)
                    place = lax.broadcasted_iota(jnp.int32, scores.shape, 1) + j * BLK
                    return kv, jnp.where(place < length, scores, -1e30)

                largest = lax.fori_loop(
                    0,
                    key_blocks,
                    lambda j, m: jnp.maximum(m, jnp.max(scores_of(j)[1], 1, keepdims=True)),
                    jnp.full((BLK, 1), -1e30, F32),
                )
                acc[part, :] = jnp.zeros((BLK, 128), F32)
                sums[part, :] = jnp.zeros((BLK, 128), F32)

                def add(j, _):
                    kv, scores = scores_of(j)
                    p = jnp.exp2(scores - largest)
                    sums[part, :] += p
                    acc[part, :] += dot(p.astype(BF16), kv)
                    return 0

                lax.fori_loop(0, key_blocks, add, 0)
                row_total = jnp.sum(sums[part, :], 1, keepdims=True)
                lse = largest + jnp.log2(row_total)
                lse_ref[h, :, part] = jnp.transpose(jnp.broadcast_to(lse, (BLK, 128)))[:8]
                o_ref[part, hs] = (acc[part, :][:, DH:] * (1.0 / row_total)).astype(BF16)
                return 0

            lax.fori_loop(0, rows // BLK, rows_step, 0)


def attend(sc, q, pieces):
    blocks, _, per = q.shape
    rows, heads = blocks * BLK, per // DH
    key_blocks = len(pieces) * pieces[0].shape[0]
    return pl.pallas_call(
        functools.partial(forward_kernel, 8, 2, len(pieces)),
        out_shape=(
            jax.ShapeDtypeStruct((rows, per), BF16),
            jax.ShapeDtypeStruct((heads, 8, rows), F32),
        ),
        in_specs=[SMEM, VMEM] + [ANY] * len(pieces),
        out_specs=(VMEM, VMEM),
        scratch_shapes=[
            pltpu.VMEM((key_blocks, BLK, 2 * per), BF16),
            pltpu.VMEM((rows, 128), BF16),
            pltpu.VMEM((rows, 128), F32),
            pltpu.VMEM((rows, 128), F32),
            pltpu.SemaphoreType.DMA((len(pieces),)),
        ],
        compiler_params=ROOM,
        cost_estimate=cost(20),
        name="attend",
    )(sc, q, *pieces)


def backward_kernel(qn, kn, count, sc, q_ref, do_ref, o_ref, lse_ref, *rest):
    pieces, dq_ref, outs = rest[:count], rest[count], rest[count + 1 : 2 * count + 1]
    kv_ref, both, dkv, dq, lse_row, delta_row, sems = rest[2 * count + 1 :]
    blocks = q_ref.shape[0]
    heads = q_ref.shape[2] // DH
    key_blocks = kv_ref.shape[0]
    tile = qn * BLK
    length, used = sc[0], sc[1]
    whole = length // (kn * BLK)
    parts = (length + kn * BLK - 1) // (kn * BLK)
    tiles = (used + qn - 1) // qn
    ones = jnp.ones((8, DH), BF16)
    load_pieces(pieces, kv_ref, sems)
    for h in range(heads):
        hs = slice(h * DH, (h + 1) * DH)

        def clear(i, _):
            dkv[pl.ds(pl.multiple_of(i * 1024, 1024), 1024), :] = jnp.zeros((1024, 128), F32)
            return 0

        lax.fori_loop(0, key_blocks // 8, clear, 0)
        dq[...] = jnp.zeros_like(dq)

        def prepare(t, _, h=h, hs=hs):
            base = pl.multiple_of(t * (2 * tile), 2 * tile)
            start = pl.multiple_of(t * tile, tile)
            places = [sc[8 + t * qn + i] for i in range(qn)]
            q = jnp.concatenate([q_ref[s, :, hs] for s in places], 0)
            do = jnp.concatenate([do_ref[s, :, hs] for s in places], 0)
            o = jnp.concatenate([o_ref[s, :, hs] for s in places], 0)
            zero = jnp.zeros_like(q)
            both[pl.ds(base, tile), :] = jnp.concatenate([q, zero], 1)
            both[pl.ds(base + tile, tile), :] = jnp.concatenate([zero, do], 1)
            product = do.astype(F32) * o.astype(F32)
            high = product.astype(BF16)
            rest_of = (product - high.astype(F32)).astype(BF16)
            delta_row[:, pl.ds(start, tile)] = dot(ones, high, NT) + dot(ones, rest_of, NT)
            lse_row[:, pl.ds(start, tile)] = jnp.concatenate(
                [lse_ref[h, :, pl.ds(pl.multiple_of(s * BLK, BLK), BLK)] for s in places], 1
            )
            return 0

        lax.fori_loop(0, tiles, prepare, 0)

        def rows_step(t, _, h=h):
            base = pl.multiple_of(t * (2 * tile), 2 * tile)
            span = pl.ds(pl.multiple_of(t * tile, tile), tile)

            def step(j, masked):
                places = [sc[8 + blocks + j * kn + i] for i in range(kn)]
                kv = jnp.concatenate([kv_ref[s, :, h * 128 : (h + 1) * 128] for s in places], 0)
                b = both[pl.ds(base, 2 * tile), :]
                found = dot(kv, b, NT)
                p = jnp.exp2(found[:, :tile] - lse_row[:1, span])
                if masked:
                    place = lax.broadcasted_iota(jnp.int32, p.shape, 0) + j * (kn * BLK)
                    p = jnp.where(place < length, p, 0.0)
                ds = (p * (found[:, tile:] - delta_row[:1, span])).astype(BF16)
                grads = dot(jnp.concatenate([ds, p.astype(BF16)], 1), b)
                for i, s in enumerate(places):
                    dkv[pl.ds(pl.multiple_of(s * BLK, BLK), BLK), :] += grads[
                        i * BLK : (i + 1) * BLK
                    ]
                dq[span, :] += dot(ds, kv, TN)

            def whole_step(j, _):
                step(j, False)
                return 0

            lax.fori_loop(0, whole, whole_step, 0)

            @pl.when(parts > whole)
            def _():
                step(whole, True)

            return 0

        lax.fori_loop(0, tiles, rows_step, 0)
        for i in range(blocks):
            dq_ref[sc[8 + i], :, hs] = (
                dq[i * BLK : (i + 1) * BLK, :DH] * DH**-0.5
            ).astype(BF16)
        level = jnp.where(lax.broadcasted_iota(jnp.int32, (1, 128), 1) < DH, LN2, 1.0)
        per_piece = key_blocks // count
        for n, out in enumerate(outs):
            for i in range(per_piece):
                b = n * per_piece + i
                out[i, :, h * 128 : (h + 1) * 128] = (
                    dkv[b * BLK : (b + 1) * BLK, :] * level
                ).astype(BF16)


def attend_back(sc, q, do, o, lse, pieces):
    blocks, _, per = q.shape
    rows = blocks * BLK
    key_blocks = len(pieces) * pieces[0].shape[0]
    return pl.pallas_call(
        functools.partial(backward_kernel, 4, 4, len(pieces)),
        out_shape=[jax.ShapeDtypeStruct(q.shape, BF16)]
        + [jax.ShapeDtypeStruct(p.shape, BF16) for p in pieces],
        in_specs=[SMEM] + [VMEM] * 4 + [ANY] * len(pieces),
        out_specs=[VMEM] * (1 + len(pieces)),
        scratch_shapes=[
            pltpu.VMEM((key_blocks, BLK, 2 * per), BF16),
            pltpu.VMEM((2 * rows, 128), BF16),
            pltpu.VMEM((key_blocks * BLK, 128), F32),
            pltpu.VMEM((rows, 128), F32),
            pltpu.VMEM((8, rows), F32),
            pltpu.VMEM((8, rows), F32),
            pltpu.SemaphoreType.DMA((len(pieces),)),
        ],
        compiler_params=ROOM,
        cost_estimate=cost(45),
        name="attend_back",
    )(sc, q, do, o, lse, *pieces)


def norm(values):
    centered = values - jnp.mean(values, -1, keepdims=True)
    inverse = lax.rsqrt(jnp.mean(centered * centered, -1, keepdims=True) + 1e-6)
    return centered * inverse, inverse


def norm_back(upstream, normed, inverse):
    return inverse * (
        upstream
        - jnp.mean(upstream, -1, keepdims=True)
        - normed * jnp.mean(upstream * normed, -1, keepdims=True)
    )


def normal_parts(x):
    z = jnp.abs(x) * (0.5**0.5)
    bell = jnp.exp(-0.5 * x * x)
    t = 1.0 / (1.0 + 0.3275911 * z)
    poly = t * (
        0.254829592
        + t * (-0.284496736 + t * (1.421413741 + t * (-1.453152027 + t * 1.061405429)))
    )
    upper = 0.5 * poly * bell
    return jnp.where(x >= 0, 1.0 - upper, upper), bell * (2.0 * math.pi) ** -0.5


def dense_kernel(sc, att4, tok, teach, vec, wide_vec, *rest):
    weights, rest = rest[:9], rest[9:]
    outs, (wo, wi, wu, slope, sems) = rest[:11], rest[11:]
    out, fg, ag, att_o, br_o, hl_o, il_o, act_o, ol_o, sums, wide_sums = outs
    rows, width = tok.shape
    hidden = wi.shape[1]
    tile = 512
    copies = [
        weight_copies(full, *weights[3 * i : 3 * i + 3], sems, 3 * i)
        for i, full in enumerate((wo, wi, wu))
    ]
    for group in copies:
        for copy in group:
            copy.start()
    per = att4.shape[2]
    att = jnp.concatenate([att4[g] for g in range(GROUPS)], 1)
    att_o[...] = att
    row = lax.broadcasted_iota(jnp.int32, (rows, 1), 0)
    mask = jnp.where(
        row < BLK, jnp.where(row < sc[0], 1.0, 0.0), jnp.where(row - BLK < sc[1], 1.0, 0.0)
    )
    out_bias, gain_one, shift_one = vec[0:1, :], vec[1:2, :], vec[2:3, :]
    outer_bias, gain_two, shift_two = vec[3:4, :], vec[4:5, :], vec[5:6, :]
    for copy in copies[0]:
        copy.wait()
    first = tok[...].astype(F32) + dot(att, wo[...]) + out_bias
    normed_one, inverse_one = norm(first)
    hidden_in = normed_one * gain_one + shift_one
    hl = hidden_in.astype(BF16)
    hl_o[...] = hl
    for copy in copies[1] + copies[2]:
        copy.wait()
    second = hidden_in + outer_bias
    for n in range(hidden // tile):
        cols = slice(n * tile, (n + 1) * tile)
        inner = dot(hl, wi[:, cols]) + wide_vec[0:1, cols]
        below, density = normal_parts(inner)
        act = (inner * below).astype(BF16)
        act_o[:, cols] = act
        slope[:, cols] = below + inner * density
        second += dot(act, wu[cols, :])
    normed_two, inverse_two = norm(second)
    final = normed_two * gain_two + shift_two
    out[...] = final.astype(BF16)
    residue = (final - teach[...].astype(F32)) * mask
    add = functools.partial(jnp.sum, axis=0, keepdims=True)
    second_grad = norm_back(residue * gain_two, normed_two, inverse_two)
    ol = second_grad.astype(BF16)
    ol_o[...] = ol
    hidden_grad = second_grad
    for n in range(hidden // tile):
        cols = slice(n * tile, (n + 1) * tile)
        il = (dot(ol, wu[cols, :], NT) * slope[:, cols]).astype(BF16)
        il_o[:, cols] = il
        wide_sums[0:1, cols] = add(il.astype(F32))
        hidden_grad += dot(il, wi[:, cols], NT)
    first_grad = norm_back(hidden_grad * gain_one, normed_one, inverse_one)
    fg[...] = first_grad
    br = first_grad.astype(BF16)
    br_o[...] = br
    att_grad = dot(br, wo[...], NT).astype(BF16)
    for g in range(GROUPS):
        ag[g] = att_grad[:, g * per : (g + 1) * per]
    sums[0:1, :] = add(residue * normed_two)
    sums[1:2, :] = add(residue)
    sums[2:3, :] = add(ol.astype(F32))
    sums[3:4, :] = add(hidden_grad * normed_one)
    sums[4:5, :] = add(hidden_grad)
    sums[5:6, :] = add(br.astype(F32))
    sums[6:7, :] = add(residue * residue)
    sums[7:8, :] = jnp.zeros((1, width), F32)


def dense(sc, att4, tok, teach, vec, wide_vec, weights):
    rows, width = tok.shape
    hidden = wide_vec.shape[1]
    narrow = jax.ShapeDtypeStruct((rows, width), BF16)
    wide = jax.ShapeDtypeStruct((rows, hidden), BF16)
    return pl.pallas_call(
        dense_kernel,
        out_shape=[
            narrow,
            jax.ShapeDtypeStruct((rows, width), F32),
            jax.ShapeDtypeStruct(att4.shape, BF16),
            narrow,
            narrow,
            narrow,
            wide,
            wide,
            narrow,
            jax.ShapeDtypeStruct((8, width), F32),
            jax.ShapeDtypeStruct((1, hidden), F32),
        ],
        in_specs=[SMEM] + [VMEM] * 5 + [ANY] * 9,
        out_specs=[VMEM] * 11,
        scratch_shapes=[
            pltpu.VMEM((width, width), BF16),
            pltpu.VMEM((width, hidden), BF16),
            pltpu.VMEM((hidden, width), BF16),
            pltpu.VMEM((rows, hidden), F32),
            pltpu.SemaphoreType.DMA((9,)),
        ],
        compiler_params=ROOM,
        cost_estimate=cost(15),
        name="dense",
    )(sc, att4, tok, teach, vec, wide_vec, *weights)


def dense_grads_kernel(seqs, *refs):
    ins, (g_out, g_inner, g_outer) = refs[: 6 * seqs], refs[6 * seqs :]
    att, br, hl, il, act, ol = (
        jnp.concatenate([ins[6 * s + i][...] for s in range(seqs)], 0) for i in range(6)
    )
    for target, left, right in ((g_out, att, br), (g_inner, hl, il), (g_outer, act, ol)):
        rows = target.shape[1]
        for n in range(4):
            piece = left[:, n * rows : (n + 1) * rows]
            for t in range(right.shape[1] // 768):
                cols = slice(t * 768, (t + 1) * 768)
                target[n, :, cols] = dot(piece, right[:, cols], TN).astype(BF16)


def dense_grads(saved):
    seqs = len(saved)
    width, hidden = saved[0][0].shape[1], saved[0][3].shape[1]
    return pl.pallas_call(
        functools.partial(dense_grads_kernel, seqs),
        out_shape=[
            jax.ShapeDtypeStruct((4, width // 4, width), BF16),
            jax.ShapeDtypeStruct((4, width // 4, hidden), BF16),
            jax.ShapeDtypeStruct((4, hidden // 4, width), BF16),
        ],
        in_specs=[VMEM] * (6 * seqs),
        out_specs=[VMEM] * 3,
        compiler_params=ROOM,
        cost_estimate=cost(10),
        name="dense_grads",
    )(*[member for group in saved for member in group])


def project_grads_kernel(seqs, tok, *refs):
    fgs, refs = refs[:seqs], refs[seqs:]
    dqs, refs = refs[:seqs], refs[seqs:]
    dkvs, refs = refs[:seqs], refs[seqs:]
    wq, wk, wv, first, second, tg, grads, sums, full, sems = refs
    rows, width = tok.shape[1:]
    per = width // GROUPS
    heads = per // DH
    quarter = wq.shape[0] // 2
    copies = []
    for i, own in enumerate((wq, wk, wv)):
        part = pl.ds(i * quarter, quarter)
        copies += weight_copies(full.at[i], own, first.at[part], second.at[part], sems, 3 * i)
    for copy in copies:
        copy.start()
    dq = jnp.concatenate(
        [jnp.concatenate([dqs[s][g] for g in range(GROUPS)], 1) for s in range(seqs)], 0
    )
    pair = [
        jnp.concatenate([dkvs[s][g] for g in range(GROUPS)], 1) for s in range(seqs)
    ]
    pair = jnp.concatenate(pair, 0)
    halves = [
        jnp.concatenate(
            [
                pair[:, n * 128 + part * DH : n * 128 + (part + 1) * DH]
                for n in range(GROUPS * heads)
            ],
            1,
        )
        for part in (0, 1)
    ]
    flat = tok[...].reshape(seqs * rows, width)
    for copy in copies:
        copy.wait()
    total = jnp.concatenate([fgs[s][...] for s in range(seqs)], 0)
    for i, grad in enumerate((dq, *halves)):
        total += dot(grad, full[i], NT)
        found = dot(flat, grad, TN).astype(BF16)
        half = width // 2
        for n in range(2):
            for t in range(width // 128):
                grads[t % 3, t // 3, n, i * half : (i + 1) * half, :] = found[
                    n * half : (n + 1) * half, t * 128 : (t + 1) * 128
                ]
    tg[...] = total.reshape(seqs, rows, width)
    sums[0:1, :] = jnp.sum(dq.astype(F32), 0, keepdims=True)
    sums[1:2, :] = jnp.sum(halves[1].astype(F32), 0, keepdims=True)
    sums[2:8, :] = jnp.zeros((6, width), F32)


def project_grads(tok, fgs, dqs, dkvs, wq, wk, wv, first, second):
    seqs, rows, width = tok.shape
    return pl.pallas_call(
        functools.partial(project_grads_kernel, seqs),
        out_shape=[
            jax.ShapeDtypeStruct(tok.shape, F32),
            jax.ShapeDtypeStruct((3, 2, 2, 3 * (width // 2), 128), BF16),
            jax.ShapeDtypeStruct((8, width), F32),
        ],
        in_specs=[VMEM] * (1 + 3 * seqs) + [ANY] * 5,
        out_specs=[VMEM] * 3,
        scratch_shapes=[pltpu.VMEM((3, width, width), BF16), pltpu.SemaphoreType.DMA((9,))],
        compiler_params=ROOM,
        cost_estimate=cost(10),
        name="project_grads",
    )(tok, *fgs, *dqs, *dkvs, wq, wk, wv, first, second)


MESH = pl.DeviceIdType.MESH


def position():
    ctx = lax.axis_index("ctx")
    return ctx // 4, lax.rem(ctx // 2, 2), lax.rem(ctx, 2), lax.axis_index("wa")


def device(z, y, c, x):
    return z * 4 + y * 2 + c, x


def greet(others):
    barrier = pltpu.get_barrier_semaphore()
    for other in others:
        pl.semaphore_signal(barrier, inc=1, device_id=other, device_id_type=MESH)
    pl.semaphore_wait(barrier, len(others))


def send(src, dst, sems, to):
    copy = pltpu.make_async_remote_copy(
        src_ref=src,
        dst_ref=dst,
        send_sem=sems[0],
        recv_sem=sems[1],
        device_id=to,
        device_id_type=MESH,
    )
    copy.start()
    return copy


def add_low(left, right):
    return (left.astype(F32) + right.astype(F32)).astype(BF16)


def return_kernel(seqs, *refs):
    ins, outs = refs[: 5 * seqs], refs[5 * seqs : 7 * seqs]
    held, from_core, from_y, local_sem, q_sem, c_sem, y_sem, z_sem = refs[7 * seqs :]
    z, y, c, x = position()
    sibling, beside = device(z, y, 1 - c, x), device(z, 1 - y, c, x)
    line = [None] + [device(z ^ d, y, c, x) for d in range(1, GROUPS)]
    greet([sibling, beside] + line[1:])
    waits = []
    for s in range(seqs):
        for d in range(1, GROUPS):
            sems = q_sem.at[0, s, d], q_sem.at[1, s, d]
            waits.append(send(ins[5 * s].at[z ^ d], outs[2 * s].at[z], sems, line[d]))
    core = {}
    for s in range(seqs):
        for d in range(GROUPS):
            for i in (1, 0):
                sems = c_sem.at[0, s, d, i], c_sem.at[1, s, d, i]
                core[s, d, i] = send(
                    ins[5 * s + 3 + i].at[z ^ d], from_core.at[s, i, z ^ d], sems, sibling
                )
    local = {}
    for s in range(seqs):
        for i in (1, 0):
            local[s, i] = pltpu.make_async_copy(
                ins[5 * s + 1 + i], held.at[s, i], local_sem.at[s, i]
            )
            local[s, i].start()
        own = pltpu.make_async_copy(ins[5 * s].at[z], outs[2 * s].at[z], local_sem.at[s, 2])
        own.start()
        waits.append(own)
    order = [1, 2, 3, 0]
    to_y = {}
    for s in range(seqs):
        local[s, 1].wait()
        local[s, 0].wait()
        for d in order:
            core[s, d, 1].wait()
            held[s, 1, z ^ d] = add_low(held[s, 1, z ^ d], from_core[s, 1, z ^ d])
            sems = y_sem.at[0, s, d], y_sem.at[1, s, d]
            to_y[s, d] = send(held.at[s, 1, z ^ d], from_y.at[s, z ^ d], sems, beside)
            core[s, d, 0].wait()
            held[s, 0, z ^ d] = add_low(held[s, 0, z ^ d], from_core[s, 0, z ^ d])
    for s in range(seqs):
        for d in order:
            to_y[s, d].wait()
            held[s, 0, z ^ d] = add_low(held[s, 0, z ^ d], from_y[s, z ^ d])
            if d == 0:
                own = pltpu.make_async_copy(
                    held.at[s, 0, z], outs[2 * s + 1].at[z], local_sem.at[s, 3]
                )
                own.start()
                waits.append(own)
            else:
                sems = z_sem.at[0, s, d], z_sem.at[1, s, d]
                waits.append(send(held.at[s, 0, z ^ d], outs[2 * s + 1].at[z], sems, line[d]))
    for copy in waits:
        copy.wait()


def return_grads(dqs, dkvs):
    seqs = len(dqs)
    groups, rows, per = dqs[0].shape
    args, shapes = [], []
    for dq, pieces in zip(dqs, dkvs):
        args += [dq, *pieces]
        shapes += [jax.ShapeDtypeStruct(dq.shape, BF16), jax.ShapeDtypeStruct(pieces[0].shape, BF16)]
    dma = pltpu.SemaphoreType.DMA
    slab = (groups, rows, 2 * per)
    return pl.pallas_call(
        functools.partial(return_kernel, seqs),
        out_shape=shapes,
        in_specs=[ANY] * len(args),
        out_specs=[ANY] * len(shapes),
        scratch_shapes=[
            pltpu.VMEM((seqs, 2, *slab), BF16),
            pltpu.VMEM((seqs, 2, *slab), BF16),
            pltpu.VMEM((seqs, *slab), BF16),
            dma((seqs, 4)),
            dma((2, seqs, groups)),
            dma((2, seqs, groups, 2)),
            dma((2, seqs, groups)),
            dma((2, seqs, groups)),
        ],
        compiler_params=pltpu.CompilerParams(
            vmem_limit_bytes=40 * 2**20, collective_id=1, has_side_effects=True
        ),
        cost_estimate=cost(70),
        name="return_grads",
    )(*args)


def middle_stage(s, att, mask, tok, teach, vec, wide_vec, weights, keep, outs, first_done):
    wo, wi, wu, slope = weights
    att_k, br_k, hl_k, il_k, act_k, ol_k = keep
    out, fg, sums, wide_sums = outs
    rows = att.shape[0]
    hidden = wi.shape[1]
    tile = 512
    rs = slice(s * rows, (s + 1) * rows)
    out_bias, gain_one, shift_one = vec[0:1, :], vec[1:2, :], vec[2:3, :]
    outer_bias, gain_two, shift_two = vec[3:4, :], vec[4:5, :], vec[5:6, :]
    add = functools.partial(jnp.sum, axis=0, keepdims=True)

    def collect(target, value):
        if s == 0:
            target[...] = value
        else:
            target[...] += value

    att_k[rs, :] = att
    first_done[0]()
    first = tok[s].astype(F32) + dot(att, wo[...]) + out_bias
    normed_one, inverse_one = norm(first)
    hidden_in = normed_one * gain_one + shift_one
    hl = hidden_in.astype(BF16)
    hl_k[rs, :] = hl
    first_done[1]()
    second = hidden_in + outer_bias
    for n in range(hidden // tile):
        cols = slice(n * tile, (n + 1) * tile)
        inner = dot(hl, wi[:, cols]) + wide_vec[0:1, cols]
        below, density = normal_parts(inner)
        act = (inner * below).astype(BF16)
        act_k[rs, cols] = act
        slope[:, cols] = below + inner * density
        second += dot(act, wu[cols, :])
    normed_two, inverse_two = norm(second)
    final = normed_two * gain_two + shift_two
    out[s] = final.astype(BF16)
    residue = (final - teach[s].astype(F32)) * mask
    collect(sums.at[0:1], add(residue * normed_two))
    collect(sums.at[1:2], add(residue))
    collect(sums.at[6:7], add(residue * residue))
    second_grad = norm_back(residue * gain_two, normed_two, inverse_two)
    ol = second_grad.astype(BF16)
    ol_k[rs, :] = ol
    collect(sums.at[2:3], add(ol.astype(F32)))
    hidden_grad = second_grad
    for n in range(hidden // tile):
        cols = slice(n * tile, (n + 1) * tile)
        il = (dot(ol, wu[cols, :], NT) * slope[:, cols]).astype(BF16)
        il_k[rs, cols] = il
        collect(wide_sums.at[0:1, cols], add(il.astype(F32)))
        hidden_grad += dot(il, wi[:, cols], NT)
    first_grad = norm_back(hidden_grad * gain_one, normed_one, inverse_one)
    fg[s] = first_grad
    br = first_grad.astype(BF16)
    br_k[rs, :] = br
    collect(sums.at[3:4], add(hidden_grad * normed_one))
    collect(sums.at[4:5], add(hidden_grad))
    collect(sums.at[5:6], add(br.astype(F32)))
    return dot(br, wo[...], NT).astype(BF16)


def middle_kernel(seqs, sc, tok, teach, vec, wide_vec, *refs):
    attended, weights, refs = refs[:seqs], refs[seqs : seqs + 9], refs[seqs + 9 :]
    out, fg, sums, wide_sums, a_own, a_give, b_own, b_give = refs[:8]
    grads_in, refs = refs[8 : 8 + seqs], refs[8 + seqs :]
    wo, wi, wu, slope, o_in, g_out, att_k, br_k, hl_k, il_k, act_k, ol_k = refs[:12]
    mine, give, given, w_sem, o_sem, g_sem, c_sem = refs[12:]
    z, y, c, x = position()
    sibling = device(z, y, 1 - c, x)
    line = [None] + [device(z ^ d, y, c, x) for d in range(1, GROUPS)]
    greet([sibling] + line[1:])
    coming, going = {}, {}
    for s in range(seqs):
        for d in range(1, GROUPS):
            sems = o_sem.at[0, s, d], o_sem.at[1, s, d]
            coming[s, d] = send(attended[s].at[z ^ d], o_in.at[s, z], sems, line[d])
        coming[s, 0] = pltpu.make_async_copy(attended[s].at[z], o_in.at[s, z], o_sem.at[0, s, 0])
        coming[s, 0].start()
    copies = [
        weight_copies(full, *weights[3 * i : 3 * i + 3], w_sem, 3 * i)
        for i, full in enumerate((wo, wi, wu))
    ]
    for group in copies:
        for copy in group:
            copy.start()

    def loaded(which):
        for i in which:
            for copy in copies[i]:
                copy.wait()

    rows = tok.shape[1]
    per = o_in.shape[3]
    row = lax.broadcasted_iota(jnp.int32, (rows, 1), 0)
    for s in range(seqs):
        for d in range(GROUPS):
            coming[s, d].wait()
        att = jnp.concatenate([o_in[s, g] for g in range(GROUPS)], 1)
        first, later = (jnp.where(row < sc[2 * s], 1.0, 0.0), jnp.where(row - BLK < sc[2 * s + 1], 1.0, 0.0))
        mask = jnp.where(row < BLK, first, later)
        waits = (lambda: loaded([0]), lambda: loaded([1, 2])) if s == 0 else (lambda: None,) * 2
        found = middle_stage(
            s,
            att,
            mask,
            tok,
            teach,
            vec,
            wide_vec,
            (wo, wi, wu, slope),
            (att_k, br_k, hl_k, il_k, act_k, ol_k),
            (out, fg, sums, wide_sums),
            waits,
        )
        for g in range(GROUPS):
            g_out[s, g] = found[:, g * per : (g + 1) * per]
        for d in range(1, GROUPS):
            sems = g_sem.at[0, s, d], g_sem.at[1, s, d]
            going[s, d] = send(g_out.at[s, z ^ d], grads_in[s].at[z], sems, line[d])
        going[s, 0] = pltpu.make_async_copy(g_out.at[s, z], grads_in[s].at[z], g_sem.at[0, s, 0])
        going[s, 0].start()
    sums[7:8, :] = jnp.zeros((1, sums.shape[1]), F32)

    half = wo.shape[0] // 2
    hidden = wi.shape[1]
    blocks = hidden // (2 * half)

    def weight_grads(target, part):
        def cols(start):
            return pl.ds(pl.multiple_of(start + part * half, 128), half)

        for k in range(2):
            ks = slice(k * half, (k + 1) * half)
            target[k, 0:half, :] = dot(att_k[:, ks], br_k[:, cols(0)], TN).astype(BF16)
            for t in range(blocks):
                target[k, (1 + t) * half : (2 + t) * half, :] = dot(
                    hl_k[:, ks], il_k[:, cols(2 * t * half)], TN
                ).astype(BF16)
            base = (1 + blocks) * half
            for t in range(blocks):
                rows_of = slice((k * blocks + t) * half, (k * blocks + t + 1) * half)
                target[k, base + t * half : base + (t + 1) * half, :] = dot(
                    act_k[:, rows_of], ol_k[:, cols(0)], TN
                ).astype(BF16)

    weight_grads(give, 1 - c)
    core = [
        send(give.at[k], given.at[k], (c_sem.at[0, k], c_sem.at[1, k]), sibling) for k in range(2)
    ]
    weight_grads(mine, c)
    for copy in core:
        copy.wait()
    cut, b_half = a_own.shape[0], b_own.shape[1]
    a_own[...] = add_low(mine[x, 0:cut], given[x, 0:cut])
    a_give[...] = add_low(mine[1 - x, 0:cut], given[1 - x, 0:cut])
    for k in range(2):
        for target, which in ((b_own, y), (b_give, 1 - y)):
            part = pl.ds(pl.multiple_of(cut + which * b_half, 16), b_half)
            target[k] = add_low(mine[k, part], given[k, part])
    for copy in going.values():
        copy.wait()


def cut_of(total):
    return total // 256 * 128


def middle(sc, tok, teach, vec, wide_vec, attended, weights):
    seqs, rows, width = tok.shape
    hidden = wide_vec.shape[1]
    half = width // 2
    total = half + hidden
    cut = cut_of(total)
    dma = pltpu.SemaphoreType.DMA
    narrow, wide = (seqs * rows, width), (seqs * rows, hidden)
    b_shape = jax.ShapeDtypeStruct((2, (total - cut) // 2, half), BF16)
    a_shape = jax.ShapeDtypeStruct((cut, half), BF16)
    groups, _, per = attended[0].shape
    return pl.pallas_call(
        functools.partial(middle_kernel, seqs),
        out_shape=[
            jax.ShapeDtypeStruct(tok.shape, BF16),
            jax.ShapeDtypeStruct(tok.shape, F32),
            jax.ShapeDtypeStruct((8, width), F32),
            jax.ShapeDtypeStruct((1, hidden), F32),
            a_shape,
            a_shape,
            b_shape,
            b_shape,
        ]
        + [jax.ShapeDtypeStruct(a.shape, BF16) for a in attended],
        in_specs=[SMEM] + [VMEM] * 4 + [ANY] * (seqs + 9),
        out_specs=[VMEM] * 8 + [ANY] * seqs,
        scratch_shapes=[
            pltpu.VMEM((width, width), BF16),
            pltpu.VMEM((width, hidden), BF16),
            pltpu.VMEM((hidden, width), BF16),
            pltpu.VMEM((rows, hidden), F32),
            pltpu.VMEM((seqs, groups, rows, per), BF16),
            pltpu.VMEM((seqs, groups, rows, per), BF16),
            pltpu.VMEM(narrow, BF16),
            pltpu.VMEM(narrow, BF16),
            pltpu.VMEM(narrow, BF16),
            pltpu.VMEM(wide, BF16),
            pltpu.VMEM(wide, BF16),
            pltpu.VMEM(narrow, BF16),
            pltpu.VMEM((2, total, half), BF16),
            pltpu.VMEM((2, total, half), BF16),
            pltpu.VMEM((2, total, half), BF16),
            dma((9,)),
            dma((2, seqs, groups)),
            dma((2, seqs, groups)),
            dma((2, 2)),
        ],
        compiler_params=pltpu.CompilerParams(
            vmem_limit_bytes=62 * 2**20, collective_id=3, has_side_effects=True
        ),
        cost_estimate=cost(60),
        name="middle",
    )(sc, tok, teach, vec, wide_vec, *attended, *weights)


def halve_kernel(a_own, a_in, b_own, b_in, a_keep, a_give, b_keep, b_give):
    _, y, _, x = position()
    half = a_keep.shape[0]
    for target, which in ((a_keep, y), (a_give, 1 - y)):
        part = pl.ds(pl.multiple_of(which * half, 16), half)
        target[...] = add_low(a_own[part, :], a_in[part, :])
    for target, which in ((b_keep, x), (b_give, 1 - x)):
        target[...] = add_low(b_own[which], b_in[which])


def halve(a_own, a_in, b_own, b_in):
    a = jax.ShapeDtypeStruct((a_own.shape[0] // 2, a_own.shape[1]), BF16)
    b = jax.ShapeDtypeStruct(b_own.shape[1:], BF16)
    return pl.pallas_call(
        halve_kernel,
        out_shape=[a, a, b, b],
        in_specs=[VMEM] * 4,
        out_specs=[VMEM] * 4,
        compiler_params=ROOM,
        cost_estimate=cost(3),
        name="halve",
    )(a_own, a_in, b_own, b_in)


def sum_kernel(grads, small, *rest):
    ready, rest = rest[:4], rest[4:]
    out, dense_out, small_out, *rest = rest
    acc, from_core, from_x, from_y, from_z, res, vec, vec_in = rest[:8]
    two, a_in, b_in, dense_res, sems, small_sems, d_sems, last_sem = rest[8:]
    z, y, c, x = position()
    sibling, beside, over = device(z, y, 1 - c, x), device(z, 1 - y, c, x), device(z, y, c, 1 - x)
    line = [None] + [device(z ^ d, y, c, x) for d in range(1, GROUPS)]
    parts, rows = grads.shape[0], grads.shape[3]
    half, piece = rows // 2, rows // 8
    own_half = pl.ds(pl.multiple_of(y * half, half), half)
    other_half = pl.ds(pl.multiple_of((1 - y) * half, half), half)

    def piece_of(g):
        return pl.ds(pl.multiple_of(y * half + g * piece, piece), piece)

    greet([sibling, beside, over] + line[1:])

    def pair(k, p):
        return sems.at[0, k, p], sems.at[1, k, p]

    def small_pair(k):
        return small_sems.at[0, k], small_sems.at[1, k]

    core = [
        send(grads.at[p, 1 - c], from_core.at[p], pair(0, p), sibling) for p in range(parts)
    ]
    a_cut = 2 * ready[0].shape[0]
    parts_of = []
    for i, landing in enumerate((a_in, b_in)):
        keep, other = ready[2 * i], ready[2 * i + 1]
        n = keep.shape[0]
        own = two.at[i, 0:n]
        own[...] = add_low(keep[...], other[...])
        parts_of.append((own, landing, n, n // GROUPS, i * a_cut + y * n))

    def d_pair(k, i):
        return d_sems.at[0, k, i], d_sems.at[1, k, i]

    dense_lines = {}
    for i, (own, landing, n, size, _) in enumerate(parts_of):
        for d in range(1, GROUPS):
            src = own.at[pl.ds(pl.multiple_of((z ^ d) * size, 16), size)]
            dense_lines[i, d] = send(src, landing.at[d], d_pair(d, i), line[d])
    short = send(small, vec_in.at[0], small_pair(0), sibling)
    flows = []
    for p in range(parts):
        core[p].wait()
        acc[p] = add_low(grads[p, c], from_core[p])
        if p == 1:
            flows.append(send(acc.at[p, :, other_half], from_y.at[p], pair(1, p), beside))
        else:
            flows.append(send(acc.at[p, 1 - x], from_x.at[p], pair(1, p), over))
    short.wait()
    vec[...] = small[...] + vec_in[0]
    short = send(vec, vec_in.at[1], small_pair(1), over)
    for p in (1, 0, 2):
        flows[p].wait()
        if p == 1:
            for k in range(2):
                acc[p, k, own_half] = add_low(acc[p, k, own_half], from_y[p, k])
            flows[p] = send(acc.at[p, 1 - x, own_half], from_x.at[p, own_half], pair(2, p), over)
        else:
            acc[p, x] = add_low(acc[p, x], from_x[p])
            flows[p] = send(acc.at[p, x, other_half], from_y.at[p, 0], pair(2, p), beside)
    short.wait()
    vec[...] = vec[...] + vec_in[1]
    short = send(vec, vec_in.at[2], small_pair(2), beside)
    lines = {}
    for p in (1, 0, 2):
        flows[p].wait()
        if p == 1:
            acc[p, x, own_half] = add_low(acc[p, x, own_half], from_x[p, own_half])
        else:
            acc[p, x, own_half] = add_low(acc[p, x, own_half], from_y[p, 0])
        for d in range(1, GROUPS):
            lines[p, d] = send(
                acc.at[p, x, piece_of(z ^ d)], from_z.at[p, d], pair(2 + d, p), line[d]
            )
    short.wait()
    vec[...] = vec[...] + vec_in[2]
    vec_in[4 + z] = vec[...]
    shorts = [
        send(vec, vec_in.at[4 + z], small_pair(2 + d), line[d]) for d in range(1, GROUPS)
    ]
    dense_spread = {}
    for i, (own, landing, n, size, base) in enumerate(parts_of):
        total = own[pl.ds(pl.multiple_of(z * size, 16), size), :].astype(F32)
        for d in range(1, GROUPS):
            dense_lines[i, d].wait()
            total += landing[d].astype(F32)
        place = dense_res.at[c, pl.ds(pl.multiple_of(base + z * size, 16), size)]
        place[...] = total.astype(BF16)
        for d in range(1, GROUPS):
            dense_spread[i, d] = send(place, place, d_pair(3 + d, i), line[d])
    spread = {}
    for p in (1, 0, 2):
        total = acc[p, x, piece_of(z)].astype(F32)
        for d in range(1, GROUPS):
            lines[p, d].wait()
            total += from_z[p, d].astype(F32)
        res[c, p, piece_of(z)] = total.astype(BF16)
        for d in range(1, GROUPS):
            spread[p, d] = send(
                res.at[c, p, piece_of(z)],
                res.at[c, p, piece_of(z)],
                pair(5 + d, p),
                line[d],
            )
    for p in (1, 0, 2):
        for d in range(1, GROUPS):
            spread[p, d].wait()
        flows[p] = send(
            res.at[c, p, own_half], res.at[c, p, own_half], pair(9, p), beside
        )
    dense_flows = []
    for i, (own, landing, n, size, base) in enumerate(parts_of):
        for d in range(1, GROUPS):
            dense_spread[i, d].wait()
        place = dense_res.at[c, pl.ds(pl.multiple_of(base, 16), n)]
        dense_flows.append(send(place, place, d_pair(7, i), beside))
    for copy in shorts:
        copy.wait()
    small_out[...] = vec_in[4] + vec_in[5] + (vec_in[6] + vec_in[7])
    for p in (1, 0, 2):
        flows[p].wait()
        flows[p] = send(res.at[c, p], res.at[c, p], pair(10, p), sibling)
    for i, (own, landing, n, size, base) in enumerate(parts_of):
        dense_flows[i].wait()
        place = dense_res.at[c, pl.ds(i * a_cut, 2 * n)]
        dense_flows[i] = send(place, place, d_pair(8, i), sibling)
    for p in (1, 0, 2):
        flows[p].wait()
    for copy in dense_flows:
        copy.wait()
    done = [
        pltpu.make_async_copy(res, out, last_sem.at[0]),
        pltpu.make_async_copy(dense_res, dense_out, last_sem.at[1]),
    ]
    for copy in done:
        copy.start()
    for copy in done:
        copy.wait()


def sum_grads(grads, small, ready):
    parts, _, _, rows, lanes = grads.shape
    a, b = ready[0].shape, ready[2].shape
    total = 2 * (a[0] + b[0])
    most = max(a[0], b[0])
    dma = pltpu.SemaphoreType.DMA
    return pl.pallas_call(
        sum_kernel,
        out_shape=[
            jax.ShapeDtypeStruct((2, parts, rows, lanes), BF16),
            jax.ShapeDtypeStruct((2, total, a[1]), BF16),
            jax.ShapeDtypeStruct(small.shape, F32),
        ],
        in_specs=[VMEM] * 6,
        out_specs=[ANY, ANY, VMEM],
        scratch_shapes=[
            pltpu.VMEM((parts, 2, rows, lanes), BF16),
            pltpu.VMEM((parts, 2, rows, lanes), BF16),
            pltpu.VMEM((parts, rows, lanes), BF16),
            pltpu.VMEM((parts, 2, rows // 2, lanes), BF16),
            pltpu.VMEM((parts, GROUPS, rows // 8, lanes), BF16),
            pltpu.VMEM((2, parts, rows, lanes), BF16),
            pltpu.VMEM(small.shape, F32),
            pltpu.VMEM((8, *small.shape), F32),
            pltpu.VMEM((2, most, a[1]), BF16),
            pltpu.VMEM((GROUPS, a[0] // GROUPS, a[1]), BF16),
            pltpu.VMEM((GROUPS, b[0] // GROUPS, b[1]), BF16),
            pltpu.VMEM((2, total, a[1]), BF16),
            dma((2, 11, parts)),
            dma((2, 6)),
            dma((2, 9, 2)),
            dma((2,)),
        ],
        compiler_params=pltpu.CompilerParams(
            vmem_limit_bytes=48 * 2**20, collective_id=2, has_side_effects=True
        ),
        cost_estimate=cost(50),
        name="sum_grads",
    )(grads, small, *ready)


def pick(table, index):
    places = jnp.arange(table.shape[0], dtype=jnp.int32)
    return jnp.sum(jnp.where(index[..., None] == places, table, 0), -1)


def shards(
    size,
    tokens,
    teacher,
    lengths,
    block_order,
    query_weight,
    query_bias,
    key_weight,
    value_weight,
    value_bias,
    out_weight,
    out_bias,
    gain_one,
    shift_one,
    inner_weight,
    inner_bias,
    outer_weight,
    outer_bias,
    gain_two,
    shift_two,
):
    seqs, rows, width = tokens.shape
    per_plane = size // GROUPS
    blocks_each = rows // BLK
    ctx, x = lax.axis_index("ctx"), lax.axis_index("wa")
    c, place = lax.rem(ctx, 2), lax.rem(ctx, per_plane)
    masks = [1 << b for b in reversed(range(per_plane.bit_length() - 1))]
    offsets = [0]
    for m in masks:
        offsets += [o ^ m for o in offsets]

    def across(value):
        return lax.ppermute(value, "wa", [(0, 1), (1, 0)])

    def flip(value, m):
        return lax.ppermute(value, "ctx", [(i, i ^ m) for i in range(size)])

    lines = [[g * per_plane + r for g in range(GROUPS)] for r in range(per_plane)]

    def turn(value):
        return lax.all_to_all(value, "ctx", 0, 0, axis_index_groups=lines)

    cores = [[i for i in range(size) if i % 2 == k] for k in range(2)]

    def paired(mine):
        sibling = flip(mine, 1)
        return jnp.where(c == 0, jnp.stack([mine, sibling]), jnp.stack([sibling, mine]))

    def reduced(grad):
        four = grad.reshape(2, 2, *grad.shape[1:])
        keep = lax.dynamic_index_in_dim(four, c, 1, False)
        give = lax.dynamic_index_in_dim(four, 1 - c, 1, False)
        keep = add_low(keep, flip(give, 1))
        mine = lax.dynamic_index_in_dim(keep, x, 0, False)
        mine = add_low(mine, across(lax.dynamic_index_in_dim(keep, 1 - x, 0, False)))
        return paired(lax.psum(mine, "ctx", axis_index_groups=cores))

    def reduced_dense(grad):
        four = grad.reshape(2, 2, *grad.shape[1:])
        keep = lax.dynamic_index_in_dim(four, c, 1, False)
        give = lax.dynamic_index_in_dim(four, 1 - c, 1, False)
        keep = add_low(keep, flip(give, 1))
        mine = lax.psum_scatter(
            keep.reshape(-1, keep.shape[-1]), "wa", scatter_dimension=0, tiled=True
        )
        return lax.psum(mine, "ctx", axis_index_groups=cores)

    vectors = (
        query_bias,
        value_bias,
        out_bias,
        gain_one,
        shift_one,
        outer_bias,
        gain_two,
        shift_two,
        inner_bias,
    )
    own_vec = jnp.concatenate(vectors)[None]
    other_vec = across(own_vec)
    pair = jnp.where(
        x == 0, jnp.stack([own_vec, other_vec]), jnp.stack([other_vec, own_vec])
    ).astype(F32)
    half = width // 2
    narrow = pair[:, 0, : 8 * half].reshape(2, 8, half).swapaxes(0, 1).reshape(8, width)
    wide_vec = pair[:, 0, 8 * half :].reshape(1, -1)

    def quarter(weight):
        n = weight.shape[0] // 2
        return lax.dynamic_slice_in_dim(weight, c * n, n, 0)

    first_qkv = across(
        jnp.concatenate([quarter(w) for w in (query_weight, key_weight, value_weight)], 0)
    )
    second_qkv = flip(first_qkv, 1)
    dense_weights = []
    last = first_qkv
    for weight in (out_weight, inner_weight, outer_weight):
        piece, last = lax.optimization_barrier((quarter(weight), last))
        last = across(piece)
        dense_weights += [weight, last, flip(last, 1)]

    count = block_order.shape[0]
    ids = jnp.arange(count, dtype=jnp.int32)
    owner = ids // blocks_each
    index_of = jnp.array([offsets.index(o) for o in range(per_plane)], jnp.int32)
    piece_of = pick(index_of, (owner % per_plane) ^ place)
    spot = (piece_of * GROUPS + owner // per_plane) * blocks_each + ids % blocks_each
    key_order = jnp.sum(jnp.where(block_order[None, :] == ids[:, None], spot[None, :], 0), 1)
    near = jnp.arange(GROUPS * blocks_each, dtype=jnp.int32)
    near_ids = (near // blocks_each * per_plane + place) * blocks_each + near % blocks_each
    near_pos = pick(block_order, near_ids)
    rank = jnp.sum((near_pos[None, :] < near_pos[:, None]).astype(jnp.int32), 1)
    query_order = jnp.sum(jnp.where(rank[None, :] == near[:, None], near[None, :], 0), 1)
    own_pos = pick(block_order, ctx * blocks_each + jnp.arange(blocks_each, dtype=jnp.int32))
    scalars, row_counts = [], []
    for s in range(seqs):
        used = jnp.sum((near_pos * BLK < lengths[s]).astype(jnp.int32))
        head = jnp.concatenate([lengths[s][None], used[None], jnp.zeros((6,), jnp.int32)])
        scalars.append(jnp.concatenate([head, query_order, key_order]))
        row_counts.append(jnp.clip(lengths[s] - own_pos * BLK, 0, BLK))

    projected = project(
        tokens, narrow, query_weight, key_weight, value_weight, first_qkv, second_qkv
    )
    queries, pieces = [], []
    for s in range(seqs):
        kv = turn(projected[2 * s + 1])
        queries.append(turn(projected[2 * s]).reshape(-1, BLK, width // GROUPS))
        held = [kv.reshape(-1, BLK, kv.shape[2])]
        for m in masks:
            held += [flip(piece, m) for piece in held]
        pieces.append(held)

    fused = per_plane == 4
    attended, lses = [], []
    for s in range(seqs):
        o, lse = attend(scalars[s], queries[s], pieces[s])
        attended.append(o.reshape(queries[s].shape))
        lses.append(lse)
    if fused:
        fours = [a.reshape(GROUPS, rows, -1) for a in attended]
        found = middle(
            jnp.concatenate(row_counts), tokens, teacher, narrow[2:], wide_vec, fours, dense_weights
        )
        output, firsts, sums, wide_sums, a_own, a_give, b_own, b_give = found[:8]
        heads_grad = [g.reshape(queries[0].shape) for g in found[8:]]
        first_grads = [firsts[s] for s in range(seqs)]
        a_in, b_in = across(a_give), flip(b_give, 2)
    else:
        dense_out = []
        for s in range(seqs):
            o4 = turn(attended[s].reshape(GROUPS, rows, -1))
            dense_out.append(
                dense(
                    row_counts[s], o4, tokens[s], teacher[s], narrow[2:], wide_vec, dense_weights
                )
            )
        output = jnp.stack([d[0] for d in dense_out])
        first_grads = [d[1] for d in dense_out]
        heads_grad = [turn(d[2]).reshape(queries[s].shape) for s, d in enumerate(dense_out)]
        sums = sum(d[9] for d in dense_out)
        wide_sums = sum(d[10] for d in dense_out)
        dense_sums = [reduced_dense(g) for g in dense_grads([d[3:9] for d in dense_out])]

    dqs, dkvs = [], []
    for s in range(seqs):
        found = attend_back(
            scalars[s], queries[s], heads_grad[s], attended[s], lses[s], pieces[s]
        )
        if fused and s == 0:
            a_in, b_in, *found = lax.optimization_barrier((a_in, b_in, *found))
            a_keep, a_give, b_keep, b_give = halve(a_own, a_in, b_own, b_in)
            a_more, b_more = flip(a_give, 2), across(b_give)
            scalars[1], a_keep, b_keep = lax.optimization_barrier((scalars[1], a_keep, b_keep))
        dqs.append(found[0].reshape(GROUPS, rows, -1))
        dkvs.append([piece.reshape(GROUPS, rows, -1) for piece in found[1:]])
    if fused:
        returned = return_grads(dqs, dkvs)
        dqs, dkvs = returned[0::2], returned[1::2]
    else:
        for s in range(seqs):
            dqs[s] = turn(dqs[s])
            held = dkvs[s]
            for m in reversed(masks):
                n = len(held) // 2
                held = [add_low(mine, flip(theirs, m)) for mine, theirs in zip(held[:n], held[n:])]
            dkvs[s] = turn(held[0])
    tokens_grad, g_qkv, sums_qkv = project_grads(
        tokens,
        first_grads,
        dqs,
        dkvs,
        query_weight,
        key_weight,
        value_weight,
        first_qkv,
        second_qkv,
    )

    loss_part = jnp.sum(sums[6])
    valid = sum(jnp.sum(r) for r in row_counts).astype(F32)
    small = jnp.concatenate(
        [
            sums[:6].reshape(-1),
            sums_qkv[:2].reshape(-1),
            wide_sums[0],
            jnp.stack([loss_part, valid]),
        ]
    )
    small = jnp.pad(small, (0, -small.shape[0] % 1024)).reshape(-1, 128)
    hidden = wide_vec.shape[1]
    if fused:
        qkv, total, small = sum_grads(g_qkv, small, (a_keep, a_more, b_keep, b_more))
        out_grad = total[:, :half].swapaxes(0, 1).reshape(half, width)
        inner_grad = total[:, half : half + hidden // 2].reshape(2, hidden // width, half, half)
        inner_grad = inner_grad.transpose(2, 1, 0, 3).reshape(half, hidden)
        outer_grad = total[:, half + hidden // 2 :].swapaxes(0, 1).reshape(hidden // 2, width)
        dense_sums = (out_grad, inner_grad, outer_grad)
    else:
        small = lax.psum(small, ("ctx", "wa"))
        qkv = reduced(jnp.moveaxis(g_qkv, (2, 1), (0, 1)).reshape(4, 3, -1, 128))
        dense_sums = [paired(g).reshape(-1, g.shape[-1]) for g in dense_sums]
    small = small.reshape(-1)
    qkv = qkv.reshape(6, 3, half, 128).astype(F32)
    query_grad, key_grad, value_grad = (
        qkv[:, i].swapaxes(0, 1).reshape(half, width) for i in range(3)
    )
    out_grad, inner_grad, outer_grad = (g.astype(F32) for g in dense_sums)

    def vector(start, length):
        return lax.dynamic_slice_in_dim(small, start + x * (length // 2), length // 2, 0)

    end = 8 * width
    loss = small[end + hidden] / (small[end + hidden + 1] * width)
    return (
        output,
        tokens_grad,
        query_grad,
        vector(6 * width, width),
        key_grad,
        value_grad,
        vector(7 * width, width),
        out_grad,
        vector(5 * width, width),
        vector(3 * width, width),
        vector(4 * width, width),
        inner_grad,
        vector(end, hidden),
        outer_grad,
        vector(2 * width, width),
        vector(0, width),
        vector(width, width),
        loss,
    )


def solution(mesh):
    row, split, both = P("wa"), P("wa", None), P("wa", "ctx", None)
    placed = (both, both, row, P(), split, row, split, split, row, split, row, row, row)
    placed += (split, row, split, row, row, row)
    return jax.shard_map(
        functools.partial(shards, mesh.shape["ctx"]),
        mesh=mesh,
        in_specs=placed,
        out_specs=(
            both,
            both,
            split,
            row,
            split,
            split,
            row,
            split,
            row,
            row,
            row,
            split,
            row,
            split,
            row,
            row,
            row,
            P(),
        ),
        check_vma=False,
    )
```

```python
import functools
import math

import jax
import jax.numpy as jnp
from jax import lax
from jax.experimental import pallas as pl
from jax.experimental.pallas import tpu as pltpu
from jax.sharding import PartitionSpec as P

DH = 64
BLK = 128
GROUPS = 4
LN2 = math.log(2.0)
NT = (((1,), (1,)), ((), ()))
NN = (((1,), (0,)), ((), ()))
TN = (((0,), (0,)), ((), ()))
F32 = jnp.float32
BF16 = jnp.bfloat16
VMEM = pl.BlockSpec(memory_space=pltpu.VMEM)
SMEM = pl.BlockSpec(memory_space=pltpu.SMEM)
ANY = pl.BlockSpec(memory_space=pl.ANY)
ROOM = pltpu.CompilerParams(vmem_limit_bytes=58 * 2**20)


def dot(left, right, dims=NN):
    return lax.dot_general(left, right, dims, preferred_element_type=F32)


def cost(us):
    return pl.CostEstimate(flops=int(us * 1.15e9), bytes_accessed=1 << 20, transcendentals=0)


def weight_copies(full, own, first, second, sems, base):
    x, c = lax.axis_index("wa"), lax.rem(lax.axis_index("ctx"), 2)
    half = own.shape[0]
    quarter = half // 2
    other = (1 - x) * half
    places = (
        (own, x * half, half),
        (first, other + c * quarter, quarter),
        (second, other + (1 - c) * quarter, quarter),
    )
    return [
        pltpu.make_async_copy(
            src, full.at[pl.ds(pl.multiple_of(start, quarter), size)], sems.at[base + i]
        )
        for i, (src, start, size) in enumerate(places)
    ]


def valid_rows(sc, s, rows):
    row = lax.broadcasted_iota(jnp.int32, (rows, 1), 0)
    first = jnp.where(row < sc[2 * s], 1.0, 0.0)
    later = jnp.where(row - BLK < sc[2 * s + 1], 1.0, 0.0)
    return jnp.where(row < BLK, first, later)


def project_kernel(sc, tok, vec, wq, wk, wv, first, second, *rest):
    seqs, rows, width = tok.shape
    outs, (full, sems) = rest[: 2 * seqs], rest[2 * seqs :]
    quarter = wq.shape[0] // 2
    copies = []
    for i, own in enumerate((wq, wk, wv)):
        part = pl.ds(i * quarter, quarter)
        copies.append(
            weight_copies(full.at[i], own, first.at[part], second.at[part], sems, 3 * i)
        )
    for group in copies:
        for copy in group:
            copy.start()
    flat = tok[...].reshape(seqs * rows, width)
    per = width // GROUPS
    heads = per // DH
    valid = jnp.concatenate([valid_rows(sc, s, rows) for s in range(seqs)], 0) > 0.0
    for copy in copies[1]:
        copy.wait()
    keys = jnp.where(valid, dot(flat, full[1]), 0.0).astype(BF16)
    for copy in copies[2]:
        copy.wait()
    values = jnp.where(valid, dot(flat, full[2]) + vec[1:2, :], 0.0).astype(BF16)
    for s in range(seqs):
        rs = slice(s * rows, (s + 1) * rows)
        for g in range(GROUPS):
            for h in range(heads):
                cols = slice(g * per + h * DH, g * per + (h + 1) * DH)
                outs[2 * s + 1][g, :, h * 128 : (h + 1) * 128] = jnp.concatenate(
                    [keys[rs, cols], values[rs, cols]], 1
                )
    for copy in copies[0]:
        copy.wait()
    queries = ((dot(flat, full[0]) + vec[0:1, :]) * (DH**-0.5 / LN2)).astype(BF16)
    for s in range(seqs):
        rs = slice(s * rows, (s + 1) * rows)
        for g in range(GROUPS):
            outs[2 * s][g] = queries[rs, g * per : (g + 1) * per]


def project(sc, tok, vec, wq, wk, wv, first, second):
    seqs, rows, width = tok.shape
    per = width // GROUPS
    shapes = [
        jax.ShapeDtypeStruct((GROUPS, rows, n), BF16) for _ in range(seqs) for n in (per, 2 * per)
    ]
    return pl.pallas_call(
        project_kernel,
        out_shape=shapes,
        in_specs=[SMEM, VMEM, VMEM] + [ANY] * 5,
        out_specs=[VMEM] * len(shapes),
        scratch_shapes=[pltpu.VMEM((3, width, width), BF16), pltpu.SemaphoreType.DMA((9,))],
        compiler_params=ROOM,
        cost_estimate=cost(5),
        name="project",
    )(sc, tok, vec, wq, wk, wv, first, second)


def load_pieces(pieces, kv, sems):
    per = pieces[0].shape[0]
    copies = [
        pltpu.make_async_copy(piece, kv.at[pl.ds(i * per, per)], sems.at[i])
        for i, piece in enumerate(pieces)
    ]
    for copy in copies:
        copy.start()
    for copy in copies:
        copy.wait()


def forward_kernel(wide, narrow, count, sc, q_ref, *rest):
    pieces, (o_ref, lse_ref, kv_ref, qa, acc, sums, sems) = rest[:count], rest[count:]
    blocks = q_ref.shape[0]
    heads = q_ref.shape[2] // DH
    rows = blocks * BLK
    length = sc[0]
    load_pieces(pieces, kv_ref, sems)

    def gather(h, start, n):
        return jnp.concatenate(
            [kv_ref[sc[8 + blocks + start + i], :, h * 128 : (h + 1) * 128] for i in range(n)], 0
        )

    whole = length // (wide * BLK)
    tail = whole * wide
    tails = (length - tail * BLK + narrow * BLK - 1) // (narrow * BLK)
    for h in range(heads):
        hs = slice(h * DH, (h + 1) * DH)
        own = jnp.concatenate([q_ref[b, :, hs] for b in range(blocks)], 0)
        qa[...] = jnp.concatenate([own, jnp.zeros_like(own)], 1)
        acc[...] = jnp.zeros_like(acc)
        sums[...] = jnp.zeros_like(sums)

        def step(start, n, masked, h=h):
            kv = gather(h, start, n)
            scores = dot(qa[...], kv, NT)
            if masked:
                place = lax.broadcasted_iota(jnp.int32, scores.shape, 1) + start * BLK
                scores = jnp.where(place < length, scores, -1e30)
            p = jnp.exp2(scores)
            sums[...] += sum(p[:, i * 128 : (i + 1) * 128] for i in range(n))
            acc[...] += dot(p.astype(BF16), kv)

        def wide_step(j, _, step=step):
            step(j * wide, wide, False)
            return 0

        def narrow_step(j, _, step=step):
            step(tail + j * narrow, narrow, True)
            return 0

        lax.fori_loop(0, whole, wide_step, 0)
        lax.fori_loop(0, tails, narrow_step, 0)
        total = jnp.sum(sums[...], 1, keepdims=True)
        across = jnp.transpose(jnp.broadcast_to(total, (rows, 128)))[:8]
        good = (jnp.min(across) > 2.0**-80) & (jnp.max(across) < 2.0**100)

        @pl.when(good)
        def _(h=h, hs=hs, total=total, across=across):
            lse_ref[h] = jnp.log2(across)
            o_ref[:, hs] = (acc[:, DH:] * (1.0 / total)).astype(BF16)

        @pl.when(jnp.logical_not(good))
        def _(h=h, hs=hs):
            key_blocks = (length + BLK - 1) // BLK

            def rows_step(t, _):
                part = pl.ds(pl.multiple_of(t * BLK, BLK), BLK)
                q = qa[part, :]

                def scores_of(j):
                    kv = gather(h, j, 1)
                    scores = dot(q, kv, NT)
                    place = lax.broadcasted_iota(jnp.int32, scores.shape, 1) + j * BLK
                    return kv, jnp.where(place < length, scores, -1e30)

                largest = lax.fori_loop(
                    0,
                    key_blocks,
                    lambda j, m: jnp.maximum(m, jnp.max(scores_of(j)[1], 1, keepdims=True)),
                    jnp.full((BLK, 1), -1e30, F32),
                )
                acc[part, :] = jnp.zeros((BLK, 128), F32)
                sums[part, :] = jnp.zeros((BLK, 128), F32)

                def add(j, _):
                    kv, scores = scores_of(j)
                    p = jnp.exp2(scores - largest)
                    sums[part, :] += p
                    acc[part, :] += dot(p.astype(BF16), kv)
                    return 0

                lax.fori_loop(0, key_blocks, add, 0)
                row_total = jnp.sum(sums[part, :], 1, keepdims=True)
                lse = largest + jnp.log2(row_total)
                lse_ref[h, :, part] = jnp.transpose(jnp.broadcast_to(lse, (BLK, 128)))[:8]
                o_ref[part, hs] = (acc[part, :][:, DH:] * (1.0 / row_total)).astype(BF16)
                return 0

            lax.fori_loop(0, rows // BLK, rows_step, 0)


def attend(sc, q, pieces):
    blocks, _, per = q.shape
    rows, heads = blocks * BLK, per // DH
    key_blocks = len(pieces) * pieces[0].shape[0]
    return pl.pallas_call(
        functools.partial(forward_kernel, 8, 2, len(pieces)),
        out_shape=(
            jax.ShapeDtypeStruct((rows, per), BF16),
            jax.ShapeDtypeStruct((heads, 8, rows), F32),
        ),
        in_specs=[SMEM, VMEM] + [ANY] * len(pieces),
        out_specs=(VMEM, VMEM),
        scratch_shapes=[
            pltpu.VMEM((key_blocks, BLK, 2 * per), BF16),
            pltpu.VMEM((rows, 128), BF16),
            pltpu.VMEM((rows, 128), F32),
            pltpu.VMEM((rows, 128), F32),
            pltpu.SemaphoreType.DMA((len(pieces),)),
        ],
        compiler_params=ROOM,
        cost_estimate=cost(20),
        name="attend",
    )(sc, q, *pieces)


def backward_kernel(qn, kn, count, sc, q_ref, do_ref, o_ref, lse_ref, *rest):
    pieces, dq_ref, outs = rest[:count], rest[count], rest[count + 1 : 2 * count + 1]
    kv_ref, both, dkv, dq, lse_row, delta_row, sems = rest[2 * count + 1 :]
    blocks = q_ref.shape[0]
    heads = q_ref.shape[2] // DH
    key_blocks = kv_ref.shape[0]
    tile = qn * BLK
    length, used = sc[0], sc[1]
    whole = length // (kn * BLK)
    parts = (length + kn * BLK - 1) // (kn * BLK)
    tiles = (used + qn - 1) // qn
    ones = jnp.ones((8, DH), BF16)
    load_pieces(pieces, kv_ref, sems)
    for h in range(heads):
        hs = slice(h * DH, (h + 1) * DH)

        def clear(i, _):
            dkv[pl.ds(pl.multiple_of(i * 1024, 1024), 1024), :] = jnp.zeros((1024, 128), F32)
            return 0

        lax.fori_loop(0, key_blocks // 8, clear, 0)
        dq[...] = jnp.zeros_like(dq)

        def prepare(t, _, h=h, hs=hs):
            base = pl.multiple_of(t * (2 * tile), 2 * tile)
            start = pl.multiple_of(t * tile, tile)
            places = [sc[8 + t * qn + i] for i in range(qn)]
            q = jnp.concatenate([q_ref[s, :, hs] for s in places], 0)
            do = jnp.concatenate([do_ref[s, :, hs] for s in places], 0)
            o = jnp.concatenate([o_ref[s, :, hs] for s in places], 0)
            zero = jnp.zeros_like(q)
            both[pl.ds(base, tile), :] = jnp.concatenate([q, zero], 1)
            both[pl.ds(base + tile, tile), :] = jnp.concatenate([zero, do], 1)
            product = do.astype(F32) * o.astype(F32)
            high = product.astype(BF16)
            rest_of = (product - high.astype(F32)).astype(BF16)
            delta_row[:, pl.ds(start, tile)] = dot(ones, high, NT) + dot(ones, rest_of, NT)
            lse_row[:, pl.ds(start, tile)] = jnp.concatenate(
                [lse_ref[h, :, pl.ds(pl.multiple_of(s * BLK, BLK), BLK)] for s in places], 1
            )
            return 0

        lax.fori_loop(0, tiles, prepare, 0)

        def rows_step(t, _, h=h):
            base = pl.multiple_of(t * (2 * tile), 2 * tile)
            span = pl.ds(pl.multiple_of(t * tile, tile), tile)

            def step(j, masked):
                places = [sc[8 + blocks + j * kn + i] for i in range(kn)]
                kv = jnp.concatenate([kv_ref[s, :, h * 128 : (h + 1) * 128] for s in places], 0)
                b = both[pl.ds(base, 2 * tile), :]
                found = dot(kv, b, NT)
                p = jnp.exp2(found[:, :tile] - lse_row[:1, span])
                if masked:
                    place = lax.broadcasted_iota(jnp.int32, p.shape, 0) + j * (kn * BLK)
                    p = jnp.where(place < length, p, 0.0)
                ds = (p * (found[:, tile:] - delta_row[:1, span])).astype(BF16)
                grads = dot(jnp.concatenate([ds, p.astype(BF16)], 1), b)
                for i, s in enumerate(places):
                    dkv[pl.ds(pl.multiple_of(s * BLK, BLK), BLK), :] += grads[
                        i * BLK : (i + 1) * BLK
                    ]
                dq[span, :] += dot(ds, kv, TN)

            def whole_step(j, _):
                step(j, False)
                return 0

            lax.fori_loop(0, whole, whole_step, 0)

            @pl.when(parts > whole)
            def _():
                step(whole, True)

            return 0

        lax.fori_loop(0, tiles, rows_step, 0)
        for i in range(blocks):
            dq_ref[sc[8 + i], :, hs] = (
                dq[i * BLK : (i + 1) * BLK, :DH] * DH**-0.5
            ).astype(BF16)
        level = jnp.where(lax.broadcasted_iota(jnp.int32, (1, 128), 1) < DH, LN2, 1.0)
        per_piece = key_blocks // count
        for n, out in enumerate(outs):
            for i in range(per_piece):
                b = n * per_piece + i
                out[i, :, h * 128 : (h + 1) * 128] = (
                    dkv[b * BLK : (b + 1) * BLK, :] * level
                ).astype(BF16)


def attend_back(sc, q, do, o, lse, pieces):
    blocks, _, per = q.shape
    rows = blocks * BLK
    key_blocks = len(pieces) * pieces[0].shape[0]
    return pl.pallas_call(
        functools.partial(backward_kernel, 4, 4, len(pieces)),
        out_shape=[jax.ShapeDtypeStruct(q.shape, BF16)]
        + [jax.ShapeDtypeStruct(p.shape, BF16) for p in pieces],
        in_specs=[SMEM] + [VMEM] * 4 + [ANY] * len(pieces),
        out_specs=[VMEM] * (1 + len(pieces)),
        scratch_shapes=[
            pltpu.VMEM((key_blocks, BLK, 2 * per), BF16),
            pltpu.VMEM((2 * rows, 128), BF16),
            pltpu.VMEM((key_blocks * BLK, 128), F32),
            pltpu.VMEM((rows, 128), F32),
            pltpu.VMEM((8, rows), F32),
            pltpu.VMEM((8, rows), F32),
            pltpu.SemaphoreType.DMA((len(pieces),)),
        ],
        compiler_params=ROOM,
        cost_estimate=cost(45),
        name="attend_back",
    )(sc, q, do, o, lse, *pieces)


def norm(values):
    centered = values - jnp.mean(values, -1, keepdims=True)
    inverse = lax.rsqrt(jnp.mean(centered * centered, -1, keepdims=True) + 1e-6)
    return centered * inverse, inverse


def norm_back(upstream, normed, inverse):
    return inverse * (
        upstream
        - jnp.mean(upstream, -1, keepdims=True)
        - normed * jnp.mean(upstream * normed, -1, keepdims=True)
    )


def normal_parts(x):
    z = jnp.abs(x) * (0.5**0.5)
    bell = jnp.exp(-0.5 * x * x)
    t = 1.0 / (1.0 + 0.3275911 * z)
    poly = t * (
        0.254829592
        + t * (-0.284496736 + t * (1.421413741 + t * (-1.453152027 + t * 1.061405429)))
    )
    upper = 0.5 * poly * bell
    return jnp.where(x >= 0, 1.0 - upper, upper), bell * (2.0 * math.pi) ** -0.5


def dense_kernel(sc, att4, tok, teach, vec, wide_vec, *rest):
    weights, rest = rest[:9], rest[9:]
    outs, (wo, wi, wu, slope, sems) = rest[:11], rest[11:]
    out, fg, ag, att_o, br_o, hl_o, il_o, act_o, ol_o, sums, wide_sums = outs
    rows, width = tok.shape
    hidden = wi.shape[1]
    tile = 512
    copies = [
        weight_copies(full, *weights[3 * i : 3 * i + 3], sems, 3 * i)
        for i, full in enumerate((wo, wi, wu))
    ]
    for group in copies:
        for copy in group:
            copy.start()
    per = att4.shape[2]
    att = jnp.concatenate([att4[g] for g in range(GROUPS)], 1)
    att_o[...] = att
    row = lax.broadcasted_iota(jnp.int32, (rows, 1), 0)
    mask = jnp.where(
        row < BLK, jnp.where(row < sc[0], 1.0, 0.0), jnp.where(row - BLK < sc[1], 1.0, 0.0)
    )
    out_bias, gain_one, shift_one = vec[0:1, :], vec[1:2, :], vec[2:3, :]
    outer_bias, gain_two, shift_two = vec[3:4, :], vec[4:5, :], vec[5:6, :]
    for copy in copies[0]:
        copy.wait()
    first = tok[...].astype(F32) + dot(att, wo[...]) + out_bias
    normed_one, inverse_one = norm(first)
    hidden_in = normed_one * gain_one + shift_one
    hl = hidden_in.astype(BF16)
    hl_o[...] = hl
    for copy in copies[1] + copies[2]:
        copy.wait()
    second = hidden_in + outer_bias
    for n in range(hidden // tile):
        cols = slice(n * tile, (n + 1) * tile)
        inner = dot(hl, wi[:, cols]) + wide_vec[0:1, cols]
        below, density = normal_parts(inner)
        act = (inner * below).astype(BF16)
        act_o[:, cols] = act
        slope[:, cols] = below + inner * density
        second += dot(act, wu[cols, :])
    normed_two, inverse_two = norm(second)
    final = normed_two * gain_two + shift_two
    out[...] = final.astype(BF16)
    residue = (final - teach[...].astype(F32)) * mask
    add = functools.partial(jnp.sum, axis=0, keepdims=True)
    second_grad = norm_back(residue * gain_two, normed_two, inverse_two)
    ol = second_grad.astype(BF16)
    ol_o[...] = ol
    hidden_grad = second_grad
    for n in range(hidden // tile):
        cols = slice(n * tile, (n + 1) * tile)
        il = (dot(ol, wu[cols, :], NT) * slope[:, cols]).astype(BF16)
        il_o[:, cols] = il
        wide_sums[0:1, cols] = add(il.astype(F32))
        hidden_grad += dot(il, wi[:, cols], NT)
    first_grad = norm_back(hidden_grad * gain_one, normed_one, inverse_one)
    fg[...] = first_grad
    br = first_grad.astype(BF16)
    br_o[...] = br
    att_grad = dot(br, wo[...], NT).astype(BF16)
    for g in range(GROUPS):
        ag[g] = att_grad[:, g * per : (g + 1) * per]
    sums[0:1, :] = add(residue * normed_two)
    sums[1:2, :] = add(residue)
    sums[2:3, :] = add(ol.astype(F32))
    sums[3:4, :] = add(hidden_grad * normed_one)
    sums[4:5, :] = add(hidden_grad)
    sums[5:6, :] = add(br.astype(F32))
    sums[6:7, :] = add(residue * residue)
    sums[7:8, :] = jnp.zeros((1, width), F32)


def dense(sc, att4, tok, teach, vec, wide_vec, weights):
    rows, width = tok.shape
    hidden = wide_vec.shape[1]
    narrow = jax.ShapeDtypeStruct((rows, width), BF16)
    wide = jax.ShapeDtypeStruct((rows, hidden), BF16)
    return pl.pallas_call(
        dense_kernel,
        out_shape=[
            narrow,
            jax.ShapeDtypeStruct((rows, width), F32),
            jax.ShapeDtypeStruct(att4.shape, BF16),
            narrow,
            narrow,
            narrow,
            wide,
            wide,
            narrow,
            jax.ShapeDtypeStruct((8, width), F32),
            jax.ShapeDtypeStruct((1, hidden), F32),
        ],
        in_specs=[SMEM] + [VMEM] * 5 + [ANY] * 9,
        out_specs=[VMEM] * 11,
        scratch_shapes=[
            pltpu.VMEM((width, width), BF16),
            pltpu.VMEM((width, hidden), BF16),
            pltpu.VMEM((hidden, width), BF16),
            pltpu.VMEM((rows, hidden), F32),
            pltpu.SemaphoreType.DMA((9,)),
        ],
        compiler_params=ROOM,
        cost_estimate=cost(15),
        name="dense",
    )(sc, att4, tok, teach, vec, wide_vec, *weights)


def dense_grads_kernel(seqs, *refs):
    ins, (g_out, g_inner, g_outer) = refs[: 6 * seqs], refs[6 * seqs :]
    att, br, hl, il, act, ol = (
        jnp.concatenate([ins[6 * s + i][...] for s in range(seqs)], 0) for i in range(6)
    )
    for target, left, right in ((g_out, att, br), (g_inner, hl, il), (g_outer, act, ol)):
        rows = target.shape[1]
        for n in range(4):
            piece = left[:, n * rows : (n + 1) * rows]
            for t in range(right.shape[1] // 768):
                cols = slice(t * 768, (t + 1) * 768)
                target[n, :, cols] = dot(piece, right[:, cols], TN).astype(BF16)


def dense_grads(saved):
    seqs = len(saved)
    width, hidden = saved[0][0].shape[1], saved[0][3].shape[1]
    return pl.pallas_call(
        functools.partial(dense_grads_kernel, seqs),
        out_shape=[
            jax.ShapeDtypeStruct((4, width // 4, width), BF16),
            jax.ShapeDtypeStruct((4, width // 4, hidden), BF16),
            jax.ShapeDtypeStruct((4, hidden // 4, width), BF16),
        ],
        in_specs=[VMEM] * (6 * seqs),
        out_specs=[VMEM] * 3,
        compiler_params=ROOM,
        cost_estimate=cost(10),
        name="dense_grads",
    )(*[member for group in saved for member in group])


def project_grads_kernel(seqs, paired, sc, tok, *refs):
    count = 2 if paired else 2 * seqs
    if paired:
        fg, refs = refs[0], refs[1:]
        fgs = [fg.at[s] for s in range(seqs)]
    else:
        fgs, refs = refs[:seqs], refs[seqs:]
    grads_in, refs = refs[:count], refs[count:]
    wq, wk, wv, first, second, tg, grads, sums, full, sems = refs
    rows, width = tok.shape[1:]
    per = width // GROUPS
    heads = per // DH
    quarter = wq.shape[0] // 2
    copies = []
    for i, own in enumerate((wq, wk, wv)):
        part = pl.ds(i * quarter, quarter)
        copies += weight_copies(full.at[i], own, first.at[part], second.at[part], sems, 3 * i)
    for copy in copies:
        copy.start()

    def head(i, s, g, h):
        if paired:
            if i == 0:
                return grads_in[0][h, g, :, s * DH : (s + 1) * DH]
            return grads_in[1][h * seqs + s, g, :, (i - 1) * DH : i * DH]
        if i == 0:
            return grads_in[s][g, :, h * DH : (h + 1) * DH]
        start = h * 128 + (i - 1) * DH
        return grads_in[seqs + s][g, :, start : start + DH]

    def whole(i):
        each = [
            jnp.concatenate([head(i, s, g, h) for g in range(GROUPS) for h in range(heads)], 1)
            for s in range(seqs)
        ]
        return jnp.concatenate(each, 0)

    valid = jnp.concatenate([valid_rows(sc, s, rows) for s in range(seqs)], 0) > 0.0
    dq = whole(0)
    halves = [jnp.where(valid, whole(i), jnp.zeros((), BF16)) for i in (1, 2)]
    flat = tok[...].reshape(seqs * rows, width)
    for copy in copies:
        copy.wait()
    total = jnp.concatenate([fgs[s][...] for s in range(seqs)], 0)
    for i, grad in enumerate((dq, *halves)):
        total += dot(grad, full[i], NT)
        found = dot(flat, grad, TN).astype(BF16)
        half = width // 2
        for n in range(2):
            for t in range(width // 128):
                grads[t % 3, t // 3, n, i * half : (i + 1) * half, :] = found[
                    n * half : (n + 1) * half, t * 128 : (t + 1) * 128
                ]
    tg[...] = total.reshape(seqs, rows, width)
    sums[0:1, :] = jnp.sum(dq.astype(F32), 0, keepdims=True)
    sums[1:2, :] = jnp.sum(halves[1].astype(F32), 0, keepdims=True)
    sums[2:8, :] = jnp.zeros((6, width), F32)


def project_grads(sc, tok, fgs, grads, wq, wk, wv, first, second, paired):
    seqs, rows, width = tok.shape
    return pl.pallas_call(
        functools.partial(project_grads_kernel, seqs, paired),
        out_shape=[
            jax.ShapeDtypeStruct(tok.shape, F32),
            jax.ShapeDtypeStruct((3, 2, 2, 3 * (width // 2), 128), BF16),
            jax.ShapeDtypeStruct((8, width), F32),
        ],
        in_specs=[SMEM] + [VMEM] * (1 + len(fgs) + len(grads)) + [ANY] * 5,
        out_specs=[VMEM] * 3,
        scratch_shapes=[pltpu.VMEM((3, width, width), BF16), pltpu.SemaphoreType.DMA((9,))],
        compiler_params=ROOM,
        cost_estimate=cost(10),
        name="project_grads",
    )(sc, tok, *fgs, *grads, wq, wk, wv, first, second)


MESH = pl.DeviceIdType.MESH


def position():
    ctx = lax.axis_index("ctx")
    return ctx // 4, lax.rem(ctx // 2, 2), lax.rem(ctx, 2), lax.axis_index("wa")


def device(z, y, c, x):
    return z * 4 + y * 2 + c, x


def greet(others):
    barrier = pltpu.get_barrier_semaphore()
    for other in others:
        pl.semaphore_signal(barrier, inc=1, device_id=other, device_id_type=MESH)
    pl.semaphore_wait(barrier, len(others))


def send(src, dst, sems, to):
    copy = pltpu.make_async_remote_copy(
        src_ref=src,
        dst_ref=dst,
        send_sem=sems[0],
        recv_sem=sems[1],
        device_id=to,
        device_id_type=MESH,
    )
    copy.start()
    return copy


def add_low(left, right):
    return (left.astype(F32) + right.astype(F32)).astype(BF16)


def back_kernel(seqs, *refs):
    per_seq = 8
    ins = [refs[per_seq * s : per_seq * (s + 1)] for s in range(seqs)]
    a_own, a_give, b_own, b_give, rq, rkv, dense_out, *refs = refs[per_seq * seqs :]
    q_v, do_v, o_v, lse_v, kv_v, both, dkv, dq, delta, obuf, qbuf = refs[:11]
    from_core, from_y, a_v, b_v, a_in, b_in, a2, b2, a2_in, b2_in = refs[11:21]
    az_in, bz_in, dres, in_sem, c_sem, y_sem, z_sem, q_sem, l_sem, x_sem, dz_sem, g_sem = refs[21:]
    z, y, c, x = position()
    sibling, beside, over = device(z, y, 1 - c, x), device(z, 1 - y, c, x), device(z, y, c, 1 - x)
    line = [None] + [device(z ^ d, y, c, x) for d in range(1, GROUPS)]
    greet([sibling, beside, over] + line[1:])

    def pair(sems, *index):
        return sems.at[(0, *index)], sems.at[(1, *index)]

    flow = {}
    flow["a"] = send(a_give, a_in, pair(x_sem, 0), over)
    flow["b"] = send(b_give, b_in, pair(x_sem, 1), beside)
    loads = []
    for s in range(seqs):
        q, do, o, lse, *pieces = ins[s]
        n = pieces[0].shape[0]
        targets = [q_v.at[s], do_v.at[s], o_v.at[s], lse_v.at[s]]
        targets += [kv_v.at[s, pl.ds(i * n, n)] for i in range(len(pieces))]
        group = [
            pltpu.make_async_copy(src, dst, in_sem.at[s, i])
            for i, (src, dst) in enumerate(zip(ins[s], targets))
        ]
        for copy in group:
            copy.start()
        loads.append(group)
    own_loads = [
        pltpu.make_async_copy(a_own, a_v, l_sem.at[0]),
        pltpu.make_async_copy(b_own, b_v, l_sem.at[1]),
    ]
    for copy in own_loads:
        copy.start()

    rows = q_v.shape[1]
    heads = q_v.shape[2] // DH
    keys = kv_v.shape[1]
    tile, ktile = rows // 2, 1024
    quarter = keys // 4
    chunk = quarter // GROUPS
    ones = jnp.ones((8, DH), BF16)
    level = jnp.where(lax.broadcasted_iota(jnp.int32, (1, 128), 1) < DH, LN2, 1.0)
    waits = []

    def group_rows(g):
        return pl.ds(pl.multiple_of(g * chunk, chunk), chunk)

    def core_stage(u):
        flow["c", u] = send(
            obuf.at[u, pl.ds(2 * quarter, 2 * quarter)], from_core.at[u], pair(c_sem, u), sibling
        )

    def y_stage(u):
        flow["c", u].wait()
        second = pl.ds(quarter, quarter)
        obuf[u, second] = add_low(obuf[u, second], from_core[u, second])
        flow["y", u] = send(obuf.at[u, second], from_y.at[u], pair(y_sem, u), beside)
        obuf[u, 0:quarter] = add_low(obuf[u, 0:quarter], from_core[u, 0:quarter])

    def z_stage(u):
        flow["y", u].wait()
        obuf[u, 0:quarter] = add_low(obuf[u, 0:quarter], from_y[u])
        for d in range(1, GROUPS):
            src = obuf.at[u, group_rows(z ^ d)]
            waits.append(send(src, rkv.at[u, z], pair(z_sem, u, d), line[d]))
        own = pltpu.make_async_copy(obuf.at[u, group_rows(z)], rkv.at[u, z], z_sem.at[0, u, 0])
        own.start()
        waits.append(own)

    def q_stage(h):
        for d in range(1, GROUPS):
            waits.append(send(qbuf.at[h, z ^ d], rq.at[h, z], pair(q_sem, h, d), line[d]))
        own = pltpu.make_async_copy(qbuf.at[h, z], rq.at[h, z], q_sem.at[0, h, 0])
        own.start()
        waits.append(own)

    a_half, b_half = a2.shape[1], b2.shape[1]

    def dense_second():
        for copy in own_loads:
            copy.wait()
        flow["a"].wait()
        for slot, which in ((0, y), (1, 1 - y)):
            part = pl.ds(pl.multiple_of(which * a_half, 16), a_half)
            a2[slot] = add_low(a_v[part, :], a_in[part, :])
        flow["a"] = send(a2.at[1], a2_in, pair(x_sem, 2), beside)
        flow["b"].wait()
        for slot, which in ((0, x), (1, 1 - x)):
            b2[slot] = add_low(b_v[which], b_in[which])
        flow["b"] = send(b2.at[1], b2_in, pair(x_sem, 3), over)

    def dense_third():
        for i, (name, held, arrived, landing) in enumerate(
            (("a", a2, a2_in, az_in), ("b", b2, b2_in, bz_in))
        ):
            flow[name].wait()
            held[0] = add_low(held[0], arrived[...])
            size = held.shape[1] // GROUPS
            for d in range(1, GROUPS):
                src = held.at[0, pl.ds(pl.multiple_of((z ^ d) * size, 16), size)]
                flow["z", i, d] = send(src, landing.at[d], pair(dz_sem, i, d), line[d])

    def dense_fourth():
        base = 0
        for i, (held, landing) in enumerate(((a2, az_in), (b2, bz_in))):
            size = held.shape[1] // GROUPS
            total = held[0, pl.ds(pl.multiple_of(z * size, 16), size), :].astype(F32)
            for d in range(1, GROUPS):
                flow["z", i, d].wait()
                total += landing[d].astype(F32)
            place = dres.at[pl.ds(pl.multiple_of(base + z * size, 16), size)]
            place[...] = total.astype(BF16)
            for d in range(1, GROUPS):
                waits.append(send(place, place, pair(g_sem, i, d), line[d]))
            base += held.shape[1]

    units = [(h, s) for h in range(heads) for s in range(seqs)]
    slots = {}
    for u in range(len(units) - 1):
        slots.setdefault(2 * u + 3, []).append(functools.partial(y_stage, u))
        slots.setdefault(2 * u + 4, []).append(functools.partial(z_stage, u))
    slots.setdefault(4, []).append(dense_second)
    slots.setdefault(6, []).append(dense_third)
    slots.setdefault(11, []).append(dense_fourth)

    for u, (h, s) in enumerate(units):
        hs = slice(h * DH, (h + 1) * DH)
        lanes = slice(h * 128, (h + 1) * 128)
        if h == 0:
            for copy in loads[s]:
                copy.wait()
        for n in range(2):
            for work in slots.get(2 * u + n, []):
                work()
            part = slice(n * tile, (n + 1) * tile)
            q, do, o = q_v[s, part, hs], do_v[s, part, hs], o_v[s, part, hs]
            zero = jnp.zeros_like(q)
            both[0:tile, :] = jnp.concatenate([q, zero], 1)
            both[tile : 2 * tile, :] = jnp.concatenate([zero, do], 1)
            product = do.astype(F32) * o.astype(F32)
            high = product.astype(BF16)
            remains = (product - high.astype(F32)).astype(BF16)
            delta[...] = dot(ones, high, NT) + dot(ones, remains, NT)
            dq[...] = jnp.zeros_like(dq)

            def step(j, _, u=u, s=s, h=h, n=n, part=part, lanes=lanes):
                span = pl.ds(pl.multiple_of(j * ktile, ktile), ktile)
                kv = kv_v[s, span, lanes]
                b = both[...]
                found = dot(kv, b, NT)
                p = jnp.exp2(jnp.minimum(found[:, :tile] - lse_v[s, h, 0:1, part], 1.0))
                ds = (p * (found[:, tile:] - delta[0:1, :])).astype(BF16)
                grads = dot(jnp.concatenate([ds, p.astype(BF16)], 1), b)
                if n == 0:
                    dkv[span, :] = grads
                else:
                    obuf[u, span, :] = ((dkv[span, :] + grads) * level).astype(BF16)
                dq[...] += dot(ds, kv, TN)
                return 0

            lax.fori_loop(0, keys // ktile, step, 0)
            found = (dq[:, :DH] * DH**-0.5).astype(BF16)
            for i in range(2):
                qbuf[h, 2 * n + i, :, s * DH : (s + 1) * DH] = found[
                    i * (tile // 2) : (i + 1) * (tile // 2)
                ]
        core_stage(u)
        if s == seqs - 1:
            q_stage(h)
    last = len(units) - 1
    for n in sorted(n for n in slots if n >= 2 * len(units)):
        for work in slots[n]:
            work()
    y_stage(last)
    z_stage(last)
    for copy in waits:
        copy.wait()
    done = pltpu.make_async_copy(dres, dense_out, l_sem.at[0])
    done.start()
    done.wait()


def attend_back_all(seqs_in, ready):
    seqs = len(seqs_in)
    q, _, _, lse, piece = seqs_in[0][:5]
    rows, per = q.shape
    heads = per // DH
    units = heads * seqs
    keys = 4 * piece.shape[0]
    chunk = rows // GROUPS
    a, b = ready[0].shape, ready[2].shape
    a_half, b_half, half = a[0] // 2, b[1], a[1]
    dma = pltpu.SemaphoreType.DMA
    return pl.pallas_call(
        functools.partial(back_kernel, seqs),
        out_shape=[
            jax.ShapeDtypeStruct((heads, GROUPS, chunk, 128), BF16),
            jax.ShapeDtypeStruct((units, GROUPS, chunk, 128), BF16),
            jax.ShapeDtypeStruct((a_half + b_half, half), BF16),
        ],
        in_specs=[ANY] * (8 * seqs + 4),
        out_specs=[ANY] * 3,
        scratch_shapes=[
            pltpu.VMEM((seqs, rows, per), BF16),
            pltpu.VMEM((seqs, rows, per), BF16),
            pltpu.VMEM((seqs, rows, per), BF16),
            pltpu.VMEM((seqs, *lse.shape), F32),
            pltpu.VMEM((seqs, keys, 2 * per), BF16),
            pltpu.VMEM((rows, 128), BF16),
            pltpu.VMEM((keys, 128), F32),
            pltpu.VMEM((rows // 2, 128), F32),
            pltpu.VMEM((8, rows // 2), F32),
            pltpu.VMEM((units, keys, 128), BF16),
            pltpu.VMEM((heads, GROUPS, chunk, 128), BF16),
            pltpu.VMEM((units, keys // 2, 128), BF16),
            pltpu.VMEM((units, keys // 4, 128), BF16),
            pltpu.VMEM(a, BF16),
            pltpu.VMEM(b, BF16),
            pltpu.VMEM(a, BF16),
            pltpu.VMEM(b, BF16),
            pltpu.VMEM((2, a_half, half), BF16),
            pltpu.VMEM((2, b_half, half), BF16),
            pltpu.VMEM((a_half, half), BF16),
            pltpu.VMEM((b_half, half), BF16),
            pltpu.VMEM((GROUPS, a_half // GROUPS, half), BF16),
            pltpu.VMEM((GROUPS, b_half // GROUPS, half), BF16),
            pltpu.VMEM((a_half + b_half, half), BF16),
            dma((seqs, 8)),
            dma((2, units)),
            dma((2, units)),
            dma((2, units, GROUPS)),
            dma((2, heads, GROUPS)),
            dma((2,)),
            dma((2, 4)),
            dma((2, 2, GROUPS)),
            dma((2, 2, GROUPS)),
        ],
        compiler_params=pltpu.CompilerParams(
            vmem_limit_bytes=62 * 2**20, collective_id=1, has_side_effects=True
        ),
        cost_estimate=cost(120),
        name="attend_back_all",
    )(*[member for group in seqs_in for member in group], *ready)


def middle_stage(s, att, mask, tok, teach, vec, wide_vec, weights, keep, outs, first_done):
    wo, wi, wu, slope = weights
    att_k, br_k, hl_k, il_k, act_k, ol_k = keep
    out, fg, sums, wide_sums = outs
    rows = att.shape[0]
    hidden = wi.shape[1]
    tile = 512
    rs = slice(s * rows, (s + 1) * rows)
    out_bias, gain_one, shift_one = vec[0:1, :], vec[1:2, :], vec[2:3, :]
    outer_bias, gain_two, shift_two = vec[3:4, :], vec[4:5, :], vec[5:6, :]
    add = functools.partial(jnp.sum, axis=0, keepdims=True)

    def collect(target, value):
        if s == 0:
            target[...] = value
        else:
            target[...] += value

    att_k[rs, :] = att
    first_done[0]()
    first = tok[s].astype(F32) + dot(att, wo[...]) + out_bias
    normed_one, inverse_one = norm(first)
    hidden_in = normed_one * gain_one + shift_one
    hl = hidden_in.astype(BF16)
    hl_k[rs, :] = hl
    first_done[1]()
    second = hidden_in + outer_bias
    for n in range(hidden // tile):
        cols = slice(n * tile, (n + 1) * tile)
        inner = dot(hl, wi[:, cols]) + wide_vec[0:1, cols]
        below, density = normal_parts(inner)
        act = (inner * below).astype(BF16)
        act_k[rs, cols] = act
        slope[:, cols] = below + inner * density
        second += dot(act, wu[cols, :])
    normed_two, inverse_two = norm(second)
    final = normed_two * gain_two + shift_two
    out[s] = final.astype(BF16)
    residue = (final - teach[s].astype(F32)) * mask
    collect(sums.at[0:1], add(residue * normed_two))
    collect(sums.at[1:2], add(residue))
    collect(sums.at[6:7], add(residue * residue))
    second_grad = norm_back(residue * gain_two, normed_two, inverse_two)
    ol = second_grad.astype(BF16)
    ol_k[rs, :] = ol
    collect(sums.at[2:3], add(ol.astype(F32)))
    hidden_grad = second_grad
    for n in range(hidden // tile):
        cols = slice(n * tile, (n + 1) * tile)
        il = (dot(ol, wu[cols, :], NT) * slope[:, cols]).astype(BF16)
        il_k[rs, cols] = il
        collect(wide_sums.at[0:1, cols], add(il.astype(F32)))
        hidden_grad += dot(il, wi[:, cols], NT)
    first_grad = norm_back(hidden_grad * gain_one, normed_one, inverse_one)
    fg[s] = first_grad
    br = first_grad.astype(BF16)
    br_k[rs, :] = br
    collect(sums.at[3:4], add(hidden_grad * normed_one))
    collect(sums.at[4:5], add(hidden_grad))
    collect(sums.at[5:6], add(br.astype(F32)))
    return dot(br, wo[...], NT).astype(BF16)


def middle_kernel(seqs, sc, tok, teach, vec, wide_vec, *refs):
    attended, weights, refs = refs[:seqs], refs[seqs : seqs + 9], refs[seqs + 9 :]
    out, fg, sums, wide_sums, a_own, a_give, b_own, b_give = refs[:8]
    grads_in, refs = refs[8 : 8 + seqs], refs[8 + seqs :]
    wo, wi, wu, slope, o_in, g_out, att_k, br_k, hl_k, il_k, act_k, ol_k = refs[:12]
    mine, give, given, w_sem, o_sem, g_sem, c_sem = refs[12:]
    z, y, c, x = position()
    sibling = device(z, y, 1 - c, x)
    line = [None] + [device(z ^ d, y, c, x) for d in range(1, GROUPS)]
    greet([sibling] + line[1:])
    coming, going = {}, {}
    for s in range(seqs):
        for d in range(1, GROUPS):
            sems = o_sem.at[0, s, d], o_sem.at[1, s, d]
            coming[s, d] = send(attended[s].at[z ^ d], o_in.at[s, z], sems, line[d])
        coming[s, 0] = pltpu.make_async_copy(attended[s].at[z], o_in.at[s, z], o_sem.at[0, s, 0])
        coming[s, 0].start()
    copies = [
        weight_copies(full, *weights[3 * i : 3 * i + 3], w_sem, 3 * i)
        for i, full in enumerate((wo, wi, wu))
    ]
    for group in copies:
        for copy in group:
            copy.start()

    def loaded(which):
        for i in which:
            for copy in copies[i]:
                copy.wait()

    rows = tok.shape[1]
    per = o_in.shape[3]
    for s in range(seqs):
        for d in range(GROUPS):
            coming[s, d].wait()
        att = jnp.concatenate([o_in[s, g] for g in range(GROUPS)], 1)
        mask = valid_rows(sc, s, rows)
        waits = (lambda: loaded([0]), lambda: loaded([1, 2])) if s == 0 else (lambda: None,) * 2
        found = middle_stage(
            s,
            att,
            mask,
            tok,
            teach,
            vec,
            wide_vec,
            (wo, wi, wu, slope),
            (att_k, br_k, hl_k, il_k, act_k, ol_k),
            (out, fg, sums, wide_sums),
            waits,
        )
        for g in range(GROUPS):
            g_out[s, g] = found[:, g * per : (g + 1) * per]
        for d in range(1, GROUPS):
            sems = g_sem.at[0, s, d], g_sem.at[1, s, d]
            going[s, d] = send(g_out.at[s, z ^ d], grads_in[s].at[z], sems, line[d])
        going[s, 0] = pltpu.make_async_copy(g_out.at[s, z], grads_in[s].at[z], g_sem.at[0, s, 0])
        going[s, 0].start()
    sums[7:8, :] = jnp.zeros((1, sums.shape[1]), F32)

    half = wo.shape[0] // 2
    hidden = wi.shape[1]
    blocks = hidden // (2 * half)

    def weight_grads(target, part):
        def cols(start):
            return pl.ds(pl.multiple_of(start + part * half, 128), half)

        for k in range(2):
            ks = slice(k * half, (k + 1) * half)
            target[k, 0:half, :] = dot(att_k[:, ks], br_k[:, cols(0)], TN).astype(BF16)
            for t in range(blocks):
                target[k, (1 + t) * half : (2 + t) * half, :] = dot(
                    hl_k[:, ks], il_k[:, cols(2 * t * half)], TN
                ).astype(BF16)
            base = (1 + blocks) * half
            for t in range(blocks):
                rows_of = slice((k * blocks + t) * half, (k * blocks + t + 1) * half)
                target[k, base + t * half : base + (t + 1) * half, :] = dot(
                    act_k[:, rows_of], ol_k[:, cols(0)], TN
                ).astype(BF16)

    weight_grads(give, 1 - c)
    core = [
        send(give.at[k], given.at[k], (c_sem.at[0, k], c_sem.at[1, k]), sibling) for k in range(2)
    ]
    weight_grads(mine, c)
    for copy in core:
        copy.wait()
    cut, b_half = a_own.shape[0], b_own.shape[1]
    a_own[...] = add_low(mine[x, 0:cut], given[x, 0:cut])
    a_give[...] = add_low(mine[1 - x, 0:cut], given[1 - x, 0:cut])
    for k in range(2):
        for target, which in ((b_own, y), (b_give, 1 - y)):
            part = pl.ds(pl.multiple_of(cut + which * b_half, 16), b_half)
            target[k] = add_low(mine[k, part], given[k, part])
    for copy in going.values():
        copy.wait()


def cut_of(total):
    return total // 256 * 128


def middle(sc, tok, teach, vec, wide_vec, attended, weights):
    seqs, rows, width = tok.shape
    hidden = wide_vec.shape[1]
    half = width // 2
    total = half + hidden
    cut = cut_of(total)
    dma = pltpu.SemaphoreType.DMA
    narrow, wide = (seqs * rows, width), (seqs * rows, hidden)
    b_shape = jax.ShapeDtypeStruct((2, (total - cut) // 2, half), BF16)
    a_shape = jax.ShapeDtypeStruct((cut, half), BF16)
    groups, _, per = attended[0].shape
    return pl.pallas_call(
        functools.partial(middle_kernel, seqs),
        out_shape=[
            jax.ShapeDtypeStruct(tok.shape, BF16),
            jax.ShapeDtypeStruct(tok.shape, F32),
            jax.ShapeDtypeStruct((8, width), F32),
            jax.ShapeDtypeStruct((1, hidden), F32),
            a_shape,
            a_shape,
            b_shape,
            b_shape,
        ]
        + [jax.ShapeDtypeStruct(a.shape, BF16) for a in attended],
        in_specs=[SMEM] + [VMEM] * 4 + [ANY] * (seqs + 9),
        out_specs=[VMEM] * 8 + [ANY] * seqs,
        scratch_shapes=[
            pltpu.VMEM((width, width), BF16),
            pltpu.VMEM((width, hidden), BF16),
            pltpu.VMEM((hidden, width), BF16),
            pltpu.VMEM((rows, hidden), F32),
            pltpu.VMEM((seqs, groups, rows, per), BF16),
            pltpu.VMEM((seqs, groups, rows, per), BF16),
            pltpu.VMEM(narrow, BF16),
            pltpu.VMEM(narrow, BF16),
            pltpu.VMEM(narrow, BF16),
            pltpu.VMEM(wide, BF16),
            pltpu.VMEM(wide, BF16),
            pltpu.VMEM(narrow, BF16),
            pltpu.VMEM((2, total, half), BF16),
            pltpu.VMEM((2, total, half), BF16),
            pltpu.VMEM((2, total, half), BF16),
            dma((9,)),
            dma((2, seqs, groups)),
            dma((2, seqs, groups)),
            dma((2, 2)),
        ],
        compiler_params=pltpu.CompilerParams(
            vmem_limit_bytes=62 * 2**20, collective_id=3, has_side_effects=True
        ),
        cost_estimate=cost(60),
        name="middle",
    )(sc, tok, teach, vec, wide_vec, *attended, *weights)


def sum_kernel(grads, small, *rest):
    ready, out, dense_out, small_out, *rest = rest
    acc, from_core, from_x, from_y, from_z, res, vec, vec_in, dense_res = rest[:9]
    sems, small_sems, d_sems, last_sem = rest[9:]
    z, y, c, x = position()
    sibling, beside, over = device(z, y, 1 - c, x), device(z, 1 - y, c, x), device(z, y, c, 1 - x)
    line = [None] + [device(z ^ d, y, c, x) for d in range(1, GROUPS)]
    parts, rows = grads.shape[0], grads.shape[3]
    half, piece = rows // 2, rows // 8
    own_half = pl.ds(pl.multiple_of(y * half, half), half)
    other_half = pl.ds(pl.multiple_of((1 - y) * half, half), half)

    def piece_of(g):
        return pl.ds(pl.multiple_of(y * half + g * piece, piece), piece)

    greet([sibling, beside, over] + line[1:])

    def pair(k, p):
        return sems.at[0, k, p], sems.at[1, k, p]

    def small_pair(k):
        return small_sems.at[0, k], small_sems.at[1, k]

    core = [
        send(grads.at[p, 1 - c], from_core.at[p], pair(0, p), sibling) for p in range(parts)
    ]
    a_half = cut_of(dense_res.shape[1]) // 2
    b_half = ready.shape[0] - a_half
    dense_flows = []
    for i, (start, n, base) in enumerate(((0, a_half, 0), (a_half, b_half, 2 * a_half))):
        place = dense_res.at[c, pl.ds(pl.multiple_of(base + y * n, 16), n)]
        src = ready.at[pl.ds(start, n)]
        dense_flows.append(send(src, place, (d_sems.at[0, 0, i], d_sems.at[1, 0, i]), beside))
        place[...] = src[...]
    short = send(small, vec_in.at[0], small_pair(0), sibling)
    flows = []
    for p in range(parts):
        core[p].wait()
        acc[p] = add_low(grads[p, c], from_core[p])
        if p == 1:
            flows.append(send(acc.at[p, :, other_half], from_y.at[p], pair(1, p), beside))
        else:
            flows.append(send(acc.at[p, 1 - x], from_x.at[p], pair(1, p), over))
    short.wait()
    vec[...] = small[...] + vec_in[0]
    short = send(vec, vec_in.at[1], small_pair(1), over)
    for p in (1, 0, 2):
        flows[p].wait()
        if p == 1:
            for k in range(2):
                acc[p, k, own_half] = add_low(acc[p, k, own_half], from_y[p, k])
            flows[p] = send(acc.at[p, 1 - x, own_half], from_x.at[p, own_half], pair(2, p), over)
        else:
            acc[p, x] = add_low(acc[p, x], from_x[p])
            flows[p] = send(acc.at[p, x, other_half], from_y.at[p, 0], pair(2, p), beside)
    short.wait()
    vec[...] = vec[...] + vec_in[1]
    short = send(vec, vec_in.at[2], small_pair(2), beside)
    lines = {}
    for p in (1, 0, 2):
        flows[p].wait()
        if p == 1:
            acc[p, x, own_half] = add_low(acc[p, x, own_half], from_x[p, own_half])
        else:
            acc[p, x, own_half] = add_low(acc[p, x, own_half], from_y[p, 0])
        for d in range(1, GROUPS):
            lines[p, d] = send(
                acc.at[p, x, piece_of(z ^ d)], from_z.at[p, d], pair(2 + d, p), line[d]
            )
    short.wait()
    vec[...] = vec[...] + vec_in[2]
    vec_in[4 + z] = vec[...]
    shorts = [
        send(vec, vec_in.at[4 + z], small_pair(2 + d), line[d]) for d in range(1, GROUPS)
    ]
    spread = {}
    for p in (1, 0, 2):
        total = acc[p, x, piece_of(z)].astype(F32)
        for d in range(1, GROUPS):
            lines[p, d].wait()
            total += from_z[p, d].astype(F32)
        res[c, p, piece_of(z)] = total.astype(BF16)
        for d in range(1, GROUPS):
            spread[p, d] = send(
                res.at[c, p, piece_of(z)],
                res.at[c, p, piece_of(z)],
                pair(5 + d, p),
                line[d],
            )
    for p in (1, 0, 2):
        for d in range(1, GROUPS):
            spread[p, d].wait()
        flows[p] = send(
            res.at[c, p, own_half], res.at[c, p, own_half], pair(9, p), beside
        )
    for i, (base, n) in enumerate(((0, 2 * a_half), (2 * a_half, 2 * b_half))):
        dense_flows[i].wait()
        place = dense_res.at[c, pl.ds(base, n)]
        dense_flows[i] = send(place, place, (d_sems.at[0, 1, i], d_sems.at[1, 1, i]), sibling)
    for copy in shorts:
        copy.wait()
    small_out[...] = vec_in[4] + vec_in[5] + (vec_in[6] + vec_in[7])
    for p in (1, 0, 2):
        flows[p].wait()
        flows[p] = send(res.at[c, p], res.at[c, p], pair(10, p), sibling)
    for p in (1, 0, 2):
        flows[p].wait()
    for copy in dense_flows:
        copy.wait()
    done = [
        pltpu.make_async_copy(res, out, last_sem.at[0]),
        pltpu.make_async_copy(dense_res, dense_out, last_sem.at[1]),
    ]
    for copy in done:
        copy.start()
    for copy in done:
        copy.wait()


def sum_grads(grads, small, ready):
    parts, _, _, rows, lanes = grads.shape
    total, half = 2 * ready.shape[0], ready.shape[1]
    dma = pltpu.SemaphoreType.DMA
    return pl.pallas_call(
        sum_kernel,
        out_shape=[
            jax.ShapeDtypeStruct((2, parts, rows, lanes), BF16),
            jax.ShapeDtypeStruct((2, total, half), BF16),
            jax.ShapeDtypeStruct(small.shape, F32),
        ],
        in_specs=[VMEM] * 3,
        out_specs=[ANY, ANY, VMEM],
        scratch_shapes=[
            pltpu.VMEM((parts, 2, rows, lanes), BF16),
            pltpu.VMEM((parts, 2, rows, lanes), BF16),
            pltpu.VMEM((parts, rows, lanes), BF16),
            pltpu.VMEM((parts, 2, rows // 2, lanes), BF16),
            pltpu.VMEM((parts, GROUPS, rows // 8, lanes), BF16),
            pltpu.VMEM((2, parts, rows, lanes), BF16),
            pltpu.VMEM(small.shape, F32),
            pltpu.VMEM((8, *small.shape), F32),
            pltpu.VMEM((2, total, half), BF16),
            dma((2, 11, parts)),
            dma((2, 6)),
            dma((2, 2, 2)),
            dma((2,)),
        ],
        compiler_params=pltpu.CompilerParams(
            vmem_limit_bytes=48 * 2**20, collective_id=2, has_side_effects=True
        ),
        cost_estimate=cost(50),
        name="sum_grads",
    )(grads, small, ready)


def unpack_kernel(qkv, total, *refs):
    outs, (narrow, inner, outer, sems) = refs[:6], refs[6:]
    half = qkv.shape[2] // 3
    blocks = inner.shape[1] // (2 * half)
    copies = []

    def leave(src, i):
        copy = pltpu.make_async_copy(src, outs[i], sems.at[i])
        copy.start()
        copies.append(copy)

    for k in range(2):
        cols = slice(k * half, (k + 1) * half)
        outer[:, cols] = total[k, (1 + blocks) * half :].astype(F32)
    leave(outer, 5)
    for k in range(2):
        for t in range(blocks):
            cols = slice((2 * t + k) * half, (2 * t + k + 1) * half)
            inner[:, cols] = total[k, (1 + t) * half : (2 + t) * half].astype(F32)
    leave(inner, 4)
    for i in range(3):
        for k in range(2):
            for p in range(3):
                cols = slice((3 * k + p) * 128, (3 * k + p + 1) * 128)
                narrow[i, :, cols] = qkv[k, p, i * half : (i + 1) * half].astype(F32)
        leave(narrow.at[i], i)
    for k in range(2):
        narrow[3, :, k * half : (k + 1) * half] = total[k, 0:half].astype(F32)
    leave(narrow.at[3], 3)
    for copy in copies:
        copy.wait()


def unpack(qkv, total, hidden):
    half = total.shape[2]
    narrow = jax.ShapeDtypeStruct((half, 2 * half), F32)
    return pl.pallas_call(
        unpack_kernel,
        out_shape=[narrow] * 4
        + [
            jax.ShapeDtypeStruct((half, hidden), F32),
            jax.ShapeDtypeStruct((hidden // 2, 2 * half), F32),
        ],
        in_specs=[VMEM] * 2,
        out_specs=[ANY] * 6,
        scratch_shapes=[
            pltpu.VMEM((4, half, 2 * half), F32),
            pltpu.VMEM((half, hidden), F32),
            pltpu.VMEM((hidden // 2, 2 * half), F32),
            pltpu.SemaphoreType.DMA((6,)),
        ],
        compiler_params=ROOM,
        cost_estimate=cost(10),
        name="unpack",
    )(qkv, total)


def pick(table, index):
    places = jnp.arange(table.shape[0], dtype=jnp.int32)
    return jnp.sum(jnp.where(index[..., None] == places, table, 0), -1)


def shards(
    size,
    tokens,
    teacher,
    lengths,
    block_order,
    query_weight,
    query_bias,
    key_weight,
    value_weight,
    value_bias,
    out_weight,
    out_bias,
    gain_one,
    shift_one,
    inner_weight,
    inner_bias,
    outer_weight,
    outer_bias,
    gain_two,
    shift_two,
):
    seqs, rows, width = tokens.shape
    per_plane = size // GROUPS
    blocks_each = rows // BLK
    ctx, x = lax.axis_index("ctx"), lax.axis_index("wa")
    c, place = lax.rem(ctx, 2), lax.rem(ctx, per_plane)
    masks = [1 << b for b in reversed(range(per_plane.bit_length() - 1))]
    offsets = [0]
    for m in masks:
        offsets += [o ^ m for o in offsets]

    def across(value):
        return lax.ppermute(value, "wa", [(0, 1), (1, 0)])

    def flip(value, m):
        return lax.ppermute(value, "ctx", [(i, i ^ m) for i in range(size)])

    lines = [[g * per_plane + r for g in range(GROUPS)] for r in range(per_plane)]

    def turn(value):
        return lax.all_to_all(value, "ctx", 0, 0, axis_index_groups=lines)

    cores = [[i for i in range(size) if i % 2 == k] for k in range(2)]

    def paired(mine):
        sibling = flip(mine, 1)
        return jnp.where(c == 0, jnp.stack([mine, sibling]), jnp.stack([sibling, mine]))

    def reduced(grad):
        four = grad.reshape(2, 2, *grad.shape[1:])
        keep = lax.dynamic_index_in_dim(four, c, 1, False)
        give = lax.dynamic_index_in_dim(four, 1 - c, 1, False)
        keep = add_low(keep, flip(give, 1))
        mine = lax.dynamic_index_in_dim(keep, x, 0, False)
        mine = add_low(mine, across(lax.dynamic_index_in_dim(keep, 1 - x, 0, False)))
        return paired(lax.psum(mine, "ctx", axis_index_groups=cores))

    def reduced_dense(grad):
        four = grad.reshape(2, 2, *grad.shape[1:])
        keep = lax.dynamic_index_in_dim(four, c, 1, False)
        give = lax.dynamic_index_in_dim(four, 1 - c, 1, False)
        keep = add_low(keep, flip(give, 1))
        mine = lax.psum_scatter(
            keep.reshape(-1, keep.shape[-1]), "wa", scatter_dimension=0, tiled=True
        )
        return lax.psum(mine, "ctx", axis_index_groups=cores)

    vectors = (
        query_bias,
        value_bias,
        out_bias,
        gain_one,
        shift_one,
        outer_bias,
        gain_two,
        shift_two,
        inner_bias,
    )
    own_vec = jnp.concatenate(vectors)[None]
    other_vec = across(own_vec)
    pair = jnp.where(
        x == 0, jnp.stack([own_vec, other_vec]), jnp.stack([other_vec, own_vec])
    ).astype(F32)
    half = width // 2
    narrow = pair[:, 0, : 8 * half].reshape(2, 8, half).swapaxes(0, 1).reshape(8, width)
    wide_vec = pair[:, 0, 8 * half :].reshape(1, -1)

    def quarter(weight):
        n = weight.shape[0] // 2
        return lax.dynamic_slice_in_dim(weight, c * n, n, 0)

    first_qkv = across(
        jnp.concatenate([quarter(w) for w in (query_weight, key_weight, value_weight)], 0)
    )
    second_qkv = flip(first_qkv, 1)
    dense_weights = []
    last = first_qkv
    for weight in (out_weight, inner_weight, outer_weight):
        piece, last = lax.optimization_barrier((quarter(weight), last))
        last = across(piece)
        dense_weights += [weight, last, flip(last, 1)]

    count = block_order.shape[0]
    ids = jnp.arange(count, dtype=jnp.int32)
    owner = ids // blocks_each
    index_of = jnp.array([offsets.index(o) for o in range(per_plane)], jnp.int32)
    piece_of = pick(index_of, (owner % per_plane) ^ place)
    spot = (piece_of * GROUPS + owner // per_plane) * blocks_each + ids % blocks_each
    key_order = jnp.sum(jnp.where(block_order[None, :] == ids[:, None], spot[None, :], 0), 1)
    near = jnp.arange(GROUPS * blocks_each, dtype=jnp.int32)
    near_ids = (near // blocks_each * per_plane + place) * blocks_each + near % blocks_each
    near_pos = pick(block_order, near_ids)
    rank = jnp.sum((near_pos[None, :] < near_pos[:, None]).astype(jnp.int32), 1)
    query_order = jnp.sum(jnp.where(rank[None, :] == near[:, None], near[None, :], 0), 1)
    own_pos = pick(block_order, ctx * blocks_each + jnp.arange(blocks_each, dtype=jnp.int32))
    scalars, row_counts = [], []
    for s in range(seqs):
        used = jnp.sum((near_pos * BLK < lengths[s]).astype(jnp.int32))
        head = jnp.concatenate([lengths[s][None], used[None], jnp.zeros((6,), jnp.int32)])
        scalars.append(jnp.concatenate([head, query_order, key_order]))
        row_counts.append(jnp.clip(lengths[s] - own_pos * BLK, 0, BLK))

    counts = jnp.concatenate(row_counts)
    projected = project(
        counts, tokens, narrow, query_weight, key_weight, value_weight, first_qkv, second_qkv
    )
    queries, pieces = [], []
    for s in range(seqs):
        kv = turn(projected[2 * s + 1])
        queries.append(turn(projected[2 * s]).reshape(-1, BLK, width // GROUPS))
        held = [kv.reshape(-1, BLK, kv.shape[2])]
        for m in masks:
            held += [flip(piece, m) for piece in held]
        pieces.append(held)

    fused = per_plane == 4
    attended, lses = [], []
    for s in range(seqs):
        o, lse = attend(scalars[s], queries[s], pieces[s])
        attended.append(o.reshape(queries[s].shape))
        lses.append(lse)
    if fused:
        fours = [a.reshape(GROUPS, rows, -1) for a in attended]
        found = middle(
            counts, tokens, teacher, narrow[2:], wide_vec, fours, dense_weights
        )
        output, firsts, sums, wide_sums, a_own, a_give, b_own, b_give = found[:8]
        heads_grad = [g.reshape(queries[0].shape) for g in found[8:]]
        ready = (a_own, a_give, b_own, b_give)
    else:
        dense_out = []
        for s in range(seqs):
            o4 = turn(attended[s].reshape(GROUPS, rows, -1))
            dense_out.append(
                dense(
                    row_counts[s], o4, tokens[s], teacher[s], narrow[2:], wide_vec, dense_weights
                )
            )
        output = jnp.stack([d[0] for d in dense_out])
        first_grads = [d[1] for d in dense_out]
        heads_grad = [turn(d[2]).reshape(queries[s].shape) for s, d in enumerate(dense_out)]
        sums = sum(d[9] for d in dense_out)
        wide_sums = sum(d[10] for d in dense_out)
        dense_sums = [reduced_dense(g) for g in dense_grads([d[3:9] for d in dense_out])]

    if fused:
        flat_rows = (GROUPS * rows, width // GROUPS)
        rq, rkv, ready = attend_back_all(
            [
                [
                    *(a.reshape(flat_rows) for a in (queries[s], heads_grad[s], attended[s])),
                    lses[s],
                    *(piece.reshape(-1, piece.shape[2]) for piece in pieces[s]),
                ]
                for s in range(seqs)
            ],
            ready,
        )
        first_grads, grads = [firsts], [rq, rkv]
    else:
        dqs, dkvs = [], []
        for s in range(seqs):
            found = attend_back(
                scalars[s], queries[s], heads_grad[s], attended[s], lses[s], pieces[s]
            )
            dqs.append(turn(found[0].reshape(GROUPS, rows, -1)))
            held = [piece.reshape(GROUPS, rows, -1) for piece in found[1:]]
            for m in reversed(masks):
                n = len(held) // 2
                held = [add_low(mine, flip(theirs, m)) for mine, theirs in zip(held[:n], held[n:])]
            dkvs.append(turn(held[0]))
        grads = dqs + dkvs
    tokens_grad, g_qkv, sums_qkv = project_grads(
        counts,
        tokens,
        first_grads,
        grads,
        query_weight,
        key_weight,
        value_weight,
        first_qkv,
        second_qkv,
        fused,
    )

    loss_part = jnp.sum(sums[6])
    valid = sum(jnp.sum(r) for r in row_counts).astype(F32)
    small = jnp.concatenate(
        [
            sums[:6].reshape(-1),
            sums_qkv[:2].reshape(-1),
            wide_sums[0],
            jnp.stack([loss_part, valid]),
        ]
    )
    small = jnp.pad(small, (0, -small.shape[0] % 1024)).reshape(-1, 128)
    hidden = wide_vec.shape[1]
    if fused:
        qkv, total, small = sum_grads(g_qkv, small, ready)
        query_grad, key_grad, value_grad, out_grad, inner_grad, outer_grad = unpack(
            qkv, total, hidden
        )
    else:
        small = lax.psum(small, ("ctx", "wa"))
        qkv = reduced(jnp.moveaxis(g_qkv, (2, 1), (0, 1)).reshape(4, 3, -1, 128))
        out_grad, inner_grad, outer_grad = (
            paired(g).reshape(-1, g.shape[-1]).astype(F32) for g in dense_sums
        )
        qkv = qkv.reshape(6, 3, half, 128).astype(F32)
        query_grad, key_grad, value_grad = (
            qkv[:, i].swapaxes(0, 1).reshape(half, width) for i in range(3)
        )
    small = small.reshape(-1)

    def vector(start, length):
        return lax.dynamic_slice_in_dim(small, start + x * (length // 2), length // 2, 0)

    end = 8 * width
    loss = small[end + hidden] / (small[end + hidden + 1] * width)
    return (
        output,
        tokens_grad,
        query_grad,
        vector(6 * width, width),
        key_grad,
        value_grad,
        vector(7 * width, width),
        out_grad,
        vector(5 * width, width),
        vector(3 * width, width),
        vector(4 * width, width),
        inner_grad,
        vector(end, hidden),
        outer_grad,
        vector(2 * width, width),
        vector(0, width),
        vector(width, width),
        loss,
    )


def solution(mesh):
    row, split, both = P("wa"), P("wa", None), P("wa", "ctx", None)
    placed = (both, both, row, P(), split, row, split, split, row, split, row, row, row)
    placed += (split, row, split, row, row, row)
    return jax.shard_map(
        functools.partial(shards, mesh.shape["ctx"]),
        mesh=mesh,
        in_specs=placed,
        out_specs=(
            both,
            both,
            split,
            row,
            split,
            split,
            row,
            split,
            row,
            row,
            row,
            split,
            row,
            split,
            row,
            row,
            row,
            P(),
        ),
        check_vma=False,
    )
```

```python
import functools
import math

import jax
import jax.numpy as jnp
from jax import lax
from jax.experimental import pallas as pl
from jax.experimental.pallas import tpu as pltpu
from jax.sharding import PartitionSpec as P

DH = 64
BLK = 128
GROUPS = 4
LN2 = math.log(2.0)
NT = (((1,), (1,)), ((), ()))
NN = (((1,), (0,)), ((), ()))
TN = (((0,), (0,)), ((), ()))
F32 = jnp.float32
BF16 = jnp.bfloat16
VMEM = pl.BlockSpec(memory_space=pltpu.VMEM)
SMEM = pl.BlockSpec(memory_space=pltpu.SMEM)
ANY = pl.BlockSpec(memory_space=pl.ANY)
ROOM = pltpu.CompilerParams(vmem_limit_bytes=58 * 2**20)


def dot(left, right, dims=NN):
    return lax.dot_general(left, right, dims, preferred_element_type=F32)


def cost(us):
    return pl.CostEstimate(flops=int(us * 1.15e9), bytes_accessed=1 << 20, transcendentals=0)


def weight_copies(full, own, first, second, sems, base):
    x, c = lax.axis_index("wa"), lax.rem(lax.axis_index("ctx"), 2)
    half = own.shape[0]
    quarter = half // 2
    other = (1 - x) * half
    places = (
        (own, x * half, half),
        (first, other + c * quarter, quarter),
        (second, other + (1 - c) * quarter, quarter),
    )
    return [
        pltpu.make_async_copy(
            src, full.at[pl.ds(pl.multiple_of(start, quarter), size)], sems.at[base + i]
        )
        for i, (src, start, size) in enumerate(places)
    ]


def valid_rows(sc, s, rows):
    row = lax.broadcasted_iota(jnp.int32, (rows, 1), 0)
    first = jnp.where(row < sc[2 * s], 1.0, 0.0)
    later = jnp.where(row - BLK < sc[2 * s + 1], 1.0, 0.0)
    return jnp.where(row < BLK, first, later)


def half_copies(full, own, other, sems, base):
    x, half = lax.axis_index("wa"), own.shape[0]
    return [
        pltpu.make_async_copy(
            src, full.at[pl.ds(pl.multiple_of(k * half, half), half)], sems.at[base + i]
        )
        for i, (src, k) in enumerate(((own, x), (other, 1 - x)))
    ]


def project_kernel(sc, tok, vec, wq, wk, wv, first, second, *rest):
    seqs, rows, width = tok.shape
    outs, (full, sems) = rest[: 2 * seqs], rest[2 * seqs :]
    quarter = wq.shape[0] // 2
    copies = []
    for i, own in enumerate((wq, wk, wv)):
        part = pl.ds(i * quarter, quarter)
        copies.append(
            weight_copies(full.at[i], own, first.at[part], second.at[part], sems, 3 * i)
        )
    for group in copies:
        for copy in group:
            copy.start()
    flat = tok[...].reshape(seqs * rows, width)
    per = width // GROUPS
    heads = per // DH
    valid = jnp.concatenate([valid_rows(sc, s, rows) for s in range(seqs)], 0) > 0.0
    for copy in copies[1]:
        copy.wait()
    keys = jnp.where(valid, dot(flat, full[1]), 0.0).astype(BF16)
    for copy in copies[2]:
        copy.wait()
    values = jnp.where(valid, dot(flat, full[2]) + vec[1:2, :], 0.0).astype(BF16)
    for s in range(seqs):
        rs = slice(s * rows, (s + 1) * rows)
        for g in range(GROUPS):
            for h in range(heads):
                cols = slice(g * per + h * DH, g * per + (h + 1) * DH)
                outs[2 * s + 1][g, :, h * 128 : (h + 1) * 128] = jnp.concatenate(
                    [keys[rs, cols], values[rs, cols]], 1
                )
    for copy in copies[0]:
        copy.wait()
    queries = ((dot(flat, full[0]) + vec[0:1, :]) * (DH**-0.5 / LN2)).astype(BF16)
    for s in range(seqs):
        rs = slice(s * rows, (s + 1) * rows)
        for g in range(GROUPS):
            outs[2 * s][g] = queries[rs, g * per : (g + 1) * per]


def project(sc, tok, vec, wq, wk, wv, first, second):
    seqs, rows, width = tok.shape
    per = width // GROUPS
    shapes = [
        jax.ShapeDtypeStruct((GROUPS, rows, n), BF16) for _ in range(seqs) for n in (per, 2 * per)
    ]
    return pl.pallas_call(
        project_kernel,
        out_shape=shapes,
        in_specs=[SMEM, VMEM, VMEM] + [ANY] * 5,
        out_specs=[VMEM] * len(shapes),
        scratch_shapes=[pltpu.VMEM((3, width, width), BF16), pltpu.SemaphoreType.DMA((9,))],
        compiler_params=ROOM,
        cost_estimate=cost(5),
        name="project",
    )(sc, tok, vec, wq, wk, wv, first, second)


def load_pieces(pieces, kv, sems):
    per = pieces[0].shape[0]
    copies = [
        pltpu.make_async_copy(piece, kv.at[pl.ds(i * per, per)], sems.at[i])
        for i, piece in enumerate(pieces)
    ]
    for copy in copies:
        copy.start()
    for copy in copies:
        copy.wait()


def forward_kernel(wide, narrow, count, sc, q_ref, *rest):
    pieces, (o_ref, lse_ref, kv_ref, qa, acc, sums, sems) = rest[:count], rest[count:]
    blocks = q_ref.shape[0]
    heads = q_ref.shape[2] // DH
    rows = blocks * BLK
    length = sc[0]
    load_pieces(pieces, kv_ref, sems)

    def gather(h, start, n):
        return jnp.concatenate(
            [kv_ref[sc[8 + blocks + start + i], :, h * 128 : (h + 1) * 128] for i in range(n)], 0
        )

    whole = length // (wide * BLK)
    tail = whole * wide
    tails = (length - tail * BLK + narrow * BLK - 1) // (narrow * BLK)
    for h in range(heads):
        hs = slice(h * DH, (h + 1) * DH)
        own = jnp.concatenate([q_ref[b, :, hs] for b in range(blocks)], 0)
        qa[...] = jnp.concatenate([own, jnp.zeros_like(own)], 1)
        acc[...] = jnp.zeros_like(acc)
        sums[...] = jnp.zeros_like(sums)

        def step(start, n, masked, h=h):
            kv = gather(h, start, n)
            scores = dot(qa[...], kv, NT)
            if masked:
                place = lax.broadcasted_iota(jnp.int32, scores.shape, 1) + start * BLK
                scores = jnp.where(place < length, scores, -1e30)
            p = jnp.exp2(scores)
            sums[...] += sum(p[:, i * 128 : (i + 1) * 128] for i in range(n))
            acc[...] += dot(p.astype(BF16), kv)

        def wide_step(j, _, step=step):
            step(j * wide, wide, False)
            return 0

        def narrow_step(j, _, step=step):
            step(tail + j * narrow, narrow, True)
            return 0

        lax.fori_loop(0, whole, wide_step, 0)
        lax.fori_loop(0, tails, narrow_step, 0)
        total = jnp.sum(sums[...], 1, keepdims=True)
        across = jnp.transpose(jnp.broadcast_to(total, (rows, 128)))[:8]
        good = (jnp.min(across) > 2.0**-80) & (jnp.max(across) < 2.0**100)

        @pl.when(good)
        def _(h=h, hs=hs, total=total, across=across):
            lse_ref[h] = jnp.log2(across)
            o_ref[:, hs] = (acc[:, DH:] * (1.0 / total)).astype(BF16)

        @pl.when(jnp.logical_not(good))
        def _(h=h, hs=hs):
            key_blocks = (length + BLK - 1) // BLK

            def rows_step(t, _):
                part = pl.ds(pl.multiple_of(t * BLK, BLK), BLK)
                q = qa[part, :]

                def scores_of(j):
                    kv = gather(h, j, 1)
                    scores = dot(q, kv, NT)
                    place = lax.broadcasted_iota(jnp.int32, scores.shape, 1) + j * BLK
                    return kv, jnp.where(place < length, scores, -1e30)

                largest = lax.fori_loop(
                    0,
                    key_blocks,
                    lambda j, m: jnp.maximum(m, jnp.max(scores_of(j)[1], 1, keepdims=True)),
                    jnp.full((BLK, 1), -1e30, F32),
                )
                acc[part, :] = jnp.zeros((BLK, 128), F32)
                sums[part, :] = jnp.zeros((BLK, 128), F32)

                def add(j, _):
                    kv, scores = scores_of(j)
                    p = jnp.exp2(scores - largest)
                    sums[part, :] += p
                    acc[part, :] += dot(p.astype(BF16), kv)
                    return 0

                lax.fori_loop(0, key_blocks, add, 0)
                row_total = jnp.sum(sums[part, :], 1, keepdims=True)
                lse = largest + jnp.log2(row_total)
                lse_ref[h, :, part] = jnp.transpose(jnp.broadcast_to(lse, (BLK, 128)))[:8]
                o_ref[part, hs] = (acc[part, :][:, DH:] * (1.0 / row_total)).astype(BF16)
                return 0

            lax.fori_loop(0, rows // BLK, rows_step, 0)


def attend(sc, q, pieces):
    blocks, _, per = q.shape
    rows, heads = blocks * BLK, per // DH
    key_blocks = len(pieces) * pieces[0].shape[0]
    return pl.pallas_call(
        functools.partial(forward_kernel, 8, 2, len(pieces)),
        out_shape=(
            jax.ShapeDtypeStruct((rows, per), BF16),
            jax.ShapeDtypeStruct((heads, 8, rows), F32),
        ),
        in_specs=[SMEM, VMEM] + [ANY] * len(pieces),
        out_specs=(VMEM, VMEM),
        scratch_shapes=[
            pltpu.VMEM((key_blocks, BLK, 2 * per), BF16),
            pltpu.VMEM((rows, 128), BF16),
            pltpu.VMEM((rows, 128), F32),
            pltpu.VMEM((rows, 128), F32),
            pltpu.SemaphoreType.DMA((len(pieces),)),
        ],
        compiler_params=ROOM,
        cost_estimate=cost(20),
        name="attend",
    )(sc, q, *pieces)


def backward_kernel(qn, kn, count, sc, q_ref, do_ref, o_ref, lse_ref, *rest):
    pieces, dq_ref, outs = rest[:count], rest[count], rest[count + 1 : 2 * count + 1]
    kv_ref, both, dkv, dq, lse_row, delta_row, sems = rest[2 * count + 1 :]
    blocks = q_ref.shape[0]
    heads = q_ref.shape[2] // DH
    key_blocks = kv_ref.shape[0]
    tile = qn * BLK
    length, used = sc[0], sc[1]
    whole = length // (kn * BLK)
    parts = (length + kn * BLK - 1) // (kn * BLK)
    tiles = (used + qn - 1) // qn
    ones = jnp.ones((8, DH), BF16)
    load_pieces(pieces, kv_ref, sems)
    for h in range(heads):
        hs = slice(h * DH, (h + 1) * DH)

        def clear(i, _):
            dkv[pl.ds(pl.multiple_of(i * 1024, 1024), 1024), :] = jnp.zeros((1024, 128), F32)
            return 0

        lax.fori_loop(0, key_blocks // 8, clear, 0)
        dq[...] = jnp.zeros_like(dq)

        def prepare(t, _, h=h, hs=hs):
            base = pl.multiple_of(t * (2 * tile), 2 * tile)
            start = pl.multiple_of(t * tile, tile)
            places = [sc[8 + t * qn + i] for i in range(qn)]
            q = jnp.concatenate([q_ref[s, :, hs] for s in places], 0)
            do = jnp.concatenate([do_ref[s, :, hs] for s in places], 0)
            o = jnp.concatenate([o_ref[s, :, hs] for s in places], 0)
            zero = jnp.zeros_like(q)
            both[pl.ds(base, tile), :] = jnp.concatenate([q, zero], 1)
            both[pl.ds(base + tile, tile), :] = jnp.concatenate([zero, do], 1)
            product = do.astype(F32) * o.astype(F32)
            high = product.astype(BF16)
            rest_of = (product - high.astype(F32)).astype(BF16)
            delta_row[:, pl.ds(start, tile)] = dot(ones, high, NT) + dot(ones, rest_of, NT)
            lse_row[:, pl.ds(start, tile)] = jnp.concatenate(
                [lse_ref[h, :, pl.ds(pl.multiple_of(s * BLK, BLK), BLK)] for s in places], 1
            )
            return 0

        lax.fori_loop(0, tiles, prepare, 0)

        def rows_step(t, _, h=h):
            base = pl.multiple_of(t * (2 * tile), 2 * tile)
            span = pl.ds(pl.multiple_of(t * tile, tile), tile)

            def step(j, masked):
                places = [sc[8 + blocks + j * kn + i] for i in range(kn)]
                kv = jnp.concatenate([kv_ref[s, :, h * 128 : (h + 1) * 128] for s in places], 0)
                b = both[pl.ds(base, 2 * tile), :]
                found = dot(kv, b, NT)
                p = jnp.exp2(found[:, :tile] - lse_row[:1, span])
                if masked:
                    place = lax.broadcasted_iota(jnp.int32, p.shape, 0) + j * (kn * BLK)
                    p = jnp.where(place < length, p, 0.0)
                ds = (p * (found[:, tile:] - delta_row[:1, span])).astype(BF16)
                grads = dot(jnp.concatenate([ds, p.astype(BF16)], 1), b)
                for i, s in enumerate(places):
                    dkv[pl.ds(pl.multiple_of(s * BLK, BLK), BLK), :] += grads[
                        i * BLK : (i + 1) * BLK
                    ]
                dq[span, :] += dot(ds, kv, TN)

            def whole_step(j, _):
                step(j, False)
                return 0

            lax.fori_loop(0, whole, whole_step, 0)

            @pl.when(parts > whole)
            def _():
                step(whole, True)

            return 0

        lax.fori_loop(0, tiles, rows_step, 0)
        for i in range(blocks):
            dq_ref[sc[8 + i], :, hs] = (
                dq[i * BLK : (i + 1) * BLK, :DH] * DH**-0.5
            ).astype(BF16)
        level = jnp.where(lax.broadcasted_iota(jnp.int32, (1, 128), 1) < DH, LN2, 1.0)
        per_piece = key_blocks // count
        for n, out in enumerate(outs):
            for i in range(per_piece):
                b = n * per_piece + i
                out[i, :, h * 128 : (h + 1) * 128] = (
                    dkv[b * BLK : (b + 1) * BLK, :] * level
                ).astype(BF16)


def attend_back(sc, q, do, o, lse, pieces):
    blocks, _, per = q.shape
    rows = blocks * BLK
    key_blocks = len(pieces) * pieces[0].shape[0]
    return pl.pallas_call(
        functools.partial(backward_kernel, 4, 4, len(pieces)),
        out_shape=[jax.ShapeDtypeStruct(q.shape, BF16)]
        + [jax.ShapeDtypeStruct(p.shape, BF16) for p in pieces],
        in_specs=[SMEM] + [VMEM] * 4 + [ANY] * len(pieces),
        out_specs=[VMEM] * (1 + len(pieces)),
        scratch_shapes=[
            pltpu.VMEM((key_blocks, BLK, 2 * per), BF16),
            pltpu.VMEM((2 * rows, 128), BF16),
            pltpu.VMEM((key_blocks * BLK, 128), F32),
            pltpu.VMEM((rows, 128), F32),
            pltpu.VMEM((8, rows), F32),
            pltpu.VMEM((8, rows), F32),
            pltpu.SemaphoreType.DMA((len(pieces),)),
        ],
        compiler_params=ROOM,
        cost_estimate=cost(45),
        name="attend_back",
    )(sc, q, do, o, lse, *pieces)


def norm(values):
    centered = values - jnp.mean(values, -1, keepdims=True)
    inverse = lax.rsqrt(jnp.mean(centered * centered, -1, keepdims=True) + 1e-6)
    return centered * inverse, inverse


def norm_back(upstream, normed, inverse):
    return inverse * (
        upstream
        - jnp.mean(upstream, -1, keepdims=True)
        - normed * jnp.mean(upstream * normed, -1, keepdims=True)
    )


def normal_parts(x):
    z = jnp.abs(x) * (0.5**0.5)
    bell = jnp.exp(-0.5 * x * x)
    t = 1.0 / (1.0 + 0.3275911 * z)
    poly = t * (
        0.254829592
        + t * (-0.284496736 + t * (1.421413741 + t * (-1.453152027 + t * 1.061405429)))
    )
    upper = 0.5 * poly * bell
    return jnp.where(x >= 0, 1.0 - upper, upper), bell * (2.0 * math.pi) ** -0.5


def dense_kernel(sc, att4, tok, teach, vec, wide_vec, *rest):
    weights, rest = rest[:9], rest[9:]
    outs, (wo, wi, wu, slope, sems) = rest[:11], rest[11:]
    out, fg, ag, att_o, br_o, hl_o, il_o, act_o, ol_o, sums, wide_sums = outs
    rows, width = tok.shape
    hidden = wi.shape[1]
    tile = 512
    copies = [
        weight_copies(full, *weights[3 * i : 3 * i + 3], sems, 3 * i)
        for i, full in enumerate((wo, wi, wu))
    ]
    for group in copies:
        for copy in group:
            copy.start()
    per = att4.shape[2]
    att = jnp.concatenate([att4[g] for g in range(GROUPS)], 1)
    att_o[...] = att
    row = lax.broadcasted_iota(jnp.int32, (rows, 1), 0)
    mask = jnp.where(
        row < BLK, jnp.where(row < sc[0], 1.0, 0.0), jnp.where(row - BLK < sc[1], 1.0, 0.0)
    )
    out_bias, gain_one, shift_one = vec[0:1, :], vec[1:2, :], vec[2:3, :]
    outer_bias, gain_two, shift_two = vec[3:4, :], vec[4:5, :], vec[5:6, :]
    for copy in copies[0]:
        copy.wait()
    first = tok[...].astype(F32) + dot(att, wo[...]) + out_bias
    normed_one, inverse_one = norm(first)
    hidden_in = normed_one * gain_one + shift_one
    hl = hidden_in.astype(BF16)
    hl_o[...] = hl
    for copy in copies[1] + copies[2]:
        copy.wait()
    second = hidden_in + outer_bias
    for n in range(hidden // tile):
        cols = slice(n * tile, (n + 1) * tile)
        inner = dot(hl, wi[:, cols]) + wide_vec[0:1, cols]
        below, density = normal_parts(inner)
        act = (inner * below).astype(BF16)
        act_o[:, cols] = act
        slope[:, cols] = below + inner * density
        second += dot(act, wu[cols, :])
    normed_two, inverse_two = norm(second)
    final = normed_two * gain_two + shift_two
    out[...] = final.astype(BF16)
    residue = (final - teach[...].astype(F32)) * mask
    add = functools.partial(jnp.sum, axis=0, keepdims=True)
    second_grad = norm_back(residue * gain_two, normed_two, inverse_two)
    ol = second_grad.astype(BF16)
    ol_o[...] = ol
    hidden_grad = second_grad
    for n in range(hidden // tile):
        cols = slice(n * tile, (n + 1) * tile)
        il = (dot(ol, wu[cols, :], NT) * slope[:, cols]).astype(BF16)
        il_o[:, cols] = il
        wide_sums[0:1, cols] = add(il.astype(F32))
        hidden_grad += dot(il, wi[:, cols], NT)
    first_grad = norm_back(hidden_grad * gain_one, normed_one, inverse_one)
    fg[...] = first_grad
    br = first_grad.astype(BF16)
    br_o[...] = br
    att_grad = dot(br, wo[...], NT).astype(BF16)
    for g in range(GROUPS):
        ag[g] = att_grad[:, g * per : (g + 1) * per]
    sums[0:1, :] = add(residue * normed_two)
    sums[1:2, :] = add(residue)
    sums[2:3, :] = add(ol.astype(F32))
    sums[3:4, :] = add(hidden_grad * normed_one)
    sums[4:5, :] = add(hidden_grad)
    sums[5:6, :] = add(br.astype(F32))
    sums[6:7, :] = add(residue * residue)
    sums[7:8, :] = jnp.zeros((1, width), F32)


def dense(sc, att4, tok, teach, vec, wide_vec, weights):
    rows, width = tok.shape
    hidden = wide_vec.shape[1]
    narrow = jax.ShapeDtypeStruct((rows, width), BF16)
    wide = jax.ShapeDtypeStruct((rows, hidden), BF16)
    return pl.pallas_call(
        dense_kernel,
        out_shape=[
            narrow,
            jax.ShapeDtypeStruct((rows, width), F32),
            jax.ShapeDtypeStruct(att4.shape, BF16),
            narrow,
            narrow,
            narrow,
            wide,
            wide,
            narrow,
            jax.ShapeDtypeStruct((8, width), F32),
            jax.ShapeDtypeStruct((1, hidden), F32),
        ],
        in_specs=[SMEM] + [VMEM] * 5 + [ANY] * 9,
        out_specs=[VMEM] * 11,
        scratch_shapes=[
            pltpu.VMEM((width, width), BF16),
            pltpu.VMEM((width, hidden), BF16),
            pltpu.VMEM((hidden, width), BF16),
            pltpu.VMEM((rows, hidden), F32),
            pltpu.SemaphoreType.DMA((9,)),
        ],
        compiler_params=ROOM,
        cost_estimate=cost(15),
        name="dense",
    )(sc, att4, tok, teach, vec, wide_vec, *weights)


def dense_grads_kernel(seqs, *refs):
    ins, (g_out, g_inner, g_outer) = refs[: 6 * seqs], refs[6 * seqs :]
    att, br, hl, il, act, ol = (
        jnp.concatenate([ins[6 * s + i][...] for s in range(seqs)], 0) for i in range(6)
    )
    for target, left, right in ((g_out, att, br), (g_inner, hl, il), (g_outer, act, ol)):
        rows = target.shape[1]
        for n in range(4):
            piece = left[:, n * rows : (n + 1) * rows]
            for t in range(right.shape[1] // 768):
                cols = slice(t * 768, (t + 1) * 768)
                target[n, :, cols] = dot(piece, right[:, cols], TN).astype(BF16)


def dense_grads(saved):
    seqs = len(saved)
    width, hidden = saved[0][0].shape[1], saved[0][3].shape[1]
    return pl.pallas_call(
        functools.partial(dense_grads_kernel, seqs),
        out_shape=[
            jax.ShapeDtypeStruct((4, width // 4, width), BF16),
            jax.ShapeDtypeStruct((4, width // 4, hidden), BF16),
            jax.ShapeDtypeStruct((4, hidden // 4, width), BF16),
        ],
        in_specs=[VMEM] * (6 * seqs),
        out_specs=[VMEM] * 3,
        compiler_params=ROOM,
        cost_estimate=cost(10),
        name="dense_grads",
    )(*[member for group in saved for member in group])


def project_grads_kernel(seqs, sc, tok, *refs):
    fgs, refs = refs[:seqs], refs[seqs:]
    grads_in, refs = refs[: 2 * seqs], refs[2 * seqs :]
    wq, wk, wv, first, second, tg, grads, sums, full, sems = refs
    rows, width = tok.shape[1:]
    per = width // GROUPS
    heads = per // DH
    quarter = wq.shape[0] // 2
    copies = []
    for i, own in enumerate((wq, wk, wv)):
        part = pl.ds(i * quarter, quarter)
        copies += weight_copies(full.at[i], own, first.at[part], second.at[part], sems, 3 * i)
    for copy in copies:
        copy.start()

    def head(i, s, g, h):
        if i == 0:
            return grads_in[s][g, :, h * DH : (h + 1) * DH]
        start = h * 128 + (i - 1) * DH
        return grads_in[seqs + s][g, :, start : start + DH]

    def whole(i):
        each = [
            jnp.concatenate([head(i, s, g, h) for g in range(GROUPS) for h in range(heads)], 1)
            for s in range(seqs)
        ]
        return jnp.concatenate(each, 0)

    valid = jnp.concatenate([valid_rows(sc, s, rows) for s in range(seqs)], 0) > 0.0
    dq = whole(0)
    halves = [jnp.where(valid, whole(i), jnp.zeros((), BF16)) for i in (1, 2)]
    flat = tok[...].reshape(seqs * rows, width)
    for copy in copies:
        copy.wait()
    total = jnp.concatenate([fgs[s][...] for s in range(seqs)], 0)
    for i, grad in enumerate((dq, *halves)):
        total += dot(grad, full[i], NT)
        found = dot(flat, grad, TN).astype(BF16)
        half = width // 2
        for n in range(2):
            for t in range(width // 128):
                grads[t % 3, t // 3, n, i * half : (i + 1) * half, :] = found[
                    n * half : (n + 1) * half, t * 128 : (t + 1) * 128
                ]
    tg[...] = total.reshape(seqs, rows, width)
    sums[0:1, :] = jnp.sum(dq.astype(F32), 0, keepdims=True)
    sums[1:2, :] = jnp.sum(halves[1].astype(F32), 0, keepdims=True)
    sums[2:8, :] = jnp.zeros((6, width), F32)


def project_grads(sc, tok, fgs, grads, wq, wk, wv, first, second):
    seqs, rows, width = tok.shape
    return pl.pallas_call(
        functools.partial(project_grads_kernel, seqs),
        out_shape=[
            jax.ShapeDtypeStruct(tok.shape, F32),
            jax.ShapeDtypeStruct((3, 2, 2, 3 * (width // 2), 128), BF16),
            jax.ShapeDtypeStruct((8, width), F32),
        ],
        in_specs=[SMEM] + [VMEM] * (1 + len(fgs) + len(grads)) + [ANY] * 5,
        out_specs=[VMEM] * 3,
        scratch_shapes=[pltpu.VMEM((3, width, width), BF16), pltpu.SemaphoreType.DMA((9,))],
        compiler_params=ROOM,
        cost_estimate=cost(10),
        name="project_grads",
    )(sc, tok, *fgs, *grads, wq, wk, wv, first, second)


MESH = pl.DeviceIdType.MESH


def position():
    ctx = lax.axis_index("ctx")
    return ctx // 4, lax.rem(ctx // 2, 2), lax.rem(ctx, 2), lax.axis_index("wa")


def device(z, y, c, x):
    return z * 4 + y * 2 + c, x


def greet(others):
    barrier = pltpu.get_barrier_semaphore()
    for other in others:
        pl.semaphore_signal(barrier, inc=1, device_id=other, device_id_type=MESH)
    pl.semaphore_wait(barrier, len(others))


def send(src, dst, sems, to):
    copy = pltpu.make_async_remote_copy(
        src_ref=src,
        dst_ref=dst,
        send_sem=sems[0],
        recv_sem=sems[1],
        device_id=to,
        device_id_type=MESH,
    )
    copy.start()
    return copy


def add_low(left, right):
    return (left.astype(F32) + right.astype(F32)).astype(BF16)


def back_kernel(seqs, *refs):
    per_seq = 5
    ins = [refs[per_seq * s : per_seq * (s + 1)] for s in range(seqs)]
    a_own, a_give, b_own, b_give, rq, rkv, dense_out, *refs = refs[per_seq * seqs :]
    q_v, do_v, o_v, lse_v, kv_v, both, dkv, dq, delta, obuf, qbuf = refs[:11]
    from_core, from_y, a_v, b_v, a_in, b_in, a2, b2, a2_in, b2_in = refs[11:21]
    az_in, bz_in, dres, in_sem, c_sem, y_sem, z_sem, q_sem, l_sem, x_sem, dz_sem = refs[21:]
    z, y, c, x = position()
    sibling, beside, over = device(z, y, 1 - c, x), device(z, 1 - y, c, x), device(z, y, c, 1 - x)
    line = [None] + [device(z ^ d, y, c, x) for d in range(1, GROUPS)]
    greet([sibling, beside, over] + line[1:])

    def pair(sems, *index):
        return sems.at[(0, *index)], sems.at[(1, *index)]

    flow = {}
    flow["a"] = send(a_give, a_in, pair(x_sem, 0), over)
    flow["b"] = send(b_give, b_in, pair(x_sem, 1), beside)
    loads = []
    for s in range(seqs):
        targets = [ref.at[s] for ref in (q_v, do_v, o_v, lse_v, kv_v)]
        group = [
            pltpu.make_async_copy(src, dst, in_sem.at[s, i])
            for i, (src, dst) in enumerate(zip(ins[s], targets))
        ]
        for copy in group:
            copy.start()
        loads.append(group)
    own_loads = [
        pltpu.make_async_copy(a_own, a_v, l_sem.at[0]),
        pltpu.make_async_copy(b_own, b_v, l_sem.at[1]),
    ]
    for copy in own_loads:
        copy.start()

    rows = q_v.shape[1]
    heads = q_v.shape[2] // DH
    keys = kv_v.shape[1]
    tile, ktile = rows // 2, 2048
    quarter = keys // 4
    chunk = quarter // GROUPS
    ones = jnp.ones((8, DH), BF16)
    level = jnp.where(lax.broadcasted_iota(jnp.int32, (1, 128), 1) < DH, LN2, 1.0)
    waits = []

    def group_rows(g):
        return pl.ds(pl.multiple_of(g * chunk, chunk), chunk)

    def core_stage(u):
        flow["c", u] = send(
            obuf.at[u, pl.ds(2 * quarter, 2 * quarter)], from_core.at[u], pair(c_sem, u), sibling
        )

    def y_stage(u):
        flow["c", u].wait()
        second = pl.ds(quarter, quarter)
        obuf[u, second] = add_low(obuf[u, second], from_core[u, second])
        flow["y", u] = send(obuf.at[u, second], from_y.at[u], pair(y_sem, u), beside)
        obuf[u, 0:quarter] = add_low(obuf[u, 0:quarter], from_core[u, 0:quarter])

    def z_stage(u):
        flow["y", u].wait()
        obuf[u, 0:quarter] = add_low(obuf[u, 0:quarter], from_y[u])
        for d in range(1, GROUPS):
            src = obuf.at[u, group_rows(z ^ d)]
            waits.append(send(src, rkv.at[u, z], pair(z_sem, u, d), line[d]))
        own = pltpu.make_async_copy(obuf.at[u, group_rows(z)], rkv.at[u, z], z_sem.at[0, u, 0])
        own.start()
        waits.append(own)

    def q_stage(h):
        for d in range(1, GROUPS):
            waits.append(send(qbuf.at[h, z ^ d], rq.at[h, z], pair(q_sem, h, d), line[d]))
        own = pltpu.make_async_copy(qbuf.at[h, z], rq.at[h, z], q_sem.at[0, h, 0])
        own.start()
        waits.append(own)

    a_half, b_half = a2.shape[1], b2.shape[1]

    def dense_second():
        for copy in own_loads:
            copy.wait()
        flow["a"].wait()
        for slot, which in ((0, y), (1, 1 - y)):
            part = pl.ds(pl.multiple_of(which * a_half, 16), a_half)
            a2[slot] = add_low(a_v[part, :], a_in[part, :])
        flow["a"] = send(a2.at[1], a2_in, pair(x_sem, 2), beside)
        flow["b"].wait()
        for slot, which in ((0, x), (1, 1 - x)):
            b2[slot] = add_low(b_v[which], b_in[which])
        flow["b"] = send(b2.at[1], b2_in, pair(x_sem, 3), over)

    low_bit, high_bit = lax.rem(z, 2), z // 2
    parts = (("a", a2, a2_in, az_in), ("b", b2, b2_in, bz_in))

    def rows_at(start, n):
        return pl.ds(pl.multiple_of(start, 16), n)

    def dense_third():
        for i, (name, held, arrived, landing) in enumerate(parts):
            flow[name].wait()
            held[0] = add_low(held[0], arrived[...])
            n = held.shape[1] // 2
            src = held.at[0, rows_at((1 - low_bit) * n, n)]
            flow[name] = send(src, landing.at[0:n], pair(dz_sem, i, 0), line[1])

    def dense_fourth():
        for i, (name, held, _, landing) in enumerate(parts):
            flow[name].wait()
            n = held.shape[1] // 2
            mine = rows_at(low_bit * n, n)
            held[0, mine] = add_low(held[0, mine], landing[0:n])
            src = held.at[0, rows_at(low_bit * n + (1 - high_bit) * (n // 2), n // 2)]
            flow[name] = send(src, landing.at[n : n + n // 2], pair(dz_sem, i, 1), line[2])

    def dense_fifth():
        base = 0
        for name, held, _, landing in parts:
            flow[name].wait()
            n = held.shape[1] // 2
            mine = rows_at(low_bit * n + high_bit * (n // 2), n // 2)
            dres[base : base + n // 2] = add_low(held[0, mine], landing[n : n + n // 2])
            base += n // 2

    units = [(h, s) for h in range(heads) for s in range(seqs)]
    slots = {}
    for u in range(len(units) - 1):
        slots.setdefault(2 * u + 3, []).append(functools.partial(y_stage, u))
        slots.setdefault(2 * u + 5, []).append(functools.partial(z_stage, u))
    slots.setdefault(5, []).append(dense_second)
    slots.setdefault(7, []).append(dense_third)
    slots.setdefault(9, []).append(dense_fourth)
    slots.setdefault(12, []).append(dense_fifth)

    for u, (h, s) in enumerate(units):
        hs = slice(h * DH, (h + 1) * DH)
        lanes = slice(h * 128, (h + 1) * 128)
        if h == 0:
            for copy in loads[s]:
                copy.wait()
        for n in range(2):
            for work in slots.get(2 * u + n, []):
                work()
            part = slice(n * tile, (n + 1) * tile)
            q, do, o = q_v[s, part, hs], do_v[s, part, hs], o_v[s, part, hs]
            zero = jnp.zeros_like(q)
            both[0:tile, :] = jnp.concatenate([q, zero], 1)
            both[tile : 2 * tile, :] = jnp.concatenate([zero, do], 1)
            product = do.astype(F32) * o.astype(F32)
            high = product.astype(BF16)
            remains = (product - high.astype(F32)).astype(BF16)
            delta[...] = dot(ones, high, NT) + dot(ones, remains, NT)
            dq[...] = jnp.zeros_like(dq)

            def step(j, _, u=u, s=s, h=h, n=n, part=part, lanes=lanes):
                span = pl.ds(pl.multiple_of(j * ktile, ktile), ktile)
                kv = kv_v[s, span, lanes]
                b = both[...]
                found = dot(kv, b, NT)
                p = jnp.exp2(jnp.minimum(found[:, :tile] - lse_v[s, h, 0:1, part], 1.0))
                ds = (p * (found[:, tile:] - delta[0:1, :])).astype(BF16)
                grads = dot(jnp.concatenate([ds, p.astype(BF16)], 1), b)
                if n == 0:
                    dkv[span, :] = grads
                else:
                    obuf[u, span, :] = ((dkv[span, :] + grads) * level).astype(BF16)
                dq[...] += dot(ds, kv, TN)
                return 0

            lax.fori_loop(0, keys // ktile, step, 0)
            found = (dq[:, :DH] * DH**-0.5).astype(BF16)
            for i in range(2):
                qbuf[h, 2 * n + i, :, s * DH : (s + 1) * DH] = found[
                    i * (tile // 2) : (i + 1) * (tile // 2)
                ]
        core_stage(u)
        if s == seqs - 1:
            q_stage(h)
    last = len(units) - 1
    for n in sorted(n for n in slots if n >= 2 * len(units)):
        for work in slots[n]:
            work()
    y_stage(last)
    z_stage(last)
    for copy in waits:
        copy.wait()
    done = pltpu.make_async_copy(dres, dense_out, l_sem.at[0])
    done.start()
    done.wait()


def attend_back_all(seqs_in, ready):
    seqs = len(seqs_in)
    q, _, _, lse, held = seqs_in[0]
    rows, per = q.shape
    heads = per // DH
    units = heads * seqs
    keys = held.shape[0]
    chunk = rows // GROUPS
    a, b = ready[0].shape, ready[2].shape
    a_half, b_half, half = a[0] // 2, b[1], a[1]
    dma = pltpu.SemaphoreType.DMA
    return pl.pallas_call(
        functools.partial(back_kernel, seqs),
        out_shape=[
            jax.ShapeDtypeStruct((heads, GROUPS, chunk, 128), BF16),
            jax.ShapeDtypeStruct((units, GROUPS, chunk, 128), BF16),
            jax.ShapeDtypeStruct(((a_half + b_half) // 4, half), BF16),
        ],
        in_specs=[ANY] * (5 * seqs + 4),
        out_specs=[ANY] * 3,
        scratch_shapes=[
            pltpu.VMEM((seqs, rows, per), BF16),
            pltpu.VMEM((seqs, rows, per), BF16),
            pltpu.VMEM((seqs, rows, per), BF16),
            pltpu.VMEM((seqs, *lse.shape), F32),
            pltpu.VMEM((seqs, keys, 2 * per), BF16),
            pltpu.VMEM((rows, 128), BF16),
            pltpu.VMEM((keys, 128), F32),
            pltpu.VMEM((rows // 2, 128), F32),
            pltpu.VMEM((8, rows // 2), F32),
            pltpu.VMEM((units, keys, 128), BF16),
            pltpu.VMEM((heads, GROUPS, chunk, 128), BF16),
            pltpu.VMEM((units, keys // 2, 128), BF16),
            pltpu.VMEM((units, keys // 4, 128), BF16),
            pltpu.VMEM(a, BF16),
            pltpu.VMEM(b, BF16),
            pltpu.VMEM(a, BF16),
            pltpu.VMEM(b, BF16),
            pltpu.VMEM((2, a_half, half), BF16),
            pltpu.VMEM((2, b_half, half), BF16),
            pltpu.VMEM((a_half, half), BF16),
            pltpu.VMEM((b_half, half), BF16),
            pltpu.VMEM((3 * a_half // 4, half), BF16),
            pltpu.VMEM((3 * b_half // 4, half), BF16),
            pltpu.VMEM(((a_half + b_half) // 4, half), BF16),
            dma((seqs, 5)),
            dma((2, units)),
            dma((2, units)),
            dma((2, units, GROUPS)),
            dma((2, heads, GROUPS)),
            dma((2,)),
            dma((2, 4)),
            dma((2, 2, 2)),
        ],
        compiler_params=pltpu.CompilerParams(
            vmem_limit_bytes=62 * 2**20, collective_id=1, has_side_effects=True
        ),
        cost_estimate=cost(120),
        name="attend_back_all",
    )(*[member for group in seqs_in for member in group], *ready)


def start_kernel(seqs, sc, tok, own_vec, wq, wk, wv, wo, wi, wu, *refs):
    q_out, kv_out, refs = refs[:seqs], refs[seqs : 2 * seqs], refs[2 * seqs :]
    vec_out, others, *dense_out = refs[:5]
    full, q_held, kv_held, vec, *sems = refs[5:]
    v_sem, wx_sem, wy_sem, wc_sem, l_sem, dx_sem, dc_sem, q_sem, z_sem, y_sem, c_sem, own_sem = sems
    z, y, c, x = position()
    sibling, beside, over = device(z, y, 1 - c, x), device(z, 1 - y, c, x), device(z, y, c, 1 - x)
    line = [None] + [device(z ^ d, y, c, x) for d in range(1, GROUPS)]
    greet([sibling, beside, over] + line[1:])

    def pair(sem, *index):
        return sem.at[(0, *index)], sem.at[(1, *index)]

    waits = []
    half = wq.shape[0]
    eighth = half // 4

    def rows_of(which, cc, yy):
        start = which * half + (2 * cc + yy) * eighth
        return pl.ds(pl.multiple_of(start, 16), eighth)

    own_rows = pl.ds(pl.multiple_of((2 * c + y) * eighth, 16), eighth)
    vec_flow = send(own_vec, vec.at[x], pair(v_sem), over)
    vec_own = pltpu.make_async_copy(own_vec, vec.at[x], l_sem.at[6])
    vec_own.start()
    flow = {}
    order = (1, 2, 0)
    locals_of = []
    for i in order:
        own = (wq, wk, wv)[i]
        flow["x", i] = send(
            own.at[own_rows], full.at[i, rows_of(x, c, y)], pair(wx_sem, i), over
        )
    for i in order:
        own = (wq, wk, wv)[i]
        place = full.at[i, pl.ds(pl.multiple_of(x * half, half), half)]
        copy = pltpu.make_async_copy(own, place, l_sem.at[i])
        copy.start()
        locals_of.append(copy)

    def after_x(i):
        flow["x", i].wait()
        got = full.at[i, rows_of(1 - x, c, y)]
        flow["y", i] = send(got, got, pair(wy_sem, i), beside)
        flow["c", i, 0] = send(got, got, pair(wc_sem, i, 0), sibling)

    def after_y(i):
        flow["y", i].wait()
        got = full.at[i, rows_of(1 - x, c, 1 - y)]
        flow["c", i, 1] = send(got, got, pair(wc_sem, i, 1), sibling)

    def after_core(i):
        flow["c", i, 0].wait()
        flow["c", i, 1].wait()

    rows, width = tok.shape[1:]
    per = width // GROUPS
    heads = per // DH
    flat = tok[...].reshape(seqs * rows, width)
    valid = jnp.concatenate([valid_rows(sc, s, rows) for s in range(seqs)], 0) > 0.0
    after_x(1)
    after_x(2)
    after_y(1)
    after_x(0)
    dense_weights = (wo, wi, wu)
    for i, weight in enumerate(dense_weights):
        n = weight.shape[0] // 2
        part = pl.ds(pl.multiple_of(c * n, 16), n)
        flow["dx", i] = send(weight.at[part], dense_out[i].at[part], pair(dx_sem, i), over)
    after_y(2)
    vec_flow.wait()
    vec_own.wait()

    def bias(row):
        both = [vec[k, row : row + 1, :].astype(F32) for k in range(2)]
        return jnp.concatenate(both, 1)

    for copy in locals_of:
        copy.wait()
    after_core(1)
    keys = jnp.where(valid, dot(flat, full[1]), 0.0).astype(BF16)
    after_y(0)
    after_core(2)
    values = jnp.where(valid, dot(flat, full[2]) + bias(1), 0.0).astype(BF16)
    for s in range(seqs):
        rs = slice(s * rows, (s + 1) * rows)
        for g in range(GROUPS):
            for h in range(heads):
                cols = slice(g * per + h * DH, g * per + (h + 1) * DH)
                kv_held[s, g, :, h * 128 : (h + 1) * 128] = jnp.concatenate(
                    [keys[rs, cols], values[rs, cols]], 1
                )
        for d in range(1, GROUPS):
            flow["z", s, d] = send(
                kv_held.at[s, z ^ d], kv_out[s].at[0, z], pair(z_sem, s, d), line[d]
            )

    def pass_on(s, d, src):
        g = z ^ d
        flow["ky", s, d] = send(src, kv_out[s].at[1, g], pair(y_sem, s, d), beside)
        waits.append(send(src, kv_out[s].at[2, g], pair(c_sem, s, d, 0), sibling))

    def pass_core(s, d):
        flow["ky", s, d].wait()
        got = kv_out[s].at[1, z ^ d]
        waits.append(send(got, kv_out[s].at[3, z ^ d], pair(c_sem, s, d, 1), sibling))

    for s in range(seqs):
        own = pltpu.make_async_copy(kv_held.at[s, z], kv_out[s].at[0, z], own_sem.at[s, 0])
        own.start()
        waits.append(own)
        pass_on(s, 0, kv_held.at[s, z])
    after_core(0)
    queries = ((dot(flat, full[0]) + bias(0)) * (DH**-0.5 / LN2)).astype(BF16)
    for s in range(seqs):
        rs = slice(s * rows, (s + 1) * rows)
        for g in range(GROUPS):
            q_held[s, g] = queries[rs, g * per : (g + 1) * per]
    for i in range(3):
        place = full.at[i, pl.ds(pl.multiple_of((1 - x) * half, half), half)]
        copy = pltpu.make_async_copy(place, others.at[i], l_sem.at[3 + i])
        copy.start()
        waits.append(copy)
    copy = pltpu.make_async_copy(vec, vec_out, l_sem.at[7])
    copy.start()
    waits.append(copy)
    for s in range(seqs):
        for d in range(1, GROUPS):
            flow["z", s, d].wait()
            pass_on(s, d, kv_out[s].at[0, z ^ d])
            if d > 1:
                pass_core(s, d - 2)
        for d in range(1, GROUPS):
            waits.append(send(q_held.at[s, z ^ d], q_out[s].at[z], pair(q_sem, s, d), line[d]))
        own = pltpu.make_async_copy(q_held.at[s, z], q_out[s].at[z], own_sem.at[s, 1])
        own.start()
        waits.append(own)
        pass_core(s, 2)
        pass_core(s, 3)
    for i, weight in enumerate(dense_weights):
        flow["dx", i].wait()
        n = weight.shape[0] // 2
        got = dense_out[i].at[pl.ds(pl.multiple_of(c * n, 16), n)]
        waits.append(send(got, got, pair(dc_sem, i), sibling))
    for copy in waits:
        copy.wait()


def start(sc, tok, own_vec, weights):
    seqs, rows, width = tok.shape
    per = width // GROUPS
    half = weights[0].shape[0]
    dma = pltpu.SemaphoreType.DMA
    return pl.pallas_call(
        functools.partial(start_kernel, seqs),
        out_shape=[jax.ShapeDtypeStruct((GROUPS, rows, per), BF16)] * seqs
        + [jax.ShapeDtypeStruct((4, GROUPS, rows, 2 * per), BF16)] * seqs
        + [
            jax.ShapeDtypeStruct((2, *own_vec.shape), BF16),
            jax.ShapeDtypeStruct((3, half, width), BF16),
        ]
        + [jax.ShapeDtypeStruct(w.shape, BF16) for w in weights[3:]],
        in_specs=[SMEM, VMEM] + [ANY] * 7,
        out_specs=[ANY] * (2 * seqs + 5),
        scratch_shapes=[
            pltpu.VMEM((3, width, width), BF16),
            pltpu.VMEM((seqs, GROUPS, rows, per), BF16),
            pltpu.VMEM((seqs, GROUPS, rows, 2 * per), BF16),
            pltpu.VMEM((2, *own_vec.shape), BF16),
            dma((2,)),
            dma((2, 3)),
            dma((2, 3)),
            dma((2, 3, 2)),
            dma((8,)),
            dma((2, 3)),
            dma((2, 3)),
            dma((2, seqs, GROUPS)),
            dma((2, seqs, GROUPS)),
            dma((2, seqs, GROUPS)),
            dma((2, seqs, GROUPS, 2)),
            dma((seqs, 2)),
        ],
        compiler_params=pltpu.CompilerParams(
            vmem_limit_bytes=48 * 2**20, collective_id=4, has_side_effects=True
        ),
        cost_estimate=cost(80),
        name="start",
    )(sc, tok, own_vec, *weights)


def middle_stage(s, att, mask, tok, teach, vec, wide_vec, weights, keep, outs, first_done):
    wo, wi, wu, slope = weights
    att_k, br_k, hl_k, il_k, act_k, ol_k = keep
    out, fg, sums, wide_sums = outs
    rows = att.shape[0]
    hidden = wi.shape[1]
    tile = 512
    rs = slice(s * rows, (s + 1) * rows)
    out_bias, gain_one, shift_one = vec[0:1, :], vec[1:2, :], vec[2:3, :]
    outer_bias, gain_two, shift_two = vec[3:4, :], vec[4:5, :], vec[5:6, :]
    add = functools.partial(jnp.sum, axis=0, keepdims=True)

    def collect(target, value):
        if s == 0:
            target[...] = value
        else:
            target[...] += value

    att_k[rs, :] = att
    first_done[0]()
    first = tok[s].astype(F32) + dot(att, wo[...]) + out_bias
    normed_one, inverse_one = norm(first)
    hidden_in = normed_one * gain_one + shift_one
    hl = hidden_in.astype(BF16)
    hl_k[rs, :] = hl
    first_done[1]()
    second = hidden_in + outer_bias
    for n in range(hidden // tile):
        cols = slice(n * tile, (n + 1) * tile)
        inner = dot(hl, wi[:, cols]) + wide_vec[0:1, cols]
        below, density = normal_parts(inner)
        act = (inner * below).astype(BF16)
        act_k[rs, cols] = act
        slope[:, cols] = below + inner * density
        second += dot(act, wu[cols, :])
    normed_two, inverse_two = norm(second)
    final = normed_two * gain_two + shift_two
    out[s] = final.astype(BF16)
    residue = (final - teach[s].astype(F32)) * mask
    collect(sums.at[0:1], add(residue * normed_two))
    collect(sums.at[1:2], add(residue))
    collect(sums.at[6:7], add(residue * residue))
    second_grad = norm_back(residue * gain_two, normed_two, inverse_two)
    ol = second_grad.astype(BF16)
    ol_k[rs, :] = ol
    collect(sums.at[2:3], add(ol.astype(F32)))
    hidden_grad = second_grad
    for n in range(hidden // tile):
        cols = slice(n * tile, (n + 1) * tile)
        il = (dot(ol, wu[cols, :], NT) * slope[:, cols]).astype(BF16)
        il_k[rs, cols] = il
        collect(wide_sums.at[0:1, cols], add(il.astype(F32)))
        hidden_grad += dot(il, wi[:, cols], NT)
    first_grad = norm_back(hidden_grad * gain_one, normed_one, inverse_one)
    fg[s] = first_grad
    br = first_grad.astype(BF16)
    br_k[rs, :] = br
    collect(sums.at[3:4], add(hidden_grad * normed_one))
    collect(sums.at[4:5], add(hidden_grad))
    collect(sums.at[5:6], add(br.astype(F32)))
    return dot(br, wo[...], NT).astype(BF16)


def middle_kernel(seqs, sc, tok, teach, vec, wide_vec, *refs):
    attended, weights, refs = refs[:seqs], refs[seqs : seqs + 6], refs[seqs + 6 :]
    out, fg, sums, wide_sums, a_own, a_give, b_own, b_give = refs[:8]
    grads_in, refs = refs[8 : 8 + seqs], refs[8 + seqs :]
    wo, wi, wu, slope, o_in, g_out, att_k, br_k, hl_k, il_k, act_k, ol_k = refs[:12]
    mine, give, given, w_sem, o_sem, g_sem, c_sem = refs[12:]
    z, y, c, x = position()
    sibling = device(z, y, 1 - c, x)
    line = [None] + [device(z ^ d, y, c, x) for d in range(1, GROUPS)]
    greet([sibling] + line[1:])
    coming, going = {}, {}
    for s in range(seqs):
        for d in range(1, GROUPS):
            sems = o_sem.at[0, s, d], o_sem.at[1, s, d]
            coming[s, d] = send(attended[s].at[z ^ d], o_in.at[s, z], sems, line[d])
        coming[s, 0] = pltpu.make_async_copy(attended[s].at[z], o_in.at[s, z], o_sem.at[0, s, 0])
        coming[s, 0].start()
    copies = [
        half_copies(full, *weights[2 * i : 2 * i + 2], w_sem, 2 * i)
        for i, full in enumerate((wo, wi, wu))
    ]
    for group in copies:
        for copy in group:
            copy.start()

    def loaded(which):
        for i in which:
            for copy in copies[i]:
                copy.wait()

    rows = tok.shape[1]
    per = o_in.shape[3]
    for s in range(seqs):
        for d in range(GROUPS):
            coming[s, d].wait()
        att = jnp.concatenate([o_in[s, g] for g in range(GROUPS)], 1)
        mask = valid_rows(sc, s, rows)
        waits = (lambda: loaded([0]), lambda: loaded([1, 2])) if s == 0 else (lambda: None,) * 2
        found = middle_stage(
            s,
            att,
            mask,
            tok,
            teach,
            vec,
            wide_vec,
            (wo, wi, wu, slope),
            (att_k, br_k, hl_k, il_k, act_k, ol_k),
            (out, fg, sums, wide_sums),
            waits,
        )
        for g in range(GROUPS):
            g_out[s, g] = found[:, g * per : (g + 1) * per]
        for d in range(1, GROUPS):
            sems = g_sem.at[0, s, d], g_sem.at[1, s, d]
            going[s, d] = send(g_out.at[s, z ^ d], grads_in[s].at[z], sems, line[d])
        going[s, 0] = pltpu.make_async_copy(g_out.at[s, z], grads_in[s].at[z], g_sem.at[0, s, 0])
        going[s, 0].start()
    sums[7:8, :] = jnp.zeros((1, sums.shape[1]), F32)

    half = wo.shape[0] // 2
    hidden = wi.shape[1]
    blocks = hidden // (2 * half)

    def weight_grads(target, part):
        def cols(start):
            return pl.ds(pl.multiple_of(start + part * half, 128), half)

        for k in range(2):
            ks = slice(k * half, (k + 1) * half)
            target[k, 0:half, :] = dot(att_k[:, ks], br_k[:, cols(0)], TN).astype(BF16)
            for t in range(blocks):
                target[k, (1 + t) * half : (2 + t) * half, :] = dot(
                    hl_k[:, ks], il_k[:, cols(2 * t * half)], TN
                ).astype(BF16)
            base = (1 + blocks) * half
            for t in range(blocks):
                rows_of = slice((k * blocks + t) * half, (k * blocks + t + 1) * half)
                target[k, base + t * half : base + (t + 1) * half, :] = dot(
                    act_k[:, rows_of], ol_k[:, cols(0)], TN
                ).astype(BF16)

    weight_grads(give, 1 - c)
    core = [
        send(give.at[k], given.at[k], (c_sem.at[0, k], c_sem.at[1, k]), sibling) for k in range(2)
    ]
    weight_grads(mine, c)
    for copy in core:
        copy.wait()
    cut, b_half = a_own.shape[0], b_own.shape[1]
    a_own[...] = add_low(mine[x, 0:cut], given[x, 0:cut])
    a_give[...] = add_low(mine[1 - x, 0:cut], given[1 - x, 0:cut])
    for k in range(2):
        for target, which in ((b_own, y), (b_give, 1 - y)):
            part = pl.ds(pl.multiple_of(cut + which * b_half, 16), b_half)
            target[k] = add_low(mine[k, part], given[k, part])
    for copy in going.values():
        copy.wait()


def cut_of(total):
    return total // 256 * 128


def middle(sc, tok, teach, vec, wide_vec, attended, weights):
    seqs, rows, width = tok.shape
    hidden = wide_vec.shape[1]
    half = width // 2
    total = half + hidden
    cut = cut_of(total)
    dma = pltpu.SemaphoreType.DMA
    narrow, wide = (seqs * rows, width), (seqs * rows, hidden)
    b_shape = jax.ShapeDtypeStruct((2, (total - cut) // 2, half), BF16)
    a_shape = jax.ShapeDtypeStruct((cut, half), BF16)
    groups, _, per = attended[0].shape
    return pl.pallas_call(
        functools.partial(middle_kernel, seqs),
        out_shape=[
            jax.ShapeDtypeStruct(tok.shape, BF16),
            jax.ShapeDtypeStruct(tok.shape, F32),
            jax.ShapeDtypeStruct((8, width), F32),
            jax.ShapeDtypeStruct((1, hidden), F32),
            a_shape,
            a_shape,
            b_shape,
            b_shape,
        ]
        + [jax.ShapeDtypeStruct(a.shape, BF16) for a in attended],
        in_specs=[SMEM] + [VMEM] * 4 + [ANY] * (seqs + 6),
        out_specs=[VMEM] * 8 + [ANY] * seqs,
        scratch_shapes=[
            pltpu.VMEM((width, width), BF16),
            pltpu.VMEM((width, hidden), BF16),
            pltpu.VMEM((hidden, width), BF16),
            pltpu.VMEM((rows, hidden), F32),
            pltpu.VMEM((seqs, groups, rows, per), BF16),
            pltpu.VMEM((seqs, groups, rows, per), BF16),
            pltpu.VMEM(narrow, BF16),
            pltpu.VMEM(narrow, BF16),
            pltpu.VMEM(narrow, BF16),
            pltpu.VMEM(wide, BF16),
            pltpu.VMEM(wide, BF16),
            pltpu.VMEM(narrow, BF16),
            pltpu.VMEM((2, total, half), BF16),
            pltpu.VMEM((2, total, half), BF16),
            pltpu.VMEM((2, total, half), BF16),
            dma((6,)),
            dma((2, seqs, groups)),
            dma((2, seqs, groups)),
            dma((2, 2)),
        ],
        compiler_params=pltpu.CompilerParams(
            vmem_limit_bytes=62 * 2**20, collective_id=3, has_side_effects=True
        ),
        cost_estimate=cost(60),
        name="middle",
    )(sc, tok, teach, vec, wide_vec, *attended, *weights)


def finish_kernel(seqs, sc, tok, fg, rq, rkv, small, ready, wq, wk, wv, others, *rest):
    tg, out, dense_out, small_out, *rest = rest
    full, grads, acc, from_core, from_x, from_y, from_z, res, vec, vec_in, dense_res = rest[:11]
    w_sems, sems, small_sems, d_sems, last_sem = rest[11:]
    z, y, c, x = position()
    sibling, beside, over = device(z, y, 1 - c, x), device(z, 1 - y, c, x), device(z, y, c, 1 - x)
    line = [None] + [device(z ^ d, y, c, x) for d in range(1, GROUPS)]
    greet([sibling, beside, over] + line[1:])

    a_half = cut_of(dense_res.shape[1]) // 2
    b_half = dense_res.shape[1] // 2 - a_half
    low_bit, high_bit = lax.rem(z, 2), z // 2
    dense_parts = ((0, a_half, y * a_half), (a_half // 4, b_half, 2 * a_half + y * b_half))

    def dense_rows(start, n):
        return dense_res.at[c, pl.ds(pl.multiple_of(start, 16), n)]

    def d_pair(k, i):
        return d_sems.at[0, k, i], d_sems.at[1, k, i]

    dense_flows = []
    for i, (start, n, base) in enumerate(dense_parts):
        place = dense_rows(base + low_bit * (n // 2) + high_bit * (n // 4), n // 4)
        src = ready.at[start : start + n // 4]
        place[...] = src[...]
        dense_flows.append(send(src, place, d_pair(0, i), line[2]))

    def dense_near():
        for i, (_, n, base) in enumerate(dense_parts):
            dense_flows[i].wait()
            place = dense_rows(base + low_bit * (n // 2), n // 2)
            dense_flows[i] = send(place, place, d_pair(1, i), line[1])

    def dense_y():
        for i, (_, n, base) in enumerate(dense_parts):
            dense_flows[i].wait()
            place = dense_rows(base, n)
            dense_flows[i] = send(place, place, d_pair(2, i), beside)

    def dense_core():
        for i, (_, n, _) in enumerate(dense_parts):
            dense_flows[i].wait()
            place = dense_res.at[c, pl.ds(2 * a_half * i, 2 * n)]
            dense_flows[i] = send(place, place, d_pair(3, i), sibling)

    rows, width = tok.shape[1:]
    heads = width // GROUPS // DH
    copies = []
    for i, own in enumerate((wq, wk, wv)):
        copies += half_copies(full.at[i], own, others.at[i], w_sems, 2 * i)
    for copy in copies:
        copy.start()

    def head(i, s, g, h):
        if i == 0:
            return rq[h, g, :, s * DH : (s + 1) * DH]
        return rkv[h * seqs + s, g, :, (i - 1) * DH : i * DH]

    def whole(i):
        each = [
            jnp.concatenate([head(i, s, g, h) for g in range(GROUPS) for h in range(heads)], 1)
            for s in range(seqs)
        ]
        return jnp.concatenate(each, 0)

    valid = jnp.concatenate([valid_rows(sc, s, rows) for s in range(seqs)], 0) > 0.0
    parted = [whole(0)] + [jnp.where(valid, whole(i), jnp.zeros((), BF16)) for i in (1, 2)]
    flat = tok[...].reshape(seqs * rows, width)
    wide = width // 2
    for i, grad in enumerate(parted):
        found = dot(flat, grad, TN).astype(BF16)
        for n in range(2):
            for t in range(width // 128):
                grads[t % 3, t // 3, n, i * wide : (i + 1) * wide, :] = found[
                    n * wide : (n + 1) * wide, t * 128 : (t + 1) * 128
                ]
    vec[...] = small[...]
    tiles = width // 128
    for i, grad in ((0, parted[0]), (1, parted[2])):
        total = jnp.sum(grad.astype(F32), 0, keepdims=True)
        for t in range(tiles):
            row = (6 + i) * tiles + t
            vec[row : row + 1, :] = total[:, t * 128 : (t + 1) * 128]

    parts, rows_each = grads.shape[0], grads.shape[3]
    half, piece = rows_each // 2, rows_each // 8
    own_half = pl.ds(pl.multiple_of(y * half, half), half)
    other_half = pl.ds(pl.multiple_of((1 - y) * half, half), half)

    def piece_of(g):
        return pl.ds(pl.multiple_of(y * half + g * piece, piece), piece)

    def pair(k, p):
        return sems.at[0, k, p], sems.at[1, k, p]

    def small_pair(k):
        return small_sems.at[0, k], small_sems.at[1, k]

    core = [
        send(grads.at[p, 1 - c], from_core.at[p], pair(0, p), sibling) for p in range(parts)
    ]
    short = send(vec, vec_in.at[0], small_pair(0), sibling)
    flows = []
    for p in range(parts):
        core[p].wait()
        acc[p] = add_low(grads[p, c], from_core[p])
        if p == 1:
            flows.append(send(acc.at[p, :, other_half], from_y.at[p], pair(1, p), beside))
        else:
            flows.append(send(acc.at[p, 1 - x], from_x.at[p], pair(1, p), over))
    dense_near()
    for copy in copies:
        copy.wait()
    total = jnp.concatenate([fg[s] for s in range(seqs)], 0)
    for i, grad in enumerate(parted):
        total += dot(grad, full[i], NT)
    tg[...] = total.reshape(seqs, rows, width)
    short.wait()
    vec_in[8] = vec[...] + vec_in[0]
    short = send(vec_in.at[8], vec_in.at[1], small_pair(1), over)
    for p in (1, 0, 2):
        flows[p].wait()
        if p == 1:
            for k in range(2):
                acc[p, k, own_half] = add_low(acc[p, k, own_half], from_y[p, k])
            flows[p] = send(acc.at[p, 1 - x, own_half], from_x.at[p, own_half], pair(2, p), over)
        else:
            acc[p, x] = add_low(acc[p, x], from_x[p])
            flows[p] = send(acc.at[p, x, other_half], from_y.at[p, 0], pair(2, p), beside)
    short.wait()
    vec[...] = vec_in[8] + vec_in[1]
    short = send(vec, vec_in.at[2], small_pair(2), beside)
    dense_y()
    lines = {}
    for p in (1, 0, 2):
        flows[p].wait()
        if p == 1:
            acc[p, x, own_half] = add_low(acc[p, x, own_half], from_x[p, own_half])
        else:
            acc[p, x, own_half] = add_low(acc[p, x, own_half], from_y[p, 0])
        for d in range(1, GROUPS):
            lines[p, d] = send(
                acc.at[p, x, piece_of(z ^ d)], from_z.at[p, d], pair(2 + d, p), line[d]
            )
    short.wait()
    vec[...] = vec[...] + vec_in[2]
    vec_in[4 + z] = vec[...]
    shorts = [
        send(vec, vec_in.at[4 + z], small_pair(2 + d), line[d]) for d in range(1, GROUPS)
    ]
    spread = {}
    for p in (1, 0, 2):
        total = acc[p, x, piece_of(z)].astype(F32)
        for d in range(1, GROUPS):
            lines[p, d].wait()
            total += from_z[p, d].astype(F32)
        res[c, p, piece_of(z)] = total.astype(BF16)
        for d in range(1, GROUPS):
            spread[p, d] = send(
                res.at[c, p, piece_of(z)],
                res.at[c, p, piece_of(z)],
                pair(5 + d, p),
                line[d],
            )
    for p in (1, 0, 2):
        for d in range(1, GROUPS):
            spread[p, d].wait()
        flows[p] = send(
            res.at[c, p, own_half], res.at[c, p, own_half], pair(9, p), beside
        )
    dense_core()
    for copy in shorts:
        copy.wait()
    small_out[...] = vec_in[4] + vec_in[5] + (vec_in[6] + vec_in[7])
    for p in (1, 0, 2):
        flows[p].wait()
        flows[p] = send(res.at[c, p], res.at[c, p], pair(10, p), sibling)
    for copy in dense_flows:
        copy.wait()
    done = [pltpu.make_async_copy(dense_res, dense_out, last_sem.at[1])]
    done[0].start()
    for p in (1, 0, 2):
        flows[p].wait()
    done.append(pltpu.make_async_copy(res, out, last_sem.at[0]))
    done[1].start()
    for copy in done:
        copy.wait()


def finish(sc, tok, fg, rq, rkv, small, ready, wq, wk, wv, others):
    seqs, _, width = tok.shape
    parts, rows, lanes = 3, 3 * (width // 2), 128
    total, half = 8 * ready.shape[0], ready.shape[1]
    dma = pltpu.SemaphoreType.DMA
    return pl.pallas_call(
        functools.partial(finish_kernel, seqs),
        out_shape=[
            jax.ShapeDtypeStruct(tok.shape, F32),
            jax.ShapeDtypeStruct((2, parts, rows, lanes), BF16),
            jax.ShapeDtypeStruct((2, total, half), BF16),
            jax.ShapeDtypeStruct(small.shape, F32),
        ],
        in_specs=[SMEM] + [VMEM] * 6 + [ANY] * 4,
        out_specs=[VMEM, ANY, ANY, VMEM],
        scratch_shapes=[
            pltpu.VMEM((3, width, width), BF16),
            pltpu.VMEM((parts, 2, 2, rows, lanes), BF16),
            pltpu.VMEM((parts, 2, rows, lanes), BF16),
            pltpu.VMEM((parts, 2, rows, lanes), BF16),
            pltpu.VMEM((parts, rows, lanes), BF16),
            pltpu.VMEM((parts, 2, rows // 2, lanes), BF16),
            pltpu.VMEM((parts, GROUPS, rows // 8, lanes), BF16),
            pltpu.VMEM((2, parts, rows, lanes), BF16),
            pltpu.VMEM(small.shape, F32),
            pltpu.VMEM((9, *small.shape), F32),
            pltpu.VMEM((2, total, half), BF16),
            dma((6,)),
            dma((2, 11, parts)),
            dma((2, 6)),
            dma((2, 4, 2)),
            dma((2,)),
        ],
        compiler_params=pltpu.CompilerParams(
            vmem_limit_bytes=60 * 2**20, collective_id=2, has_side_effects=True
        ),
        cost_estimate=cost(70),
        name="finish",
    )(sc, tok, fg, rq, rkv, small, ready, wq, wk, wv, others)


def unpack_kernel(qkv, total, *refs):
    outs, (narrow, inner, outer, sems) = refs[:6], refs[6:]
    half = qkv.shape[2] // 3
    blocks = inner.shape[1] // (2 * half)
    copies = []

    def leave(src, i):
        copy = pltpu.make_async_copy(src, outs[i], sems.at[i])
        copy.start()
        copies.append(copy)

    for k in range(2):
        cols = slice(k * half, (k + 1) * half)
        outer[:, cols] = total[k, (1 + blocks) * half :].astype(F32)
    leave(outer, 5)
    for k in range(2):
        for t in range(blocks):
            cols = slice((2 * t + k) * half, (2 * t + k + 1) * half)
            inner[:, cols] = total[k, (1 + t) * half : (2 + t) * half].astype(F32)
    leave(inner, 4)
    for i in range(3):
        for k in range(2):
            for p in range(3):
                cols = slice((3 * k + p) * 128, (3 * k + p + 1) * 128)
                narrow[i, :, cols] = qkv[k, p, i * half : (i + 1) * half].astype(F32)
        leave(narrow.at[i], i)
    for k in range(2):
        narrow[3, :, k * half : (k + 1) * half] = total[k, 0:half].astype(F32)
    leave(narrow.at[3], 3)
    for copy in copies:
        copy.wait()


def unpack(qkv, total, hidden):
    half = total.shape[2]
    narrow = jax.ShapeDtypeStruct((half, 2 * half), F32)
    return pl.pallas_call(
        unpack_kernel,
        out_shape=[narrow] * 4
        + [
            jax.ShapeDtypeStruct((half, hidden), F32),
            jax.ShapeDtypeStruct((hidden // 2, 2 * half), F32),
        ],
        in_specs=[VMEM] * 2,
        out_specs=[ANY] * 6,
        scratch_shapes=[
            pltpu.VMEM((4, half, 2 * half), F32),
            pltpu.VMEM((half, hidden), F32),
            pltpu.VMEM((hidden // 2, 2 * half), F32),
            pltpu.SemaphoreType.DMA((6,)),
        ],
        compiler_params=ROOM,
        cost_estimate=cost(10),
        name="unpack",
    )(qkv, total)


def pick(table, index):
    places = jnp.arange(table.shape[0], dtype=jnp.int32)
    return jnp.sum(jnp.where(index[..., None] == places, table, 0), -1)


def shards(
    size,
    tokens,
    teacher,
    lengths,
    block_order,
    query_weight,
    query_bias,
    key_weight,
    value_weight,
    value_bias,
    out_weight,
    out_bias,
    gain_one,
    shift_one,
    inner_weight,
    inner_bias,
    outer_weight,
    outer_bias,
    gain_two,
    shift_two,
):
    seqs, rows, width = tokens.shape
    per_plane = size // GROUPS
    blocks_each = rows // BLK
    ctx, x = lax.axis_index("ctx"), lax.axis_index("wa")
    c, place = lax.rem(ctx, 2), lax.rem(ctx, per_plane)
    masks = [1 << b for b in reversed(range(per_plane.bit_length() - 1))]
    offsets = [0]
    for m in masks:
        offsets += [o ^ m for o in offsets]

    def across(value):
        return lax.ppermute(value, "wa", [(0, 1), (1, 0)])

    def flip(value, m):
        return lax.ppermute(value, "ctx", [(i, i ^ m) for i in range(size)])

    lines = [[g * per_plane + r for g in range(GROUPS)] for r in range(per_plane)]

    def turn(value):
        return lax.all_to_all(value, "ctx", 0, 0, axis_index_groups=lines)

    cores = [[i for i in range(size) if i % 2 == k] for k in range(2)]

    def paired(mine):
        sibling = flip(mine, 1)
        return jnp.where(c == 0, jnp.stack([mine, sibling]), jnp.stack([sibling, mine]))

    def reduced(grad):
        four = grad.reshape(2, 2, *grad.shape[1:])
        keep = lax.dynamic_index_in_dim(four, c, 1, False)
        give = lax.dynamic_index_in_dim(four, 1 - c, 1, False)
        keep = add_low(keep, flip(give, 1))
        mine = lax.dynamic_index_in_dim(keep, x, 0, False)
        mine = add_low(mine, across(lax.dynamic_index_in_dim(keep, 1 - x, 0, False)))
        return paired(lax.psum(mine, "ctx", axis_index_groups=cores))

    def reduced_dense(grad):
        four = grad.reshape(2, 2, *grad.shape[1:])
        keep = lax.dynamic_index_in_dim(four, c, 1, False)
        give = lax.dynamic_index_in_dim(four, 1 - c, 1, False)
        keep = add_low(keep, flip(give, 1))
        mine = lax.psum_scatter(
            keep.reshape(-1, keep.shape[-1]), "wa", scatter_dimension=0, tiled=True
        )
        return lax.psum(mine, "ctx", axis_index_groups=cores)

    vectors = (
        query_bias,
        value_bias,
        out_bias,
        gain_one,
        shift_one,
        outer_bias,
        gain_two,
        shift_two,
        inner_bias,
    )
    half, hidden = width // 2, 2 * inner_bias.shape[0]
    fused = per_plane == 4

    count = block_order.shape[0]
    ids = jnp.arange(count, dtype=jnp.int32)
    owner = ids // blocks_each
    index_of = jnp.array([offsets.index(o) for o in range(per_plane)], jnp.int32)
    piece_of = pick(index_of, (owner % per_plane) ^ place)
    spot = (piece_of * GROUPS + owner // per_plane) * blocks_each + ids % blocks_each
    key_order = jnp.sum(jnp.where(block_order[None, :] == ids[:, None], spot[None, :], 0), 1)
    near = jnp.arange(GROUPS * blocks_each, dtype=jnp.int32)
    near_ids = (near // blocks_each * per_plane + place) * blocks_each + near % blocks_each
    near_pos = pick(block_order, near_ids)
    rank = jnp.sum((near_pos[None, :] < near_pos[:, None]).astype(jnp.int32), 1)
    query_order = jnp.sum(jnp.where(rank[None, :] == near[:, None], near[None, :], 0), 1)
    own_pos = pick(block_order, ctx * blocks_each + jnp.arange(blocks_each, dtype=jnp.int32))
    scalars, row_counts = [], []
    for s in range(seqs):
        used = jnp.sum((near_pos * BLK < lengths[s]).astype(jnp.int32))
        head = jnp.concatenate([lengths[s][None], used[None], jnp.zeros((6,), jnp.int32)])
        scalars.append(jnp.concatenate([head, query_order, key_order]))
        row_counts.append(jnp.clip(lengths[s] - own_pos * BLK, 0, BLK))

    counts = jnp.concatenate(row_counts)
    if fused:
        own_vec = jnp.concatenate(vectors).reshape(-1, half)
        own_vec = jnp.pad(own_vec, ((0, -own_vec.shape[0] % 16), (0, 0)))
        found = start(
            counts,
            tokens,
            own_vec,
            (query_weight, key_weight, value_weight, out_weight, inner_weight, outer_weight),
        )
        queries = [q.reshape(-1, BLK, q.shape[2]) for q in found[:seqs]]
        pieces = [[kv.reshape(-1, BLK, kv.shape[3])] for kv in found[seqs : 2 * seqs]]
        pair, others, *rest = found[2 * seqs :]
        pair = pair.astype(F32)
        narrow = pair[:, :8].swapaxes(0, 1).reshape(8, width)
        wide_vec = pair[:, 8 : 8 + hidden // width].reshape(1, hidden)
        dense_weights = [out_weight, rest[0], inner_weight, rest[1], outer_weight, rest[2]]
    else:
        own_vec = jnp.concatenate(vectors)[None]
        other_vec = across(own_vec)
        pair = jnp.where(
            x == 0, jnp.stack([own_vec, other_vec]), jnp.stack([other_vec, own_vec])
        ).astype(F32)
        narrow = pair[:, 0, : 8 * half].reshape(2, 8, half).swapaxes(0, 1).reshape(8, width)
        wide_vec = pair[:, 0, 8 * half :].reshape(1, -1)

        def quarter(weight):
            n = weight.shape[0] // 2
            return lax.dynamic_slice_in_dim(weight, c * n, n, 0)

        first_qkv = across(
            jnp.concatenate([quarter(w) for w in (query_weight, key_weight, value_weight)], 0)
        )
        second_qkv = flip(first_qkv, 1)
        dense_weights = []
        last = first_qkv
        for weight in (out_weight, inner_weight, outer_weight):
            piece, last = lax.optimization_barrier((quarter(weight), last))
            last = across(piece)
            dense_weights += [weight, last, flip(last, 1)]

        projected = project(
            counts, tokens, narrow, query_weight, key_weight, value_weight, first_qkv, second_qkv
        )
        queries, pieces = [], []
        for s in range(seqs):
            kv = turn(projected[2 * s + 1])
            queries.append(turn(projected[2 * s]).reshape(-1, BLK, width // GROUPS))
            held = [kv.reshape(-1, BLK, kv.shape[2])]
            for m in masks:
                held += [flip(piece, m) for piece in held]
            pieces.append(held)

    attended, lses = [], []
    for s in range(seqs):
        o, lse = attend(scalars[s], queries[s], pieces[s])
        attended.append(o.reshape(queries[s].shape))
        lses.append(lse)
    if fused:
        fours = [a.reshape(GROUPS, rows, -1) for a in attended]
        found = middle(
            counts, tokens, teacher, narrow[2:], wide_vec, fours, dense_weights
        )
        output, firsts, sums, wide_sums, a_own, a_give, b_own, b_give = found[:8]
        heads_grad = [g.reshape(queries[0].shape) for g in found[8:]]
        ready = (a_own, a_give, b_own, b_give)
    else:
        dense_out = []
        for s in range(seqs):
            o4 = turn(attended[s].reshape(GROUPS, rows, -1))
            dense_out.append(
                dense(
                    row_counts[s], o4, tokens[s], teacher[s], narrow[2:], wide_vec, dense_weights
                )
            )
        output = jnp.stack([d[0] for d in dense_out])
        first_grads = [d[1] for d in dense_out]
        heads_grad = [turn(d[2]).reshape(queries[s].shape) for s, d in enumerate(dense_out)]
        sums = sum(d[9] for d in dense_out)
        wide_sums = sum(d[10] for d in dense_out)
        dense_sums = [reduced_dense(g) for g in dense_grads([d[3:9] for d in dense_out])]

    if fused:
        flat_rows = (GROUPS * rows, width // GROUPS)
        rq, rkv, ready = attend_back_all(
            [
                [
                    *(a.reshape(flat_rows) for a in (queries[s], heads_grad[s], attended[s])),
                    lses[s],
                    pieces[s][0].reshape(-1, pieces[s][0].shape[2]),
                ]
                for s in range(seqs)
            ],
            ready,
        )
    else:
        dqs, dkvs = [], []
        for s in range(seqs):
            found = attend_back(
                scalars[s], queries[s], heads_grad[s], attended[s], lses[s], pieces[s]
            )
            dqs.append(turn(found[0].reshape(GROUPS, rows, -1)))
            held = [piece.reshape(GROUPS, rows, -1) for piece in found[1:]]
            for m in reversed(masks):
                n = len(held) // 2
                held = [add_low(mine, flip(theirs, m)) for mine, theirs in zip(held[:n], held[n:])]
            dkvs.append(turn(held[0]))
        tokens_grad, g_qkv, sums_qkv = project_grads(
            counts,
            tokens,
            first_grads,
            dqs + dkvs,
            query_weight,
            key_weight,
            value_weight,
            first_qkv,
            second_qkv,
        )

    loss_part = jnp.sum(sums[6])
    valid = sum(jnp.sum(r) for r in row_counts).astype(F32)
    between = jnp.zeros((2 * width,), F32) if fused else sums_qkv[:2].reshape(-1)
    small = jnp.concatenate(
        [sums[:6].reshape(-1), between, wide_sums[0], jnp.stack([loss_part, valid])]
    )
    small = jnp.pad(small, (0, -small.shape[0] % 1024)).reshape(-1, 128)
    if fused:
        tokens_grad, qkv, total, small = finish(
            counts,
            tokens,
            firsts,
            rq,
            rkv,
            small,
            ready,
            query_weight,
            key_weight,
            value_weight,
            others,
        )
        query_grad, key_grad, value_grad, out_grad, inner_grad, outer_grad = unpack(
            qkv, total, hidden
        )
    else:
        small = lax.psum(small, ("ctx", "wa"))
        qkv = reduced(jnp.moveaxis(g_qkv, (2, 1), (0, 1)).reshape(4, 3, -1, 128))
        out_grad, inner_grad, outer_grad = (
            paired(g).reshape(-1, g.shape[-1]).astype(F32) for g in dense_sums
        )
        qkv = qkv.reshape(6, 3, half, 128).astype(F32)
        query_grad, key_grad, value_grad = (
            qkv[:, i].swapaxes(0, 1).reshape(half, width) for i in range(3)
        )
    small = small.reshape(-1)

    def vector(start, length):
        return lax.dynamic_slice_in_dim(small, start + x * (length // 2), length // 2, 0)

    end = 8 * width
    loss = small[end + hidden] / (small[end + hidden + 1] * width)
    return (
        output,
        tokens_grad,
        query_grad,
        vector(6 * width, width),
        key_grad,
        value_grad,
        vector(7 * width, width),
        out_grad,
        vector(5 * width, width),
        vector(3 * width, width),
        vector(4 * width, width),
        inner_grad,
        vector(end, hidden),
        outer_grad,
        vector(2 * width, width),
        vector(0, width),
        vector(width, width),
        loss,
    )


def solution(mesh):
    row, split, both = P("wa"), P("wa", None), P("wa", "ctx", None)
    placed = (both, both, row, P(), split, row, split, split, row, split, row, row, row)
    placed += (split, row, split, row, row, row)
    return jax.shard_map(
        functools.partial(shards, mesh.shape["ctx"]),
        mesh=mesh,
        in_specs=placed,
        out_specs=(
            both,
            both,
            split,
            row,
            split,
            split,
            row,
            split,
            row,
            row,
            row,
            split,
            row,
            split,
            row,
            row,
            row,
            P(),
        ),
        check_vma=False,
    )
```

```python
import functools
import math

import jax
import jax.numpy as jnp
from jax import lax
from jax.experimental import pallas as pl
from jax.experimental.pallas import tpu as pltpu
from jax.sharding import PartitionSpec as P

DH = 64
BLK = 128
GROUPS = 4
LN2 = math.log(2.0)
NT = (((1,), (1,)), ((), ()))
NN = (((1,), (0,)), ((), ()))
TN = (((0,), (0,)), ((), ()))
F32 = jnp.float32
BF16 = jnp.bfloat16
VMEM = pl.BlockSpec(memory_space=pltpu.VMEM)
SMEM = pl.BlockSpec(memory_space=pltpu.SMEM)
ANY = pl.BlockSpec(memory_space=pl.ANY)
ROOM = pltpu.CompilerParams(vmem_limit_bytes=62 * 2**20)


def dot(left, right, dims=NN):
    return lax.dot_general(left, right, dims, preferred_element_type=F32)


def cost(us):
    return pl.CostEstimate(flops=int(us * 1.15e9), bytes_accessed=1 << 20, transcendentals=0)


def weight_copies(full, own, first, second, sems, base):
    x, c = lax.axis_index("wa"), lax.rem(lax.axis_index("ctx"), 2)
    half = own.shape[0]
    quarter = half // 2
    other = (1 - x) * half
    places = (
        (own, x * half, half),
        (first, other + c * quarter, quarter),
        (second, other + (1 - c) * quarter, quarter),
    )
    return [
        pltpu.make_async_copy(
            src, full.at[pl.ds(pl.multiple_of(start, quarter), size)], sems.at[base + i]
        )
        for i, (src, start, size) in enumerate(places)
    ]


class Counts:
    def __init__(self, lengths, order):
        self.lengths, self.order = lengths, order

    def __getitem__(self, i):
        place = 2 * lax.axis_index("ctx") + i % 2
        return self.lengths[i // 2] - self.order[place] * BLK


def valid_rows(sc, s, rows):
    row = lax.broadcasted_iota(jnp.int32, (rows, 1), 0)
    first = jnp.where(row < sc[2 * s], 1.0, 0.0)
    later = jnp.where(row - BLK < sc[2 * s + 1], 1.0, 0.0)
    return jnp.where(row < BLK, first, later)


def half_copies(full, own, other, sems, base):
    x, half = lax.axis_index("wa"), own.shape[0]
    return [
        pltpu.make_async_copy(
            src, full.at[pl.ds(pl.multiple_of(k * half, half), half)], sems.at[base + i]
        )
        for i, (src, k) in enumerate(((own, x), (other, 1 - x)))
    ]


def project_kernel(sc, tok, vec, wq, wk, wv, first, second, *rest):
    seqs, rows, width = tok.shape
    outs, (full, sems) = rest[: 2 * seqs], rest[2 * seqs :]
    quarter = wq.shape[0] // 2
    copies = []
    for i, own in enumerate((wq, wk, wv)):
        part = pl.ds(i * quarter, quarter)
        copies.append(
            weight_copies(full.at[i], own, first.at[part], second.at[part], sems, 3 * i)
        )
    for group in copies:
        for copy in group:
            copy.start()
    flat = tok[...].reshape(seqs * rows, width)
    per = width // GROUPS
    heads = per // DH
    valid = jnp.concatenate([valid_rows(sc, s, rows) for s in range(seqs)], 0) > 0.0
    for copy in copies[1]:
        copy.wait()
    keys = jnp.where(valid, dot(flat, full[1]), 0.0).astype(BF16)
    for copy in copies[2]:
        copy.wait()
    values = jnp.where(valid, dot(flat, full[2]) + vec[1:2, :], 0.0).astype(BF16)
    for s in range(seqs):
        rs = slice(s * rows, (s + 1) * rows)
        for g in range(GROUPS):
            for h in range(heads):
                cols = slice(g * per + h * DH, g * per + (h + 1) * DH)
                outs[2 * s + 1][g, :, h * 128 : (h + 1) * 128] = jnp.concatenate(
                    [keys[rs, cols], values[rs, cols]], 1
                )
    for copy in copies[0]:
        copy.wait()
    queries = ((dot(flat, full[0]) + vec[0:1, :]) * (DH**-0.5 / LN2)).astype(BF16)
    for s in range(seqs):
        rs = slice(s * rows, (s + 1) * rows)
        for g in range(GROUPS):
            outs[2 * s][g] = queries[rs, g * per : (g + 1) * per]


def project(sc, tok, vec, wq, wk, wv, first, second):
    seqs, rows, width = tok.shape
    per = width // GROUPS
    shapes = [
        jax.ShapeDtypeStruct((GROUPS, rows, n), BF16) for _ in range(seqs) for n in (per, 2 * per)
    ]
    return pl.pallas_call(
        project_kernel,
        out_shape=shapes,
        in_specs=[SMEM, VMEM, VMEM] + [ANY] * 5,
        out_specs=[VMEM] * len(shapes),
        scratch_shapes=[pltpu.VMEM((3, width, width), BF16), pltpu.SemaphoreType.DMA((9,))],
        compiler_params=ROOM,
        cost_estimate=cost(5),
        name="project",
    )(sc, tok, vec, wq, wk, wv, first, second)


def load_pieces(pieces, kv, sems):
    per = pieces[0].shape[0]
    copies = [
        pltpu.make_async_copy(piece, kv.at[pl.ds(i * per, per)], sems.at[i])
        for i, piece in enumerate(pieces)
    ]
    for copy in copies:
        copy.start()
    for copy in copies:
        copy.wait()


def forward_kernel(wide, narrow, count, s, per_plane, lengths, order, q_ref, *rest):
    pieces, rest = rest[:count], rest[count:]
    o_ref, lse_ref, kv_ref, qa, acc, sums, spots, sems = rest
    blocks = q_ref.shape[0]
    heads = q_ref.shape[2] // DH
    rows = blocks * BLK
    length = lengths[s]
    place = lax.rem(lax.axis_index("ctx"), per_plane)

    def put(b, _):
        owner = b // 2
        offset = lax.bitwise_xor(lax.rem(owner, per_plane), place)
        piece = 0
        for bit in range(per_plane.bit_length() - 1):
            piece = 2 * piece + lax.rem(lax.div(offset, 1 << bit), 2)
        spots[order[b]] = (piece * GROUPS + lax.div(owner, per_plane)) * 2 + lax.rem(b, 2)
        return 0

    lax.fori_loop(0, order.shape[0], put, 0)
    load_pieces(pieces, kv_ref, sems)

    def gather(h, start, n):
        return jnp.concatenate(
            [kv_ref[spots[start + i], :, h * 128 : (h + 1) * 128] for i in range(n)], 0
        )

    whole = length // (wide * BLK)
    tail = whole * wide
    tails = (length - tail * BLK + narrow * BLK - 1) // (narrow * BLK)
    for h in range(heads):
        hs = slice(h * DH, (h + 1) * DH)
        own = jnp.concatenate([q_ref[b, :, hs] for b in range(blocks)], 0)
        qa[...] = jnp.concatenate([own, jnp.zeros_like(own)], 1)
        acc[...] = jnp.zeros_like(acc)
        sums[...] = jnp.zeros_like(sums)

        def step(start, n, masked, h=h):
            kv = gather(h, start, n)
            scores = dot(qa[...], kv, NT)
            if masked:
                place = lax.broadcasted_iota(jnp.int32, scores.shape, 1) + start * BLK
                scores = jnp.where(place < length, scores, -1e30)
            p = jnp.exp2(scores)
            sums[...] += sum(p[:, i * 128 : (i + 1) * 128] for i in range(n))
            acc[...] += dot(p.astype(BF16), kv)

        def wide_step(j, _, step=step):
            step(j * wide, wide, False)
            return 0

        def narrow_step(j, _, step=step):
            step(tail + j * narrow, narrow, True)
            return 0

        lax.fori_loop(0, whole, wide_step, 0)
        lax.fori_loop(0, tails, narrow_step, 0)
        total = jnp.sum(sums[...], 1, keepdims=True)
        across = jnp.transpose(jnp.broadcast_to(total, (rows, 128)))[:8]
        good = (jnp.min(across) > 2.0**-80) & (jnp.max(across) < 2.0**100)

        @pl.when(good)
        def _(h=h, hs=hs, total=total, across=across):
            lse_ref[h] = jnp.log2(across)
            o_ref[:, hs] = (acc[:, DH:] * (1.0 / total)).astype(BF16)

        @pl.when(jnp.logical_not(good))
        def _(h=h, hs=hs):
            key_blocks = (length + BLK - 1) // BLK

            def rows_step(t, _):
                part = pl.ds(pl.multiple_of(t * BLK, BLK), BLK)
                q = qa[part, :]

                def scores_of(j):
                    kv = gather(h, j, 1)
                    scores = dot(q, kv, NT)
                    place = lax.broadcasted_iota(jnp.int32, scores.shape, 1) + j * BLK
                    return kv, jnp.where(place < length, scores, -1e30)

                largest = lax.fori_loop(
                    0,
                    key_blocks,
                    lambda j, m: jnp.maximum(m, jnp.max(scores_of(j)[1], 1, keepdims=True)),
                    jnp.full((BLK, 1), -1e30, F32),
                )
                acc[part, :] = jnp.zeros((BLK, 128), F32)
                sums[part, :] = jnp.zeros((BLK, 128), F32)

                def add(j, _):
                    kv, scores = scores_of(j)
                    p = jnp.exp2(scores - largest)
                    sums[part, :] += p
                    acc[part, :] += dot(p.astype(BF16), kv)
                    return 0

                lax.fori_loop(0, key_blocks, add, 0)
                row_total = jnp.sum(sums[part, :], 1, keepdims=True)
                lse = largest + jnp.log2(row_total)
                lse_ref[h, :, part] = jnp.transpose(jnp.broadcast_to(lse, (BLK, 128)))[:8]
                o_ref[part, hs] = (acc[part, :][:, DH:] * (1.0 / row_total)).astype(BF16)
                return 0

            lax.fori_loop(0, rows // BLK, rows_step, 0)


def attend(s, per_plane, lengths, order, q, pieces):
    blocks, _, per = q.shape
    rows, heads = blocks * BLK, per // DH
    key_blocks = len(pieces) * pieces[0].shape[0]
    return pl.pallas_call(
        functools.partial(forward_kernel, 8, 2, len(pieces), s, per_plane),
        out_shape=(
            jax.ShapeDtypeStruct((rows, per), BF16),
            jax.ShapeDtypeStruct((heads, 8, rows), F32),
        ),
        in_specs=[SMEM, SMEM, VMEM] + [ANY] * len(pieces),
        out_specs=(VMEM, VMEM),
        scratch_shapes=[
            pltpu.VMEM((key_blocks, BLK, 2 * per), BF16),
            pltpu.VMEM((rows, 128), BF16),
            pltpu.VMEM((rows, 128), F32),
            pltpu.VMEM((rows, 128), F32),
            pltpu.SMEM((key_blocks,), jnp.int32),
            pltpu.SemaphoreType.DMA((len(pieces),)),
        ],
        compiler_params=ROOM,
        cost_estimate=cost(20),
        name="attend",
    )(lengths, order, q, *pieces)


def backward_kernel(qn, kn, count, sc, q_ref, do_ref, o_ref, lse_ref, *rest):
    pieces, dq_ref, outs = rest[:count], rest[count], rest[count + 1 : 2 * count + 1]
    kv_ref, both, dkv, dq, lse_row, delta_row, sems = rest[2 * count + 1 :]
    blocks = q_ref.shape[0]
    heads = q_ref.shape[2] // DH
    key_blocks = kv_ref.shape[0]
    tile = qn * BLK
    length, used = sc[0], sc[1]
    whole = length // (kn * BLK)
    parts = (length + kn * BLK - 1) // (kn * BLK)
    tiles = (used + qn - 1) // qn
    ones = jnp.ones((8, DH), BF16)
    load_pieces(pieces, kv_ref, sems)
    for h in range(heads):
        hs = slice(h * DH, (h + 1) * DH)

        def clear(i, _):
            dkv[pl.ds(pl.multiple_of(i * 1024, 1024), 1024), :] = jnp.zeros((1024, 128), F32)
            return 0

        lax.fori_loop(0, key_blocks // 8, clear, 0)
        dq[...] = jnp.zeros_like(dq)

        def prepare(t, _, h=h, hs=hs):
            base = pl.multiple_of(t * (2 * tile), 2 * tile)
            start = pl.multiple_of(t * tile, tile)
            places = [sc[8 + t * qn + i] for i in range(qn)]
            q = jnp.concatenate([q_ref[s, :, hs] for s in places], 0)
            do = jnp.concatenate([do_ref[s, :, hs] for s in places], 0)
            o = jnp.concatenate([o_ref[s, :, hs] for s in places], 0)
            zero = jnp.zeros_like(q)
            both[pl.ds(base, tile), :] = jnp.concatenate([q, zero], 1)
            both[pl.ds(base + tile, tile), :] = jnp.concatenate([zero, do], 1)
            product = do.astype(F32) * o.astype(F32)
            high = product.astype(BF16)
            rest_of = (product - high.astype(F32)).astype(BF16)
            delta_row[:, pl.ds(start, tile)] = dot(ones, high, NT) + dot(ones, rest_of, NT)
            lse_row[:, pl.ds(start, tile)] = jnp.concatenate(
                [lse_ref[h, :, pl.ds(pl.multiple_of(s * BLK, BLK), BLK)] for s in places], 1
            )
            return 0

        lax.fori_loop(0, tiles, prepare, 0)

        def rows_step(t, _, h=h):
            base = pl.multiple_of(t * (2 * tile), 2 * tile)
            span = pl.ds(pl.multiple_of(t * tile, tile), tile)

            def step(j, masked):
                places = [sc[8 + blocks + j * kn + i] for i in range(kn)]
                kv = jnp.concatenate([kv_ref[s, :, h * 128 : (h + 1) * 128] for s in places], 0)
                b = both[pl.ds(base, 2 * tile), :]
                found = dot(kv, b, NT)
                p = jnp.exp2(found[:, :tile] - lse_row[:1, span])
                if masked:
                    place = lax.broadcasted_iota(jnp.int32, p.shape, 0) + j * (kn * BLK)
                    p = jnp.where(place < length, p, 0.0)
                ds = (p * (found[:, tile:] - delta_row[:1, span])).astype(BF16)
                grads = dot(jnp.concatenate([ds, p.astype(BF16)], 1), b)
                for i, s in enumerate(places):
                    dkv[pl.ds(pl.multiple_of(s * BLK, BLK), BLK), :] += grads[
                        i * BLK : (i + 1) * BLK
                    ]
                dq[span, :] += dot(ds, kv, TN)

            def whole_step(j, _):
                step(j, False)
                return 0

            lax.fori_loop(0, whole, whole_step, 0)

            @pl.when(parts > whole)
            def _():
                step(whole, True)

            return 0

        lax.fori_loop(0, tiles, rows_step, 0)
        for i in range(blocks):
            dq_ref[sc[8 + i], :, hs] = (
                dq[i * BLK : (i + 1) * BLK, :DH] * DH**-0.5
            ).astype(BF16)
        level = jnp.where(lax.broadcasted_iota(jnp.int32, (1, 128), 1) < DH, LN2, 1.0)
        per_piece = key_blocks // count
        for n, out in enumerate(outs):
            for i in range(per_piece):
                b = n * per_piece + i
                out[i, :, h * 128 : (h + 1) * 128] = (
                    dkv[b * BLK : (b + 1) * BLK, :] * level
                ).astype(BF16)


def attend_back(sc, q, do, o, lse, pieces):
    blocks, _, per = q.shape
    rows = blocks * BLK
    key_blocks = len(pieces) * pieces[0].shape[0]
    return pl.pallas_call(
        functools.partial(backward_kernel, 4, 4, len(pieces)),
        out_shape=[jax.ShapeDtypeStruct(q.shape, BF16)]
        + [jax.ShapeDtypeStruct(p.shape, BF16) for p in pieces],
        in_specs=[SMEM] + [VMEM] * 4 + [ANY] * len(pieces),
        out_specs=[VMEM] * (1 + len(pieces)),
        scratch_shapes=[
            pltpu.VMEM((key_blocks, BLK, 2 * per), BF16),
            pltpu.VMEM((2 * rows, 128), BF16),
            pltpu.VMEM((key_blocks * BLK, 128), F32),
            pltpu.VMEM((rows, 128), F32),
            pltpu.VMEM((8, rows), F32),
            pltpu.VMEM((8, rows), F32),
            pltpu.SemaphoreType.DMA((len(pieces),)),
        ],
        compiler_params=ROOM,
        cost_estimate=cost(45),
        name="attend_back",
    )(sc, q, do, o, lse, *pieces)


def norm(values):
    centered = values - jnp.mean(values, -1, keepdims=True)
    inverse = lax.rsqrt(jnp.mean(centered * centered, -1, keepdims=True) + 1e-6)
    return centered * inverse, inverse


def norm_back(upstream, normed, inverse):
    return inverse * (
        upstream
        - jnp.mean(upstream, -1, keepdims=True)
        - normed * jnp.mean(upstream * normed, -1, keepdims=True)
    )


def normal_parts(x):
    z = jnp.abs(x) * (0.5**0.5)
    bell = jnp.exp(-0.5 * x * x)
    t = 1.0 / (1.0 + 0.3275911 * z)
    poly = t * (
        0.254829592
        + t * (-0.284496736 + t * (1.421413741 + t * (-1.453152027 + t * 1.061405429)))
    )
    upper = 0.5 * poly * bell
    return jnp.where(x >= 0, 1.0 - upper, upper), bell * (2.0 * math.pi) ** -0.5


def dense_kernel(sc, att4, tok, teach, vec, wide_vec, *rest):
    weights, rest = rest[:9], rest[9:]
    outs, (wo, wi, wu, slope, sems) = rest[:11], rest[11:]
    out, fg, ag, att_o, br_o, hl_o, il_o, act_o, ol_o, sums, wide_sums = outs
    rows, width = tok.shape
    hidden = wi.shape[1]
    tile = 512
    copies = [
        weight_copies(full, *weights[3 * i : 3 * i + 3], sems, 3 * i)
        for i, full in enumerate((wo, wi, wu))
    ]
    for group in copies:
        for copy in group:
            copy.start()
    per = att4.shape[2]
    att = jnp.concatenate([att4[g] for g in range(GROUPS)], 1)
    att_o[...] = att
    row = lax.broadcasted_iota(jnp.int32, (rows, 1), 0)
    mask = jnp.where(
        row < BLK, jnp.where(row < sc[0], 1.0, 0.0), jnp.where(row - BLK < sc[1], 1.0, 0.0)
    )
    out_bias, gain_one, shift_one = vec[0:1, :], vec[1:2, :], vec[2:3, :]
    outer_bias, gain_two, shift_two = vec[3:4, :], vec[4:5, :], vec[5:6, :]
    for copy in copies[0]:
        copy.wait()
    first = tok[...].astype(F32) + dot(att, wo[...]) + out_bias
    normed_one, inverse_one = norm(first)
    hidden_in = normed_one * gain_one + shift_one
    hl = hidden_in.astype(BF16)
    hl_o[...] = hl
    for copy in copies[1] + copies[2]:
        copy.wait()
    second = hidden_in + outer_bias
    for n in range(hidden // tile):
        cols = slice(n * tile, (n + 1) * tile)
        inner = dot(hl, wi[:, cols]) + wide_vec[0:1, cols]
        below, density = normal_parts(inner)
        act = (inner * below).astype(BF16)
        act_o[:, cols] = act
        slope[:, cols] = below + inner * density
        second += dot(act, wu[cols, :])
    normed_two, inverse_two = norm(second)
    final = normed_two * gain_two + shift_two
    out[...] = final.astype(BF16)
    residue = (final - teach[...].astype(F32)) * mask
    add = functools.partial(jnp.sum, axis=0, keepdims=True)
    second_grad = norm_back(residue * gain_two, normed_two, inverse_two)
    ol = second_grad.astype(BF16)
    ol_o[...] = ol
    hidden_grad = second_grad
    for n in range(hidden // tile):
        cols = slice(n * tile, (n + 1) * tile)
        il = (dot(ol, wu[cols, :], NT) * slope[:, cols]).astype(BF16)
        il_o[:, cols] = il
        wide_sums[0:1, cols] = add(il.astype(F32))
        hidden_grad += dot(il, wi[:, cols], NT)
    first_grad = norm_back(hidden_grad * gain_one, normed_one, inverse_one)
    fg[...] = first_grad
    br = first_grad.astype(BF16)
    br_o[...] = br
    att_grad = dot(br, wo[...], NT).astype(BF16)
    for g in range(GROUPS):
        ag[g] = att_grad[:, g * per : (g + 1) * per]
    sums[0:1, :] = add(residue * normed_two)
    sums[1:2, :] = add(residue)
    sums[2:3, :] = add(ol.astype(F32))
    sums[3:4, :] = add(hidden_grad * normed_one)
    sums[4:5, :] = add(hidden_grad)
    sums[5:6, :] = add(br.astype(F32))
    sums[6:7, :] = add(residue * residue)
    sums[7:8, :] = jnp.zeros((1, width), F32)


def dense(sc, att4, tok, teach, vec, wide_vec, weights):
    rows, width = tok.shape
    hidden = wide_vec.shape[1]
    narrow = jax.ShapeDtypeStruct((rows, width), BF16)
    wide = jax.ShapeDtypeStruct((rows, hidden), BF16)
    return pl.pallas_call(
        dense_kernel,
        out_shape=[
            narrow,
            jax.ShapeDtypeStruct((rows, width), F32),
            jax.ShapeDtypeStruct(att4.shape, BF16),
            narrow,
            narrow,
            narrow,
            wide,
            wide,
            narrow,
            jax.ShapeDtypeStruct((8, width), F32),
            jax.ShapeDtypeStruct((1, hidden), F32),
        ],
        in_specs=[SMEM] + [VMEM] * 5 + [ANY] * 9,
        out_specs=[VMEM] * 11,
        scratch_shapes=[
            pltpu.VMEM((width, width), BF16),
            pltpu.VMEM((width, hidden), BF16),
            pltpu.VMEM((hidden, width), BF16),
            pltpu.VMEM((rows, hidden), F32),
            pltpu.SemaphoreType.DMA((9,)),
        ],
        compiler_params=ROOM,
        cost_estimate=cost(15),
        name="dense",
    )(sc, att4, tok, teach, vec, wide_vec, *weights)


def dense_grads_kernel(seqs, *refs):
    ins, (g_out, g_inner, g_outer) = refs[: 6 * seqs], refs[6 * seqs :]
    att, br, hl, il, act, ol = (
        jnp.concatenate([ins[6 * s + i][...] for s in range(seqs)], 0) for i in range(6)
    )
    for target, left, right in ((g_out, att, br), (g_inner, hl, il), (g_outer, act, ol)):
        rows = target.shape[1]
        for n in range(4):
            piece = left[:, n * rows : (n + 1) * rows]
            for t in range(right.shape[1] // 768):
                cols = slice(t * 768, (t + 1) * 768)
                target[n, :, cols] = dot(piece, right[:, cols], TN).astype(BF16)


def dense_grads(saved):
    seqs = len(saved)
    width, hidden = saved[0][0].shape[1], saved[0][3].shape[1]
    return pl.pallas_call(
        functools.partial(dense_grads_kernel, seqs),
        out_shape=[
            jax.ShapeDtypeStruct((4, width // 4, width), BF16),
            jax.ShapeDtypeStruct((4, width // 4, hidden), BF16),
            jax.ShapeDtypeStruct((4, hidden // 4, width), BF16),
        ],
        in_specs=[VMEM] * (6 * seqs),
        out_specs=[VMEM] * 3,
        compiler_params=ROOM,
        cost_estimate=cost(10),
        name="dense_grads",
    )(*[member for group in saved for member in group])


def project_grads_kernel(seqs, sc, tok, *refs):
    fgs, refs = refs[:seqs], refs[seqs:]
    grads_in, refs = refs[: 2 * seqs], refs[2 * seqs :]
    wq, wk, wv, first, second, tg, grads, sums, full, sems = refs
    rows, width = tok.shape[1:]
    per = width // GROUPS
    heads = per // DH
    quarter = wq.shape[0] // 2
    copies = []
    for i, own in enumerate((wq, wk, wv)):
        part = pl.ds(i * quarter, quarter)
        copies += weight_copies(full.at[i], own, first.at[part], second.at[part], sems, 3 * i)
    for copy in copies:
        copy.start()

    def head(i, s, g, h):
        if i == 0:
            return grads_in[s][g, :, h * DH : (h + 1) * DH]
        start = h * 128 + (i - 1) * DH
        return grads_in[seqs + s][g, :, start : start + DH]

    def whole(i):
        each = [
            jnp.concatenate([head(i, s, g, h) for g in range(GROUPS) for h in range(heads)], 1)
            for s in range(seqs)
        ]
        return jnp.concatenate(each, 0)

    valid = jnp.concatenate([valid_rows(sc, s, rows) for s in range(seqs)], 0) > 0.0
    dq = whole(0)
    halves = [jnp.where(valid, whole(i), jnp.zeros((), BF16)) for i in (1, 2)]
    flat = tok[...].reshape(seqs * rows, width)
    for copy in copies:
        copy.wait()
    total = jnp.concatenate([fgs[s][...] for s in range(seqs)], 0)
    for i, grad in enumerate((dq, *halves)):
        total += dot(grad, full[i], NT)
        found = dot(flat, grad, TN).astype(BF16)
        half = width // 2
        for n in range(2):
            for t in range(width // 128):
                grads[t % 3, t // 3, n, i * half : (i + 1) * half, :] = found[
                    n * half : (n + 1) * half, t * 128 : (t + 1) * 128
                ]
    tg[...] = total.reshape(seqs, rows, width)
    sums[0:1, :] = jnp.sum(dq.astype(F32), 0, keepdims=True)
    sums[1:2, :] = jnp.sum(halves[1].astype(F32), 0, keepdims=True)
    sums[2:8, :] = jnp.zeros((6, width), F32)


def project_grads(sc, tok, fgs, grads, wq, wk, wv, first, second):
    seqs, rows, width = tok.shape
    return pl.pallas_call(
        functools.partial(project_grads_kernel, seqs),
        out_shape=[
            jax.ShapeDtypeStruct(tok.shape, F32),
            jax.ShapeDtypeStruct((3, 2, 2, 3 * (width // 2), 128), BF16),
            jax.ShapeDtypeStruct((8, width), F32),
        ],
        in_specs=[SMEM] + [VMEM] * (1 + len(fgs) + len(grads)) + [ANY] * 5,
        out_specs=[VMEM] * 3,
        scratch_shapes=[pltpu.VMEM((3, width, width), BF16), pltpu.SemaphoreType.DMA((9,))],
        compiler_params=ROOM,
        cost_estimate=cost(10),
        name="project_grads",
    )(sc, tok, *fgs, *grads, wq, wk, wv, first, second)


MESH = pl.DeviceIdType.MESH


def position():
    ctx = lax.axis_index("ctx")
    return ctx // 4, lax.rem(ctx // 2, 2), lax.rem(ctx, 2), lax.axis_index("wa")


def device(z, y, c, x):
    return z * 4 + y * 2 + c, x


def greet(others):
    barrier = pltpu.get_barrier_semaphore()
    for other in others:
        pl.semaphore_signal(barrier, inc=1, device_id=other, device_id_type=MESH)
    pl.semaphore_wait(barrier, len(others))


def send(src, dst, sems, to):
    copy = pltpu.make_async_remote_copy(
        src_ref=src,
        dst_ref=dst,
        send_sem=sems[0],
        recv_sem=sems[1],
        device_id=to,
        device_id_type=MESH,
    )
    copy.start()
    return copy


def add_low(left, right):
    return (left.astype(F32) + right.astype(F32)).astype(BF16)


def back_kernel(seqs, *refs):
    per_seq = 5
    ins = [refs[per_seq * s : per_seq * (s + 1)] for s in range(seqs)]
    a_own, a_give, b_own, b_give, rq, rkv, dense_out, *refs = refs[per_seq * seqs :]
    q_v, do_v, o_v, lse_v, kv_v, both, dkv, dq, delta, obuf, qbuf = refs[:11]
    from_core, from_y, a_v, b_v, a_in, b_in, a2, b2, a2_in, b2_in = refs[11:21]
    az_in, bz_in, dres, in_sem, c_sem, y_sem, z_sem, q_sem, l_sem, x_sem, dz_sem = refs[21:]
    z, y, c, x = position()
    sibling, beside, over = device(z, y, 1 - c, x), device(z, 1 - y, c, x), device(z, y, c, 1 - x)
    line = [None] + [device(z ^ d, y, c, x) for d in range(1, GROUPS)]
    greet([sibling, beside, over] + line[1:])

    def pair(sems, *index):
        return sems.at[(0, *index)], sems.at[(1, *index)]

    flow = {}
    flow["a"] = send(a_give, a_in, pair(x_sem, 0), over)
    flow["b"] = send(b_give, b_in, pair(x_sem, 1), beside)
    loads = []
    for s in range(seqs):
        targets = [ref.at[s] for ref in (q_v, do_v, o_v, lse_v, kv_v)]
        group = [
            pltpu.make_async_copy(src, dst, in_sem.at[s, i])
            for i, (src, dst) in enumerate(zip(ins[s], targets))
        ]
        for copy in group:
            copy.start()
        loads.append(group)
    own_loads = [
        pltpu.make_async_copy(a_own, a_v, l_sem.at[0]),
        pltpu.make_async_copy(b_own, b_v, l_sem.at[1]),
    ]
    for copy in own_loads:
        copy.start()

    rows = q_v.shape[1]
    heads = q_v.shape[2] // DH
    keys = kv_v.shape[1]
    tile, ktile = rows // 2, 2048
    quarter = keys // 4
    chunk = quarter // GROUPS
    ones = jnp.ones((8, DH), BF16)
    level = jnp.where(lax.broadcasted_iota(jnp.int32, (1, 128), 1) < DH, LN2, 1.0)
    waits = []

    def group_rows(g):
        return pl.ds(pl.multiple_of(g * chunk, chunk), chunk)

    def core_stage(u):
        flow["c", u] = send(
            obuf.at[u, pl.ds(2 * quarter, 2 * quarter)], from_core.at[u], pair(c_sem, u), sibling
        )

    def y_stage(u):
        flow["c", u].wait()
        second = pl.ds(quarter, quarter)
        obuf[u, second] = add_low(obuf[u, second], from_core[u, second])
        flow["y", u] = send(obuf.at[u, second], from_y.at[u], pair(y_sem, u), beside)
        obuf[u, 0:quarter] = add_low(obuf[u, 0:quarter], from_core[u, 0:quarter])

    def z_stage(u):
        flow["y", u].wait()
        obuf[u, 0:quarter] = add_low(obuf[u, 0:quarter], from_y[u])
        for d in range(1, GROUPS):
            src = obuf.at[u, group_rows(z ^ d)]
            waits.append(send(src, rkv.at[u, z], pair(z_sem, u, d), line[d]))
        own = pltpu.make_async_copy(obuf.at[u, group_rows(z)], rkv.at[u, z], z_sem.at[0, u, 0])
        own.start()
        waits.append(own)

    def q_stage(h):
        for d in range(1, GROUPS):
            waits.append(send(qbuf.at[h, z ^ d], rq.at[h, z], pair(q_sem, h, d), line[d]))
        own = pltpu.make_async_copy(qbuf.at[h, z], rq.at[h, z], q_sem.at[0, h, 0])
        own.start()
        waits.append(own)

    a_half, b_half = a2.shape[1], b2.shape[1]

    def dense_second():
        for copy in own_loads:
            copy.wait()
        flow["a"].wait()
        for slot, which in ((0, y), (1, 1 - y)):
            part = pl.ds(pl.multiple_of(which * a_half, 16), a_half)
            a2[slot] = add_low(a_v[part, :], a_in[part, :])
        flow["a"] = send(a2.at[1], a2_in, pair(x_sem, 2), beside)
        flow["b"].wait()
        for slot, which in ((0, x), (1, 1 - x)):
            b2[slot] = add_low(b_v[which], b_in[which])
        flow["b"] = send(b2.at[1], b2_in, pair(x_sem, 3), over)

    low_bit, high_bit = lax.rem(z, 2), z // 2
    parts = (("a", a2, a2_in, az_in), ("b", b2, b2_in, bz_in))

    def rows_at(start, n):
        return pl.ds(pl.multiple_of(start, 16), n)

    def dense_third():
        for i, (name, held, arrived, landing) in enumerate(parts):
            flow[name].wait()
            held[0] = add_low(held[0], arrived[...])
            n = held.shape[1] // 2
            src = held.at[0, rows_at((1 - low_bit) * n, n)]
            flow[name] = send(src, landing.at[0:n], pair(dz_sem, i, 0), line[1])

    def dense_fourth():
        for i, (name, held, _, landing) in enumerate(parts):
            flow[name].wait()
            n = held.shape[1] // 2
            mine = rows_at(low_bit * n, n)
            held[0, mine] = add_low(held[0, mine], landing[0:n])
            src = held.at[0, rows_at(low_bit * n + (1 - high_bit) * (n // 2), n // 2)]
            flow[name] = send(src, landing.at[n : n + n // 2], pair(dz_sem, i, 1), line[2])

    def dense_fifth():
        base = 0
        for name, held, _, landing in parts:
            flow[name].wait()
            n = held.shape[1] // 2
            mine = rows_at(low_bit * n + high_bit * (n // 2), n // 2)
            dres[base : base + n // 2] = add_low(held[0, mine], landing[n : n + n // 2])
            base += n // 2

    units = [(h, s) for h in range(heads) for s in range(seqs)]
    slots = {}
    for u in range(len(units) - 1):
        slots.setdefault(2 * u + 3, []).append(functools.partial(y_stage, u))
        slots.setdefault(2 * u + 5, []).append(functools.partial(z_stage, u))
    slots.setdefault(5, []).append(dense_second)
    slots.setdefault(7, []).append(dense_third)
    slots.setdefault(9, []).append(dense_fourth)
    slots.setdefault(12, []).append(dense_fifth)

    for u, (h, s) in enumerate(units):
        hs = slice(h * DH, (h + 1) * DH)
        lanes = slice(h * 128, (h + 1) * 128)
        if h == 0:
            for copy in loads[s]:
                copy.wait()
        for n in range(2):
            for work in slots.get(2 * u + n, []):
                work()
            part = slice(n * tile, (n + 1) * tile)
            q, do, o = q_v[s, part, hs], do_v[s, part, hs], o_v[s, part, hs]
            zero = jnp.zeros_like(q)
            both[0:tile, :] = jnp.concatenate([q, zero], 1)
            both[tile : 2 * tile, :] = jnp.concatenate([zero, do], 1)
            product = do.astype(F32) * o.astype(F32)
            high = product.astype(BF16)
            remains = (product - high.astype(F32)).astype(BF16)
            delta[...] = dot(ones, high, NT) + dot(ones, remains, NT)
            dq[...] = jnp.zeros_like(dq)

            def step(j, _, u=u, s=s, h=h, n=n, part=part, lanes=lanes):
                span = pl.ds(pl.multiple_of(j * ktile, ktile), ktile)
                kv = kv_v[s, span, lanes]
                b = both[...]
                found = dot(kv, b, NT)
                p = jnp.exp2(jnp.minimum(found[:, :tile] - lse_v[s, h, 0:1, part], 1.0))
                ds = (p * (found[:, tile:] - delta[0:1, :])).astype(BF16)
                grads = dot(jnp.concatenate([ds, p.astype(BF16)], 1), b)
                if n == 0:
                    dkv[span, :] = grads
                else:
                    obuf[u, span, :] = ((dkv[span, :] + grads) * level).astype(BF16)
                dq[...] += dot(ds, kv, TN)
                return 0

            lax.fori_loop(0, keys // ktile, step, 0)
            found = (dq[:, :DH] * DH**-0.5).astype(BF16)
            for i in range(2):
                qbuf[h, 2 * n + i, :, s * DH : (s + 1) * DH] = found[
                    i * (tile // 2) : (i + 1) * (tile // 2)
                ]
        core_stage(u)
        if s == seqs - 1:
            q_stage(h)
    last = len(units) - 1
    for n in sorted(n for n in slots if n >= 2 * len(units)):
        for work in slots[n]:
            work()
    y_stage(last)
    z_stage(last)
    for copy in waits:
        copy.wait()
    done = pltpu.make_async_copy(dres, dense_out, l_sem.at[0])
    done.start()
    done.wait()


def attend_back_all(seqs_in, ready):
    seqs = len(seqs_in)
    q, _, _, lse, held = seqs_in[0]
    rows, per = q.shape
    heads = per // DH
    units = heads * seqs
    keys = held.shape[0]
    chunk = rows // GROUPS
    a, b = ready[0].shape, ready[2].shape
    a_half, b_half, half = a[0] // 2, b[1], a[1]
    dma = pltpu.SemaphoreType.DMA
    return pl.pallas_call(
        functools.partial(back_kernel, seqs),
        out_shape=[
            jax.ShapeDtypeStruct((heads, GROUPS, chunk, 128), BF16),
            jax.ShapeDtypeStruct((units, GROUPS, chunk, 128), BF16),
            jax.ShapeDtypeStruct(((a_half + b_half) // 4, half), BF16),
        ],
        in_specs=[ANY] * (5 * seqs + 4),
        out_specs=[ANY] * 3,
        scratch_shapes=[
            pltpu.VMEM((seqs, rows, per), BF16),
            pltpu.VMEM((seqs, rows, per), BF16),
            pltpu.VMEM((seqs, rows, per), BF16),
            pltpu.VMEM((seqs, *lse.shape), F32),
            pltpu.VMEM((seqs, keys, 2 * per), BF16),
            pltpu.VMEM((rows, 128), BF16),
            pltpu.VMEM((keys, 128), F32),
            pltpu.VMEM((rows // 2, 128), F32),
            pltpu.VMEM((8, rows // 2), F32),
            pltpu.VMEM((units, keys, 128), BF16),
            pltpu.VMEM((heads, GROUPS, chunk, 128), BF16),
            pltpu.VMEM((units, keys // 2, 128), BF16),
            pltpu.VMEM((units, keys // 4, 128), BF16),
            pltpu.VMEM(a, BF16),
            pltpu.VMEM(b, BF16),
            pltpu.VMEM(a, BF16),
            pltpu.VMEM(b, BF16),
            pltpu.VMEM((2, a_half, half), BF16),
            pltpu.VMEM((2, b_half, half), BF16),
            pltpu.VMEM((a_half, half), BF16),
            pltpu.VMEM((b_half, half), BF16),
            pltpu.VMEM((3 * a_half // 4, half), BF16),
            pltpu.VMEM((3 * b_half // 4, half), BF16),
            pltpu.VMEM(((a_half + b_half) // 4, half), BF16),
            dma((seqs, 5)),
            dma((2, units)),
            dma((2, units)),
            dma((2, units, GROUPS)),
            dma((2, heads, GROUPS)),
            dma((2,)),
            dma((2, 4)),
            dma((2, 2, 2)),
        ],
        compiler_params=pltpu.CompilerParams(
            vmem_limit_bytes=63 * 2**20, collective_id=1, has_side_effects=True
        ),
        cost_estimate=cost(120),
        name="attend_back_all",
    )(*[member for group in seqs_in for member in group], *ready)


def vector_of(vec, row, half):
    both = [vec[k, row + 1 : row + 2, :half].astype(F32) for k in range(2)]
    return jnp.concatenate(both, 1)


def start_kernel(seqs, lengths, order, tokens, wq, wk, wv, wo, wi, wu, *refs):
    sc = Counts(lengths, order)
    vectors, refs = refs[:9], refs[9:]
    q_out, kv_out, refs = refs[:seqs], refs[seqs : 2 * seqs], refs[2 * seqs :]
    vec_out, others, *dense_out = refs[:5]
    full, q_held, kv_held, vec, own_vec, tok, *sems = refs[5:]
    v_sem, wx_sem, wy_sem, wc_sem, l_sem, dx_sem, dc_sem, q_sem, z_sem, y_sem, c_sem, own_sem = sems
    z, y, c, x = position()
    sibling, beside, over = device(z, y, 1 - c, x), device(z, 1 - y, c, x), device(z, y, c, 1 - x)
    line = [None] + [device(z ^ d, y, c, x) for d in range(1, GROUPS)]
    greet([sibling, beside, over] + line[1:])

    def pair(sem, *index):
        return sem.at[(0, *index)], sem.at[(1, *index)]

    waits = []
    half = wq.shape[0]
    eighth = half // 4

    def rows_of(which, cc, yy):
        start = which * half + (2 * cc + yy) * eighth
        return pl.ds(pl.multiple_of(start, 16), eighth)

    own_rows = pl.ds(pl.multiple_of((2 * c + y) * eighth, 16), eighth)
    tok_in = pltpu.make_async_copy(tokens, tok, l_sem.at[6])
    tok_in.start()
    flow = {}
    turns = (1, 2, 0)
    locals_of = []
    for i in turns:
        own = (wq, wk, wv)[i]
        flow["x", i] = send(
            own.at[own_rows], full.at[i, rows_of(x, c, y)], pair(wx_sem, i), over
        )
    for i in turns:
        own = (wq, wk, wv)[i]
        place = full.at[i, pl.ds(pl.multiple_of(x * half, half), half)]
        copy = pltpu.make_async_copy(own, place, l_sem.at[i])
        copy.start()
        locals_of.append(copy)
    own_vec[...] = jnp.zeros_like(own_vec)
    for i, one in enumerate(vectors):
        row = (i + 1) % len(vectors)
        own_vec[row : row + 1, : one.shape[0]] = one[...].astype(F32)[None].astype(BF16)
    vec[x] = own_vec[...]
    vec_flow = send(own_vec, vec.at[x], pair(v_sem), over)

    def after_x(i):
        flow["x", i].wait()
        got = full.at[i, rows_of(1 - x, c, y)]
        flow["y", i] = send(got, got, pair(wy_sem, i), beside)
        flow["c", i, 0] = send(got, got, pair(wc_sem, i, 0), sibling)

    def after_y(i):
        flow["y", i].wait()
        got = full.at[i, rows_of(1 - x, c, 1 - y)]
        flow["c", i, 1] = send(got, got, pair(wc_sem, i, 1), sibling)

    def after_core(i):
        flow["c", i, 0].wait()
        flow["c", i, 1].wait()

    rows, width = tok.shape[1:]
    per = width // GROUPS
    heads = per // DH
    tok_in.wait()
    flat = tok[...].reshape(seqs * rows, width)
    valid = jnp.concatenate([valid_rows(sc, s, rows) for s in range(seqs)], 0) > 0.0
    after_x(1)
    after_x(2)
    after_y(1)
    after_x(0)
    dense_weights = (wo, wi, wu)
    for i, weight in enumerate(dense_weights):
        n = weight.shape[0] // 2
        part = pl.ds(pl.multiple_of(c * n, 16), n)
        flow["dx", i] = send(weight.at[part], dense_out[i].at[part], pair(dx_sem, i), over)
    after_y(2)
    vec_flow.wait()

    def bias(row):
        return vector_of(vec, row, half)

    for copy in locals_of:
        copy.wait()
    after_core(1)
    keys = jnp.where(valid, dot(flat, full[1]), 0.0).astype(BF16)
    after_y(0)
    after_core(2)
    values = jnp.where(valid, dot(flat, full[2]) + bias(1), 0.0).astype(BF16)
    for s in range(seqs):
        rs = slice(s * rows, (s + 1) * rows)
        for g in range(GROUPS):
            for h in range(heads):
                cols = slice(g * per + h * DH, g * per + (h + 1) * DH)
                kv_held[s, g, :, h * 128 : (h + 1) * 128] = jnp.concatenate(
                    [keys[rs, cols], values[rs, cols]], 1
                )
        for d in range(1, GROUPS):
            flow["z", s, d] = send(
                kv_held.at[s, z ^ d], kv_out[s].at[0, z], pair(z_sem, s, d), line[d]
            )

    def pass_on(s, d, src):
        g = z ^ d
        flow["ky", s, d] = send(src, kv_out[s].at[1, g], pair(y_sem, s, d), beside)
        waits.append(send(src, kv_out[s].at[2, g], pair(c_sem, s, d, 0), sibling))

    def pass_core(s, d):
        flow["ky", s, d].wait()
        got = kv_out[s].at[1, z ^ d]
        waits.append(send(got, kv_out[s].at[3, z ^ d], pair(c_sem, s, d, 1), sibling))

    for s in range(seqs):
        own = pltpu.make_async_copy(kv_held.at[s, z], kv_out[s].at[0, z], own_sem.at[s, 0])
        own.start()
        waits.append(own)
        pass_on(s, 0, kv_held.at[s, z])
    after_core(0)
    queries = ((dot(flat, full[0]) + bias(0)) * (DH**-0.5 / LN2)).astype(BF16)
    for s in range(seqs):
        rs = slice(s * rows, (s + 1) * rows)
        for g in range(GROUPS):
            q_held[s, g] = queries[rs, g * per : (g + 1) * per]
    for i in range(3):
        place = full.at[i, pl.ds(pl.multiple_of((1 - x) * half, half), half)]
        copy = pltpu.make_async_copy(place, others.at[i], l_sem.at[3 + i])
        copy.start()
        waits.append(copy)
    copy = pltpu.make_async_copy(vec, vec_out, l_sem.at[7])
    copy.start()
    waits.append(copy)
    for s in range(seqs):
        for d in range(1, GROUPS):
            flow["z", s, d].wait()
            pass_on(s, d, kv_out[s].at[0, z ^ d])
            if d > 1:
                pass_core(s, d - 2)
        for d in range(1, GROUPS):
            waits.append(send(q_held.at[s, z ^ d], q_out[s].at[z], pair(q_sem, s, d), line[d]))
        own = pltpu.make_async_copy(q_held.at[s, z], q_out[s].at[z], own_sem.at[s, 1])
        own.start()
        waits.append(own)
        pass_core(s, 2)
        pass_core(s, 3)
    for i, weight in enumerate(dense_weights):
        flow["dx", i].wait()
        n = weight.shape[0] // 2
        got = dense_out[i].at[pl.ds(pl.multiple_of(c * n, 16), n)]
        waits.append(send(got, got, pair(dc_sem, i), sibling))
    for copy in waits:
        copy.wait()


def start(lengths, order, tok, weights, vectors):
    seqs, rows, width = tok.shape
    per = width // GROUPS
    half = weights[0].shape[0]
    joined = (16, vectors[-1].shape[0])
    dma = pltpu.SemaphoreType.DMA
    return pl.pallas_call(
        functools.partial(start_kernel, seqs),
        out_shape=[jax.ShapeDtypeStruct((GROUPS, rows, per), BF16)] * seqs
        + [jax.ShapeDtypeStruct((4, GROUPS, rows, 2 * per), BF16)] * seqs
        + [
            jax.ShapeDtypeStruct((2, *joined), BF16),
            jax.ShapeDtypeStruct((3, half, width), BF16),
        ]
        + [jax.ShapeDtypeStruct(w.shape, BF16) for w in weights[3:]],
        in_specs=[SMEM] * 2 + [ANY] * 7 + [VMEM] * 9,
        out_specs=[ANY] * (2 * seqs + 5),
        scratch_shapes=[
            pltpu.VMEM((3, width, width), BF16),
            pltpu.VMEM((seqs, GROUPS, rows, per), BF16),
            pltpu.VMEM((seqs, GROUPS, rows, 2 * per), BF16),
            pltpu.VMEM((2, *joined), BF16),
            pltpu.VMEM(joined, BF16),
            pltpu.VMEM(tok.shape, BF16),
            dma((2,)),
            dma((2, 3)),
            dma((2, 3)),
            dma((2, 3, 2)),
            dma((8,)),
            dma((2, 3)),
            dma((2, 3)),
            dma((2, seqs, GROUPS)),
            dma((2, seqs, GROUPS)),
            dma((2, seqs, GROUPS)),
            dma((2, seqs, GROUPS, 2)),
            dma((seqs, 2)),
        ],
        compiler_params=pltpu.CompilerParams(
            vmem_limit_bytes=63 * 2**20, collective_id=4, has_side_effects=True
        ),
        cost_estimate=cost(80),
        name="start",
    )(lengths, order, tok, *weights, *vectors)


def middle_stage(s, att, mask, tok, teach, vec, weights, keep, outs, first_done):
    wo, wi, wu, slope = weights
    att_k, br_k, hl_k, il_k, act_k, ol_k = keep
    out, fg, sums, wide_sums = outs
    rows = att.shape[0]
    hidden = wi.shape[1]
    tile = 512
    rs = slice(s * rows, (s + 1) * rows)
    half = tok.shape[2] // 2
    out_bias, gain_one, shift_one, outer_bias, gain_two, shift_two = (
        vector_of(vec, row, half) for row in range(2, 8)
    )
    add = functools.partial(jnp.sum, axis=0, keepdims=True)

    def collect(target, value):
        if s == 0:
            target[...] = value
        else:
            target[...] += value

    att_k[rs, :] = att
    first_done[0]()
    first = tok[s].astype(F32) + dot(att, wo[...]) + out_bias
    normed_one, inverse_one = norm(first)
    hidden_in = normed_one * gain_one + shift_one
    hl = hidden_in.astype(BF16)
    hl_k[rs, :] = hl
    first_done[1]()
    second = hidden_in + outer_bias
    for n in range(hidden // tile):
        cols = slice(n * tile, (n + 1) * tile)
        k, begin = divmod(n * tile, hidden // 2)
        inner = dot(hl, wi[:, cols]) + vec[k, 0:1, begin : begin + tile].astype(F32)
        below, density = normal_parts(inner)
        act = (inner * below).astype(BF16)
        act_k[rs, cols] = act
        slope[:, cols] = below + inner * density
        second += dot(act, wu[cols, :])
    normed_two, inverse_two = norm(second)
    final = normed_two * gain_two + shift_two
    out[s] = final.astype(BF16)
    residue = (final - teach[s].astype(F32)) * mask
    collect(sums.at[0:1], add(residue * normed_two))
    collect(sums.at[1:2], add(residue))
    collect(sums.at[6:7], add(residue * residue))
    second_grad = norm_back(residue * gain_two, normed_two, inverse_two)
    ol = second_grad.astype(BF16)
    ol_k[rs, :] = ol
    collect(sums.at[2:3], add(ol.astype(F32)))
    hidden_grad = second_grad
    for n in range(hidden // tile):
        cols = slice(n * tile, (n + 1) * tile)
        il = (dot(ol, wu[cols, :], NT) * slope[:, cols]).astype(BF16)
        il_k[rs, cols] = il
        collect(wide_sums.at[0:1, cols], add(il.astype(F32)))
        hidden_grad += dot(il, wi[:, cols], NT)
    first_grad = norm_back(hidden_grad * gain_one, normed_one, inverse_one)
    fg[s] = first_grad
    br = first_grad.astype(BF16)
    br_k[rs, :] = br
    collect(sums.at[3:4], add(hidden_grad * normed_one))
    collect(sums.at[4:5], add(hidden_grad))
    collect(sums.at[5:6], add(br.astype(F32)))
    return dot(br, wo[...], NT).astype(BF16)


def middle_kernel(seqs, lengths, order, tok, teach, vec, *refs):
    sc = Counts(lengths, order)
    attended, weights, refs = refs[:seqs], refs[seqs : seqs + 6], refs[seqs + 6 :]
    out, fg, sums, wide_sums, a_own, a_give, b_own, b_give = refs[:8]
    grads_in, refs = refs[8 : 8 + seqs], refs[8 + seqs :]
    wo, wi, wu, slope, o_in, g_out, att_k, br_k, hl_k, il_k, act_k, ol_k = refs[:12]
    mine, give, given, w_sem, o_sem, g_sem, c_sem = refs[12:]
    z, y, c, x = position()
    sibling = device(z, y, 1 - c, x)
    line = [None] + [device(z ^ d, y, c, x) for d in range(1, GROUPS)]
    greet([sibling] + line[1:])
    coming, going = {}, {}
    for s in range(seqs):
        for d in range(1, GROUPS):
            sems = o_sem.at[0, s, d], o_sem.at[1, s, d]
            coming[s, d] = send(attended[s].at[z ^ d], o_in.at[s, z], sems, line[d])
        coming[s, 0] = pltpu.make_async_copy(attended[s].at[z], o_in.at[s, z], o_sem.at[0, s, 0])
        coming[s, 0].start()
    copies = [
        half_copies(full, *weights[2 * i : 2 * i + 2], w_sem, 2 * i)
        for i, full in enumerate((wo, wi, wu))
    ]
    for group in copies:
        for copy in group:
            copy.start()

    def loaded(which):
        for i in which:
            for copy in copies[i]:
                copy.wait()

    rows = tok.shape[1]
    per = o_in.shape[3]
    for s in range(seqs):
        for d in range(GROUPS):
            coming[s, d].wait()
        att = jnp.concatenate([o_in[s, g] for g in range(GROUPS)], 1)
        mask = valid_rows(sc, s, rows)
        waits = (lambda: loaded([0]), lambda: loaded([1, 2])) if s == 0 else (lambda: None,) * 2
        found = middle_stage(
            s,
            att,
            mask,
            tok,
            teach,
            vec,
            (wo, wi, wu, slope),
            (att_k, br_k, hl_k, il_k, act_k, ol_k),
            (out, fg, sums, wide_sums),
            waits,
        )
        for g in range(GROUPS):
            g_out[s, g] = found[:, g * per : (g + 1) * per]
        for d in range(1, GROUPS):
            sems = g_sem.at[0, s, d], g_sem.at[1, s, d]
            going[s, d] = send(g_out.at[s, z ^ d], grads_in[s].at[z], sems, line[d])
        going[s, 0] = pltpu.make_async_copy(g_out.at[s, z], grads_in[s].at[z], g_sem.at[0, s, 0])
        going[s, 0].start()
    sums[7:8, :] = jnp.zeros((1, sums.shape[1]), F32)

    half = wo.shape[0] // 2
    hidden = wi.shape[1]
    blocks = hidden // (2 * half)

    def weight_grads(target, part):
        def cols(start):
            return pl.ds(pl.multiple_of(start + part * half, 128), half)

        for k in range(2):
            ks = slice(k * half, (k + 1) * half)
            target[k, 0:half, :] = dot(att_k[:, ks], br_k[:, cols(0)], TN).astype(BF16)
            for t in range(blocks):
                target[k, (1 + t) * half : (2 + t) * half, :] = dot(
                    hl_k[:, ks], il_k[:, cols(2 * t * half)], TN
                ).astype(BF16)
            base = (1 + blocks) * half
            for t in range(blocks):
                rows_of = slice((k * blocks + t) * half, (k * blocks + t + 1) * half)
                target[k, base + t * half : base + (t + 1) * half, :] = dot(
                    act_k[:, rows_of], ol_k[:, cols(0)], TN
                ).astype(BF16)

    weight_grads(give, 1 - c)
    core = [
        send(give.at[k], given.at[k], (c_sem.at[0, k], c_sem.at[1, k]), sibling) for k in range(2)
    ]
    weight_grads(mine, c)
    for copy in core:
        copy.wait()
    cut, b_half = a_own.shape[0], b_own.shape[1]
    a_own[...] = add_low(mine[x, 0:cut], given[x, 0:cut])
    a_give[...] = add_low(mine[1 - x, 0:cut], given[1 - x, 0:cut])
    for k in range(2):
        for target, which in ((b_own, y), (b_give, 1 - y)):
            part = pl.ds(pl.multiple_of(cut + which * b_half, 16), b_half)
            target[k] = add_low(mine[k, part], given[k, part])
    for copy in going.values():
        copy.wait()


def cut_of(total):
    return total // 256 * 128


def middle(lengths, order, tok, teach, vec, attended, weights):
    seqs, rows, width = tok.shape
    hidden = 2 * vec.shape[2]
    half = width // 2
    total = half + hidden
    cut = cut_of(total)
    dma = pltpu.SemaphoreType.DMA
    narrow, wide = (seqs * rows, width), (seqs * rows, hidden)
    b_shape = jax.ShapeDtypeStruct((2, (total - cut) // 2, half), BF16)
    a_shape = jax.ShapeDtypeStruct((cut, half), BF16)
    groups, _, per = attended[0].shape
    return pl.pallas_call(
        functools.partial(middle_kernel, seqs),
        out_shape=[
            jax.ShapeDtypeStruct(tok.shape, BF16),
            jax.ShapeDtypeStruct(tok.shape, F32),
            jax.ShapeDtypeStruct((8, width), F32),
            jax.ShapeDtypeStruct((1, hidden), F32),
            a_shape,
            a_shape,
            b_shape,
            b_shape,
        ]
        + [jax.ShapeDtypeStruct(a.shape, BF16) for a in attended],
        in_specs=[SMEM] * 2 + [VMEM] * 3 + [ANY] * (seqs + 6),
        out_specs=[VMEM] * 8 + [ANY] * seqs,
        scratch_shapes=[
            pltpu.VMEM((width, width), BF16),
            pltpu.VMEM((width, hidden), BF16),
            pltpu.VMEM((hidden, width), BF16),
            pltpu.VMEM((rows, hidden), F32),
            pltpu.VMEM((seqs, groups, rows, per), BF16),
            pltpu.VMEM((seqs, groups, rows, per), BF16),
            pltpu.VMEM(narrow, BF16),
            pltpu.VMEM(narrow, BF16),
            pltpu.VMEM(narrow, BF16),
            pltpu.VMEM(wide, BF16),
            pltpu.VMEM(wide, BF16),
            pltpu.VMEM(narrow, BF16),
            pltpu.VMEM((2, total, half), BF16),
            pltpu.VMEM((2, total, half), BF16),
            pltpu.VMEM((2, total, half), BF16),
            dma((6,)),
            dma((2, seqs, groups)),
            dma((2, seqs, groups)),
            dma((2, 2)),
        ],
        compiler_params=pltpu.CompilerParams(
            vmem_limit_bytes=63 * 2**20, collective_id=3, has_side_effects=True
        ),
        cost_estimate=cost(60),
        name="middle",
    )(lengths, order, tok, teach, vec, *attended, *weights)


def finish_kernel(
    seqs, lengths, order, tok, fg, rq, rkv, dense_sums, wide_sums, ready, wq, wk, wv, others, *rest
):
    sc = Counts(lengths, order)
    tg, out, dense_out, small_out, *rest = rest
    full, grads, acc, from_core, from_x, from_y, from_z, res, vec, vec_in, dense_res = rest[:11]
    w_sems, sems, small_sems, d_sems, last_sem = rest[11:]
    z, y, c, x = position()
    sibling, beside, over = device(z, y, 1 - c, x), device(z, 1 - y, c, x), device(z, y, c, 1 - x)
    line = [None] + [device(z ^ d, y, c, x) for d in range(1, GROUPS)]
    greet([sibling, beside, over] + line[1:])

    a_half = cut_of(dense_res.shape[1]) // 2
    b_half = dense_res.shape[1] // 2 - a_half
    low_bit, high_bit = lax.rem(z, 2), z // 2
    dense_parts = ((0, a_half, y * a_half), (a_half // 4, b_half, 2 * a_half + y * b_half))

    def dense_rows(start, n):
        return dense_res.at[c, pl.ds(pl.multiple_of(start, 16), n)]

    def d_pair(k, i):
        return d_sems.at[0, k, i], d_sems.at[1, k, i]

    dense_flows = []
    for i, (start, n, base) in enumerate(dense_parts):
        place = dense_rows(base + low_bit * (n // 2) + high_bit * (n // 4), n // 4)
        src = ready.at[start : start + n // 4]
        place[...] = src[...]
        dense_flows.append(send(src, place, d_pair(0, i), line[2]))

    def dense_near():
        for i, (_, n, base) in enumerate(dense_parts):
            dense_flows[i].wait()
            place = dense_rows(base + low_bit * (n // 2), n // 2)
            dense_flows[i] = send(place, place, d_pair(1, i), line[1])

    def dense_y():
        for i, (_, n, base) in enumerate(dense_parts):
            dense_flows[i].wait()
            place = dense_rows(base, n)
            dense_flows[i] = send(place, place, d_pair(2, i), beside)

    def dense_core():
        for i, (_, n, _) in enumerate(dense_parts):
            dense_flows[i].wait()
            place = dense_res.at[c, pl.ds(2 * a_half * i, 2 * n)]
            dense_flows[i] = send(place, place, d_pair(3, i), sibling)

    rows, width = tok.shape[1:]
    heads = width // GROUPS // DH
    copies = []
    for i, own in enumerate((wq, wk, wv)):
        copies += half_copies(full.at[i], own, others.at[i], w_sems, 2 * i)
    for copy in copies:
        copy.start()

    def head(i, s, g, h):
        if i == 0:
            return rq[h, g, :, s * DH : (s + 1) * DH]
        return rkv[h * seqs + s, g, :, (i - 1) * DH : i * DH]

    def whole(i):
        each = [
            jnp.concatenate([head(i, s, g, h) for g in range(GROUPS) for h in range(heads)], 1)
            for s in range(seqs)
        ]
        return jnp.concatenate(each, 0)

    valid = jnp.concatenate([valid_rows(sc, s, rows) for s in range(seqs)], 0) > 0.0
    parted = [whole(0)] + [jnp.where(valid, whole(i), jnp.zeros((), BF16)) for i in (1, 2)]
    flat = tok[...].reshape(seqs * rows, width)
    wide = width // 2
    for i, grad in enumerate(parted):
        found = dot(flat, grad, TN).astype(BF16)
        for n in range(2):
            for t in range(width // 128):
                grads[t % 3, t // 3, n, i * wide : (i + 1) * wide, :] = found[
                    n * wide : (n + 1) * wide, t * 128 : (t + 1) * 128
                ]
    lines_of = [dense_sums[i : i + 1, :] for i in range(7)]
    lines_of += [jnp.sum(grad.astype(F32), 0, keepdims=True) for grad in (parted[0], parted[2])]
    lines_of.append(wide_sums[...])
    row = 0
    for one in lines_of:
        for t in range(one.shape[1] // 128):
            vec[row : row + 1, :] = one[:, t * 128 : (t + 1) * 128]
            row += 1
    valid_count = sum(jnp.clip(sc[i], 0, BLK) for i in range(2 * seqs))
    vec[row:, :] = jnp.full((vec.shape[0] - row, 128), valid_count.astype(F32))

    parts, rows_each = grads.shape[0], grads.shape[3]
    half, piece = rows_each // 2, rows_each // 8
    own_half = pl.ds(pl.multiple_of(y * half, half), half)
    other_half = pl.ds(pl.multiple_of((1 - y) * half, half), half)

    def piece_of(g):
        return pl.ds(pl.multiple_of(y * half + g * piece, piece), piece)

    def pair(k, p):
        return sems.at[0, k, p], sems.at[1, k, p]

    def small_pair(k):
        return small_sems.at[0, k], small_sems.at[1, k]

    core = [
        send(grads.at[p, 1 - c], from_core.at[p], pair(0, p), sibling) for p in range(parts)
    ]
    short = send(vec, vec_in.at[0], small_pair(0), sibling)
    flows = []
    for p in range(parts):
        core[p].wait()
        acc[p] = add_low(grads[p, c], from_core[p])
        if p == 1:
            flows.append(send(acc.at[p, :, other_half], from_y.at[p], pair(1, p), beside))
        else:
            flows.append(send(acc.at[p, 1 - x], from_x.at[p], pair(1, p), over))
    dense_near()
    for copy in copies:
        copy.wait()
    total = jnp.concatenate([fg[s] for s in range(seqs)], 0)
    for i, grad in enumerate(parted):
        total += dot(grad, full[i], NT)
    tg[...] = total.reshape(seqs, rows, width)
    short.wait()
    vec_in[8] = vec[...] + vec_in[0]
    short = send(vec_in.at[8], vec_in.at[1], small_pair(1), over)
    for p in (1, 0, 2):
        flows[p].wait()
        if p == 1:
            for k in range(2):
                acc[p, k, own_half] = add_low(acc[p, k, own_half], from_y[p, k])
            flows[p] = send(acc.at[p, 1 - x, own_half], from_x.at[p, own_half], pair(2, p), over)
        else:
            acc[p, x] = add_low(acc[p, x], from_x[p])
            flows[p] = send(acc.at[p, x, other_half], from_y.at[p, 0], pair(2, p), beside)
    short.wait()
    vec[...] = vec_in[8] + vec_in[1]
    short = send(vec, vec_in.at[2], small_pair(2), beside)
    dense_y()
    lines = {}
    for p in (1, 0, 2):
        flows[p].wait()
        if p == 1:
            acc[p, x, own_half] = add_low(acc[p, x, own_half], from_x[p, own_half])
        else:
            acc[p, x, own_half] = add_low(acc[p, x, own_half], from_y[p, 0])
        for d in range(1, GROUPS):
            lines[p, d] = send(
                acc.at[p, x, piece_of(z ^ d)], from_z.at[p, d], pair(2 + d, p), line[d]
            )
    short.wait()
    vec[...] = vec[...] + vec_in[2]
    vec_in[4 + z] = vec[...]
    shorts = [
        send(vec, vec_in.at[4 + z], small_pair(2 + d), line[d]) for d in range(1, GROUPS)
    ]
    spread = {}
    for p in (1, 0, 2):
        total = acc[p, x, piece_of(z)].astype(F32)
        for d in range(1, GROUPS):
            lines[p, d].wait()
            total += from_z[p, d].astype(F32)
        res[c, p, piece_of(z)] = total.astype(BF16)
        for d in range(1, GROUPS):
            spread[p, d] = send(
                res.at[c, p, piece_of(z)],
                res.at[c, p, piece_of(z)],
                pair(5 + d, p),
                line[d],
            )
    for p in (1, 0, 2):
        for d in range(1, GROUPS):
            spread[p, d].wait()
        flows[p] = send(
            res.at[c, p, own_half], res.at[c, p, own_half], pair(9, p), beside
        )
    dense_core()
    for copy in shorts:
        copy.wait()
    small_out[...] = vec_in[4] + vec_in[5] + (vec_in[6] + vec_in[7])
    for p in (1, 0, 2):
        flows[p].wait()
        flows[p] = send(res.at[c, p], res.at[c, p], pair(10, p), sibling)
    for copy in dense_flows:
        copy.wait()
    done = [pltpu.make_async_copy(dense_res, dense_out, last_sem.at[1])]
    done[0].start()
    for p in (1, 0, 2):
        flows[p].wait()
    done.append(pltpu.make_async_copy(res, out, last_sem.at[0]))
    done[1].start()
    for copy in done:
        copy.wait()


def finish(lengths, order, tok, fg, rq, rkv, sums, wide_sums, ready, wq, wk, wv, others):
    seqs, _, width = tok.shape
    short = (-(-(9 * width + wide_sums.shape[1] + 128) // 1024) * 8, 128)
    parts, rows, lanes = 3, 3 * (width // 2), 128
    total, half = 8 * ready.shape[0], ready.shape[1]
    dma = pltpu.SemaphoreType.DMA
    return pl.pallas_call(
        functools.partial(finish_kernel, seqs),
        out_shape=[
            jax.ShapeDtypeStruct(tok.shape, F32),
            jax.ShapeDtypeStruct((2, parts, rows, lanes), BF16),
            jax.ShapeDtypeStruct((2, total, half), BF16),
            jax.ShapeDtypeStruct(short, F32),
        ],
        in_specs=[SMEM] * 2 + [VMEM] * 7 + [ANY] * 4,
        out_specs=[VMEM, ANY, ANY, VMEM],
        scratch_shapes=[
            pltpu.VMEM((3, width, width), BF16),
            pltpu.VMEM((parts, 2, 2, rows, lanes), BF16),
            pltpu.VMEM((parts, 2, rows, lanes), BF16),
            pltpu.VMEM((parts, 2, rows, lanes), BF16),
            pltpu.VMEM((parts, rows, lanes), BF16),
            pltpu.VMEM((parts, 2, rows // 2, lanes), BF16),
            pltpu.VMEM((parts, GROUPS, rows // 8, lanes), BF16),
            pltpu.VMEM((2, parts, rows, lanes), BF16),
            pltpu.VMEM(short, F32),
            pltpu.VMEM((9, *short), F32),
            pltpu.VMEM((2, total, half), BF16),
            dma((6,)),
            dma((2, 11, parts)),
            dma((2, 6)),
            dma((2, 4, 2)),
            dma((2,)),
        ],
        compiler_params=pltpu.CompilerParams(
            vmem_limit_bytes=63 * 2**20, collective_id=2, has_side_effects=True
        ),
        cost_estimate=cost(70),
        name="finish",
    )(lengths, order, tok, fg, rq, rkv, sums, wide_sums, ready, wq, wk, wv, others)


def unpack_kernel(qkv, total, *refs):
    outs, (narrow, inner, outer, sems) = refs[:6], refs[6:]
    half = qkv.shape[2] // 3
    blocks = inner.shape[1] // (2 * half)
    copies = []

    def leave(src, i):
        copy = pltpu.make_async_copy(src, outs[i], sems.at[i])
        copy.start()
        copies.append(copy)

    for k in range(2):
        cols = slice(k * half, (k + 1) * half)
        outer[:, cols] = total[k, (1 + blocks) * half :].astype(F32)
    leave(outer, 5)
    for k in range(2):
        for t in range(blocks):
            cols = slice((2 * t + k) * half, (2 * t + k + 1) * half)
            inner[:, cols] = total[k, (1 + t) * half : (2 + t) * half].astype(F32)
    leave(inner, 4)
    for i in range(3):
        for k in range(2):
            for p in range(3):
                cols = slice((3 * k + p) * 128, (3 * k + p + 1) * 128)
                narrow[i, :, cols] = qkv[k, p, i * half : (i + 1) * half].astype(F32)
        leave(narrow.at[i], i)
    for k in range(2):
        narrow[3, :, k * half : (k + 1) * half] = total[k, 0:half].astype(F32)
    leave(narrow.at[3], 3)
    for copy in copies:
        copy.wait()


def unpack(qkv, total, hidden):
    half = total.shape[2]
    narrow = jax.ShapeDtypeStruct((half, 2 * half), F32)
    return pl.pallas_call(
        unpack_kernel,
        out_shape=[narrow] * 4
        + [
            jax.ShapeDtypeStruct((half, hidden), F32),
            jax.ShapeDtypeStruct((hidden // 2, 2 * half), F32),
        ],
        in_specs=[VMEM] * 2,
        out_specs=[ANY] * 6,
        scratch_shapes=[
            pltpu.VMEM((4, half, 2 * half), F32),
            pltpu.VMEM((half, hidden), F32),
            pltpu.VMEM((hidden // 2, 2 * half), F32),
            pltpu.SemaphoreType.DMA((6,)),
        ],
        compiler_params=ROOM,
        cost_estimate=cost(10),
        name="unpack",
    )(qkv, total)


def pick(table, index):
    places = jnp.arange(table.shape[0], dtype=jnp.int32)
    return jnp.sum(jnp.where(index[..., None] == places, table, 0), -1)


def shards(
    size,
    tokens,
    teacher,
    lengths,
    block_order,
    query_weight,
    query_bias,
    key_weight,
    value_weight,
    value_bias,
    out_weight,
    out_bias,
    gain_one,
    shift_one,
    inner_weight,
    inner_bias,
    outer_weight,
    outer_bias,
    gain_two,
    shift_two,
):
    seqs, rows, width = tokens.shape
    per_plane = size // GROUPS
    blocks_each = rows // BLK
    ctx, x = lax.axis_index("ctx"), lax.axis_index("wa")
    c, place = lax.rem(ctx, 2), lax.rem(ctx, per_plane)
    masks = [1 << b for b in reversed(range(per_plane.bit_length() - 1))]
    offsets = [0]
    for m in masks:
        offsets += [o ^ m for o in offsets]

    def across(value):
        return lax.ppermute(value, "wa", [(0, 1), (1, 0)])

    def flip(value, m):
        return lax.ppermute(value, "ctx", [(i, i ^ m) for i in range(size)])

    lines = [[g * per_plane + r for g in range(GROUPS)] for r in range(per_plane)]

    def turn(value):
        return lax.all_to_all(value, "ctx", 0, 0, axis_index_groups=lines)

    cores = [[i for i in range(size) if i % 2 == k] for k in range(2)]

    def paired(mine):
        sibling = flip(mine, 1)
        return jnp.where(c == 0, jnp.stack([mine, sibling]), jnp.stack([sibling, mine]))

    def reduced(grad):
        four = grad.reshape(2, 2, *grad.shape[1:])
        keep = lax.dynamic_index_in_dim(four, c, 1, False)
        give = lax.dynamic_index_in_dim(four, 1 - c, 1, False)
        keep = add_low(keep, flip(give, 1))
        mine = lax.dynamic_index_in_dim(keep, x, 0, False)
        mine = add_low(mine, across(lax.dynamic_index_in_dim(keep, 1 - x, 0, False)))
        return paired(lax.psum(mine, "ctx", axis_index_groups=cores))

    def reduced_dense(grad):
        four = grad.reshape(2, 2, *grad.shape[1:])
        keep = lax.dynamic_index_in_dim(four, c, 1, False)
        give = lax.dynamic_index_in_dim(four, 1 - c, 1, False)
        keep = add_low(keep, flip(give, 1))
        mine = lax.psum_scatter(
            keep.reshape(-1, keep.shape[-1]), "wa", scatter_dimension=0, tiled=True
        )
        return lax.psum(mine, "ctx", axis_index_groups=cores)

    vectors = (
        query_bias,
        value_bias,
        out_bias,
        gain_one,
        shift_one,
        outer_bias,
        gain_two,
        shift_two,
        inner_bias,
    )
    half, hidden = width // 2, 2 * inner_bias.shape[0]
    fused = per_plane == 4

    if fused:
        found = start(
            lengths,
            block_order,
            tokens,
            (query_weight, key_weight, value_weight, out_weight, inner_weight, outer_weight),
            vectors,
        )
        queries = [q.reshape(-1, BLK, q.shape[2]) for q in found[:seqs]]
        pieces = [[kv.reshape(-1, BLK, kv.shape[3])] for kv in found[seqs : 2 * seqs]]
        pair, others, *rest = found[2 * seqs :]
        dense_weights = [out_weight, rest[0], inner_weight, rest[1], outer_weight, rest[2]]
    else:
        count = block_order.shape[0]
        ids = jnp.arange(count, dtype=jnp.int32)
        owner = ids // blocks_each
        index_of = jnp.array([offsets.index(o) for o in range(per_plane)], jnp.int32)
        piece_of = pick(index_of, (owner % per_plane) ^ place)
        spot = (piece_of * GROUPS + owner // per_plane) * blocks_each + ids % blocks_each
        key_order = jnp.sum(jnp.where(block_order[None, :] == ids[:, None], spot[None, :], 0), 1)
        near = jnp.arange(GROUPS * blocks_each, dtype=jnp.int32)
        near_ids = (near // blocks_each * per_plane + place) * blocks_each + near % blocks_each
        near_pos = pick(block_order, near_ids)
        rank = jnp.sum((near_pos[None, :] < near_pos[:, None]).astype(jnp.int32), 1)
        query_order = jnp.sum(jnp.where(rank[None, :] == near[:, None], near[None, :], 0), 1)
        own_pos = pick(block_order, ctx * blocks_each + jnp.arange(blocks_each, dtype=jnp.int32))
        scalars, row_counts = [], []
        for s in range(seqs):
            used = jnp.sum((near_pos * BLK < lengths[s]).astype(jnp.int32))
            head = jnp.concatenate([lengths[s][None], used[None], jnp.zeros((6,), jnp.int32)])
            scalars.append(jnp.concatenate([head, query_order, key_order]))
            row_counts.append(jnp.clip(lengths[s] - own_pos * BLK, 0, BLK))

        counts = jnp.concatenate(row_counts)
        own_vec = jnp.concatenate(vectors)[None]
        other_vec = across(own_vec)
        pair = jnp.where(
            x == 0, jnp.stack([own_vec, other_vec]), jnp.stack([other_vec, own_vec])
        ).astype(F32)
        narrow = pair[:, 0, : 8 * half].reshape(2, 8, half).swapaxes(0, 1).reshape(8, width)
        wide_vec = pair[:, 0, 8 * half :].reshape(1, -1)

        def quarter(weight):
            n = weight.shape[0] // 2
            return lax.dynamic_slice_in_dim(weight, c * n, n, 0)

        first_qkv = across(
            jnp.concatenate([quarter(w) for w in (query_weight, key_weight, value_weight)], 0)
        )
        second_qkv = flip(first_qkv, 1)
        dense_weights = []
        last = first_qkv
        for weight in (out_weight, inner_weight, outer_weight):
            piece, last = lax.optimization_barrier((quarter(weight), last))
            last = across(piece)
            dense_weights += [weight, last, flip(last, 1)]

        projected = project(
            counts, tokens, narrow, query_weight, key_weight, value_weight, first_qkv, second_qkv
        )
        queries, pieces = [], []
        for s in range(seqs):
            kv = turn(projected[2 * s + 1])
            queries.append(turn(projected[2 * s]).reshape(-1, BLK, width // GROUPS))
            held = [kv.reshape(-1, BLK, kv.shape[2])]
            for m in masks:
                held += [flip(piece, m) for piece in held]
            pieces.append(held)

    attended, lses = [], []
    for s in range(seqs):
        o, lse = attend(s, per_plane, lengths, block_order, queries[s], pieces[s])
        attended.append(o.reshape(queries[s].shape))
        lses.append(lse)
    if fused:
        fours = [a.reshape(GROUPS, rows, -1) for a in attended]
        found = middle(lengths, block_order, tokens, teacher, pair, fours, dense_weights)
        output, firsts, sums, wide_sums, a_own, a_give, b_own, b_give = found[:8]
        heads_grad = [g.reshape(queries[0].shape) for g in found[8:]]
        ready = (a_own, a_give, b_own, b_give)
    else:
        dense_out = []
        for s in range(seqs):
            o4 = turn(attended[s].reshape(GROUPS, rows, -1))
            dense_out.append(
                dense(
                    row_counts[s], o4, tokens[s], teacher[s], narrow[2:], wide_vec, dense_weights
                )
            )
        output = jnp.stack([d[0] for d in dense_out])
        first_grads = [d[1] for d in dense_out]
        heads_grad = [turn(d[2]).reshape(queries[s].shape) for s, d in enumerate(dense_out)]
        sums = sum(d[9] for d in dense_out)
        wide_sums = sum(d[10] for d in dense_out)
        dense_sums = [reduced_dense(g) for g in dense_grads([d[3:9] for d in dense_out])]

    if fused:
        flat_rows = (GROUPS * rows, width // GROUPS)
        rq, rkv, ready = attend_back_all(
            [
                [
                    *(a.reshape(flat_rows) for a in (queries[s], heads_grad[s], attended[s])),
                    lses[s],
                    pieces[s][0].reshape(-1, pieces[s][0].shape[2]),
                ]
                for s in range(seqs)
            ],
            ready,
        )
    else:
        dqs, dkvs = [], []
        for s in range(seqs):
            found = attend_back(
                scalars[s], queries[s], heads_grad[s], attended[s], lses[s], pieces[s]
            )
            dqs.append(turn(found[0].reshape(GROUPS, rows, -1)))
            held = [piece.reshape(GROUPS, rows, -1) for piece in found[1:]]
            for m in reversed(masks):
                n = len(held) // 2
                held = [add_low(mine, flip(theirs, m)) for mine, theirs in zip(held[:n], held[n:])]
            dkvs.append(turn(held[0]))
        tokens_grad, g_qkv, sums_qkv = project_grads(
            counts,
            tokens,
            first_grads,
            dqs + dkvs,
            query_weight,
            key_weight,
            value_weight,
            first_qkv,
            second_qkv,
        )

    if fused:
        tokens_grad, qkv, total, small = finish(
            lengths,
            block_order,
            tokens,
            firsts,
            rq,
            rkv,
            sums,
            wide_sums,
            ready,
            query_weight,
            key_weight,
            value_weight,
            others,
        )
        query_grad, key_grad, value_grad, out_grad, inner_grad, outer_grad = unpack(
            qkv, total, hidden
        )
        small = small.reshape(-1)
    else:
        valid = jnp.full((128,), sum(jnp.sum(r) for r in row_counts).astype(F32))
        small = jnp.concatenate(
            [sums[:7].reshape(-1), sums_qkv[:2].reshape(-1), wide_sums[0], valid]
        )
        small = lax.psum(small, ("ctx", "wa"))
        qkv = reduced(jnp.moveaxis(g_qkv, (2, 1), (0, 1)).reshape(4, 3, -1, 128))
        out_grad, inner_grad, outer_grad = (
            paired(g).reshape(-1, g.shape[-1]).astype(F32) for g in dense_sums
        )
        qkv = qkv.reshape(6, 3, half, 128).astype(F32)
        query_grad, key_grad, value_grad = (
            qkv[:, i].swapaxes(0, 1).reshape(half, width) for i in range(3)
        )

    def vector(start, length):
        return lax.dynamic_slice_in_dim(small, start + x * (length // 2), length // 2, 0)

    end = 9 * width
    loss = jnp.sum(small[6 * width : 7 * width]) / (small[end + hidden] * width)
    return (
        output,
        tokens_grad,
        query_grad,
        vector(7 * width, width),
        key_grad,
        value_grad,
        vector(8 * width, width),
        out_grad,
        vector(5 * width, width),
        vector(3 * width, width),
        vector(4 * width, width),
        inner_grad,
        vector(end, hidden),
        outer_grad,
        vector(2 * width, width),
        vector(0, width),
        vector(width, width),
        loss,
    )


def solution(mesh):
    row, split, both = P("wa"), P("wa", None), P("wa", "ctx", None)
    placed = (both, both, row, P(), split, row, split, split, row, split, row, row, row)
    placed += (split, row, split, row, row, row)
    return jax.shard_map(
        functools.partial(shards, mesh.shape["ctx"]),
        mesh=mesh,
        in_specs=placed,
        out_specs=(
            both,
            both,
            split,
            row,
            split,
            split,
            row,
            split,
            row,
            row,
            row,
            split,
            row,
            split,
            row,
            row,
            row,
            P(),
        ),
        check_vma=False,
    )
```

```python
import functools
import math

import jax
import jax.numpy as jnp
from jax import lax
from jax.experimental import pallas as pl
from jax.experimental.pallas import tpu as pltpu
from jax.sharding import PartitionSpec as P

DH = 64
BLK = 128
GROUPS = 4
LN2 = math.log(2.0)
NT = (((1,), (1,)), ((), ()))
NN = (((1,), (0,)), ((), ()))
TN = (((0,), (0,)), ((), ()))
F32 = jnp.float32
BF16 = jnp.bfloat16
VMEM = pl.BlockSpec(memory_space=pltpu.VMEM)
SMEM = pl.BlockSpec(memory_space=pltpu.SMEM)
ANY = pl.BlockSpec(memory_space=pl.ANY)
ROOM = pltpu.CompilerParams(vmem_limit_bytes=62 * 2**20)


def dot(left, right, dims=NN):
    return lax.dot_general(left, right, dims, preferred_element_type=F32)


def cost(us):
    return pl.CostEstimate(flops=int(us * 1.15e9), bytes_accessed=1 << 20, transcendentals=0)


def weight_copies(full, own, first, second, sems, base):
    x, c = lax.axis_index("wa"), lax.rem(lax.axis_index("ctx"), 2)
    half = own.shape[0]
    quarter = half // 2
    other = (1 - x) * half
    places = (
        (own, x * half, half),
        (first, other + c * quarter, quarter),
        (second, other + (1 - c) * quarter, quarter),
    )
    return [
        pltpu.make_async_copy(
            src, full.at[pl.ds(pl.multiple_of(start, quarter), size)], sems.at[base + i]
        )
        for i, (src, start, size) in enumerate(places)
    ]


class Counts:
    def __init__(self, lengths, order):
        self.lengths, self.order = lengths, order

    def __getitem__(self, i):
        place = 2 * lax.axis_index("ctx") + i % 2
        return self.lengths[i // 2] - self.order[place] * BLK


def valid_rows(sc, s, rows):
    row = lax.broadcasted_iota(jnp.int32, (rows, 1), 0)
    first = jnp.where(row < sc[2 * s], 1.0, 0.0)
    later = jnp.where(row - BLK < sc[2 * s + 1], 1.0, 0.0)
    return jnp.where(row < BLK, first, later)


def half_copies(full, own, other, sems, base):
    x, half = lax.axis_index("wa"), own.shape[0]
    return [
        pltpu.make_async_copy(
            src, full.at[pl.ds(pl.multiple_of(k * half, half), half)], sems.at[base + i]
        )
        for i, (src, k) in enumerate(((own, x), (other, 1 - x)))
    ]


def project_kernel(sc, tok, vec, wq, wk, wv, first, second, *rest):
    seqs, rows, width = tok.shape
    outs, (full, sems) = rest[: 2 * seqs], rest[2 * seqs :]
    quarter = wq.shape[0] // 2
    copies = []
    for i, own in enumerate((wq, wk, wv)):
        part = pl.ds(i * quarter, quarter)
        copies.append(
            weight_copies(full.at[i], own, first.at[part], second.at[part], sems, 3 * i)
        )
    for group in copies:
        for copy in group:
            copy.start()
    flat = tok[...].reshape(seqs * rows, width)
    per = width // GROUPS
    heads = per // DH
    valid = jnp.concatenate([valid_rows(sc, s, rows) for s in range(seqs)], 0) > 0.0
    for copy in copies[1]:
        copy.wait()
    keys = jnp.where(valid, dot(flat, full[1]), 0.0).astype(BF16)
    for copy in copies[2]:
        copy.wait()
    values = jnp.where(valid, dot(flat, full[2]) + vec[1:2, :], 0.0).astype(BF16)
    for s in range(seqs):
        rs = slice(s * rows, (s + 1) * rows)
        for g in range(GROUPS):
            for h in range(heads):
                cols = slice(g * per + h * DH, g * per + (h + 1) * DH)
                outs[2 * s + 1][g, :, h * 128 : (h + 1) * 128] = jnp.concatenate(
                    [keys[rs, cols], values[rs, cols]], 1
                )
    for copy in copies[0]:
        copy.wait()
    queries = ((dot(flat, full[0]) + vec[0:1, :]) * (DH**-0.5 / LN2)).astype(BF16)
    for s in range(seqs):
        rs = slice(s * rows, (s + 1) * rows)
        for g in range(GROUPS):
            outs[2 * s][g] = queries[rs, g * per : (g + 1) * per]


def project(sc, tok, vec, wq, wk, wv, first, second):
    seqs, rows, width = tok.shape
    per = width // GROUPS
    shapes = [
        jax.ShapeDtypeStruct((GROUPS, rows, n), BF16) for _ in range(seqs) for n in (per, 2 * per)
    ]
    return pl.pallas_call(
        project_kernel,
        out_shape=shapes,
        in_specs=[SMEM, VMEM, VMEM] + [ANY] * 5,
        out_specs=[VMEM] * len(shapes),
        scratch_shapes=[pltpu.VMEM((3, width, width), BF16), pltpu.SemaphoreType.DMA((9,))],
        compiler_params=ROOM,
        cost_estimate=cost(5),
        name="project",
    )(sc, tok, vec, wq, wk, wv, first, second)


def load_pieces(pieces, kv, sems):
    per = pieces[0].shape[0]
    copies = [
        pltpu.make_async_copy(piece, kv.at[pl.ds(i * per, per)], sems.at[i])
        for i, piece in enumerate(pieces)
    ]
    for copy in copies:
        copy.start()
    for copy in copies:
        copy.wait()


def forward_kernel(wide, narrow, count, s, per_plane, lengths, order, q_ref, *rest):
    pieces, rest = rest[:count], rest[count:]
    o_ref, lse_ref, kv_ref, qa, acc, sums, spots, sems = rest
    blocks = q_ref.shape[0]
    heads = q_ref.shape[2] // DH
    rows = blocks * BLK
    length = lengths[s]
    place = lax.rem(lax.axis_index("ctx"), per_plane)

    def put(b, _):
        owner = b // 2
        offset = lax.bitwise_xor(lax.rem(owner, per_plane), place)
        piece = 0
        for bit in range(per_plane.bit_length() - 1):
            piece = 2 * piece + lax.rem(lax.div(offset, 1 << bit), 2)
        spots[order[b]] = (piece * GROUPS + lax.div(owner, per_plane)) * 2 + lax.rem(b, 2)
        return 0

    lax.fori_loop(0, order.shape[0], put, 0)
    load_pieces(pieces, kv_ref, sems)

    def gather(h, start, n):
        return jnp.concatenate(
            [kv_ref[spots[start + i], :, h * 128 : (h + 1) * 128] for i in range(n)], 0
        )

    whole = length // (wide * BLK)
    tail = whole * wide
    tails = (length - tail * BLK + narrow * BLK - 1) // (narrow * BLK)
    for h in range(heads):
        hs = slice(h * DH, (h + 1) * DH)
        own = jnp.concatenate([q_ref[b, :, hs] for b in range(blocks)], 0)
        qa[...] = jnp.concatenate([own, jnp.zeros_like(own)], 1)
        acc[...] = jnp.zeros_like(acc)
        sums[...] = jnp.zeros_like(sums)

        def step(start, n, masked, h=h):
            kv = gather(h, start, n)
            scores = dot(qa[...], kv, NT)
            if masked:
                place = lax.broadcasted_iota(jnp.int32, scores.shape, 1) + start * BLK
                scores = jnp.where(place < length, scores, -1e30)
            p = jnp.exp2(scores)
            sums[...] += sum(p[:, i * 128 : (i + 1) * 128] for i in range(n))
            acc[...] += dot(p.astype(BF16), kv)

        def wide_step(j, _, step=step):
            step(j * wide, wide, False)
            return 0

        def narrow_step(j, _, step=step):
            step(tail + j * narrow, narrow, True)
            return 0

        lax.fori_loop(0, whole, wide_step, 0)
        lax.fori_loop(0, tails, narrow_step, 0)
        total = jnp.sum(sums[...], 1, keepdims=True)
        across = jnp.transpose(jnp.broadcast_to(total, (rows, 128)))[:8]
        good = (jnp.min(across) > 2.0**-80) & (jnp.max(across) < 2.0**100)

        @pl.when(good)
        def _(h=h, hs=hs, total=total, across=across):
            lse_ref[h] = jnp.log2(across)
            o_ref[:, hs] = (acc[:, DH:] * (1.0 / total)).astype(BF16)

        @pl.when(jnp.logical_not(good))
        def _(h=h, hs=hs):
            key_blocks = (length + BLK - 1) // BLK

            def rows_step(t, _):
                part = pl.ds(pl.multiple_of(t * BLK, BLK), BLK)
                q = qa[part, :]

                def scores_of(j):
                    kv = gather(h, j, 1)
                    scores = dot(q, kv, NT)
                    place = lax.broadcasted_iota(jnp.int32, scores.shape, 1) + j * BLK
                    return kv, jnp.where(place < length, scores, -1e30)

                largest = lax.fori_loop(
                    0,
                    key_blocks,
                    lambda j, m: jnp.maximum(m, jnp.max(scores_of(j)[1], 1, keepdims=True)),
                    jnp.full((BLK, 1), -1e30, F32),
                )
                acc[part, :] = jnp.zeros((BLK, 128), F32)
                sums[part, :] = jnp.zeros((BLK, 128), F32)

                def add(j, _):
                    kv, scores = scores_of(j)
                    p = jnp.exp2(scores - largest)
                    sums[part, :] += p
                    acc[part, :] += dot(p.astype(BF16), kv)
                    return 0

                lax.fori_loop(0, key_blocks, add, 0)
                row_total = jnp.sum(sums[part, :], 1, keepdims=True)
                lse = largest + jnp.log2(row_total)
                lse_ref[h, :, part] = jnp.transpose(jnp.broadcast_to(lse, (BLK, 128)))[:8]
                o_ref[part, hs] = (acc[part, :][:, DH:] * (1.0 / row_total)).astype(BF16)
                return 0

            lax.fori_loop(0, rows // BLK, rows_step, 0)


def attend(s, per_plane, lengths, order, q, pieces):
    blocks, _, per = q.shape
    rows, heads = blocks * BLK, per // DH
    key_blocks = len(pieces) * pieces[0].shape[0]
    return pl.pallas_call(
        functools.partial(forward_kernel, 8, 2, len(pieces), s, per_plane),
        out_shape=(
            jax.ShapeDtypeStruct((rows, per), BF16),
            jax.ShapeDtypeStruct((heads, 8, rows), F32),
        ),
        in_specs=[SMEM, SMEM, VMEM] + [ANY] * len(pieces),
        out_specs=(VMEM, VMEM),
        scratch_shapes=[
            pltpu.VMEM((key_blocks, BLK, 2 * per), BF16),
            pltpu.VMEM((rows, 128), BF16),
            pltpu.VMEM((rows, 128), F32),
            pltpu.VMEM((rows, 128), F32),
            pltpu.SMEM((key_blocks,), jnp.int32),
            pltpu.SemaphoreType.DMA((len(pieces),)),
        ],
        compiler_params=ROOM,
        cost_estimate=cost(20),
        name="attend",
    )(lengths, order, q, *pieces)


def backward_kernel(qn, kn, count, sc, q_ref, do_ref, o_ref, lse_ref, *rest):
    pieces, dq_ref, outs = rest[:count], rest[count], rest[count + 1 : 2 * count + 1]
    kv_ref, both, dkv, dq, lse_row, delta_row, sems = rest[2 * count + 1 :]
    blocks = q_ref.shape[0]
    heads = q_ref.shape[2] // DH
    key_blocks = kv_ref.shape[0]
    tile = qn * BLK
    length, used = sc[0], sc[1]
    whole = length // (kn * BLK)
    parts = (length + kn * BLK - 1) // (kn * BLK)
    tiles = (used + qn - 1) // qn
    ones = jnp.ones((8, DH), BF16)
    load_pieces(pieces, kv_ref, sems)
    for h in range(heads):
        hs = slice(h * DH, (h + 1) * DH)

        def clear(i, _):
            dkv[pl.ds(pl.multiple_of(i * 1024, 1024), 1024), :] = jnp.zeros((1024, 128), F32)
            return 0

        lax.fori_loop(0, key_blocks // 8, clear, 0)
        dq[...] = jnp.zeros_like(dq)

        def prepare(t, _, h=h, hs=hs):
            base = pl.multiple_of(t * (2 * tile), 2 * tile)
            start = pl.multiple_of(t * tile, tile)
            places = [sc[8 + t * qn + i] for i in range(qn)]
            q = jnp.concatenate([q_ref[s, :, hs] for s in places], 0)
            do = jnp.concatenate([do_ref[s, :, hs] for s in places], 0)
            o = jnp.concatenate([o_ref[s, :, hs] for s in places], 0)
            zero = jnp.zeros_like(q)
            both[pl.ds(base, tile), :] = jnp.concatenate([q, zero], 1)
            both[pl.ds(base + tile, tile), :] = jnp.concatenate([zero, do], 1)
            product = do.astype(F32) * o.astype(F32)
            high = product.astype(BF16)
            rest_of = (product - high.astype(F32)).astype(BF16)
            delta_row[:, pl.ds(start, tile)] = dot(ones, high, NT) + dot(ones, rest_of, NT)
            lse_row[:, pl.ds(start, tile)] = jnp.concatenate(
                [lse_ref[h, :, pl.ds(pl.multiple_of(s * BLK, BLK), BLK)] for s in places], 1
            )
            return 0

        lax.fori_loop(0, tiles, prepare, 0)

        def rows_step(t, _, h=h):
            base = pl.multiple_of(t * (2 * tile), 2 * tile)
            span = pl.ds(pl.multiple_of(t * tile, tile), tile)

            def step(j, masked):
                places = [sc[8 + blocks + j * kn + i] for i in range(kn)]
                kv = jnp.concatenate([kv_ref[s, :, h * 128 : (h + 1) * 128] for s in places], 0)
                b = both[pl.ds(base, 2 * tile), :]
                found = dot(kv, b, NT)
                p = jnp.exp2(found[:, :tile] - lse_row[:1, span])
                if masked:
                    place = lax.broadcasted_iota(jnp.int32, p.shape, 0) + j * (kn * BLK)
                    p = jnp.where(place < length, p, 0.0)
                ds = (p * (found[:, tile:] - delta_row[:1, span])).astype(BF16)
                grads = dot(jnp.concatenate([ds, p.astype(BF16)], 1), b)
                for i, s in enumerate(places):
                    dkv[pl.ds(pl.multiple_of(s * BLK, BLK), BLK), :] += grads[
                        i * BLK : (i + 1) * BLK
                    ]
                dq[span, :] += dot(ds, kv, TN)

            def whole_step(j, _):
                step(j, False)
                return 0

            lax.fori_loop(0, whole, whole_step, 0)

            @pl.when(parts > whole)
            def _():
                step(whole, True)

            return 0

        lax.fori_loop(0, tiles, rows_step, 0)
        for i in range(blocks):
            dq_ref[sc[8 + i], :, hs] = (
                dq[i * BLK : (i + 1) * BLK, :DH] * DH**-0.5
            ).astype(BF16)
        level = jnp.where(lax.broadcasted_iota(jnp.int32, (1, 128), 1) < DH, LN2, 1.0)
        per_piece = key_blocks // count
        for n, out in enumerate(outs):
            for i in range(per_piece):
                b = n * per_piece + i
                out[i, :, h * 128 : (h + 1) * 128] = (
                    dkv[b * BLK : (b + 1) * BLK, :] * level
                ).astype(BF16)


def attend_back(sc, q, do, o, lse, pieces):
    blocks, _, per = q.shape
    rows = blocks * BLK
    key_blocks = len(pieces) * pieces[0].shape[0]
    return pl.pallas_call(
        functools.partial(backward_kernel, 4, 4, len(pieces)),
        out_shape=[jax.ShapeDtypeStruct(q.shape, BF16)]
        + [jax.ShapeDtypeStruct(p.shape, BF16) for p in pieces],
        in_specs=[SMEM] + [VMEM] * 4 + [ANY] * len(pieces),
        out_specs=[VMEM] * (1 + len(pieces)),
        scratch_shapes=[
            pltpu.VMEM((key_blocks, BLK, 2 * per), BF16),
            pltpu.VMEM((2 * rows, 128), BF16),
            pltpu.VMEM((key_blocks * BLK, 128), F32),
            pltpu.VMEM((rows, 128), F32),
            pltpu.VMEM((8, rows), F32),
            pltpu.VMEM((8, rows), F32),
            pltpu.SemaphoreType.DMA((len(pieces),)),
        ],
        compiler_params=ROOM,
        cost_estimate=cost(45),
        name="attend_back",
    )(sc, q, do, o, lse, *pieces)


def norm(values):
    centered = values - jnp.mean(values, -1, keepdims=True)
    inverse = lax.rsqrt(jnp.mean(centered * centered, -1, keepdims=True) + 1e-6)
    return centered * inverse, inverse


def norm_back(upstream, normed, inverse):
    return inverse * (
        upstream
        - jnp.mean(upstream, -1, keepdims=True)
        - normed * jnp.mean(upstream * normed, -1, keepdims=True)
    )


def normal_parts(x):
    z = jnp.abs(x) * (0.5**0.5)
    bell = jnp.exp(-0.5 * x * x)
    t = 1.0 / (1.0 + 0.3275911 * z)
    poly = t * (
        0.254829592
        + t * (-0.284496736 + t * (1.421413741 + t * (-1.453152027 + t * 1.061405429)))
    )
    upper = 0.5 * poly * bell
    return jnp.where(x >= 0, 1.0 - upper, upper), bell * (2.0 * math.pi) ** -0.5


def dense_kernel(sc, att4, tok, teach, vec, wide_vec, *rest):
    weights, rest = rest[:9], rest[9:]
    outs, (wo, wi, wu, slope, sems) = rest[:11], rest[11:]
    out, fg, ag, att_o, br_o, hl_o, il_o, act_o, ol_o, sums, wide_sums = outs
    rows, width = tok.shape
    hidden = wi.shape[1]
    tile = 512
    copies = [
        weight_copies(full, *weights[3 * i : 3 * i + 3], sems, 3 * i)
        for i, full in enumerate((wo, wi, wu))
    ]
    for group in copies:
        for copy in group:
            copy.start()
    per = att4.shape[2]
    att = jnp.concatenate([att4[g] for g in range(GROUPS)], 1)
    att_o[...] = att
    row = lax.broadcasted_iota(jnp.int32, (rows, 1), 0)
    mask = jnp.where(
        row < BLK, jnp.where(row < sc[0], 1.0, 0.0), jnp.where(row - BLK < sc[1], 1.0, 0.0)
    )
    out_bias, gain_one, shift_one = vec[0:1, :], vec[1:2, :], vec[2:3, :]
    outer_bias, gain_two, shift_two = vec[3:4, :], vec[4:5, :], vec[5:6, :]
    for copy in copies[0]:
        copy.wait()
    first = tok[...].astype(F32) + dot(att, wo[...]) + out_bias
    normed_one, inverse_one = norm(first)
    hidden_in = normed_one * gain_one + shift_one
    hl = hidden_in.astype(BF16)
    hl_o[...] = hl
    for copy in copies[1] + copies[2]:
        copy.wait()
    second = hidden_in + outer_bias
    for n in range(hidden // tile):
        cols = slice(n * tile, (n + 1) * tile)
        inner = dot(hl, wi[:, cols]) + wide_vec[0:1, cols]
        below, density = normal_parts(inner)
        act = (inner * below).astype(BF16)
        act_o[:, cols] = act
        slope[:, cols] = below + inner * density
        second += dot(act, wu[cols, :])
    normed_two, inverse_two = norm(second)
    final = normed_two * gain_two + shift_two
    out[...] = final.astype(BF16)
    residue = (final - teach[...].astype(F32)) * mask
    add = functools.partial(jnp.sum, axis=0, keepdims=True)
    second_grad = norm_back(residue * gain_two, normed_two, inverse_two)
    ol = second_grad.astype(BF16)
    ol_o[...] = ol
    hidden_grad = second_grad
    for n in range(hidden // tile):
        cols = slice(n * tile, (n + 1) * tile)
        il = (dot(ol, wu[cols, :], NT) * slope[:, cols]).astype(BF16)
        il_o[:, cols] = il
        wide_sums[0:1, cols] = add(il.astype(F32))
        hidden_grad += dot(il, wi[:, cols], NT)
    first_grad = norm_back(hidden_grad * gain_one, normed_one, inverse_one)
    fg[...] = first_grad
    br = first_grad.astype(BF16)
    br_o[...] = br
    att_grad = dot(br, wo[...], NT).astype(BF16)
    for g in range(GROUPS):
        ag[g] = att_grad[:, g * per : (g + 1) * per]
    sums[0:1, :] = add(residue * normed_two)
    sums[1:2, :] = add(residue)
    sums[2:3, :] = add(ol.astype(F32))
    sums[3:4, :] = add(hidden_grad * normed_one)
    sums[4:5, :] = add(hidden_grad)
    sums[5:6, :] = add(br.astype(F32))
    sums[6:7, :] = add(residue * residue)
    sums[7:8, :] = jnp.zeros((1, width), F32)


def dense(sc, att4, tok, teach, vec, wide_vec, weights):
    rows, width = tok.shape
    hidden = wide_vec.shape[1]
    narrow = jax.ShapeDtypeStruct((rows, width), BF16)
    wide = jax.ShapeDtypeStruct((rows, hidden), BF16)
    return pl.pallas_call(
        dense_kernel,
        out_shape=[
            narrow,
            jax.ShapeDtypeStruct((rows, width), F32),
            jax.ShapeDtypeStruct(att4.shape, BF16),
            narrow,
            narrow,
            narrow,
            wide,
            wide,
            narrow,
            jax.ShapeDtypeStruct((8, width), F32),
            jax.ShapeDtypeStruct((1, hidden), F32),
        ],
        in_specs=[SMEM] + [VMEM] * 5 + [ANY] * 9,
        out_specs=[VMEM] * 11,
        scratch_shapes=[
            pltpu.VMEM((width, width), BF16),
            pltpu.VMEM((width, hidden), BF16),
            pltpu.VMEM((hidden, width), BF16),
            pltpu.VMEM((rows, hidden), F32),
            pltpu.SemaphoreType.DMA((9,)),
        ],
        compiler_params=ROOM,
        cost_estimate=cost(15),
        name="dense",
    )(sc, att4, tok, teach, vec, wide_vec, *weights)


def dense_grads_kernel(seqs, *refs):
    ins, (g_out, g_inner, g_outer) = refs[: 6 * seqs], refs[6 * seqs :]
    att, br, hl, il, act, ol = (
        jnp.concatenate([ins[6 * s + i][...] for s in range(seqs)], 0) for i in range(6)
    )
    for target, left, right in ((g_out, att, br), (g_inner, hl, il), (g_outer, act, ol)):
        rows = target.shape[1]
        for n in range(4):
            piece = left[:, n * rows : (n + 1) * rows]
            for t in range(right.shape[1] // 768):
                cols = slice(t * 768, (t + 1) * 768)
                target[n, :, cols] = dot(piece, right[:, cols], TN).astype(BF16)


def dense_grads(saved):
    seqs = len(saved)
    width, hidden = saved[0][0].shape[1], saved[0][3].shape[1]
    return pl.pallas_call(
        functools.partial(dense_grads_kernel, seqs),
        out_shape=[
            jax.ShapeDtypeStruct((4, width // 4, width), BF16),
            jax.ShapeDtypeStruct((4, width // 4, hidden), BF16),
            jax.ShapeDtypeStruct((4, hidden // 4, width), BF16),
        ],
        in_specs=[VMEM] * (6 * seqs),
        out_specs=[VMEM] * 3,
        compiler_params=ROOM,
        cost_estimate=cost(10),
        name="dense_grads",
    )(*[member for group in saved for member in group])


def project_grads_kernel(seqs, sc, tok, *refs):
    fgs, refs = refs[:seqs], refs[seqs:]
    grads_in, refs = refs[: 2 * seqs], refs[2 * seqs :]
    wq, wk, wv, first, second, tg, grads, sums, full, sems = refs
    rows, width = tok.shape[1:]
    per = width // GROUPS
    heads = per // DH
    quarter = wq.shape[0] // 2
    copies = []
    for i, own in enumerate((wq, wk, wv)):
        part = pl.ds(i * quarter, quarter)
        copies += weight_copies(full.at[i], own, first.at[part], second.at[part], sems, 3 * i)
    for copy in copies:
        copy.start()

    def head(i, s, g, h):
        if i == 0:
            return grads_in[s][g, :, h * DH : (h + 1) * DH]
        start = h * 128 + (i - 1) * DH
        return grads_in[seqs + s][g, :, start : start + DH]

    def whole(i):
        each = [
            jnp.concatenate([head(i, s, g, h) for g in range(GROUPS) for h in range(heads)], 1)
            for s in range(seqs)
        ]
        return jnp.concatenate(each, 0)

    valid = jnp.concatenate([valid_rows(sc, s, rows) for s in range(seqs)], 0) > 0.0
    dq = whole(0)
    halves = [jnp.where(valid, whole(i), jnp.zeros((), BF16)) for i in (1, 2)]
    flat = tok[...].reshape(seqs * rows, width)
    for copy in copies:
        copy.wait()
    total = jnp.concatenate([fgs[s][...] for s in range(seqs)], 0)
    for i, grad in enumerate((dq, *halves)):
        total += dot(grad, full[i], NT)
        found = dot(flat, grad, TN).astype(BF16)
        half = width // 2
        for n in range(2):
            for t in range(width // 128):
                grads[t % 3, t // 3, n, i * half : (i + 1) * half, :] = found[
                    n * half : (n + 1) * half, t * 128 : (t + 1) * 128
                ]
    tg[...] = total.reshape(seqs, rows, width)
    sums[0:1, :] = jnp.sum(dq.astype(F32), 0, keepdims=True)
    sums[1:2, :] = jnp.sum(halves[1].astype(F32), 0, keepdims=True)
    sums[2:8, :] = jnp.zeros((6, width), F32)


def project_grads(sc, tok, fgs, grads, wq, wk, wv, first, second):
    seqs, rows, width = tok.shape
    return pl.pallas_call(
        functools.partial(project_grads_kernel, seqs),
        out_shape=[
            jax.ShapeDtypeStruct(tok.shape, F32),
            jax.ShapeDtypeStruct((3, 2, 2, 3 * (width // 2), 128), BF16),
            jax.ShapeDtypeStruct((8, width), F32),
        ],
        in_specs=[SMEM] + [VMEM] * (1 + len(fgs) + len(grads)) + [ANY] * 5,
        out_specs=[VMEM] * 3,
        scratch_shapes=[pltpu.VMEM((3, width, width), BF16), pltpu.SemaphoreType.DMA((9,))],
        compiler_params=ROOM,
        cost_estimate=cost(10),
        name="project_grads",
    )(sc, tok, *fgs, *grads, wq, wk, wv, first, second)


MESH = pl.DeviceIdType.MESH


def position():
    ctx = lax.axis_index("ctx")
    return ctx // 4, lax.rem(ctx // 2, 2), lax.rem(ctx, 2), lax.axis_index("wa")


def device(z, y, c, x):
    return z * 4 + y * 2 + c, x


def greet(others):
    barrier = pltpu.get_barrier_semaphore()
    for other in others:
        pl.semaphore_signal(barrier, inc=1, device_id=other, device_id_type=MESH)
    pl.semaphore_wait(barrier, len(others))


def send(src, dst, sems, to):
    copy = pltpu.make_async_remote_copy(
        src_ref=src,
        dst_ref=dst,
        send_sem=sems[0],
        recv_sem=sems[1],
        device_id=to,
        device_id_type=MESH,
    )
    copy.start()
    return copy


def add_low(left, right):
    return (left.astype(F32) + right.astype(F32)).astype(BF16)


def back_kernel(seqs, *refs):
    per_seq = 5
    ins = [refs[per_seq * s : per_seq * (s + 1)] for s in range(seqs)]
    a_own, a_give, b_own, b_give, rq, rkv, dense_out, *refs = refs[per_seq * seqs :]
    q_v, do_v, o_v, lse_v, kv_v, both, dkv, dq, delta, obuf, qbuf = refs[:11]
    from_core, from_y, a_v, b_v, a_in, b_in, a2, b2, a2_in, b2_in = refs[11:21]
    az_in, bz_in, dres, in_sem, c_sem, y_sem, z_sem, q_sem, l_sem, x_sem, dz_sem = refs[21:]
    z, y, c, x = position()
    sibling, beside, over = device(z, y, 1 - c, x), device(z, 1 - y, c, x), device(z, y, c, 1 - x)
    line = [None] + [device(z ^ d, y, c, x) for d in range(1, GROUPS)]
    greet([sibling, beside, over] + line[1:])

    def pair(sems, *index):
        return sems.at[(0, *index)], sems.at[(1, *index)]

    flow = {}
    flow["a"] = send(a_give, a_in, pair(x_sem, 0), over)
    flow["b"] = send(b_give, b_in, pair(x_sem, 1), beside)
    loads = []
    for s in range(seqs):
        targets = [ref.at[s] for ref in (q_v, do_v, o_v, lse_v, kv_v)]
        group = [
            pltpu.make_async_copy(src, dst, in_sem.at[s, i])
            for i, (src, dst) in enumerate(zip(ins[s], targets))
        ]
        for copy in group:
            copy.start()
        loads.append(group)
    own_loads = [
        pltpu.make_async_copy(a_own, a_v, l_sem.at[0]),
        pltpu.make_async_copy(b_own, b_v, l_sem.at[1]),
    ]
    for copy in own_loads:
        copy.start()

    rows = q_v.shape[1]
    heads = q_v.shape[2] // DH
    keys = kv_v.shape[1]
    tile, ktile = rows // 2, 2048
    quarter = keys // 4
    chunk = quarter // GROUPS
    ones = jnp.ones((8, DH), BF16)
    level = jnp.where(lax.broadcasted_iota(jnp.int32, (1, 128), 1) < DH, LN2, 1.0)
    waits = []

    def group_rows(g):
        return pl.ds(pl.multiple_of(g * chunk, chunk), chunk)

    def core_stage(u):
        flow["c", u] = send(
            obuf.at[u, pl.ds(2 * quarter, 2 * quarter)], from_core.at[u], pair(c_sem, u), sibling
        )

    def y_stage(u):
        flow["c", u].wait()
        second = pl.ds(quarter, quarter)
        obuf[u, second] = add_low(obuf[u, second], from_core[u, second])
        flow["y", u] = send(obuf.at[u, second], from_y.at[u], pair(y_sem, u), beside)
        obuf[u, 0:quarter] = add_low(obuf[u, 0:quarter], from_core[u, 0:quarter])

    def z_stage(u):
        flow["y", u].wait()
        obuf[u, 0:quarter] = add_low(obuf[u, 0:quarter], from_y[u])
        for d in range(1, GROUPS):
            src = obuf.at[u, group_rows(z ^ d)]
            waits.append(send(src, rkv.at[u, z], pair(z_sem, u, d), line[d]))
        own = pltpu.make_async_copy(obuf.at[u, group_rows(z)], rkv.at[u, z], z_sem.at[0, u, 0])
        own.start()
        waits.append(own)

    def q_stage(h):
        for d in range(1, GROUPS):
            waits.append(send(qbuf.at[h, z ^ d], rq.at[h, z], pair(q_sem, h, d), line[d]))
        own = pltpu.make_async_copy(qbuf.at[h, z], rq.at[h, z], q_sem.at[0, h, 0])
        own.start()
        waits.append(own)

    a_half, b_half = a2.shape[1], b2.shape[1]

    def dense_second():
        for copy in own_loads:
            copy.wait()
        flow["a"].wait()
        for slot, which in ((0, y), (1, 1 - y)):
            part = pl.ds(pl.multiple_of(which * a_half, 16), a_half)
            a2[slot] = add_low(a_v[part, :], a_in[part, :])
        flow["a"] = send(a2.at[1], a2_in, pair(x_sem, 2), beside)
        flow["b"].wait()
        for slot, which in ((0, x), (1, 1 - x)):
            b2[slot] = add_low(b_v[which], b_in[which])
        flow["b"] = send(b2.at[1], b2_in, pair(x_sem, 3), over)

    low_bit, high_bit = lax.rem(z, 2), z // 2
    parts = (("a", a2, a2_in, az_in), ("b", b2, b2_in, bz_in))

    def rows_at(start, n):
        return pl.ds(pl.multiple_of(start, 16), n)

    def dense_third():
        for i, (name, held, arrived, landing) in enumerate(parts):
            flow[name].wait()
            held[0] = add_low(held[0], arrived[...])
            n = held.shape[1] // 2
            src = held.at[0, rows_at((1 - low_bit) * n, n)]
            flow[name] = send(src, landing.at[0:n], pair(dz_sem, i, 0), line[1])

    def dense_fourth():
        for i, (name, held, _, landing) in enumerate(parts):
            flow[name].wait()
            n = held.shape[1] // 2
            mine = rows_at(low_bit * n, n)
            held[0, mine] = add_low(held[0, mine], landing[0:n])
            src = held.at[0, rows_at(low_bit * n + (1 - high_bit) * (n // 2), n // 2)]
            flow[name] = send(src, landing.at[n : n + n // 2], pair(dz_sem, i, 1), line[2])

    def dense_fifth():
        base = 0
        for name, held, _, landing in parts:
            flow[name].wait()
            n = held.shape[1] // 2
            mine = rows_at(low_bit * n + high_bit * (n // 2), n // 2)
            dres[base : base + n // 2] = add_low(held[0, mine], landing[n : n + n // 2])
            base += n // 2

    units = [(h, s) for h in range(heads) for s in range(seqs)]
    slots = {}
    for u in range(len(units) - 1):
        slots.setdefault(2 * u + 3, []).append(functools.partial(y_stage, u))
        slots.setdefault(2 * u + 5, []).append(functools.partial(z_stage, u))
    slots.setdefault(5, []).append(dense_second)
    slots.setdefault(7, []).append(dense_third)
    slots.setdefault(9, []).append(dense_fourth)
    slots.setdefault(12, []).append(dense_fifth)

    for u, (h, s) in enumerate(units):
        hs = slice(h * DH, (h + 1) * DH)
        lanes = slice(h * 128, (h + 1) * 128)
        if h == 0:
            for copy in loads[s]:
                copy.wait()
        for n in range(2):
            for work in slots.get(2 * u + n, []):
                work()
            part = slice(n * tile, (n + 1) * tile)
            q, do, o = q_v[s, part, hs], do_v[s, part, hs], o_v[s, part, hs]
            zero = jnp.zeros_like(q)
            both[0:tile, :] = jnp.concatenate([q, zero], 1)
            both[tile : 2 * tile, :] = jnp.concatenate([zero, do], 1)
            product = do.astype(F32) * o.astype(F32)
            high = product.astype(BF16)
            remains = (product - high.astype(F32)).astype(BF16)
            delta[...] = dot(ones, high, NT) + dot(ones, remains, NT)
            dq[...] = jnp.zeros_like(dq)

            def step(j, _, u=u, s=s, h=h, n=n, part=part, lanes=lanes):
                span = pl.ds(pl.multiple_of(j * ktile, ktile), ktile)
                kv = kv_v[s, span, lanes]
                b = both[...]
                found = dot(kv, b, NT)
                p = jnp.exp2(jnp.minimum(found[:, :tile] - lse_v[s, h, 0:1, part], 1.0))
                ds = (p * (found[:, tile:] - delta[0:1, :])).astype(BF16)
                grads = dot(jnp.concatenate([ds, p.astype(BF16)], 1), b)
                if n == 0:
                    dkv[span, :] = grads
                else:
                    obuf[u, span, :] = ((dkv[span, :] + grads) * level).astype(BF16)
                dq[...] += dot(ds, kv, TN)
                return 0

            lax.fori_loop(0, keys // ktile, step, 0)
            found = (dq[:, :DH] * DH**-0.5).astype(BF16)
            for i in range(2):
                qbuf[h, 2 * n + i, :, s * DH : (s + 1) * DH] = found[
                    i * (tile // 2) : (i + 1) * (tile // 2)
                ]
        core_stage(u)
        if s == seqs - 1:
            q_stage(h)
    last = len(units) - 1
    for n in sorted(n for n in slots if n >= 2 * len(units)):
        for work in slots[n]:
            work()
    y_stage(last)
    z_stage(last)
    for copy in waits:
        copy.wait()
    done = pltpu.make_async_copy(dres, dense_out, l_sem.at[0])
    done.start()
    done.wait()


def attend_back_all(seqs_in, ready):
    seqs = len(seqs_in)
    q, _, _, lse, held = seqs_in[0]
    rows, per = q.shape
    heads = per // DH
    units = heads * seqs
    keys = held.shape[0]
    chunk = rows // GROUPS
    a, b = ready[0].shape, ready[2].shape
    a_half, b_half, half = a[0] // 2, b[1], a[1]
    dma = pltpu.SemaphoreType.DMA
    return pl.pallas_call(
        functools.partial(back_kernel, seqs),
        out_shape=[
            jax.ShapeDtypeStruct((heads, GROUPS, chunk, 128), BF16),
            jax.ShapeDtypeStruct((units, GROUPS, chunk, 128), BF16),
            jax.ShapeDtypeStruct(((a_half + b_half) // 4, half), BF16),
        ],
        in_specs=[ANY] * (5 * seqs + 4),
        out_specs=[ANY] * 3,
        scratch_shapes=[
            pltpu.VMEM((seqs, rows, per), BF16),
            pltpu.VMEM((seqs, rows, per), BF16),
            pltpu.VMEM((seqs, rows, per), BF16),
            pltpu.VMEM((seqs, *lse.shape), F32),
            pltpu.VMEM((seqs, keys, 2 * per), BF16),
            pltpu.VMEM((rows, 128), BF16),
            pltpu.VMEM((keys, 128), F32),
            pltpu.VMEM((rows // 2, 128), F32),
            pltpu.VMEM((8, rows // 2), F32),
            pltpu.VMEM((units, keys, 128), BF16),
            pltpu.VMEM((heads, GROUPS, chunk, 128), BF16),
            pltpu.VMEM((units, keys // 2, 128), BF16),
            pltpu.VMEM((units, keys // 4, 128), BF16),
            pltpu.VMEM(a, BF16),
            pltpu.VMEM(b, BF16),
            pltpu.VMEM(a, BF16),
            pltpu.VMEM(b, BF16),
            pltpu.VMEM((2, a_half, half), BF16),
            pltpu.VMEM((2, b_half, half), BF16),
            pltpu.VMEM((a_half, half), BF16),
            pltpu.VMEM((b_half, half), BF16),
            pltpu.VMEM((3 * a_half // 4, half), BF16),
            pltpu.VMEM((3 * b_half // 4, half), BF16),
            pltpu.VMEM(((a_half + b_half) // 4, half), BF16),
            dma((seqs, 5)),
            dma((2, units)),
            dma((2, units)),
            dma((2, units, GROUPS)),
            dma((2, heads, GROUPS)),
            dma((2,)),
            dma((2, 4)),
            dma((2, 2, 2)),
        ],
        compiler_params=pltpu.CompilerParams(
            vmem_limit_bytes=63 * 2**20, collective_id=1, has_side_effects=True
        ),
        cost_estimate=cost(120),
        name="attend_back_all",
    )(*[member for group in seqs_in for member in group], *ready)


def vector_of(vec, row, half):
    both = [vec[k, row + 1 : row + 2, :half].astype(F32) for k in range(2)]
    return jnp.concatenate(both, 1)


def start_kernel(seqs, lengths, order, tokens, wq, wk, wv, wo, wi, wu, *refs):
    sc = Counts(lengths, order)
    vectors, refs = refs[:9], refs[9:]
    q_out, kv_out, o_out, lse_out = (refs[i * seqs : (i + 1) * seqs] for i in range(4))
    refs = refs[4 * seqs :]
    back_out, vec_out, others, *dense_out = refs[:6]
    full, q_held, kv_held, vec, own_vec, tok, *refs = refs[6:]
    q_v, kv_v, o_v, lse_v, shade, qa, acc, sums, top, *sems = refs
    v_sem, wx_sem, wy_sem, wc_sem, l_sem, dx_sem, dc_sem, q_sem, z_sem, y_sem, c_sem = sems[:11]
    own_sem, b_sem = sems[11:]
    z, y, c, x = position()
    sibling, beside, over = device(z, y, 1 - c, x), device(z, 1 - y, c, x), device(z, y, c, 1 - x)
    line = [None] + [device(z ^ d, y, c, x) for d in range(1, GROUPS)]
    greet([sibling, beside, over] + line[1:])

    def pair(sem, *index):
        return sem.at[(0, *index)], sem.at[(1, *index)]

    waits = []
    half = wq.shape[0]
    eighth = half // 4

    def rows_of(which, cc, yy):
        start = which * half + (2 * cc + yy) * eighth
        return pl.ds(pl.multiple_of(start, 16), eighth)

    own_rows = pl.ds(pl.multiple_of((2 * c + y) * eighth, 16), eighth)
    tok_in = pltpu.make_async_copy(tokens, tok, l_sem.at[6])
    tok_in.start()
    flow = {}
    turns = (1, 2, 0)
    locals_of = []
    for i in turns:
        own = (wq, wk, wv)[i]
        flow["x", i] = send(
            own.at[own_rows], full.at[i, rows_of(x, c, y)], pair(wx_sem, i), over
        )
    for i in turns:
        own = (wq, wk, wv)[i]
        place = full.at[i, pl.ds(pl.multiple_of(x * half, half), half)]
        copy = pltpu.make_async_copy(own, place, l_sem.at[i])
        copy.start()
        locals_of.append(copy)
    own_vec[...] = jnp.zeros_like(own_vec)
    for i, one in enumerate(vectors):
        row = (i + 1) % len(vectors)
        own_vec[row : row + 1, : one.shape[0]] = one[...].astype(F32)[None].astype(BF16)
    vec[x] = own_vec[...]
    vec_flow = send(own_vec, vec.at[x], pair(v_sem), over)

    def after_x(i):
        flow["x", i].wait()
        got = full.at[i, rows_of(1 - x, c, y)]
        flow["y", i] = send(got, got, pair(wy_sem, i), beside)
        flow["c", i, 0] = send(got, got, pair(wc_sem, i, 0), sibling)

    def after_y(i):
        flow["y", i].wait()
        got = full.at[i, rows_of(1 - x, c, 1 - y)]
        flow["c", i, 1] = send(got, got, pair(wc_sem, i, 1), sibling)

    def after_core(i):
        flow["c", i, 0].wait()
        flow["c", i, 1].wait()

    rows, width = tok.shape[1:]
    per = width // GROUPS
    heads = per // DH
    tok_in.wait()
    flat = tok[...].reshape(seqs * rows, width)
    valid = jnp.concatenate([valid_rows(sc, s, rows) for s in range(seqs)], 0) > 0.0
    lane = lax.broadcasted_iota(jnp.int32, (8, BLK), 1)
    for piece, offset in enumerate((0, 2, 1, 3)):
        owner = lax.bitwise_xor(2 * y + c, offset)
        for g in range(GROUPS):
            for k in range(2):
                start_of = order[(4 * g + owner) * 2 + k] * BLK
                for s in range(seqs):
                    inside = lane + start_of < lengths[s]
                    cols = slice((2 * g + k) * BLK, (2 * g + k + 1) * BLK)
                    shade[s, piece, :, cols] = jnp.where(inside, 0.0, -1e30)
    after_x(1)
    after_x(2)
    after_y(1)
    after_x(0)
    dense_weights = (wo, wi, wu)
    for i, weight in enumerate(dense_weights):
        n = weight.shape[0] // 2
        part = pl.ds(pl.multiple_of(c * n, 16), n)
        flow["dx", i] = send(weight.at[part], dense_out[i].at[part], pair(dx_sem, i), over)
    after_y(2)
    vec_flow.wait()

    def bias(row):
        return vector_of(vec, row, half)

    for copy in locals_of:
        copy.wait()
    after_core(1)
    keys = jnp.where(valid, dot(flat, full[1]), 0.0).astype(BF16)
    after_y(0)
    after_core(2)
    values = jnp.where(valid, dot(flat, full[2]) + bias(1), 0.0).astype(BF16)
    for s in range(seqs):
        rs = slice(s * rows, (s + 1) * rows)
        for g in range(GROUPS):
            for h in range(heads):
                cols = slice(g * per + h * DH, g * per + (h + 1) * DH)
                kv_held[s, g, :, h * 128 : (h + 1) * 128] = jnp.concatenate(
                    [keys[rs, cols], values[rs, cols]], 1
                )

    def kv_sends(s):
        for d in range(1, GROUPS):
            flow["z", s, d] = send(
                kv_held.at[s, z ^ d], kv_v.at[s, 0, z], pair(z_sem, s, d), line[d]
            )

    def q_sends(s):
        for d in range(1, GROUPS):
            flow["q", s, d] = send(q_held.at[s, z ^ d], q_v.at[s, z], pair(q_sem, s, d), line[d])

    kv_sends(0)

    def pass_on(s, d, src):
        g = z ^ d
        flow["ky", s, d] = send(src, kv_v.at[s, 1, g], pair(y_sem, s, d), beside)
        flow["kc", s, d, 0] = send(src, kv_v.at[s, 2, g], pair(c_sem, s, d, 0), sibling)

    def pass_core(s, d):
        flow["ky", s, d].wait()
        got = kv_v.at[s, 1, z ^ d]
        flow["kc", s, d, 1] = send(got, kv_v.at[s, 3, z ^ d], pair(c_sem, s, d, 1), sibling)

    pass_on(0, 0, kv_held.at[0, z])
    after_core(0)
    queries = ((dot(flat, full[0]) + bias(0)) * (DH**-0.5 / LN2)).astype(BF16)
    for s in range(seqs):
        rs = slice(s * rows, (s + 1) * rows)
        for g in range(GROUPS):
            q_held[s, g] = queries[rs, g * per : (g + 1) * per]
    for i in range(3):
        place = full.at[i, pl.ds(pl.multiple_of((1 - x) * half, half), half)]
        copy = pltpu.make_async_copy(place, others.at[i], l_sem.at[3 + i])
        copy.start()
        waits.append(copy)
    copy = pltpu.make_async_copy(vec, vec_out, l_sem.at[7])
    copy.start()
    waits.append(copy)
    q_sends(0)
    for s in range(seqs):
        kv_v[s, 0, z] = kv_held[s, z]
        q_v[s, z] = q_held[s, z]

    def arrive(s, d):
        flow["z", s, d].wait()
        pass_on(s, d, kv_v.at[s, 0, z ^ d])

    def own_and_core(s):
        for d in range(GROUPS):
            flow["kc", s, d, 0].wait()

    def dense_core(i):
        flow["dx", i].wait()
        n = dense_weights[i].shape[0] // 2
        got = dense_out[i].at[pl.ds(pl.multiple_of(c * n, 16), n)]
        waits.append(send(got, got, pair(dc_sem, i), sibling))

    def leave(src, dst, i):
        copy = pltpu.make_async_copy(src, dst, b_sem.at[i])
        copy.start()
        waits.append(copy)

    def attend_part(s, h, pieces):
        lanes = slice(h * 128, (h + 1) * 128)
        count, tile = GROUPS * rows, 256

        def step(j, _):
            piece = pieces[0] + j * (pieces[1] - pieces[0])
            kv = kv_v[s, piece, :, :, lanes].reshape(count, 128)
            dark = shade[s, piece, 0:1, :]
            for n in range(count // tile):
                part = slice(n * tile, (n + 1) * tile)
                scores = dot(qa[part, :], kv, NT) + dark
                high = scores[:, :128]
                for i in range(1, count // 128):
                    high = jnp.maximum(high, scores[:, i * 128 : (i + 1) * 128])
                old = top[part, :]
                new = jnp.maximum(old, jnp.max(high, 1, keepdims=True))
                fade = jnp.exp2(old - new)
                each = [
                    jnp.exp2(scores[:, i * 128 : (i + 1) * 128] - new) for i in range(count // 128)
                ]
                sums[part, :] = sums[part, :] * fade + sum(each)
                p = jnp.concatenate([one.astype(BF16) for one in each], 1)
                acc[part, :] = acc[part, :] * fade + dot(p, kv)
                top[part, :] = new
            return 0

        lax.fori_loop(0, 2, step, 0)

    def attend_begin(s, h):
        hs = slice(h * DH, (h + 1) * DH)
        mine = q_v[s, :, :, hs].reshape(GROUPS * rows, DH)
        qa[...] = jnp.concatenate([mine, jnp.zeros_like(mine)], 1)
        acc[...] = jnp.zeros_like(acc)
        sums[...] = jnp.zeros_like(sums)
        top[...] = jnp.full_like(top, -1e30)

    def attend_end(s, h):
        hs = slice(h * DH, (h + 1) * DH)
        total = jnp.sum(sums[...], 1, keepdims=True)
        logs = top[...] + jnp.log2(jnp.broadcast_to(total, top.shape))
        lse_v[s, h] = jnp.transpose(logs)[:8]
        found = (acc[:, DH:] * (1.0 / total)).astype(BF16)
        o_v[s, :, :, hs] = found.reshape(GROUPS, rows, DH)

    for d in range(1, GROUPS):
        arrive(0, d)
        if d > 1:
            pass_core(0, d - 2)
    kv_sends(1)
    pass_on(1, 0, kv_held.at[1, z])
    pass_core(0, 2)
    pass_core(0, 3)
    for d in range(1, GROUPS):
        flow["q", 0, d].wait()
    q_sends(1)
    own_and_core(0)
    slots = {
        2: (lambda: pass_core(1, 0), lambda: arrive(1, 1)),
        3: (lambda: arrive(1, 2), lambda: arrive(1, 3)),
        4: (lambda: pass_core(1, 1), lambda: dense_core(0)),
        5: (lambda: pass_core(1, 2),),
        6: (lambda: own_and_core(1), lambda: [flow["q", 1, d].wait() for d in range(1, GROUPS)]),
        7: (lambda: pass_core(1, 3),),
        8: (lambda: dense_core(1),),
        10: (lambda: dense_core(2),),
    }
    for s in range(seqs):
        for h in range(heads):
            for n, pieces in enumerate(((0, 2), (1, 3))):
                for work in slots.get(6 * s + 2 * h + n, ()):
                    work()
                if n == 0:
                    attend_begin(s, h)
                if h == 0 and n == 1:
                    for d in range(GROUPS):
                        flow["kc", s, d, 1].wait()
                attend_part(s, h, pieces)
            attend_end(s, h)
        if s == 0:
            for d in range(1, GROUPS):
                waits.append(
                    send(o_v.at[0, z ^ d], back_out.at[z], pair(own_sem, d), line[d])
                )
            leave(o_v.at[0, z], back_out.at[z], 4 * seqs)
        for i, (src, dst) in enumerate(
            ((q_v, q_out), (kv_v, kv_out), (o_v, o_out), (lse_v, lse_out))
        ):
            leave(src.at[s], dst[s], 4 * s + i)
    for copy in waits:
        copy.wait()


def start(lengths, order, tok, weights, vectors):
    seqs, rows, width = tok.shape
    per = width // GROUPS
    half = weights[0].shape[0]
    joined = (16, vectors[-1].shape[0])
    heads, total = per // DH, GROUPS * rows
    narrow = jax.ShapeDtypeStruct((GROUPS, rows, per), BF16)
    dma = pltpu.SemaphoreType.DMA
    return pl.pallas_call(
        functools.partial(start_kernel, seqs),
        out_shape=[narrow] * seqs
        + [jax.ShapeDtypeStruct((4, GROUPS, rows, 2 * per), BF16)] * seqs
        + [narrow] * seqs
        + [jax.ShapeDtypeStruct((heads, 8, total), F32)] * seqs
        + [
            narrow,
            jax.ShapeDtypeStruct((2, *joined), BF16),
            jax.ShapeDtypeStruct((3, half, width), BF16),
        ]
        + [jax.ShapeDtypeStruct(w.shape, BF16) for w in weights[3:]],
        in_specs=[SMEM] * 2 + [ANY] * 7 + [VMEM] * 9,
        out_specs=[ANY] * (4 * seqs + 6),
        scratch_shapes=[
            pltpu.VMEM((3, width, width), BF16),
            pltpu.VMEM((seqs, GROUPS, rows, per), BF16),
            pltpu.VMEM((seqs, GROUPS, rows, 2 * per), BF16),
            pltpu.VMEM((2, *joined), BF16),
            pltpu.VMEM(joined, BF16),
            pltpu.VMEM(tok.shape, BF16),
            pltpu.VMEM((seqs, GROUPS, rows, per), BF16),
            pltpu.VMEM((seqs, 4, GROUPS, rows, 2 * per), BF16),
            pltpu.VMEM((seqs, GROUPS, rows, per), BF16),
            pltpu.VMEM((seqs, heads, 8, total), F32),
            pltpu.VMEM((seqs, 4, 8, total), F32),
            pltpu.VMEM((total, 128), BF16),
            pltpu.VMEM((total, 128), F32),
            pltpu.VMEM((total, 128), F32),
            pltpu.VMEM((total, 128), F32),
            dma((2,)),
            dma((2, 3)),
            dma((2, 3)),
            dma((2, 3, 2)),
            dma((8,)),
            dma((2, 3)),
            dma((2, 3)),
            dma((2, seqs, GROUPS)),
            dma((2, seqs, GROUPS)),
            dma((2, seqs, GROUPS)),
            dma((2, seqs, GROUPS, 2)),
            dma((2, GROUPS)),
            dma((4 * seqs + 1,)),
        ],
        compiler_params=pltpu.CompilerParams(
            vmem_limit_bytes=63 * 2**20, collective_id=4, has_side_effects=True
        ),
        cost_estimate=cost(80),
        name="start",
    )(lengths, order, tok, *weights, *vectors)


def middle_stage(s, att, mask, tok, teach, vec, weights, keep, outs, first_done, outer_done):
    wo, wi, wu, slope = weights
    att_k, br_k, hl_k, il_k, act_k, ol_k = keep
    out, fg, sums, wide_sums = outs
    rows = att.shape[0]
    hidden = wi.shape[1]
    tile = 512
    rs = slice(s * rows, (s + 1) * rows)
    half = tok.shape[2] // 2
    out_bias, gain_one, shift_one, outer_bias, gain_two, shift_two = (
        vector_of(vec, row, half) for row in range(2, 8)
    )
    add = functools.partial(jnp.sum, axis=0, keepdims=True)

    def collect(target, value):
        if s == 0:
            target[...] = value
        else:
            target[...] += value

    att_k[rs, :] = att
    first_done[0]()
    first = tok[s].astype(F32) + dot(att, wo[...]) + out_bias
    normed_one, inverse_one = norm(first)
    hidden_in = normed_one * gain_one + shift_one
    hl = hidden_in.astype(BF16)
    hl_k[rs, :] = hl
    first_done[1]()
    second = hidden_in + outer_bias
    for n in range(hidden // tile):
        cols = slice(n * tile, (n + 1) * tile)
        k, begin = divmod(n * tile, hidden // 2)
        inner = dot(hl, wi[:, cols]) + vec[k, 0:1, begin : begin + tile].astype(F32)
        below, density = normal_parts(inner)
        act = (inner * below).astype(BF16)
        act_k[rs, cols] = act
        slope[:, cols] = below + inner * density
        second += dot(act, wu[cols, :])
    normed_two, inverse_two = norm(second)
    final = normed_two * gain_two + shift_two
    out[s] = final.astype(BF16)
    residue = (final - teach[s].astype(F32)) * mask
    collect(sums.at[0:1], add(residue * normed_two))
    collect(sums.at[1:2], add(residue))
    collect(sums.at[6:7], add(residue * residue))
    second_grad = norm_back(residue * gain_two, normed_two, inverse_two)
    ol = second_grad.astype(BF16)
    ol_k[rs, :] = ol
    collect(sums.at[2:3], add(ol.astype(F32)))
    outer_done()
    hidden_grad = second_grad
    for n in range(hidden // tile):
        cols = slice(n * tile, (n + 1) * tile)
        il = (dot(ol, wu[cols, :], NT) * slope[:, cols]).astype(BF16)
        il_k[rs, cols] = il
        collect(wide_sums.at[0:1, cols], add(il.astype(F32)))
        hidden_grad += dot(il, wi[:, cols], NT)
    first_grad = norm_back(hidden_grad * gain_one, normed_one, inverse_one)
    fg[s] = first_grad
    br = first_grad.astype(BF16)
    br_k[rs, :] = br
    collect(sums.at[3:4], add(hidden_grad * normed_one))
    collect(sums.at[4:5], add(hidden_grad))
    collect(sums.at[5:6], add(br.astype(F32)))
    return dot(br, wo[...], NT).astype(BF16)


def middle_kernel(seqs, lengths, order, tok, teach, vec, *refs):
    sc = Counts(lengths, order)
    attended, weights, refs = refs[:seqs], refs[seqs : seqs + 6], refs[seqs + 6 :]
    out, fg, sums, wide_sums, a_own, a_give, b_own, b_give = refs[:8]
    grads_in, refs = refs[8 : 8 + seqs], refs[8 + seqs :]
    wo, wi, wu, slope, o_in, g_out, att_k, br_k, hl_k, il_k, act_k, ol_k = refs[:12]
    own, given, w_sem, o_sem, g_sem, c_sem = refs[12:]
    z, y, c, x = position()
    sibling = device(z, y, 1 - c, x)
    line = [None] + [device(z ^ d, y, c, x) for d in range(1, GROUPS)]
    greet([sibling] + line[1:])
    coming, going = {}, {}
    for s in range(seqs):
        if s == 0:
            coming[s, 0] = pltpu.make_async_copy(attended[s], o_in.at[s], o_sem.at[0, s, 0])
            coming[s, 0].start()
            continue
        for d in range(1, GROUPS):
            sems = o_sem.at[0, s, d], o_sem.at[1, s, d]
            coming[s, d] = send(attended[s].at[z ^ d], o_in.at[s, z], sems, line[d])
        coming[s, 0] = pltpu.make_async_copy(attended[s].at[z], o_in.at[s, z], o_sem.at[0, s, 0])
        coming[s, 0].start()
    copies = [
        half_copies(full, *weights[2 * i : 2 * i + 2], w_sem, 2 * i)
        for i, full in enumerate((wo, wi, wu))
    ]
    for group in copies:
        for copy in group:
            copy.start()

    def loaded(which):
        for i in which:
            for copy in copies[i]:
                copy.wait()

    half = wo.shape[0] // 2
    blocks = wi.shape[1] // (2 * half)
    base = (1 + blocks) * half
    core = []

    def store(k, start, value):
        low_value = value.astype(BF16)
        own[0, k, start : start + half, :] = low_value[:, :half]
        own[1, k, start : start + half, :] = low_value[:, half:]

    def pass_core(k, start, stop):
        place = pl.ds(start, stop - start)
        i = len(core)
        sems = c_sem.at[0, i], c_sem.at[1, i]
        core.append(send(own.at[1 - c, k, place], given.at[k, place], sems, sibling))

    def outer_grads():
        for k in range(2):
            for t in range(blocks):
                rows_of = slice((k * blocks + t) * half, (k * blocks + t + 1) * half)
                store(k, base + t * half, dot(act_k[:, rows_of], ol_k[...], TN))
            pass_core(k, base, base + blocks * half)

    rows = tok.shape[1]
    per = o_in.shape[3]
    for s in range(seqs):
        for d in range(GROUPS if s > 0 else 1):
            coming[s, d].wait()
        att = jnp.concatenate([o_in[s, g] for g in range(GROUPS)], 1)
        mask = valid_rows(sc, s, rows)
        waits = (lambda: loaded([0]), lambda: loaded([1, 2])) if s == 0 else (lambda: None,) * 2
        found = middle_stage(
            s,
            att,
            mask,
            tok,
            teach,
            vec,
            (wo, wi, wu, slope),
            (att_k, br_k, hl_k, il_k, act_k, ol_k),
            (out, fg, sums, wide_sums),
            waits,
            outer_grads if s == seqs - 1 else lambda: None,
        )
        for g in range(GROUPS):
            g_out[s, g] = found[:, g * per : (g + 1) * per]
        for d in range(1, GROUPS):
            sems = g_sem.at[0, s, d], g_sem.at[1, s, d]
            going[s, d] = send(g_out.at[s, z ^ d], grads_in[s].at[z], sems, line[d])
        going[s, 0] = pltpu.make_async_copy(g_out.at[s, z], grads_in[s].at[z], g_sem.at[0, s, 0])
        going[s, 0].start()
    sums[7:8, :] = jnp.zeros((1, sums.shape[1]), F32)

    for k in range(2):
        ks = slice(k * half, (k + 1) * half)
        store(k, 0, dot(att_k[:, ks], br_k[...], TN))
        for t in range(blocks):
            cols = slice(2 * t * half, 2 * (t + 1) * half)
            store(k, (1 + t) * half, dot(hl_k[:, ks], il_k[:, cols], TN))
        pass_core(k, 0, base)
    for copy in core:
        copy.wait()
    mine = own.at[c]
    cut, b_half = a_own.shape[0], b_own.shape[1]
    a_own[...] = add_low(mine[x, 0:cut], given[x, 0:cut])
    a_give[...] = add_low(mine[1 - x, 0:cut], given[1 - x, 0:cut])
    for k in range(2):
        for target, which in ((b_own, y), (b_give, 1 - y)):
            part = pl.ds(pl.multiple_of(cut + which * b_half, 16), b_half)
            target[k] = add_low(mine[k, part], given[k, part])
    for copy in going.values():
        copy.wait()


def cut_of(total):
    return total // 256 * 128


def middle(lengths, order, tok, teach, vec, attended, weights):
    seqs, rows, width = tok.shape
    hidden = 2 * vec.shape[2]
    half = width // 2
    total = half + hidden
    cut = cut_of(total)
    dma = pltpu.SemaphoreType.DMA
    narrow, wide = (seqs * rows, width), (seqs * rows, hidden)
    b_shape = jax.ShapeDtypeStruct((2, (total - cut) // 2, half), BF16)
    a_shape = jax.ShapeDtypeStruct((cut, half), BF16)
    groups, _, per = attended[0].shape
    return pl.pallas_call(
        functools.partial(middle_kernel, seqs),
        out_shape=[
            jax.ShapeDtypeStruct(tok.shape, BF16),
            jax.ShapeDtypeStruct(tok.shape, F32),
            jax.ShapeDtypeStruct((8, width), F32),
            jax.ShapeDtypeStruct((1, hidden), F32),
            a_shape,
            a_shape,
            b_shape,
            b_shape,
        ]
        + [jax.ShapeDtypeStruct(a.shape, BF16) for a in attended],
        in_specs=[SMEM] * 2 + [VMEM] * 3 + [ANY] * (seqs + 6),
        out_specs=[VMEM] * 8 + [ANY] * seqs,
        scratch_shapes=[
            pltpu.VMEM((width, width), BF16),
            pltpu.VMEM((width, hidden), BF16),
            pltpu.VMEM((hidden, width), BF16),
            pltpu.VMEM((rows, hidden), F32),
            pltpu.VMEM((seqs, groups, rows, per), BF16),
            pltpu.VMEM((seqs, groups, rows, per), BF16),
            pltpu.VMEM(narrow, BF16),
            pltpu.VMEM(narrow, BF16),
            pltpu.VMEM(narrow, BF16),
            pltpu.VMEM(wide, BF16),
            pltpu.VMEM(wide, BF16),
            pltpu.VMEM(narrow, BF16),
            pltpu.VMEM((2, 2, total, half), BF16),
            pltpu.VMEM((2, total, half), BF16),
            dma((6,)),
            dma((2, seqs, groups)),
            dma((2, seqs, groups)),
            dma((2, 4)),
        ],
        compiler_params=pltpu.CompilerParams(
            vmem_limit_bytes=63 * 2**20, collective_id=3, has_side_effects=True
        ),
        cost_estimate=cost(60),
        name="middle",
    )(lengths, order, tok, teach, vec, *attended, *weights)


def finish_kernel(
    seqs, lengths, order, tok, fg, rq, rkv, dense_sums, wide_sums, ready, wq, wk, wv, others, *rest
):
    sc = Counts(lengths, order)
    tg, out, dense_out, small_out, *rest = rest
    full, grads, acc, from_core, from_x, from_y, from_z, res, vec, vec_in, dense_res = rest[:11]
    w_sems, sems, small_sems, d_sems, last_sem = rest[11:]
    z, y, c, x = position()
    sibling, beside, over = device(z, y, 1 - c, x), device(z, 1 - y, c, x), device(z, y, c, 1 - x)
    line = [None] + [device(z ^ d, y, c, x) for d in range(1, GROUPS)]
    greet([sibling, beside, over] + line[1:])

    a_half = cut_of(dense_res.shape[1]) // 2
    b_half = dense_res.shape[1] // 2 - a_half
    low_bit, high_bit = lax.rem(z, 2), z // 2
    dense_parts = ((0, a_half, y * a_half), (a_half // 4, b_half, 2 * a_half + y * b_half))

    def dense_rows(start, n):
        return dense_res.at[c, pl.ds(pl.multiple_of(start, 16), n)]

    def d_pair(k, i):
        return d_sems.at[0, k, i], d_sems.at[1, k, i]

    dense_flows = []
    for i, (start, n, base) in enumerate(dense_parts):
        place = dense_rows(base + low_bit * (n // 2) + high_bit * (n // 4), n // 4)
        src = ready.at[start : start + n // 4]
        place[...] = src[...]
        dense_flows.append(send(src, place, d_pair(0, i), line[2]))

    def dense_near():
        for i, (_, n, base) in enumerate(dense_parts):
            dense_flows[i].wait()
            place = dense_rows(base + low_bit * (n // 2), n // 2)
            dense_flows[i] = send(place, place, d_pair(1, i), line[1])

    def dense_y():
        for i, (_, n, base) in enumerate(dense_parts):
            dense_flows[i].wait()
            place = dense_rows(base, n)
            dense_flows[i] = send(place, place, d_pair(2, i), beside)

    def dense_core():
        for i, (_, n, _) in enumerate(dense_parts):
            dense_flows[i].wait()
            place = dense_res.at[c, pl.ds(2 * a_half * i, 2 * n)]
            dense_flows[i] = send(place, place, d_pair(3, i), sibling)

    rows, width = tok.shape[1:]
    heads = width // GROUPS // DH
    copies = []
    for i, own in enumerate((wq, wk, wv)):
        copies += half_copies(full.at[i], own, others.at[i], w_sems, 2 * i)
    for copy in copies:
        copy.start()

    def head(i, s, g, h):
        if i == 0:
            return rq[h, g, :, s * DH : (s + 1) * DH]
        return rkv[h * seqs + s, g, :, (i - 1) * DH : i * DH]

    def whole(i):
        each = [
            jnp.concatenate([head(i, s, g, h) for g in range(GROUPS) for h in range(heads)], 1)
            for s in range(seqs)
        ]
        return jnp.concatenate(each, 0)

    valid = jnp.concatenate([valid_rows(sc, s, rows) for s in range(seqs)], 0) > 0.0
    parted = [whole(0)] + [jnp.where(valid, whole(i), jnp.zeros((), BF16)) for i in (1, 2)]
    flat = tok[...].reshape(seqs * rows, width)
    wide = width // 2
    for i, grad in enumerate(parted):
        found = dot(flat, grad, TN).astype(BF16)
        for n in range(2):
            for t in range(width // 128):
                grads[t % 3, t // 3, n, i * wide : (i + 1) * wide, :] = found[
                    n * wide : (n + 1) * wide, t * 128 : (t + 1) * 128
                ]
    lines_of = [dense_sums[i : i + 1, :] for i in range(7)]
    lines_of += [jnp.sum(grad.astype(F32), 0, keepdims=True) for grad in (parted[0], parted[2])]
    lines_of.append(wide_sums[...])
    row = 0
    for one in lines_of:
        for t in range(one.shape[1] // 128):
            vec[row : row + 1, :] = one[:, t * 128 : (t + 1) * 128]
            row += 1
    valid_count = sum(jnp.clip(sc[i], 0, BLK) for i in range(2 * seqs))
    vec[row:, :] = jnp.full((vec.shape[0] - row, 128), valid_count.astype(F32))

    parts, rows_each = grads.shape[0], grads.shape[3]
    half, piece = rows_each // 2, rows_each // 8
    own_half = pl.ds(pl.multiple_of(y * half, half), half)
    other_half = pl.ds(pl.multiple_of((1 - y) * half, half), half)

    def piece_of(g):
        return pl.ds(pl.multiple_of(y * half + g * piece, piece), piece)

    def pair(k, p):
        return sems.at[0, k, p], sems.at[1, k, p]

    def small_pair(k):
        return small_sems.at[0, k], small_sems.at[1, k]

    core = [
        send(grads.at[p, 1 - c], from_core.at[p], pair(0, p), sibling) for p in range(parts)
    ]
    short = send(vec, vec_in.at[0], small_pair(0), sibling)
    flows = []
    for p in range(parts):
        core[p].wait()
        acc[p] = add_low(grads[p, c], from_core[p])
        if p == 1:
            flows.append(send(acc.at[p, :, other_half], from_y.at[p], pair(1, p), beside))
        else:
            flows.append(send(acc.at[p, 1 - x], from_x.at[p], pair(1, p), over))
    dense_near()
    for copy in copies:
        copy.wait()
    total = jnp.concatenate([fg[s] for s in range(seqs)], 0)
    for i, grad in enumerate(parted):
        total += dot(grad, full[i], NT)
    tg[...] = total.reshape(seqs, rows, width)
    short.wait()
    vec_in[8] = vec[...] + vec_in[0]
    short = send(vec_in.at[8], vec_in.at[1], small_pair(1), over)
    for p in (1, 0, 2):
        flows[p].wait()
        if p == 1:
            for k in range(2):
                acc[p, k, own_half] = add_low(acc[p, k, own_half], from_y[p, k])
            flows[p] = send(acc.at[p, 1 - x, own_half], from_x.at[p, own_half], pair(2, p), over)
        else:
            acc[p, x] = add_low(acc[p, x], from_x[p])
            flows[p] = send(acc.at[p, x, other_half], from_y.at[p, 0], pair(2, p), beside)
    short.wait()
    vec[...] = vec_in[8] + vec_in[1]
    short = send(vec, vec_in.at[2], small_pair(2), beside)
    dense_y()
    lines = {}
    for p in (1, 0, 2):
        flows[p].wait()
        if p == 1:
            acc[p, x, own_half] = add_low(acc[p, x, own_half], from_x[p, own_half])
        else:
            acc[p, x, own_half] = add_low(acc[p, x, own_half], from_y[p, 0])
        for d in range(1, GROUPS):
            lines[p, d] = send(
                acc.at[p, x, piece_of(z ^ d)], from_z.at[p, d], pair(2 + d, p), line[d]
            )
    short.wait()
    vec[...] = vec[...] + vec_in[2]
    vec_in[4 + z] = vec[...]
    shorts = [
        send(vec, vec_in.at[4 + z], small_pair(2 + d), line[d]) for d in range(1, GROUPS)
    ]
    spread = {}
    for p in (1, 0, 2):
        total = acc[p, x, piece_of(z)].astype(F32)
        for d in range(1, GROUPS):
            lines[p, d].wait()
            total += from_z[p, d].astype(F32)
        res[c, p, piece_of(z)] = total.astype(BF16)
        for d in range(1, GROUPS):
            spread[p, d] = send(
                res.at[c, p, piece_of(z)],
                res.at[c, p, piece_of(z)],
                pair(5 + d, p),
                line[d],
            )
    for p in (1, 0, 2):
        for d in range(1, GROUPS):
            spread[p, d].wait()
        flows[p] = send(
            res.at[c, p, own_half], res.at[c, p, own_half], pair(9, p), beside
        )
    dense_core()
    for copy in shorts:
        copy.wait()
    small_out[...] = vec_in[4] + vec_in[5] + (vec_in[6] + vec_in[7])
    for p in (1, 0, 2):
        flows[p].wait()
        flows[p] = send(res.at[c, p], res.at[c, p], pair(10, p), sibling)
    for copy in dense_flows:
        copy.wait()
    done = [pltpu.make_async_copy(dense_res, dense_out, last_sem.at[1])]
    done[0].start()
    for p in (1, 0, 2):
        flows[p].wait()
    done.append(pltpu.make_async_copy(res, out, last_sem.at[0]))
    done[1].start()
    for copy in done:
        copy.wait()


def finish(lengths, order, tok, fg, rq, rkv, sums, wide_sums, ready, wq, wk, wv, others):
    seqs, _, width = tok.shape
    short = (-(-(9 * width + wide_sums.shape[1] + 128) // 1024) * 8, 128)
    parts, rows, lanes = 3, 3 * (width // 2), 128
    total, half = 8 * ready.shape[0], ready.shape[1]
    dma = pltpu.SemaphoreType.DMA
    return pl.pallas_call(
        functools.partial(finish_kernel, seqs),
        out_shape=[
            jax.ShapeDtypeStruct(tok.shape, F32),
            jax.ShapeDtypeStruct((2, parts, rows, lanes), BF16),
            jax.ShapeDtypeStruct((2, total, half), BF16),
            jax.ShapeDtypeStruct(short, F32),
        ],
        in_specs=[SMEM] * 2 + [VMEM] * 7 + [ANY] * 4,
        out_specs=[VMEM, ANY, ANY, VMEM],
        scratch_shapes=[
            pltpu.VMEM((3, width, width), BF16),
            pltpu.VMEM((parts, 2, 2, rows, lanes), BF16),
            pltpu.VMEM((parts, 2, rows, lanes), BF16),
            pltpu.VMEM((parts, 2, rows, lanes), BF16),
            pltpu.VMEM((parts, rows, lanes), BF16),
            pltpu.VMEM((parts, 2, rows // 2, lanes), BF16),
            pltpu.VMEM((parts, GROUPS, rows // 8, lanes), BF16),
            pltpu.VMEM((2, parts, rows, lanes), BF16),
            pltpu.VMEM(short, F32),
            pltpu.VMEM((9, *short), F32),
            pltpu.VMEM((2, total, half), BF16),
            dma((6,)),
            dma((2, 11, parts)),
            dma((2, 6)),
            dma((2, 4, 2)),
            dma((2,)),
        ],
        compiler_params=pltpu.CompilerParams(
            vmem_limit_bytes=63 * 2**20, collective_id=2, has_side_effects=True
        ),
        cost_estimate=cost(70),
        name="finish",
    )(lengths, order, tok, fg, rq, rkv, sums, wide_sums, ready, wq, wk, wv, others)


def unpack_kernel(qkv, total, *refs):
    outs, (narrow, inner, outer, sems) = refs[:6], refs[6:]
    half = qkv.shape[2] // 3
    blocks = inner.shape[1] // (2 * half)
    copies = []

    def leave(src, i):
        copy = pltpu.make_async_copy(src, outs[i], sems.at[i])
        copy.start()
        copies.append(copy)

    for k in range(2):
        cols = slice(k * half, (k + 1) * half)
        outer[:, cols] = total[k, (1 + blocks) * half :].astype(F32)
    leave(outer, 5)
    for k in range(2):
        for t in range(blocks):
            cols = slice((2 * t + k) * half, (2 * t + k + 1) * half)
            inner[:, cols] = total[k, (1 + t) * half : (2 + t) * half].astype(F32)
    leave(inner, 4)
    for i in range(3):
        for k in range(2):
            for p in range(3):
                cols = slice((3 * k + p) * 128, (3 * k + p + 1) * 128)
                narrow[i, :, cols] = qkv[k, p, i * half : (i + 1) * half].astype(F32)
        leave(narrow.at[i], i)
    for k in range(2):
        narrow[3, :, k * half : (k + 1) * half] = total[k, 0:half].astype(F32)
    leave(narrow.at[3], 3)
    for copy in copies:
        copy.wait()


def unpack(qkv, total, hidden):
    half = total.shape[2]
    narrow = jax.ShapeDtypeStruct((half, 2 * half), F32)
    return pl.pallas_call(
        unpack_kernel,
        out_shape=[narrow] * 4
        + [
            jax.ShapeDtypeStruct((half, hidden), F32),
            jax.ShapeDtypeStruct((hidden // 2, 2 * half), F32),
        ],
        in_specs=[VMEM] * 2,
        out_specs=[ANY] * 6,
        scratch_shapes=[
            pltpu.VMEM((4, half, 2 * half), F32),
            pltpu.VMEM((half, hidden), F32),
            pltpu.VMEM((hidden // 2, 2 * half), F32),
            pltpu.SemaphoreType.DMA((6,)),
        ],
        compiler_params=ROOM,
        cost_estimate=cost(10),
        name="unpack",
    )(qkv, total)


def pick(table, index):
    places = jnp.arange(table.shape[0], dtype=jnp.int32)
    return jnp.sum(jnp.where(index[..., None] == places, table, 0), -1)


def shards(
    size,
    tokens,
    teacher,
    lengths,
    block_order,
    query_weight,
    query_bias,
    key_weight,
    value_weight,
    value_bias,
    out_weight,
    out_bias,
    gain_one,
    shift_one,
    inner_weight,
    inner_bias,
    outer_weight,
    outer_bias,
    gain_two,
    shift_two,
):
    seqs, rows, width = tokens.shape
    per_plane = size // GROUPS
    blocks_each = rows // BLK
    ctx, x = lax.axis_index("ctx"), lax.axis_index("wa")
    c, place = lax.rem(ctx, 2), lax.rem(ctx, per_plane)
    masks = [1 << b for b in reversed(range(per_plane.bit_length() - 1))]
    offsets = [0]
    for m in masks:
        offsets += [o ^ m for o in offsets]

    def across(value):
        return lax.ppermute(value, "wa", [(0, 1), (1, 0)])

    def flip(value, m):
        return lax.ppermute(value, "ctx", [(i, i ^ m) for i in range(size)])

    lines = [[g * per_plane + r for g in range(GROUPS)] for r in range(per_plane)]

    def turn(value):
        return lax.all_to_all(value, "ctx", 0, 0, axis_index_groups=lines)

    cores = [[i for i in range(size) if i % 2 == k] for k in range(2)]

    def paired(mine):
        sibling = flip(mine, 1)
        return jnp.where(c == 0, jnp.stack([mine, sibling]), jnp.stack([sibling, mine]))

    def reduced(grad):
        four = grad.reshape(2, 2, *grad.shape[1:])
        keep = lax.dynamic_index_in_dim(four, c, 1, False)
        give = lax.dynamic_index_in_dim(four, 1 - c, 1, False)
        keep = add_low(keep, flip(give, 1))
        mine = lax.dynamic_index_in_dim(keep, x, 0, False)
        mine = add_low(mine, across(lax.dynamic_index_in_dim(keep, 1 - x, 0, False)))
        return paired(lax.psum(mine, "ctx", axis_index_groups=cores))

    def reduced_dense(grad):
        four = grad.reshape(2, 2, *grad.shape[1:])
        keep = lax.dynamic_index_in_dim(four, c, 1, False)
        give = lax.dynamic_index_in_dim(four, 1 - c, 1, False)
        keep = add_low(keep, flip(give, 1))
        mine = lax.psum_scatter(
            keep.reshape(-1, keep.shape[-1]), "wa", scatter_dimension=0, tiled=True
        )
        return lax.psum(mine, "ctx", axis_index_groups=cores)

    vectors = (
        query_bias,
        value_bias,
        out_bias,
        gain_one,
        shift_one,
        outer_bias,
        gain_two,
        shift_two,
        inner_bias,
    )
    half, hidden = width // 2, 2 * inner_bias.shape[0]
    fused = per_plane == 4

    if fused:
        found = start(
            lengths,
            block_order,
            tokens,
            (query_weight, key_weight, value_weight, out_weight, inner_weight, outer_weight),
            vectors,
        )
        queries = [q.reshape(-1, BLK, q.shape[2]) for q in found[:seqs]]
        pieces = [[kv.reshape(-1, BLK, kv.shape[3])] for kv in found[seqs : 2 * seqs]]
        attended, lses = found[2 * seqs : 3 * seqs], found[3 * seqs : 4 * seqs]
        first_back, pair, others, *rest = found[4 * seqs :]
        dense_weights = [out_weight, rest[0], inner_weight, rest[1], outer_weight, rest[2]]
    else:
        count = block_order.shape[0]
        ids = jnp.arange(count, dtype=jnp.int32)
        owner = ids // blocks_each
        index_of = jnp.array([offsets.index(o) for o in range(per_plane)], jnp.int32)
        piece_of = pick(index_of, (owner % per_plane) ^ place)
        spot = (piece_of * GROUPS + owner // per_plane) * blocks_each + ids % blocks_each
        key_order = jnp.sum(jnp.where(block_order[None, :] == ids[:, None], spot[None, :], 0), 1)
        near = jnp.arange(GROUPS * blocks_each, dtype=jnp.int32)
        near_ids = (near // blocks_each * per_plane + place) * blocks_each + near % blocks_each
        near_pos = pick(block_order, near_ids)
        rank = jnp.sum((near_pos[None, :] < near_pos[:, None]).astype(jnp.int32), 1)
        query_order = jnp.sum(jnp.where(rank[None, :] == near[:, None], near[None, :], 0), 1)
        own_pos = pick(block_order, ctx * blocks_each + jnp.arange(blocks_each, dtype=jnp.int32))
        scalars, row_counts = [], []
        for s in range(seqs):
            used = jnp.sum((near_pos * BLK < lengths[s]).astype(jnp.int32))
            head = jnp.concatenate([lengths[s][None], used[None], jnp.zeros((6,), jnp.int32)])
            scalars.append(jnp.concatenate([head, query_order, key_order]))
            row_counts.append(jnp.clip(lengths[s] - own_pos * BLK, 0, BLK))

        counts = jnp.concatenate(row_counts)
        own_vec = jnp.concatenate(vectors)[None]
        other_vec = across(own_vec)
        pair = jnp.where(
            x == 0, jnp.stack([own_vec, other_vec]), jnp.stack([other_vec, own_vec])
        ).astype(F32)
        narrow = pair[:, 0, : 8 * half].reshape(2, 8, half).swapaxes(0, 1).reshape(8, width)
        wide_vec = pair[:, 0, 8 * half :].reshape(1, -1)

        def quarter(weight):
            n = weight.shape[0] // 2
            return lax.dynamic_slice_in_dim(weight, c * n, n, 0)

        first_qkv = across(
            jnp.concatenate([quarter(w) for w in (query_weight, key_weight, value_weight)], 0)
        )
        second_qkv = flip(first_qkv, 1)
        dense_weights = []
        last = first_qkv
        for weight in (out_weight, inner_weight, outer_weight):
            piece, last = lax.optimization_barrier((quarter(weight), last))
            last = across(piece)
            dense_weights += [weight, last, flip(last, 1)]

        projected = project(
            counts, tokens, narrow, query_weight, key_weight, value_weight, first_qkv, second_qkv
        )
        queries, pieces = [], []
        for s in range(seqs):
            kv = turn(projected[2 * s + 1])
            queries.append(turn(projected[2 * s]).reshape(-1, BLK, width // GROUPS))
            held = [kv.reshape(-1, BLK, kv.shape[2])]
            for m in masks:
                held += [flip(piece, m) for piece in held]
            pieces.append(held)

        attended, lses = [], []
        for s in range(seqs):
            o, lse = attend(s, per_plane, lengths, block_order, queries[s], pieces[s])
            attended.append(o.reshape(queries[s].shape))
            lses.append(lse)
    if fused:
        fours = [first_back, *attended[1:]]
        found = middle(lengths, block_order, tokens, teacher, pair, fours, dense_weights)
        output, firsts, sums, wide_sums, a_own, a_give, b_own, b_give = found[:8]
        heads_grad = [g.reshape(queries[0].shape) for g in found[8:]]
        ready = (a_own, a_give, b_own, b_give)
    else:
        dense_out = []
        for s in range(seqs):
            o4 = turn(attended[s].reshape(GROUPS, rows, -1))
            dense_out.append(
                dense(
                    row_counts[s], o4, tokens[s], teacher[s], narrow[2:], wide_vec, dense_weights
                )
            )
        output = jnp.stack([d[0] for d in dense_out])
        first_grads = [d[1] for d in dense_out]
        heads_grad = [turn(d[2]).reshape(queries[s].shape) for s, d in enumerate(dense_out)]
        sums = sum(d[9] for d in dense_out)
        wide_sums = sum(d[10] for d in dense_out)
        dense_sums = [reduced_dense(g) for g in dense_grads([d[3:9] for d in dense_out])]

    if fused:
        flat_rows = (GROUPS * rows, width // GROUPS)
        rq, rkv, ready = attend_back_all(
            [
                [
                    *(a.reshape(flat_rows) for a in (queries[s], heads_grad[s], attended[s])),
                    lses[s],
                    pieces[s][0].reshape(-1, pieces[s][0].shape[2]),
                ]
                for s in range(seqs)
            ],
            ready,
        )
    else:
        dqs, dkvs = [], []
        for s in range(seqs):
            found = attend_back(
                scalars[s], queries[s], heads_grad[s], attended[s], lses[s], pieces[s]
            )
            dqs.append(turn(found[0].reshape(GROUPS, rows, -1)))
            held = [piece.reshape(GROUPS, rows, -1) for piece in found[1:]]
            for m in reversed(masks):
                n = len(held) // 2
                held = [add_low(mine, flip(theirs, m)) for mine, theirs in zip(held[:n], held[n:])]
            dkvs.append(turn(held[0]))
        tokens_grad, g_qkv, sums_qkv = project_grads(
            counts,
            tokens,
            first_grads,
            dqs + dkvs,
            query_weight,
            key_weight,
            value_weight,
            first_qkv,
            second_qkv,
        )

    if fused:
        tokens_grad, qkv, total, small = finish(
            lengths,
            block_order,
            tokens,
            firsts,
            rq,
            rkv,
            sums,
            wide_sums,
            ready,
            query_weight,
            key_weight,
            value_weight,
            others,
        )
        query_grad, key_grad, value_grad, out_grad, inner_grad, outer_grad = unpack(
            qkv, total, hidden
        )
        small = small.reshape(-1)
    else:
        valid = jnp.full((128,), sum(jnp.sum(r) for r in row_counts).astype(F32))
        small = jnp.concatenate(
            [sums[:7].reshape(-1), sums_qkv[:2].reshape(-1), wide_sums[0], valid]
        )
        small = lax.psum(small, ("ctx", "wa"))
        qkv = reduced(jnp.moveaxis(g_qkv, (2, 1), (0, 1)).reshape(4, 3, -1, 128))
        out_grad, inner_grad, outer_grad = (
            paired(g).reshape(-1, g.shape[-1]).astype(F32) for g in dense_sums
        )
        qkv = qkv.reshape(6, 3, half, 128).astype(F32)
        query_grad, key_grad, value_grad = (
            qkv[:, i].swapaxes(0, 1).reshape(half, width) for i in range(3)
        )

    def vector(start, length):
        return lax.dynamic_slice_in_dim(small, start + x * (length // 2), length // 2, 0)

    end = 9 * width
    loss = jnp.sum(small[6 * width : 7 * width]) / (small[end + hidden] * width)
    return (
        output,
        tokens_grad,
        query_grad,
        vector(7 * width, width),
        key_grad,
        value_grad,
        vector(8 * width, width),
        out_grad,
        vector(5 * width, width),
        vector(3 * width, width),
        vector(4 * width, width),
        inner_grad,
        vector(end, hidden),
        outer_grad,
        vector(2 * width, width),
        vector(0, width),
        vector(width, width),
        loss,
    )


def solution(mesh):
    row, split, both = P("wa"), P("wa", None), P("wa", "ctx", None)
    placed = (both, both, row, P(), split, row, split, split, row, split, row, row, row)
    placed += (split, row, split, row, row, row)
    return jax.shard_map(
        functools.partial(shards, mesh.shape["ctx"]),
        mesh=mesh,
        in_specs=placed,
        out_specs=(
            both,
            both,
            split,
            row,
            split,
            split,
            row,
            split,
            row,
            row,
            row,
            split,
            row,
            split,
            row,
            row,
            row,
            P(),
        ),
        check_vma=False,
    )
```

```python
import functools
import math

import jax
import jax.numpy as jnp
from jax import lax
from jax.experimental import pallas as pl
from jax.experimental.pallas import tpu as pltpu
from jax.sharding import PartitionSpec as P

DH = 64
BLK = 128
GROUPS = 4
LN2 = math.log(2.0)
NT = (((1,), (1,)), ((), ()))
NN = (((1,), (0,)), ((), ()))
TN = (((0,), (0,)), ((), ()))
F32 = jnp.float32
BF16 = jnp.bfloat16
VMEM = pl.BlockSpec(memory_space=pltpu.VMEM)
SMEM = pl.BlockSpec(memory_space=pltpu.SMEM)
ANY = pl.BlockSpec(memory_space=pl.ANY)
ROOM = pltpu.CompilerParams(vmem_limit_bytes=62 * 2**20)


def dot(left, right, dims=NN):
    return lax.dot_general(left, right, dims, preferred_element_type=F32)


def cost(us):
    return pl.CostEstimate(flops=int(us * 1.15e9), bytes_accessed=1 << 20, transcendentals=0)


def weight_copies(full, own, first, second, sems, base):
    x, c = lax.axis_index("wa"), lax.rem(lax.axis_index("ctx"), 2)
    half = own.shape[0]
    quarter = half // 2
    other = (1 - x) * half
    places = (
        (own, x * half, half),
        (first, other + c * quarter, quarter),
        (second, other + (1 - c) * quarter, quarter),
    )
    return [
        pltpu.make_async_copy(
            src, full.at[pl.ds(pl.multiple_of(start, quarter), size)], sems.at[base + i]
        )
        for i, (src, start, size) in enumerate(places)
    ]


class Counts:
    def __init__(self, lengths, order):
        self.lengths, self.order = lengths, order

    def __getitem__(self, i):
        place = 2 * lax.axis_index("ctx") + i % 2
        return self.lengths[i // 2] - self.order[place] * BLK


def valid_rows(sc, s, rows):
    row = lax.broadcasted_iota(jnp.int32, (rows, 1), 0)
    first = jnp.where(row < sc[2 * s], 1.0, 0.0)
    later = jnp.where(row - BLK < sc[2 * s + 1], 1.0, 0.0)
    return jnp.where(row < BLK, first, later)


def half_copies(full, own, other, sems, base):
    x, half = lax.axis_index("wa"), own.shape[0]
    return [
        pltpu.make_async_copy(
            src, full.at[pl.ds(pl.multiple_of(k * half, half), half)], sems.at[base + i]
        )
        for i, (src, k) in enumerate(((own, x), (other, 1 - x)))
    ]


def project_kernel(sc, tok, vec, wq, wk, wv, first, second, *rest):
    seqs, rows, width = tok.shape
    outs, (full, sems) = rest[: 2 * seqs], rest[2 * seqs :]
    quarter = wq.shape[0] // 2
    copies = []
    for i, own in enumerate((wq, wk, wv)):
        part = pl.ds(i * quarter, quarter)
        copies.append(
            weight_copies(full.at[i], own, first.at[part], second.at[part], sems, 3 * i)
        )
    for group in copies:
        for copy in group:
            copy.start()
    flat = tok[...].reshape(seqs * rows, width)
    per = width // GROUPS
    heads = per // DH
    valid = jnp.concatenate([valid_rows(sc, s, rows) for s in range(seqs)], 0) > 0.0
    for copy in copies[1]:
        copy.wait()
    keys = jnp.where(valid, dot(flat, full[1]), 0.0).astype(BF16)
    for copy in copies[2]:
        copy.wait()
    values = jnp.where(valid, dot(flat, full[2]) + vec[1:2, :], 0.0).astype(BF16)
    for s in range(seqs):
        rs = slice(s * rows, (s + 1) * rows)
        for g in range(GROUPS):
            for h in range(heads):
                cols = slice(g * per + h * DH, g * per + (h + 1) * DH)
                outs[2 * s + 1][g, :, h * 128 : (h + 1) * 128] = jnp.concatenate(
                    [keys[rs, cols], values[rs, cols]], 1
                )
    for copy in copies[0]:
        copy.wait()
    queries = ((dot(flat, full[0]) + vec[0:1, :]) * (DH**-0.5 / LN2)).astype(BF16)
    for s in range(seqs):
        rs = slice(s * rows, (s + 1) * rows)
        for g in range(GROUPS):
            outs[2 * s][g] = queries[rs, g * per : (g + 1) * per]


def project(sc, tok, vec, wq, wk, wv, first, second):
    seqs, rows, width = tok.shape
    per = width // GROUPS
    shapes = [
        jax.ShapeDtypeStruct((GROUPS, rows, n), BF16) for _ in range(seqs) for n in (per, 2 * per)
    ]
    return pl.pallas_call(
        project_kernel,
        out_shape=shapes,
        in_specs=[SMEM, VMEM, VMEM] + [ANY] * 5,
        out_specs=[VMEM] * len(shapes),
        scratch_shapes=[pltpu.VMEM((3, width, width), BF16), pltpu.SemaphoreType.DMA((9,))],
        compiler_params=ROOM,
        cost_estimate=cost(5),
        name="project",
    )(sc, tok, vec, wq, wk, wv, first, second)


def load_pieces(pieces, kv, sems):
    per = pieces[0].shape[0]
    copies = [
        pltpu.make_async_copy(piece, kv.at[pl.ds(i * per, per)], sems.at[i])
        for i, piece in enumerate(pieces)
    ]
    for copy in copies:
        copy.start()
    for copy in copies:
        copy.wait()


def forward_kernel(wide, narrow, count, s, per_plane, lengths, order, q_ref, *rest):
    pieces, rest = rest[:count], rest[count:]
    o_ref, lse_ref, kv_ref, qa, acc, sums, spots, sems = rest
    blocks = q_ref.shape[0]
    heads = q_ref.shape[2] // DH
    rows = blocks * BLK
    length = lengths[s]
    place = lax.rem(lax.axis_index("ctx"), per_plane)

    def put(b, _):
        owner = b // 2
        offset = lax.bitwise_xor(lax.rem(owner, per_plane), place)
        piece = 0
        for bit in range(per_plane.bit_length() - 1):
            piece = 2 * piece + lax.rem(lax.div(offset, 1 << bit), 2)
        spots[order[b]] = (piece * GROUPS + lax.div(owner, per_plane)) * 2 + lax.rem(b, 2)
        return 0

    lax.fori_loop(0, order.shape[0], put, 0)
    load_pieces(pieces, kv_ref, sems)

    def gather(h, start, n):
        return jnp.concatenate(
            [kv_ref[spots[start + i], :, h * 128 : (h + 1) * 128] for i in range(n)], 0
        )

    whole = length // (wide * BLK)
    tail = whole * wide
    tails = (length - tail * BLK + narrow * BLK - 1) // (narrow * BLK)
    for h in range(heads):
        hs = slice(h * DH, (h + 1) * DH)
        own = jnp.concatenate([q_ref[b, :, hs] for b in range(blocks)], 0)
        qa[...] = jnp.concatenate([own, jnp.zeros_like(own)], 1)
        acc[...] = jnp.zeros_like(acc)
        sums[...] = jnp.zeros_like(sums)

        def step(start, n, masked, h=h):
            kv = gather(h, start, n)
            scores = dot(qa[...], kv, NT)
            if masked:
                place = lax.broadcasted_iota(jnp.int32, scores.shape, 1) + start * BLK
                scores = jnp.where(place < length, scores, -1e30)
            p = jnp.exp2(scores)
            sums[...] += sum(p[:, i * 128 : (i + 1) * 128] for i in range(n))
            acc[...] += dot(p.astype(BF16), kv)

        def wide_step(j, _, step=step):
            step(j * wide, wide, False)
            return 0

        def narrow_step(j, _, step=step):
            step(tail + j * narrow, narrow, True)
            return 0

        lax.fori_loop(0, whole, wide_step, 0)
        lax.fori_loop(0, tails, narrow_step, 0)
        total = jnp.sum(sums[...], 1, keepdims=True)
        across = jnp.transpose(jnp.broadcast_to(total, (rows, 128)))[:8]
        good = (jnp.min(across) > 2.0**-80) & (jnp.max(across) < 2.0**100)

        @pl.when(good)
        def _(h=h, hs=hs, total=total, across=across):
            lse_ref[h] = jnp.log2(across)
            o_ref[:, hs] = (acc[:, DH:] * (1.0 / total)).astype(BF16)

        @pl.when(jnp.logical_not(good))
        def _(h=h, hs=hs):
            key_blocks = (length + BLK - 1) // BLK

            def rows_step(t, _):
                part = pl.ds(pl.multiple_of(t * BLK, BLK), BLK)
                q = qa[part, :]

                def scores_of(j):
                    kv = gather(h, j, 1)
                    scores = dot(q, kv, NT)
                    place = lax.broadcasted_iota(jnp.int32, scores.shape, 1) + j * BLK
                    return kv, jnp.where(place < length, scores, -1e30)

                largest = lax.fori_loop(
                    0,
                    key_blocks,
                    lambda j, m: jnp.maximum(m, jnp.max(scores_of(j)[1], 1, keepdims=True)),
                    jnp.full((BLK, 1), -1e30, F32),
                )
                acc[part, :] = jnp.zeros((BLK, 128), F32)
                sums[part, :] = jnp.zeros((BLK, 128), F32)

                def add(j, _):
                    kv, scores = scores_of(j)
                    p = jnp.exp2(scores - largest)
                    sums[part, :] += p
                    acc[part, :] += dot(p.astype(BF16), kv)
                    return 0

                lax.fori_loop(0, key_blocks, add, 0)
                row_total = jnp.sum(sums[part, :], 1, keepdims=True)
                lse = largest + jnp.log2(row_total)
                lse_ref[h, :, part] = jnp.transpose(jnp.broadcast_to(lse, (BLK, 128)))[:8]
                o_ref[part, hs] = (acc[part, :][:, DH:] * (1.0 / row_total)).astype(BF16)
                return 0

            lax.fori_loop(0, rows // BLK, rows_step, 0)


def attend(s, per_plane, lengths, order, q, pieces):
    blocks, _, per = q.shape
    rows, heads = blocks * BLK, per // DH
    key_blocks = len(pieces) * pieces[0].shape[0]
    return pl.pallas_call(
        functools.partial(forward_kernel, 8, 2, len(pieces), s, per_plane),
        out_shape=(
            jax.ShapeDtypeStruct((rows, per), BF16),
            jax.ShapeDtypeStruct((heads, 8, rows), F32),
        ),
        in_specs=[SMEM, SMEM, VMEM] + [ANY] * len(pieces),
        out_specs=(VMEM, VMEM),
        scratch_shapes=[
            pltpu.VMEM((key_blocks, BLK, 2 * per), BF16),
            pltpu.VMEM((rows, 128), BF16),
            pltpu.VMEM((rows, 128), F32),
            pltpu.VMEM((rows, 128), F32),
            pltpu.SMEM((key_blocks,), jnp.int32),
            pltpu.SemaphoreType.DMA((len(pieces),)),
        ],
        compiler_params=ROOM,
        cost_estimate=cost(20),
        name="attend",
    )(lengths, order, q, *pieces)


def backward_kernel(qn, kn, count, sc, q_ref, do_ref, o_ref, lse_ref, *rest):
    pieces, dq_ref, outs = rest[:count], rest[count], rest[count + 1 : 2 * count + 1]
    kv_ref, both, dkv, dq, lse_row, delta_row, sems = rest[2 * count + 1 :]
    blocks = q_ref.shape[0]
    heads = q_ref.shape[2] // DH
    key_blocks = kv_ref.shape[0]
    tile = qn * BLK
    length, used = sc[0], sc[1]
    whole = length // (kn * BLK)
    parts = (length + kn * BLK - 1) // (kn * BLK)
    tiles = (used + qn - 1) // qn
    ones = jnp.ones((8, DH), BF16)
    load_pieces(pieces, kv_ref, sems)
    for h in range(heads):
        hs = slice(h * DH, (h + 1) * DH)

        def clear(i, _):
            dkv[pl.ds(pl.multiple_of(i * 1024, 1024), 1024), :] = jnp.zeros((1024, 128), F32)
            return 0

        lax.fori_loop(0, key_blocks // 8, clear, 0)
        dq[...] = jnp.zeros_like(dq)

        def prepare(t, _, h=h, hs=hs):
            base = pl.multiple_of(t * (2 * tile), 2 * tile)
            start = pl.multiple_of(t * tile, tile)
            places = [sc[8 + t * qn + i] for i in range(qn)]
            q = jnp.concatenate([q_ref[s, :, hs] for s in places], 0)
            do = jnp.concatenate([do_ref[s, :, hs] for s in places], 0)
            o = jnp.concatenate([o_ref[s, :, hs] for s in places], 0)
            zero = jnp.zeros_like(q)
            both[pl.ds(base, tile), :] = jnp.concatenate([q, zero], 1)
            both[pl.ds(base + tile, tile), :] = jnp.concatenate([zero, do], 1)
            product = do.astype(F32) * o.astype(F32)
            high = product.astype(BF16)
            rest_of = (product - high.astype(F32)).astype(BF16)
            delta_row[:, pl.ds(start, tile)] = dot(ones, high, NT) + dot(ones, rest_of, NT)
            lse_row[:, pl.ds(start, tile)] = jnp.concatenate(
                [lse_ref[h, :, pl.ds(pl.multiple_of(s * BLK, BLK), BLK)] for s in places], 1
            )
            return 0

        lax.fori_loop(0, tiles, prepare, 0)

        def rows_step(t, _, h=h):
            base = pl.multiple_of(t * (2 * tile), 2 * tile)
            span = pl.ds(pl.multiple_of(t * tile, tile), tile)

            def step(j, masked):
                places = [sc[8 + blocks + j * kn + i] for i in range(kn)]
                kv = jnp.concatenate([kv_ref[s, :, h * 128 : (h + 1) * 128] for s in places], 0)
                b = both[pl.ds(base, 2 * tile), :]
                found = dot(kv, b, NT)
                p = jnp.exp2(found[:, :tile] - lse_row[:1, span])
                if masked:
                    place = lax.broadcasted_iota(jnp.int32, p.shape, 0) + j * (kn * BLK)
                    p = jnp.where(place < length, p, 0.0)
                ds = (p * (found[:, tile:] - delta_row[:1, span])).astype(BF16)
                grads = dot(jnp.concatenate([ds, p.astype(BF16)], 1), b)
                for i, s in enumerate(places):
                    dkv[pl.ds(pl.multiple_of(s * BLK, BLK), BLK), :] += grads[
                        i * BLK : (i + 1) * BLK
                    ]
                dq[span, :] += dot(ds, kv, TN)

            def whole_step(j, _):
                step(j, False)
                return 0

            lax.fori_loop(0, whole, whole_step, 0)

            @pl.when(parts > whole)
            def _():
                step(whole, True)

            return 0

        lax.fori_loop(0, tiles, rows_step, 0)
        for i in range(blocks):
            dq_ref[sc[8 + i], :, hs] = (
                dq[i * BLK : (i + 1) * BLK, :DH] * DH**-0.5
            ).astype(BF16)
        level = jnp.where(lax.broadcasted_iota(jnp.int32, (1, 128), 1) < DH, LN2, 1.0)
        per_piece = key_blocks // count
        for n, out in enumerate(outs):
            for i in range(per_piece):
                b = n * per_piece + i
                out[i, :, h * 128 : (h + 1) * 128] = (
                    dkv[b * BLK : (b + 1) * BLK, :] * level
                ).astype(BF16)


def attend_back(sc, q, do, o, lse, pieces):
    blocks, _, per = q.shape
    rows = blocks * BLK
    key_blocks = len(pieces) * pieces[0].shape[0]
    return pl.pallas_call(
        functools.partial(backward_kernel, 4, 4, len(pieces)),
        out_shape=[jax.ShapeDtypeStruct(q.shape, BF16)]
        + [jax.ShapeDtypeStruct(p.shape, BF16) for p in pieces],
        in_specs=[SMEM] + [VMEM] * 4 + [ANY] * len(pieces),
        out_specs=[VMEM] * (1 + len(pieces)),
        scratch_shapes=[
            pltpu.VMEM((key_blocks, BLK, 2 * per), BF16),
            pltpu.VMEM((2 * rows, 128), BF16),
            pltpu.VMEM((key_blocks * BLK, 128), F32),
            pltpu.VMEM((rows, 128), F32),
            pltpu.VMEM((8, rows), F32),
            pltpu.VMEM((8, rows), F32),
            pltpu.SemaphoreType.DMA((len(pieces),)),
        ],
        compiler_params=ROOM,
        cost_estimate=cost(45),
        name="attend_back",
    )(sc, q, do, o, lse, *pieces)


def norm(values):
    centered = values - jnp.mean(values, -1, keepdims=True)
    inverse = lax.rsqrt(jnp.mean(centered * centered, -1, keepdims=True) + 1e-6)
    return centered * inverse, inverse


def norm_back(upstream, normed, inverse):
    return inverse * (
        upstream
        - jnp.mean(upstream, -1, keepdims=True)
        - normed * jnp.mean(upstream * normed, -1, keepdims=True)
    )


def normal_parts(x):
    z = jnp.abs(x) * (0.5**0.5)
    bell = jnp.exp(-0.5 * x * x)
    t = 1.0 / (1.0 + 0.3275911 * z)
    poly = t * (
        0.254829592
        + t * (-0.284496736 + t * (1.421413741 + t * (-1.453152027 + t * 1.061405429)))
    )
    upper = 0.5 * poly * bell
    return jnp.where(x >= 0, 1.0 - upper, upper), bell * (2.0 * math.pi) ** -0.5


def dense_kernel(sc, att4, tok, teach, vec, wide_vec, *rest):
    weights, rest = rest[:9], rest[9:]
    outs, (wo, wi, wu, slope, sems) = rest[:11], rest[11:]
    out, fg, ag, att_o, br_o, hl_o, il_o, act_o, ol_o, sums, wide_sums = outs
    rows, width = tok.shape
    hidden = wi.shape[1]
    tile = 512
    copies = [
        weight_copies(full, *weights[3 * i : 3 * i + 3], sems, 3 * i)
        for i, full in enumerate((wo, wi, wu))
    ]
    for group in copies:
        for copy in group:
            copy.start()
    per = att4.shape[2]
    att = jnp.concatenate([att4[g] for g in range(GROUPS)], 1)
    att_o[...] = att
    row = lax.broadcasted_iota(jnp.int32, (rows, 1), 0)
    mask = jnp.where(
        row < BLK, jnp.where(row < sc[0], 1.0, 0.0), jnp.where(row - BLK < sc[1], 1.0, 0.0)
    )
    out_bias, gain_one, shift_one = vec[0:1, :], vec[1:2, :], vec[2:3, :]
    outer_bias, gain_two, shift_two = vec[3:4, :], vec[4:5, :], vec[5:6, :]
    for copy in copies[0]:
        copy.wait()
    first = tok[...].astype(F32) + dot(att, wo[...]) + out_bias
    normed_one, inverse_one = norm(first)
    hidden_in = normed_one * gain_one + shift_one
    hl = hidden_in.astype(BF16)
    hl_o[...] = hl
    for copy in copies[1] + copies[2]:
        copy.wait()
    second = hidden_in + outer_bias
    for n in range(hidden // tile):
        cols = slice(n * tile, (n + 1) * tile)
        inner = dot(hl, wi[:, cols]) + wide_vec[0:1, cols]
        below, density = normal_parts(inner)
        act = (inner * below).astype(BF16)
        act_o[:, cols] = act
        slope[:, cols] = below + inner * density
        second += dot(act, wu[cols, :])
    normed_two, inverse_two = norm(second)
    final = normed_two * gain_two + shift_two
    out[...] = final.astype(BF16)
    residue = (final - teach[...].astype(F32)) * mask
    add = functools.partial(jnp.sum, axis=0, keepdims=True)
    second_grad = norm_back(residue * gain_two, normed_two, inverse_two)
    ol = second_grad.astype(BF16)
    ol_o[...] = ol
    hidden_grad = second_grad
    for n in range(hidden // tile):
        cols = slice(n * tile, (n + 1) * tile)
        il = (dot(ol, wu[cols, :], NT) * slope[:, cols]).astype(BF16)
        il_o[:, cols] = il
        wide_sums[0:1, cols] = add(il.astype(F32))
        hidden_grad += dot(il, wi[:, cols], NT)
    first_grad = norm_back(hidden_grad * gain_one, normed_one, inverse_one)
    fg[...] = first_grad
    br = first_grad.astype(BF16)
    br_o[...] = br
    att_grad = dot(br, wo[...], NT).astype(BF16)
    for g in range(GROUPS):
        ag[g] = att_grad[:, g * per : (g + 1) * per]
    sums[0:1, :] = add(residue * normed_two)
    sums[1:2, :] = add(residue)
    sums[2:3, :] = add(ol.astype(F32))
    sums[3:4, :] = add(hidden_grad * normed_one)
    sums[4:5, :] = add(hidden_grad)
    sums[5:6, :] = add(br.astype(F32))
    sums[6:7, :] = add(residue * residue)
    sums[7:8, :] = jnp.zeros((1, width), F32)


def dense(sc, att4, tok, teach, vec, wide_vec, weights):
    rows, width = tok.shape
    hidden = wide_vec.shape[1]
    narrow = jax.ShapeDtypeStruct((rows, width), BF16)
    wide = jax.ShapeDtypeStruct((rows, hidden), BF16)
    return pl.pallas_call(
        dense_kernel,
        out_shape=[
            narrow,
            jax.ShapeDtypeStruct((rows, width), F32),
            jax.ShapeDtypeStruct(att4.shape, BF16),
            narrow,
            narrow,
            narrow,
            wide,
            wide,
            narrow,
            jax.ShapeDtypeStruct((8, width), F32),
            jax.ShapeDtypeStruct((1, hidden), F32),
        ],
        in_specs=[SMEM] + [VMEM] * 5 + [ANY] * 9,
        out_specs=[VMEM] * 11,
        scratch_shapes=[
            pltpu.VMEM((width, width), BF16),
            pltpu.VMEM((width, hidden), BF16),
            pltpu.VMEM((hidden, width), BF16),
            pltpu.VMEM((rows, hidden), F32),
            pltpu.SemaphoreType.DMA((9,)),
        ],
        compiler_params=ROOM,
        cost_estimate=cost(15),
        name="dense",
    )(sc, att4, tok, teach, vec, wide_vec, *weights)


def dense_grads_kernel(seqs, *refs):
    ins, (g_out, g_inner, g_outer) = refs[: 6 * seqs], refs[6 * seqs :]
    att, br, hl, il, act, ol = (
        jnp.concatenate([ins[6 * s + i][...] for s in range(seqs)], 0) for i in range(6)
    )
    for target, left, right in ((g_out, att, br), (g_inner, hl, il), (g_outer, act, ol)):
        rows = target.shape[1]
        for n in range(4):
            piece = left[:, n * rows : (n + 1) * rows]
            for t in range(right.shape[1] // 768):
                cols = slice(t * 768, (t + 1) * 768)
                target[n, :, cols] = dot(piece, right[:, cols], TN).astype(BF16)


def dense_grads(saved):
    seqs = len(saved)
    width, hidden = saved[0][0].shape[1], saved[0][3].shape[1]
    return pl.pallas_call(
        functools.partial(dense_grads_kernel, seqs),
        out_shape=[
            jax.ShapeDtypeStruct((4, width // 4, width), BF16),
            jax.ShapeDtypeStruct((4, width // 4, hidden), BF16),
            jax.ShapeDtypeStruct((4, hidden // 4, width), BF16),
        ],
        in_specs=[VMEM] * (6 * seqs),
        out_specs=[VMEM] * 3,
        compiler_params=ROOM,
        cost_estimate=cost(10),
        name="dense_grads",
    )(*[member for group in saved for member in group])


def project_grads_kernel(seqs, sc, tok, *refs):
    fgs, refs = refs[:seqs], refs[seqs:]
    grads_in, refs = refs[: 2 * seqs], refs[2 * seqs :]
    wq, wk, wv, first, second, tg, grads, sums, full, sems = refs
    rows, width = tok.shape[1:]
    per = width // GROUPS
    heads = per // DH
    quarter = wq.shape[0] // 2
    copies = []
    for i, own in enumerate((wq, wk, wv)):
        part = pl.ds(i * quarter, quarter)
        copies += weight_copies(full.at[i], own, first.at[part], second.at[part], sems, 3 * i)
    for copy in copies:
        copy.start()

    def head(i, s, g, h):
        if i == 0:
            return grads_in[s][g, :, h * DH : (h + 1) * DH]
        start = h * 128 + (i - 1) * DH
        return grads_in[seqs + s][g, :, start : start + DH]

    def whole(i):
        each = [
            jnp.concatenate([head(i, s, g, h) for g in range(GROUPS) for h in range(heads)], 1)
            for s in range(seqs)
        ]
        return jnp.concatenate(each, 0)

    valid = jnp.concatenate([valid_rows(sc, s, rows) for s in range(seqs)], 0) > 0.0
    dq = whole(0)
    halves = [jnp.where(valid, whole(i), jnp.zeros((), BF16)) for i in (1, 2)]
    flat = tok[...].reshape(seqs * rows, width)
    for copy in copies:
        copy.wait()
    total = jnp.concatenate([fgs[s][...] for s in range(seqs)], 0)
    for i, grad in enumerate((dq, *halves)):
        total += dot(grad, full[i], NT)
        found = dot(flat, grad, TN).astype(BF16)
        half = width // 2
        for n in range(2):
            for t in range(width // 128):
                grads[t % 3, t // 3, n, i * half : (i + 1) * half, :] = found[
                    n * half : (n + 1) * half, t * 128 : (t + 1) * 128
                ]
    tg[...] = total.reshape(seqs, rows, width)
    sums[0:1, :] = jnp.sum(dq.astype(F32), 0, keepdims=True)
    sums[1:2, :] = jnp.sum(halves[1].astype(F32), 0, keepdims=True)
    sums[2:8, :] = jnp.zeros((6, width), F32)


def project_grads(sc, tok, fgs, grads, wq, wk, wv, first, second):
    seqs, rows, width = tok.shape
    return pl.pallas_call(
        functools.partial(project_grads_kernel, seqs),
        out_shape=[
            jax.ShapeDtypeStruct(tok.shape, F32),
            jax.ShapeDtypeStruct((3, 2, 2, 3 * (width // 2), 128), BF16),
            jax.ShapeDtypeStruct((8, width), F32),
        ],
        in_specs=[SMEM] + [VMEM] * (1 + len(fgs) + len(grads)) + [ANY] * 5,
        out_specs=[VMEM] * 3,
        scratch_shapes=[pltpu.VMEM((3, width, width), BF16), pltpu.SemaphoreType.DMA((9,))],
        compiler_params=ROOM,
        cost_estimate=cost(10),
        name="project_grads",
    )(sc, tok, *fgs, *grads, wq, wk, wv, first, second)


MESH = pl.DeviceIdType.MESH


def position():
    ctx = lax.axis_index("ctx")
    return ctx // 4, lax.rem(ctx // 2, 2), lax.rem(ctx, 2), lax.axis_index("wa")


def device(z, y, c, x):
    return z * 4 + y * 2 + c, x


def greet(others):
    barrier = pltpu.get_barrier_semaphore()
    for other in others:
        pl.semaphore_signal(barrier, inc=1, device_id=other, device_id_type=MESH)
    pl.semaphore_wait(barrier, len(others))


def send(src, dst, sems, to):
    copy = pltpu.make_async_remote_copy(
        src_ref=src,
        dst_ref=dst,
        send_sem=sems[0],
        recv_sem=sems[1],
        device_id=to,
        device_id_type=MESH,
    )
    copy.start()
    return copy


def add_low(left, right):
    return (left.astype(F32) + right.astype(F32)).astype(BF16)


def back_kernel(seqs, *refs):
    per_seq = 5
    ins = [refs[per_seq * s : per_seq * (s + 1)] for s in range(seqs)]
    a_own, a_give, b_own, b_give, rq, rkv, dense_out, *refs = refs[per_seq * seqs :]
    q_v, do_v, o_v, lse_v, kv_v, both, dkv, dq, delta, obuf, qbuf = refs[:11]
    from_core, from_y, a_v, b_v, a_in, b_in, a2, b2, a2_in, b2_in = refs[11:21]
    az_in, bz_in, dres, in_sem, c_sem, y_sem, z_sem, q_sem, l_sem, x_sem, dz_sem = refs[21:]
    z, y, c, x = position()
    sibling, beside, over = device(z, y, 1 - c, x), device(z, 1 - y, c, x), device(z, y, c, 1 - x)
    line = [None] + [device(z ^ d, y, c, x) for d in range(1, GROUPS)]
    greet([sibling, beside, over] + line[1:])

    def pair(sems, *index):
        return sems.at[(0, *index)], sems.at[(1, *index)]

    flow = {}
    flow["a"] = send(a_give, a_in, pair(x_sem, 0), over)
    flow["b"] = send(b_give, b_in, pair(x_sem, 1), beside)
    loads = []
    for s in range(seqs):
        targets = [ref.at[s] for ref in (q_v, do_v, o_v, lse_v, kv_v)]
        group = [
            pltpu.make_async_copy(src, dst, in_sem.at[s, i])
            for i, (src, dst) in enumerate(zip(ins[s], targets))
        ]
        for copy in group:
            copy.start()
        loads.append(group)
    own_loads = [
        pltpu.make_async_copy(a_own, a_v, l_sem.at[0]),
        pltpu.make_async_copy(b_own, b_v, l_sem.at[1]),
    ]
    for copy in own_loads:
        copy.start()

    rows = q_v.shape[1]
    heads = q_v.shape[2] // DH
    keys = kv_v.shape[1]
    tile, ktile = rows // 2, 2048
    quarter = keys // 4
    chunk = quarter // GROUPS
    ones = jnp.ones((8, DH), BF16)
    level = jnp.where(lax.broadcasted_iota(jnp.int32, (1, 128), 1) < DH, LN2, 1.0)
    waits = []

    def group_rows(g):
        return pl.ds(pl.multiple_of(g * chunk, chunk), chunk)

    def core_stage(u):
        flow["c", u] = send(
            obuf.at[u, pl.ds(2 * quarter, 2 * quarter)], from_core.at[u], pair(c_sem, u), sibling
        )

    def y_stage(u):
        flow["c", u].wait()
        second = pl.ds(quarter, quarter)
        obuf[u, second] = add_low(obuf[u, second], from_core[u, second])
        flow["y", u] = send(obuf.at[u, second], from_y.at[u], pair(y_sem, u), beside)
        obuf[u, 0:quarter] = add_low(obuf[u, 0:quarter], from_core[u, 0:quarter])

    def z_stage(u):
        flow["y", u].wait()
        obuf[u, 0:quarter] = add_low(obuf[u, 0:quarter], from_y[u])
        for d in range(1, GROUPS):
            src = obuf.at[u, group_rows(z ^ d)]
            waits.append(send(src, rkv.at[u, z], pair(z_sem, u, d), line[d]))
        own = pltpu.make_async_copy(obuf.at[u, group_rows(z)], rkv.at[u, z], z_sem.at[0, u, 0])
        own.start()
        waits.append(own)

    def q_stage(h):
        for d in range(1, GROUPS):
            waits.append(send(qbuf.at[h, z ^ d], rq.at[h, z], pair(q_sem, h, d), line[d]))
        own = pltpu.make_async_copy(qbuf.at[h, z], rq.at[h, z], q_sem.at[0, h, 0])
        own.start()
        waits.append(own)

    a_half, b_half = a2.shape[1], b2.shape[1]

    def dense_second():
        for copy in own_loads:
            copy.wait()
        flow["a"].wait()
        for slot, which in ((0, y), (1, 1 - y)):
            part = pl.ds(pl.multiple_of(which * a_half, 16), a_half)
            a2[slot] = add_low(a_v[part, :], a_in[part, :])
        flow["a"] = send(a2.at[1], a2_in, pair(x_sem, 2), beside)
        flow["b"].wait()
        for slot, which in ((0, x), (1, 1 - x)):
            b2[slot] = add_low(b_v[which], b_in[which])
        flow["b"] = send(b2.at[1], b2_in, pair(x_sem, 3), over)

    low_bit, high_bit = lax.rem(z, 2), z // 2
    parts = (("a", a2, a2_in, az_in), ("b", b2, b2_in, bz_in))

    def rows_at(start, n):
        return pl.ds(pl.multiple_of(start, 16), n)

    def dense_third():
        for i, (name, held, arrived, landing) in enumerate(parts):
            flow[name].wait()
            held[0] = add_low(held[0], arrived[...])
            n = held.shape[1] // 2
            src = held.at[0, rows_at((1 - low_bit) * n, n)]
            flow[name] = send(src, landing.at[0:n], pair(dz_sem, i, 0), line[1])

    def dense_fourth():
        for i, (name, held, _, landing) in enumerate(parts):
            flow[name].wait()
            n = held.shape[1] // 2
            mine = rows_at(low_bit * n, n)
            held[0, mine] = add_low(held[0, mine], landing[0:n])
            src = held.at[0, rows_at(low_bit * n + (1 - high_bit) * (n // 2), n // 2)]
            flow[name] = send(src, landing.at[n : n + n // 2], pair(dz_sem, i, 1), line[2])

    def dense_fifth():
        base = 0
        for name, held, _, landing in parts:
            flow[name].wait()
            n = held.shape[1] // 2
            mine = rows_at(low_bit * n + high_bit * (n // 2), n // 2)
            dres[base : base + n // 2] = add_low(held[0, mine], landing[n : n + n // 2])
            base += n // 2

    units = [(h, s) for h in range(heads) for s in range(seqs)]
    slots = {}
    for u in range(len(units) - 1):
        slots.setdefault(2 * u + 3, []).append(functools.partial(y_stage, u))
        slots.setdefault(2 * u + 5, []).append(functools.partial(z_stage, u))
    slots.setdefault(5, []).append(dense_second)
    slots.setdefault(7, []).append(dense_third)
    slots.setdefault(9, []).append(dense_fourth)
    slots.setdefault(12, []).append(dense_fifth)

    for u, (h, s) in enumerate(units):
        hs = slice(h * DH, (h + 1) * DH)
        lanes = slice(h * 128, (h + 1) * 128)
        if h == 0:
            for copy in loads[s]:
                copy.wait()
        for n in range(2):
            for work in slots.get(2 * u + n, []):
                work()
            part = slice(n * tile, (n + 1) * tile)
            q, do, o = q_v[s, part, hs], do_v[s, part, hs], o_v[s, part, hs]
            zero = jnp.zeros_like(q)
            both[0:tile, :] = jnp.concatenate([q, zero], 1)
            both[tile : 2 * tile, :] = jnp.concatenate([zero, do], 1)
            product = do.astype(F32) * o.astype(F32)
            high = product.astype(BF16)
            remains = (product - high.astype(F32)).astype(BF16)
            delta[...] = dot(ones, high, NT) + dot(ones, remains, NT)
            dq[...] = jnp.zeros_like(dq)

            def step(j, _, u=u, s=s, h=h, n=n, part=part, lanes=lanes):
                span = pl.ds(pl.multiple_of(j * ktile, ktile), ktile)
                kv = kv_v[s, span, lanes]
                b = both[...]
                found = dot(kv, b, NT)
                p = jnp.exp2(jnp.minimum(found[:, :tile] - lse_v[s, h, 0:1, part], 1.0))
                ds = (p * (found[:, tile:] - delta[0:1, :])).astype(BF16)
                grads = dot(jnp.concatenate([ds, p.astype(BF16)], 1), b)
                if n == 0:
                    dkv[span, :] = grads
                else:
                    obuf[u, span, :] = ((dkv[span, :] + grads) * level).astype(BF16)
                dq[...] += dot(ds, kv, TN)
                return 0

            lax.fori_loop(0, keys // ktile, step, 0)
            found = (dq[:, :DH] * DH**-0.5).astype(BF16)
            for i in range(2):
                qbuf[h, 2 * n + i, :, s * DH : (s + 1) * DH] = found[
                    i * (tile // 2) : (i + 1) * (tile // 2)
                ]
        core_stage(u)
        if s == seqs - 1:
            q_stage(h)
    last = len(units) - 1
    for n in sorted(n for n in slots if n >= 2 * len(units)):
        for work in slots[n]:
            work()
    y_stage(last)
    z_stage(last)
    for copy in waits:
        copy.wait()
    done = pltpu.make_async_copy(dres, dense_out, l_sem.at[0])
    done.start()
    done.wait()


def attend_back_all(seqs_in, ready):
    seqs = len(seqs_in)
    q, _, _, lse, held = seqs_in[0]
    rows, per = q.shape
    heads = per // DH
    units = heads * seqs
    keys = held.shape[0]
    chunk = rows // GROUPS
    a, b = ready[0].shape, ready[2].shape
    a_half, b_half, half = a[0] // 2, b[1], a[1]
    dma = pltpu.SemaphoreType.DMA
    return pl.pallas_call(
        functools.partial(back_kernel, seqs),
        out_shape=[
            jax.ShapeDtypeStruct((heads, GROUPS, chunk, 128), BF16),
            jax.ShapeDtypeStruct((units, GROUPS, chunk, 128), BF16),
            jax.ShapeDtypeStruct(((a_half + b_half) // 4, half), BF16),
        ],
        in_specs=[ANY] * (5 * seqs + 4),
        out_specs=[ANY] * 3,
        scratch_shapes=[
            pltpu.VMEM((seqs, rows, per), BF16),
            pltpu.VMEM((seqs, rows, per), BF16),
            pltpu.VMEM((seqs, rows, per), BF16),
            pltpu.VMEM((seqs, *lse.shape), F32),
            pltpu.VMEM((seqs, keys, 2 * per), BF16),
            pltpu.VMEM((rows, 128), BF16),
            pltpu.VMEM((keys, 128), F32),
            pltpu.VMEM((rows // 2, 128), F32),
            pltpu.VMEM((8, rows // 2), F32),
            pltpu.VMEM((units, keys, 128), BF16),
            pltpu.VMEM((heads, GROUPS, chunk, 128), BF16),
            pltpu.VMEM((units, keys // 2, 128), BF16),
            pltpu.VMEM((units, keys // 4, 128), BF16),
            pltpu.VMEM(a, BF16),
            pltpu.VMEM(b, BF16),
            pltpu.VMEM(a, BF16),
            pltpu.VMEM(b, BF16),
            pltpu.VMEM((2, a_half, half), BF16),
            pltpu.VMEM((2, b_half, half), BF16),
            pltpu.VMEM((a_half, half), BF16),
            pltpu.VMEM((b_half, half), BF16),
            pltpu.VMEM((3 * a_half // 4, half), BF16),
            pltpu.VMEM((3 * b_half // 4, half), BF16),
            pltpu.VMEM(((a_half + b_half) // 4, half), BF16),
            dma((seqs, 5)),
            dma((2, units)),
            dma((2, units)),
            dma((2, units, GROUPS)),
            dma((2, heads, GROUPS)),
            dma((2,)),
            dma((2, 4)),
            dma((2, 2, 2)),
        ],
        compiler_params=pltpu.CompilerParams(
            vmem_limit_bytes=63 * 2**20, collective_id=1, has_side_effects=True
        ),
        cost_estimate=cost(120),
        name="attend_back_all",
    )(*[member for group in seqs_in for member in group], *ready)


def vector_of(vec, row, half):
    both = [vec[k, row + 1 : row + 2, :half].astype(F32) for k in range(2)]
    return jnp.concatenate(both, 1)


def start_kernel(seqs, lengths, order, tokens, wq, wk, wv, wo, wi, wu, *refs):
    sc = Counts(lengths, order)
    vectors, refs = refs[:9], refs[9:]
    q_out, kv_out, o_out, lse_out = (refs[i * seqs : (i + 1) * seqs] for i in range(4))
    refs = refs[4 * seqs :]
    back_out, vec_out, others, *dense_out = refs[:6]
    full, q_held, kv_held, vec, own_vec, tok, *refs = refs[6:]
    q_v, kv_v, o_v, lse_v, shade, qa, acc, sums, top, *sems = refs
    v_sem, wx_sem, wy_sem, wc_sem, l_sem, dx_sem, dc_sem, q_sem, z_sem, y_sem, c_sem = sems[:11]
    own_sem, b_sem = sems[11:]
    z, y, c, x = position()
    sibling, beside, over = device(z, y, 1 - c, x), device(z, 1 - y, c, x), device(z, y, c, 1 - x)
    line = [None] + [device(z ^ d, y, c, x) for d in range(1, GROUPS)]
    greet([sibling, beside, over] + line[1:])

    def pair(sem, *index):
        return sem.at[(0, *index)], sem.at[(1, *index)]

    waits = []
    half = wq.shape[0]
    eighth = half // 4

    def rows_of(which, cc, yy):
        start = which * half + (2 * cc + yy) * eighth
        return pl.ds(pl.multiple_of(start, 16), eighth)

    own_rows = pl.ds(pl.multiple_of((2 * c + y) * eighth, 16), eighth)
    tok_in = pltpu.make_async_copy(tokens, tok, l_sem.at[6])
    tok_in.start()
    flow = {}
    turns = (1, 2, 0)
    locals_of = []
    for i in turns:
        own = (wq, wk, wv)[i]
        flow["x", i] = send(
            own.at[own_rows], full.at[i, rows_of(x, c, y)], pair(wx_sem, i), over
        )
    for i in turns:
        own = (wq, wk, wv)[i]
        place = full.at[i, pl.ds(pl.multiple_of(x * half, half), half)]
        copy = pltpu.make_async_copy(own, place, l_sem.at[i])
        copy.start()
        locals_of.append(copy)
    own_vec[...] = jnp.zeros_like(own_vec)
    for i, one in enumerate(vectors):
        row = (i + 1) % len(vectors)
        own_vec[row : row + 1, : one.shape[0]] = one[...].astype(F32)[None].astype(BF16)
    vec[x] = own_vec[...]
    vec_flow = send(own_vec, vec.at[x], pair(v_sem), over)

    def after_x(i):
        flow["x", i].wait()
        got = full.at[i, rows_of(1 - x, c, y)]
        flow["y", i] = send(got, got, pair(wy_sem, i), beside)
        flow["c", i, 0] = send(got, got, pair(wc_sem, i, 0), sibling)

    def after_y(i):
        flow["y", i].wait()
        got = full.at[i, rows_of(1 - x, c, 1 - y)]
        flow["c", i, 1] = send(got, got, pair(wc_sem, i, 1), sibling)

    def after_core(i):
        flow["c", i, 0].wait()
        flow["c", i, 1].wait()

    rows, width = tok.shape[1:]
    per = width // GROUPS
    heads = per // DH
    tok_in.wait()
    flat = tok[...].reshape(seqs * rows, width)
    valid = jnp.concatenate([valid_rows(sc, s, rows) for s in range(seqs)], 0) > 0.0
    lane = lax.broadcasted_iota(jnp.int32, (8, BLK), 1)
    for piece, offset in enumerate((0, 2, 1, 3)):
        owner = lax.bitwise_xor(2 * y + c, offset)
        for g in range(GROUPS):
            for k in range(2):
                start_of = order[(4 * g + owner) * 2 + k] * BLK
                for s in range(seqs):
                    inside = lane + start_of < lengths[s]
                    cols = slice((2 * g + k) * BLK, (2 * g + k + 1) * BLK)
                    shade[s, piece, :, cols] = jnp.where(inside, 0.0, -1e30)
    after_x(1)
    after_x(2)
    after_y(1)
    after_x(0)
    dense_weights = (wo, wi, wu)
    for i, weight in enumerate(dense_weights):
        n = weight.shape[0] // 2
        part = pl.ds(pl.multiple_of(c * n, 16), n)
        flow["dx", i] = send(weight.at[part], dense_out[i].at[part], pair(dx_sem, i), over)
    after_y(2)
    vec_flow.wait()

    def bias(row):
        return vector_of(vec, row, half)

    for copy in locals_of:
        copy.wait()
    after_core(1)
    keys = jnp.where(valid, dot(flat, full[1]), 0.0).astype(BF16)
    after_y(0)
    after_core(2)
    values = jnp.where(valid, dot(flat, full[2]) + bias(1), 0.0).astype(BF16)
    for s in range(seqs):
        rs = slice(s * rows, (s + 1) * rows)
        for g in range(GROUPS):
            for h in range(heads):
                cols = slice(g * per + h * DH, g * per + (h + 1) * DH)
                kv_held[s, g, :, h * 128 : (h + 1) * 128] = jnp.concatenate(
                    [keys[rs, cols], values[rs, cols]], 1
                )

    def kv_sends(s):
        for d in range(1, GROUPS):
            flow["z", s, d] = send(
                kv_held.at[s, z ^ d], kv_v.at[s, 0, z], pair(z_sem, s, d), line[d]
            )

    def q_sends(s):
        for d in range(1, GROUPS):
            flow["q", s, d] = send(q_held.at[s, z ^ d], q_v.at[s, z], pair(q_sem, s, d), line[d])

    kv_sends(0)

    def pass_on(s, d, src):
        g = z ^ d
        flow["ky", s, d] = send(src, kv_v.at[s, 1, g], pair(y_sem, s, d), beside)
        flow["kc", s, d, 0] = send(src, kv_v.at[s, 2, g], pair(c_sem, s, d, 0), sibling)

    def pass_core(s, d):
        flow["ky", s, d].wait()
        got = kv_v.at[s, 1, z ^ d]
        flow["kc", s, d, 1] = send(got, kv_v.at[s, 3, z ^ d], pair(c_sem, s, d, 1), sibling)

    pass_on(0, 0, kv_held.at[0, z])
    after_core(0)
    queries = ((dot(flat, full[0]) + bias(0)) * (DH**-0.5 / LN2)).astype(BF16)
    for s in range(seqs):
        rs = slice(s * rows, (s + 1) * rows)
        for g in range(GROUPS):
            q_held[s, g] = queries[rs, g * per : (g + 1) * per]
    for i in range(3):
        place = full.at[i, pl.ds(pl.multiple_of((1 - x) * half, half), half)]
        copy = pltpu.make_async_copy(place, others.at[i], l_sem.at[3 + i])
        copy.start()
        waits.append(copy)
    copy = pltpu.make_async_copy(vec, vec_out, l_sem.at[7])
    copy.start()
    waits.append(copy)
    q_sends(0)
    for s in range(seqs):
        kv_v[s, 0, z] = kv_held[s, z]
        q_v[s, z] = q_held[s, z]

    def arrive(s, d):
        flow["z", s, d].wait()
        pass_on(s, d, kv_v.at[s, 0, z ^ d])

    def own_and_core(s):
        for d in range(GROUPS):
            flow["kc", s, d, 0].wait()

    def dense_core(i):
        flow["dx", i].wait()
        n = dense_weights[i].shape[0] // 2
        got = dense_out[i].at[pl.ds(pl.multiple_of(c * n, 16), n)]
        waits.append(send(got, got, pair(dc_sem, i), sibling))

    def leave(src, dst, i):
        copy = pltpu.make_async_copy(src, dst, b_sem.at[i])
        copy.start()
        waits.append(copy)

    def attend_part(s, h, pieces):
        lanes = slice(h * 128, (h + 1) * 128)
        count, tile = GROUPS * rows, 1024

        def step(j, _):
            piece = pieces[0] + j * (pieces[1] - pieces[0])
            kv = kv_v[s, piece, :, :, lanes].reshape(count, 128)
            dark = shade[s, piece, 0:1, :]
            for n in range(count // tile):
                part = slice(n * tile, (n + 1) * tile)
                scores = dot(qa[part, :], kv, NT) + dark
                high = scores[:, :128]
                for i in range(1, count // 128):
                    high = jnp.maximum(high, scores[:, i * 128 : (i + 1) * 128])
                old = top[part, :]
                new = jnp.maximum(old, jnp.max(high, 1, keepdims=True))
                fade = jnp.exp2(old - new)
                each = [
                    jnp.exp2(scores[:, i * 128 : (i + 1) * 128] - new) for i in range(count // 128)
                ]
                sums[part, :] = sums[part, :] * fade + sum(each)
                p = jnp.concatenate([one.astype(BF16) for one in each], 1)
                acc[part, :] = acc[part, :] * fade + dot(p, kv)
                top[part, :] = new
            return 0

        lax.fori_loop(0, 2, step, 0)

    def attend_begin(s, h):
        hs = slice(h * DH, (h + 1) * DH)
        mine = q_v[s, :, :, hs].reshape(GROUPS * rows, DH)
        qa[...] = jnp.concatenate([mine, jnp.zeros_like(mine)], 1)
        acc[...] = jnp.zeros_like(acc)
        sums[...] = jnp.zeros_like(sums)
        top[...] = jnp.full_like(top, -1e30)

    def attend_end(s, h):
        hs = slice(h * DH, (h + 1) * DH)
        total = jnp.sum(sums[...], 1, keepdims=True)
        logs = top[...] + jnp.log2(jnp.broadcast_to(total, top.shape))
        lse_v[s, h] = jnp.transpose(logs)[:8]
        found = (acc[:, DH:] * (1.0 / total)).astype(BF16)
        o_v[s, :, :, hs] = found.reshape(GROUPS, rows, DH)

    for d in range(1, GROUPS):
        arrive(0, d)
        if d > 1:
            pass_core(0, d - 2)
    kv_sends(1)
    pass_on(1, 0, kv_held.at[1, z])
    pass_core(0, 2)
    pass_core(0, 3)
    for d in range(1, GROUPS):
        flow["q", 0, d].wait()
    q_sends(1)
    own_and_core(0)
    slots = {
        2: (lambda: pass_core(1, 0), lambda: arrive(1, 1)),
        3: (lambda: arrive(1, 2), lambda: arrive(1, 3)),
        4: (lambda: pass_core(1, 1), lambda: dense_core(0)),
        5: (lambda: pass_core(1, 2),),
        6: (lambda: own_and_core(1), lambda: [flow["q", 1, d].wait() for d in range(1, GROUPS)]),
        7: (lambda: pass_core(1, 3),),
        8: (lambda: dense_core(1),),
        10: (lambda: dense_core(2),),
    }
    for s in range(seqs):
        for h in range(heads):
            for n, pieces in enumerate(((0, 2), (1, 3))):
                for work in slots.get(6 * s + 2 * h + n, ()):
                    work()
                if n == 0:
                    attend_begin(s, h)
                if h == 0 and n == 1:
                    for d in range(GROUPS):
                        flow["kc", s, d, 1].wait()
                attend_part(s, h, pieces)
            attend_end(s, h)
        if s == 0:
            for d in range(1, GROUPS):
                waits.append(
                    send(o_v.at[0, z ^ d], back_out.at[z], pair(own_sem, d), line[d])
                )
            leave(o_v.at[0, z], back_out.at[z], 4 * seqs)
        for i, (src, dst) in enumerate(
            ((q_v, q_out), (kv_v, kv_out), (o_v, o_out), (lse_v, lse_out))
        ):
            leave(src.at[s], dst[s], 4 * s + i)
    for copy in waits:
        copy.wait()


def start(lengths, order, tok, weights, vectors):
    seqs, rows, width = tok.shape
    per = width // GROUPS
    half = weights[0].shape[0]
    joined = (16, vectors[-1].shape[0])
    heads, total = per // DH, GROUPS * rows
    narrow = jax.ShapeDtypeStruct((GROUPS, rows, per), BF16)
    dma = pltpu.SemaphoreType.DMA
    return pl.pallas_call(
        functools.partial(start_kernel, seqs),
        out_shape=[narrow] * seqs
        + [jax.ShapeDtypeStruct((4, GROUPS, rows, 2 * per), BF16)] * seqs
        + [narrow] * seqs
        + [jax.ShapeDtypeStruct((heads, 8, total), F32)] * seqs
        + [
            narrow,
            jax.ShapeDtypeStruct((2, *joined), BF16),
            jax.ShapeDtypeStruct((3, half, width), BF16),
        ]
        + [jax.ShapeDtypeStruct(w.shape, BF16) for w in weights[3:]],
        in_specs=[SMEM] * 2 + [ANY] * 7 + [VMEM] * 9,
        out_specs=[ANY] * (4 * seqs + 6),
        scratch_shapes=[
            pltpu.VMEM((3, width, width), BF16),
            pltpu.VMEM((seqs, GROUPS, rows, per), BF16),
            pltpu.VMEM((seqs, GROUPS, rows, 2 * per), BF16),
            pltpu.VMEM((2, *joined), BF16),
            pltpu.VMEM(joined, BF16),
            pltpu.VMEM(tok.shape, BF16),
            pltpu.VMEM((seqs, GROUPS, rows, per), BF16),
            pltpu.VMEM((seqs, 4, GROUPS, rows, 2 * per), BF16),
            pltpu.VMEM((seqs, GROUPS, rows, per), BF16),
            pltpu.VMEM((seqs, heads, 8, total), F32),
            pltpu.VMEM((seqs, 4, 8, total), F32),
            pltpu.VMEM((total, 128), BF16),
            pltpu.VMEM((total, 128), F32),
            pltpu.VMEM((total, 128), F32),
            pltpu.VMEM((total, 128), F32),
            dma((2,)),
            dma((2, 3)),
            dma((2, 3)),
            dma((2, 3, 2)),
            dma((8,)),
            dma((2, 3)),
            dma((2, 3)),
            dma((2, seqs, GROUPS)),
            dma((2, seqs, GROUPS)),
            dma((2, seqs, GROUPS)),
            dma((2, seqs, GROUPS, 2)),
            dma((2, GROUPS)),
            dma((4 * seqs + 1,)),
        ],
        compiler_params=pltpu.CompilerParams(
            vmem_limit_bytes=63 * 2**20, collective_id=4, has_side_effects=True
        ),
        cost_estimate=cost(80),
        name="start",
    )(lengths, order, tok, *weights, *vectors)


def middle_stage(s, att, mask, tok, teach, vec, weights, keep, outs, first_done, outer_done):
    wo, wi, wu, slope = weights
    att_k, br_k, hl_k, il_k, act_k, ol_k = keep
    out, fg, sums, wide_sums = outs
    rows = att.shape[0]
    hidden = wi.shape[1]
    tile = 512
    rs = slice(s * rows, (s + 1) * rows)
    half = tok.shape[2] // 2
    out_bias, gain_one, shift_one, outer_bias, gain_two, shift_two = (
        vector_of(vec, row, half) for row in range(2, 8)
    )
    add = functools.partial(jnp.sum, axis=0, keepdims=True)

    def collect(target, value):
        if s == 0:
            target[...] = value
        else:
            target[...] += value

    att_k[rs, :] = att
    first_done[0]()
    first = tok[s].astype(F32) + dot(att, wo[...]) + out_bias
    normed_one, inverse_one = norm(first)
    hidden_in = normed_one * gain_one + shift_one
    hl = hidden_in.astype(BF16)
    hl_k[rs, :] = hl
    first_done[1]()
    second = hidden_in + outer_bias
    for n in range(hidden // tile):
        cols = slice(n * tile, (n + 1) * tile)
        k, begin = divmod(n * tile, hidden // 2)
        inner = dot(hl, wi[:, cols]) + vec[k, 0:1, begin : begin + tile].astype(F32)
        below, density = normal_parts(inner)
        act = (inner * below).astype(BF16)
        act_k[rs, cols] = act
        slope[:, cols] = below + inner * density
        second += dot(act, wu[cols, :])
    normed_two, inverse_two = norm(second)
    final = normed_two * gain_two + shift_two
    out[s] = final.astype(BF16)
    residue = (final - teach[s].astype(F32)) * mask
    collect(sums.at[0:1], add(residue * normed_two))
    collect(sums.at[1:2], add(residue))
    collect(sums.at[6:7], add(residue * residue))
    second_grad = norm_back(residue * gain_two, normed_two, inverse_two)
    ol = second_grad.astype(BF16)
    ol_k[rs, :] = ol
    collect(sums.at[2:3], add(ol.astype(F32)))
    outer_done()
    hidden_grad = second_grad
    for n in range(hidden // tile):
        cols = slice(n * tile, (n + 1) * tile)
        il = (dot(ol, wu[cols, :], NT) * slope[:, cols]).astype(BF16)
        il_k[rs, cols] = il
        collect(wide_sums.at[0:1, cols], add(il.astype(F32)))
        hidden_grad += dot(il, wi[:, cols], NT)
    first_grad = norm_back(hidden_grad * gain_one, normed_one, inverse_one)
    fg[s] = first_grad
    br = first_grad.astype(BF16)
    br_k[rs, :] = br
    collect(sums.at[3:4], add(hidden_grad * normed_one))
    collect(sums.at[4:5], add(hidden_grad))
    collect(sums.at[5:6], add(br.astype(F32)))
    return dot(br, wo[...], NT).astype(BF16)


def middle_kernel(seqs, lengths, order, tok, teach, vec, *refs):
    sc = Counts(lengths, order)
    attended, weights, refs = refs[:seqs], refs[seqs : seqs + 6], refs[seqs + 6 :]
    out, fg, sums, wide_sums, a_own, a_give, b_own, b_give = refs[:8]
    grads_in, refs = refs[8 : 8 + seqs], refs[8 + seqs :]
    wo, wi, wu, slope, o_in, g_out, att_k, br_k, hl_k, il_k, act_k, ol_k = refs[:12]
    own, given, w_sem, o_sem, g_sem, c_sem = refs[12:]
    z, y, c, x = position()
    sibling = device(z, y, 1 - c, x)
    line = [None] + [device(z ^ d, y, c, x) for d in range(1, GROUPS)]
    greet([sibling] + line[1:])
    coming, going = {}, {}
    for s in range(seqs):
        if s == 0:
            coming[s, 0] = pltpu.make_async_copy(attended[s], o_in.at[s], o_sem.at[0, s, 0])
            coming[s, 0].start()
            continue
        for d in range(1, GROUPS):
            sems = o_sem.at[0, s, d], o_sem.at[1, s, d]
            coming[s, d] = send(attended[s].at[z ^ d], o_in.at[s, z], sems, line[d])
        coming[s, 0] = pltpu.make_async_copy(attended[s].at[z], o_in.at[s, z], o_sem.at[0, s, 0])
        coming[s, 0].start()
    copies = [
        half_copies(full, *weights[2 * i : 2 * i + 2], w_sem, 2 * i)
        for i, full in enumerate((wo, wi, wu))
    ]
    for group in copies:
        for copy in group:
            copy.start()

    def loaded(which):
        for i in which:
            for copy in copies[i]:
                copy.wait()

    half = wo.shape[0] // 2
    blocks = wi.shape[1] // (2 * half)
    base = (1 + blocks) * half
    core = []

    def store(k, start, value):
        low_value = value.astype(BF16)
        own[0, k, start : start + half, :] = low_value[:, :half]
        own[1, k, start : start + half, :] = low_value[:, half:]

    def pass_core(k, start, stop):
        place = pl.ds(start, stop - start)
        i = len(core)
        sems = c_sem.at[0, i], c_sem.at[1, i]
        core.append(send(own.at[1 - c, k, place], given.at[k, place], sems, sibling))

    def outer_grads():
        for k in range(2):
            for t in range(blocks):
                rows_of = slice((k * blocks + t) * half, (k * blocks + t + 1) * half)
                store(k, base + t * half, dot(act_k[:, rows_of], ol_k[...], TN))
            pass_core(k, base, base + blocks * half)

    rows = tok.shape[1]
    per = o_in.shape[3]
    for s in range(seqs):
        for d in range(GROUPS if s > 0 else 1):
            coming[s, d].wait()
        att = jnp.concatenate([o_in[s, g] for g in range(GROUPS)], 1)
        mask = valid_rows(sc, s, rows)
        waits = (lambda: loaded([0]), lambda: loaded([1, 2])) if s == 0 else (lambda: None,) * 2
        found = middle_stage(
            s,
            att,
            mask,
            tok,
            teach,
            vec,
            (wo, wi, wu, slope),
            (att_k, br_k, hl_k, il_k, act_k, ol_k),
            (out, fg, sums, wide_sums),
            waits,
            outer_grads if s == seqs - 1 else lambda: None,
        )
        for g in range(GROUPS):
            g_out[s, g] = found[:, g * per : (g + 1) * per]
        for d in range(1, GROUPS):
            sems = g_sem.at[0, s, d], g_sem.at[1, s, d]
            going[s, d] = send(g_out.at[s, z ^ d], grads_in[s].at[z], sems, line[d])
        going[s, 0] = pltpu.make_async_copy(g_out.at[s, z], grads_in[s].at[z], g_sem.at[0, s, 0])
        going[s, 0].start()
    sums[7:8, :] = jnp.zeros((1, sums.shape[1]), F32)

    for k in range(2):
        ks = slice(k * half, (k + 1) * half)
        store(k, 0, dot(att_k[:, ks], br_k[...], TN))
        for t in range(blocks):
            cols = slice(2 * t * half, 2 * (t + 1) * half)
            store(k, (1 + t) * half, dot(hl_k[:, ks], il_k[:, cols], TN))
        pass_core(k, 0, base)
    for copy in core:
        copy.wait()
    mine = own.at[c]
    cut, b_half = a_own.shape[0], b_own.shape[1]
    a_own[...] = add_low(mine[x, 0:cut], given[x, 0:cut])
    a_give[...] = add_low(mine[1 - x, 0:cut], given[1 - x, 0:cut])
    for k in range(2):
        for target, which in ((b_own, y), (b_give, 1 - y)):
            part = pl.ds(pl.multiple_of(cut + which * b_half, 16), b_half)
            target[k] = add_low(mine[k, part], given[k, part])
    for copy in going.values():
        copy.wait()


def cut_of(total):
    return total // 256 * 128


def middle(lengths, order, tok, teach, vec, attended, weights):
    seqs, rows, width = tok.shape
    hidden = 2 * vec.shape[2]
    half = width // 2
    total = half + hidden
    cut = cut_of(total)
    dma = pltpu.SemaphoreType.DMA
    narrow, wide = (seqs * rows, width), (seqs * rows, hidden)
    b_shape = jax.ShapeDtypeStruct((2, (total - cut) // 2, half), BF16)
    a_shape = jax.ShapeDtypeStruct((cut, half), BF16)
    groups, _, per = attended[0].shape
    return pl.pallas_call(
        functools.partial(middle_kernel, seqs),
        out_shape=[
            jax.ShapeDtypeStruct(tok.shape, BF16),
            jax.ShapeDtypeStruct(tok.shape, F32),
            jax.ShapeDtypeStruct((8, width), F32),
            jax.ShapeDtypeStruct((1, hidden), F32),
            a_shape,
            a_shape,
            b_shape,
            b_shape,
        ]
        + [jax.ShapeDtypeStruct(a.shape, BF16) for a in attended],
        in_specs=[SMEM] * 2 + [VMEM] * 3 + [ANY] * (seqs + 6),
        out_specs=[VMEM] * 8 + [ANY] * seqs,
        scratch_shapes=[
            pltpu.VMEM((width, width), BF16),
            pltpu.VMEM((width, hidden), BF16),
            pltpu.VMEM((hidden, width), BF16),
            pltpu.VMEM((rows, hidden), F32),
            pltpu.VMEM((seqs, groups, rows, per), BF16),
            pltpu.VMEM((seqs, groups, rows, per), BF16),
            pltpu.VMEM(narrow, BF16),
            pltpu.VMEM(narrow, BF16),
            pltpu.VMEM(narrow, BF16),
            pltpu.VMEM(wide, BF16),
            pltpu.VMEM(wide, BF16),
            pltpu.VMEM(narrow, BF16),
            pltpu.VMEM((2, 2, total, half), BF16),
            pltpu.VMEM((2, total, half), BF16),
            dma((6,)),
            dma((2, seqs, groups)),
            dma((2, seqs, groups)),
            dma((2, 4)),
        ],
        compiler_params=pltpu.CompilerParams(
            vmem_limit_bytes=63 * 2**20, collective_id=3, has_side_effects=True
        ),
        cost_estimate=cost(60),
        name="middle",
    )(lengths, order, tok, teach, vec, *attended, *weights)


def finish_kernel(
    seqs, lengths, order, tok, fg, rq, rkv, dense_sums, wide_sums, ready, wq, wk, wv, others, *rest
):
    sc = Counts(lengths, order)
    tg, out, dense_out, small_out, *rest = rest
    full, grads, acc, from_core, from_x, from_y, from_z, res, vec, vec_in, dense_res = rest[:11]
    w_sems, sems, small_sems, d_sems, last_sem = rest[11:]
    z, y, c, x = position()
    sibling, beside, over = device(z, y, 1 - c, x), device(z, 1 - y, c, x), device(z, y, c, 1 - x)
    line = [None] + [device(z ^ d, y, c, x) for d in range(1, GROUPS)]
    greet([sibling, beside, over] + line[1:])

    a_half = cut_of(dense_res.shape[1]) // 2
    b_half = dense_res.shape[1] // 2 - a_half
    low_bit, high_bit = lax.rem(z, 2), z // 2
    dense_parts = ((0, a_half, y * a_half), (a_half // 4, b_half, 2 * a_half + y * b_half))

    def dense_rows(start, n):
        return dense_res.at[c, pl.ds(pl.multiple_of(start, 16), n)]

    def d_pair(k, i):
        return d_sems.at[0, k, i], d_sems.at[1, k, i]

    dense_flows = [None, None]

    def dense_step(i, k):
        start, n, base = dense_parts[i]
        if k > 0:
            dense_flows[i].wait()
        begin = base + (low_bit * (n // 2) if k < 2 else 0) + (high_bit * (n // 4) if k < 1 else 0)
        size = (n // 4, n // 2, n, 2 * n)[k]
        place = dense_rows(begin if k < 3 else 2 * a_half * i, size)
        if k == 0:
            place[...] = ready[start : start + size]
        to = (line[2], line[1], beside, sibling)[k]
        dense_flows[i] = send(place, place, d_pair(k, i), to)

    dense_step(0, 0)
    rows, width = tok.shape[1:]
    heads = width // GROUPS // DH
    copies = []
    for i, own in enumerate((wq, wk, wv)):
        copies += half_copies(full.at[i], own, others.at[i], w_sems, 2 * i)
    for copy in copies:
        copy.start()

    def head(i, s, g, h):
        if i == 0:
            return rq[h, g, :, s * DH : (s + 1) * DH]
        return rkv[h * seqs + s, g, :, (i - 1) * DH : i * DH]

    def whole(i):
        each = [
            jnp.concatenate([head(i, s, g, h) for g in range(GROUPS) for h in range(heads)], 1)
            for s in range(seqs)
        ]
        return jnp.concatenate(each, 0)

    valid = jnp.concatenate([valid_rows(sc, s, rows) for s in range(seqs)], 0) > 0.0
    parted = [whole(0)] + [jnp.where(valid, whole(i), jnp.zeros((), BF16)) for i in (1, 2)]
    flat = tok[...].reshape(seqs * rows, width)
    wide = width // 2
    for i, grad in enumerate(parted):
        found = dot(flat, grad, TN).astype(BF16)
        for n in range(2):
            for t in range(width // 128):
                grads[t % 3, t // 3, n, i * wide : (i + 1) * wide, :] = found[
                    n * wide : (n + 1) * wide, t * 128 : (t + 1) * 128
                ]
    lines_of = [dense_sums[i : i + 1, :] for i in range(7)]
    lines_of += [jnp.sum(grad.astype(F32), 0, keepdims=True) for grad in (parted[0], parted[2])]
    lines_of.append(wide_sums[...])
    row = 0
    for one in lines_of:
        for t in range(one.shape[1] // 128):
            vec[row : row + 1, :] = one[:, t * 128 : (t + 1) * 128]
            row += 1
    valid_count = sum(jnp.clip(sc[i], 0, BLK) for i in range(2 * seqs))
    vec[row:, :] = jnp.full((vec.shape[0] - row, 128), valid_count.astype(F32))

    parts, rows_each = grads.shape[0], grads.shape[3]
    half, piece = rows_each // 2, rows_each // 8
    own_half = pl.ds(pl.multiple_of(y * half, half), half)
    other_half = pl.ds(pl.multiple_of((1 - y) * half, half), half)

    def piece_of(g):
        return pl.ds(pl.multiple_of(y * half + g * piece, piece), piece)

    def pair(k, p):
        return sems.at[0, k, p], sems.at[1, k, p]

    def small_pair(k):
        return small_sems.at[0, k], small_sems.at[1, k]

    core = [
        send(grads.at[p, 1 - c], from_core.at[p], pair(0, p), sibling) for p in range(parts)
    ]
    short = send(vec, vec_in.at[0], small_pair(0), sibling)
    flows, lines, spread = {}, {}, {}

    def from_pair(p):
        core[p].wait()
        acc[p] = add_low(grads[p, c], from_core[p])

    def x_send(p):
        if p == 1:
            flows[p] = send(acc.at[p, 1 - x, own_half], from_x.at[p, own_half], pair(2, p), over)
        else:
            flows[p] = send(acc.at[p, 1 - x], from_x.at[p], pair(1, p), over)

    def x_add(p):
        flows[p].wait()
        if p == 1:
            acc[p, x, own_half] = add_low(acc[p, x, own_half], from_x[p, own_half])
        else:
            acc[p, x] = add_low(acc[p, x], from_x[p])

    def y_send(p):
        if p == 1:
            flows[p] = send(acc.at[p, :, other_half], from_y.at[p], pair(1, p), beside)
        else:
            flows[p] = send(acc.at[p, x, other_half], from_y.at[p, 0], pair(2, p), beside)

    def y_add(p):
        flows[p].wait()
        if p == 1:
            for k in range(2):
                acc[p, k, own_half] = add_low(acc[p, k, own_half], from_y[p, k])
        else:
            acc[p, x, own_half] = add_low(acc[p, x, own_half], from_y[p, 0])

    def z_send(p):
        for d in range(1, GROUPS):
            lines[p, d] = send(
                acc.at[p, x, piece_of(z ^ d)], from_z.at[p, d], pair(2 + d, p), line[d]
            )

    def z_add(p):
        total = acc[p, x, piece_of(z)].astype(F32)
        for d in range(1, GROUPS):
            lines[p, d].wait()
            total += from_z[p, d].astype(F32)
        place = res.at[c, p, piece_of(z)]
        place[...] = total.astype(BF16)
        for d in range(1, GROUPS):
            spread[p, d] = send(place, place, pair(5 + d, p), line[d])

    def y_gather(p):
        for d in range(1, GROUPS):
            spread[p, d].wait()
        place = res.at[c, p, own_half]
        flows[p] = send(place, place, pair(9, p), beside)

    def core_gather(p):
        flows[p].wait()
        flows[p] = send(res.at[c, p], res.at[c, p], pair(10, p), sibling)

    from_pair(0)
    x_send(0)
    from_pair(1)
    y_send(1)
    from_pair(2)
    short.wait()
    vec_in[8] = vec[...] + vec_in[0]
    short = send(vec_in.at[8], vec_in.at[1], small_pair(1), over)
    dense_step(0, 1)
    dense_step(1, 0)
    for copy in copies:
        copy.wait()
    total = jnp.concatenate([fg[s] for s in range(seqs)], 0)
    for i, grad in enumerate(parted):
        total += dot(grad, full[i], NT)
    tg[...] = total.reshape(seqs, rows, width)
    x_add(0)
    x_send(2)
    y_send(0)
    y_add(1)
    x_send(1)
    short.wait()
    vec[...] = vec_in[8] + vec_in[1]
    short = send(vec, vec_in.at[2], small_pair(2), beside)
    y_add(0)
    z_send(0)
    dense_step(0, 2)
    dense_step(1, 1)
    x_add(2)
    y_send(2)
    x_add(1)
    z_send(1)
    z_add(0)
    short.wait()
    vec[...] = vec[...] + vec_in[2]
    vec_in[4 + z] = vec[...]
    shorts = [
        send(vec, vec_in.at[4 + z], small_pair(2 + d), line[d]) for d in range(1, GROUPS)
    ]
    y_add(2)
    z_send(2)
    dense_step(1, 2)
    z_add(1)
    y_gather(0)
    z_add(2)
    dense_step(0, 3)
    y_gather(1)
    y_gather(2)
    for copy in shorts:
        copy.wait()
    small_out[...] = vec_in[4] + vec_in[5] + (vec_in[6] + vec_in[7])
    for p in range(parts):
        core_gather(p)
    dense_step(1, 3)
    for copy in dense_flows:
        copy.wait()
    done = [pltpu.make_async_copy(dense_res, dense_out, last_sem.at[1])]
    done[0].start()
    for p in (1, 0, 2):
        flows[p].wait()
    done.append(pltpu.make_async_copy(res, out, last_sem.at[0]))
    done[1].start()
    for copy in done:
        copy.wait()


def finish(lengths, order, tok, fg, rq, rkv, sums, wide_sums, ready, wq, wk, wv, others):
    seqs, _, width = tok.shape
    short = (-(-(9 * width + wide_sums.shape[1] + 128) // 1024) * 8, 128)
    parts, rows, lanes = 3, 3 * (width // 2), 128
    total, half = 8 * ready.shape[0], ready.shape[1]
    dma = pltpu.SemaphoreType.DMA
    return pl.pallas_call(
        functools.partial(finish_kernel, seqs),
        out_shape=[
            jax.ShapeDtypeStruct(tok.shape, F32),
            jax.ShapeDtypeStruct((2, parts, rows, lanes), BF16),
            jax.ShapeDtypeStruct((2, total, half), BF16),
            jax.ShapeDtypeStruct(short, F32),
        ],
        in_specs=[SMEM] * 2 + [VMEM] * 7 + [ANY] * 4,
        out_specs=[VMEM, ANY, ANY, VMEM],
        scratch_shapes=[
            pltpu.VMEM((3, width, width), BF16),
            pltpu.VMEM((parts, 2, 2, rows, lanes), BF16),
            pltpu.VMEM((parts, 2, rows, lanes), BF16),
            pltpu.VMEM((parts, 2, rows, lanes), BF16),
            pltpu.VMEM((parts, rows, lanes), BF16),
            pltpu.VMEM((parts, 2, rows // 2, lanes), BF16),
            pltpu.VMEM((parts, GROUPS, rows // 8, lanes), BF16),
            pltpu.VMEM((2, parts, rows, lanes), BF16),
            pltpu.VMEM(short, F32),
            pltpu.VMEM((9, *short), F32),
            pltpu.VMEM((2, total, half), BF16),
            dma((6,)),
            dma((2, 11, parts)),
            dma((2, 6)),
            dma((2, 4, 2)),
            dma((2,)),
        ],
        compiler_params=pltpu.CompilerParams(
            vmem_limit_bytes=63 * 2**20, collective_id=2, has_side_effects=True
        ),
        cost_estimate=cost(70),
        name="finish",
    )(lengths, order, tok, fg, rq, rkv, sums, wide_sums, ready, wq, wk, wv, others)


def unpack_kernel(qkv, total, small, *refs):
    outs, rows, loss, refs = refs[:6], refs[6:15], refs[15], refs[16:]
    narrow, inner, outer, sems = refs
    half = qkv.shape[2] // 3
    blocks = inner.shape[1] // (2 * half)
    copies = []

    def leave(src, i):
        copy = pltpu.make_async_copy(src, outs[i], sems.at[i])
        copy.start()
        copies.append(copy)

    for k in range(2):
        cols = slice(k * half, (k + 1) * half)
        outer[:, cols] = total[k, (1 + blocks) * half :].astype(F32)
    leave(outer, 5)
    for k in range(2):
        for t in range(blocks):
            cols = slice((2 * t + k) * half, (2 * t + k + 1) * half)
            inner[:, cols] = total[k, (1 + t) * half : (2 + t) * half].astype(F32)
    leave(inner, 4)
    for i in range(3):
        for k in range(2):
            for p in range(3):
                cols = slice((3 * k + p) * 128, (3 * k + p + 1) * 128)
                narrow[i, :, cols] = qkv[k, p, i * half : (i + 1) * half].astype(F32)
        leave(narrow.at[i], i)
    for k in range(2):
        narrow[3, :, k * half : (k + 1) * half] = total[k, 0:half].astype(F32)
    leave(narrow.at[3], 3)
    x = lax.axis_index("wa")
    tiles = 2 * half // 128
    starts = [tiles * i for i in (0, 1, 2, 3, 4, 5, 7, 8)] + [9 * tiles]
    for one, begin in zip(rows, starts):
        n = one.shape[0] // 128
        for t in range(n):
            one[t * 128 : (t + 1) * 128] = small[pl.ds(begin + x * n + t, 1), :][0]
    end = 9 * tiles + 2 * rows[8].shape[0] // 128
    squares = jnp.sum(small[6 * tiles : 7 * tiles, :], keepdims=True)
    loss[...] = squares / (small[end : end + 1, :1] * (2.0 * half))
    for copy in copies:
        copy.wait()


def unpack(qkv, total, small, hidden):
    half = total.shape[2]
    narrow = jax.ShapeDtypeStruct((half, 2 * half), F32)
    return pl.pallas_call(
        unpack_kernel,
        out_shape=[narrow] * 4
        + [
            jax.ShapeDtypeStruct((half, hidden), F32),
            jax.ShapeDtypeStruct((hidden // 2, 2 * half), F32),
        ]
        + [jax.ShapeDtypeStruct((half,), F32)] * 8
        + [jax.ShapeDtypeStruct((hidden // 2,), F32), jax.ShapeDtypeStruct((1, 1), F32)],
        in_specs=[VMEM] * 3,
        out_specs=[ANY] * 6 + [VMEM] * 10,
        scratch_shapes=[
            pltpu.VMEM((4, half, 2 * half), F32),
            pltpu.VMEM((half, hidden), F32),
            pltpu.VMEM((hidden // 2, 2 * half), F32),
            pltpu.SemaphoreType.DMA((6,)),
        ],
        compiler_params=ROOM,
        cost_estimate=cost(10),
        name="unpack",
    )(qkv, total, small)


def pick(table, index):
    places = jnp.arange(table.shape[0], dtype=jnp.int32)
    return jnp.sum(jnp.where(index[..., None] == places, table, 0), -1)


def shards(
    size,
    tokens,
    teacher,
    lengths,
    block_order,
    query_weight,
    query_bias,
    key_weight,
    value_weight,
    value_bias,
    out_weight,
    out_bias,
    gain_one,
    shift_one,
    inner_weight,
    inner_bias,
    outer_weight,
    outer_bias,
    gain_two,
    shift_two,
):
    seqs, rows, width = tokens.shape
    per_plane = size // GROUPS
    blocks_each = rows // BLK
    ctx, x = lax.axis_index("ctx"), lax.axis_index("wa")
    c, place = lax.rem(ctx, 2), lax.rem(ctx, per_plane)
    masks = [1 << b for b in reversed(range(per_plane.bit_length() - 1))]
    offsets = [0]
    for m in masks:
        offsets += [o ^ m for o in offsets]

    def across(value):
        return lax.ppermute(value, "wa", [(0, 1), (1, 0)])

    def flip(value, m):
        return lax.ppermute(value, "ctx", [(i, i ^ m) for i in range(size)])

    lines = [[g * per_plane + r for g in range(GROUPS)] for r in range(per_plane)]

    def turn(value):
        return lax.all_to_all(value, "ctx", 0, 0, axis_index_groups=lines)

    cores = [[i for i in range(size) if i % 2 == k] for k in range(2)]

    def paired(mine):
        sibling = flip(mine, 1)
        return jnp.where(c == 0, jnp.stack([mine, sibling]), jnp.stack([sibling, mine]))

    def reduced(grad):
        four = grad.reshape(2, 2, *grad.shape[1:])
        keep = lax.dynamic_index_in_dim(four, c, 1, False)
        give = lax.dynamic_index_in_dim(four, 1 - c, 1, False)
        keep = add_low(keep, flip(give, 1))
        mine = lax.dynamic_index_in_dim(keep, x, 0, False)
        mine = add_low(mine, across(lax.dynamic_index_in_dim(keep, 1 - x, 0, False)))
        return paired(lax.psum(mine, "ctx", axis_index_groups=cores))

    def reduced_dense(grad):
        four = grad.reshape(2, 2, *grad.shape[1:])
        keep = lax.dynamic_index_in_dim(four, c, 1, False)
        give = lax.dynamic_index_in_dim(four, 1 - c, 1, False)
        keep = add_low(keep, flip(give, 1))
        mine = lax.psum_scatter(
            keep.reshape(-1, keep.shape[-1]), "wa", scatter_dimension=0, tiled=True
        )
        return lax.psum(mine, "ctx", axis_index_groups=cores)

    vectors = (
        query_bias,
        value_bias,
        out_bias,
        gain_one,
        shift_one,
        outer_bias,
        gain_two,
        shift_two,
        inner_bias,
    )
    half, hidden = width // 2, 2 * inner_bias.shape[0]
    fused = per_plane == 4

    if fused:
        found = start(
            lengths,
            block_order,
            tokens,
            (query_weight, key_weight, value_weight, out_weight, inner_weight, outer_weight),
            vectors,
        )
        queries = [q.reshape(-1, BLK, q.shape[2]) for q in found[:seqs]]
        pieces = [[kv.reshape(-1, BLK, kv.shape[3])] for kv in found[seqs : 2 * seqs]]
        attended, lses = found[2 * seqs : 3 * seqs], found[3 * seqs : 4 * seqs]
        first_back, pair, others, *rest = found[4 * seqs :]
        dense_weights = [out_weight, rest[0], inner_weight, rest[1], outer_weight, rest[2]]
    else:
        count = block_order.shape[0]
        ids = jnp.arange(count, dtype=jnp.int32)
        owner = ids // blocks_each
        index_of = jnp.array([offsets.index(o) for o in range(per_plane)], jnp.int32)
        piece_of = pick(index_of, (owner % per_plane) ^ place)
        spot = (piece_of * GROUPS + owner // per_plane) * blocks_each + ids % blocks_each
        key_order = jnp.sum(jnp.where(block_order[None, :] == ids[:, None], spot[None, :], 0), 1)
        near = jnp.arange(GROUPS * blocks_each, dtype=jnp.int32)
        near_ids = (near // blocks_each * per_plane + place) * blocks_each + near % blocks_each
        near_pos = pick(block_order, near_ids)
        rank = jnp.sum((near_pos[None, :] < near_pos[:, None]).astype(jnp.int32), 1)
        query_order = jnp.sum(jnp.where(rank[None, :] == near[:, None], near[None, :], 0), 1)
        own_pos = pick(block_order, ctx * blocks_each + jnp.arange(blocks_each, dtype=jnp.int32))
        scalars, row_counts = [], []
        for s in range(seqs):
            used = jnp.sum((near_pos * BLK < lengths[s]).astype(jnp.int32))
            head = jnp.concatenate([lengths[s][None], used[None], jnp.zeros((6,), jnp.int32)])
            scalars.append(jnp.concatenate([head, query_order, key_order]))
            row_counts.append(jnp.clip(lengths[s] - own_pos * BLK, 0, BLK))

        counts = jnp.concatenate(row_counts)
        own_vec = jnp.concatenate(vectors)[None]
        other_vec = across(own_vec)
        pair = jnp.where(
            x == 0, jnp.stack([own_vec, other_vec]), jnp.stack([other_vec, own_vec])
        ).astype(F32)
        narrow = pair[:, 0, : 8 * half].reshape(2, 8, half).swapaxes(0, 1).reshape(8, width)
        wide_vec = pair[:, 0, 8 * half :].reshape(1, -1)

        def quarter(weight):
            n = weight.shape[0] // 2
            return lax.dynamic_slice_in_dim(weight, c * n, n, 0)

        first_qkv = across(
            jnp.concatenate([quarter(w) for w in (query_weight, key_weight, value_weight)], 0)
        )
        second_qkv = flip(first_qkv, 1)
        dense_weights = []
        last = first_qkv
        for weight in (out_weight, inner_weight, outer_weight):
            piece, last = lax.optimization_barrier((quarter(weight), last))
            last = across(piece)
            dense_weights += [weight, last, flip(last, 1)]

        projected = project(
            counts, tokens, narrow, query_weight, key_weight, value_weight, first_qkv, second_qkv
        )
        queries, pieces = [], []
        for s in range(seqs):
            kv = turn(projected[2 * s + 1])
            queries.append(turn(projected[2 * s]).reshape(-1, BLK, width // GROUPS))
            held = [kv.reshape(-1, BLK, kv.shape[2])]
            for m in masks:
                held += [flip(piece, m) for piece in held]
            pieces.append(held)

        attended, lses = [], []
        for s in range(seqs):
            o, lse = attend(s, per_plane, lengths, block_order, queries[s], pieces[s])
            attended.append(o.reshape(queries[s].shape))
            lses.append(lse)
    if fused:
        fours = [first_back, *attended[1:]]
        found = middle(lengths, block_order, tokens, teacher, pair, fours, dense_weights)
        output, firsts, sums, wide_sums, a_own, a_give, b_own, b_give = found[:8]
        heads_grad = [g.reshape(queries[0].shape) for g in found[8:]]
        ready = (a_own, a_give, b_own, b_give)
    else:
        dense_out = []
        for s in range(seqs):
            o4 = turn(attended[s].reshape(GROUPS, rows, -1))
            dense_out.append(
                dense(
                    row_counts[s], o4, tokens[s], teacher[s], narrow[2:], wide_vec, dense_weights
                )
            )
        output = jnp.stack([d[0] for d in dense_out])
        first_grads = [d[1] for d in dense_out]
        heads_grad = [turn(d[2]).reshape(queries[s].shape) for s, d in enumerate(dense_out)]
        sums = sum(d[9] for d in dense_out)
        wide_sums = sum(d[10] for d in dense_out)
        dense_sums = [reduced_dense(g) for g in dense_grads([d[3:9] for d in dense_out])]

    if fused:
        flat_rows = (GROUPS * rows, width // GROUPS)
        rq, rkv, ready = attend_back_all(
            [
                [
                    *(a.reshape(flat_rows) for a in (queries[s], heads_grad[s], attended[s])),
                    lses[s],
                    pieces[s][0].reshape(-1, pieces[s][0].shape[2]),
                ]
                for s in range(seqs)
            ],
            ready,
        )
    else:
        dqs, dkvs = [], []
        for s in range(seqs):
            found = attend_back(
                scalars[s], queries[s], heads_grad[s], attended[s], lses[s], pieces[s]
            )
            dqs.append(turn(found[0].reshape(GROUPS, rows, -1)))
            held = [piece.reshape(GROUPS, rows, -1) for piece in found[1:]]
            for m in reversed(masks):
                n = len(held) // 2
                held = [add_low(mine, flip(theirs, m)) for mine, theirs in zip(held[:n], held[n:])]
            dkvs.append(turn(held[0]))
        tokens_grad, g_qkv, sums_qkv = project_grads(
            counts,
            tokens,
            first_grads,
            dqs + dkvs,
            query_weight,
            key_weight,
            value_weight,
            first_qkv,
            second_qkv,
        )

    if fused:
        tokens_grad, qkv, total, small = finish(
            lengths,
            block_order,
            tokens,
            firsts,
            rq,
            rkv,
            sums,
            wide_sums,
            ready,
            query_weight,
            key_weight,
            value_weight,
            others,
        )
        grads = unpack(qkv, total, small, hidden)
        query_grad, key_grad, value_grad, out_grad, inner_grad, outer_grad = grads[:6]
        rows_of = dict(zip((0, 1, 2, 3, 4, 5, 7, 8, 9), grads[6:15]))
        loss = grads[15].reshape(())

        def vector(start, length):
            return rows_of[start // width]

    else:
        valid = jnp.full((128,), sum(jnp.sum(r) for r in row_counts).astype(F32))
        small = jnp.concatenate(
            [sums[:7].reshape(-1), sums_qkv[:2].reshape(-1), wide_sums[0], valid]
        )
        small = lax.psum(small, ("ctx", "wa"))
        qkv = reduced(jnp.moveaxis(g_qkv, (2, 1), (0, 1)).reshape(4, 3, -1, 128))
        out_grad, inner_grad, outer_grad = (
            paired(g).reshape(-1, g.shape[-1]).astype(F32) for g in dense_sums
        )
        qkv = qkv.reshape(6, 3, half, 128).astype(F32)
        query_grad, key_grad, value_grad = (
            qkv[:, i].swapaxes(0, 1).reshape(half, width) for i in range(3)
        )

        def vector(start, length):
            return lax.dynamic_slice_in_dim(small, start + x * (length // 2), length // 2, 0)

        loss = jnp.sum(small[6 * width : 7 * width]) / (small[9 * width + hidden] * width)

    end = 9 * width
    return (
        output,
        tokens_grad,
        query_grad,
        vector(7 * width, width),
        key_grad,
        value_grad,
        vector(8 * width, width),
        out_grad,
        vector(5 * width, width),
        vector(3 * width, width),
        vector(4 * width, width),
        inner_grad,
        vector(end, hidden),
        outer_grad,
        vector(2 * width, width),
        vector(0, width),
        vector(width, width),
        loss,
    )


def solution(mesh):
    row, split, both = P("wa"), P("wa", None), P("wa", "ctx", None)
    placed = (both, both, row, P(), split, row, split, split, row, split, row, row, row)
    placed += (split, row, split, row, row, row)
    return jax.shard_map(
        functools.partial(shards, mesh.shape["ctx"]),
        mesh=mesh,
        in_specs=placed,
        out_specs=(
            both,
            both,
            split,
            row,
            split,
            split,
            row,
            split,
            row,
            row,
            row,
            split,
            row,
            split,
            row,
            row,
            row,
            P(),
        ),
        check_vma=False,
    )
```

```python
import functools
import math

import jax
import jax.numpy as jnp
from jax import lax
from jax.experimental import pallas as pl
from jax.experimental.pallas import tpu as pltpu
from jax.sharding import PartitionSpec as P

DH = 64
BLK = 128
GROUPS = 4
LN2 = math.log(2.0)
NT = (((1,), (1,)), ((), ()))
NN = (((1,), (0,)), ((), ()))
TN = (((0,), (0,)), ((), ()))
F32 = jnp.float32
BF16 = jnp.bfloat16
VMEM = pl.BlockSpec(memory_space=pltpu.VMEM)
SMEM = pl.BlockSpec(memory_space=pltpu.SMEM)
ANY = pl.BlockSpec(memory_space=pl.ANY)
ROOM = pltpu.CompilerParams(vmem_limit_bytes=62 * 2**20)


def dot(left, right, dims=NN):
    return lax.dot_general(left, right, dims, preferred_element_type=F32)


def cost(us):
    return pl.CostEstimate(flops=int(us * 1.15e9), bytes_accessed=1 << 20, transcendentals=0)


def weight_copies(full, own, first, second, sems, base):
    x, c = lax.axis_index("wa"), lax.rem(lax.axis_index("ctx"), 2)
    half = own.shape[0]
    quarter = half // 2
    other = (1 - x) * half
    places = (
        (own, x * half, half),
        (first, other + c * quarter, quarter),
        (second, other + (1 - c) * quarter, quarter),
    )
    return [
        pltpu.make_async_copy(
            src, full.at[pl.ds(pl.multiple_of(start, quarter), size)], sems.at[base + i]
        )
        for i, (src, start, size) in enumerate(places)
    ]


class Counts:
    def __init__(self, lengths, order):
        self.lengths, self.order = lengths, order

    def __getitem__(self, i):
        place = 2 * lax.axis_index("ctx") + i % 2
        return self.lengths[i // 2] - self.order[place] * BLK


def valid_rows(sc, s, rows):
    row = lax.broadcasted_iota(jnp.int32, (rows, 1), 0)
    first = jnp.where(row < sc[2 * s], 1.0, 0.0)
    later = jnp.where(row - BLK < sc[2 * s + 1], 1.0, 0.0)
    return jnp.where(row < BLK, first, later)


def half_copies(full, own, other, sems, base):
    x, half = lax.axis_index("wa"), own.shape[0]
    return [
        pltpu.make_async_copy(
            src, full.at[pl.ds(pl.multiple_of(k * half, half), half)], sems.at[base + i]
        )
        for i, (src, k) in enumerate(((own, x), (other, 1 - x)))
    ]


def project_kernel(sc, tok, vec, wq, wk, wv, first, second, *rest):
    seqs, rows, width = tok.shape
    outs, (full, sems) = rest[: 2 * seqs], rest[2 * seqs :]
    quarter = wq.shape[0] // 2
    copies = []
    for i, own in enumerate((wq, wk, wv)):
        part = pl.ds(i * quarter, quarter)
        copies.append(
            weight_copies(full.at[i], own, first.at[part], second.at[part], sems, 3 * i)
        )
    for group in copies:
        for copy in group:
            copy.start()
    flat = tok[...].reshape(seqs * rows, width)
    per = width // GROUPS
    heads = per // DH
    valid = jnp.concatenate([valid_rows(sc, s, rows) for s in range(seqs)], 0) > 0.0
    for copy in copies[1]:
        copy.wait()
    keys = jnp.where(valid, dot(flat, full[1]), 0.0).astype(BF16)
    for copy in copies[2]:
        copy.wait()
    values = jnp.where(valid, dot(flat, full[2]) + vec[1:2, :], 0.0).astype(BF16)
    for s in range(seqs):
        rs = slice(s * rows, (s + 1) * rows)
        for g in range(GROUPS):
            for h in range(heads):
                cols = slice(g * per + h * DH, g * per + (h + 1) * DH)
                outs[2 * s + 1][g, :, h * 128 : (h + 1) * 128] = jnp.concatenate(
                    [keys[rs, cols], values[rs, cols]], 1
                )
    for copy in copies[0]:
        copy.wait()
    queries = ((dot(flat, full[0]) + vec[0:1, :]) * (DH**-0.5 / LN2)).astype(BF16)
    for s in range(seqs):
        rs = slice(s * rows, (s + 1) * rows)
        for g in range(GROUPS):
            outs[2 * s][g] = queries[rs, g * per : (g + 1) * per]


def project(sc, tok, vec, wq, wk, wv, first, second):
    seqs, rows, width = tok.shape
    per = width // GROUPS
    shapes = [
        jax.ShapeDtypeStruct((GROUPS, rows, n), BF16) for _ in range(seqs) for n in (per, 2 * per)
    ]
    return pl.pallas_call(
        project_kernel,
        out_shape=shapes,
        in_specs=[SMEM, VMEM, VMEM] + [ANY] * 5,
        out_specs=[VMEM] * len(shapes),
        scratch_shapes=[pltpu.VMEM((3, width, width), BF16), pltpu.SemaphoreType.DMA((9,))],
        compiler_params=ROOM,
        cost_estimate=cost(5),
        name="project",
    )(sc, tok, vec, wq, wk, wv, first, second)


def load_pieces(pieces, kv, sems):
    per = pieces[0].shape[0]
    copies = [
        pltpu.make_async_copy(piece, kv.at[pl.ds(i * per, per)], sems.at[i])
        for i, piece in enumerate(pieces)
    ]
    for copy in copies:
        copy.start()
    for copy in copies:
        copy.wait()


def forward_kernel(wide, narrow, count, s, per_plane, lengths, order, q_ref, *rest):
    pieces, rest = rest[:count], rest[count:]
    o_ref, lse_ref, kv_ref, qa, acc, sums, spots, sems = rest
    blocks = q_ref.shape[0]
    heads = q_ref.shape[2] // DH
    rows = blocks * BLK
    length = lengths[s]
    place = lax.rem(lax.axis_index("ctx"), per_plane)

    def put(b, _):
        owner = b // 2
        offset = lax.bitwise_xor(lax.rem(owner, per_plane), place)
        piece = 0
        for bit in range(per_plane.bit_length() - 1):
            piece = 2 * piece + lax.rem(lax.div(offset, 1 << bit), 2)
        spots[order[b]] = (piece * GROUPS + lax.div(owner, per_plane)) * 2 + lax.rem(b, 2)
        return 0

    lax.fori_loop(0, order.shape[0], put, 0)
    load_pieces(pieces, kv_ref, sems)

    def gather(h, start, n):
        return jnp.concatenate(
            [kv_ref[spots[start + i], :, h * 128 : (h + 1) * 128] for i in range(n)], 0
        )

    whole = length // (wide * BLK)
    tail = whole * wide
    tails = (length - tail * BLK + narrow * BLK - 1) // (narrow * BLK)
    for h in range(heads):
        hs = slice(h * DH, (h + 1) * DH)
        own = jnp.concatenate([q_ref[b, :, hs] for b in range(blocks)], 0)
        qa[...] = jnp.concatenate([own, jnp.zeros_like(own)], 1)
        acc[...] = jnp.zeros_like(acc)
        sums[...] = jnp.zeros_like(sums)

        def step(start, n, masked, h=h):
            kv = gather(h, start, n)
            scores = dot(qa[...], kv, NT)
            if masked:
                place = lax.broadcasted_iota(jnp.int32, scores.shape, 1) + start * BLK
                scores = jnp.where(place < length, scores, -1e30)
            p = jnp.exp2(scores)
            sums[...] += sum(p[:, i * 128 : (i + 1) * 128] for i in range(n))
            acc[...] += dot(p.astype(BF16), kv)

        def wide_step(j, _, step=step):
            step(j * wide, wide, False)
            return 0

        def narrow_step(j, _, step=step):
            step(tail + j * narrow, narrow, True)
            return 0

        lax.fori_loop(0, whole, wide_step, 0)
        lax.fori_loop(0, tails, narrow_step, 0)
        total = jnp.sum(sums[...], 1, keepdims=True)
        across = jnp.transpose(jnp.broadcast_to(total, (rows, 128)))[:8]
        good = (jnp.min(across) > 2.0**-80) & (jnp.max(across) < 2.0**100)

        @pl.when(good)
        def _(h=h, hs=hs, total=total, across=across):
            lse_ref[h] = jnp.log2(across)
            o_ref[:, hs] = (acc[:, DH:] * (1.0 / total)).astype(BF16)

        @pl.when(jnp.logical_not(good))
        def _(h=h, hs=hs):
            key_blocks = (length + BLK - 1) // BLK

            def rows_step(t, _):
                part = pl.ds(pl.multiple_of(t * BLK, BLK), BLK)
                q = qa[part, :]

                def scores_of(j):
                    kv = gather(h, j, 1)
                    scores = dot(q, kv, NT)
                    place = lax.broadcasted_iota(jnp.int32, scores.shape, 1) + j * BLK
                    return kv, jnp.where(place < length, scores, -1e30)

                largest = lax.fori_loop(
                    0,
                    key_blocks,
                    lambda j, m: jnp.maximum(m, jnp.max(scores_of(j)[1], 1, keepdims=True)),
                    jnp.full((BLK, 1), -1e30, F32),
                )
                acc[part, :] = jnp.zeros((BLK, 128), F32)
                sums[part, :] = jnp.zeros((BLK, 128), F32)

                def add(j, _):
                    kv, scores = scores_of(j)
                    p = jnp.exp2(scores - largest)
                    sums[part, :] += p
                    acc[part, :] += dot(p.astype(BF16), kv)
                    return 0

                lax.fori_loop(0, key_blocks, add, 0)
                row_total = jnp.sum(sums[part, :], 1, keepdims=True)
                lse = largest + jnp.log2(row_total)
                lse_ref[h, :, part] = jnp.transpose(jnp.broadcast_to(lse, (BLK, 128)))[:8]
                o_ref[part, hs] = (acc[part, :][:, DH:] * (1.0 / row_total)).astype(BF16)
                return 0

            lax.fori_loop(0, rows // BLK, rows_step, 0)


def attend(s, per_plane, lengths, order, q, pieces):
    blocks, _, per = q.shape
    rows, heads = blocks * BLK, per // DH
    key_blocks = len(pieces) * pieces[0].shape[0]
    return pl.pallas_call(
        functools.partial(forward_kernel, 8, 2, len(pieces), s, per_plane),
        out_shape=(
            jax.ShapeDtypeStruct((rows, per), BF16),
            jax.ShapeDtypeStruct((heads, 8, rows), F32),
        ),
        in_specs=[SMEM, SMEM, VMEM] + [ANY] * len(pieces),
        out_specs=(VMEM, VMEM),
        scratch_shapes=[
            pltpu.VMEM((key_blocks, BLK, 2 * per), BF16),
            pltpu.VMEM((rows, 128), BF16),
            pltpu.VMEM((rows, 128), F32),
            pltpu.VMEM((rows, 128), F32),
            pltpu.SMEM((key_blocks,), jnp.int32),
            pltpu.SemaphoreType.DMA((len(pieces),)),
        ],
        compiler_params=ROOM,
        cost_estimate=cost(20),
        name="attend",
    )(lengths, order, q, *pieces)


def backward_kernel(qn, kn, count, sc, q_ref, do_ref, o_ref, lse_ref, *rest):
    pieces, dq_ref, outs = rest[:count], rest[count], rest[count + 1 : 2 * count + 1]
    kv_ref, both, dkv, dq, lse_row, delta_row, sems = rest[2 * count + 1 :]
    blocks = q_ref.shape[0]
    heads = q_ref.shape[2] // DH
    key_blocks = kv_ref.shape[0]
    tile = qn * BLK
    length, used = sc[0], sc[1]
    whole = length // (kn * BLK)
    parts = (length + kn * BLK - 1) // (kn * BLK)
    tiles = (used + qn - 1) // qn
    ones = jnp.ones((8, DH), BF16)
    load_pieces(pieces, kv_ref, sems)
    for h in range(heads):
        hs = slice(h * DH, (h + 1) * DH)

        def clear(i, _):
            dkv[pl.ds(pl.multiple_of(i * 1024, 1024), 1024), :] = jnp.zeros((1024, 128), F32)
            return 0

        lax.fori_loop(0, key_blocks // 8, clear, 0)
        dq[...] = jnp.zeros_like(dq)

        def prepare(t, _, h=h, hs=hs):
            base = pl.multiple_of(t * (2 * tile), 2 * tile)
            start = pl.multiple_of(t * tile, tile)
            places = [sc[8 + t * qn + i] for i in range(qn)]
            q = jnp.concatenate([q_ref[s, :, hs] for s in places], 0)
            do = jnp.concatenate([do_ref[s, :, hs] for s in places], 0)
            o = jnp.concatenate([o_ref[s, :, hs] for s in places], 0)
            zero = jnp.zeros_like(q)
            both[pl.ds(base, tile), :] = jnp.concatenate([q, zero], 1)
            both[pl.ds(base + tile, tile), :] = jnp.concatenate([zero, do], 1)
            product = do.astype(F32) * o.astype(F32)
            high = product.astype(BF16)
            rest_of = (product - high.astype(F32)).astype(BF16)
            delta_row[:, pl.ds(start, tile)] = dot(ones, high, NT) + dot(ones, rest_of, NT)
            lse_row[:, pl.ds(start, tile)] = jnp.concatenate(
                [lse_ref[h, :, pl.ds(pl.multiple_of(s * BLK, BLK), BLK)] for s in places], 1
            )
            return 0

        lax.fori_loop(0, tiles, prepare, 0)

        def rows_step(t, _, h=h):
            base = pl.multiple_of(t * (2 * tile), 2 * tile)
            span = pl.ds(pl.multiple_of(t * tile, tile), tile)

            def step(j, masked):
                places = [sc[8 + blocks + j * kn + i] for i in range(kn)]
                kv = jnp.concatenate([kv_ref[s, :, h * 128 : (h + 1) * 128] for s in places], 0)
                b = both[pl.ds(base, 2 * tile), :]
                found = dot(kv, b, NT)
                p = jnp.exp2(found[:, :tile] - lse_row[:1, span])
                if masked:
                    place = lax.broadcasted_iota(jnp.int32, p.shape, 0) + j * (kn * BLK)
                    p = jnp.where(place < length, p, 0.0)
                ds = (p * (found[:, tile:] - delta_row[:1, span])).astype(BF16)
                grads = dot(jnp.concatenate([ds, p.astype(BF16)], 1), b)
                for i, s in enumerate(places):
                    dkv[pl.ds(pl.multiple_of(s * BLK, BLK), BLK), :] += grads[
                        i * BLK : (i + 1) * BLK
                    ]
                dq[span, :] += dot(ds, kv, TN)

            def whole_step(j, _):
                step(j, False)
                return 0

            lax.fori_loop(0, whole, whole_step, 0)

            @pl.when(parts > whole)
            def _():
                step(whole, True)

            return 0

        lax.fori_loop(0, tiles, rows_step, 0)
        for i in range(blocks):
            dq_ref[sc[8 + i], :, hs] = (
                dq[i * BLK : (i + 1) * BLK, :DH] * DH**-0.5
            ).astype(BF16)
        level = jnp.where(lax.broadcasted_iota(jnp.int32, (1, 128), 1) < DH, LN2, 1.0)
        per_piece = key_blocks // count
        for n, out in enumerate(outs):
            for i in range(per_piece):
                b = n * per_piece + i
                out[i, :, h * 128 : (h + 1) * 128] = (
                    dkv[b * BLK : (b + 1) * BLK, :] * level
                ).astype(BF16)


def attend_back(sc, q, do, o, lse, pieces):
    blocks, _, per = q.shape
    rows = blocks * BLK
    key_blocks = len(pieces) * pieces[0].shape[0]
    return pl.pallas_call(
        functools.partial(backward_kernel, 4, 4, len(pieces)),
        out_shape=[jax.ShapeDtypeStruct(q.shape, BF16)]
        + [jax.ShapeDtypeStruct(p.shape, BF16) for p in pieces],
        in_specs=[SMEM] + [VMEM] * 4 + [ANY] * len(pieces),
        out_specs=[VMEM] * (1 + len(pieces)),
        scratch_shapes=[
            pltpu.VMEM((key_blocks, BLK, 2 * per), BF16),
            pltpu.VMEM((2 * rows, 128), BF16),
            pltpu.VMEM((key_blocks * BLK, 128), F32),
            pltpu.VMEM((rows, 128), F32),
            pltpu.VMEM((8, rows), F32),
            pltpu.VMEM((8, rows), F32),
            pltpu.SemaphoreType.DMA((len(pieces),)),
        ],
        compiler_params=ROOM,
        cost_estimate=cost(45),
        name="attend_back",
    )(sc, q, do, o, lse, *pieces)


def norm(values):
    centered = values - jnp.mean(values, -1, keepdims=True)
    inverse = lax.rsqrt(jnp.mean(centered * centered, -1, keepdims=True) + 1e-6)
    return centered * inverse, inverse


def norm_back(upstream, normed, inverse):
    return inverse * (
        upstream
        - jnp.mean(upstream, -1, keepdims=True)
        - normed * jnp.mean(upstream * normed, -1, keepdims=True)
    )


def normal_parts(x):
    z = jnp.abs(x) * (0.5**0.5)
    bell = jnp.exp(-0.5 * x * x)
    t = 1.0 / (1.0 + 0.3275911 * z)
    poly = t * (
        0.254829592
        + t * (-0.284496736 + t * (1.421413741 + t * (-1.453152027 + t * 1.061405429)))
    )
    upper = 0.5 * poly * bell
    return jnp.where(x >= 0, 1.0 - upper, upper), bell * (2.0 * math.pi) ** -0.5


def dense_kernel(sc, att4, tok, teach, vec, wide_vec, *rest):
    weights, rest = rest[:9], rest[9:]
    outs, (wo, wi, wu, slope, sems) = rest[:11], rest[11:]
    out, fg, ag, att_o, br_o, hl_o, il_o, act_o, ol_o, sums, wide_sums = outs
    rows, width = tok.shape
    hidden = wi.shape[1]
    tile = 512
    copies = [
        weight_copies(full, *weights[3 * i : 3 * i + 3], sems, 3 * i)
        for i, full in enumerate((wo, wi, wu))
    ]
    for group in copies:
        for copy in group:
            copy.start()
    per = att4.shape[2]
    att = jnp.concatenate([att4[g] for g in range(GROUPS)], 1)
    att_o[...] = att
    row = lax.broadcasted_iota(jnp.int32, (rows, 1), 0)
    mask = jnp.where(
        row < BLK, jnp.where(row < sc[0], 1.0, 0.0), jnp.where(row - BLK < sc[1], 1.0, 0.0)
    )
    out_bias, gain_one, shift_one = vec[0:1, :], vec[1:2, :], vec[2:3, :]
    outer_bias, gain_two, shift_two = vec[3:4, :], vec[4:5, :], vec[5:6, :]
    for copy in copies[0]:
        copy.wait()
    first = tok[...].astype(F32) + dot(att, wo[...]) + out_bias
    normed_one, inverse_one = norm(first)
    hidden_in = normed_one * gain_one + shift_one
    hl = hidden_in.astype(BF16)
    hl_o[...] = hl
    for copy in copies[1] + copies[2]:
        copy.wait()
    second = hidden_in + outer_bias
    for n in range(hidden // tile):
        cols = slice(n * tile, (n + 1) * tile)
        inner = dot(hl, wi[:, cols]) + wide_vec[0:1, cols]
        below, density = normal_parts(inner)
        act = (inner * below).astype(BF16)
        act_o[:, cols] = act
        slope[:, cols] = below + inner * density
        second += dot(act, wu[cols, :])
    normed_two, inverse_two = norm(second)
    final = normed_two * gain_two + shift_two
    out[...] = final.astype(BF16)
    residue = (final - teach[...].astype(F32)) * mask
    add = functools.partial(jnp.sum, axis=0, keepdims=True)
    second_grad = norm_back(residue * gain_two, normed_two, inverse_two)
    ol = second_grad.astype(BF16)
    ol_o[...] = ol
    hidden_grad = second_grad
    for n in range(hidden // tile):
        cols = slice(n * tile, (n + 1) * tile)
        il = (dot(ol, wu[cols, :], NT) * slope[:, cols]).astype(BF16)
        il_o[:, cols] = il
        wide_sums[0:1, cols] = add(il.astype(F32))
        hidden_grad += dot(il, wi[:, cols], NT)
    first_grad = norm_back(hidden_grad * gain_one, normed_one, inverse_one)
    fg[...] = first_grad
    br = first_grad.astype(BF16)
    br_o[...] = br
    att_grad = dot(br, wo[...], NT).astype(BF16)
    for g in range(GROUPS):
        ag[g] = att_grad[:, g * per : (g + 1) * per]
    sums[0:1, :] = add(residue * normed_two)
    sums[1:2, :] = add(residue)
    sums[2:3, :] = add(ol.astype(F32))
    sums[3:4, :] = add(hidden_grad * normed_one)
    sums[4:5, :] = add(hidden_grad)
    sums[5:6, :] = add(br.astype(F32))
    sums[6:7, :] = add(residue * residue)
    sums[7:8, :] = jnp.zeros((1, width), F32)


def dense(sc, att4, tok, teach, vec, wide_vec, weights):
    rows, width = tok.shape
    hidden = wide_vec.shape[1]
    narrow = jax.ShapeDtypeStruct((rows, width), BF16)
    wide = jax.ShapeDtypeStruct((rows, hidden), BF16)
    return pl.pallas_call(
        dense_kernel,
        out_shape=[
            narrow,
            jax.ShapeDtypeStruct((rows, width), F32),
            jax.ShapeDtypeStruct(att4.shape, BF16),
            narrow,
            narrow,
            narrow,
            wide,
            wide,
            narrow,
            jax.ShapeDtypeStruct((8, width), F32),
            jax.ShapeDtypeStruct((1, hidden), F32),
        ],
        in_specs=[SMEM] + [VMEM] * 5 + [ANY] * 9,
        out_specs=[VMEM] * 11,
        scratch_shapes=[
            pltpu.VMEM((width, width), BF16),
            pltpu.VMEM((width, hidden), BF16),
            pltpu.VMEM((hidden, width), BF16),
            pltpu.VMEM((rows, hidden), F32),
            pltpu.SemaphoreType.DMA((9,)),
        ],
        compiler_params=ROOM,
        cost_estimate=cost(15),
        name="dense",
    )(sc, att4, tok, teach, vec, wide_vec, *weights)


def dense_grads_kernel(seqs, *refs):
    ins, (g_out, g_inner, g_outer) = refs[: 6 * seqs], refs[6 * seqs :]
    att, br, hl, il, act, ol = (
        jnp.concatenate([ins[6 * s + i][...] for s in range(seqs)], 0) for i in range(6)
    )
    for target, left, right in ((g_out, att, br), (g_inner, hl, il), (g_outer, act, ol)):
        rows = target.shape[1]
        for n in range(4):
            piece = left[:, n * rows : (n + 1) * rows]
            for t in range(right.shape[1] // 768):
                cols = slice(t * 768, (t + 1) * 768)
                target[n, :, cols] = dot(piece, right[:, cols], TN).astype(BF16)


def dense_grads(saved):
    seqs = len(saved)
    width, hidden = saved[0][0].shape[1], saved[0][3].shape[1]
    return pl.pallas_call(
        functools.partial(dense_grads_kernel, seqs),
        out_shape=[
            jax.ShapeDtypeStruct((4, width // 4, width), BF16),
            jax.ShapeDtypeStruct((4, width // 4, hidden), BF16),
            jax.ShapeDtypeStruct((4, hidden // 4, width), BF16),
        ],
        in_specs=[VMEM] * (6 * seqs),
        out_specs=[VMEM] * 3,
        compiler_params=ROOM,
        cost_estimate=cost(10),
        name="dense_grads",
    )(*[member for group in saved for member in group])


def project_grads_kernel(seqs, sc, tok, *refs):
    fgs, refs = refs[:seqs], refs[seqs:]
    grads_in, refs = refs[: 2 * seqs], refs[2 * seqs :]
    wq, wk, wv, first, second, tg, grads, sums, full, sems = refs
    rows, width = tok.shape[1:]
    per = width // GROUPS
    heads = per // DH
    quarter = wq.shape[0] // 2
    copies = []
    for i, own in enumerate((wq, wk, wv)):
        part = pl.ds(i * quarter, quarter)
        copies += weight_copies(full.at[i], own, first.at[part], second.at[part], sems, 3 * i)
    for copy in copies:
        copy.start()

    def head(i, s, g, h):
        if i == 0:
            return grads_in[s][g, :, h * DH : (h + 1) * DH]
        start = h * 128 + (i - 1) * DH
        return grads_in[seqs + s][g, :, start : start + DH]

    def whole(i):
        each = [
            jnp.concatenate([head(i, s, g, h) for g in range(GROUPS) for h in range(heads)], 1)
            for s in range(seqs)
        ]
        return jnp.concatenate(each, 0)

    valid = jnp.concatenate([valid_rows(sc, s, rows) for s in range(seqs)], 0) > 0.0
    dq = whole(0)
    halves = [jnp.where(valid, whole(i), jnp.zeros((), BF16)) for i in (1, 2)]
    flat = tok[...].reshape(seqs * rows, width)
    for copy in copies:
        copy.wait()
    total = jnp.concatenate([fgs[s][...] for s in range(seqs)], 0)
    for i, grad in enumerate((dq, *halves)):
        total += dot(grad, full[i], NT)
        found = dot(flat, grad, TN).astype(BF16)
        half = width // 2
        for n in range(2):
            for t in range(width // 128):
                grads[t % 3, t // 3, n, i * half : (i + 1) * half, :] = found[
                    n * half : (n + 1) * half, t * 128 : (t + 1) * 128
                ]
    tg[...] = total.reshape(seqs, rows, width)
    sums[0:1, :] = jnp.sum(dq.astype(F32), 0, keepdims=True)
    sums[1:2, :] = jnp.sum(halves[1].astype(F32), 0, keepdims=True)
    sums[2:8, :] = jnp.zeros((6, width), F32)


def project_grads(sc, tok, fgs, grads, wq, wk, wv, first, second):
    seqs, rows, width = tok.shape
    return pl.pallas_call(
        functools.partial(project_grads_kernel, seqs),
        out_shape=[
            jax.ShapeDtypeStruct(tok.shape, F32),
            jax.ShapeDtypeStruct((3, 2, 2, 3 * (width // 2), 128), BF16),
            jax.ShapeDtypeStruct((8, width), F32),
        ],
        in_specs=[SMEM] + [VMEM] * (1 + len(fgs) + len(grads)) + [ANY] * 5,
        out_specs=[VMEM] * 3,
        scratch_shapes=[pltpu.VMEM((3, width, width), BF16), pltpu.SemaphoreType.DMA((9,))],
        compiler_params=ROOM,
        cost_estimate=cost(10),
        name="project_grads",
    )(sc, tok, *fgs, *grads, wq, wk, wv, first, second)


MESH = pl.DeviceIdType.MESH


def position():
    ctx = lax.axis_index("ctx")
    return ctx // 4, lax.rem(ctx // 2, 2), lax.rem(ctx, 2), lax.axis_index("wa")


def device(z, y, c, x):
    return z * 4 + y * 2 + c, x


def greet(others):
    barrier = pltpu.get_barrier_semaphore()
    for other in others:
        pl.semaphore_signal(barrier, inc=1, device_id=other, device_id_type=MESH)
    pl.semaphore_wait(barrier, len(others))


def send(src, dst, sems, to):
    copy = pltpu.make_async_remote_copy(
        src_ref=src,
        dst_ref=dst,
        send_sem=sems[0],
        recv_sem=sems[1],
        device_id=to,
        device_id_type=MESH,
    )
    copy.start()
    return copy


def add_low(left, right):
    return (left.astype(F32) + right.astype(F32)).astype(BF16)


def back_kernel(seqs, *refs):
    per_seq = 5
    ins = [refs[per_seq * s : per_seq * (s + 1)] for s in range(seqs)]
    a_own, a_give, b_own, b_give, rq, rkv, dense_out, *refs = refs[per_seq * seqs :]
    q_v, do_v, o_v, lse_v, kv_v, both, dkv, dq, delta, obuf, qbuf = refs[:11]
    from_core, from_y, a_v, b_v, a_in, b_in, a2, b2, a2_in, b2_in = refs[11:21]
    az_in, bz_in, dres, in_sem, c_sem, y_sem, z_sem, q_sem, l_sem, x_sem, dz_sem = refs[21:]
    z, y, c, x = position()
    sibling, beside, over = device(z, y, 1 - c, x), device(z, 1 - y, c, x), device(z, y, c, 1 - x)
    line = [None] + [device(z ^ d, y, c, x) for d in range(1, GROUPS)]
    greet([sibling, beside, over] + line[1:])

    def pair(sems, *index):
        return sems.at[(0, *index)], sems.at[(1, *index)]

    flow = {}
    flow["a"] = send(a_give, a_in, pair(x_sem, 0), over)
    flow["b"] = send(b_give, b_in, pair(x_sem, 1), beside)
    loads = []
    for s in range(seqs):
        targets = [ref.at[s] for ref in (q_v, do_v, o_v, lse_v, kv_v)]
        group = [
            pltpu.make_async_copy(src, dst, in_sem.at[s, i])
            for i, (src, dst) in enumerate(zip(ins[s], targets))
        ]
        for copy in group:
            copy.start()
        loads.append(group)
    own_loads = [
        pltpu.make_async_copy(a_own, a_v, l_sem.at[0]),
        pltpu.make_async_copy(b_own, b_v, l_sem.at[1]),
    ]
    for copy in own_loads:
        copy.start()

    rows = q_v.shape[1]
    heads = q_v.shape[2] // DH
    keys = kv_v.shape[1]
    tile, ktile = rows // 2, 2048
    quarter = keys // 4
    chunk = quarter // GROUPS
    ones = jnp.ones((8, DH), BF16)
    level = jnp.where(lax.broadcasted_iota(jnp.int32, (1, 128), 1) < DH, LN2, 1.0)
    waits = []

    def group_rows(g):
        return pl.ds(pl.multiple_of(g * chunk, chunk), chunk)

    def core_stage(u):
        flow["c", u] = send(
            obuf.at[u, pl.ds(2 * quarter, 2 * quarter)], from_core.at[u], pair(c_sem, u), sibling
        )

    def y_stage(u):
        flow["c", u].wait()
        second = pl.ds(quarter, quarter)
        obuf[u, second] = add_low(obuf[u, second], from_core[u, second])
        flow["y", u] = send(obuf.at[u, second], from_y.at[u], pair(y_sem, u), beside)
        obuf[u, 0:quarter] = add_low(obuf[u, 0:quarter], from_core[u, 0:quarter])

    def z_stage(u):
        flow["y", u].wait()
        obuf[u, 0:quarter] = add_low(obuf[u, 0:quarter], from_y[u])
        for d in range(1, GROUPS):
            src = obuf.at[u, group_rows(z ^ d)]
            waits.append(send(src, rkv.at[u, z], pair(z_sem, u, d), line[d]))
        own = pltpu.make_async_copy(obuf.at[u, group_rows(z)], rkv.at[u, z], z_sem.at[0, u, 0])
        own.start()
        waits.append(own)

    def q_stage(h):
        for d in range(1, GROUPS):
            waits.append(send(qbuf.at[h, z ^ d], rq.at[h, z], pair(q_sem, h, d), line[d]))
        own = pltpu.make_async_copy(qbuf.at[h, z], rq.at[h, z], q_sem.at[0, h, 0])
        own.start()
        waits.append(own)

    a_half, b_half = a2.shape[1], b2.shape[1]

    def dense_second():
        for copy in own_loads:
            copy.wait()
        flow["a"].wait()
        for slot, which in ((0, y), (1, 1 - y)):
            part = pl.ds(pl.multiple_of(which * a_half, 16), a_half)
            a2[slot] = add_low(a_v[part, :], a_in[part, :])
        flow["a"] = send(a2.at[1], a2_in, pair(x_sem, 2), beside)
        flow["b"].wait()
        for slot, which in ((0, x), (1, 1 - x)):
            b2[slot] = add_low(b_v[which], b_in[which])
        flow["b"] = send(b2.at[1], b2_in, pair(x_sem, 3), over)

    low_bit, high_bit = lax.rem(z, 2), z // 2
    parts = (("a", a2, a2_in, az_in), ("b", b2, b2_in, bz_in))

    def rows_at(start, n):
        return pl.ds(pl.multiple_of(start, 16), n)

    def dense_third():
        for i, (name, held, arrived, landing) in enumerate(parts):
            flow[name].wait()
            held[0] = add_low(held[0], arrived[...])
            n = held.shape[1] // 2
            src = held.at[0, rows_at((1 - low_bit) * n, n)]
            flow[name] = send(src, landing.at[0:n], pair(dz_sem, i, 0), line[1])

    def dense_fourth():
        for i, (name, held, _, landing) in enumerate(parts):
            flow[name].wait()
            n = held.shape[1] // 2
            mine = rows_at(low_bit * n, n)
            held[0, mine] = add_low(held[0, mine], landing[0:n])
            src = held.at[0, rows_at(low_bit * n + (1 - high_bit) * (n // 2), n // 2)]
            flow[name] = send(src, landing.at[n : n + n // 2], pair(dz_sem, i, 1), line[2])

    def dense_fifth():
        base = 0
        for name, held, _, landing in parts:
            flow[name].wait()
            n = held.shape[1] // 2
            mine = rows_at(low_bit * n + high_bit * (n // 2), n // 2)
            dres[base : base + n // 2] = add_low(held[0, mine], landing[n : n + n // 2])
            base += n // 2

    units = [(h, s) for h in range(heads) for s in range(seqs)]
    slots = {}
    for u in range(len(units) - 1):
        slots.setdefault(2 * u + 3, []).append(functools.partial(y_stage, u))
        slots.setdefault(2 * u + 5, []).append(functools.partial(z_stage, u))
    slots.setdefault(5, []).append(dense_second)
    slots.setdefault(7, []).append(dense_third)
    slots.setdefault(9, []).append(dense_fourth)
    slots.setdefault(12, []).append(dense_fifth)

    for u, (h, s) in enumerate(units):
        hs = slice(h * DH, (h + 1) * DH)
        lanes = slice(h * 128, (h + 1) * 128)
        if h == 0:
            for copy in loads[s]:
                copy.wait()
        for n in range(2):
            for work in slots.get(2 * u + n, []):
                work()
            part = slice(n * tile, (n + 1) * tile)
            q, do, o = q_v[s, part, hs], do_v[s, part, hs], o_v[s, part, hs]
            zero = jnp.zeros_like(q)
            both[0:tile, :] = jnp.concatenate([q, zero], 1)
            both[tile : 2 * tile, :] = jnp.concatenate([zero, do], 1)
            product = do.astype(F32) * o.astype(F32)
            high = product.astype(BF16)
            remains = (product - high.astype(F32)).astype(BF16)
            delta[...] = dot(ones, high, NT) + dot(ones, remains, NT)
            dq[...] = jnp.zeros_like(dq)

            def step(j, _, u=u, s=s, h=h, n=n, part=part, lanes=lanes):
                span = pl.ds(pl.multiple_of(j * ktile, ktile), ktile)
                kv = kv_v[s, span, lanes]
                b = both[...]
                found = dot(kv, b, NT)
                p = jnp.exp2(jnp.minimum(found[:, :tile] - lse_v[s, h, 0:1, part], 1.0))
                ds = (p * (found[:, tile:] - delta[0:1, :])).astype(BF16)
                grads = dot(jnp.concatenate([ds, p.astype(BF16)], 1), b)
                if n == 0:
                    dkv[span, :] = grads
                else:
                    obuf[u, span, :] = ((dkv[span, :] + grads) * level).astype(BF16)
                dq[...] += dot(ds, kv, TN)
                return 0

            lax.fori_loop(0, keys // ktile, step, 0)
            found = (dq[:, :DH] * DH**-0.5).astype(BF16)
            for i in range(2):
                qbuf[h, 2 * n + i, :, s * DH : (s + 1) * DH] = found[
                    i * (tile // 2) : (i + 1) * (tile // 2)
                ]
        core_stage(u)
        if s == seqs - 1:
            q_stage(h)
    last = len(units) - 1
    for n in sorted(n for n in slots if n >= 2 * len(units)):
        for work in slots[n]:
            work()
    y_stage(last)
    z_stage(last)
    for copy in waits:
        copy.wait()
    done = pltpu.make_async_copy(dres, dense_out, l_sem.at[0])
    done.start()
    done.wait()


def attend_back_all(seqs_in, ready):
    seqs = len(seqs_in)
    q, _, _, lse, held = seqs_in[0]
    rows, per = q.shape
    heads = per // DH
    units = heads * seqs
    keys = held.shape[0]
    chunk = rows // GROUPS
    a, b = ready[0].shape, ready[2].shape
    a_half, b_half, half = a[0] // 2, b[1], a[1]
    dma = pltpu.SemaphoreType.DMA
    return pl.pallas_call(
        functools.partial(back_kernel, seqs),
        out_shape=[
            jax.ShapeDtypeStruct((heads, GROUPS, chunk, 128), BF16),
            jax.ShapeDtypeStruct((units, GROUPS, chunk, 128), BF16),
            jax.ShapeDtypeStruct(((a_half + b_half) // 4, half), BF16),
        ],
        in_specs=[ANY] * (5 * seqs + 4),
        out_specs=[ANY] * 3,
        scratch_shapes=[
            pltpu.VMEM((seqs, rows, per), BF16),
            pltpu.VMEM((seqs, rows, per), BF16),
            pltpu.VMEM((seqs, rows, per), BF16),
            pltpu.VMEM((seqs, *lse.shape), F32),
            pltpu.VMEM((seqs, keys, 2 * per), BF16),
            pltpu.VMEM((rows, 128), BF16),
            pltpu.VMEM((keys, 128), F32),
            pltpu.VMEM((rows // 2, 128), F32),
            pltpu.VMEM((8, rows // 2), F32),
            pltpu.VMEM((units, keys, 128), BF16),
            pltpu.VMEM((heads, GROUPS, chunk, 128), BF16),
            pltpu.VMEM((units, keys // 2, 128), BF16),
            pltpu.VMEM((units, keys // 4, 128), BF16),
            pltpu.VMEM(a, BF16),
            pltpu.VMEM(b, BF16),
            pltpu.VMEM(a, BF16),
            pltpu.VMEM(b, BF16),
            pltpu.VMEM((2, a_half, half), BF16),
            pltpu.VMEM((2, b_half, half), BF16),
            pltpu.VMEM((a_half, half), BF16),
            pltpu.VMEM((b_half, half), BF16),
            pltpu.VMEM((3 * a_half // 4, half), BF16),
            pltpu.VMEM((3 * b_half // 4, half), BF16),
            pltpu.VMEM(((a_half + b_half) // 4, half), BF16),
            dma((seqs, 5)),
            dma((2, units)),
            dma((2, units)),
            dma((2, units, GROUPS)),
            dma((2, heads, GROUPS)),
            dma((2,)),
            dma((2, 4)),
            dma((2, 2, 2)),
        ],
        compiler_params=pltpu.CompilerParams(
            vmem_limit_bytes=63 * 2**20, collective_id=1, has_side_effects=True
        ),
        cost_estimate=cost(120),
        name="attend_back_all",
    )(*[member for group in seqs_in for member in group], *ready)


def vector_of(vec, row, half):
    both = [vec[k, row + 1 : row + 2, :half].astype(F32) for k in range(2)]
    return jnp.concatenate(both, 1)


def start_kernel(seqs, lengths, order, tokens, wq, wk, wv, wo, wi, wu, *refs):
    sc = Counts(lengths, order)
    vectors, refs = refs[:9], refs[9:]
    q_out, kv_out, o_out, lse_out = (refs[i * seqs : (i + 1) * seqs] for i in range(4))
    refs = refs[4 * seqs :]
    back_out, vec_out, others, *dense_out = refs[:6]
    full, q_held, kv_held, vec, own_vec, tok, *refs = refs[6:]
    q_v, kv_v, o_v, lse_v, shade, qa, acc, sums, top, *sems = refs
    v_sem, wx_sem, wy_sem, wc_sem, l_sem, dx_sem, dc_sem, q_sem, z_sem, y_sem, c_sem = sems[:11]
    own_sem, b_sem = sems[11:]
    z, y, c, x = position()
    sibling, beside, over = device(z, y, 1 - c, x), device(z, 1 - y, c, x), device(z, y, c, 1 - x)
    line = [None] + [device(z ^ d, y, c, x) for d in range(1, GROUPS)]
    greet([sibling, beside, over] + line[1:])

    def pair(sem, *index):
        return sem.at[(0, *index)], sem.at[(1, *index)]

    waits = []
    half = wq.shape[0]
    eighth = half // 4

    def rows_of(which, cc, yy):
        start = which * half + (2 * cc + yy) * eighth
        return pl.ds(pl.multiple_of(start, 16), eighth)

    own_rows = pl.ds(pl.multiple_of((2 * c + y) * eighth, 16), eighth)
    tok_in = pltpu.make_async_copy(tokens, tok, l_sem.at[6])
    tok_in.start()
    flow = {}
    turns = (1, 2, 0)
    locals_of = []
    for i in turns:
        own = (wq, wk, wv)[i]
        flow["x", i] = send(
            own.at[own_rows], full.at[i, rows_of(x, c, y)], pair(wx_sem, i), over
        )
    for i in turns:
        own = (wq, wk, wv)[i]
        place = full.at[i, pl.ds(pl.multiple_of(x * half, half), half)]
        copy = pltpu.make_async_copy(own, place, l_sem.at[i])
        copy.start()
        locals_of.append(copy)
    own_vec[...] = jnp.zeros_like(own_vec)
    for i, one in enumerate(vectors):
        row = (i + 1) % len(vectors)
        own_vec[row : row + 1, : one.shape[0]] = one[...].astype(F32)[None].astype(BF16)
    vec[x] = own_vec[...]
    vec_flow = send(own_vec, vec.at[x], pair(v_sem), over)

    def after_x(i):
        flow["x", i].wait()
        got = full.at[i, rows_of(1 - x, c, y)]
        flow["y", i] = send(got, got, pair(wy_sem, i), beside)
        flow["c", i, 0] = send(got, got, pair(wc_sem, i, 0), sibling)

    def after_y(i):
        flow["y", i].wait()
        got = full.at[i, rows_of(1 - x, c, 1 - y)]
        flow["c", i, 1] = send(got, got, pair(wc_sem, i, 1), sibling)

    def after_core(i):
        flow["c", i, 0].wait()
        flow["c", i, 1].wait()

    rows, width = tok.shape[1:]
    per = width // GROUPS
    heads = per // DH
    tok_in.wait()
    flat = tok[...].reshape(seqs * rows, width)
    valid = jnp.concatenate([valid_rows(sc, s, rows) for s in range(seqs)], 0) > 0.0
    lane = lax.broadcasted_iota(jnp.int32, (8, BLK), 1)
    for piece, offset in enumerate((0, 2, 1, 3)):
        owner = lax.bitwise_xor(2 * y + c, offset)
        for g in range(GROUPS):
            for k in range(2):
                start_of = order[(4 * g + owner) * 2 + k] * BLK
                for s in range(seqs):
                    inside = lane + start_of < lengths[s]
                    cols = slice((2 * g + k) * BLK, (2 * g + k + 1) * BLK)
                    shade[s, piece, :, cols] = jnp.where(inside, 0.0, -1e30)
    after_x(1)
    after_x(2)
    after_y(1)
    after_x(0)
    dense_weights = (wo, wi, wu)
    for i, weight in enumerate(dense_weights):
        n = weight.shape[0] // 2
        part = pl.ds(pl.multiple_of(c * n, 16), n)
        flow["dx", i] = send(weight.at[part], dense_out[i].at[part], pair(dx_sem, i), over)
    after_y(2)
    vec_flow.wait()

    def bias(row):
        return vector_of(vec, row, half)

    for copy in locals_of:
        copy.wait()
    after_core(1)
    keys = jnp.where(valid, dot(flat, full[1]), 0.0).astype(BF16)
    after_y(0)
    after_core(2)
    values = jnp.where(valid, dot(flat, full[2]) + bias(1), 0.0).astype(BF16)
    for s in range(seqs):
        rs = slice(s * rows, (s + 1) * rows)
        for g in range(GROUPS):
            for h in range(heads):
                cols = slice(g * per + h * DH, g * per + (h + 1) * DH)
                kv_held[s, g, :, h * 128 : (h + 1) * 128] = jnp.concatenate(
                    [keys[rs, cols], values[rs, cols]], 1
                )

    def kv_sends(s):
        for d in range(1, GROUPS):
            flow["z", s, d] = send(
                kv_held.at[s, z ^ d], kv_v.at[s, 0, z], pair(z_sem, s, d), line[d]
            )

    def q_sends(s):
        for d in range(1, GROUPS):
            flow["q", s, d] = send(q_held.at[s, z ^ d], q_v.at[s, z], pair(q_sem, s, d), line[d])

    kv_sends(0)

    def pass_on(s, d, src):
        g = z ^ d
        flow["ky", s, d] = send(src, kv_v.at[s, 1, g], pair(y_sem, s, d), beside)
        flow["kc", s, d, 0] = send(src, kv_v.at[s, 2, g], pair(c_sem, s, d, 0), sibling)

    def pass_core(s, d):
        flow["ky", s, d].wait()
        got = kv_v.at[s, 1, z ^ d]
        flow["kc", s, d, 1] = send(got, kv_v.at[s, 3, z ^ d], pair(c_sem, s, d, 1), sibling)

    pass_on(0, 0, kv_held.at[0, z])
    after_core(0)
    queries = ((dot(flat, full[0]) + bias(0)) * (DH**-0.5 / LN2)).astype(BF16)
    for s in range(seqs):
        rs = slice(s * rows, (s + 1) * rows)
        for g in range(GROUPS):
            q_held[s, g] = queries[rs, g * per : (g + 1) * per]
    for i in range(3):
        place = full.at[i, pl.ds(pl.multiple_of((1 - x) * half, half), half)]
        copy = pltpu.make_async_copy(place, others.at[i], l_sem.at[3 + i])
        copy.start()
        waits.append(copy)
    copy = pltpu.make_async_copy(vec, vec_out, l_sem.at[7])
    copy.start()
    waits.append(copy)
    for s in range(seqs):
        kv_v[s, 0, z] = kv_held[s, z]
        q_v[s, z] = q_held[s, z]

    def arrive(s, d):
        flow["z", s, d].wait()
        pass_on(s, d, kv_v.at[s, 0, z ^ d])

    def own_and_core(s):
        for d in range(GROUPS):
            flow["kc", s, d, 0].wait()

    def dense_core(i):
        flow["dx", i].wait()
        n = dense_weights[i].shape[0] // 2
        got = dense_out[i].at[pl.ds(pl.multiple_of(c * n, 16), n)]
        waits.append(send(got, got, pair(dc_sem, i), sibling))

    def leave(src, dst, i):
        copy = pltpu.make_async_copy(src, dst, b_sem.at[i])
        copy.start()
        waits.append(copy)

    def attend_part(s, h, pieces):
        lanes = slice(h * 128, (h + 1) * 128)
        count, tile = GROUPS * rows, 1024

        def step(j, _):
            piece = pieces[0] + j * (pieces[1] - pieces[0])
            kv = kv_v[s, piece, :, :, lanes].reshape(count, 128)
            dark = shade[s, piece, 0:1, :]
            for n in range(count // tile):
                part = slice(n * tile, (n + 1) * tile)
                scores = dot(qa[h, part, :], kv, NT) + dark
                high = scores[:, :128]
                for i in range(1, count // 128):
                    high = jnp.maximum(high, scores[:, i * 128 : (i + 1) * 128])
                old = top[h, part, :]
                new = jnp.maximum(old, jnp.max(high, 1, keepdims=True))
                fade = jnp.exp2(old - new)
                each = [
                    jnp.exp2(scores[:, i * 128 : (i + 1) * 128] - new) for i in range(count // 128)
                ]
                sums[h, part, :] = sums[h, part, :] * fade + sum(each)
                p = jnp.concatenate([one.astype(BF16) for one in each], 1)
                acc[h, part, :] = acc[h, part, :] * fade + dot(p, kv)
                top[h, part, :] = new
            return 0

        lax.fori_loop(0, 2, step, 0)

    def attend_begin(s, h):
        hs = slice(h * DH, (h + 1) * DH)
        mine = q_v[s, :, :, hs].reshape(GROUPS * rows, DH)
        qa[h] = jnp.concatenate([mine, jnp.zeros_like(mine)], 1)
        zero = jnp.zeros(acc.shape[1:], F32)
        acc[h], sums[h], top[h] = zero, zero, zero - 1e30

    def attend_end(s, h):
        hs = slice(h * DH, (h + 1) * DH)
        total = jnp.sum(sums[h], 1, keepdims=True)
        logs = top[h] + jnp.log2(jnp.broadcast_to(total, top.shape[1:]))
        lse_v[s, h] = jnp.transpose(logs)[:8]
        found = (acc[h][:, DH:] * (1.0 / total)).astype(BF16)
        o_v[s, :, :, hs] = found.reshape(GROUPS, rows, DH)

    def leave_all(s):
        for i, (src, dst) in enumerate(
            ((q_v, q_out), (kv_v, kv_out), (o_v, o_out), (lse_v, lse_out))
        ):
            leave(src.at[s], dst[s], 4 * s + i)

    for d in range(1, GROUPS):
        arrive(0, d)
        if d > 1:
            pass_core(0, d - 2)
    q_sends(0)
    pass_core(0, 2)
    pass_core(0, 3)
    for d in range(1, GROUPS):
        flow["q", 0, d].wait()
    kv_sends(1)
    own_and_core(0)
    pass_on(1, 0, kv_held.at[1, z])
    for d in range(GROUPS):
        flow["kc", 0, d, 1].wait()
    for h in range(heads):
        attend_begin(0, h)
        attend_part(0, h, (0, 2))
        if h == 1:
            dense_core(0)
        if h == 2:
            pass_core(1, 0)
            q_sends(1)
            for d in range(1, GROUPS):
                arrive(1, d)
        attend_part(0, h, (1, 3))
        attend_end(0, h)
    leave_all(0)
    own_and_core(1)
    for d in range(1, GROUPS):
        flow["q", 1, d].wait()
    for d in range(1, GROUPS):
        waits.append(send(o_v.at[0, z ^ d], back_out.at[z], pair(own_sem, d), line[d]))
    leave(o_v.at[0, z], back_out.at[z], 4 * seqs)
    for h in range(heads):
        attend_begin(1, h)
        attend_part(1, h, (0, 2))
        pass_core(1, h + 1)
    dense_core(1)
    dense_core(2)
    for d in range(GROUPS):
        flow["kc", 1, d, 1].wait()
    for h in range(heads):
        attend_part(1, h, (1, 3))
        attend_end(1, h)
    leave_all(1)
    for copy in waits:
        copy.wait()


def start(lengths, order, tok, weights, vectors):
    seqs, rows, width = tok.shape
    per = width // GROUPS
    half = weights[0].shape[0]
    joined = (16, vectors[-1].shape[0])
    heads, total = per // DH, GROUPS * rows
    narrow = jax.ShapeDtypeStruct((GROUPS, rows, per), BF16)
    dma = pltpu.SemaphoreType.DMA
    return pl.pallas_call(
        functools.partial(start_kernel, seqs),
        out_shape=[narrow] * seqs
        + [jax.ShapeDtypeStruct((4, GROUPS, rows, 2 * per), BF16)] * seqs
        + [narrow] * seqs
        + [jax.ShapeDtypeStruct((heads, 8, total), F32)] * seqs
        + [
            narrow,
            jax.ShapeDtypeStruct((2, *joined), BF16),
            jax.ShapeDtypeStruct((3, half, width), BF16),
        ]
        + [jax.ShapeDtypeStruct(w.shape, BF16) for w in weights[3:]],
        in_specs=[SMEM] * 2 + [ANY] * 7 + [VMEM] * 9,
        out_specs=[ANY] * (4 * seqs + 6),
        scratch_shapes=[
            pltpu.VMEM((3, width, width), BF16),
            pltpu.VMEM((seqs, GROUPS, rows, per), BF16),
            pltpu.VMEM((seqs, GROUPS, rows, 2 * per), BF16),
            pltpu.VMEM((2, *joined), BF16),
            pltpu.VMEM(joined, BF16),
            pltpu.VMEM(tok.shape, BF16),
            pltpu.VMEM((seqs, GROUPS, rows, per), BF16),
            pltpu.VMEM((seqs, 4, GROUPS, rows, 2 * per), BF16),
            pltpu.VMEM((seqs, GROUPS, rows, per), BF16),
            pltpu.VMEM((seqs, heads, 8, total), F32),
            pltpu.VMEM((seqs, 4, 8, total), F32),
            pltpu.VMEM((heads, total, 128), BF16),
            pltpu.VMEM((heads, total, 128), F32),
            pltpu.VMEM((heads, total, 128), F32),
            pltpu.VMEM((heads, total, 128), F32),
            dma((2,)),
            dma((2, 3)),
            dma((2, 3)),
            dma((2, 3, 2)),
            dma((8,)),
            dma((2, 3)),
            dma((2, 3)),
            dma((2, seqs, GROUPS)),
            dma((2, seqs, GROUPS)),
            dma((2, seqs, GROUPS)),
            dma((2, seqs, GROUPS, 2)),
            dma((2, GROUPS)),
            dma((4 * seqs + 1,)),
        ],
        compiler_params=pltpu.CompilerParams(
            vmem_limit_bytes=63 * 2**20, collective_id=4, has_side_effects=True
        ),
        cost_estimate=cost(80),
        name="start",
    )(lengths, order, tok, *weights, *vectors)


def middle_stage(s, att, mask, tok, teach, vec, weights, keep, outs, first_done, outer_done):
    wo, wi, wu, slope = weights
    att_k, br_k, hl_k, il_k, act_k, ol_k = keep
    out, fg, sums, wide_sums = outs
    rows = att.shape[0]
    hidden = wi.shape[1]
    tile = 512
    rs = slice(s * rows, (s + 1) * rows)
    half = tok.shape[2] // 2
    out_bias, gain_one, shift_one, outer_bias, gain_two, shift_two = (
        vector_of(vec, row, half) for row in range(2, 8)
    )
    add = functools.partial(jnp.sum, axis=0, keepdims=True)

    def collect(target, value):
        if s == 0:
            target[...] = value
        else:
            target[...] += value

    att_k[rs, :] = att
    first_done[0]()
    first = tok[s].astype(F32) + dot(att, wo[...]) + out_bias
    normed_one, inverse_one = norm(first)
    hidden_in = normed_one * gain_one + shift_one
    hl = hidden_in.astype(BF16)
    hl_k[rs, :] = hl
    first_done[1]()
    second = hidden_in + outer_bias
    for n in range(hidden // tile):
        cols = slice(n * tile, (n + 1) * tile)
        k, begin = divmod(n * tile, hidden // 2)
        inner = dot(hl, wi[:, cols]) + vec[k, 0:1, begin : begin + tile].astype(F32)
        below, density = normal_parts(inner)
        act = (inner * below).astype(BF16)
        act_k[rs, cols] = act
        slope[:, cols] = below + inner * density
        second += dot(act, wu[cols, :])
    normed_two, inverse_two = norm(second)
    final = normed_two * gain_two + shift_two
    out[s] = final.astype(BF16)
    residue = (final - teach[s].astype(F32)) * mask
    collect(sums.at[0:1], add(residue * normed_two))
    collect(sums.at[1:2], add(residue))
    collect(sums.at[6:7], add(residue * residue))
    second_grad = norm_back(residue * gain_two, normed_two, inverse_two)
    ol = second_grad.astype(BF16)
    ol_k[rs, :] = ol
    collect(sums.at[2:3], add(ol.astype(F32)))
    outer_done()
    hidden_grad = second_grad
    for n in range(hidden // tile):
        cols = slice(n * tile, (n + 1) * tile)
        il = (dot(ol, wu[cols, :], NT) * slope[:, cols]).astype(BF16)
        il_k[rs, cols] = il
        collect(wide_sums.at[0:1, cols], add(il.astype(F32)))
        hidden_grad += dot(il, wi[:, cols], NT)
    first_grad = norm_back(hidden_grad * gain_one, normed_one, inverse_one)
    fg[s] = first_grad
    br = first_grad.astype(BF16)
    br_k[rs, :] = br
    collect(sums.at[3:4], add(hidden_grad * normed_one))
    collect(sums.at[4:5], add(hidden_grad))
    collect(sums.at[5:6], add(br.astype(F32)))
    return dot(br, wo[...], NT).astype(BF16)


def middle_kernel(seqs, lengths, order, tok, teach, vec, *refs):
    sc = Counts(lengths, order)
    attended, weights, refs = refs[:seqs], refs[seqs : seqs + 6], refs[seqs + 6 :]
    out, fg, sums, wide_sums, a_own, a_give, b_own, b_give = refs[:8]
    grads_in, refs = refs[8 : 8 + seqs], refs[8 + seqs :]
    wo, wi, wu, slope, o_in, g_out, att_k, br_k, hl_k, il_k, act_k, ol_k = refs[:12]
    own, given, w_sem, o_sem, g_sem, c_sem = refs[12:]
    z, y, c, x = position()
    sibling = device(z, y, 1 - c, x)
    line = [None] + [device(z ^ d, y, c, x) for d in range(1, GROUPS)]
    greet([sibling] + line[1:])
    coming, going = {}, {}
    for s in range(seqs):
        if s == 0:
            coming[s, 0] = pltpu.make_async_copy(attended[s], o_in.at[s], o_sem.at[0, s, 0])
            coming[s, 0].start()
            continue
        for d in range(1, GROUPS):
            sems = o_sem.at[0, s, d], o_sem.at[1, s, d]
            coming[s, d] = send(attended[s].at[z ^ d], o_in.at[s, z], sems, line[d])
        coming[s, 0] = pltpu.make_async_copy(attended[s].at[z], o_in.at[s, z], o_sem.at[0, s, 0])
        coming[s, 0].start()
    copies = [
        half_copies(full, *weights[2 * i : 2 * i + 2], w_sem, 2 * i)
        for i, full in enumerate((wo, wi, wu))
    ]
    for group in copies:
        for copy in group:
            copy.start()

    def loaded(which):
        for i in which:
            for copy in copies[i]:
                copy.wait()

    half = wo.shape[0] // 2
    blocks = wi.shape[1] // (2 * half)
    base = (1 + blocks) * half
    core = []

    def store(k, start, value):
        low_value = value.astype(BF16)
        own[0, k, start : start + half, :] = low_value[:, :half]
        own[1, k, start : start + half, :] = low_value[:, half:]

    def pass_core(k, start, stop):
        place = pl.ds(start, stop - start)
        i = len(core)
        sems = c_sem.at[0, i], c_sem.at[1, i]
        core.append(send(own.at[1 - c, k, place], given.at[k, place], sems, sibling))

    def outer_grads():
        for k in range(2):
            for t in range(blocks):
                rows_of = slice((k * blocks + t) * half, (k * blocks + t + 1) * half)
                store(k, base + t * half, dot(act_k[:, rows_of], ol_k[...], TN))
            pass_core(k, base, base + blocks * half)

    rows = tok.shape[1]
    per = o_in.shape[3]
    for s in range(seqs):
        for d in range(GROUPS if s > 0 else 1):
            coming[s, d].wait()
        att = jnp.concatenate([o_in[s, g] for g in range(GROUPS)], 1)
        mask = valid_rows(sc, s, rows)
        waits = (lambda: loaded([0]), lambda: loaded([1, 2])) if s == 0 else (lambda: None,) * 2
        found = middle_stage(
            s,
            att,
            mask,
            tok,
            teach,
            vec,
            (wo, wi, wu, slope),
            (att_k, br_k, hl_k, il_k, act_k, ol_k),
            (out, fg, sums, wide_sums),
            waits,
            outer_grads if s == seqs - 1 else lambda: None,
        )
        for g in range(GROUPS):
            g_out[s, g] = found[:, g * per : (g + 1) * per]
        for d in range(1, GROUPS):
            sems = g_sem.at[0, s, d], g_sem.at[1, s, d]
            going[s, d] = send(g_out.at[s, z ^ d], grads_in[s].at[z], sems, line[d])
        going[s, 0] = pltpu.make_async_copy(g_out.at[s, z], grads_in[s].at[z], g_sem.at[0, s, 0])
        going[s, 0].start()
    sums[7:8, :] = jnp.zeros((1, sums.shape[1]), F32)

    for k in range(2):
        ks = slice(k * half, (k + 1) * half)
        store(k, 0, dot(att_k[:, ks], br_k[...], TN))
        for t in range(blocks):
            cols = slice(2 * t * half, 2 * (t + 1) * half)
            store(k, (1 + t) * half, dot(hl_k[:, ks], il_k[:, cols], TN))
        pass_core(k, 0, base)
    for copy in core:
        copy.wait()
    mine = own.at[c]
    cut, b_half = a_own.shape[0], b_own.shape[1]
    a_own[...] = add_low(mine[x, 0:cut], given[x, 0:cut])
    a_give[...] = add_low(mine[1 - x, 0:cut], given[1 - x, 0:cut])
    for k in range(2):
        for target, which in ((b_own, y), (b_give, 1 - y)):
            part = pl.ds(pl.multiple_of(cut + which * b_half, 16), b_half)
            target[k] = add_low(mine[k, part], given[k, part])
    for copy in going.values():
        copy.wait()


def cut_of(total):
    return total // 256 * 128


def middle(lengths, order, tok, teach, vec, attended, weights):
    seqs, rows, width = tok.shape
    hidden = 2 * vec.shape[2]
    half = width // 2
    total = half + hidden
    cut = cut_of(total)
    dma = pltpu.SemaphoreType.DMA
    narrow, wide = (seqs * rows, width), (seqs * rows, hidden)
    b_shape = jax.ShapeDtypeStruct((2, (total - cut) // 2, half), BF16)
    a_shape = jax.ShapeDtypeStruct((cut, half), BF16)
    groups, _, per = attended[0].shape
    return pl.pallas_call(
        functools.partial(middle_kernel, seqs),
        out_shape=[
            jax.ShapeDtypeStruct(tok.shape, BF16),
            jax.ShapeDtypeStruct(tok.shape, F32),
            jax.ShapeDtypeStruct((8, width), F32),
            jax.ShapeDtypeStruct((1, hidden), F32),
            a_shape,
            a_shape,
            b_shape,
            b_shape,
        ]
        + [jax.ShapeDtypeStruct(a.shape, BF16) for a in attended],
        in_specs=[SMEM] * 2 + [VMEM] * 3 + [ANY] * (seqs + 6),
        out_specs=[VMEM] * 8 + [ANY] * seqs,
        scratch_shapes=[
            pltpu.VMEM((width, width), BF16),
            pltpu.VMEM((width, hidden), BF16),
            pltpu.VMEM((hidden, width), BF16),
            pltpu.VMEM((rows, hidden), F32),
            pltpu.VMEM((seqs, groups, rows, per), BF16),
            pltpu.VMEM((seqs, groups, rows, per), BF16),
            pltpu.VMEM(narrow, BF16),
            pltpu.VMEM(narrow, BF16),
            pltpu.VMEM(narrow, BF16),
            pltpu.VMEM(wide, BF16),
            pltpu.VMEM(wide, BF16),
            pltpu.VMEM(narrow, BF16),
            pltpu.VMEM((2, 2, total, half), BF16),
            pltpu.VMEM((2, total, half), BF16),
            dma((6,)),
            dma((2, seqs, groups)),
            dma((2, seqs, groups)),
            dma((2, 4)),
        ],
        compiler_params=pltpu.CompilerParams(
            vmem_limit_bytes=63 * 2**20, collective_id=3, has_side_effects=True
        ),
        cost_estimate=cost(60),
        name="middle",
    )(lengths, order, tok, teach, vec, *attended, *weights)


def finish_kernel(
    seqs, lengths, order, tok, fg, rq, rkv, dense_sums, wide_sums, ready, wq, wk, wv, others, *rest
):
    sc = Counts(lengths, order)
    tg, out, dense_out, small_out, *rest = rest
    full, grads, acc, from_core, from_x, from_y, from_z, res, vec, vec_in, dense_res = rest[:11]
    w_sems, sems, small_sems, d_sems, last_sem = rest[11:]
    z, y, c, x = position()
    sibling, beside, over = device(z, y, 1 - c, x), device(z, 1 - y, c, x), device(z, y, c, 1 - x)
    line = [None] + [device(z ^ d, y, c, x) for d in range(1, GROUPS)]
    greet([sibling, beside, over] + line[1:])

    a_half = cut_of(dense_res.shape[1]) // 2
    b_half = dense_res.shape[1] // 2 - a_half
    low_bit, high_bit = lax.rem(z, 2), z // 2
    dense_parts = ((0, a_half, y * a_half), (a_half // 4, b_half, 2 * a_half + y * b_half))

    def dense_rows(start, n):
        return dense_res.at[c, pl.ds(pl.multiple_of(start, 16), n)]

    def d_pair(k, i):
        return d_sems.at[0, k, i], d_sems.at[1, k, i]

    dense_flows = [None, None]

    def dense_step(i, k):
        start, n, base = dense_parts[i]
        if k > 0:
            dense_flows[i].wait()
        begin = base + (low_bit * (n // 2) if k < 2 else 0) + (high_bit * (n // 4) if k < 1 else 0)
        size = (n // 4, n // 2, n, 2 * n)[k]
        place = dense_rows(begin if k < 3 else 2 * a_half * i, size)
        if k == 0:
            place[...] = ready[start : start + size]
        to = (line[2], line[1], beside, sibling)[k]
        dense_flows[i] = send(place, place, d_pair(k, i), to)

    dense_step(0, 0)
    rows, width = tok.shape[1:]
    heads = width // GROUPS // DH
    copies = []
    for i, own in enumerate((wq, wk, wv)):
        copies += half_copies(full.at[i], own, others.at[i], w_sems, 2 * i)
    for copy in copies:
        copy.start()

    def head(i, s, g, h):
        if i == 0:
            return rq[h, g, :, s * DH : (s + 1) * DH]
        return rkv[h * seqs + s, g, :, (i - 1) * DH : i * DH]

    def whole(i):
        each = [
            jnp.concatenate([head(i, s, g, h) for g in range(GROUPS) for h in range(heads)], 1)
            for s in range(seqs)
        ]
        return jnp.concatenate(each, 0)

    valid = jnp.concatenate([valid_rows(sc, s, rows) for s in range(seqs)], 0) > 0.0
    parted = [whole(0)] + [jnp.where(valid, whole(i), jnp.zeros((), BF16)) for i in (1, 2)]
    flat = tok[...].reshape(seqs * rows, width)
    wide = width // 2
    for i, grad in enumerate(parted):
        found = dot(flat, grad, TN).astype(BF16)
        for n in range(2):
            for t in range(width // 128):
                grads[t % 3, t // 3, n, i * wide : (i + 1) * wide, :] = found[
                    n * wide : (n + 1) * wide, t * 128 : (t + 1) * 128
                ]
    lines_of = [dense_sums[i : i + 1, :] for i in range(7)]
    lines_of += [jnp.sum(grad.astype(F32), 0, keepdims=True) for grad in (parted[0], parted[2])]
    lines_of.append(wide_sums[...])
    row = 0
    for one in lines_of:
        for t in range(one.shape[1] // 128):
            vec[row : row + 1, :] = one[:, t * 128 : (t + 1) * 128]
            row += 1
    valid_count = sum(jnp.clip(sc[i], 0, BLK) for i in range(2 * seqs))
    vec[row:, :] = jnp.full((vec.shape[0] - row, 128), valid_count.astype(F32))

    parts, rows_each = grads.shape[0], grads.shape[3]
    half, piece = rows_each // 2, rows_each // 8
    own_half = pl.ds(pl.multiple_of(y * half, half), half)
    other_half = pl.ds(pl.multiple_of((1 - y) * half, half), half)

    def piece_of(g):
        return pl.ds(pl.multiple_of(y * half + g * piece, piece), piece)

    def pair(k, p):
        return sems.at[0, k, p], sems.at[1, k, p]

    def small_pair(k):
        return small_sems.at[0, k], small_sems.at[1, k]

    core = [
        send(grads.at[p, 1 - c], from_core.at[p], pair(0, p), sibling) for p in range(parts)
    ]
    short = send(vec, vec_in.at[0], small_pair(0), sibling)
    flows, lines, spread = {}, {}, {}

    def from_pair(p):
        core[p].wait()
        acc[p] = add_low(grads[p, c], from_core[p])

    def x_send(p):
        if p == 1:
            flows[p] = send(acc.at[p, 1 - x, own_half], from_x.at[p, own_half], pair(2, p), over)
        else:
            flows[p] = send(acc.at[p, 1 - x], from_x.at[p], pair(1, p), over)

    def x_add(p):
        flows[p].wait()
        if p == 1:
            acc[p, x, own_half] = add_low(acc[p, x, own_half], from_x[p, own_half])
        else:
            acc[p, x] = add_low(acc[p, x], from_x[p])

    def y_send(p):
        if p == 1:
            flows[p] = send(acc.at[p, :, other_half], from_y.at[p], pair(1, p), beside)
        else:
            flows[p] = send(acc.at[p, x, other_half], from_y.at[p, 0], pair(2, p), beside)

    def y_add(p):
        flows[p].wait()
        if p == 1:
            for k in range(2):
                acc[p, k, own_half] = add_low(acc[p, k, own_half], from_y[p, k])
        else:
            acc[p, x, own_half] = add_low(acc[p, x, own_half], from_y[p, 0])

    def z_send(p):
        for d in range(1, GROUPS):
            lines[p, d] = send(
                acc.at[p, x, piece_of(z ^ d)], from_z.at[p, d], pair(2 + d, p), line[d]
            )

    def z_add(p):
        total = acc[p, x, piece_of(z)].astype(F32)
        for d in range(1, GROUPS):
            lines[p, d].wait()
            total += from_z[p, d].astype(F32)
        place = res.at[c, p, piece_of(z)]
        place[...] = total.astype(BF16)
        for d in range(1, GROUPS):
            spread[p, d] = send(place, place, pair(5 + d, p), line[d])

    def y_gather(p):
        for d in range(1, GROUPS):
            spread[p, d].wait()
        place = res.at[c, p, own_half]
        flows[p] = send(place, place, pair(9, p), beside)

    def core_gather(p):
        flows[p].wait()
        flows[p] = send(res.at[c, p], res.at[c, p], pair(10, p), sibling)

    from_pair(0)
    x_send(0)
    from_pair(1)
    y_send(1)
    from_pair(2)
    short.wait()
    vec_in[8] = vec[...] + vec_in[0]
    short = send(vec_in.at[8], vec_in.at[1], small_pair(1), over)
    dense_step(0, 1)
    dense_step(1, 0)
    for copy in copies:
        copy.wait()
    total = jnp.concatenate([fg[s] for s in range(seqs)], 0)
    for i, grad in enumerate(parted):
        total += dot(grad, full[i], NT)
    tg[...] = total.reshape(seqs, rows, width)
    x_add(0)
    x_send(2)
    y_send(0)
    y_add(1)
    x_send(1)
    short.wait()
    vec[...] = vec_in[8] + vec_in[1]
    short = send(vec, vec_in.at[2], small_pair(2), beside)
    y_add(0)
    z_send(0)
    dense_step(0, 2)
    dense_step(1, 1)
    x_add(2)
    y_send(2)
    x_add(1)
    z_send(1)
    z_add(0)
    short.wait()
    vec[...] = vec[...] + vec_in[2]
    vec_in[4 + z] = vec[...]
    shorts = [
        send(vec, vec_in.at[4 + z], small_pair(2 + d), line[d]) for d in range(1, GROUPS)
    ]
    y_add(2)
    z_send(2)
    dense_step(1, 2)
    z_add(1)
    y_gather(0)
    z_add(2)
    dense_step(0, 3)
    y_gather(1)
    y_gather(2)
    for copy in shorts:
        copy.wait()
    small_out[...] = vec_in[4] + vec_in[5] + (vec_in[6] + vec_in[7])
    for p in range(parts):
        core_gather(p)
    dense_step(1, 3)
    for copy in dense_flows:
        copy.wait()
    done = [pltpu.make_async_copy(dense_res, dense_out, last_sem.at[1])]
    done[0].start()
    for p in (1, 0, 2):
        flows[p].wait()
    done.append(pltpu.make_async_copy(res, out, last_sem.at[0]))
    done[1].start()
    for copy in done:
        copy.wait()


def finish(lengths, order, tok, fg, rq, rkv, sums, wide_sums, ready, wq, wk, wv, others):
    seqs, _, width = tok.shape
    short = (-(-(9 * width + wide_sums.shape[1] + 128) // 1024) * 8, 128)
    parts, rows, lanes = 3, 3 * (width // 2), 128
    total, half = 8 * ready.shape[0], ready.shape[1]
    dma = pltpu.SemaphoreType.DMA
    return pl.pallas_call(
        functools.partial(finish_kernel, seqs),
        out_shape=[
            jax.ShapeDtypeStruct(tok.shape, F32),
            jax.ShapeDtypeStruct((2, parts, rows, lanes), BF16),
            jax.ShapeDtypeStruct((2, total, half), BF16),
            jax.ShapeDtypeStruct(short, F32),
        ],
        in_specs=[SMEM] * 2 + [VMEM] * 7 + [ANY] * 4,
        out_specs=[VMEM, ANY, ANY, VMEM],
        scratch_shapes=[
            pltpu.VMEM((3, width, width), BF16),
            pltpu.VMEM((parts, 2, 2, rows, lanes), BF16),
            pltpu.VMEM((parts, 2, rows, lanes), BF16),
            pltpu.VMEM((parts, 2, rows, lanes), BF16),
            pltpu.VMEM((parts, rows, lanes), BF16),
            pltpu.VMEM((parts, 2, rows // 2, lanes), BF16),
            pltpu.VMEM((parts, GROUPS, rows // 8, lanes), BF16),
            pltpu.VMEM((2, parts, rows, lanes), BF16),
            pltpu.VMEM(short, F32),
            pltpu.VMEM((9, *short), F32),
            pltpu.VMEM((2, total, half), BF16),
            dma((6,)),
            dma((2, 11, parts)),
            dma((2, 6)),
            dma((2, 4, 2)),
            dma((2,)),
        ],
        compiler_params=pltpu.CompilerParams(
            vmem_limit_bytes=63 * 2**20, collective_id=2, has_side_effects=True
        ),
        cost_estimate=cost(70),
        name="finish",
    )(lengths, order, tok, fg, rq, rkv, sums, wide_sums, ready, wq, wk, wv, others)


def unpack_kernel(qkv, total, small, *refs):
    outs, rows, loss, refs = refs[:6], refs[6:15], refs[15], refs[16:]
    narrow, inner, outer, sems = refs
    half = qkv.shape[2] // 3
    blocks = inner.shape[1] // (2 * half)
    copies = []

    def leave(src, i):
        copy = pltpu.make_async_copy(src, outs[i], sems.at[i])
        copy.start()
        copies.append(copy)

    for k in range(2):
        cols = slice(k * half, (k + 1) * half)
        outer[:, cols] = total[k, (1 + blocks) * half :].astype(F32)
    leave(outer, 5)
    for k in range(2):
        for t in range(blocks):
            cols = slice((2 * t + k) * half, (2 * t + k + 1) * half)
            inner[:, cols] = total[k, (1 + t) * half : (2 + t) * half].astype(F32)
    leave(inner, 4)
    for i in range(3):
        for k in range(2):
            for p in range(3):
                cols = slice((3 * k + p) * 128, (3 * k + p + 1) * 128)
                narrow[i, :, cols] = qkv[k, p, i * half : (i + 1) * half].astype(F32)
        leave(narrow.at[i], i)
    for k in range(2):
        narrow[3, :, k * half : (k + 1) * half] = total[k, 0:half].astype(F32)
    leave(narrow.at[3], 3)
    x = lax.axis_index("wa")
    tiles = 2 * half // 128
    starts = [tiles * i for i in (0, 1, 2, 3, 4, 5, 7, 8)] + [9 * tiles]
    for one, begin in zip(rows, starts):
        n = one.shape[0] // 128
        for t in range(n):
            one[t * 128 : (t + 1) * 128] = small[pl.ds(begin + x * n + t, 1), :][0]
    end = 9 * tiles + 2 * rows[8].shape[0] // 128
    squares = jnp.sum(small[6 * tiles : 7 * tiles, :], keepdims=True)
    loss[...] = squares / (small[end : end + 1, :1] * (2.0 * half))
    for copy in copies:
        copy.wait()


def unpack(qkv, total, small, hidden):
    half = total.shape[2]
    narrow = jax.ShapeDtypeStruct((half, 2 * half), F32)
    return pl.pallas_call(
        unpack_kernel,
        out_shape=[narrow] * 4
        + [
            jax.ShapeDtypeStruct((half, hidden), F32),
            jax.ShapeDtypeStruct((hidden // 2, 2 * half), F32),
        ]
        + [jax.ShapeDtypeStruct((half,), F32)] * 8
        + [jax.ShapeDtypeStruct((hidden // 2,), F32), jax.ShapeDtypeStruct((1, 1), F32)],
        in_specs=[VMEM] * 3,
        out_specs=[ANY] * 6 + [VMEM] * 10,
        scratch_shapes=[
            pltpu.VMEM((4, half, 2 * half), F32),
            pltpu.VMEM((half, hidden), F32),
            pltpu.VMEM((hidden // 2, 2 * half), F32),
            pltpu.SemaphoreType.DMA((6,)),
        ],
        compiler_params=ROOM,
        cost_estimate=cost(10),
        name="unpack",
    )(qkv, total, small)


def pick(table, index):
    places = jnp.arange(table.shape[0], dtype=jnp.int32)
    return jnp.sum(jnp.where(index[..., None] == places, table, 0), -1)


def shards(
    size,
    tokens,
    teacher,
    lengths,
    block_order,
    query_weight,
    query_bias,
    key_weight,
    value_weight,
    value_bias,
    out_weight,
    out_bias,
    gain_one,
    shift_one,
    inner_weight,
    inner_bias,
    outer_weight,
    outer_bias,
    gain_two,
    shift_two,
):
    seqs, rows, width = tokens.shape
    per_plane = size // GROUPS
    blocks_each = rows // BLK
    ctx, x = lax.axis_index("ctx"), lax.axis_index("wa")
    c, place = lax.rem(ctx, 2), lax.rem(ctx, per_plane)
    masks = [1 << b for b in reversed(range(per_plane.bit_length() - 1))]
    offsets = [0]
    for m in masks:
        offsets += [o ^ m for o in offsets]

    def across(value):
        return lax.ppermute(value, "wa", [(0, 1), (1, 0)])

    def flip(value, m):
        return lax.ppermute(value, "ctx", [(i, i ^ m) for i in range(size)])

    lines = [[g * per_plane + r for g in range(GROUPS)] for r in range(per_plane)]

    def turn(value):
        return lax.all_to_all(value, "ctx", 0, 0, axis_index_groups=lines)

    cores = [[i for i in range(size) if i % 2 == k] for k in range(2)]

    def paired(mine):
        sibling = flip(mine, 1)
        return jnp.where(c == 0, jnp.stack([mine, sibling]), jnp.stack([sibling, mine]))

    def reduced(grad):
        four = grad.reshape(2, 2, *grad.shape[1:])
        keep = lax.dynamic_index_in_dim(four, c, 1, False)
        give = lax.dynamic_index_in_dim(four, 1 - c, 1, False)
        keep = add_low(keep, flip(give, 1))
        mine = lax.dynamic_index_in_dim(keep, x, 0, False)
        mine = add_low(mine, across(lax.dynamic_index_in_dim(keep, 1 - x, 0, False)))
        return paired(lax.psum(mine, "ctx", axis_index_groups=cores))

    def reduced_dense(grad):
        four = grad.reshape(2, 2, *grad.shape[1:])
        keep = lax.dynamic_index_in_dim(four, c, 1, False)
        give = lax.dynamic_index_in_dim(four, 1 - c, 1, False)
        keep = add_low(keep, flip(give, 1))
        mine = lax.psum_scatter(
            keep.reshape(-1, keep.shape[-1]), "wa", scatter_dimension=0, tiled=True
        )
        return lax.psum(mine, "ctx", axis_index_groups=cores)

    vectors = (
        query_bias,
        value_bias,
        out_bias,
        gain_one,
        shift_one,
        outer_bias,
        gain_two,
        shift_two,
        inner_bias,
    )
    half, hidden = width // 2, 2 * inner_bias.shape[0]
    fused = per_plane == 4

    if fused:
        found = start(
            lengths,
            block_order,
            tokens,
            (query_weight, key_weight, value_weight, out_weight, inner_weight, outer_weight),
            vectors,
        )
        queries = [q.reshape(-1, BLK, q.shape[2]) for q in found[:seqs]]
        pieces = [[kv.reshape(-1, BLK, kv.shape[3])] for kv in found[seqs : 2 * seqs]]
        attended, lses = found[2 * seqs : 3 * seqs], found[3 * seqs : 4 * seqs]
        first_back, pair, others, *rest = found[4 * seqs :]
        dense_weights = [out_weight, rest[0], inner_weight, rest[1], outer_weight, rest[2]]
    else:
        count = block_order.shape[0]
        ids = jnp.arange(count, dtype=jnp.int32)
        owner = ids // blocks_each
        index_of = jnp.array([offsets.index(o) for o in range(per_plane)], jnp.int32)
        piece_of = pick(index_of, (owner % per_plane) ^ place)
        spot = (piece_of * GROUPS + owner // per_plane) * blocks_each + ids % blocks_each
        key_order = jnp.sum(jnp.where(block_order[None, :] == ids[:, None], spot[None, :], 0), 1)
        near = jnp.arange(GROUPS * blocks_each, dtype=jnp.int32)
        near_ids = (near // blocks_each * per_plane + place) * blocks_each + near % blocks_each
        near_pos = pick(block_order, near_ids)
        rank = jnp.sum((near_pos[None, :] < near_pos[:, None]).astype(jnp.int32), 1)
        query_order = jnp.sum(jnp.where(rank[None, :] == near[:, None], near[None, :], 0), 1)
        own_pos = pick(block_order, ctx * blocks_each + jnp.arange(blocks_each, dtype=jnp.int32))
        scalars, row_counts = [], []
        for s in range(seqs):
            used = jnp.sum((near_pos * BLK < lengths[s]).astype(jnp.int32))
            head = jnp.concatenate([lengths[s][None], used[None], jnp.zeros((6,), jnp.int32)])
            scalars.append(jnp.concatenate([head, query_order, key_order]))
            row_counts.append(jnp.clip(lengths[s] - own_pos * BLK, 0, BLK))

        counts = jnp.concatenate(row_counts)
        own_vec = jnp.concatenate(vectors)[None]
        other_vec = across(own_vec)
        pair = jnp.where(
            x == 0, jnp.stack([own_vec, other_vec]), jnp.stack([other_vec, own_vec])
        ).astype(F32)
        narrow = pair[:, 0, : 8 * half].reshape(2, 8, half).swapaxes(0, 1).reshape(8, width)
        wide_vec = pair[:, 0, 8 * half :].reshape(1, -1)

        def quarter(weight):
            n = weight.shape[0] // 2
            return lax.dynamic_slice_in_dim(weight, c * n, n, 0)

        first_qkv = across(
            jnp.concatenate([quarter(w) for w in (query_weight, key_weight, value_weight)], 0)
        )
        second_qkv = flip(first_qkv, 1)
        dense_weights = []
        last = first_qkv
        for weight in (out_weight, inner_weight, outer_weight):
            piece, last = lax.optimization_barrier((quarter(weight), last))
            last = across(piece)
            dense_weights += [weight, last, flip(last, 1)]

        projected = project(
            counts, tokens, narrow, query_weight, key_weight, value_weight, first_qkv, second_qkv
        )
        queries, pieces = [], []
        for s in range(seqs):
            kv = turn(projected[2 * s + 1])
            queries.append(turn(projected[2 * s]).reshape(-1, BLK, width // GROUPS))
            held = [kv.reshape(-1, BLK, kv.shape[2])]
            for m in masks:
                held += [flip(piece, m) for piece in held]
            pieces.append(held)

        attended, lses = [], []
        for s in range(seqs):
            o, lse = attend(s, per_plane, lengths, block_order, queries[s], pieces[s])
            attended.append(o.reshape(queries[s].shape))
            lses.append(lse)
    if fused:
        fours = [first_back, *attended[1:]]
        found = middle(lengths, block_order, tokens, teacher, pair, fours, dense_weights)
        output, firsts, sums, wide_sums, a_own, a_give, b_own, b_give = found[:8]
        heads_grad = [g.reshape(queries[0].shape) for g in found[8:]]
        ready = (a_own, a_give, b_own, b_give)
    else:
        dense_out = []
        for s in range(seqs):
            o4 = turn(attended[s].reshape(GROUPS, rows, -1))
            dense_out.append(
                dense(
                    row_counts[s], o4, tokens[s], teacher[s], narrow[2:], wide_vec, dense_weights
                )
            )
        output = jnp.stack([d[0] for d in dense_out])
        first_grads = [d[1] for d in dense_out]
        heads_grad = [turn(d[2]).reshape(queries[s].shape) for s, d in enumerate(dense_out)]
        sums = sum(d[9] for d in dense_out)
        wide_sums = sum(d[10] for d in dense_out)
        dense_sums = [reduced_dense(g) for g in dense_grads([d[3:9] for d in dense_out])]

    if fused:
        flat_rows = (GROUPS * rows, width // GROUPS)
        rq, rkv, ready = attend_back_all(
            [
                [
                    *(a.reshape(flat_rows) for a in (queries[s], heads_grad[s], attended[s])),
                    lses[s],
                    pieces[s][0].reshape(-1, pieces[s][0].shape[2]),
                ]
                for s in range(seqs)
            ],
            ready,
        )
    else:
        dqs, dkvs = [], []
        for s in range(seqs):
            found = attend_back(
                scalars[s], queries[s], heads_grad[s], attended[s], lses[s], pieces[s]
            )
            dqs.append(turn(found[0].reshape(GROUPS, rows, -1)))
            held = [piece.reshape(GROUPS, rows, -1) for piece in found[1:]]
            for m in reversed(masks):
                n = len(held) // 2
                held = [add_low(mine, flip(theirs, m)) for mine, theirs in zip(held[:n], held[n:])]
            dkvs.append(turn(held[0]))
        tokens_grad, g_qkv, sums_qkv = project_grads(
            counts,
            tokens,
            first_grads,
            dqs + dkvs,
            query_weight,
            key_weight,
            value_weight,
            first_qkv,
            second_qkv,
        )

    if fused:
        tokens_grad, qkv, total, small = finish(
            lengths,
            block_order,
            tokens,
            firsts,
            rq,
            rkv,
            sums,
            wide_sums,
            ready,
            query_weight,
            key_weight,
            value_weight,
            others,
        )
        grads = unpack(qkv, total, small, hidden)
        query_grad, key_grad, value_grad, out_grad, inner_grad, outer_grad = grads[:6]
        rows_of = dict(zip((0, 1, 2, 3, 4, 5, 7, 8, 9), grads[6:15]))
        loss = grads[15].reshape(())

        def vector(start, length):
            return rows_of[start // width]

    else:
        valid = jnp.full((128,), sum(jnp.sum(r) for r in row_counts).astype(F32))
        small = jnp.concatenate(
            [sums[:7].reshape(-1), sums_qkv[:2].reshape(-1), wide_sums[0], valid]
        )
        small = lax.psum(small, ("ctx", "wa"))
        qkv = reduced(jnp.moveaxis(g_qkv, (2, 1), (0, 1)).reshape(4, 3, -1, 128))
        out_grad, inner_grad, outer_grad = (
            paired(g).reshape(-1, g.shape[-1]).astype(F32) for g in dense_sums
        )
        qkv = qkv.reshape(6, 3, half, 128).astype(F32)
        query_grad, key_grad, value_grad = (
            qkv[:, i].swapaxes(0, 1).reshape(half, width) for i in range(3)
        )

        def vector(start, length):
            return lax.dynamic_slice_in_dim(small, start + x * (length // 2), length // 2, 0)

        loss = jnp.sum(small[6 * width : 7 * width]) / (small[9 * width + hidden] * width)

    end = 9 * width
    return (
        output,
        tokens_grad,
        query_grad,
        vector(7 * width, width),
        key_grad,
        value_grad,
        vector(8 * width, width),
        out_grad,
        vector(5 * width, width),
        vector(3 * width, width),
        vector(4 * width, width),
        inner_grad,
        vector(end, hidden),
        outer_grad,
        vector(2 * width, width),
        vector(0, width),
        vector(width, width),
        loss,
    )


def solution(mesh):
    row, split, both = P("wa"), P("wa", None), P("wa", "ctx", None)
    placed = (both, both, row, P(), split, row, split, split, row, split, row, row, row)
    placed += (split, row, split, row, row, row)
    return jax.shard_map(
        functools.partial(shards, mesh.shape["ctx"]),
        mesh=mesh,
        in_specs=placed,
        out_specs=(
            both,
            both,
            split,
            row,
            split,
            split,
            row,
            split,
            row,
            row,
            row,
            split,
            row,
            split,
            row,
            row,
            row,
            P(),
        ),
        check_vma=False,
    )
```

```python
import functools
import math

import jax
import jax.numpy as jnp
from jax import lax
from jax.experimental import pallas as pl
from jax.experimental.pallas import tpu as pltpu
from jax.sharding import PartitionSpec as P

DH = 64
BLK = 128
GROUPS = 4
LN2 = math.log(2.0)
NT = (((1,), (1,)), ((), ()))
NN = (((1,), (0,)), ((), ()))
TN = (((0,), (0,)), ((), ()))
F32 = jnp.float32
BF16 = jnp.bfloat16
VMEM = pl.BlockSpec(memory_space=pltpu.VMEM)
SMEM = pl.BlockSpec(memory_space=pltpu.SMEM)
ANY = pl.BlockSpec(memory_space=pl.ANY)
ROOM = pltpu.CompilerParams(vmem_limit_bytes=62 * 2**20)


def dot(left, right, dims=NN):
    return lax.dot_general(left, right, dims, preferred_element_type=F32)


def cost(us):
    return pl.CostEstimate(flops=int(us * 1.15e9), bytes_accessed=1 << 20, transcendentals=0)


def weight_copies(full, own, first, second, sems, base):
    x, c = lax.axis_index("wa"), lax.rem(lax.axis_index("ctx"), 2)
    half = own.shape[0]
    quarter = half // 2
    other = (1 - x) * half
    places = (
        (own, x * half, half),
        (first, other + c * quarter, quarter),
        (second, other + (1 - c) * quarter, quarter),
    )
    return [
        pltpu.make_async_copy(
            src, full.at[pl.ds(pl.multiple_of(start, quarter), size)], sems.at[base + i]
        )
        for i, (src, start, size) in enumerate(places)
    ]


class Counts:
    def __init__(self, lengths, order):
        self.lengths, self.order = lengths, order

    def __getitem__(self, i):
        place = 2 * lax.axis_index("ctx") + i % 2
        return self.lengths[i // 2] - self.order[place] * BLK


def valid_rows(sc, s, rows):
    row = lax.broadcasted_iota(jnp.int32, (rows, 1), 0)
    first = jnp.where(row < sc[2 * s], 1.0, 0.0)
    later = jnp.where(row - BLK < sc[2 * s + 1], 1.0, 0.0)
    return jnp.where(row < BLK, first, later)


def half_copies(full, own, other, sems, base):
    x, half = lax.axis_index("wa"), own.shape[0]
    return [
        pltpu.make_async_copy(
            src, full.at[pl.ds(pl.multiple_of(k * half, half), half)], sems.at[base + i]
        )
        for i, (src, k) in enumerate(((own, x), (other, 1 - x)))
    ]


def project_kernel(sc, tok, vec, wq, wk, wv, first, second, *rest):
    seqs, rows, width = tok.shape
    outs, (full, sems) = rest[: 2 * seqs], rest[2 * seqs :]
    quarter = wq.shape[0] // 2
    copies = []
    for i, own in enumerate((wq, wk, wv)):
        part = pl.ds(i * quarter, quarter)
        copies.append(
            weight_copies(full.at[i], own, first.at[part], second.at[part], sems, 3 * i)
        )
    for group in copies:
        for copy in group:
            copy.start()
    flat = tok[...].reshape(seqs * rows, width)
    per = width // GROUPS
    heads = per // DH
    valid = jnp.concatenate([valid_rows(sc, s, rows) for s in range(seqs)], 0) > 0.0
    for copy in copies[1]:
        copy.wait()
    keys = jnp.where(valid, dot(flat, full[1]), 0.0).astype(BF16)
    for copy in copies[2]:
        copy.wait()
    values = jnp.where(valid, dot(flat, full[2]) + vec[1:2, :], 0.0).astype(BF16)
    for s in range(seqs):
        rs = slice(s * rows, (s + 1) * rows)
        for g in range(GROUPS):
            for h in range(heads):
                cols = slice(g * per + h * DH, g * per + (h + 1) * DH)
                outs[2 * s + 1][g, :, h * 128 : (h + 1) * 128] = jnp.concatenate(
                    [keys[rs, cols], values[rs, cols]], 1
                )
    for copy in copies[0]:
        copy.wait()
    queries = ((dot(flat, full[0]) + vec[0:1, :]) * (DH**-0.5 / LN2)).astype(BF16)
    for s in range(seqs):
        rs = slice(s * rows, (s + 1) * rows)
        for g in range(GROUPS):
            outs[2 * s][g] = queries[rs, g * per : (g + 1) * per]


def project(sc, tok, vec, wq, wk, wv, first, second):
    seqs, rows, width = tok.shape
    per = width // GROUPS
    shapes = [
        jax.ShapeDtypeStruct((GROUPS, rows, n), BF16) for _ in range(seqs) for n in (per, 2 * per)
    ]
    return pl.pallas_call(
        project_kernel,
        out_shape=shapes,
        in_specs=[SMEM, VMEM, VMEM] + [ANY] * 5,
        out_specs=[VMEM] * len(shapes),
        scratch_shapes=[pltpu.VMEM((3, width, width), BF16), pltpu.SemaphoreType.DMA((9,))],
        compiler_params=ROOM,
        cost_estimate=cost(5),
        name="project",
    )(sc, tok, vec, wq, wk, wv, first, second)


def load_pieces(pieces, kv, sems):
    per = pieces[0].shape[0]
    copies = [
        pltpu.make_async_copy(piece, kv.at[pl.ds(i * per, per)], sems.at[i])
        for i, piece in enumerate(pieces)
    ]
    for copy in copies:
        copy.start()
    for copy in copies:
        copy.wait()


def forward_kernel(wide, narrow, count, s, per_plane, lengths, order, q_ref, *rest):
    pieces, rest = rest[:count], rest[count:]
    o_ref, lse_ref, kv_ref, qa, acc, sums, spots, sems = rest
    blocks = q_ref.shape[0]
    heads = q_ref.shape[2] // DH
    rows = blocks * BLK
    length = lengths[s]
    place = lax.rem(lax.axis_index("ctx"), per_plane)

    def put(b, _):
        owner = b // 2
        offset = lax.bitwise_xor(lax.rem(owner, per_plane), place)
        piece = 0
        for bit in range(per_plane.bit_length() - 1):
            piece = 2 * piece + lax.rem(lax.div(offset, 1 << bit), 2)
        spots[order[b]] = (piece * GROUPS + lax.div(owner, per_plane)) * 2 + lax.rem(b, 2)
        return 0

    lax.fori_loop(0, order.shape[0], put, 0)
    load_pieces(pieces, kv_ref, sems)

    def gather(h, start, n):
        return jnp.concatenate(
            [kv_ref[spots[start + i], :, h * 128 : (h + 1) * 128] for i in range(n)], 0
        )

    whole = length // (wide * BLK)
    tail = whole * wide
    tails = (length - tail * BLK + narrow * BLK - 1) // (narrow * BLK)
    for h in range(heads):
        hs = slice(h * DH, (h + 1) * DH)
        own = jnp.concatenate([q_ref[b, :, hs] for b in range(blocks)], 0)
        qa[...] = jnp.concatenate([own, jnp.zeros_like(own)], 1)
        acc[...] = jnp.zeros_like(acc)
        sums[...] = jnp.zeros_like(sums)

        def step(start, n, masked, h=h):
            kv = gather(h, start, n)
            scores = dot(qa[...], kv, NT)
            if masked:
                place = lax.broadcasted_iota(jnp.int32, scores.shape, 1) + start * BLK
                scores = jnp.where(place < length, scores, -1e30)
            p = jnp.exp2(scores)
            sums[...] += sum(p[:, i * 128 : (i + 1) * 128] for i in range(n))
            acc[...] += dot(p.astype(BF16), kv)

        def wide_step(j, _, step=step):
            step(j * wide, wide, False)
            return 0

        def narrow_step(j, _, step=step):
            step(tail + j * narrow, narrow, True)
            return 0

        lax.fori_loop(0, whole, wide_step, 0)
        lax.fori_loop(0, tails, narrow_step, 0)
        total = jnp.sum(sums[...], 1, keepdims=True)
        across = jnp.transpose(jnp.broadcast_to(total, (rows, 128)))[:8]
        good = (jnp.min(across) > 2.0**-80) & (jnp.max(across) < 2.0**100)

        @pl.when(good)
        def _(h=h, hs=hs, total=total, across=across):
            lse_ref[h] = jnp.log2(across)
            o_ref[:, hs] = (acc[:, DH:] * (1.0 / total)).astype(BF16)

        @pl.when(jnp.logical_not(good))
        def _(h=h, hs=hs):
            key_blocks = (length + BLK - 1) // BLK

            def rows_step(t, _):
                part = pl.ds(pl.multiple_of(t * BLK, BLK), BLK)
                q = qa[part, :]

                def scores_of(j):
                    kv = gather(h, j, 1)
                    scores = dot(q, kv, NT)
                    place = lax.broadcasted_iota(jnp.int32, scores.shape, 1) + j * BLK
                    return kv, jnp.where(place < length, scores, -1e30)

                largest = lax.fori_loop(
                    0,
                    key_blocks,
                    lambda j, m: jnp.maximum(m, jnp.max(scores_of(j)[1], 1, keepdims=True)),
                    jnp.full((BLK, 1), -1e30, F32),
                )
                acc[part, :] = jnp.zeros((BLK, 128), F32)
                sums[part, :] = jnp.zeros((BLK, 128), F32)

                def add(j, _):
                    kv, scores = scores_of(j)
                    p = jnp.exp2(scores - largest)
                    sums[part, :] += p
                    acc[part, :] += dot(p.astype(BF16), kv)
                    return 0

                lax.fori_loop(0, key_blocks, add, 0)
                row_total = jnp.sum(sums[part, :], 1, keepdims=True)
                lse = largest + jnp.log2(row_total)
                lse_ref[h, :, part] = jnp.transpose(jnp.broadcast_to(lse, (BLK, 128)))[:8]
                o_ref[part, hs] = (acc[part, :][:, DH:] * (1.0 / row_total)).astype(BF16)
                return 0

            lax.fori_loop(0, rows // BLK, rows_step, 0)


def attend(s, per_plane, lengths, order, q, pieces):
    blocks, _, per = q.shape
    rows, heads = blocks * BLK, per // DH
    key_blocks = len(pieces) * pieces[0].shape[0]
    return pl.pallas_call(
        functools.partial(forward_kernel, 8, 2, len(pieces), s, per_plane),
        out_shape=(
            jax.ShapeDtypeStruct((rows, per), BF16),
            jax.ShapeDtypeStruct((heads, 8, rows), F32),
        ),
        in_specs=[SMEM, SMEM, VMEM] + [ANY] * len(pieces),
        out_specs=(VMEM, VMEM),
        scratch_shapes=[
            pltpu.VMEM((key_blocks, BLK, 2 * per), BF16),
            pltpu.VMEM((rows, 128), BF16),
            pltpu.VMEM((rows, 128), F32),
            pltpu.VMEM((rows, 128), F32),
            pltpu.SMEM((key_blocks,), jnp.int32),
            pltpu.SemaphoreType.DMA((len(pieces),)),
        ],
        compiler_params=ROOM,
        cost_estimate=cost(20),
        name="attend",
    )(lengths, order, q, *pieces)


def backward_kernel(qn, kn, count, sc, q_ref, do_ref, o_ref, lse_ref, *rest):
    pieces, dq_ref, outs = rest[:count], rest[count], rest[count + 1 : 2 * count + 1]
    kv_ref, both, dkv, dq, lse_row, delta_row, sems = rest[2 * count + 1 :]
    blocks = q_ref.shape[0]
    heads = q_ref.shape[2] // DH
    key_blocks = kv_ref.shape[0]
    tile = qn * BLK
    length, used = sc[0], sc[1]
    whole = length // (kn * BLK)
    parts = (length + kn * BLK - 1) // (kn * BLK)
    tiles = (used + qn - 1) // qn
    ones = jnp.ones((8, DH), BF16)
    load_pieces(pieces, kv_ref, sems)
    for h in range(heads):
        hs = slice(h * DH, (h + 1) * DH)

        def clear(i, _):
            dkv[pl.ds(pl.multiple_of(i * 1024, 1024), 1024), :] = jnp.zeros((1024, 128), F32)
            return 0

        lax.fori_loop(0, key_blocks // 8, clear, 0)
        dq[...] = jnp.zeros_like(dq)

        def prepare(t, _, h=h, hs=hs):
            base = pl.multiple_of(t * (2 * tile), 2 * tile)
            start = pl.multiple_of(t * tile, tile)
            places = [sc[8 + t * qn + i] for i in range(qn)]
            q = jnp.concatenate([q_ref[s, :, hs] for s in places], 0)
            do = jnp.concatenate([do_ref[s, :, hs] for s in places], 0)
            o = jnp.concatenate([o_ref[s, :, hs] for s in places], 0)
            zero = jnp.zeros_like(q)
            both[pl.ds(base, tile), :] = jnp.concatenate([q, zero], 1)
            both[pl.ds(base + tile, tile), :] = jnp.concatenate([zero, do], 1)
            product = do.astype(F32) * o.astype(F32)
            high = product.astype(BF16)
            rest_of = (product - high.astype(F32)).astype(BF16)
            delta_row[:, pl.ds(start, tile)] = dot(ones, high, NT) + dot(ones, rest_of, NT)
            lse_row[:, pl.ds(start, tile)] = jnp.concatenate(
                [lse_ref[h, :, pl.ds(pl.multiple_of(s * BLK, BLK), BLK)] for s in places], 1
            )
            return 0

        lax.fori_loop(0, tiles, prepare, 0)

        def rows_step(t, _, h=h):
            base = pl.multiple_of(t * (2 * tile), 2 * tile)
            span = pl.ds(pl.multiple_of(t * tile, tile), tile)

            def step(j, masked):
                places = [sc[8 + blocks + j * kn + i] for i in range(kn)]
                kv = jnp.concatenate([kv_ref[s, :, h * 128 : (h + 1) * 128] for s in places], 0)
                b = both[pl.ds(base, 2 * tile), :]
                found = dot(kv, b, NT)
                p = jnp.exp2(found[:, :tile] - lse_row[:1, span])
                if masked:
                    place = lax.broadcasted_iota(jnp.int32, p.shape, 0) + j * (kn * BLK)
                    p = jnp.where(place < length, p, 0.0)
                ds = (p * (found[:, tile:] - delta_row[:1, span])).astype(BF16)
                grads = dot(jnp.concatenate([ds, p.astype(BF16)], 1), b)
                for i, s in enumerate(places):
                    dkv[pl.ds(pl.multiple_of(s * BLK, BLK), BLK), :] += grads[
                        i * BLK : (i + 1) * BLK
                    ]
                dq[span, :] += dot(ds, kv, TN)

            def whole_step(j, _):
                step(j, False)
                return 0

            lax.fori_loop(0, whole, whole_step, 0)

            @pl.when(parts > whole)
            def _():
                step(whole, True)

            return 0

        lax.fori_loop(0, tiles, rows_step, 0)
        for i in range(blocks):
            dq_ref[sc[8 + i], :, hs] = (
                dq[i * BLK : (i + 1) * BLK, :DH] * DH**-0.5
            ).astype(BF16)
        level = jnp.where(lax.broadcasted_iota(jnp.int32, (1, 128), 1) < DH, LN2, 1.0)
        per_piece = key_blocks // count
        for n, out in enumerate(outs):
            for i in range(per_piece):
                b = n * per_piece + i
                out[i, :, h * 128 : (h + 1) * 128] = (
                    dkv[b * BLK : (b + 1) * BLK, :] * level
                ).astype(BF16)


def attend_back(sc, q, do, o, lse, pieces):
    blocks, _, per = q.shape
    rows = blocks * BLK
    key_blocks = len(pieces) * pieces[0].shape[0]
    return pl.pallas_call(
        functools.partial(backward_kernel, 4, 4, len(pieces)),
        out_shape=[jax.ShapeDtypeStruct(q.shape, BF16)]
        + [jax.ShapeDtypeStruct(p.shape, BF16) for p in pieces],
        in_specs=[SMEM] + [VMEM] * 4 + [ANY] * len(pieces),
        out_specs=[VMEM] * (1 + len(pieces)),
        scratch_shapes=[
            pltpu.VMEM((key_blocks, BLK, 2 * per), BF16),
            pltpu.VMEM((2 * rows, 128), BF16),
            pltpu.VMEM((key_blocks * BLK, 128), F32),
            pltpu.VMEM((rows, 128), F32),
            pltpu.VMEM((8, rows), F32),
            pltpu.VMEM((8, rows), F32),
            pltpu.SemaphoreType.DMA((len(pieces),)),
        ],
        compiler_params=ROOM,
        cost_estimate=cost(45),
        name="attend_back",
    )(sc, q, do, o, lse, *pieces)


def norm(values):
    centered = values - jnp.mean(values, -1, keepdims=True)
    inverse = lax.rsqrt(jnp.mean(centered * centered, -1, keepdims=True) + 1e-6)
    return centered * inverse, inverse


def norm_back(upstream, normed, inverse):
    return inverse * (
        upstream
        - jnp.mean(upstream, -1, keepdims=True)
        - normed * jnp.mean(upstream * normed, -1, keepdims=True)
    )


def normal_parts(x):
    z = jnp.abs(x) * (0.5**0.5)
    bell = jnp.exp(-0.5 * x * x)
    t = 1.0 / (1.0 + 0.3275911 * z)
    poly = t * (
        0.254829592
        + t * (-0.284496736 + t * (1.421413741 + t * (-1.453152027 + t * 1.061405429)))
    )
    upper = 0.5 * poly * bell
    return jnp.where(x >= 0, 1.0 - upper, upper), bell * (2.0 * math.pi) ** -0.5


def dense_kernel(sc, att4, tok, teach, vec, wide_vec, *rest):
    weights, rest = rest[:9], rest[9:]
    outs, (wo, wi, wu, slope, sems) = rest[:11], rest[11:]
    out, fg, ag, att_o, br_o, hl_o, il_o, act_o, ol_o, sums, wide_sums = outs
    rows, width = tok.shape
    hidden = wi.shape[1]
    tile = 512
    copies = [
        weight_copies(full, *weights[3 * i : 3 * i + 3], sems, 3 * i)
        for i, full in enumerate((wo, wi, wu))
    ]
    for group in copies:
        for copy in group:
            copy.start()
    per = att4.shape[2]
    att = jnp.concatenate([att4[g] for g in range(GROUPS)], 1)
    att_o[...] = att
    row = lax.broadcasted_iota(jnp.int32, (rows, 1), 0)
    mask = jnp.where(
        row < BLK, jnp.where(row < sc[0], 1.0, 0.0), jnp.where(row - BLK < sc[1], 1.0, 0.0)
    )
    out_bias, gain_one, shift_one = vec[0:1, :], vec[1:2, :], vec[2:3, :]
    outer_bias, gain_two, shift_two = vec[3:4, :], vec[4:5, :], vec[5:6, :]
    for copy in copies[0]:
        copy.wait()
    first = tok[...].astype(F32) + dot(att, wo[...]) + out_bias
    normed_one, inverse_one = norm(first)
    hidden_in = normed_one * gain_one + shift_one
    hl = hidden_in.astype(BF16)
    hl_o[...] = hl
    for copy in copies[1] + copies[2]:
        copy.wait()
    second = hidden_in + outer_bias
    for n in range(hidden // tile):
        cols = slice(n * tile, (n + 1) * tile)
        inner = dot(hl, wi[:, cols]) + wide_vec[0:1, cols]
        below, density = normal_parts(inner)
        act = (inner * below).astype(BF16)
        act_o[:, cols] = act
        slope[:, cols] = below + inner * density
        second += dot(act, wu[cols, :])
    normed_two, inverse_two = norm(second)
    final = normed_two * gain_two + shift_two
    out[...] = final.astype(BF16)
    residue = (final - teach[...].astype(F32)) * mask
    add = functools.partial(jnp.sum, axis=0, keepdims=True)
    second_grad = norm_back(residue * gain_two, normed_two, inverse_two)
    ol = second_grad.astype(BF16)
    ol_o[...] = ol
    hidden_grad = second_grad
    for n in range(hidden // tile):
        cols = slice(n * tile, (n + 1) * tile)
        il = (dot(ol, wu[cols, :], NT) * slope[:, cols]).astype(BF16)
        il_o[:, cols] = il
        wide_sums[0:1, cols] = add(il.astype(F32))
        hidden_grad += dot(il, wi[:, cols], NT)
    first_grad = norm_back(hidden_grad * gain_one, normed_one, inverse_one)
    fg[...] = first_grad
    br = first_grad.astype(BF16)
    br_o[...] = br
    att_grad = dot(br, wo[...], NT).astype(BF16)
    for g in range(GROUPS):
        ag[g] = att_grad[:, g * per : (g + 1) * per]
    sums[0:1, :] = add(residue * normed_two)
    sums[1:2, :] = add(residue)
    sums[2:3, :] = add(ol.astype(F32))
    sums[3:4, :] = add(hidden_grad * normed_one)
    sums[4:5, :] = add(hidden_grad)
    sums[5:6, :] = add(br.astype(F32))
    sums[6:7, :] = add(residue * residue)
    sums[7:8, :] = jnp.zeros((1, width), F32)


def dense(sc, att4, tok, teach, vec, wide_vec, weights):
    rows, width = tok.shape
    hidden = wide_vec.shape[1]
    narrow = jax.ShapeDtypeStruct((rows, width), BF16)
    wide = jax.ShapeDtypeStruct((rows, hidden), BF16)
    return pl.pallas_call(
        dense_kernel,
        out_shape=[
            narrow,
            jax.ShapeDtypeStruct((rows, width), F32),
            jax.ShapeDtypeStruct(att4.shape, BF16),
            narrow,
            narrow,
            narrow,
            wide,
            wide,
            narrow,
            jax.ShapeDtypeStruct((8, width), F32),
            jax.ShapeDtypeStruct((1, hidden), F32),
        ],
        in_specs=[SMEM] + [VMEM] * 5 + [ANY] * 9,
        out_specs=[VMEM] * 11,
        scratch_shapes=[
            pltpu.VMEM((width, width), BF16),
            pltpu.VMEM((width, hidden), BF16),
            pltpu.VMEM((hidden, width), BF16),
            pltpu.VMEM((rows, hidden), F32),
            pltpu.SemaphoreType.DMA((9,)),
        ],
        compiler_params=ROOM,
        cost_estimate=cost(15),
        name="dense",
    )(sc, att4, tok, teach, vec, wide_vec, *weights)


def dense_grads_kernel(seqs, *refs):
    ins, (g_out, g_inner, g_outer) = refs[: 6 * seqs], refs[6 * seqs :]
    att, br, hl, il, act, ol = (
        jnp.concatenate([ins[6 * s + i][...] for s in range(seqs)], 0) for i in range(6)
    )
    for target, left, right in ((g_out, att, br), (g_inner, hl, il), (g_outer, act, ol)):
        rows = target.shape[1]
        for n in range(4):
            piece = left[:, n * rows : (n + 1) * rows]
            for t in range(right.shape[1] // 768):
                cols = slice(t * 768, (t + 1) * 768)
                target[n, :, cols] = dot(piece, right[:, cols], TN).astype(BF16)


def dense_grads(saved):
    seqs = len(saved)
    width, hidden = saved[0][0].shape[1], saved[0][3].shape[1]
    return pl.pallas_call(
        functools.partial(dense_grads_kernel, seqs),
        out_shape=[
            jax.ShapeDtypeStruct((4, width // 4, width), BF16),
            jax.ShapeDtypeStruct((4, width // 4, hidden), BF16),
            jax.ShapeDtypeStruct((4, hidden // 4, width), BF16),
        ],
        in_specs=[VMEM] * (6 * seqs),
        out_specs=[VMEM] * 3,
        compiler_params=ROOM,
        cost_estimate=cost(10),
        name="dense_grads",
    )(*[member for group in saved for member in group])


def project_grads_kernel(seqs, sc, tok, *refs):
    fgs, refs = refs[:seqs], refs[seqs:]
    grads_in, refs = refs[: 2 * seqs], refs[2 * seqs :]
    wq, wk, wv, first, second, tg, grads, sums, full, sems = refs
    rows, width = tok.shape[1:]
    per = width // GROUPS
    heads = per // DH
    quarter = wq.shape[0] // 2
    copies = []
    for i, own in enumerate((wq, wk, wv)):
        part = pl.ds(i * quarter, quarter)
        copies += weight_copies(full.at[i], own, first.at[part], second.at[part], sems, 3 * i)
    for copy in copies:
        copy.start()

    def head(i, s, g, h):
        if i == 0:
            return grads_in[s][g, :, h * DH : (h + 1) * DH]
        start = h * 128 + (i - 1) * DH
        return grads_in[seqs + s][g, :, start : start + DH]

    def whole(i):
        each = [
            jnp.concatenate([head(i, s, g, h) for g in range(GROUPS) for h in range(heads)], 1)
            for s in range(seqs)
        ]
        return jnp.concatenate(each, 0)

    valid = jnp.concatenate([valid_rows(sc, s, rows) for s in range(seqs)], 0) > 0.0
    dq = whole(0)
    halves = [jnp.where(valid, whole(i), jnp.zeros((), BF16)) for i in (1, 2)]
    flat = tok[...].reshape(seqs * rows, width)
    for copy in copies:
        copy.wait()
    total = jnp.concatenate([fgs[s][...] for s in range(seqs)], 0)
    for i, grad in enumerate((dq, *halves)):
        total += dot(grad, full[i], NT)
        found = dot(flat, grad, TN).astype(BF16)
        half = width // 2
        for n in range(2):
            for t in range(width // 128):
                grads[t % 3, t // 3, n, i * half : (i + 1) * half, :] = found[
                    n * half : (n + 1) * half, t * 128 : (t + 1) * 128
                ]
    tg[...] = total.reshape(seqs, rows, width)
    sums[0:1, :] = jnp.sum(dq.astype(F32), 0, keepdims=True)
    sums[1:2, :] = jnp.sum(halves[1].astype(F32), 0, keepdims=True)
    sums[2:8, :] = jnp.zeros((6, width), F32)


def project_grads(sc, tok, fgs, grads, wq, wk, wv, first, second):
    seqs, rows, width = tok.shape
    return pl.pallas_call(
        functools.partial(project_grads_kernel, seqs),
        out_shape=[
            jax.ShapeDtypeStruct(tok.shape, F32),
            jax.ShapeDtypeStruct((3, 2, 2, 3 * (width // 2), 128), BF16),
            jax.ShapeDtypeStruct((8, width), F32),
        ],
        in_specs=[SMEM] + [VMEM] * (1 + len(fgs) + len(grads)) + [ANY] * 5,
        out_specs=[VMEM] * 3,
        scratch_shapes=[pltpu.VMEM((3, width, width), BF16), pltpu.SemaphoreType.DMA((9,))],
        compiler_params=ROOM,
        cost_estimate=cost(10),
        name="project_grads",
    )(sc, tok, *fgs, *grads, wq, wk, wv, first, second)


MESH = pl.DeviceIdType.MESH


def position():
    ctx = lax.axis_index("ctx")
    return ctx // 4, lax.rem(ctx // 2, 2), lax.rem(ctx, 2), lax.axis_index("wa")


def device(z, y, c, x):
    return z * 4 + y * 2 + c, x


def greet(others):
    barrier = pltpu.get_barrier_semaphore()
    for other in others:
        pl.semaphore_signal(barrier, inc=1, device_id=other, device_id_type=MESH)
    pl.semaphore_wait(barrier, len(others))


def send(src, dst, sems, to):
    copy = pltpu.make_async_remote_copy(
        src_ref=src,
        dst_ref=dst,
        send_sem=sems[0],
        recv_sem=sems[1],
        device_id=to,
        device_id_type=MESH,
    )
    copy.start()
    return copy


def add_low(left, right):
    return (left.astype(F32) + right.astype(F32)).astype(BF16)


def back_kernel(seqs, *refs):
    per_seq = 5
    ins = [refs[per_seq * s : per_seq * (s + 1)] for s in range(seqs)]
    a_own, a_give, b_own, b_give, rq, rkv, dense_out, *refs = refs[per_seq * seqs :]
    q_v, do_v, o_v, lse_v, kv_v, both, dkv, dq, delta, obuf, qbuf = refs[:11]
    from_core, from_y, a_v, b_v, a_in, b_in, a2, b2, a2_in, b2_in = refs[11:21]
    az_in, bz_in, dres, in_sem, c_sem, y_sem, z_sem, q_sem, l_sem, x_sem, dz_sem = refs[21:]
    z, y, c, x = position()
    sibling, beside, over = device(z, y, 1 - c, x), device(z, 1 - y, c, x), device(z, y, c, 1 - x)
    line = [None] + [device(z ^ d, y, c, x) for d in range(1, GROUPS)]
    greet([sibling, beside, over] + line[1:])

    def pair(sems, *index):
        return sems.at[(0, *index)], sems.at[(1, *index)]

    flow = {}
    flow["a"] = send(a_give, a_in, pair(x_sem, 0), over)
    flow["b"] = send(b_give, b_in, pair(x_sem, 1), beside)
    loads = []
    for s in range(seqs):
        targets = [ref.at[s] for ref in (q_v, do_v, o_v, lse_v, kv_v)]
        group = [
            pltpu.make_async_copy(src, dst, in_sem.at[s, i])
            for i, (src, dst) in enumerate(zip(ins[s], targets))
        ]
        for copy in group:
            copy.start()
        loads.append(group)
    own_loads = [
        pltpu.make_async_copy(a_own, a_v, l_sem.at[0]),
        pltpu.make_async_copy(b_own, b_v, l_sem.at[1]),
    ]
    for copy in own_loads:
        copy.start()

    rows = q_v.shape[1]
    heads = q_v.shape[2] // DH
    keys = kv_v.shape[1]
    tile, ktile = rows // 2, 2048
    quarter = keys // 4
    chunk = quarter // GROUPS
    ones = jnp.ones((8, DH), BF16)
    level = jnp.where(lax.broadcasted_iota(jnp.int32, (1, 128), 1) < DH, LN2, 1.0)
    waits = []

    def group_rows(g):
        return pl.ds(pl.multiple_of(g * chunk, chunk), chunk)

    def core_stage(u):
        flow["c", u] = send(
            obuf.at[u, pl.ds(2 * quarter, 2 * quarter)], from_core.at[u], pair(c_sem, u), sibling
        )

    def y_stage(u):
        flow["c", u].wait()
        second = pl.ds(quarter, quarter)
        obuf[u, second] = add_low(obuf[u, second], from_core[u, second])
        flow["y", u] = send(obuf.at[u, second], from_y.at[u], pair(y_sem, u), beside)
        obuf[u, 0:quarter] = add_low(obuf[u, 0:quarter], from_core[u, 0:quarter])

    def z_stage(u):
        flow["y", u].wait()
        obuf[u, 0:quarter] = add_low(obuf[u, 0:quarter], from_y[u])
        for d in range(1, GROUPS):
            src = obuf.at[u, group_rows(z ^ d)]
            waits.append(send(src, rkv.at[u, z], pair(z_sem, u, d), line[d]))
        own = pltpu.make_async_copy(obuf.at[u, group_rows(z)], rkv.at[u, z], z_sem.at[0, u, 0])
        own.start()
        waits.append(own)

    def q_stage(h):
        for d in range(1, GROUPS):
            waits.append(send(qbuf.at[h, z ^ d], rq.at[h, z], pair(q_sem, h, d), line[d]))
        own = pltpu.make_async_copy(qbuf.at[h, z], rq.at[h, z], q_sem.at[0, h, 0])
        own.start()
        waits.append(own)

    a_half, b_half = a2.shape[1], b2.shape[1]

    def dense_second():
        for copy in own_loads:
            copy.wait()
        flow["a"].wait()
        for slot, which in ((0, y), (1, 1 - y)):
            part = pl.ds(pl.multiple_of(which * a_half, 16), a_half)
            a2[slot] = add_low(a_v[part, :], a_in[part, :])
        flow["a"] = send(a2.at[1], a2_in, pair(x_sem, 2), beside)
        flow["b"].wait()
        for slot, which in ((0, x), (1, 1 - x)):
            b2[slot] = add_low(b_v[which], b_in[which])
        flow["b"] = send(b2.at[1], b2_in, pair(x_sem, 3), over)

    low_bit, high_bit = lax.rem(z, 2), z // 2
    parts = (("a", a2, a2_in, az_in), ("b", b2, b2_in, bz_in))

    def rows_at(start, n):
        return pl.ds(pl.multiple_of(start, 16), n)

    def dense_third():
        for i, (name, held, arrived, landing) in enumerate(parts):
            flow[name].wait()
            held[0] = add_low(held[0], arrived[...])
            n = held.shape[1] // 2
            src = held.at[0, rows_at((1 - low_bit) * n, n)]
            flow[name] = send(src, landing.at[0:n], pair(dz_sem, i, 0), line[1])

    def dense_fourth():
        for i, (name, held, _, landing) in enumerate(parts):
            flow[name].wait()
            n = held.shape[1] // 2
            mine = rows_at(low_bit * n, n)
            held[0, mine] = add_low(held[0, mine], landing[0:n])
            src = held.at[0, rows_at(low_bit * n + (1 - high_bit) * (n // 2), n // 2)]
            flow[name] = send(src, landing.at[n : n + n // 2], pair(dz_sem, i, 1), line[2])

    def dense_fifth():
        base = 0
        for name, held, _, landing in parts:
            flow[name].wait()
            n = held.shape[1] // 2
            mine = rows_at(low_bit * n + high_bit * (n // 2), n // 2)
            dres[base : base + n // 2] = add_low(held[0, mine], landing[n : n + n // 2])
            base += n // 2

    units = [(h, s) for h in range(heads) for s in range(seqs)]
    slots = {}
    for u in range(len(units) - 1):
        slots.setdefault(2 * u + 3, []).append(functools.partial(y_stage, u))
        slots.setdefault(2 * u + 5, []).append(functools.partial(z_stage, u))
    slots.setdefault(5, []).append(dense_second)
    slots.setdefault(7, []).append(dense_third)
    slots.setdefault(9, []).append(dense_fourth)
    slots.setdefault(12, []).append(dense_fifth)

    for u, (h, s) in enumerate(units):
        hs = slice(h * DH, (h + 1) * DH)
        lanes = slice(h * 128, (h + 1) * 128)
        if h == 0:
            for copy in loads[s]:
                copy.wait()
        for n in range(2):
            for work in slots.get(2 * u + n, []):
                work()
            part = slice(n * tile, (n + 1) * tile)
            q, do, o = q_v[s, part, hs], do_v[s, part, hs], o_v[s, part, hs]
            zero = jnp.zeros_like(q)
            both[0:tile, :] = jnp.concatenate([q, zero], 1)
            both[tile : 2 * tile, :] = jnp.concatenate([zero, do], 1)
            product = do.astype(F32) * o.astype(F32)
            high = product.astype(BF16)
            remains = (product - high.astype(F32)).astype(BF16)
            delta[...] = dot(ones, high, NT) + dot(ones, remains, NT)
            dq[...] = jnp.zeros_like(dq)

            def step(j, _, u=u, s=s, h=h, n=n, part=part, lanes=lanes):
                span = pl.ds(pl.multiple_of(j * ktile, ktile), ktile)
                kv = kv_v[s, span, lanes]
                b = both[...]
                found = dot(kv, b, NT)
                p = jnp.exp2(jnp.minimum(found[:, :tile] - lse_v[s, h, 0:1, part], 1.0))
                ds = (p * (found[:, tile:] - delta[0:1, :])).astype(BF16)
                grads = dot(jnp.concatenate([ds, p.astype(BF16)], 1), b)
                if n == 0:
                    dkv[span, :] = grads
                else:
                    obuf[u, span, :] = ((dkv[span, :] + grads) * level).astype(BF16)
                dq[...] += dot(ds, kv, TN)
                return 0

            lax.fori_loop(0, keys // ktile, step, 0)
            found = (dq[:, :DH] * DH**-0.5).astype(BF16)
            for i in range(2):
                qbuf[h, 2 * n + i, :, s * DH : (s + 1) * DH] = found[
                    i * (tile // 2) : (i + 1) * (tile // 2)
                ]
        core_stage(u)
        if s == seqs - 1:
            q_stage(h)
    last = len(units) - 1
    for n in sorted(n for n in slots if n >= 2 * len(units)):
        for work in slots[n]:
            work()
    y_stage(last)
    z_stage(last)
    for copy in waits:
        copy.wait()
    done = pltpu.make_async_copy(dres, dense_out, l_sem.at[0])
    done.start()
    done.wait()


def attend_back_all(seqs_in, ready):
    seqs = len(seqs_in)
    q, _, _, lse, held = seqs_in[0]
    rows, per = q.shape
    heads = per // DH
    units = heads * seqs
    keys = held.shape[0]
    chunk = rows // GROUPS
    a, b = ready[0].shape, ready[2].shape
    a_half, b_half, half = a[0] // 2, b[1], a[1]
    dma = pltpu.SemaphoreType.DMA
    return pl.pallas_call(
        functools.partial(back_kernel, seqs),
        out_shape=[
            jax.ShapeDtypeStruct((heads, GROUPS, chunk, 128), BF16),
            jax.ShapeDtypeStruct((units, GROUPS, chunk, 128), BF16),
            jax.ShapeDtypeStruct(((a_half + b_half) // 4, half), BF16),
        ],
        in_specs=[ANY] * (5 * seqs + 4),
        out_specs=[ANY] * 3,
        scratch_shapes=[
            pltpu.VMEM((seqs, rows, per), BF16),
            pltpu.VMEM((seqs, rows, per), BF16),
            pltpu.VMEM((seqs, rows, per), BF16),
            pltpu.VMEM((seqs, *lse.shape), F32),
            pltpu.VMEM((seqs, keys, 2 * per), BF16),
            pltpu.VMEM((rows, 128), BF16),
            pltpu.VMEM((keys, 128), F32),
            pltpu.VMEM((rows // 2, 128), F32),
            pltpu.VMEM((8, rows // 2), F32),
            pltpu.VMEM((units, keys, 128), BF16),
            pltpu.VMEM((heads, GROUPS, chunk, 128), BF16),
            pltpu.VMEM((units, keys // 2, 128), BF16),
            pltpu.VMEM((units, keys // 4, 128), BF16),
            pltpu.VMEM(a, BF16),
            pltpu.VMEM(b, BF16),
            pltpu.VMEM(a, BF16),
            pltpu.VMEM(b, BF16),
            pltpu.VMEM((2, a_half, half), BF16),
            pltpu.VMEM((2, b_half, half), BF16),
            pltpu.VMEM((a_half, half), BF16),
            pltpu.VMEM((b_half, half), BF16),
            pltpu.VMEM((3 * a_half // 4, half), BF16),
            pltpu.VMEM((3 * b_half // 4, half), BF16),
            pltpu.VMEM(((a_half + b_half) // 4, half), BF16),
            dma((seqs, 5)),
            dma((2, units)),
            dma((2, units)),
            dma((2, units, GROUPS)),
            dma((2, heads, GROUPS)),
            dma((2,)),
            dma((2, 4)),
            dma((2, 2, 2)),
        ],
        compiler_params=pltpu.CompilerParams(
            vmem_limit_bytes=63 * 2**20, collective_id=1, has_side_effects=True
        ),
        cost_estimate=cost(120),
        name="attend_back_all",
    )(*[member for group in seqs_in for member in group], *ready)


def vector_of(vec, row, half):
    both = [vec[k, row + 1 : row + 2, :half].astype(F32) for k in range(2)]
    return jnp.concatenate(both, 1)


def start_kernel(seqs, lengths, order, tokens, wq, wk, wv, wo, wi, wu, *refs):
    sc = Counts(lengths, order)
    vectors, refs = refs[:9], refs[9:]
    q_out, kv_out, o_out, lse_out = (refs[i * seqs : (i + 1) * seqs] for i in range(4))
    refs = refs[4 * seqs :]
    back_out, vec_out, others, *dense_out = refs[:6]
    full, q_held, kv_held, vec, own_vec, tok, *refs = refs[6:]
    q_v, kv_v, o_v, lse_v, shade, qa, acc, sums, top, *sems = refs
    v_sem, wx_sem, wy_sem, wc_sem, l_sem, dx_sem, dc_sem, q_sem, z_sem, y_sem, c_sem = sems[:11]
    own_sem, b_sem = sems[11:]
    z, y, c, x = position()
    sibling, beside, over = device(z, y, 1 - c, x), device(z, 1 - y, c, x), device(z, y, c, 1 - x)
    line = [None] + [device(z ^ d, y, c, x) for d in range(1, GROUPS)]
    greet([sibling, beside, over] + line[1:])

    def pair(sem, *index):
        return sem.at[(0, *index)], sem.at[(1, *index)]

    waits = []
    half = wq.shape[0]
    eighth = half // 4

    def rows_of(which, cc, yy):
        start = which * half + (2 * cc + yy) * eighth
        return pl.ds(pl.multiple_of(start, 16), eighth)

    own_rows = pl.ds(pl.multiple_of((2 * c + y) * eighth, 16), eighth)
    tok_in = pltpu.make_async_copy(tokens, tok, l_sem.at[6])
    tok_in.start()
    flow = {}
    turns = (1, 2, 0)
    locals_of = []
    for i in turns:
        own = (wq, wk, wv)[i]
        flow["x", i] = send(
            own.at[own_rows], full.at[i, rows_of(x, c, y)], pair(wx_sem, i), over
        )
    for i in turns:
        own = (wq, wk, wv)[i]
        place = full.at[i, pl.ds(pl.multiple_of(x * half, half), half)]
        copy = pltpu.make_async_copy(own, place, l_sem.at[i])
        copy.start()
        locals_of.append(copy)
    own_vec[...] = jnp.zeros_like(own_vec)
    for i, one in enumerate(vectors):
        row = (i + 1) % len(vectors)
        own_vec[row : row + 1, : one.shape[0]] = one[...].astype(F32)[None].astype(BF16)
    vec[x] = own_vec[...]
    vec_flow = send(own_vec, vec.at[x], pair(v_sem), over)

    def after_x(i):
        flow["x", i].wait()
        got = full.at[i, rows_of(1 - x, c, y)]
        flow["y", i] = send(got, got, pair(wy_sem, i), beside)
        flow["c", i, 0] = send(got, got, pair(wc_sem, i, 0), sibling)

    def after_y(i):
        flow["y", i].wait()
        got = full.at[i, rows_of(1 - x, c, 1 - y)]
        flow["c", i, 1] = send(got, got, pair(wc_sem, i, 1), sibling)

    def after_core(i):
        flow["c", i, 0].wait()
        flow["c", i, 1].wait()

    rows, width = tok.shape[1:]
    per = width // GROUPS
    heads = per // DH
    tok_in.wait()
    flat = tok[...].reshape(seqs * rows, width)
    valid = jnp.concatenate([valid_rows(sc, s, rows) for s in range(seqs)], 0) > 0.0
    lane = lax.broadcasted_iota(jnp.int32, (8, BLK), 1)
    for piece, offset in enumerate((0, 2, 1, 3)):
        owner = lax.bitwise_xor(2 * y + c, offset)
        for g in range(GROUPS):
            for k in range(2):
                start_of = order[(4 * g + owner) * 2 + k] * BLK
                for s in range(seqs):
                    inside = lane + start_of < lengths[s]
                    cols = slice((2 * g + k) * BLK, (2 * g + k + 1) * BLK)
                    shade[s, piece, :, cols] = jnp.where(inside, 0.0, -1e30)
    after_x(1)
    after_x(2)
    after_y(1)
    after_x(0)
    dense_weights = (wo, wi, wu)
    for i, weight in enumerate(dense_weights):
        n = weight.shape[0] // 2
        part = pl.ds(pl.multiple_of(c * n, 16), n)
        flow["dx", i] = send(weight.at[part], dense_out[i].at[part], pair(dx_sem, i), over)
    after_y(2)
    vec_flow.wait()

    def bias(row):
        return vector_of(vec, row, half)

    for copy in locals_of:
        copy.wait()
    after_core(1)
    keys = jnp.where(valid, dot(flat, full[1]), 0.0).astype(BF16)
    after_y(0)
    after_core(2)
    values = jnp.where(valid, dot(flat, full[2]) + bias(1), 0.0).astype(BF16)
    for s in range(seqs):
        rs = slice(s * rows, (s + 1) * rows)
        for g in range(GROUPS):
            for h in range(heads):
                cols = slice(g * per + h * DH, g * per + (h + 1) * DH)
                kv_held[s, g, :, h * 128 : (h + 1) * 128] = jnp.concatenate(
                    [keys[rs, cols], values[rs, cols]], 1
                )

    def kv_sends(s):
        for d in range(1, GROUPS):
            flow["z", s, d] = send(
                kv_held.at[s, z ^ d], kv_v.at[s, 0, z], pair(z_sem, s, d), line[d]
            )

    def q_sends(s):
        for d in range(1, GROUPS):
            flow["q", s, d] = send(q_held.at[s, z ^ d], q_v.at[s, z], pair(q_sem, s, d), line[d])

    kv_sends(0)

    def pass_on(s, d, src):
        g = z ^ d
        flow["ky", s, d] = send(src, kv_v.at[s, 1, g], pair(y_sem, s, d), beside)
        flow["kc", s, d, 0] = send(src, kv_v.at[s, 2, g], pair(c_sem, s, d, 0), sibling)

    def pass_core(s, d):
        flow["ky", s, d].wait()
        got = kv_v.at[s, 1, z ^ d]
        flow["kc", s, d, 1] = send(got, kv_v.at[s, 3, z ^ d], pair(c_sem, s, d, 1), sibling)

    pass_on(0, 0, kv_held.at[0, z])
    after_core(0)
    queries = ((dot(flat, full[0]) + bias(0)) * (DH**-0.5 / LN2)).astype(BF16)
    for s in range(seqs):
        rs = slice(s * rows, (s + 1) * rows)
        for g in range(GROUPS):
            q_held[s, g] = queries[rs, g * per : (g + 1) * per]
    for i in range(3):
        place = full.at[i, pl.ds(pl.multiple_of((1 - x) * half, half), half)]
        copy = pltpu.make_async_copy(place, others.at[i], l_sem.at[3 + i])
        copy.start()
        waits.append(copy)
    copy = pltpu.make_async_copy(vec, vec_out, l_sem.at[7])
    copy.start()
    waits.append(copy)
    for s in range(seqs):
        kv_v[s, 0, z] = kv_held[s, z]
        q_v[s, z] = q_held[s, z]

    def arrive(s, d):
        flow["z", s, d].wait()
        pass_on(s, d, kv_v.at[s, 0, z ^ d])

    def own_and_core(s):
        for d in range(GROUPS):
            flow["kc", s, d, 0].wait()

    def dense_core(i):
        flow["dx", i].wait()
        n = dense_weights[i].shape[0] // 2
        got = dense_out[i].at[pl.ds(pl.multiple_of(c * n, 16), n)]
        waits.append(send(got, got, pair(dc_sem, i), sibling))

    def leave(src, dst, i):
        copy = pltpu.make_async_copy(src, dst, b_sem.at[i])
        copy.start()
        waits.append(copy)

    def attend_part(s, h, pieces):
        lanes = slice(h * 128, (h + 1) * 128)
        count, tile = GROUPS * rows, 1024

        def step(j, _):
            piece = pieces[0] + j * (pieces[1] - pieces[0])
            kv = kv_v[s, piece, :, :, lanes].reshape(count, 128)
            dark = shade[s, piece, 0:1, :]
            for n in range(count // tile):
                part = slice(n * tile, (n + 1) * tile)
                scores = dot(qa[h, part, :], kv, NT) + dark
                high = scores[:, :128]
                for i in range(1, count // 128):
                    high = jnp.maximum(high, scores[:, i * 128 : (i + 1) * 128])
                old = top[h, part, :]
                new = jnp.maximum(old, jnp.max(high, 1, keepdims=True))
                fade = jnp.exp2(old - new)
                each = [
                    jnp.exp2(scores[:, i * 128 : (i + 1) * 128] - new) for i in range(count // 128)
                ]
                sums[h, part, :] = sums[h, part, :] * fade + sum(each)
                p = jnp.concatenate([one.astype(BF16) for one in each], 1)
                acc[h, part, :] = acc[h, part, :] * fade + dot(p, kv)
                top[h, part, :] = new
            return 0

        lax.fori_loop(0, 2, step, 0)

    def attend_begin(s, h):
        hs = slice(h * DH, (h + 1) * DH)
        mine = q_v[s, :, :, hs].reshape(GROUPS * rows, DH)
        qa[h] = jnp.concatenate([mine, jnp.zeros_like(mine)], 1)
        zero = jnp.zeros(acc.shape[1:], F32)
        acc[h], sums[h], top[h] = zero, zero, zero - 1e30

    def attend_end(s, h):
        hs = slice(h * DH, (h + 1) * DH)
        total = jnp.sum(sums[h], 1, keepdims=True)
        logs = top[h] + jnp.log2(jnp.broadcast_to(total, top.shape[1:]))
        lse_v[s, h] = jnp.transpose(logs)[:8]
        found = (acc[h][:, DH:] * (1.0 / total)).astype(BF16)
        o_v[s, :, :, hs] = found.reshape(GROUPS, rows, DH)

    def leave_all(s):
        for i, (src, dst) in enumerate(
            ((q_v, q_out), (kv_v, kv_out), (o_v, o_out), (lse_v, lse_out))
        ):
            leave(src.at[s], dst[s], 4 * s + i)

    for d in range(1, GROUPS):
        arrive(0, d)
        if d > 1:
            pass_core(0, d - 2)
    q_sends(0)
    pass_core(0, 2)
    pass_core(0, 3)
    for d in range(1, GROUPS):
        flow["q", 0, d].wait()
    kv_sends(1)
    own_and_core(0)
    pass_on(1, 0, kv_held.at[1, z])
    for d in range(GROUPS):
        flow["kc", 0, d, 1].wait()
    for h in range(heads):
        attend_begin(0, h)
        attend_part(0, h, (0, 2))
        if h == 1:
            dense_core(0)
        if h == 2:
            pass_core(1, 0)
            q_sends(1)
            for d in range(1, GROUPS):
                arrive(1, d)
        attend_part(0, h, (1, 3))
        attend_end(0, h)
    leave_all(0)
    own_and_core(1)
    for d in range(1, GROUPS):
        flow["q", 1, d].wait()
    for d in range(1, GROUPS):
        waits.append(send(o_v.at[0, z ^ d], back_out.at[z], pair(own_sem, d), line[d]))
    leave(o_v.at[0, z], back_out.at[z], 4 * seqs)
    for h in range(heads):
        attend_begin(1, h)
        attend_part(1, h, (0, 2))
        pass_core(1, h + 1)
    dense_core(1)
    dense_core(2)
    for d in range(GROUPS):
        flow["kc", 1, d, 1].wait()
    for h in range(heads):
        attend_part(1, h, (1, 3))
        attend_end(1, h)
    leave_all(1)
    for copy in waits:
        copy.wait()


def start(lengths, order, tok, weights, vectors):
    seqs, rows, width = tok.shape
    per = width // GROUPS
    half = weights[0].shape[0]
    joined = (16, vectors[-1].shape[0])
    heads, total = per // DH, GROUPS * rows
    narrow = jax.ShapeDtypeStruct((GROUPS, rows, per), BF16)
    dma = pltpu.SemaphoreType.DMA
    return pl.pallas_call(
        functools.partial(start_kernel, seqs),
        out_shape=[narrow] * seqs
        + [jax.ShapeDtypeStruct((4, GROUPS, rows, 2 * per), BF16)] * seqs
        + [narrow] * seqs
        + [jax.ShapeDtypeStruct((heads, 8, total), F32)] * seqs
        + [
            narrow,
            jax.ShapeDtypeStruct((2, *joined), BF16),
            jax.ShapeDtypeStruct((3, half, width), BF16),
        ]
        + [jax.ShapeDtypeStruct(w.shape, BF16) for w in weights[3:]],
        in_specs=[SMEM] * 2 + [ANY] * 7 + [VMEM] * 9,
        out_specs=[ANY] * (4 * seqs + 6),
        scratch_shapes=[
            pltpu.VMEM((3, width, width), BF16),
            pltpu.VMEM((seqs, GROUPS, rows, per), BF16),
            pltpu.VMEM((seqs, GROUPS, rows, 2 * per), BF16),
            pltpu.VMEM((2, *joined), BF16),
            pltpu.VMEM(joined, BF16),
            pltpu.VMEM(tok.shape, BF16),
            pltpu.VMEM((seqs, GROUPS, rows, per), BF16),
            pltpu.VMEM((seqs, 4, GROUPS, rows, 2 * per), BF16),
            pltpu.VMEM((seqs, GROUPS, rows, per), BF16),
            pltpu.VMEM((seqs, heads, 8, total), F32),
            pltpu.VMEM((seqs, 4, 8, total), F32),
            pltpu.VMEM((heads, total, 128), BF16),
            pltpu.VMEM((heads, total, 128), F32),
            pltpu.VMEM((heads, total, 128), F32),
            pltpu.VMEM((heads, total, 128), F32),
            dma((2,)),
            dma((2, 3)),
            dma((2, 3)),
            dma((2, 3, 2)),
            dma((8,)),
            dma((2, 3)),
            dma((2, 3)),
            dma((2, seqs, GROUPS)),
            dma((2, seqs, GROUPS)),
            dma((2, seqs, GROUPS)),
            dma((2, seqs, GROUPS, 2)),
            dma((2, GROUPS)),
            dma((4 * seqs + 1,)),
        ],
        compiler_params=pltpu.CompilerParams(
            vmem_limit_bytes=63 * 2**20, collective_id=4, has_side_effects=True
        ),
        cost_estimate=cost(80),
        name="start",
    )(lengths, order, tok, *weights, *vectors)


def middle_stage(s, att, mask, tok, teach, vec, weights, keep, outs, first_done, outer_done):
    wo, wi, wu, slope = weights
    att_k, br_k, hl_k, il_k, act_k, ol_k = keep
    out, fg, sums, wide_sums = outs
    rows = att.shape[0]
    hidden = wi.shape[1]
    tile = 768
    rs = slice(s * rows, (s + 1) * rows)
    half = tok.shape[2] // 2
    out_bias, gain_one, shift_one, outer_bias, gain_two, shift_two = (
        vector_of(vec, row, half) for row in range(2, 8)
    )
    add = functools.partial(jnp.sum, axis=0, keepdims=True)

    def collect(target, value):
        if s == 0:
            target[...] = value
        else:
            target[...] += value

    att_k[rs, :] = att
    first_done[0]()
    first = tok[s].astype(F32) + dot(att, wo[...]) + out_bias
    normed_one, inverse_one = norm(first)
    hidden_in = normed_one * gain_one + shift_one
    hl = hidden_in.astype(BF16)
    hl_k[rs, :] = hl
    first_done[1]()
    second = hidden_in + outer_bias
    for n in range(hidden // tile):
        cols = slice(n * tile, (n + 1) * tile)
        k, begin = divmod(n * tile, hidden // 2)
        inner = dot(hl, wi[:, cols]) + vec[k, 0:1, begin : begin + tile].astype(F32)
        below, density = normal_parts(inner)
        act = (inner * below).astype(BF16)
        act_k[rs, cols] = act
        slope[:, cols] = below + inner * density
        second += dot(act, wu[cols, :])
    normed_two, inverse_two = norm(second)
    final = normed_two * gain_two + shift_two
    out[s] = final.astype(BF16)
    residue = (final - teach[s].astype(F32)) * mask
    collect(sums.at[0:1], add(residue * normed_two))
    collect(sums.at[1:2], add(residue))
    collect(sums.at[6:7], add(residue * residue))
    second_grad = norm_back(residue * gain_two, normed_two, inverse_two)
    ol = second_grad.astype(BF16)
    ol_k[rs, :] = ol
    collect(sums.at[2:3], add(ol.astype(F32)))
    outer_done()
    hidden_grad = second_grad
    for n in range(hidden // tile):
        cols = slice(n * tile, (n + 1) * tile)
        il = (dot(ol, wu[cols, :], NT) * slope[:, cols]).astype(BF16)
        il_k[rs, cols] = il
        collect(wide_sums.at[0:1, cols], add(il.astype(F32)))
        hidden_grad += dot(il, wi[:, cols], NT)
    first_grad = norm_back(hidden_grad * gain_one, normed_one, inverse_one)
    fg[s] = first_grad
    br = first_grad.astype(BF16)
    br_k[rs, :] = br
    collect(sums.at[3:4], add(hidden_grad * normed_one))
    collect(sums.at[4:5], add(hidden_grad))
    collect(sums.at[5:6], add(br.astype(F32)))
    return dot(br, wo[...], NT).astype(BF16)


def middle_kernel(seqs, lengths, order, tok, teach, vec, *refs):
    sc = Counts(lengths, order)
    attended, weights, refs = refs[:seqs], refs[seqs : seqs + 6], refs[seqs + 6 :]
    out, fg, sums, wide_sums, a_own, a_give, b_own, b_give = refs[:8]
    grads_in, refs = refs[8 : 8 + seqs], refs[8 + seqs :]
    wo, wi, wu, slope, o_in, g_out, att_k, br_k, hl_k, il_k, act_k, ol_k = refs[:12]
    own, given, w_sem, o_sem, g_sem, c_sem = refs[12:]
    z, y, c, x = position()
    sibling = device(z, y, 1 - c, x)
    line = [None] + [device(z ^ d, y, c, x) for d in range(1, GROUPS)]
    greet([sibling] + line[1:])
    coming, going = {}, {}
    for s in range(seqs):
        if s == 0:
            coming[s, 0] = pltpu.make_async_copy(attended[s], o_in.at[s], o_sem.at[0, s, 0])
            coming[s, 0].start()
            continue
        for d in range(1, GROUPS):
            sems = o_sem.at[0, s, d], o_sem.at[1, s, d]
            coming[s, d] = send(attended[s].at[z ^ d], o_in.at[s, z], sems, line[d])
        coming[s, 0] = pltpu.make_async_copy(attended[s].at[z], o_in.at[s, z], o_sem.at[0, s, 0])
        coming[s, 0].start()
    copies = [
        half_copies(full, *weights[2 * i : 2 * i + 2], w_sem, 2 * i)
        for i, full in enumerate((wo, wi, wu))
    ]
    for group in copies:
        for copy in group:
            copy.start()

    def loaded(which):
        for i in which:
            for copy in copies[i]:
                copy.wait()

    half = wo.shape[0] // 2
    blocks = wi.shape[1] // (2 * half)
    base = (1 + blocks) * half
    core = []

    def store(k, start, value):
        low_value = value.astype(BF16)
        own[0, k, start : start + half, :] = low_value[:, :half]
        own[1, k, start : start + half, :] = low_value[:, half:]

    def pass_core(k, start, stop):
        place = pl.ds(start, stop - start)
        i = len(core)
        sems = c_sem.at[0, i], c_sem.at[1, i]
        core.append(send(own.at[1 - c, k, place], given.at[k, place], sems, sibling))

    def outer_grads():
        for k in range(2):
            for t in range(blocks):
                rows_of = slice((k * blocks + t) * half, (k * blocks + t + 1) * half)
                store(k, base + t * half, dot(act_k[:, rows_of], ol_k[...], TN))
            pass_core(k, base, base + blocks * half)

    rows = tok.shape[1]
    per = o_in.shape[3]
    for s in range(seqs):
        for d in range(GROUPS if s > 0 else 1):
            coming[s, d].wait()
        att = jnp.concatenate([o_in[s, g] for g in range(GROUPS)], 1)
        mask = valid_rows(sc, s, rows)
        waits = (lambda: loaded([0]), lambda: loaded([1, 2])) if s == 0 else (lambda: None,) * 2
        found = middle_stage(
            s,
            att,
            mask,
            tok,
            teach,
            vec,
            (wo, wi, wu, slope),
            (att_k, br_k, hl_k, il_k, act_k, ol_k),
            (out, fg, sums, wide_sums),
            waits,
            outer_grads if s == seqs - 1 else lambda: None,
        )
        for g in range(GROUPS):
            g_out[s, g] = found[:, g * per : (g + 1) * per]
        for d in range(1, GROUPS):
            sems = g_sem.at[0, s, d], g_sem.at[1, s, d]
            going[s, d] = send(g_out.at[s, z ^ d], grads_in[s].at[z], sems, line[d])
        going[s, 0] = pltpu.make_async_copy(g_out.at[s, z], grads_in[s].at[z], g_sem.at[0, s, 0])
        going[s, 0].start()
    sums[7:8, :] = jnp.zeros((1, sums.shape[1]), F32)

    for k in range(2):
        ks = slice(k * half, (k + 1) * half)
        store(k, 0, dot(att_k[:, ks], br_k[...], TN))
        for t in range(blocks):
            cols = slice(2 * t * half, 2 * (t + 1) * half)
            store(k, (1 + t) * half, dot(hl_k[:, ks], il_k[:, cols], TN))
        pass_core(k, 0, base)
    for copy in core:
        copy.wait()
    mine = own.at[c]
    cut, b_half = a_own.shape[0], b_own.shape[1]
    a_own[...] = add_low(mine[x, 0:cut], given[x, 0:cut])
    a_give[...] = add_low(mine[1 - x, 0:cut], given[1 - x, 0:cut])
    for k in range(2):
        for target, which in ((b_own, y), (b_give, 1 - y)):
            part = pl.ds(pl.multiple_of(cut + which * b_half, 16), b_half)
            target[k] = add_low(mine[k, part], given[k, part])
    for copy in going.values():
        copy.wait()


def cut_of(total):
    return total // 256 * 128


def middle(lengths, order, tok, teach, vec, attended, weights):
    seqs, rows, width = tok.shape
    hidden = 2 * vec.shape[2]
    half = width // 2
    total = half + hidden
    cut = cut_of(total)
    dma = pltpu.SemaphoreType.DMA
    narrow, wide = (seqs * rows, width), (seqs * rows, hidden)
    b_shape = jax.ShapeDtypeStruct((2, (total - cut) // 2, half), BF16)
    a_shape = jax.ShapeDtypeStruct((cut, half), BF16)
    groups, _, per = attended[0].shape
    return pl.pallas_call(
        functools.partial(middle_kernel, seqs),
        out_shape=[
            jax.ShapeDtypeStruct(tok.shape, BF16),
            jax.ShapeDtypeStruct(tok.shape, F32),
            jax.ShapeDtypeStruct((8, width), F32),
            jax.ShapeDtypeStruct((1, hidden), F32),
            a_shape,
            a_shape,
            b_shape,
            b_shape,
        ]
        + [jax.ShapeDtypeStruct(a.shape, BF16) for a in attended],
        in_specs=[SMEM] * 2 + [VMEM] * 3 + [ANY] * (seqs + 6),
        out_specs=[VMEM] * 8 + [ANY] * seqs,
        scratch_shapes=[
            pltpu.VMEM((width, width), BF16),
            pltpu.VMEM((width, hidden), BF16),
            pltpu.VMEM((hidden, width), BF16),
            pltpu.VMEM((rows, hidden), F32),
            pltpu.VMEM((seqs, groups, rows, per), BF16),
            pltpu.VMEM((seqs, groups, rows, per), BF16),
            pltpu.VMEM(narrow, BF16),
            pltpu.VMEM(narrow, BF16),
            pltpu.VMEM(narrow, BF16),
            pltpu.VMEM(wide, BF16),
            pltpu.VMEM(wide, BF16),
            pltpu.VMEM(narrow, BF16),
            pltpu.VMEM((2, 2, total, half), BF16),
            pltpu.VMEM((2, total, half), BF16),
            dma((6,)),
            dma((2, seqs, groups)),
            dma((2, seqs, groups)),
            dma((2, 4)),
        ],
        compiler_params=pltpu.CompilerParams(
            vmem_limit_bytes=63 * 2**20, collective_id=3, has_side_effects=True
        ),
        cost_estimate=cost(60),
        name="middle",
    )(lengths, order, tok, teach, vec, *attended, *weights)


def finish_kernel(
    seqs, lengths, order, tok, fg, rq, rkv, dense_sums, wide_sums, ready, wq, wk, wv, others, *rest
):
    sc = Counts(lengths, order)
    tg, out, dense_out, small_out, *rest = rest
    full, grads, acc, from_core, from_x, from_y, from_z, res, vec, vec_in, dense_res = rest[:11]
    w_sems, sems, small_sems, d_sems, last_sem = rest[11:]
    z, y, c, x = position()
    sibling, beside, over = device(z, y, 1 - c, x), device(z, 1 - y, c, x), device(z, y, c, 1 - x)
    line = [None] + [device(z ^ d, y, c, x) for d in range(1, GROUPS)]
    greet([sibling, beside, over] + line[1:])

    a_half = cut_of(dense_res.shape[1]) // 2
    b_half = dense_res.shape[1] // 2 - a_half
    low_bit, high_bit = lax.rem(z, 2), z // 2
    dense_parts = ((0, a_half, y * a_half), (a_half // 4, b_half, 2 * a_half + y * b_half))

    def dense_rows(start, n):
        return dense_res.at[c, pl.ds(pl.multiple_of(start, 16), n)]

    def d_pair(k, i):
        return d_sems.at[0, k, i], d_sems.at[1, k, i]

    dense_flows = [None, None]

    def dense_step(i, k):
        start, n, base = dense_parts[i]
        if k > 0:
            dense_flows[i].wait()
        begin = base + (low_bit * (n // 2) if k < 2 else 0) + (high_bit * (n // 4) if k < 1 else 0)
        size = (n // 4, n // 2, n, 2 * n)[k]
        place = dense_rows(begin if k < 3 else 2 * a_half * i, size)
        if k == 0:
            place[...] = ready[start : start + size]
        to = (line[2], line[1], beside, sibling)[k]
        dense_flows[i] = send(place, place, d_pair(k, i), to)

    dense_step(0, 0)
    rows, width = tok.shape[1:]
    heads = width // GROUPS // DH
    copies = []
    for i, own in enumerate((wq, wk, wv)):
        copies += half_copies(full.at[i], own, others.at[i], w_sems, 2 * i)
    for copy in copies:
        copy.start()

    def head(i, s, g, h):
        if i == 0:
            return rq[h, g, :, s * DH : (s + 1) * DH]
        return rkv[h * seqs + s, g, :, (i - 1) * DH : i * DH]

    def whole(i):
        each = [
            jnp.concatenate([head(i, s, g, h) for g in range(GROUPS) for h in range(heads)], 1)
            for s in range(seqs)
        ]
        return jnp.concatenate(each, 0)

    valid = jnp.concatenate([valid_rows(sc, s, rows) for s in range(seqs)], 0) > 0.0
    parted = [whole(0)] + [jnp.where(valid, whole(i), jnp.zeros((), BF16)) for i in (1, 2)]
    flat = tok[...].reshape(seqs * rows, width)
    wide = width // 2
    for i, grad in enumerate(parted):
        found = dot(flat, grad, TN).astype(BF16)
        for n in range(2):
            for t in range(width // 128):
                grads[t % 3, t // 3, n, i * wide : (i + 1) * wide, :] = found[
                    n * wide : (n + 1) * wide, t * 128 : (t + 1) * 128
                ]
    lines_of = [dense_sums[i : i + 1, :] for i in range(7)]
    lines_of += [jnp.sum(grad.astype(F32), 0, keepdims=True) for grad in (parted[0], parted[2])]
    lines_of.append(wide_sums[...])
    row = 0
    for one in lines_of:
        for t in range(one.shape[1] // 128):
            vec[row : row + 1, :] = one[:, t * 128 : (t + 1) * 128]
            row += 1
    valid_count = sum(jnp.clip(sc[i], 0, BLK) for i in range(2 * seqs))
    vec[row:, :] = jnp.full((vec.shape[0] - row, 128), valid_count.astype(F32))

    parts, rows_each = grads.shape[0], grads.shape[3]
    half, piece = rows_each // 2, rows_each // 8
    own_half = pl.ds(pl.multiple_of(y * half, half), half)
    other_half = pl.ds(pl.multiple_of((1 - y) * half, half), half)

    def piece_of(g):
        return pl.ds(pl.multiple_of(y * half + g * piece, piece), piece)

    def pair(k, p):
        return sems.at[0, k, p], sems.at[1, k, p]

    def small_pair(k):
        return small_sems.at[0, k], small_sems.at[1, k]

    core = [
        send(grads.at[p, 1 - c], from_core.at[p], pair(0, p), sibling) for p in range(parts)
    ]
    short = send(vec, vec_in.at[0], small_pair(0), sibling)
    flows, lines, spread = {}, {}, {}

    def from_pair(p):
        core[p].wait()
        acc[p] = add_low(grads[p, c], from_core[p])

    def x_send(p):
        if p == 1:
            flows[p] = send(acc.at[p, 1 - x, own_half], from_x.at[p, own_half], pair(2, p), over)
        else:
            flows[p] = send(acc.at[p, 1 - x], from_x.at[p], pair(1, p), over)

    def x_add(p):
        flows[p].wait()
        if p == 1:
            acc[p, x, own_half] = add_low(acc[p, x, own_half], from_x[p, own_half])
        else:
            acc[p, x] = add_low(acc[p, x], from_x[p])

    def y_send(p):
        if p == 1:
            flows[p] = send(acc.at[p, :, other_half], from_y.at[p], pair(1, p), beside)
        else:
            flows[p] = send(acc.at[p, x, other_half], from_y.at[p, 0], pair(2, p), beside)

    def y_add(p):
        flows[p].wait()
        if p == 1:
            for k in range(2):
                acc[p, k, own_half] = add_low(acc[p, k, own_half], from_y[p, k])
        else:
            acc[p, x, own_half] = add_low(acc[p, x, own_half], from_y[p, 0])

    def z_send(p):
        for d in range(1, GROUPS):
            lines[p, d] = send(
                acc.at[p, x, piece_of(z ^ d)], from_z.at[p, d], pair(2 + d, p), line[d]
            )

    def z_add(p):
        total = acc[p, x, piece_of(z)].astype(F32)
        for d in range(1, GROUPS):
            lines[p, d].wait()
            total += from_z[p, d].astype(F32)
        place = res.at[c, p, piece_of(z)]
        place[...] = total.astype(BF16)
        for d in range(1, GROUPS):
            spread[p, d] = send(place, place, pair(5 + d, p), line[d])

    def y_gather(p):
        for d in range(1, GROUPS):
            spread[p, d].wait()
        place = res.at[c, p, own_half]
        flows[p] = send(place, place, pair(9, p), beside)

    def core_gather(p):
        flows[p].wait()
        flows[p] = send(res.at[c, p], res.at[c, p], pair(10, p), sibling)

    from_pair(0)
    x_send(0)
    from_pair(1)
    y_send(1)
    from_pair(2)
    short.wait()
    vec_in[8] = vec[...] + vec_in[0]
    short = send(vec_in.at[8], vec_in.at[1], small_pair(1), over)
    dense_step(0, 1)
    dense_step(1, 0)
    for copy in copies:
        copy.wait()
    total = jnp.concatenate([fg[s] for s in range(seqs)], 0)
    for i, grad in enumerate(parted):
        total += dot(grad, full[i], NT)
    tg[...] = total.reshape(seqs, rows, width)
    x_add(0)
    x_send(2)
    y_send(0)
    y_add(1)
    x_send(1)
    short.wait()
    vec[...] = vec_in[8] + vec_in[1]
    short = send(vec, vec_in.at[2], small_pair(2), beside)
    y_add(0)
    z_send(0)
    dense_step(0, 2)
    dense_step(1, 1)
    x_add(2)
    y_send(2)
    x_add(1)
    z_send(1)
    z_add(0)
    short.wait()
    vec[...] = vec[...] + vec_in[2]
    vec_in[4 + z] = vec[...]
    shorts = [
        send(vec, vec_in.at[4 + z], small_pair(2 + d), line[d]) for d in range(1, GROUPS)
    ]
    y_add(2)
    z_send(2)
    dense_step(1, 2)
    z_add(1)
    y_gather(0)
    z_add(2)
    dense_step(0, 3)
    y_gather(1)
    y_gather(2)
    for copy in shorts:
        copy.wait()
    small_out[...] = vec_in[4] + vec_in[5] + (vec_in[6] + vec_in[7])
    for p in range(parts):
        core_gather(p)
    dense_step(1, 3)
    for copy in dense_flows:
        copy.wait()
    done = [pltpu.make_async_copy(dense_res, dense_out, last_sem.at[1])]
    done[0].start()
    for p in (1, 0, 2):
        flows[p].wait()
    done.append(pltpu.make_async_copy(res, out, last_sem.at[0]))
    done[1].start()
    for copy in done:
        copy.wait()


def finish(lengths, order, tok, fg, rq, rkv, sums, wide_sums, ready, wq, wk, wv, others):
    seqs, _, width = tok.shape
    short = (-(-(9 * width + wide_sums.shape[1] + 128) // 1024) * 8, 128)
    parts, rows, lanes = 3, 3 * (width // 2), 128
    total, half = 8 * ready.shape[0], ready.shape[1]
    dma = pltpu.SemaphoreType.DMA
    return pl.pallas_call(
        functools.partial(finish_kernel, seqs),
        out_shape=[
            jax.ShapeDtypeStruct(tok.shape, F32),
            jax.ShapeDtypeStruct((2, parts, rows, lanes), BF16),
            jax.ShapeDtypeStruct((2, total, half), BF16),
            jax.ShapeDtypeStruct(short, F32),
        ],
        in_specs=[SMEM] * 2 + [VMEM] * 7 + [ANY] * 4,
        out_specs=[VMEM, ANY, ANY, VMEM],
        scratch_shapes=[
            pltpu.VMEM((3, width, width), BF16),
            pltpu.VMEM((parts, 2, 2, rows, lanes), BF16),
            pltpu.VMEM((parts, 2, rows, lanes), BF16),
            pltpu.VMEM((parts, 2, rows, lanes), BF16),
            pltpu.VMEM((parts, rows, lanes), BF16),
            pltpu.VMEM((parts, 2, rows // 2, lanes), BF16),
            pltpu.VMEM((parts, GROUPS, rows // 8, lanes), BF16),
            pltpu.VMEM((2, parts, rows, lanes), BF16),
            pltpu.VMEM(short, F32),
            pltpu.VMEM((9, *short), F32),
            pltpu.VMEM((2, total, half), BF16),
            dma((6,)),
            dma((2, 11, parts)),
            dma((2, 6)),
            dma((2, 4, 2)),
            dma((2,)),
        ],
        compiler_params=pltpu.CompilerParams(
            vmem_limit_bytes=63 * 2**20, collective_id=2, has_side_effects=True
        ),
        cost_estimate=cost(70),
        name="finish",
    )(lengths, order, tok, fg, rq, rkv, sums, wide_sums, ready, wq, wk, wv, others)


def unpack_kernel(qkv_in, total_in, small, rows_in, tokens_in, *refs):
    outs, moved, rows, loss, refs = refs[:6], refs[6:8], refs[8:17], refs[17], refs[18:]
    qkv, total, narrow, inner, outer, sems, in_sems = refs
    loads = [
        pltpu.make_async_copy(src, dst, in_sems.at[i])
        for i, (src, dst) in enumerate(((total_in, total), (qkv_in, qkv)))
    ]
    for copy in loads:
        copy.start()
    half = qkv.shape[2] // 3
    blocks = inner.shape[1] // (2 * half)
    copies = []

    def leave(src, i):
        copy = pltpu.make_async_copy(src, outs[i], sems.at[i])
        copy.start()
        copies.append(copy)

    loads[0].wait()
    for k in range(2):
        cols = slice(k * half, (k + 1) * half)
        outer[:, cols] = total[k, (1 + blocks) * half :].astype(F32)
    leave(outer, 5)
    for k in range(2):
        for t in range(blocks):
            cols = slice((2 * t + k) * half, (2 * t + k + 1) * half)
            inner[:, cols] = total[k, (1 + t) * half : (2 + t) * half].astype(F32)
    leave(inner, 4)
    for i, (src, dst) in enumerate(zip((rows_in, tokens_in), moved)):
        copy = pltpu.make_async_copy(src, dst, sems.at[6 + i])
        copy.start()
        copies.append(copy)
    loads[1].wait()
    for i in range(3):
        for k in range(2):
            for p in range(3):
                cols = slice((3 * k + p) * 128, (3 * k + p + 1) * 128)
                narrow[i, :, cols] = qkv[k, p, i * half : (i + 1) * half].astype(F32)
        leave(narrow.at[i], i)
    for k in range(2):
        narrow[3, :, k * half : (k + 1) * half] = total[k, 0:half].astype(F32)
    leave(narrow.at[3], 3)
    x = lax.axis_index("wa")
    tiles = 2 * half // 128
    starts = [tiles * i for i in (0, 1, 2, 3, 4, 5, 7, 8)] + [9 * tiles]
    for one, begin in zip(rows, starts):
        n = one.shape[0] // 128
        for t in range(n):
            one[t * 128 : (t + 1) * 128] = small[pl.ds(begin + x * n + t, 1), :][0]
    end = 9 * tiles + 2 * rows[8].shape[0] // 128
    squares = jnp.sum(small[6 * tiles : 7 * tiles, :], keepdims=True)
    loss[...] = squares / (small[end : end + 1, :1] * (2.0 * half))
    for copy in copies:
        copy.wait()


def unpack(qkv, total, small, output, tokens_grad, hidden):
    half = total.shape[2]
    narrow = jax.ShapeDtypeStruct((half, 2 * half), F32)
    return pl.pallas_call(
        unpack_kernel,
        out_shape=[narrow] * 4
        + [
            jax.ShapeDtypeStruct((half, hidden), F32),
            jax.ShapeDtypeStruct((hidden // 2, 2 * half), F32),
            jax.ShapeDtypeStruct(output.shape, BF16),
            jax.ShapeDtypeStruct(tokens_grad.shape, F32),
        ]
        + [jax.ShapeDtypeStruct((half,), F32)] * 8
        + [jax.ShapeDtypeStruct((hidden // 2,), F32), jax.ShapeDtypeStruct((1, 1), F32)],
        in_specs=[ANY, ANY, VMEM, ANY, ANY],
        out_specs=[ANY] * 8 + [VMEM] * 10,
        scratch_shapes=[
            pltpu.VMEM(qkv.shape, BF16),
            pltpu.VMEM(total.shape, BF16),
            pltpu.VMEM((4, half, 2 * half), F32),
            pltpu.VMEM((half, hidden), F32),
            pltpu.VMEM((hidden // 2, 2 * half), F32),
            pltpu.SemaphoreType.DMA((8,)),
            pltpu.SemaphoreType.DMA((2,)),
        ],
        compiler_params=ROOM,
        cost_estimate=cost(10),
        name="unpack",
    )(qkv, total, small, output, tokens_grad)


def pick(table, index):
    places = jnp.arange(table.shape[0], dtype=jnp.int32)
    return jnp.sum(jnp.where(index[..., None] == places, table, 0), -1)


def shards(
    size,
    tokens,
    teacher,
    lengths,
    block_order,
    query_weight,
    query_bias,
    key_weight,
    value_weight,
    value_bias,
    out_weight,
    out_bias,
    gain_one,
    shift_one,
    inner_weight,
    inner_bias,
    outer_weight,
    outer_bias,
    gain_two,
    shift_two,
):
    seqs, rows, width = tokens.shape
    per_plane = size // GROUPS
    blocks_each = rows // BLK
    ctx, x = lax.axis_index("ctx"), lax.axis_index("wa")
    c, place = lax.rem(ctx, 2), lax.rem(ctx, per_plane)
    masks = [1 << b for b in reversed(range(per_plane.bit_length() - 1))]
    offsets = [0]
    for m in masks:
        offsets += [o ^ m for o in offsets]

    def across(value):
        return lax.ppermute(value, "wa", [(0, 1), (1, 0)])

    def flip(value, m):
        return lax.ppermute(value, "ctx", [(i, i ^ m) for i in range(size)])

    lines = [[g * per_plane + r for g in range(GROUPS)] for r in range(per_plane)]

    def turn(value):
        return lax.all_to_all(value, "ctx", 0, 0, axis_index_groups=lines)

    cores = [[i for i in range(size) if i % 2 == k] for k in range(2)]

    def paired(mine):
        sibling = flip(mine, 1)
        return jnp.where(c == 0, jnp.stack([mine, sibling]), jnp.stack([sibling, mine]))

    def reduced(grad):
        four = grad.reshape(2, 2, *grad.shape[1:])
        keep = lax.dynamic_index_in_dim(four, c, 1, False)
        give = lax.dynamic_index_in_dim(four, 1 - c, 1, False)
        keep = add_low(keep, flip(give, 1))
        mine = lax.dynamic_index_in_dim(keep, x, 0, False)
        mine = add_low(mine, across(lax.dynamic_index_in_dim(keep, 1 - x, 0, False)))
        return paired(lax.psum(mine, "ctx", axis_index_groups=cores))

    def reduced_dense(grad):
        four = grad.reshape(2, 2, *grad.shape[1:])
        keep = lax.dynamic_index_in_dim(four, c, 1, False)
        give = lax.dynamic_index_in_dim(four, 1 - c, 1, False)
        keep = add_low(keep, flip(give, 1))
        mine = lax.psum_scatter(
            keep.reshape(-1, keep.shape[-1]), "wa", scatter_dimension=0, tiled=True
        )
        return lax.psum(mine, "ctx", axis_index_groups=cores)

    vectors = (
        query_bias,
        value_bias,
        out_bias,
        gain_one,
        shift_one,
        outer_bias,
        gain_two,
        shift_two,
        inner_bias,
    )
    half, hidden = width // 2, 2 * inner_bias.shape[0]
    fused = per_plane == 4

    if fused:
        found = start(
            lengths,
            block_order,
            tokens,
            (query_weight, key_weight, value_weight, out_weight, inner_weight, outer_weight),
            vectors,
        )
        queries = [q.reshape(-1, BLK, q.shape[2]) for q in found[:seqs]]
        pieces = [[kv.reshape(-1, BLK, kv.shape[3])] for kv in found[seqs : 2 * seqs]]
        attended, lses = found[2 * seqs : 3 * seqs], found[3 * seqs : 4 * seqs]
        first_back, pair, others, *rest = found[4 * seqs :]
        dense_weights = [out_weight, rest[0], inner_weight, rest[1], outer_weight, rest[2]]
    else:
        count = block_order.shape[0]
        ids = jnp.arange(count, dtype=jnp.int32)
        owner = ids // blocks_each
        index_of = jnp.array([offsets.index(o) for o in range(per_plane)], jnp.int32)
        piece_of = pick(index_of, (owner % per_plane) ^ place)
        spot = (piece_of * GROUPS + owner // per_plane) * blocks_each + ids % blocks_each
        key_order = jnp.sum(jnp.where(block_order[None, :] == ids[:, None], spot[None, :], 0), 1)
        near = jnp.arange(GROUPS * blocks_each, dtype=jnp.int32)
        near_ids = (near // blocks_each * per_plane + place) * blocks_each + near % blocks_each
        near_pos = pick(block_order, near_ids)
        rank = jnp.sum((near_pos[None, :] < near_pos[:, None]).astype(jnp.int32), 1)
        query_order = jnp.sum(jnp.where(rank[None, :] == near[:, None], near[None, :], 0), 1)
        own_pos = pick(block_order, ctx * blocks_each + jnp.arange(blocks_each, dtype=jnp.int32))
        scalars, row_counts = [], []
        for s in range(seqs):
            used = jnp.sum((near_pos * BLK < lengths[s]).astype(jnp.int32))
            head = jnp.concatenate([lengths[s][None], used[None], jnp.zeros((6,), jnp.int32)])
            scalars.append(jnp.concatenate([head, query_order, key_order]))
            row_counts.append(jnp.clip(lengths[s] - own_pos * BLK, 0, BLK))

        counts = jnp.concatenate(row_counts)
        own_vec = jnp.concatenate(vectors)[None]
        other_vec = across(own_vec)
        pair = jnp.where(
            x == 0, jnp.stack([own_vec, other_vec]), jnp.stack([other_vec, own_vec])
        ).astype(F32)
        narrow = pair[:, 0, : 8 * half].reshape(2, 8, half).swapaxes(0, 1).reshape(8, width)
        wide_vec = pair[:, 0, 8 * half :].reshape(1, -1)

        def quarter(weight):
            n = weight.shape[0] // 2
            return lax.dynamic_slice_in_dim(weight, c * n, n, 0)

        first_qkv = across(
            jnp.concatenate([quarter(w) for w in (query_weight, key_weight, value_weight)], 0)
        )
        second_qkv = flip(first_qkv, 1)
        dense_weights = []
        last = first_qkv
        for weight in (out_weight, inner_weight, outer_weight):
            piece, last = lax.optimization_barrier((quarter(weight), last))
            last = across(piece)
            dense_weights += [weight, last, flip(last, 1)]

        projected = project(
            counts, tokens, narrow, query_weight, key_weight, value_weight, first_qkv, second_qkv
        )
        queries, pieces = [], []
        for s in range(seqs):
            kv = turn(projected[2 * s + 1])
            queries.append(turn(projected[2 * s]).reshape(-1, BLK, width // GROUPS))
            held = [kv.reshape(-1, BLK, kv.shape[2])]
            for m in masks:
                held += [flip(piece, m) for piece in held]
            pieces.append(held)

        attended, lses = [], []
        for s in range(seqs):
            o, lse = attend(s, per_plane, lengths, block_order, queries[s], pieces[s])
            attended.append(o.reshape(queries[s].shape))
            lses.append(lse)
    if fused:
        fours = [first_back, *attended[1:]]
        found = middle(lengths, block_order, tokens, teacher, pair, fours, dense_weights)
        output, firsts, sums, wide_sums, a_own, a_give, b_own, b_give = found[:8]
        heads_grad = [g.reshape(queries[0].shape) for g in found[8:]]
        ready = (a_own, a_give, b_own, b_give)
    else:
        dense_out = []
        for s in range(seqs):
            o4 = turn(attended[s].reshape(GROUPS, rows, -1))
            dense_out.append(
                dense(
                    row_counts[s], o4, tokens[s], teacher[s], narrow[2:], wide_vec, dense_weights
                )
            )
        output = jnp.stack([d[0] for d in dense_out])
        first_grads = [d[1] for d in dense_out]
        heads_grad = [turn(d[2]).reshape(queries[s].shape) for s, d in enumerate(dense_out)]
        sums = sum(d[9] for d in dense_out)
        wide_sums = sum(d[10] for d in dense_out)
        dense_sums = [reduced_dense(g) for g in dense_grads([d[3:9] for d in dense_out])]

    if fused:
        flat_rows = (GROUPS * rows, width // GROUPS)
        rq, rkv, ready = attend_back_all(
            [
                [
                    *(a.reshape(flat_rows) for a in (queries[s], heads_grad[s], attended[s])),
                    lses[s],
                    pieces[s][0].reshape(-1, pieces[s][0].shape[2]),
                ]
                for s in range(seqs)
            ],
            ready,
        )
    else:
        dqs, dkvs = [], []
        for s in range(seqs):
            found = attend_back(
                scalars[s], queries[s], heads_grad[s], attended[s], lses[s], pieces[s]
            )
            dqs.append(turn(found[0].reshape(GROUPS, rows, -1)))
            held = [piece.reshape(GROUPS, rows, -1) for piece in found[1:]]
            for m in reversed(masks):
                n = len(held) // 2
                held = [add_low(mine, flip(theirs, m)) for mine, theirs in zip(held[:n], held[n:])]
            dkvs.append(turn(held[0]))
        tokens_grad, g_qkv, sums_qkv = project_grads(
            counts,
            tokens,
            first_grads,
            dqs + dkvs,
            query_weight,
            key_weight,
            value_weight,
            first_qkv,
            second_qkv,
        )

    if fused:
        tokens_grad, qkv, total, small = finish(
            lengths,
            block_order,
            tokens,
            firsts,
            rq,
            rkv,
            sums,
            wide_sums,
            ready,
            query_weight,
            key_weight,
            value_weight,
            others,
        )
        grads = unpack(qkv, total, small, output, tokens_grad, hidden)
        query_grad, key_grad, value_grad, out_grad, inner_grad, outer_grad = grads[:6]
        output, tokens_grad = grads[6:8]
        rows_of = dict(zip((0, 1, 2, 3, 4, 5, 7, 8, 9), grads[8:17]))
        loss = grads[17].reshape(())

        def vector(start, length):
            return rows_of[start // width]

    else:
        valid = jnp.full((128,), sum(jnp.sum(r) for r in row_counts).astype(F32))
        small = jnp.concatenate(
            [sums[:7].reshape(-1), sums_qkv[:2].reshape(-1), wide_sums[0], valid]
        )
        small = lax.psum(small, ("ctx", "wa"))
        qkv = reduced(jnp.moveaxis(g_qkv, (2, 1), (0, 1)).reshape(4, 3, -1, 128))
        out_grad, inner_grad, outer_grad = (
            paired(g).reshape(-1, g.shape[-1]).astype(F32) for g in dense_sums
        )
        qkv = qkv.reshape(6, 3, half, 128).astype(F32)
        query_grad, key_grad, value_grad = (
            qkv[:, i].swapaxes(0, 1).reshape(half, width) for i in range(3)
        )

        def vector(start, length):
            return lax.dynamic_slice_in_dim(small, start + x * (length // 2), length // 2, 0)

        loss = jnp.sum(small[6 * width : 7 * width]) / (small[9 * width + hidden] * width)

    end = 9 * width
    return (
        output,
        tokens_grad,
        query_grad,
        vector(7 * width, width),
        key_grad,
        value_grad,
        vector(8 * width, width),
        out_grad,
        vector(5 * width, width),
        vector(3 * width, width),
        vector(4 * width, width),
        inner_grad,
        vector(end, hidden),
        outer_grad,
        vector(2 * width, width),
        vector(0, width),
        vector(width, width),
        loss,
    )


def solution(mesh):
    row, split, both = P("wa"), P("wa", None), P("wa", "ctx", None)
    placed = (both, both, row, P(), split, row, split, split, row, split, row, row, row)
    placed += (split, row, split, row, row, row)
    return jax.shard_map(
        functools.partial(shards, mesh.shape["ctx"]),
        mesh=mesh,
        in_specs=placed,
        out_specs=(
            both,
            both,
            split,
            row,
            split,
            split,
            row,
            split,
            row,
            row,
            row,
            split,
            row,
            split,
            row,
            row,
            row,
            P(),
        ),
        check_vma=False,
    )
```

```python
import functools
import math

import jax
import jax.numpy as jnp
from jax import lax
from jax.experimental import pallas as pl
from jax.experimental.pallas import tpu as pltpu
from jax.sharding import PartitionSpec as P

DH = 64
BLK = 128
GROUPS = 4
LN2 = math.log(2.0)
NT = (((1,), (1,)), ((), ()))
NN = (((1,), (0,)), ((), ()))
TN = (((0,), (0,)), ((), ()))
F32 = jnp.float32
BF16 = jnp.bfloat16
VMEM = pl.BlockSpec(memory_space=pltpu.VMEM)
SMEM = pl.BlockSpec(memory_space=pltpu.SMEM)
ANY = pl.BlockSpec(memory_space=pl.ANY)
ROOM = pltpu.CompilerParams(vmem_limit_bytes=62 * 2**20)


def dot(left, right, dims=NN):
    return lax.dot_general(left, right, dims, preferred_element_type=F32)


def cost(us):
    return pl.CostEstimate(flops=int(us * 1.15e9), bytes_accessed=1 << 20, transcendentals=0)


def weight_copies(full, own, first, second, sems, base):
    x, c = lax.axis_index("wa"), lax.rem(lax.axis_index("ctx"), 2)
    half = own.shape[0]
    quarter = half // 2
    other = (1 - x) * half
    places = (
        (own, x * half, half),
        (first, other + c * quarter, quarter),
        (second, other + (1 - c) * quarter, quarter),
    )
    return [
        pltpu.make_async_copy(
            src, full.at[pl.ds(pl.multiple_of(start, quarter), size)], sems.at[base + i]
        )
        for i, (src, start, size) in enumerate(places)
    ]


class Counts:
    def __init__(self, lengths, order):
        self.lengths, self.order = lengths, order

    def __getitem__(self, i):
        place = 2 * lax.axis_index("ctx") + i % 2
        return self.lengths[i // 2] - self.order[place] * BLK


def valid_rows(sc, s, rows):
    row = lax.broadcasted_iota(jnp.int32, (rows, 1), 0)
    first = jnp.where(row < sc[2 * s], 1.0, 0.0)
    later = jnp.where(row - BLK < sc[2 * s + 1], 1.0, 0.0)
    return jnp.where(row < BLK, first, later)


def half_copies(full, own, other, sems, base):
    x, half = lax.axis_index("wa"), own.shape[0]
    return [
        pltpu.make_async_copy(
            src, full.at[pl.ds(pl.multiple_of(k * half, half), half)], sems.at[base + i]
        )
        for i, (src, k) in enumerate(((own, x), (other, 1 - x)))
    ]


def project_kernel(sc, tok, vec, wq, wk, wv, first, second, *rest):
    seqs, rows, width = tok.shape
    outs, (full, sems) = rest[: 2 * seqs], rest[2 * seqs :]
    quarter = wq.shape[0] // 2
    copies = []
    for i, own in enumerate((wq, wk, wv)):
        part = pl.ds(i * quarter, quarter)
        copies.append(
            weight_copies(full.at[i], own, first.at[part], second.at[part], sems, 3 * i)
        )
    for group in copies:
        for copy in group:
            copy.start()
    flat = tok[...].reshape(seqs * rows, width)
    per = width // GROUPS
    heads = per // DH
    valid = jnp.concatenate([valid_rows(sc, s, rows) for s in range(seqs)], 0) > 0.0
    for copy in copies[1]:
        copy.wait()
    keys = jnp.where(valid, dot(flat, full[1]), 0.0).astype(BF16)
    for copy in copies[2]:
        copy.wait()
    values = jnp.where(valid, dot(flat, full[2]) + vec[1:2, :], 0.0).astype(BF16)
    for s in range(seqs):
        rs = slice(s * rows, (s + 1) * rows)
        for g in range(GROUPS):
            for h in range(heads):
                cols = slice(g * per + h * DH, g * per + (h + 1) * DH)
                outs[2 * s + 1][g, :, h * 128 : (h + 1) * 128] = jnp.concatenate(
                    [keys[rs, cols], values[rs, cols]], 1
                )
    for copy in copies[0]:
        copy.wait()
    queries = ((dot(flat, full[0]) + vec[0:1, :]) * (DH**-0.5 / LN2)).astype(BF16)
    for s in range(seqs):
        rs = slice(s * rows, (s + 1) * rows)
        for g in range(GROUPS):
            outs[2 * s][g] = queries[rs, g * per : (g + 1) * per]


def project(sc, tok, vec, wq, wk, wv, first, second):
    seqs, rows, width = tok.shape
    per = width // GROUPS
    shapes = [
        jax.ShapeDtypeStruct((GROUPS, rows, n), BF16) for _ in range(seqs) for n in (per, 2 * per)
    ]
    return pl.pallas_call(
        project_kernel,
        out_shape=shapes,
        in_specs=[SMEM, VMEM, VMEM] + [ANY] * 5,
        out_specs=[VMEM] * len(shapes),
        scratch_shapes=[pltpu.VMEM((3, width, width), BF16), pltpu.SemaphoreType.DMA((9,))],
        compiler_params=ROOM,
        cost_estimate=cost(5),
        name="project",
    )(sc, tok, vec, wq, wk, wv, first, second)


def load_pieces(pieces, kv, sems):
    per = pieces[0].shape[0]
    copies = [
        pltpu.make_async_copy(piece, kv.at[pl.ds(i * per, per)], sems.at[i])
        for i, piece in enumerate(pieces)
    ]
    for copy in copies:
        copy.start()
    for copy in copies:
        copy.wait()


def forward_kernel(wide, narrow, count, s, per_plane, lengths, order, q_ref, *rest):
    pieces, rest = rest[:count], rest[count:]
    o_ref, lse_ref, kv_ref, qa, acc, sums, spots, sems = rest
    blocks = q_ref.shape[0]
    heads = q_ref.shape[2] // DH
    rows = blocks * BLK
    length = lengths[s]
    place = lax.rem(lax.axis_index("ctx"), per_plane)

    def put(b, _):
        owner = b // 2
        offset = lax.bitwise_xor(lax.rem(owner, per_plane), place)
        piece = 0
        for bit in range(per_plane.bit_length() - 1):
            piece = 2 * piece + lax.rem(lax.div(offset, 1 << bit), 2)
        spots[order[b]] = (piece * GROUPS + lax.div(owner, per_plane)) * 2 + lax.rem(b, 2)
        return 0

    lax.fori_loop(0, order.shape[0], put, 0)
    load_pieces(pieces, kv_ref, sems)

    def gather(h, start, n):
        return jnp.concatenate(
            [kv_ref[spots[start + i], :, h * 128 : (h + 1) * 128] for i in range(n)], 0
        )

    whole = length // (wide * BLK)
    tail = whole * wide
    tails = (length - tail * BLK + narrow * BLK - 1) // (narrow * BLK)
    for h in range(heads):
        hs = slice(h * DH, (h + 1) * DH)
        own = jnp.concatenate([q_ref[b, :, hs] for b in range(blocks)], 0)
        qa[...] = jnp.concatenate([own, jnp.zeros_like(own)], 1)
        acc[...] = jnp.zeros_like(acc)
        sums[...] = jnp.zeros_like(sums)

        def step(start, n, masked, h=h):
            kv = gather(h, start, n)
            scores = dot(qa[...], kv, NT)
            if masked:
                place = lax.broadcasted_iota(jnp.int32, scores.shape, 1) + start * BLK
                scores = jnp.where(place < length, scores, -1e30)
            p = jnp.exp2(scores)
            sums[...] += sum(p[:, i * 128 : (i + 1) * 128] for i in range(n))
            acc[...] += dot(p.astype(BF16), kv)

        def wide_step(j, _, step=step):
            step(j * wide, wide, False)
            return 0

        def narrow_step(j, _, step=step):
            step(tail + j * narrow, narrow, True)
            return 0

        lax.fori_loop(0, whole, wide_step, 0)
        lax.fori_loop(0, tails, narrow_step, 0)
        total = jnp.sum(sums[...], 1, keepdims=True)
        across = jnp.transpose(jnp.broadcast_to(total, (rows, 128)))[:8]
        good = (jnp.min(across) > 2.0**-80) & (jnp.max(across) < 2.0**100)

        @pl.when(good)
        def _(h=h, hs=hs, total=total, across=across):
            lse_ref[h] = jnp.log2(across)
            o_ref[:, hs] = (acc[:, DH:] * (1.0 / total)).astype(BF16)

        @pl.when(jnp.logical_not(good))
        def _(h=h, hs=hs):
            key_blocks = (length + BLK - 1) // BLK

            def rows_step(t, _):
                part = pl.ds(pl.multiple_of(t * BLK, BLK), BLK)
                q = qa[part, :]

                def scores_of(j):
                    kv = gather(h, j, 1)
                    scores = dot(q, kv, NT)
                    place = lax.broadcasted_iota(jnp.int32, scores.shape, 1) + j * BLK
                    return kv, jnp.where(place < length, scores, -1e30)

                largest = lax.fori_loop(
                    0,
                    key_blocks,
                    lambda j, m: jnp.maximum(m, jnp.max(scores_of(j)[1], 1, keepdims=True)),
                    jnp.full((BLK, 1), -1e30, F32),
                )
                acc[part, :] = jnp.zeros((BLK, 128), F32)
                sums[part, :] = jnp.zeros((BLK, 128), F32)

                def add(j, _):
                    kv, scores = scores_of(j)
                    p = jnp.exp2(scores - largest)
                    sums[part, :] += p
                    acc[part, :] += dot(p.astype(BF16), kv)
                    return 0

                lax.fori_loop(0, key_blocks, add, 0)
                row_total = jnp.sum(sums[part, :], 1, keepdims=True)
                lse = largest + jnp.log2(row_total)
                lse_ref[h, :, part] = jnp.transpose(jnp.broadcast_to(lse, (BLK, 128)))[:8]
                o_ref[part, hs] = (acc[part, :][:, DH:] * (1.0 / row_total)).astype(BF16)
                return 0

            lax.fori_loop(0, rows // BLK, rows_step, 0)


def attend(s, per_plane, lengths, order, q, pieces):
    blocks, _, per = q.shape
    rows, heads = blocks * BLK, per // DH
    key_blocks = len(pieces) * pieces[0].shape[0]
    return pl.pallas_call(
        functools.partial(forward_kernel, 8, 2, len(pieces), s, per_plane),
        out_shape=(
            jax.ShapeDtypeStruct((rows, per), BF16),
            jax.ShapeDtypeStruct((heads, 8, rows), F32),
        ),
        in_specs=[SMEM, SMEM, VMEM] + [ANY] * len(pieces),
        out_specs=(VMEM, VMEM),
        scratch_shapes=[
            pltpu.VMEM((key_blocks, BLK, 2 * per), BF16),
            pltpu.VMEM((rows, 128), BF16),
            pltpu.VMEM((rows, 128), F32),
            pltpu.VMEM((rows, 128), F32),
            pltpu.SMEM((key_blocks,), jnp.int32),
            pltpu.SemaphoreType.DMA((len(pieces),)),
        ],
        compiler_params=ROOM,
        cost_estimate=cost(20),
        name="attend",
    )(lengths, order, q, *pieces)


def backward_kernel(qn, kn, count, sc, q_ref, do_ref, o_ref, lse_ref, *rest):
    pieces, dq_ref, outs = rest[:count], rest[count], rest[count + 1 : 2 * count + 1]
    kv_ref, both, dkv, dq, lse_row, delta_row, sems = rest[2 * count + 1 :]
    blocks = q_ref.shape[0]
    heads = q_ref.shape[2] // DH
    key_blocks = kv_ref.shape[0]
    tile = qn * BLK
    length, used = sc[0], sc[1]
    whole = length // (kn * BLK)
    parts = (length + kn * BLK - 1) // (kn * BLK)
    tiles = (used + qn - 1) // qn
    ones = jnp.ones((8, DH), BF16)
    load_pieces(pieces, kv_ref, sems)
    for h in range(heads):
        hs = slice(h * DH, (h + 1) * DH)

        def clear(i, _):
            dkv[pl.ds(pl.multiple_of(i * 1024, 1024), 1024), :] = jnp.zeros((1024, 128), F32)
            return 0

        lax.fori_loop(0, key_blocks // 8, clear, 0)
        dq[...] = jnp.zeros_like(dq)

        def prepare(t, _, h=h, hs=hs):
            base = pl.multiple_of(t * (2 * tile), 2 * tile)
            start = pl.multiple_of(t * tile, tile)
            places = [sc[8 + t * qn + i] for i in range(qn)]
            q = jnp.concatenate([q_ref[s, :, hs] for s in places], 0)
            do = jnp.concatenate([do_ref[s, :, hs] for s in places], 0)
            o = jnp.concatenate([o_ref[s, :, hs] for s in places], 0)
            zero = jnp.zeros_like(q)
            both[pl.ds(base, tile), :] = jnp.concatenate([q, zero], 1)
            both[pl.ds(base + tile, tile), :] = jnp.concatenate([zero, do], 1)
            product = do.astype(F32) * o.astype(F32)
            high = product.astype(BF16)
            rest_of = (product - high.astype(F32)).astype(BF16)
            delta_row[:, pl.ds(start, tile)] = dot(ones, high, NT) + dot(ones, rest_of, NT)
            lse_row[:, pl.ds(start, tile)] = jnp.concatenate(
                [lse_ref[h, :, pl.ds(pl.multiple_of(s * BLK, BLK), BLK)] for s in places], 1
            )
            return 0

        lax.fori_loop(0, tiles, prepare, 0)

        def rows_step(t, _, h=h):
            base = pl.multiple_of(t * (2 * tile), 2 * tile)
            span = pl.ds(pl.multiple_of(t * tile, tile), tile)

            def step(j, masked):
                places = [sc[8 + blocks + j * kn + i] for i in range(kn)]
                kv = jnp.concatenate([kv_ref[s, :, h * 128 : (h + 1) * 128] for s in places], 0)
                b = both[pl.ds(base, 2 * tile), :]
                found = dot(kv, b, NT)
                p = jnp.exp2(found[:, :tile] - lse_row[:1, span])
                if masked:
                    place = lax.broadcasted_iota(jnp.int32, p.shape, 0) + j * (kn * BLK)
                    p = jnp.where(place < length, p, 0.0)
                ds = (p * (found[:, tile:] - delta_row[:1, span])).astype(BF16)
                grads = dot(jnp.concatenate([ds, p.astype(BF16)], 1), b)
                for i, s in enumerate(places):
                    dkv[pl.ds(pl.multiple_of(s * BLK, BLK), BLK), :] += grads[
                        i * BLK : (i + 1) * BLK
                    ]
                dq[span, :] += dot(ds, kv, TN)

            def whole_step(j, _):
                step(j, False)
                return 0

            lax.fori_loop(0, whole, whole_step, 0)

            @pl.when(parts > whole)
            def _():
                step(whole, True)

            return 0

        lax.fori_loop(0, tiles, rows_step, 0)
        for i in range(blocks):
            dq_ref[sc[8 + i], :, hs] = (
                dq[i * BLK : (i + 1) * BLK, :DH] * DH**-0.5
            ).astype(BF16)
        level = jnp.where(lax.broadcasted_iota(jnp.int32, (1, 128), 1) < DH, LN2, 1.0)
        per_piece = key_blocks // count
        for n, out in enumerate(outs):
            for i in range(per_piece):
                b = n * per_piece + i
                out[i, :, h * 128 : (h + 1) * 128] = (
                    dkv[b * BLK : (b + 1) * BLK, :] * level
                ).astype(BF16)


def attend_back(sc, q, do, o, lse, pieces):
    blocks, _, per = q.shape
    rows = blocks * BLK
    key_blocks = len(pieces) * pieces[0].shape[0]
    return pl.pallas_call(
        functools.partial(backward_kernel, 4, 4, len(pieces)),
        out_shape=[jax.ShapeDtypeStruct(q.shape, BF16)]
        + [jax.ShapeDtypeStruct(p.shape, BF16) for p in pieces],
        in_specs=[SMEM] + [VMEM] * 4 + [ANY] * len(pieces),
        out_specs=[VMEM] * (1 + len(pieces)),
        scratch_shapes=[
            pltpu.VMEM((key_blocks, BLK, 2 * per), BF16),
            pltpu.VMEM((2 * rows, 128), BF16),
            pltpu.VMEM((key_blocks * BLK, 128), F32),
            pltpu.VMEM((rows, 128), F32),
            pltpu.VMEM((8, rows), F32),
            pltpu.VMEM((8, rows), F32),
            pltpu.SemaphoreType.DMA((len(pieces),)),
        ],
        compiler_params=ROOM,
        cost_estimate=cost(45),
        name="attend_back",
    )(sc, q, do, o, lse, *pieces)


def norm(values):
    centered = values - jnp.mean(values, -1, keepdims=True)
    inverse = lax.rsqrt(jnp.mean(centered * centered, -1, keepdims=True) + 1e-6)
    return centered * inverse, inverse


def norm_back(upstream, normed, inverse):
    return inverse * (
        upstream
        - jnp.mean(upstream, -1, keepdims=True)
        - normed * jnp.mean(upstream * normed, -1, keepdims=True)
    )


def normal_parts(x):
    z = jnp.abs(x) * (0.5**0.5)
    bell = jnp.exp(-0.5 * x * x)
    t = 1.0 / (1.0 + 0.3275911 * z)
    poly = t * (
        0.254829592
        + t * (-0.284496736 + t * (1.421413741 + t * (-1.453152027 + t * 1.061405429)))
    )
    upper = 0.5 * poly * bell
    return jnp.where(x >= 0, 1.0 - upper, upper), bell * (2.0 * math.pi) ** -0.5


def dense_kernel(sc, att4, tok, teach, vec, wide_vec, *rest):
    weights, rest = rest[:9], rest[9:]
    outs, (wo, wi, wu, slope, sems) = rest[:11], rest[11:]
    out, fg, ag, att_o, br_o, hl_o, il_o, act_o, ol_o, sums, wide_sums = outs
    rows, width = tok.shape
    hidden = wi.shape[1]
    tile = 512
    copies = [
        weight_copies(full, *weights[3 * i : 3 * i + 3], sems, 3 * i)
        for i, full in enumerate((wo, wi, wu))
    ]
    for group in copies:
        for copy in group:
            copy.start()
    per = att4.shape[2]
    att = jnp.concatenate([att4[g] for g in range(GROUPS)], 1)
    att_o[...] = att
    row = lax.broadcasted_iota(jnp.int32, (rows, 1), 0)
    mask = jnp.where(
        row < BLK, jnp.where(row < sc[0], 1.0, 0.0), jnp.where(row - BLK < sc[1], 1.0, 0.0)
    )
    out_bias, gain_one, shift_one = vec[0:1, :], vec[1:2, :], vec[2:3, :]
    outer_bias, gain_two, shift_two = vec[3:4, :], vec[4:5, :], vec[5:6, :]
    for copy in copies[0]:
        copy.wait()
    first = tok[...].astype(F32) + dot(att, wo[...]) + out_bias
    normed_one, inverse_one = norm(first)
    hidden_in = normed_one * gain_one + shift_one
    hl = hidden_in.astype(BF16)
    hl_o[...] = hl
    for copy in copies[1] + copies[2]:
        copy.wait()
    second = hidden_in + outer_bias
    for n in range(hidden // tile):
        cols = slice(n * tile, (n + 1) * tile)
        inner = dot(hl, wi[:, cols]) + wide_vec[0:1, cols]
        below, density = normal_parts(inner)
        act = (inner * below).astype(BF16)
        act_o[:, cols] = act
        slope[:, cols] = below + inner * density
        second += dot(act, wu[cols, :])
    normed_two, inverse_two = norm(second)
    final = normed_two * gain_two + shift_two
    out[...] = final.astype(BF16)
    residue = (final - teach[...].astype(F32)) * mask
    add = functools.partial(jnp.sum, axis=0, keepdims=True)
    second_grad = norm_back(residue * gain_two, normed_two, inverse_two)
    ol = second_grad.astype(BF16)
    ol_o[...] = ol
    hidden_grad = second_grad
    for n in range(hidden // tile):
        cols = slice(n * tile, (n + 1) * tile)
        il = (dot(ol, wu[cols, :], NT) * slope[:, cols]).astype(BF16)
        il_o[:, cols] = il
        wide_sums[0:1, cols] = add(il.astype(F32))
        hidden_grad += dot(il, wi[:, cols], NT)
    first_grad = norm_back(hidden_grad * gain_one, normed_one, inverse_one)
    fg[...] = first_grad
    br = first_grad.astype(BF16)
    br_o[...] = br
    att_grad = dot(br, wo[...], NT).astype(BF16)
    for g in range(GROUPS):
        ag[g] = att_grad[:, g * per : (g + 1) * per]
    sums[0:1, :] = add(residue * normed_two)
    sums[1:2, :] = add(residue)
    sums[2:3, :] = add(ol.astype(F32))
    sums[3:4, :] = add(hidden_grad * normed_one)
    sums[4:5, :] = add(hidden_grad)
    sums[5:6, :] = add(br.astype(F32))
    sums[6:7, :] = add(residue * residue)
    sums[7:8, :] = jnp.zeros((1, width), F32)


def dense(sc, att4, tok, teach, vec, wide_vec, weights):
    rows, width = tok.shape
    hidden = wide_vec.shape[1]
    narrow = jax.ShapeDtypeStruct((rows, width), BF16)
    wide = jax.ShapeDtypeStruct((rows, hidden), BF16)
    return pl.pallas_call(
        dense_kernel,
        out_shape=[
            narrow,
            jax.ShapeDtypeStruct((rows, width), F32),
            jax.ShapeDtypeStruct(att4.shape, BF16),
            narrow,
            narrow,
            narrow,
            wide,
            wide,
            narrow,
            jax.ShapeDtypeStruct((8, width), F32),
            jax.ShapeDtypeStruct((1, hidden), F32),
        ],
        in_specs=[SMEM] + [VMEM] * 5 + [ANY] * 9,
        out_specs=[VMEM] * 11,
        scratch_shapes=[
            pltpu.VMEM((width, width), BF16),
            pltpu.VMEM((width, hidden), BF16),
            pltpu.VMEM((hidden, width), BF16),
            pltpu.VMEM((rows, hidden), F32),
            pltpu.SemaphoreType.DMA((9,)),
        ],
        compiler_params=ROOM,
        cost_estimate=cost(15),
        name="dense",
    )(sc, att4, tok, teach, vec, wide_vec, *weights)


def dense_grads_kernel(seqs, *refs):
    ins, (g_out, g_inner, g_outer) = refs[: 6 * seqs], refs[6 * seqs :]
    att, br, hl, il, act, ol = (
        jnp.concatenate([ins[6 * s + i][...] for s in range(seqs)], 0) for i in range(6)
    )
    for target, left, right in ((g_out, att, br), (g_inner, hl, il), (g_outer, act, ol)):
        rows = target.shape[1]
        for n in range(4):
            piece = left[:, n * rows : (n + 1) * rows]
            for t in range(right.shape[1] // 768):
                cols = slice(t * 768, (t + 1) * 768)
                target[n, :, cols] = dot(piece, right[:, cols], TN).astype(BF16)


def dense_grads(saved):
    seqs = len(saved)
    width, hidden = saved[0][0].shape[1], saved[0][3].shape[1]
    return pl.pallas_call(
        functools.partial(dense_grads_kernel, seqs),
        out_shape=[
            jax.ShapeDtypeStruct((4, width // 4, width), BF16),
            jax.ShapeDtypeStruct((4, width // 4, hidden), BF16),
            jax.ShapeDtypeStruct((4, hidden // 4, width), BF16),
        ],
        in_specs=[VMEM] * (6 * seqs),
        out_specs=[VMEM] * 3,
        compiler_params=ROOM,
        cost_estimate=cost(10),
        name="dense_grads",
    )(*[member for group in saved for member in group])


def project_grads_kernel(seqs, sc, tok, *refs):
    fgs, refs = refs[:seqs], refs[seqs:]
    grads_in, refs = refs[: 2 * seqs], refs[2 * seqs :]
    wq, wk, wv, first, second, tg, grads, sums, full, sems = refs
    rows, width = tok.shape[1:]
    per = width // GROUPS
    heads = per // DH
    quarter = wq.shape[0] // 2
    copies = []
    for i, own in enumerate((wq, wk, wv)):
        part = pl.ds(i * quarter, quarter)
        copies += weight_copies(full.at[i], own, first.at[part], second.at[part], sems, 3 * i)
    for copy in copies:
        copy.start()

    def head(i, s, g, h):
        if i == 0:
            return grads_in[s][g, :, h * DH : (h + 1) * DH]
        start = h * 128 + (i - 1) * DH
        return grads_in[seqs + s][g, :, start : start + DH]

    def whole(i):
        each = [
            jnp.concatenate([head(i, s, g, h) for g in range(GROUPS) for h in range(heads)], 1)
            for s in range(seqs)
        ]
        return jnp.concatenate(each, 0)

    valid = jnp.concatenate([valid_rows(sc, s, rows) for s in range(seqs)], 0) > 0.0
    dq = whole(0)
    halves = [jnp.where(valid, whole(i), jnp.zeros((), BF16)) for i in (1, 2)]
    flat = tok[...].reshape(seqs * rows, width)
    for copy in copies:
        copy.wait()
    total = jnp.concatenate([fgs[s][...] for s in range(seqs)], 0)
    for i, grad in enumerate((dq, *halves)):
        total += dot(grad, full[i], NT)
        found = dot(flat, grad, TN).astype(BF16)
        half = width // 2
        for n in range(2):
            for t in range(width // 128):
                grads[t % 3, t // 3, n, i * half : (i + 1) * half, :] = found[
                    n * half : (n + 1) * half, t * 128 : (t + 1) * 128
                ]
    tg[...] = total.reshape(seqs, rows, width)
    sums[0:1, :] = jnp.sum(dq.astype(F32), 0, keepdims=True)
    sums[1:2, :] = jnp.sum(halves[1].astype(F32), 0, keepdims=True)
    sums[2:8, :] = jnp.zeros((6, width), F32)


def project_grads(sc, tok, fgs, grads, wq, wk, wv, first, second):
    seqs, rows, width = tok.shape
    return pl.pallas_call(
        functools.partial(project_grads_kernel, seqs),
        out_shape=[
            jax.ShapeDtypeStruct(tok.shape, F32),
            jax.ShapeDtypeStruct((3, 2, 2, 3 * (width // 2), 128), BF16),
            jax.ShapeDtypeStruct((8, width), F32),
        ],
        in_specs=[SMEM] + [VMEM] * (1 + len(fgs) + len(grads)) + [ANY] * 5,
        out_specs=[VMEM] * 3,
        scratch_shapes=[pltpu.VMEM((3, width, width), BF16), pltpu.SemaphoreType.DMA((9,))],
        compiler_params=ROOM,
        cost_estimate=cost(10),
        name="project_grads",
    )(sc, tok, *fgs, *grads, wq, wk, wv, first, second)


MESH = pl.DeviceIdType.MESH


def position():
    ctx = lax.axis_index("ctx")
    return ctx // 4, lax.rem(ctx // 2, 2), lax.rem(ctx, 2), lax.axis_index("wa")


def device(z, y, c, x):
    return z * 4 + y * 2 + c, x


def greet(others):
    barrier = pltpu.get_barrier_semaphore()
    for other in others:
        pl.semaphore_signal(barrier, inc=1, device_id=other, device_id_type=MESH)
    pl.semaphore_wait(barrier, len(others))


def send(src, dst, sems, to):
    copy = pltpu.make_async_remote_copy(
        src_ref=src,
        dst_ref=dst,
        send_sem=sems[0],
        recv_sem=sems[1],
        device_id=to,
        device_id_type=MESH,
    )
    copy.start()
    return copy


def add_low(left, right):
    return (left.astype(F32) + right.astype(F32)).astype(BF16)


def back_kernel(seqs, *refs):
    per_seq = 5
    ins = [refs[per_seq * s : per_seq * (s + 1)] for s in range(seqs)]
    a_own, a_give, b_own, b_give, rq, rkv, dense_out, *refs = refs[per_seq * seqs :]
    q_v, do_v, o_v, lse_v, kv_v, both, dkv, dq, delta, obuf, qbuf = refs[:11]
    from_core, from_y, a_v, b_v, a_in, b_in, a2, b2, a2_in, b2_in = refs[11:21]
    az_in, bz_in, dres, in_sem, c_sem, y_sem, z_sem, q_sem, l_sem, x_sem, dz_sem = refs[21:]
    z, y, c, x = position()
    sibling, beside, over = device(z, y, 1 - c, x), device(z, 1 - y, c, x), device(z, y, c, 1 - x)
    line = [None] + [device(z ^ d, y, c, x) for d in range(1, GROUPS)]
    greet([sibling, beside, over] + line[1:])

    def pair(sems, *index):
        return sems.at[(0, *index)], sems.at[(1, *index)]

    flow = {}
    flow["a"] = send(a_give, a_in, pair(x_sem, 0), over)
    flow["b"] = send(b_give, b_in, pair(x_sem, 1), beside)
    loads = []
    for s in range(seqs):
        targets = [ref.at[s] for ref in (q_v, do_v, o_v, lse_v, kv_v)]
        group = [
            pltpu.make_async_copy(src, dst, in_sem.at[s, i])
            for i, (src, dst) in enumerate(zip(ins[s], targets))
        ]
        for copy in group:
            copy.start()
        loads.append(group)
    own_loads = [
        pltpu.make_async_copy(a_own, a_v, l_sem.at[0]),
        pltpu.make_async_copy(b_own, b_v, l_sem.at[1]),
    ]
    for copy in own_loads:
        copy.start()

    rows = q_v.shape[1]
    heads = q_v.shape[2] // DH
    keys = kv_v.shape[1]
    tile, ktile = rows // 2, 2048
    quarter = keys // 4
    chunk = quarter // GROUPS
    ones = jnp.ones((8, DH), BF16)
    level = jnp.where(lax.broadcasted_iota(jnp.int32, (1, 128), 1) < DH, LN2, 1.0)
    waits = []

    def group_rows(g):
        return pl.ds(pl.multiple_of(g * chunk, chunk), chunk)

    def core_stage(u):
        flow["c", u] = send(
            obuf.at[u, pl.ds(2 * quarter, 2 * quarter)], from_core.at[u], pair(c_sem, u), sibling
        )

    def y_stage(u):
        flow["c", u].wait()
        second = pl.ds(quarter, quarter)
        obuf[u, second] = add_low(obuf[u, second], from_core[u, second])
        flow["y", u] = send(obuf.at[u, second], from_y.at[u], pair(y_sem, u), beside)
        obuf[u, 0:quarter] = add_low(obuf[u, 0:quarter], from_core[u, 0:quarter])

    def z_stage(u):
        flow["y", u].wait()
        obuf[u, 0:quarter] = add_low(obuf[u, 0:quarter], from_y[u])
        for d in range(1, GROUPS):
            src = obuf.at[u, group_rows(z ^ d)]
            waits.append(send(src, rkv.at[u, z], pair(z_sem, u, d), line[d]))
        own = pltpu.make_async_copy(obuf.at[u, group_rows(z)], rkv.at[u, z], z_sem.at[0, u, 0])
        own.start()
        waits.append(own)

    def q_stage(h):
        for d in range(1, GROUPS):
            waits.append(send(qbuf.at[h, z ^ d], rq.at[h, z], pair(q_sem, h, d), line[d]))
        own = pltpu.make_async_copy(qbuf.at[h, z], rq.at[h, z], q_sem.at[0, h, 0])
        own.start()
        waits.append(own)

    a_half, b_half = a2.shape[1], b2.shape[1]

    def dense_second():
        for copy in own_loads:
            copy.wait()
        flow["a"].wait()
        for slot, which in ((0, y), (1, 1 - y)):
            part = pl.ds(pl.multiple_of(which * a_half, 16), a_half)
            a2[slot] = add_low(a_v[part, :], a_in[part, :])
        flow["a"] = send(a2.at[1], a2_in, pair(x_sem, 2), beside)
        flow["b"].wait()
        for slot, which in ((0, x), (1, 1 - x)):
            b2[slot] = add_low(b_v[which], b_in[which])
        flow["b"] = send(b2.at[1], b2_in, pair(x_sem, 3), over)

    low_bit, high_bit = lax.rem(z, 2), z // 2
    parts = (("a", a2, a2_in, az_in), ("b", b2, b2_in, bz_in))

    def rows_at(start, n):
        return pl.ds(pl.multiple_of(start, 16), n)

    def dense_third():
        for i, (name, held, arrived, landing) in enumerate(parts):
            flow[name].wait()
            held[0] = add_low(held[0], arrived[...])
            n = held.shape[1] // 2
            src = held.at[0, rows_at((1 - low_bit) * n, n)]
            flow[name] = send(src, landing.at[0:n], pair(dz_sem, i, 0), line[1])

    def dense_fourth():
        for i, (name, held, _, landing) in enumerate(parts):
            flow[name].wait()
            n = held.shape[1] // 2
            mine = rows_at(low_bit * n, n)
            held[0, mine] = add_low(held[0, mine], landing[0:n])
            src = held.at[0, rows_at(low_bit * n + (1 - high_bit) * (n // 2), n // 2)]
            flow[name] = send(src, landing.at[n : n + n // 2], pair(dz_sem, i, 1), line[2])

    def dense_fifth():
        base = 0
        for name, held, _, landing in parts:
            flow[name].wait()
            n = held.shape[1] // 2
            mine = rows_at(low_bit * n + high_bit * (n // 2), n // 2)
            dres[base : base + n // 2] = add_low(held[0, mine], landing[n : n + n // 2])
            base += n // 2

    units = [(h, s) for h in range(heads) for s in range(seqs)]
    slots = {}
    for u in range(len(units) - 1):
        slots.setdefault(2 * u + 3, []).append(functools.partial(y_stage, u))
        slots.setdefault(2 * u + 5, []).append(functools.partial(z_stage, u))
    slots.setdefault(5, []).append(dense_second)
    slots.setdefault(7, []).append(dense_third)
    slots.setdefault(9, []).append(dense_fourth)
    slots.setdefault(12, []).append(dense_fifth)

    for u, (h, s) in enumerate(units):
        hs = slice(h * DH, (h + 1) * DH)
        lanes = slice(h * 128, (h + 1) * 128)
        if h == 0:
            for copy in loads[s]:
                copy.wait()
        for n in range(2):
            for work in slots.get(2 * u + n, []):
                work()
            part = slice(n * tile, (n + 1) * tile)
            q, do, o = q_v[s, part, hs], do_v[s, part, hs], o_v[s, part, hs]
            zero = jnp.zeros_like(q)
            both[0:tile, :] = jnp.concatenate([q, zero], 1)
            both[tile : 2 * tile, :] = jnp.concatenate([zero, do], 1)
            product = do.astype(F32) * o.astype(F32)
            high = product.astype(BF16)
            remains = (product - high.astype(F32)).astype(BF16)
            delta[...] = dot(ones, high, NT) + dot(ones, remains, NT)
            dq[...] = jnp.zeros_like(dq)

            def step(j, _, u=u, s=s, h=h, n=n, part=part, lanes=lanes):
                span = pl.ds(pl.multiple_of(j * ktile, ktile), ktile)
                kv = kv_v[s, span, lanes]
                b = both[...]
                found = dot(kv, b, NT)
                p = jnp.exp2(jnp.minimum(found[:, :tile] - lse_v[s, h, 0:1, part], 1.0))
                ds = (p * (found[:, tile:] - delta[0:1, :])).astype(BF16)
                grads = dot(jnp.concatenate([ds, p.astype(BF16)], 1), b)
                if n == 0:
                    dkv[span, :] = grads
                else:
                    obuf[u, span, :] = ((dkv[span, :] + grads) * level).astype(BF16)
                dq[...] += dot(ds, kv, TN)
                return 0

            lax.fori_loop(0, keys // ktile, step, 0)
            found = (dq[:, :DH] * DH**-0.5).astype(BF16)
            for i in range(2):
                qbuf[h, 2 * n + i, :, s * DH : (s + 1) * DH] = found[
                    i * (tile // 2) : (i + 1) * (tile // 2)
                ]
        core_stage(u)
        if s == seqs - 1:
            q_stage(h)
    last = len(units) - 1
    for n in sorted(n for n in slots if n >= 2 * len(units)):
        for work in slots[n]:
            work()
    y_stage(last)
    z_stage(last)
    for copy in waits:
        copy.wait()
    done = pltpu.make_async_copy(dres, dense_out, l_sem.at[0])
    done.start()
    done.wait()


def attend_back_all(seqs_in, ready):
    seqs = len(seqs_in)
    q, _, _, lse, held = seqs_in[0]
    rows, per = q.shape
    heads = per // DH
    units = heads * seqs
    keys = held.shape[0]
    chunk = rows // GROUPS
    a, b = ready[0].shape, ready[2].shape
    a_half, b_half, half = a[0] // 2, b[1], a[1]
    dma = pltpu.SemaphoreType.DMA
    return pl.pallas_call(
        functools.partial(back_kernel, seqs),
        out_shape=[
            jax.ShapeDtypeStruct((heads, GROUPS, chunk, 128), BF16),
            jax.ShapeDtypeStruct((units, GROUPS, chunk, 128), BF16),
            jax.ShapeDtypeStruct(((a_half + b_half) // 4, half), BF16),
        ],
        in_specs=[ANY] * (5 * seqs + 4),
        out_specs=[ANY] * 3,
        scratch_shapes=[
            pltpu.VMEM((seqs, rows, per), BF16),
            pltpu.VMEM((seqs, rows, per), BF16),
            pltpu.VMEM((seqs, rows, per), BF16),
            pltpu.VMEM((seqs, *lse.shape), F32),
            pltpu.VMEM((seqs, keys, 2 * per), BF16),
            pltpu.VMEM((rows, 128), BF16),
            pltpu.VMEM((keys, 128), F32),
            pltpu.VMEM((rows // 2, 128), F32),
            pltpu.VMEM((8, rows // 2), F32),
            pltpu.VMEM((units, keys, 128), BF16),
            pltpu.VMEM((heads, GROUPS, chunk, 128), BF16),
            pltpu.VMEM((units, keys // 2, 128), BF16),
            pltpu.VMEM((units, keys // 4, 128), BF16),
            pltpu.VMEM(a, BF16),
            pltpu.VMEM(b, BF16),
            pltpu.VMEM(a, BF16),
            pltpu.VMEM(b, BF16),
            pltpu.VMEM((2, a_half, half), BF16),
            pltpu.VMEM((2, b_half, half), BF16),
            pltpu.VMEM((a_half, half), BF16),
            pltpu.VMEM((b_half, half), BF16),
            pltpu.VMEM((3 * a_half // 4, half), BF16),
            pltpu.VMEM((3 * b_half // 4, half), BF16),
            pltpu.VMEM(((a_half + b_half) // 4, half), BF16),
            dma((seqs, 5)),
            dma((2, units)),
            dma((2, units)),
            dma((2, units, GROUPS)),
            dma((2, heads, GROUPS)),
            dma((2,)),
            dma((2, 4)),
            dma((2, 2, 2)),
        ],
        compiler_params=pltpu.CompilerParams(
            vmem_limit_bytes=63 * 2**20, collective_id=1, has_side_effects=True
        ),
        cost_estimate=cost(120),
        name="attend_back_all",
    )(*[member for group in seqs_in for member in group], *ready)


def vector_of(vec, row, half):
    both = [vec[k, row + 1 : row + 2, :half].astype(F32) for k in range(2)]
    return jnp.concatenate(both, 1)


def start_kernel(seqs, lengths, order, tokens, wq, wk, wv, wo, wi, wu, *refs):
    sc = Counts(lengths, order)
    vectors, refs = refs[:9], refs[9:]
    q_out, kv_out, o_out, lse_out = (refs[i * seqs : (i + 1) * seqs] for i in range(4))
    refs = refs[4 * seqs :]
    back_out, vec_out, others, *dense_out = refs[:6]
    full, q_held, kv_held, vec, own_vec, tok, *refs = refs[6:]
    q_v, kv_v, o_v, lse_v, shade, qa, acc, sums, top, *sems = refs
    v_sem, wx_sem, wy_sem, wc_sem, l_sem, dx_sem, dc_sem, q_sem, z_sem, y_sem, c_sem = sems[:11]
    own_sem, b_sem = sems[11:]
    z, y, c, x = position()
    sibling, beside, over = device(z, y, 1 - c, x), device(z, 1 - y, c, x), device(z, y, c, 1 - x)
    line = [None] + [device(z ^ d, y, c, x) for d in range(1, GROUPS)]
    greet([sibling, beside, over] + line[1:])

    def pair(sem, *index):
        return sem.at[(0, *index)], sem.at[(1, *index)]

    waits = []
    half = wq.shape[0]
    eighth = half // 4

    def rows_of(which, cc, yy):
        start = which * half + (2 * cc + yy) * eighth
        return pl.ds(pl.multiple_of(start, 16), eighth)

    own_rows = pl.ds(pl.multiple_of((2 * c + y) * eighth, 16), eighth)
    tok_in = pltpu.make_async_copy(tokens, tok, l_sem.at[6])
    tok_in.start()
    flow = {}
    turns = (1, 2, 0)
    locals_of = []
    for i in turns:
        own = (wq, wk, wv)[i]
        flow["x", i] = send(
            own.at[own_rows], full.at[i, rows_of(x, c, y)], pair(wx_sem, i), over
        )
    for i in turns:
        own = (wq, wk, wv)[i]
        place = full.at[i, pl.ds(pl.multiple_of(x * half, half), half)]
        copy = pltpu.make_async_copy(own, place, l_sem.at[i])
        copy.start()
        locals_of.append(copy)
    own_vec[...] = jnp.zeros_like(own_vec)
    for i, one in enumerate(vectors):
        row = (i + 1) % len(vectors)
        own_vec[row : row + 1, : one.shape[0]] = one[...].astype(F32)[None].astype(BF16)
    vec[x] = own_vec[...]
    vec_flow = send(own_vec, vec.at[x], pair(v_sem), over)

    def after_x(i):
        flow["x", i].wait()
        got = full.at[i, rows_of(1 - x, c, y)]
        flow["y", i] = send(got, got, pair(wy_sem, i), beside)
        flow["c", i, 0] = send(got, got, pair(wc_sem, i, 0), sibling)

    def after_y(i):
        flow["y", i].wait()
        got = full.at[i, rows_of(1 - x, c, 1 - y)]
        flow["c", i, 1] = send(got, got, pair(wc_sem, i, 1), sibling)

    def after_core(i):
        flow["c", i, 0].wait()
        flow["c", i, 1].wait()

    rows, width = tok.shape[1:]
    per = width // GROUPS
    heads = per // DH
    tok_in.wait()
    flat = tok[...].reshape(seqs * rows, width)
    valid = jnp.concatenate([valid_rows(sc, s, rows) for s in range(seqs)], 0) > 0.0
    lane = lax.broadcasted_iota(jnp.int32, (8, BLK), 1)
    for piece, offset in enumerate((0, 2, 1, 3)):
        owner = lax.bitwise_xor(2 * y + c, offset)
        for g in range(GROUPS):
            for k in range(2):
                start_of = order[(4 * g + owner) * 2 + k] * BLK
                for s in range(seqs):
                    inside = lane + start_of < lengths[s]
                    cols = slice((2 * g + k) * BLK, (2 * g + k + 1) * BLK)
                    shade[s, piece, :, cols] = jnp.where(inside, 0.0, -1e30)
    after_x(1)
    after_x(2)
    after_y(1)
    after_x(0)
    dense_weights = (wo, wi, wu)
    for i, weight in enumerate(dense_weights):
        n = weight.shape[0] // 2
        part = pl.ds(pl.multiple_of(c * n, 16), n)
        flow["dx", i] = send(weight.at[part], dense_out[i].at[part], pair(dx_sem, i), over)
    after_y(2)
    vec_flow.wait()

    def bias(row):
        return vector_of(vec, row, half)

    for copy in locals_of:
        copy.wait()
    after_core(1)
    keys = jnp.where(valid, dot(flat, full[1]), 0.0).astype(BF16)
    after_y(0)
    after_core(2)
    values = jnp.where(valid, dot(flat, full[2]) + bias(1), 0.0).astype(BF16)
    for s in range(seqs):
        rs = slice(s * rows, (s + 1) * rows)
        for g in range(GROUPS):
            for h in range(heads):
                cols = slice(g * per + h * DH, g * per + (h + 1) * DH)
                kv_held[s, g, :, h * 128 : (h + 1) * 128] = jnp.concatenate(
                    [keys[rs, cols], values[rs, cols]], 1
                )

    def kv_sends(s):
        for d in range(1, GROUPS):
            flow["z", s, d] = send(
                kv_held.at[s, z ^ d], kv_v.at[s, 0, z], pair(z_sem, s, d), line[d]
            )

    def q_sends(s):
        for d in range(1, GROUPS):
            flow["q", s, d] = send(q_held.at[s, z ^ d], q_v.at[s, z], pair(q_sem, s, d), line[d])

    kv_sends(0)

    def pass_on(s, d, src):
        g = z ^ d
        flow["ky", s, d] = send(src, kv_v.at[s, 1, g], pair(y_sem, s, d), beside)
        flow["kc", s, d, 0] = send(src, kv_v.at[s, 2, g], pair(c_sem, s, d, 0), sibling)

    def pass_core(s, d):
        flow["ky", s, d].wait()
        got = kv_v.at[s, 1, z ^ d]
        flow["kc", s, d, 1] = send(got, kv_v.at[s, 3, z ^ d], pair(c_sem, s, d, 1), sibling)

    pass_on(0, 0, kv_held.at[0, z])
    after_core(0)
    queries = ((dot(flat, full[0]) + bias(0)) * (DH**-0.5 / LN2)).astype(BF16)
    for s in range(seqs):
        rs = slice(s * rows, (s + 1) * rows)
        for g in range(GROUPS):
            q_held[s, g] = queries[rs, g * per : (g + 1) * per]
    for i in range(3):
        place = full.at[i, pl.ds(pl.multiple_of((1 - x) * half, half), half)]
        copy = pltpu.make_async_copy(place, others.at[i], l_sem.at[3 + i])
        copy.start()
        waits.append(copy)
    copy = pltpu.make_async_copy(vec, vec_out, l_sem.at[7])
    copy.start()
    waits.append(copy)
    for s in range(seqs):
        kv_v[s, 0, z] = kv_held[s, z]
        q_v[s, z] = q_held[s, z]

    def arrive(s, d):
        flow["z", s, d].wait()
        pass_on(s, d, kv_v.at[s, 0, z ^ d])

    def own_and_core(s):
        for d in range(GROUPS):
            flow["kc", s, d, 0].wait()

    def dense_core(i):
        flow["dx", i].wait()
        n = dense_weights[i].shape[0] // 2
        got = dense_out[i].at[pl.ds(pl.multiple_of(c * n, 16), n)]
        waits.append(send(got, got, pair(dc_sem, i), sibling))

    def leave(src, dst, i):
        copy = pltpu.make_async_copy(src, dst, b_sem.at[i])
        copy.start()
        waits.append(copy)

    def attend_part(s, h, pieces):
        lanes = slice(h * 128, (h + 1) * 128)
        count, tile = GROUPS * rows, 1024

        def step(j, _):
            piece = pieces[0] + j * (pieces[1] - pieces[0])
            kv = kv_v[s, piece, :, :, lanes].reshape(count, 128)
            dark = shade[s, piece, 0:1, :]
            for n in range(count // tile):
                part = slice(n * tile, (n + 1) * tile)
                scores = dot(qa[h, part, :], kv, NT) + dark
                high = scores[:, :128]
                for i in range(1, count // 128):
                    high = jnp.maximum(high, scores[:, i * 128 : (i + 1) * 128])
                old = top[h, part, :]
                new = jnp.maximum(old, jnp.max(high, 1, keepdims=True))
                fade = jnp.exp2(old - new)
                each = [
                    jnp.exp2(scores[:, i * 128 : (i + 1) * 128] - new) for i in range(count // 128)
                ]
                sums[h, part, :] = sums[h, part, :] * fade + sum(each)
                p = jnp.concatenate([one.astype(BF16) for one in each], 1)
                acc[h, part, :] = acc[h, part, :] * fade + dot(p, kv)
                top[h, part, :] = new
            return 0

        lax.fori_loop(0, 2, step, 0)

    def attend_begin(s, h):
        hs = slice(h * DH, (h + 1) * DH)
        mine = q_v[s, :, :, hs].reshape(GROUPS * rows, DH)
        qa[h] = jnp.concatenate([mine, jnp.zeros_like(mine)], 1)
        zero = jnp.zeros(acc.shape[1:], F32)
        acc[h], sums[h], top[h] = zero, zero, zero - 1e30

    def attend_end(s, h):
        hs = slice(h * DH, (h + 1) * DH)
        total = jnp.sum(sums[h], 1, keepdims=True)
        logs = top[h] + jnp.log2(jnp.broadcast_to(total, top.shape[1:]))
        lse_v[s, h] = jnp.transpose(logs)[:8]
        found = (acc[h][:, DH:] * (1.0 / total)).astype(BF16)
        o_v[s, :, :, hs] = found.reshape(GROUPS, rows, DH)

    def leave_all(s):
        for i, (src, dst) in enumerate(
            ((q_v, q_out), (kv_v, kv_out), (o_v, o_out), (lse_v, lse_out))
        ):
            leave(src.at[s], dst[s], 4 * s + i)

    for d in range(1, GROUPS):
        arrive(0, d)
        if d > 1:
            pass_core(0, d - 2)
    q_sends(0)
    pass_core(0, 2)
    pass_core(0, 3)
    for d in range(1, GROUPS):
        flow["q", 0, d].wait()
    kv_sends(1)
    own_and_core(0)
    pass_on(1, 0, kv_held.at[1, z])
    for d in range(GROUPS):
        flow["kc", 0, d, 1].wait()
    for h in range(heads):
        attend_begin(0, h)
        attend_part(0, h, (0, 2))
        if h == 1:
            dense_core(0)
        if h == 2:
            pass_core(1, 0)
            q_sends(1)
            for d in range(1, GROUPS):
                arrive(1, d)
        attend_part(0, h, (1, 3))
        attend_end(0, h)
    leave_all(0)
    own_and_core(1)
    for d in range(1, GROUPS):
        flow["q", 1, d].wait()
    for d in range(1, GROUPS):
        waits.append(send(o_v.at[0, z ^ d], back_out.at[z], pair(own_sem, d), line[d]))
    leave(o_v.at[0, z], back_out.at[z], 4 * seqs)
    for h in range(heads):
        attend_begin(1, h)
        attend_part(1, h, (0, 2))
        pass_core(1, h + 1)
    dense_core(1)
    dense_core(2)
    for d in range(GROUPS):
        flow["kc", 1, d, 1].wait()
    for h in range(heads):
        attend_part(1, h, (1, 3))
        attend_end(1, h)
    leave_all(1)
    for copy in waits:
        copy.wait()


def start(lengths, order, tok, weights, vectors):
    seqs, rows, width = tok.shape
    per = width // GROUPS
    half = weights[0].shape[0]
    joined = (16, vectors[-1].shape[0])
    heads, total = per // DH, GROUPS * rows
    narrow = jax.ShapeDtypeStruct((GROUPS, rows, per), BF16)
    dma = pltpu.SemaphoreType.DMA
    return pl.pallas_call(
        functools.partial(start_kernel, seqs),
        out_shape=[narrow] * seqs
        + [jax.ShapeDtypeStruct((4, GROUPS, rows, 2 * per), BF16)] * seqs
        + [narrow] * seqs
        + [jax.ShapeDtypeStruct((heads, 8, total), F32)] * seqs
        + [
            narrow,
            jax.ShapeDtypeStruct((2, *joined), BF16),
            jax.ShapeDtypeStruct((3, half, width), BF16),
        ]
        + [jax.ShapeDtypeStruct(w.shape, BF16) for w in weights[3:]],
        in_specs=[SMEM] * 2 + [ANY] * 7 + [VMEM] * 9,
        out_specs=[ANY] * (4 * seqs + 6),
        scratch_shapes=[
            pltpu.VMEM((3, width, width), BF16),
            pltpu.VMEM((seqs, GROUPS, rows, per), BF16),
            pltpu.VMEM((seqs, GROUPS, rows, 2 * per), BF16),
            pltpu.VMEM((2, *joined), BF16),
            pltpu.VMEM(joined, BF16),
            pltpu.VMEM(tok.shape, BF16),
            pltpu.VMEM((seqs, GROUPS, rows, per), BF16),
            pltpu.VMEM((seqs, 4, GROUPS, rows, 2 * per), BF16),
            pltpu.VMEM((seqs, GROUPS, rows, per), BF16),
            pltpu.VMEM((seqs, heads, 8, total), F32),
            pltpu.VMEM((seqs, 4, 8, total), F32),
            pltpu.VMEM((heads, total, 128), BF16),
            pltpu.VMEM((heads, total, 128), F32),
            pltpu.VMEM((heads, total, 128), F32),
            pltpu.VMEM((heads, total, 128), F32),
            dma((2,)),
            dma((2, 3)),
            dma((2, 3)),
            dma((2, 3, 2)),
            dma((8,)),
            dma((2, 3)),
            dma((2, 3)),
            dma((2, seqs, GROUPS)),
            dma((2, seqs, GROUPS)),
            dma((2, seqs, GROUPS)),
            dma((2, seqs, GROUPS, 2)),
            dma((2, GROUPS)),
            dma((4 * seqs + 1,)),
        ],
        compiler_params=pltpu.CompilerParams(
            vmem_limit_bytes=63 * 2**20, collective_id=4, has_side_effects=True
        ),
        cost_estimate=cost(80),
        name="start",
    )(lengths, order, tok, *weights, *vectors)


def middle_stage(s, att, mask, tok, teach, vec, weights, keep, outs, first_done, outer_done):
    wo, wi, wu, slope = weights
    att_k, br_k, hl_k, il_k, act_k, ol_k = keep
    out, fg, sums, wide_sums = outs
    rows = att.shape[0]
    hidden = wi.shape[1]
    tile = 768
    rs = slice(s * rows, (s + 1) * rows)
    half = tok.shape[2] // 2
    out_bias, gain_one, shift_one, outer_bias, gain_two, shift_two = (
        vector_of(vec, row, half) for row in range(2, 8)
    )
    add = functools.partial(jnp.sum, axis=0, keepdims=True)

    def collect(target, value):
        if s == 0:
            target[...] = value
        else:
            target[...] += value

    att_k[rs, :] = att
    first_done[0]()
    first = tok[s].astype(F32) + dot(att, wo[...]) + out_bias
    normed_one, inverse_one = norm(first)
    hidden_in = normed_one * gain_one + shift_one
    hl = hidden_in.astype(BF16)
    hl_k[rs, :] = hl
    first_done[1]()
    second = hidden_in + outer_bias
    for n in range(hidden // tile):
        cols = slice(n * tile, (n + 1) * tile)
        k, begin = divmod(n * tile, hidden // 2)
        inner = dot(hl, wi[:, cols]) + vec[k, 0:1, begin : begin + tile].astype(F32)
        below, density = normal_parts(inner)
        act = (inner * below).astype(BF16)
        act_k[rs, cols] = act
        slope[:, cols] = below + inner * density
        second += dot(act, wu[cols, :])
    normed_two, inverse_two = norm(second)
    final = normed_two * gain_two + shift_two
    out[s] = final.astype(BF16)
    residue = (final - teach[s].astype(F32)) * mask
    collect(sums.at[0:1], add(residue * normed_two))
    collect(sums.at[1:2], add(residue))
    collect(sums.at[6:7], add(residue * residue))
    second_grad = norm_back(residue * gain_two, normed_two, inverse_two)
    ol = second_grad.astype(BF16)
    ol_k[rs, :] = ol
    collect(sums.at[2:3], add(ol.astype(F32)))
    outer_done()
    hidden_grad = second_grad
    for n in range(hidden // tile):
        cols = slice(n * tile, (n + 1) * tile)
        il = (dot(ol, wu[cols, :], NT) * slope[:, cols]).astype(BF16)
        il_k[rs, cols] = il
        collect(wide_sums.at[0:1, cols], add(il.astype(F32)))
        hidden_grad += dot(il, wi[:, cols], NT)
    first_grad = norm_back(hidden_grad * gain_one, normed_one, inverse_one)
    fg[s] = first_grad
    br = first_grad.astype(BF16)
    br_k[rs, :] = br
    collect(sums.at[3:4], add(hidden_grad * normed_one))
    collect(sums.at[4:5], add(hidden_grad))
    collect(sums.at[5:6], add(br.astype(F32)))
    return dot(br, wo[...], NT).astype(BF16)


def middle_kernel(seqs, lengths, order, tok, teach, vec, *refs):
    sc = Counts(lengths, order)
    attended, weights, refs = refs[:seqs], refs[seqs : seqs + 6], refs[seqs + 6 :]
    out, fg, sums, wide_sums, a_own, a_give, b_own, b_give = refs[:8]
    grads_in, refs = refs[8 : 8 + seqs], refs[8 + seqs :]
    wo, wi, wu, slope, o_in, g_out, att_k, br_k, hl_k, il_k, act_k, ol_k = refs[:12]
    own, given, w_sem, o_sem, g_sem, c_sem = refs[12:]
    z, y, c, x = position()
    sibling = device(z, y, 1 - c, x)
    line = [None] + [device(z ^ d, y, c, x) for d in range(1, GROUPS)]
    greet([sibling] + line[1:])
    coming, going = {}, {}
    for s in range(seqs):
        if s == 0:
            coming[s, 0] = pltpu.make_async_copy(attended[s], o_in.at[s], o_sem.at[0, s, 0])
            coming[s, 0].start()
            continue
        for d in range(1, GROUPS):
            sems = o_sem.at[0, s, d], o_sem.at[1, s, d]
            coming[s, d] = send(attended[s].at[z ^ d], o_in.at[s, z], sems, line[d])
        coming[s, 0] = pltpu.make_async_copy(attended[s].at[z], o_in.at[s, z], o_sem.at[0, s, 0])
        coming[s, 0].start()
    copies = [
        half_copies(full, *weights[2 * i : 2 * i + 2], w_sem, 2 * i)
        for i, full in enumerate((wo, wi, wu))
    ]
    for group in copies:
        for copy in group:
            copy.start()

    def loaded(which):
        for i in which:
            for copy in copies[i]:
                copy.wait()

    half = wo.shape[0] // 2
    blocks = wi.shape[1] // (2 * half)
    base = (1 + blocks) * half
    core = []

    def store(k, start, value):
        low_value = value.astype(BF16)
        own[0, k, start : start + half, :] = low_value[:, :half]
        own[1, k, start : start + half, :] = low_value[:, half:]

    def pass_core(k, start, stop):
        place = pl.ds(start, stop - start)
        i = len(core)
        sems = c_sem.at[0, i], c_sem.at[1, i]
        core.append(send(own.at[1 - c, k, place], given.at[k, place], sems, sibling))

    def outer_grads():
        for k in range(2):
            for t in range(blocks):
                rows_of = slice((k * blocks + t) * half, (k * blocks + t + 1) * half)
                store(k, base + t * half, dot(act_k[:, rows_of], ol_k[...], TN))
            pass_core(k, base, base + blocks * half)

    rows = tok.shape[1]
    per = o_in.shape[3]
    for s in range(seqs):
        for d in range(GROUPS if s > 0 else 1):
            coming[s, d].wait()
        att = jnp.concatenate([o_in[s, g] for g in range(GROUPS)], 1)
        mask = valid_rows(sc, s, rows)
        waits = (lambda: loaded([0]), lambda: loaded([1, 2])) if s == 0 else (lambda: None,) * 2
        found = middle_stage(
            s,
            att,
            mask,
            tok,
            teach,
            vec,
            (wo, wi, wu, slope),
            (att_k, br_k, hl_k, il_k, act_k, ol_k),
            (out, fg, sums, wide_sums),
            waits,
            outer_grads if s == seqs - 1 else lambda: None,
        )
        for g in range(GROUPS):
            g_out[s, g] = found[:, g * per : (g + 1) * per]
        for d in range(1, GROUPS):
            sems = g_sem.at[0, s, d], g_sem.at[1, s, d]
            going[s, d] = send(g_out.at[s, z ^ d], grads_in[s].at[z], sems, line[d])
        going[s, 0] = pltpu.make_async_copy(g_out.at[s, z], grads_in[s].at[z], g_sem.at[0, s, 0])
        going[s, 0].start()
    sums[7:8, :] = jnp.zeros((1, sums.shape[1]), F32)

    for k in range(2):
        ks = slice(k * half, (k + 1) * half)
        store(k, 0, dot(att_k[:, ks], br_k[...], TN))
        for t in range(blocks):
            cols = slice(2 * t * half, 2 * (t + 1) * half)
            store(k, (1 + t) * half, dot(hl_k[:, ks], il_k[:, cols], TN))
        pass_core(k, 0, base)
    for copy in core:
        copy.wait()
    mine = own.at[c]
    cut, b_half = a_own.shape[0], b_own.shape[1]
    a_own[...] = add_low(mine[x, 0:cut], given[x, 0:cut])
    a_give[...] = add_low(mine[1 - x, 0:cut], given[1 - x, 0:cut])
    for k in range(2):
        for target, which in ((b_own, y), (b_give, 1 - y)):
            part = pl.ds(pl.multiple_of(cut + which * b_half, 16), b_half)
            target[k] = add_low(mine[k, part], given[k, part])
    for copy in going.values():
        copy.wait()


def cut_of(total):
    return total // 256 * 128


def middle(lengths, order, tok, teach, vec, attended, weights):
    seqs, rows, width = tok.shape
    hidden = 2 * vec.shape[2]
    half = width // 2
    total = half + hidden
    cut = cut_of(total)
    dma = pltpu.SemaphoreType.DMA
    narrow, wide = (seqs * rows, width), (seqs * rows, hidden)
    b_shape = jax.ShapeDtypeStruct((2, (total - cut) // 2, half), BF16)
    a_shape = jax.ShapeDtypeStruct((cut, half), BF16)
    groups, _, per = attended[0].shape
    return pl.pallas_call(
        functools.partial(middle_kernel, seqs),
        out_shape=[
            jax.ShapeDtypeStruct(tok.shape, BF16),
            jax.ShapeDtypeStruct(tok.shape, F32),
            jax.ShapeDtypeStruct((8, width), F32),
            jax.ShapeDtypeStruct((1, hidden), F32),
            a_shape,
            a_shape,
            b_shape,
            b_shape,
        ]
        + [jax.ShapeDtypeStruct(a.shape, BF16) for a in attended],
        in_specs=[SMEM] * 2 + [VMEM] * 3 + [ANY] * (seqs + 6),
        out_specs=[VMEM] * 8 + [ANY] * seqs,
        scratch_shapes=[
            pltpu.VMEM((width, width), BF16),
            pltpu.VMEM((width, hidden), BF16),
            pltpu.VMEM((hidden, width), BF16),
            pltpu.VMEM((rows, hidden), F32),
            pltpu.VMEM((seqs, groups, rows, per), BF16),
            pltpu.VMEM((seqs, groups, rows, per), BF16),
            pltpu.VMEM(narrow, BF16),
            pltpu.VMEM(narrow, BF16),
            pltpu.VMEM(narrow, BF16),
            pltpu.VMEM(wide, BF16),
            pltpu.VMEM(wide, BF16),
            pltpu.VMEM(narrow, BF16),
            pltpu.VMEM((2, 2, total, half), BF16),
            pltpu.VMEM((2, total, half), BF16),
            dma((6,)),
            dma((2, seqs, groups)),
            dma((2, seqs, groups)),
            dma((2, 4)),
        ],
        compiler_params=pltpu.CompilerParams(
            vmem_limit_bytes=63 * 2**20, collective_id=3, has_side_effects=True
        ),
        cost_estimate=cost(60),
        name="middle",
    )(lengths, order, tok, teach, vec, *attended, *weights)


def finish_kernel(
    seqs, lengths, order, tok, fg, rq, rkv, dense_sums, wide_sums, ready, wq, wk, wv, others, *rest
):
    sc = Counts(lengths, order)
    tg, out, dense_out, small_out, *rest = rest
    full, grads, acc, from_core, from_x, from_y, from_z, res, vec, vec_in, dense_res = rest[:11]
    w_sems, sems, small_sems, d_sems, last_sem = rest[11:]
    z, y, c, x = position()
    sibling, beside, over = device(z, y, 1 - c, x), device(z, 1 - y, c, x), device(z, y, c, 1 - x)
    line = [None] + [device(z ^ d, y, c, x) for d in range(1, GROUPS)]
    greet([sibling, beside, over] + line[1:])

    a_half = cut_of(dense_res.shape[1]) // 2
    b_half = dense_res.shape[1] // 2 - a_half
    low_bit, high_bit = lax.rem(z, 2), z // 2
    dense_parts = ((0, a_half, y * a_half), (a_half // 4, b_half, 2 * a_half + y * b_half))

    def dense_rows(start, n):
        return dense_res.at[c, pl.ds(pl.multiple_of(start, 16), n)]

    def d_pair(k, i):
        return d_sems.at[0, k, i], d_sems.at[1, k, i]

    dense_flows = [None, None]

    def dense_step(i, k):
        start, n, base = dense_parts[i]
        if k > 0:
            dense_flows[i].wait()
        begin = base + (low_bit * (n // 2) if k < 2 else 0) + (high_bit * (n // 4) if k < 1 else 0)
        size = (n // 4, n // 2, n, 2 * n)[k]
        place = dense_rows(begin if k < 3 else 2 * a_half * i, size)
        if k == 0:
            place[...] = ready[start : start + size]
        to = (line[2], line[1], beside, sibling)[k]
        dense_flows[i] = send(place, place, d_pair(k, i), to)

    dense_step(0, 0)
    rows, width = tok.shape[1:]
    heads = width // GROUPS // DH
    copies = []
    for i, own in enumerate((wq, wk, wv)):
        copies += half_copies(full.at[i], own, others.at[i], w_sems, 2 * i)
    for copy in copies:
        copy.start()

    def head(i, s, g, h):
        if i == 0:
            return rq[h, g, :, s * DH : (s + 1) * DH]
        return rkv[h * seqs + s, g, :, (i - 1) * DH : i * DH]

    def whole(i):
        each = [
            jnp.concatenate([head(i, s, g, h) for g in range(GROUPS) for h in range(heads)], 1)
            for s in range(seqs)
        ]
        return jnp.concatenate(each, 0)

    valid = jnp.concatenate([valid_rows(sc, s, rows) for s in range(seqs)], 0) > 0.0
    parted = [whole(0)] + [jnp.where(valid, whole(i), jnp.zeros((), BF16)) for i in (1, 2)]
    flat = tok[...].reshape(seqs * rows, width)
    wide = width // 2
    for i, grad in enumerate(parted):
        found = dot(flat, grad, TN).astype(BF16)
        for n in range(2):
            for t in range(width // 128):
                grads[t % 3, t // 3, n, i * wide : (i + 1) * wide, :] = found[
                    n * wide : (n + 1) * wide, t * 128 : (t + 1) * 128
                ]
    lines_of = [dense_sums[i : i + 1, :] for i in range(7)]
    lines_of += [jnp.sum(grad.astype(F32), 0, keepdims=True) for grad in (parted[0], parted[2])]
    lines_of.append(wide_sums[...])
    row = 0
    for one in lines_of:
        for t in range(one.shape[1] // 128):
            vec[row : row + 1, :] = one[:, t * 128 : (t + 1) * 128]
            row += 1
    valid_count = sum(jnp.clip(sc[i], 0, BLK) for i in range(2 * seqs))
    vec[row:, :] = jnp.full((vec.shape[0] - row, 128), valid_count.astype(F32))

    parts, rows_each = grads.shape[0], grads.shape[3]
    half, piece = rows_each // 2, rows_each // 8
    own_half = pl.ds(pl.multiple_of(y * half, half), half)
    other_half = pl.ds(pl.multiple_of((1 - y) * half, half), half)

    def piece_of(g):
        return pl.ds(pl.multiple_of(y * half + g * piece, piece), piece)

    def pair(k, p):
        return sems.at[0, k, p], sems.at[1, k, p]

    def small_pair(k):
        return small_sems.at[0, k], small_sems.at[1, k]

    core = [
        send(grads.at[p, 1 - c], from_core.at[p], pair(0, p), sibling) for p in range(parts)
    ]
    short = send(vec, vec_in.at[0], small_pair(0), sibling)
    flows, lines, spread = {}, {}, {}

    def from_pair(p):
        core[p].wait()
        acc[p] = add_low(grads[p, c], from_core[p])

    def x_send(p):
        if p == 1:
            flows[p] = send(acc.at[p, 1 - x, own_half], from_x.at[p, own_half], pair(2, p), over)
        else:
            flows[p] = send(acc.at[p, 1 - x], from_x.at[p], pair(1, p), over)

    def x_add(p):
        flows[p].wait()
        if p == 1:
            acc[p, x, own_half] = add_low(acc[p, x, own_half], from_x[p, own_half])
        else:
            acc[p, x] = add_low(acc[p, x], from_x[p])

    def y_send(p):
        if p == 1:
            flows[p] = send(acc.at[p, :, other_half], from_y.at[p], pair(1, p), beside)
        else:
            flows[p] = send(acc.at[p, x, other_half], from_y.at[p, 0], pair(2, p), beside)

    def y_add(p):
        flows[p].wait()
        if p == 1:
            for k in range(2):
                acc[p, k, own_half] = add_low(acc[p, k, own_half], from_y[p, k])
        else:
            acc[p, x, own_half] = add_low(acc[p, x, own_half], from_y[p, 0])

    def z_send(p):
        for d in range(1, GROUPS):
            lines[p, d] = send(
                acc.at[p, x, piece_of(z ^ d)], from_z.at[p, d], pair(2 + d, p), line[d]
            )

    def z_add(p):
        total = acc[p, x, piece_of(z)].astype(F32)
        for d in range(1, GROUPS):
            lines[p, d].wait()
            total += from_z[p, d].astype(F32)
        place = res.at[c, p, piece_of(z)]
        place[...] = total.astype(BF16)
        for d in range(1, GROUPS):
            spread[p, d] = send(place, place, pair(5 + d, p), line[d])

    def y_gather(p):
        for d in range(1, GROUPS):
            spread[p, d].wait()
        place = res.at[c, p, own_half]
        flows[p] = send(place, place, pair(9, p), beside)

    def core_gather(p):
        flows[p].wait()
        flows[p] = send(res.at[c, p], res.at[c, p], pair(10, p), sibling)

    from_pair(0)
    x_send(0)
    from_pair(1)
    y_send(1)
    from_pair(2)
    short.wait()
    vec_in[8] = vec[...] + vec_in[0]
    short = send(vec_in.at[8], vec_in.at[1], small_pair(1), over)
    dense_step(0, 1)
    dense_step(1, 0)
    for copy in copies:
        copy.wait()
    total = jnp.concatenate([fg[s] for s in range(seqs)], 0)
    for i, grad in enumerate(parted):
        total += dot(grad, full[i], NT)
    tg[...] = total.reshape(seqs, rows, width)
    x_add(0)
    x_send(2)
    y_send(0)
    y_add(1)
    x_send(1)
    short.wait()
    vec[...] = vec_in[8] + vec_in[1]
    short = send(vec, vec_in.at[2], small_pair(2), beside)
    y_add(0)
    z_send(0)
    dense_step(0, 2)
    dense_step(1, 1)
    x_add(2)
    y_send(2)
    x_add(1)
    z_send(1)
    z_add(0)
    short.wait()
    vec[...] = vec[...] + vec_in[2]
    vec_in[4 + z] = vec[...]
    shorts = [
        send(vec, vec_in.at[4 + z], small_pair(2 + d), line[d]) for d in range(1, GROUPS)
    ]
    y_add(2)
    z_send(2)
    dense_step(1, 2)
    z_add(1)
    y_gather(0)
    z_add(2)
    dense_step(0, 3)
    y_gather(1)
    y_gather(2)
    for copy in shorts:
        copy.wait()
    small_out[...] = vec_in[4] + vec_in[5] + (vec_in[6] + vec_in[7])
    for p in range(parts):
        core_gather(p)
    dense_step(1, 3)
    for copy in dense_flows:
        copy.wait()
    done = [pltpu.make_async_copy(dense_res, dense_out, last_sem.at[1])]
    done[0].start()
    for p in (1, 0, 2):
        flows[p].wait()
    done.append(pltpu.make_async_copy(res, out, last_sem.at[0]))
    done[1].start()
    for copy in done:
        copy.wait()


def finish(lengths, order, tok, fg, rq, rkv, sums, wide_sums, ready, wq, wk, wv, others):
    seqs, _, width = tok.shape
    short = (-(-(9 * width + wide_sums.shape[1] + 128) // 1024) * 8, 128)
    parts, rows, lanes = 3, 3 * (width // 2), 128
    total, half = 8 * ready.shape[0], ready.shape[1]
    dma = pltpu.SemaphoreType.DMA
    return pl.pallas_call(
        functools.partial(finish_kernel, seqs),
        out_shape=[
            jax.ShapeDtypeStruct(tok.shape, F32),
            jax.ShapeDtypeStruct((2, parts, rows, lanes), BF16),
            jax.ShapeDtypeStruct((2, total, half), BF16),
            jax.ShapeDtypeStruct(short, F32),
        ],
        in_specs=[SMEM] * 2 + [VMEM] * 7 + [ANY] * 4,
        out_specs=[VMEM, ANY, ANY, VMEM],
        scratch_shapes=[
            pltpu.VMEM((3, width, width), BF16),
            pltpu.VMEM((parts, 2, 2, rows, lanes), BF16),
            pltpu.VMEM((parts, 2, rows, lanes), BF16),
            pltpu.VMEM((parts, 2, rows, lanes), BF16),
            pltpu.VMEM((parts, rows, lanes), BF16),
            pltpu.VMEM((parts, 2, rows // 2, lanes), BF16),
            pltpu.VMEM((parts, GROUPS, rows // 8, lanes), BF16),
            pltpu.VMEM((2, parts, rows, lanes), BF16),
            pltpu.VMEM(short, F32),
            pltpu.VMEM((9, *short), F32),
            pltpu.VMEM((2, total, half), BF16),
            dma((6,)),
            dma((2, 11, parts)),
            dma((2, 6)),
            dma((2, 4, 2)),
            dma((2,)),
        ],
        compiler_params=pltpu.CompilerParams(
            vmem_limit_bytes=63 * 2**20, collective_id=2, has_side_effects=True
        ),
        cost_estimate=cost(70),
        name="finish",
    )(lengths, order, tok, fg, rq, rkv, sums, wide_sums, ready, wq, wk, wv, others)


def unpack_kernel(qkv_in, total_in, small, rows_in, tokens_in, *refs):
    outs, moved, rows, loss, refs = refs[:6], refs[6:8], refs[8:17], refs[17], refs[18:]
    qkv, total, rows_v, tokens_v, narrow, inner, outer, sems, in_sems = refs
    loads = [
        pltpu.make_async_copy(src, dst, in_sems.at[i])
        for i, (src, dst) in enumerate(
            ((total_in, total), (qkv_in, qkv), (rows_in, rows_v), (tokens_in, tokens_v))
        )
    ]
    for copy in loads:
        copy.start()
    half = qkv.shape[2] // 3
    blocks = inner.shape[1] // (2 * half)
    copies = []

    def leave(src, i):
        copy = pltpu.make_async_copy(src, outs[i], sems.at[i])
        copy.start()
        copies.append(copy)

    loads[0].wait()
    for k in range(2):
        cols = slice(k * half, (k + 1) * half)
        outer[:, cols] = total[k, (1 + blocks) * half :].astype(F32)
    leave(outer, 5)
    for k in range(2):
        for t in range(blocks):
            cols = slice((2 * t + k) * half, (2 * t + k + 1) * half)
            inner[:, cols] = total[k, (1 + t) * half : (2 + t) * half].astype(F32)
    leave(inner, 4)
    for i, (src, dst) in enumerate(zip((rows_v, tokens_v), moved)):
        loads[2 + i].wait()
        copy = pltpu.make_async_copy(src, dst, sems.at[6 + i])
        copy.start()
        copies.append(copy)
    loads[1].wait()
    for i in range(3):
        for k in range(2):
            for p in range(3):
                cols = slice((3 * k + p) * 128, (3 * k + p + 1) * 128)
                narrow[i, :, cols] = qkv[k, p, i * half : (i + 1) * half].astype(F32)
        leave(narrow.at[i], i)
    for k in range(2):
        narrow[3, :, k * half : (k + 1) * half] = total[k, 0:half].astype(F32)
    leave(narrow.at[3], 3)
    x = lax.axis_index("wa")
    tiles = 2 * half // 128
    starts = [tiles * i for i in (0, 1, 2, 3, 4, 5, 7, 8)] + [9 * tiles]
    for one, begin in zip(rows, starts):
        n = one.shape[0] // 128
        for t in range(n):
            one[t * 128 : (t + 1) * 128] = small[pl.ds(begin + x * n + t, 1), :][0]
    end = 9 * tiles + 2 * rows[8].shape[0] // 128
    squares = jnp.sum(small[6 * tiles : 7 * tiles, :], keepdims=True)
    loss[...] = squares / (small[end : end + 1, :1] * (2.0 * half))
    for copy in copies:
        copy.wait()


def unpack(qkv, total, small, output, tokens_grad, hidden):
    half = total.shape[2]
    narrow = jax.ShapeDtypeStruct((half, 2 * half), F32)
    return pl.pallas_call(
        unpack_kernel,
        out_shape=[narrow] * 4
        + [
            jax.ShapeDtypeStruct((half, hidden), F32),
            jax.ShapeDtypeStruct((hidden // 2, 2 * half), F32),
            jax.ShapeDtypeStruct(output.shape, BF16),
            jax.ShapeDtypeStruct(tokens_grad.shape, F32),
        ]
        + [jax.ShapeDtypeStruct((half,), F32)] * 8
        + [jax.ShapeDtypeStruct((hidden // 2,), F32), jax.ShapeDtypeStruct((1, 1), F32)],
        in_specs=[ANY, ANY, VMEM, ANY, ANY],
        out_specs=[ANY] * 8 + [VMEM] * 10,
        scratch_shapes=[
            pltpu.VMEM(qkv.shape, BF16),
            pltpu.VMEM(total.shape, BF16),
            pltpu.VMEM(output.shape, BF16),
            pltpu.VMEM(tokens_grad.shape, F32),
            pltpu.VMEM((4, half, 2 * half), F32),
            pltpu.VMEM((half, hidden), F32),
            pltpu.VMEM((hidden // 2, 2 * half), F32),
            pltpu.SemaphoreType.DMA((8,)),
            pltpu.SemaphoreType.DMA((4,)),
        ],
        compiler_params=ROOM,
        cost_estimate=cost(10),
        name="unpack",
    )(qkv, total, small, output, tokens_grad)


def pick(table, index):
    places = jnp.arange(table.shape[0], dtype=jnp.int32)
    return jnp.sum(jnp.where(index[..., None] == places, table, 0), -1)


def shards(
    size,
    tokens,
    teacher,
    lengths,
    block_order,
    query_weight,
    query_bias,
    key_weight,
    value_weight,
    value_bias,
    out_weight,
    out_bias,
    gain_one,
    shift_one,
    inner_weight,
    inner_bias,
    outer_weight,
    outer_bias,
    gain_two,
    shift_two,
):
    seqs, rows, width = tokens.shape
    per_plane = size // GROUPS
    blocks_each = rows // BLK
    ctx, x = lax.axis_index("ctx"), lax.axis_index("wa")
    c, place = lax.rem(ctx, 2), lax.rem(ctx, per_plane)
    masks = [1 << b for b in reversed(range(per_plane.bit_length() - 1))]
    offsets = [0]
    for m in masks:
        offsets += [o ^ m for o in offsets]

    def across(value):
        return lax.ppermute(value, "wa", [(0, 1), (1, 0)])

    def flip(value, m):
        return lax.ppermute(value, "ctx", [(i, i ^ m) for i in range(size)])

    lines = [[g * per_plane + r for g in range(GROUPS)] for r in range(per_plane)]

    def turn(value):
        return lax.all_to_all(value, "ctx", 0, 0, axis_index_groups=lines)

    cores = [[i for i in range(size) if i % 2 == k] for k in range(2)]

    def paired(mine):
        sibling = flip(mine, 1)
        return jnp.where(c == 0, jnp.stack([mine, sibling]), jnp.stack([sibling, mine]))

    def reduced(grad):
        four = grad.reshape(2, 2, *grad.shape[1:])
        keep = lax.dynamic_index_in_dim(four, c, 1, False)
        give = lax.dynamic_index_in_dim(four, 1 - c, 1, False)
        keep = add_low(keep, flip(give, 1))
        mine = lax.dynamic_index_in_dim(keep, x, 0, False)
        mine = add_low(mine, across(lax.dynamic_index_in_dim(keep, 1 - x, 0, False)))
        return paired(lax.psum(mine, "ctx", axis_index_groups=cores))

    def reduced_dense(grad):
        four = grad.reshape(2, 2, *grad.shape[1:])
        keep = lax.dynamic_index_in_dim(four, c, 1, False)
        give = lax.dynamic_index_in_dim(four, 1 - c, 1, False)
        keep = add_low(keep, flip(give, 1))
        mine = lax.psum_scatter(
            keep.reshape(-1, keep.shape[-1]), "wa", scatter_dimension=0, tiled=True
        )
        return lax.psum(mine, "ctx", axis_index_groups=cores)

    vectors = (
        query_bias,
        value_bias,
        out_bias,
        gain_one,
        shift_one,
        outer_bias,
        gain_two,
        shift_two,
        inner_bias,
    )
    half, hidden = width // 2, 2 * inner_bias.shape[0]
    fused = per_plane == 4

    if fused:
        found = start(
            lengths,
            block_order,
            tokens,
            (query_weight, key_weight, value_weight, out_weight, inner_weight, outer_weight),
            vectors,
        )
        queries = [q.reshape(-1, BLK, q.shape[2]) for q in found[:seqs]]
        pieces = [[kv.reshape(-1, BLK, kv.shape[3])] for kv in found[seqs : 2 * seqs]]
        attended, lses = found[2 * seqs : 3 * seqs], found[3 * seqs : 4 * seqs]
        first_back, pair, others, *rest = found[4 * seqs :]
        dense_weights = [out_weight, rest[0], inner_weight, rest[1], outer_weight, rest[2]]
    else:
        count = block_order.shape[0]
        ids = jnp.arange(count, dtype=jnp.int32)
        owner = ids // blocks_each
        index_of = jnp.array([offsets.index(o) for o in range(per_plane)], jnp.int32)
        piece_of = pick(index_of, (owner % per_plane) ^ place)
        spot = (piece_of * GROUPS + owner // per_plane) * blocks_each + ids % blocks_each
        key_order = jnp.sum(jnp.where(block_order[None, :] == ids[:, None], spot[None, :], 0), 1)
        near = jnp.arange(GROUPS * blocks_each, dtype=jnp.int32)
        near_ids = (near // blocks_each * per_plane + place) * blocks_each + near % blocks_each
        near_pos = pick(block_order, near_ids)
        rank = jnp.sum((near_pos[None, :] < near_pos[:, None]).astype(jnp.int32), 1)
        query_order = jnp.sum(jnp.where(rank[None, :] == near[:, None], near[None, :], 0), 1)
        own_pos = pick(block_order, ctx * blocks_each + jnp.arange(blocks_each, dtype=jnp.int32))
        scalars, row_counts = [], []
        for s in range(seqs):
            used = jnp.sum((near_pos * BLK < lengths[s]).astype(jnp.int32))
            head = jnp.concatenate([lengths[s][None], used[None], jnp.zeros((6,), jnp.int32)])
            scalars.append(jnp.concatenate([head, query_order, key_order]))
            row_counts.append(jnp.clip(lengths[s] - own_pos * BLK, 0, BLK))

        counts = jnp.concatenate(row_counts)
        own_vec = jnp.concatenate(vectors)[None]
        other_vec = across(own_vec)
        pair = jnp.where(
            x == 0, jnp.stack([own_vec, other_vec]), jnp.stack([other_vec, own_vec])
        ).astype(F32)
        narrow = pair[:, 0, : 8 * half].reshape(2, 8, half).swapaxes(0, 1).reshape(8, width)
        wide_vec = pair[:, 0, 8 * half :].reshape(1, -1)

        def quarter(weight):
            n = weight.shape[0] // 2
            return lax.dynamic_slice_in_dim(weight, c * n, n, 0)

        first_qkv = across(
            jnp.concatenate([quarter(w) for w in (query_weight, key_weight, value_weight)], 0)
        )
        second_qkv = flip(first_qkv, 1)
        dense_weights = []
        last = first_qkv
        for weight in (out_weight, inner_weight, outer_weight):
            piece, last = lax.optimization_barrier((quarter(weight), last))
            last = across(piece)
            dense_weights += [weight, last, flip(last, 1)]

        projected = project(
            counts, tokens, narrow, query_weight, key_weight, value_weight, first_qkv, second_qkv
        )
        queries, pieces = [], []
        for s in range(seqs):
            kv = turn(projected[2 * s + 1])
            queries.append(turn(projected[2 * s]).reshape(-1, BLK, width // GROUPS))
            held = [kv.reshape(-1, BLK, kv.shape[2])]
            for m in masks:
                held += [flip(piece, m) for piece in held]
            pieces.append(held)

        attended, lses = [], []
        for s in range(seqs):
            o, lse = attend(s, per_plane, lengths, block_order, queries[s], pieces[s])
            attended.append(o.reshape(queries[s].shape))
            lses.append(lse)
    if fused:
        fours = [first_back, *attended[1:]]
        found = middle(lengths, block_order, tokens, teacher, pair, fours, dense_weights)
        output, firsts, sums, wide_sums, a_own, a_give, b_own, b_give = found[:8]
        heads_grad = [g.reshape(queries[0].shape) for g in found[8:]]
        ready = (a_own, a_give, b_own, b_give)
    else:
        dense_out = []
        for s in range(seqs):
            o4 = turn(attended[s].reshape(GROUPS, rows, -1))
            dense_out.append(
                dense(
                    row_counts[s], o4, tokens[s], teacher[s], narrow[2:], wide_vec, dense_weights
                )
            )
        output = jnp.stack([d[0] for d in dense_out])
        first_grads = [d[1] for d in dense_out]
        heads_grad = [turn(d[2]).reshape(queries[s].shape) for s, d in enumerate(dense_out)]
        sums = sum(d[9] for d in dense_out)
        wide_sums = sum(d[10] for d in dense_out)
        dense_sums = [reduced_dense(g) for g in dense_grads([d[3:9] for d in dense_out])]

    if fused:
        flat_rows = (GROUPS * rows, width // GROUPS)
        rq, rkv, ready = attend_back_all(
            [
                [
                    *(a.reshape(flat_rows) for a in (queries[s], heads_grad[s], attended[s])),
                    lses[s],
                    pieces[s][0].reshape(-1, pieces[s][0].shape[2]),
                ]
                for s in range(seqs)
            ],
            ready,
        )
    else:
        dqs, dkvs = [], []
        for s in range(seqs):
            found = attend_back(
                scalars[s], queries[s], heads_grad[s], attended[s], lses[s], pieces[s]
            )
            dqs.append(turn(found[0].reshape(GROUPS, rows, -1)))
            held = [piece.reshape(GROUPS, rows, -1) for piece in found[1:]]
            for m in reversed(masks):
                n = len(held) // 2
                held = [add_low(mine, flip(theirs, m)) for mine, theirs in zip(held[:n], held[n:])]
            dkvs.append(turn(held[0]))
        tokens_grad, g_qkv, sums_qkv = project_grads(
            counts,
            tokens,
            first_grads,
            dqs + dkvs,
            query_weight,
            key_weight,
            value_weight,
            first_qkv,
            second_qkv,
        )

    if fused:
        tokens_grad, qkv, total, small = finish(
            lengths,
            block_order,
            tokens,
            firsts,
            rq,
            rkv,
            sums,
            wide_sums,
            ready,
            query_weight,
            key_weight,
            value_weight,
            others,
        )
        grads = unpack(qkv, total, small, output, tokens_grad, hidden)
        query_grad, key_grad, value_grad, out_grad, inner_grad, outer_grad = grads[:6]
        output, tokens_grad = grads[6:8]
        rows_of = dict(zip((0, 1, 2, 3, 4, 5, 7, 8, 9), grads[8:17]))
        loss = grads[17].reshape(())

        def vector(start, length):
            return rows_of[start // width]

    else:
        valid = jnp.full((128,), sum(jnp.sum(r) for r in row_counts).astype(F32))
        small = jnp.concatenate(
            [sums[:7].reshape(-1), sums_qkv[:2].reshape(-1), wide_sums[0], valid]
        )
        small = lax.psum(small, ("ctx", "wa"))
        qkv = reduced(jnp.moveaxis(g_qkv, (2, 1), (0, 1)).reshape(4, 3, -1, 128))
        out_grad, inner_grad, outer_grad = (
            paired(g).reshape(-1, g.shape[-1]).astype(F32) for g in dense_sums
        )
        qkv = qkv.reshape(6, 3, half, 128).astype(F32)
        query_grad, key_grad, value_grad = (
            qkv[:, i].swapaxes(0, 1).reshape(half, width) for i in range(3)
        )

        def vector(start, length):
            return lax.dynamic_slice_in_dim(small, start + x * (length // 2), length // 2, 0)

        loss = jnp.sum(small[6 * width : 7 * width]) / (small[9 * width + hidden] * width)

    end = 9 * width
    return (
        output,
        tokens_grad,
        query_grad,
        vector(7 * width, width),
        key_grad,
        value_grad,
        vector(8 * width, width),
        out_grad,
        vector(5 * width, width),
        vector(3 * width, width),
        vector(4 * width, width),
        inner_grad,
        vector(end, hidden),
        outer_grad,
        vector(2 * width, width),
        vector(0, width),
        vector(width, width),
        loss,
    )


def solution(mesh):
    row, split, both = P("wa"), P("wa", None), P("wa", "ctx", None)
    placed = (both, both, row, P(), split, row, split, split, row, split, row, row, row)
    placed += (split, row, split, row, row, row)
    return jax.shard_map(
        functools.partial(shards, mesh.shape["ctx"]),
        mesh=mesh,
        in_specs=placed,
        out_specs=(
            both,
            both,
            split,
            row,
            split,
            split,
            row,
            split,
            row,
            row,
            row,
            split,
            row,
            split,
            row,
            row,
            row,
            P(),
        ),
        check_vma=False,
    )
```
